32 devices in a mesh: rep: 4 (over y, x), fsdp: 8 (over z, core).
Axes of the slice: x: 2, y: 2, z: 4, core: 2. Of those that a mesh axis runs over, the one named last changes fastest.
Arguments:
- block_input: bfloat16 [4, 2048, 2048], P('rep', 'fsdp')
- cotangent: bfloat16 [4, 2048, 2048], P('rep', 'fsdp'), may hold values from -6 to 6
- glob_select: int32 [4, 64, 2048], P('rep', None, 'fsdp'), may hold values from 0 to 1, as said below
- assignment: int32 [8, 464], P('fsdp'), may hold values from 0 to 463, as said below
- master: float32 [8, 464, 128, 128], P('fsdp', 'rep')
- first_moment: float32 [8, 464, 128, 128], P('fsdp', 'rep')
- second_moment: float32 [8, 464, 128, 128], P('fsdp', 'rep')
- left_basis: float32 [8, 464, 128, 128], P('fsdp', 'rep'), may hold values from -0.5 to 0.5
- right_basis: float32 [8, 464, 128, 128], P('fsdp', 'rep'), may hold values from -0.5 to 0.5
- gains: float32 [2, 2048], replicated, may hold values from 0.5 to 1.5
- gain_first: float32 [2, 2048], replicated, may hold values from -448 to 448
- gain_second: float32 [2, 2048], replicated, may hold values from 5242.88 to 20971.52
Outputs:
- block_output: float32 [4, 2048, 2048], P('rep', 'fsdp')
- input_grad: float32 [4, 2048, 2048], P('rep', 'fsdp')
- new_first_moment: float32 [8, 464, 128, 128], P('fsdp', 'rep')
- new_second_moment: float32 [8, 464, 128, 128], P('fsdp', 'rep')
- new_master: float32 [8, 464, 128, 128], P('fsdp', 'rep')
- master_copy: bfloat16 [8, 464, 128, 128], P('fsdp', 'rep')
- new_gain_first: float32 [2, 2048], replicated
- new_gain_second: float32 [2, 2048], replicated
- new_gains: float32 [2, 2048], replicated
- rms_stats: float32 [3], replicated
The draws below stay inside these ranges and needn't reach their ends.
Inputs may be any that keep to these rules, and one draw needn't show every extreme that they name: `glob_select`: each of the 64 rows of a sequence holds a single 1, and the rows mark 64 different positions. `assignment`: each row names every slot of its band once.
All inputs are finite; a program needn't handle non-finite values.
Results may differ from the reference program's by a relative error of at most 0.025.
Values may be sent and summed in bfloat16 or wider, within the bound.
A program may use at most 512 MiB of HBM per device.

```python
import math
import jax
import jax.numpy as jnp
from jax import lax

D = 2048
H = 32
KVH = 8
HD = 64
FF = 8192
WINDOW = 512
GLOB = 64
BLK = 128
STEP = 10
BANDS = 8
LEN = 2048
SEQS = 4
TPB = 464


def matrix_shapes_drawn():
    kv_width = KVH * HD
    return [(D, D), (D, kv_width), (D, kv_width), (D, D), (D, FF), (D, FF), (FF, D)]


def kind_values(level_list):
    pieces = []
    for (row_total, col_total), level_value in zip(matrix_shapes_drawn(), level_list):
        tile_count = row_total // BANDS // BLK * (col_total // BLK)
        pieces.append(jnp.full((tile_count,), level_value, jnp.float32))
    return jnp.concatenate(pieces)


def band_orders(key):
    band_keys = jax.random.split(jax.random.fold_in(key, 71), BANDS)
    return jax.vmap(lambda single: jax.random.permutation(single, TPB))(band_keys)


def slot_levels(key, level_list):
    inverse = jnp.argsort(band_orders(key), axis=1)
    return jnp.take(kind_values(level_list), inverse)


def grad_levels():
    token_root = (SEQS * LEN) ** 0.5
    return [0.5 * token_root, 0.5 * token_root, 0.8 * token_root, token_root * (WINDOW / 4.0) ** (-0.5), 0.3 * token_root, 0.3 * token_root, 0.6 * token_root]


def draw_assignment(key, part):
    orders = band_orders(key)
    return orders.astype(jnp.int32)


def draw_master(key, part):
    levels = slot_levels(key, [D ** (-0.5), D ** (-0.5), D ** (-0.5), (D * 8 // WINDOW) ** (-0.5), D ** (-0.5), D ** (-0.5), FF ** (-0.5)])
    key = jax.random.fold_in(key, 5)
    full_shape = (BANDS, TPB, BLK, BLK)
    noise_draw = jax.random.normal(key, full_shape, jnp.float32)
    return noise_draw * levels[:, :, None, None]


def draw_first_moment(key, part):
    levels = slot_levels(key, grad_levels())
    key = jax.random.fold_in(key, 6)
    noise_draw = jax.random.normal(key, (BANDS, TPB, BLK, BLK), jnp.float32)
    return noise_draw * levels[:, :, None, None]


def draw_second_moment(key, part):
    levels = slot_levels(key, grad_levels())
    key = jax.random.fold_in(key, 7)
    factor = jnp.exp(jax.random.uniform(key, (BANDS, TPB, BLK, BLK), jnp.float32, 0.0, 1.3862944))
    return factor * (levels * levels)[:, :, None, None]


def draw_block_input(key, part):
    key = jax.random.fold_in(key, 11)
    place = jnp.arange(LEN, dtype=jnp.float32) / max(LEN - 1, 1)
    sequence = jnp.arange(SEQS, dtype=jnp.float32) / max(SEQS - 1, 1)
    top_scale = 3.0 ** 0.5
    noise_draw = jax.random.normal(key, (SEQS, LEN, D), jnp.float32)
    ramp = (1.0 + (top_scale - 1.0) * sequence)[:, None, None] * (1.0 + (top_scale - 1.0) * place)[None, :, None]
    return (noise_draw * ramp).astype(jnp.bfloat16)


def draw_glob_select(key, part):
    key = jax.random.fold_in(key, 13)
    sequence_keys = jax.random.split(key, SEQS)
    chosen = jax.vmap(lambda single: jax.random.permutation(single, LEN)[:GLOB])(sequence_keys)
    return (chosen[:, :, None] == jnp.arange(LEN, dtype=jnp.int32)[None, None, :]).astype(jnp.int32)


def steps_of(key, extent, cuts, smallest, top_value):
    def one(dim, blocks):
        steps = jax.random.uniform(jax.random.fold_in(jax.random.fold_in(key, 6), dim), (blocks,), jnp.float32, smallest / len(cuts), top_value / len(cuts))
        return jnp.repeat(jnp.exp(steps), extent[dim] // blocks).reshape((-1,) + (1,) * (len(extent) - dim - 1))

    loudness = one(*cuts[0])
    for cut in cuts[1:]:
        loudness = loudness * one(*cut)
    return loudness


def centred(stream_key, dims, scale, most, cuts=(), held_as=jnp.bfloat16):
    factor_of = steps_of(stream_key, dims, cuts, -0.22, 0.18) if cuts else 1.0
    array = jax.random.normal(stream_key, dims, jnp.float32) * scale * factor_of
    return jnp.minimum(jnp.maximum(array, -most), most).astype(held_as)


def setup_inputs(seed: int = 0) -> dict:
    seeds = jax.random.split(jax.random.key(seed), 13)
    return {
        "block_input": draw_block_input(jax.random.fold_in(seeds[12], 71), 0),
        "cotangent": centred(seeds[1], (SEQS, LEN, D), 1.0, 6.0, ((0, 4), (1, 8))),
        "glob_select": draw_glob_select(jax.random.fold_in(seeds[12], 71), 0),
        "assignment": draw_assignment(jax.random.fold_in(seeds[12], 71), 0),
        "master": draw_master(jax.random.fold_in(seeds[12], 71), 0),
        "first_moment": draw_first_moment(jax.random.fold_in(seeds[12], 71), 0),
        "second_moment": draw_second_moment(jax.random.fold_in(seeds[12], 71), 0),
        "left_basis": centred(seeds[7], (BANDS, TPB, BLK, BLK), BLK ** -0.5, 0.5, ((0, 8), (1, 4)), jnp.float32),
        "right_basis": centred(seeds[8], (BANDS, TPB, BLK, BLK), BLK ** -0.5, 0.5, ((0, 8), (1, 4)), jnp.float32),
        "gains": jnp.clip(1.0 + 0.1 * jax.random.normal(seeds[9], (2, D), jnp.float32), 0.5, 1.5),
        "gain_first": centred(seeds[10], (2, D), (0.8 * (SEQS * LEN) ** 0.5), 448.0, (), jnp.float32),
        "gain_second": jnp.clip(jnp.exp(jax.random.uniform(seeds[11], (2, D), jnp.float32, math.log(5242.88), math.log(20971.52))), 5242.88, 20971.52),
    }


norm_eps = 1e-05
rope_theta = 500000.0
beta_one = 0.5
beta_two = 0.5
adam_eps = 1e-08
weight_decay = 0.1
gain_rate = 0.5
masked_value = -1e+30

@jax.custom_vjp
def low(v):
    return lax.optimization_barrier(v.astype(jnp.bfloat16)).astype(jnp.float32)

@jax.custom_vjp
def low_back(v):
    return v

def low_keep(v):
    return (low(v), None)

def low_pass(kept, grad):
    return (grad,)

def back_keep(v):
    return (v, None)

def back_low(kept, grad):
    return (low(grad),)
low.defvjp(low_keep, low_pass)
low_back.defvjp(back_keep, back_low)

def matrix_shapes():
    kv_width = KVH * HD
    return [(D, D), (D, kv_width), (D, kv_width), (D, D), (D, FF), (D, FF), (FF, D)]

def kind_rates():
    rate_list = [D ** (-0.5), D ** (-0.5), D ** (-0.5), (D * 8 // WINDOW) ** (-0.5), D ** (-0.5), D ** (-0.5), FF ** (-0.5)]
    pieces = []
    for (row_total, col_total), rate_value in zip(matrix_shapes(), rate_list):
        tile_count = row_total // BANDS // BLK * (col_total // BLK)
        pieces.append(jnp.full((tile_count,), rate_value, jnp.float32))
    return jnp.concatenate(pieces)

def assemble(tiles):
    matrices = []
    offset = 0
    for row_total, col_total in matrix_shapes():
        band_rows = row_total // BANDS
        tile_count = band_rows // BLK * (col_total // BLK)
        segment = tiles[:, offset:offset + tile_count]
        segment = segment.reshape(BANDS, band_rows // BLK, col_total // BLK, BLK, BLK)
        matrices.append(segment.transpose(0, 1, 3, 2, 4).reshape(row_total, col_total))
        offset += tile_count
    return matrices

def slice_tiles(matrices):
    pieces = []
    for matrix in matrices:
        row_total, col_total = matrix.shape
        segment = matrix.reshape(BANDS, row_total // (BANDS * BLK), BLK, col_total // BLK, BLK)
        pieces.append(segment.transpose(0, 1, 3, 2, 4).reshape(BANDS, -1, BLK, BLK))
    return jnp.concatenate(pieces, 1)

def rope_tables(position):
    halves = jnp.arange(HD // 2, dtype=jnp.float32) * (2.0 / HD)
    frequency = rope_theta ** (-halves)
    angles = position.astype(jnp.float32)[:, None] * frequency[None, :]
    angles = jnp.concatenate([angles, angles], 1)
    return (jnp.cos(angles), jnp.sin(angles))

def rotate(vectors, cosine_table, sine_table):
    half_width = vectors.shape[-1] // 2
    turned = jnp.concatenate([-vectors[..., half_width:], vectors[..., :half_width]], -1)
    return vectors * cosine_table[:, None, :] + turned * sine_table[:, None, :]

def rms_norm(values, gain_row):
    return values * lax.rsqrt(lax.optimization_barrier(jnp.mean(values * values, -1, keepdims=True)) + norm_eps) * gain_row

def layer_pass(inputs, w_query, w_key, w_value, w_output, w_gate, w_up, w_down, gain_rows, pick_rows):
    highest = lax.Precision.HIGHEST
    kv_width = KVH * HD
    group_size = H // KVH
    score_scale = HD ** (-0.5)
    position = jnp.arange(LEN, dtype=jnp.int32)
    cosine_table, sine_table = rope_tables(position)
    normed_one = low(rms_norm(inputs, gain_rows[0]))
    query_pre = low_back(jnp.dot(normed_one, w_query, precision=highest)).reshape(LEN, H, HD)
    key_pre = low_back(jnp.dot(normed_one, w_key, precision=highest)).reshape(LEN, KVH, HD)
    value_rows = low(low_back(jnp.dot(normed_one, w_value, precision=highest)))
    query_rows = low(rotate(query_pre, cosine_table, sine_table))
    key_rows = low(rotate(key_pre, cosine_table, sine_table)).reshape(LEN, kv_width)
    glob_keys = jnp.dot(pick_rows, key_rows, precision=highest)
    glob_values = jnp.dot(pick_rows, value_rows, precision=highest)
    glob_place = jnp.dot(pick_rows, position.astype(jnp.float32), precision=highest)
    block_rows = min(512, LEN)
    pad_keys = jnp.concatenate([jnp.zeros((WINDOW, kv_width), jnp.float32), key_rows], 0)
    pad_values = jnp.concatenate([jnp.zeros((WINDOW, kv_width), jnp.float32), value_rows], 0)

    def block_attention(block_index):
        first_row = block_index * block_rows
        query_block = lax.dynamic_slice_in_dim(query_rows, first_row, block_rows, 0)
        query_block = query_block.reshape(block_rows, KVH, group_size, HD)
        key_block = lax.dynamic_slice_in_dim(pad_keys, first_row, WINDOW + block_rows, 0)
        value_block = lax.dynamic_slice_in_dim(pad_values, first_row, WINDOW + block_rows, 0)
        all_keys = jnp.concatenate([key_block, glob_keys], 0).reshape(-1, KVH, HD)
        all_values = jnp.concatenate([value_block, glob_values], 0).reshape(-1, KVH, HD)
        query_pos = (first_row + jnp.arange(block_rows, dtype=jnp.int32))[:, None]
        key_pos = (first_row - WINDOW + jnp.arange(WINDOW + block_rows, dtype=jnp.int32))[None, :]
        window_mask = (key_pos > query_pos - WINDOW) & (key_pos <= query_pos) & (key_pos >= 0)
        glob_mask = glob_place[None, :] <= (query_pos - WINDOW).astype(jnp.float32)
        allowed = jnp.concatenate([window_mask, glob_mask], 1)
        scores = jnp.einsum('qhgd,khd->hgqk', query_block, all_keys, precision=highest) * score_scale
        scores = low_back(scores)
        scores = jnp.where(allowed[None, None], scores, masked_value)
        row_max = lax.optimization_barrier(jnp.max(scores, -1, keepdims=True))
        exp_rows = jnp.exp(scores - row_max)
        softmax_rows = exp_rows / lax.optimization_barrier(jnp.sum(exp_rows, -1, keepdims=True))
        attended = jnp.einsum('hgqk,khd->qhgd', low(softmax_rows), all_values, precision=highest)
        return attended.reshape(block_rows, D)
    attended = lax.map(jax.checkpoint(block_attention), jnp.arange(LEN // block_rows, dtype=jnp.int32))
    attended = attended.reshape(LEN, D)
    attn_branch = low_back(jnp.dot(low(low_back(attended)), w_output, precision=highest))
    middle = inputs + attn_branch
    normed_two = low(rms_norm(middle, gain_rows[1]))
    gate_rows = low_back(jnp.dot(normed_two, w_gate, precision=highest))
    up_rows = low_back(jnp.dot(normed_two, w_up, precision=highest))
    activation = low(gate_rows * jax.nn.sigmoid(gate_rows) * up_rows)
    ffn_branch = low_back(jnp.dot(activation, w_down, precision=highest))
    return (middle + ffn_branch, middle)

def reference(block_input, cotangent, glob_select, assignment, master, first_moment, second_moment, left_basis, right_basis, gains, gain_first, gain_second):
    highest = lax.Precision.HIGHEST
    tile_weights = jnp.take_along_axis(master, assignment[:, :, None, None], axis=1)
    weights = [low(matrix) for matrix in assemble(tile_weights)]

    def one_sequence(totals, items):
        inputs, grad_seq, pick_rows = items

        def forward(inputs_now, w_query, w_key, w_value, w_output, w_gate, w_up, w_down, gain_rows):
            return layer_pass(inputs_now, w_query, w_key, w_value, w_output, w_gate, w_up, w_down, gain_rows, pick_rows)
        output, pullback, middle = jax.vjp(forward, inputs, *weights, gains, has_aux=True)
        grad_list = pullback(grad_seq)
        new_totals = tuple((total_now + grad_now for total_now, grad_now in zip(totals, grad_list[1:])))
        squares = jnp.stack([jnp.sum(inputs * inputs), jnp.sum(middle * middle), jnp.sum(output * output)])
        return (new_totals, (output, grad_list[0], squares))
    initial = tuple((jnp.zeros_like(matrix) for matrix in weights)) + (jnp.zeros_like(gains),)
    items = (block_input.astype(jnp.float32), cotangent.astype(jnp.float32), glob_select.astype(jnp.float32))
    totals, (block_output, input_grad, squares) = lax.scan(one_sequence, initial, items)
    tile_grads = slice_tiles(list(totals[:7]))
    inverse = jnp.argsort(assignment, axis=1)
    slot_grads = jnp.take_along_axis(tile_grads, inverse[:, :, None, None], axis=1)
    rotated = jnp.einsum('fsia,fsij->fsaj', left_basis, slot_grads, precision=highest)
    rotated = jnp.einsum('fsaj,fsjb->fsab', rotated, right_basis, precision=highest)
    new_first = beta_one * first_moment + (1.0 - beta_one) * rotated
    new_second = beta_two * second_moment + (1.0 - beta_two) * rotated * rotated
    direction = new_first / (1.0 - beta_one ** STEP) / (jnp.sqrt(new_second / (1.0 - beta_two ** STEP)) + adam_eps)
    update = jnp.einsum('fsia,fsab->fsib', left_basis, direction, precision=highest)
    update = jnp.einsum('fsib,fsjb->fsij', update, right_basis, precision=highest)
    slot_rates = jnp.take(kind_rates(), inverse)
    new_master = master - slot_rates[:, :, None, None] * (update + weight_decay * master)
    gain_grad = totals[7]
    new_gain_first = beta_one * gain_first + (1.0 - beta_one) * gain_grad
    new_gain_second = beta_two * gain_second + (1.0 - beta_two) * gain_grad * gain_grad
    gain_step = new_gain_first / (1.0 - beta_one ** STEP) / (jnp.sqrt(new_gain_second / (1.0 - beta_two ** STEP)) + adam_eps)
    new_gains = gains - gain_rate * gain_step
    rms_stats = jnp.sqrt(lax.optimization_barrier(jnp.sum(squares, 0)) / (SEQS * LEN * D))
    return (block_output, input_grad, new_first, new_second, new_master, new_master.astype(jnp.bfloat16), new_gain_first, new_gain_second, new_gains, rms_stats)
```

```python
import jax
import jax.numpy as jnp
import numpy as np
from jax import lax
from jax.sharding import PartitionSpec as P

D = 2048
H = 32
KVH = 8
HD = 64
FF = 8192
WINDOW = 512
BLK = 128
STEP = 10


norm_eps = 1e-05
rope_theta = 500000.0
beta_one = 0.5
beta_two = 0.5
adam_eps = 1e-08
weight_decay = 0.1
gain_rate = 0.5
masked_value = -1e30


def matrix_shapes():
    kv_width = KVH * HD
    return [(D, D), (D, kv_width), (D, kv_width), (D, D), (D, FF), (D, FF), (FF, D)]


def kind_rates(band_total):
    rate_list = [
        D ** (-0.5),
        D ** (-0.5),
        D ** (-0.5),
        (D * 8 // WINDOW) ** (-0.5),
        D ** (-0.5),
        D ** (-0.5),
        FF ** (-0.5),
    ]
    pieces = []
    for (row_total, col_total), rate_value in zip(matrix_shapes(), rate_list):
        tile_count = row_total // band_total // BLK * (col_total // BLK)
        pieces.append(jnp.full((tile_count,), rate_value, jnp.float32))
    return jnp.concatenate(pieces)


def band_matrices(tiles, band_total):
    matrices = []
    offset = 0
    for row_total, col_total in matrix_shapes():
        band_rows = row_total // band_total
        tile_count = band_rows // BLK * (col_total // BLK)
        segment = tiles[offset : offset + tile_count].reshape(
            band_rows // BLK, col_total // BLK, BLK, BLK
        )
        matrices.append(segment.transpose(0, 2, 1, 3).reshape(band_rows, col_total))
        offset += tile_count
    return matrices


def band_tiles(matrices):
    pieces = []
    for matrix in matrices:
        row_count, col_count = matrix.shape
        segment = matrix.reshape(row_count // BLK, BLK, col_count // BLK, BLK).transpose(0, 2, 1, 3)
        pieces.append(segment.reshape(-1, BLK, BLK))
    return jnp.concatenate(pieces, 0)


def rope_tables(position):
    halves = jnp.arange(HD // 2, dtype=jnp.float32) * (2.0 / HD)
    frequency = rope_theta ** (-halves)
    angles = position.astype(jnp.float32)[:, None] * frequency[None, :]
    angles = jnp.concatenate([angles, angles], 1)
    return (jnp.cos(angles), jnp.sin(angles))


def rotate(vectors, cosine_table, sine_table):
    half_width = vectors.shape[-1] // 2
    turned = jnp.concatenate([-vectors[..., half_width:], vectors[..., :half_width]], -1)
    return vectors * cosine_table[:, None, :] + turned * sine_table[:, None, :]


def rotate_back(grad_rows, cosine_table, sine_table):
    half_width = grad_rows.shape[-1] // 2
    scaled = grad_rows * sine_table[:, None, :]
    turned = jnp.concatenate([scaled[..., half_width:], -scaled[..., :half_width]], -1)
    return grad_rows * cosine_table[:, None, :] + turned


def norm_back(values, row_scale, gain_row, grad_rows):
    weighted = grad_rows * gain_row
    return row_scale * weighted - values * row_scale**3 * jnp.mean(
        weighted * values, -1, keepdims=True
    )


def to_rep(block, distance):
    route = [(i, i ^ distance) for i in range(lax.axis_size("rep"))]
    return lax.ppermute(block, "rep", route)


def square():
    return lax.axis_size("rep") == 4


def rep_gather(block):
    if not square():
        return lax.all_gather(block, "rep", axis=0)
    cut = block.shape[0] // 2
    near = to_rep(block, 1)
    far = to_rep(block, 2)
    low = to_rep(near[:cut], 2)
    high = to_rep(far[cut:], 1)
    return jnp.stack([block, near, far, jnp.concatenate([low, high], 0)], 0)


def rep_of(entry):
    place = lax.axis_index("rep")
    return place ^ entry if square() else entry


def rep_scatter(parts):
    if not square():
        flat = parts.reshape(-1, parts.shape[-1])
        return lax.psum_scatter(flat, "rep", scatter_dimension=0, tiled=True).astype(jnp.float32)
    half = parts.shape[-1] // 2
    totals = []
    for side, (first, second) in ((parts[..., :half], (1, 2)), (parts[..., half:], (2, 1))):
        away = to_rep(jnp.stack([side[first], side[3]], 0), first)
        other = (side[second].astype(jnp.float32) + away[1].astype(jnp.float32)).astype(parts.dtype)
        own = side[0].astype(jnp.float32) + away[0].astype(jnp.float32)
        totals.append(own + to_rep(other, second).astype(jnp.float32))
    return jnp.concatenate(totals, -1)


def add_all(value, axis):
    total = value.astype(jnp.float32)
    distance = 1
    while distance < lax.axis_size(axis):
        route = [(i, i ^ distance) for i in range(lax.axis_size(axis))]
        total = total + lax.ppermute(total.astype(value.dtype), axis, route).astype(jnp.float32)
        distance *= 2
    return total


def shifted(block, axis, distance):
    devices = range(lax.axis_size(axis))
    route = [(i - distance, i) for i in devices if i - distance in devices]
    return lax.ppermute(block, axis, route)


def tile_offsets(band_total):
    offsets = [0]
    for row_total, col_total in matrix_shapes():
        offsets.append(offsets[-1] + row_total // band_total // BLK * (col_total // BLK))
    return offsets


def whole_tiles(band_total, rep_total):
    return KVH * HD // rep_total % BLK == 0 and FF // band_total // rep_total % BLK == 0


def slice_layout(band_total, rep_total):
    offsets = tile_offsets(band_total)
    layout = []
    for kind, (row_total, col_total) in enumerate(matrix_shapes()):
        rows, cols = row_total // band_total // BLK, col_total // BLK
        grid = offsets[kind] + np.arange(rows * cols).reshape(rows, cols)
        if kind == 6:
            layout.append(grid.reshape(rep_total, rows // rep_total, cols))
        elif kind in (4, 5):
            cut = grid.reshape(rows, band_total, rep_total, -1).transpose(2, 0, 1, 3)
            layout.append(cut.reshape(rep_total, rows, -1))
        else:
            layout.append(grid.reshape(rows, rep_total, -1).transpose(1, 0, 2))
    return layout


def tiles_to_matrix(tiles):
    rows, cols = tiles.shape[:2]
    return tiles.transpose(0, 2, 1, 3).reshape(rows * BLK, cols * BLK)


def matrix_to_tiles(matrix):
    rows, cols = matrix.shape
    cut = matrix.reshape(rows // BLK, BLK, cols // BLK, BLK)
    return cut.transpose(0, 2, 1, 3).reshape(-1, BLK, BLK)


def cut_slices(matrices, band_total, rep_total):
    place = lax.axis_index("rep")
    slices = []
    for kind, matrix in enumerate(matrices):
        rows, cols = matrix.shape
        if kind == 3:
            slices.append(matrix)
        elif kind == 6:
            slices.append(lax.dynamic_slice_in_dim(matrix, place * (rows // rep_total), rows // rep_total, 0))
        elif kind in (4, 5):
            cut = matrix.reshape(rows, band_total, rep_total, -1)
            slices.append(lax.dynamic_index_in_dim(cut, place, 2, False).reshape(rows, -1))
        else:
            slices.append(lax.dynamic_slice_in_dim(matrix, place * (cols // rep_total), cols // rep_total, 1))
    return slices


def join_slices(stacks, band_total, rep_total):
    matrices = []
    for kind, stack in enumerate(stacks):
        rows, cols = stack.shape[1:]
        if kind == 3:
            matrices.append(stack[0])
        elif kind == 6:
            matrices.append(stack.reshape(-1, cols))
        elif kind in (4, 5):
            cut = stack.reshape(rep_total, rows, band_total, -1).transpose(1, 2, 0, 3)
            matrices.append(cut.reshape(rows, -1))
        else:
            matrices.append(stack.transpose(1, 0, 2).reshape(rows, -1))
    return matrices


def per_device(
    block_input,
    cotangent,
    glob_select,
    assignment,
    master,
    first_moment,
    second_moment,
    left_basis,
    right_basis,
    gains,
    gain_first,
    gain_second,
):
    highest = lax.Precision.HIGHEST
    band_total = lax.axis_size("fsdp")
    rep_total = lax.axis_size("rep")
    place = lax.axis_index("rep")
    band = lax.axis_index("fsdp")
    heads = H // rep_total
    kv_heads = KVH // rep_total
    group_size = H // KVH
    q_width = heads * HD
    kv_width = kv_heads * HD
    score_scale = HD ** (-0.5)
    tok_count = block_input.shape[1]
    own_count = master.shape[1]
    tile_total = own_count * rep_total
    aligned = whole_tiles(band_total, rep_total)
    tile_order = assignment[0]

    slots = rep_gather(master[0].astype(jnp.bfloat16))
    slots = slots.reshape(tile_total, BLK, BLK)
    slot_entry = tile_order // own_count
    if square():
        slot_entry = slot_entry ^ place
    tile_place = slot_entry * own_count + tile_order % own_count

    residual = block_input[0].astype(jnp.float32)
    grad_top = cotangent[0]
    position = band * tok_count + jnp.arange(tok_count, dtype=jnp.int32)
    cosine_table, sine_table = rope_tables(position)
    scale_one = lax.rsqrt(jnp.mean(residual * residual, -1, keepdims=True) + norm_eps)
    normed_one = (residual * scale_one * gains[0]).astype(jnp.bfloat16)
    normed_one_all = rep_gather(normed_one).reshape(-1, D)
    pick_rows = glob_select[0]
    selector = pick_rows.astype(jnp.bfloat16)
    glob_pos_part = jnp.sum(pick_rows * position[None, :], 1)
    digits = jnp.stack([glob_pos_part // 256, glob_pos_part % 256], 1).astype(jnp.bfloat16)
    digits = jnp.pad(digits, ((0, 0), (0, BLK - 2)))
    glob_part = jnp.concatenate(
        [jnp.dot(selector, normed_one, preferred_element_type=jnp.float32).astype(jnp.bfloat16), digits], 1
    )
    glob_rows = lax.psum(glob_part, "fsdp")
    glob_rows_all = rep_gather(glob_rows)
    selector_all = rep_gather(selector)
    glob_normed = glob_rows_all[..., :D].reshape(-1, D)
    glob_digits = glob_rows_all[..., D : D + 2].astype(jnp.float32)
    glob_place = glob_digits[..., 0] * 256.0 + glob_digits[..., 1]
    glob_total = glob_place.shape[1]
    grad_top_all = rep_gather(grad_top).reshape(-1, D)

    if aligned:
        layout = slice_layout(band_total, rep_total)
        slices = []
        for kind, grid in enumerate(layout):
            if kind == 3:
                numbers = jnp.asarray(grid.transpose(1, 0, 2).reshape(grid.shape[1], -1))
            else:
                numbers = lax.dynamic_index_in_dim(jnp.asarray(grid), place, 0, False)
            tiles = jnp.take(slots, jnp.take(tile_place, numbers, mode="clip"), axis=0, mode="clip")
            slices.append(tiles_to_matrix(tiles))
    else:
        tiles = jnp.take(slots, tile_place, axis=0, mode="clip")
        slices = cut_slices(band_matrices(tiles, band_total), band_total, rep_total)

    def over_bands(slice_rows):
        return lax.all_gather(slice_rows, "fsdp", axis=0, tiled=True)

    w_inner = over_bands(jnp.concatenate(slices[0:3], 1))
    per_rep = band_total // rep_total
    lanes = (jnp.arange(per_rep) + place * per_rep == band)[:, None, None]
    w_output = lax.psum(jnp.where(lanes, slices[3][None], 0), "fsdp").reshape(q_width, D)
    w_gate = over_bands(slices[4])
    w_up = over_bands(slices[5])
    w_down = over_bands(slices[6])

    def mul(rows, weight):
        return jnp.dot(rows, weight, preferred_element_type=jnp.float32)

    def mul_back(rows, weight):
        return lax.dot_general(rows, weight, (((1,), (1,)), ((), ())), preferred_element_type=jnp.float32)

    def weight_grad(rows, grad_rows):
        return lax.dot_general(
            rows, grad_rows, (((0,), (0,)), ((), ())), preferred_element_type=jnp.float32
        ).astype(jnp.bfloat16)

    def own_sum(partial):
        return rep_scatter(partial.astype(jnp.bfloat16).reshape(rep_total, tok_count, D))

    inner_rows = mul(normed_one_all, w_inner)
    query_pre = inner_rows[:, :q_width].reshape(rep_total, tok_count, heads, HD)
    key_pre = inner_rows[:, q_width : q_width + kv_width].reshape(rep_total, tok_count, kv_heads, HD)
    value_rows = inner_rows[:, q_width + kv_width :].astype(jnp.bfloat16).reshape(rep_total, tok_count, kv_width)
    query_rows = rotate(query_pre, cosine_table, sine_table).astype(jnp.bfloat16)
    key_rows = rotate(key_pre, cosine_table, sine_table).astype(jnp.bfloat16).reshape(rep_total, tok_count, kv_width)
    glob_inner = mul(glob_normed, w_inner[:, q_width:])
    glob_cosine, glob_sine = rope_tables(glob_place.reshape(-1))
    glob_keys = rotate(glob_inner[:, :kv_width].reshape(-1, kv_heads, HD), glob_cosine, glob_sine)
    glob_keys = glob_keys.astype(jnp.bfloat16).reshape(rep_total, glob_total, kv_width)
    glob_values = glob_inner[:, kv_width:].astype(jnp.bfloat16).reshape(rep_total, glob_total, kv_width)
    back_count = (WINDOW + tok_count - 2) // tok_count
    own_pairs = jnp.concatenate([key_rows, value_rows], -1)
    pair_blocks = [own_pairs]
    for distance in range(1, back_count + 1):
        pair_blocks.insert(0, shifted(own_pairs, "fsdp", distance))
    pair_blocks.append(jnp.concatenate([glob_keys, glob_values], -1))
    all_pairs = jnp.concatenate(pair_blocks, 1)
    window_len = (back_count + 1) * tok_count
    window_pos = (band - back_count) * tok_count + jnp.arange(window_len, dtype=jnp.int32)
    all_keys = all_pairs[..., :kv_width].reshape(rep_total, -1, kv_heads, HD)
    all_values = all_pairs[..., kv_width:].reshape(rep_total, -1, kv_heads, HD)
    query_pos = position[:, None]
    window_mask = (
        (window_pos[None, :] > query_pos - WINDOW)
        & (window_pos[None, :] <= query_pos)
        & (window_pos[None, :] >= 0)
    )
    glob_mask = glob_place[:, None, :] <= (query_pos - WINDOW).astype(jnp.float32)[None]
    allowed = jnp.concatenate(
        [jnp.broadcast_to(window_mask[None], (rep_total, tok_count, window_len)), glob_mask], 2
    )
    grouped_query = query_rows.reshape(rep_total, tok_count, kv_heads, group_size, HD)

    def attention_scores():
        raw_scores = (
            jnp.einsum(
                "sqhgd,skhd->shgqk", grouped_query, all_keys, preferred_element_type=jnp.float32
            )
            * score_scale
        )
        return jnp.where(allowed[:, None, None], raw_scores, masked_value)

    scores = attention_scores()
    row_max = jnp.max(scores, -1, keepdims=True)
    exp_rows = jnp.exp(scores - row_max)
    row_total = jnp.sum(exp_rows, -1, keepdims=True)
    log_total = row_max + jnp.log(row_total)
    softmax_rows = exp_rows / row_total
    attended = jnp.einsum(
        "shgqk,skhd->sqhgd",
        softmax_rows.astype(jnp.bfloat16),
        all_values,
        preferred_element_type=jnp.float32,
    )
    attended_low = attended.reshape(rep_total * tok_count, q_width).astype(jnp.bfloat16)
    middle = residual + own_sum(mul(attended_low, w_output))
    scale_two = lax.rsqrt(jnp.mean(middle * middle, -1, keepdims=True) + norm_eps)
    normed_two = (middle * scale_two * gains[1]).astype(jnp.bfloat16)
    normed_two_all = rep_gather(normed_two).reshape(-1, D)

    gate_rows = mul(normed_two_all, w_gate)
    up_rows = mul(normed_two_all, w_up)
    sigmoid_gate = jax.nn.sigmoid(gate_rows)
    silu_gate = gate_rows * sigmoid_gate
    activation = (silu_gate * up_rows).astype(jnp.bfloat16)
    g_down = weight_grad(activation, grad_top_all)
    grad_act = mul_back(grad_top_all, w_down)
    grad_gate = (
        grad_act * up_rows * sigmoid_gate * (1.0 + gate_rows * (1.0 - sigmoid_gate))
    ).astype(jnp.bfloat16)
    grad_up = (grad_act * silu_gate).astype(jnp.bfloat16)
    grad_normed_two = own_sum(mul_back(grad_gate, w_gate) + mul_back(grad_up, w_up))
    g_gate = weight_grad(normed_two_all, grad_gate)
    g_up = weight_grad(normed_two_all, grad_up)
    block_out = middle + own_sum(mul(activation, w_down))

    def over_tokens(partial):
        return lax.psum_scatter(partial, "fsdp", scatter_dimension=0, tiled=True)

    s_down = over_tokens(g_down)
    s_gate = over_tokens(g_gate)
    s_up = over_tokens(g_up)

    grad_middle = grad_top.astype(jnp.float32) + norm_back(middle, scale_two, gains[1], grad_normed_two)
    grad_branch_all = rep_gather(grad_middle.astype(jnp.bfloat16)).reshape(-1, D)
    grad_attended = mul_back(grad_branch_all, w_output).astype(jnp.bfloat16)
    g_output = lax.psum(weight_grad(attended_low, grad_branch_all), "fsdp")
    grouped_grad = grad_attended.reshape(rep_total, tok_count, kv_heads, group_size, HD)
    softmax_again = jnp.exp(attention_scores() - log_total)
    grad_soft = jnp.einsum(
        "sqhgd,skhd->shgqk", grouped_grad, all_values, preferred_element_type=jnp.float32
    )
    inner_sum = jnp.sum(softmax_again * grad_soft, -1, keepdims=True)
    grad_scores = (softmax_again * (grad_soft - inner_sum)).astype(jnp.bfloat16)
    grad_values_all = jnp.einsum(
        "shgqk,sqhgd->skhd",
        softmax_again.astype(jnp.bfloat16),
        grouped_grad,
        preferred_element_type=jnp.float32,
    ).reshape(rep_total, -1, kv_width)
    grad_query = (
        jnp.einsum("shgqk,skhd->sqhgd", grad_scores, all_keys, preferred_element_type=jnp.float32)
        .reshape(rep_total, tok_count, heads, HD)
        * score_scale
    )
    grad_keys_all = (
        jnp.einsum(
            "shgqk,sqhgd->skhd", grad_scores, grouped_query, preferred_element_type=jnp.float32
        ).reshape(rep_total, -1, kv_width)
        * score_scale
    )
    grad_pairs_all = jnp.concatenate([grad_keys_all, grad_values_all], -1)
    grad_pairs = grad_pairs_all[:, window_len - tok_count : window_len]
    for distance in range(1, back_count + 1):
        start_row = window_len - (distance + 1) * tok_count
        sent = grad_pairs_all[:, start_row : start_row + tok_count].astype(jnp.bfloat16)
        grad_pairs = grad_pairs + shifted(sent, "fsdp", -distance).astype(jnp.float32)
    glob_pairs = add_all(grad_pairs_all[:, window_len:].astype(jnp.bfloat16), "fsdp")
    grad_pairs = grad_pairs + jnp.einsum(
        "sgt,sgw->stw", selector_all.astype(jnp.float32), glob_pairs, precision=highest
    )
    grad_query_pre = rotate_back(grad_query, cosine_table, sine_table).reshape(-1, q_width)
    grad_key_pre = rotate_back(
        grad_pairs[..., :kv_width].reshape(rep_total, tok_count, kv_heads, HD), cosine_table, sine_table
    ).reshape(-1, kv_width)
    grad_inner = jnp.concatenate(
        [grad_query_pre, grad_key_pre, grad_pairs[..., kv_width:].reshape(-1, kv_width)], 1
    ).astype(jnp.bfloat16)
    s_inner = over_tokens(weight_grad(normed_one_all, grad_inner))
    grad_normed_one = own_sum(mul_back(grad_inner, w_inner))
    grad_input = grad_middle + norm_back(residual, scale_one, gains[0], grad_normed_one)

    source = band // per_rep
    mine = lax.dynamic_index_in_dim(g_output.reshape(per_rep, D // band_total, D), band % per_rep, 0, False)
    out_entry = source ^ place if square() else source
    out_band = lax.dynamic_index_in_dim(rep_gather(mine), out_entry, 0, False)
    grad_slices = [
        s_inner[:, :q_width],
        s_inner[:, q_width : q_width + kv_width],
        s_inner[:, q_width + kv_width :],
        None,
        s_gate,
        s_up,
        s_down,
    ]
    slot_ids = jnp.arange(tile_total, dtype=jnp.int32)
    inverse = jnp.sum(jnp.where(tile_order[None, :] == slot_ids[:, None], slot_ids[None, :], 0), 1)
    own_slots = place * own_count + jnp.arange(own_count, dtype=jnp.int32)
    owned_tiles = jnp.take(inverse, own_slots, mode="clip")
    if aligned:
        pieces = []
        rows_of = np.zeros((rep_total, tile_total), np.int32)
        start = 0
        for kind, grid in enumerate(layout):
            if kind == 3:
                pieces.append(matrix_to_tiles(out_band))
                tile_ids = np.sort(grid.reshape(-1))
                rows_of[:, tile_ids] = start + np.arange(tile_ids.size)
                start += tile_ids.size
                continue
            tiles = rep_gather(matrix_to_tiles(grad_slices[kind]))
            pieces.append(tiles.reshape(-1, BLK, BLK))
            count = tiles.shape[1]
            for here in range(rep_total):
                for there in range(rep_total):
                    entry = here ^ there if square() else there
                    rows_of[here, grid[there].reshape(-1)] = start + entry * count + np.arange(count)
            start += rep_total * count
        tile_grads = jnp.concatenate(pieces, 0)
        tile_rows = lax.dynamic_index_in_dim(jnp.asarray(rows_of), place, 0, False)
        wanted = jnp.take(tile_rows, owned_tiles, mode="clip")
    else:
        stacks = [
            out_band[None] if piece is None else lax.all_gather(piece, "rep", axis=0) for piece in grad_slices
        ]
        tile_grads = band_tiles(join_slices(stacks, band_total, rep_total))
        wanted = owned_tiles
    owned_grad = jnp.take(tile_grads, wanted, axis=0, mode="clip").astype(jnp.float32)
    slot_rates = jnp.take(kind_rates(band_total), owned_tiles, mode="clip")
    left_rows = left_basis[0]
    right_rows = right_basis[0]
    rotated = jnp.einsum("sia,sij->saj", left_rows, owned_grad, precision=highest)
    rotated = jnp.einsum("saj,sjb->sab", rotated, right_rows, precision=highest)
    new_first = beta_one * first_moment[0] + (1.0 - beta_one) * rotated
    new_second = beta_two * second_moment[0] + (1.0 - beta_two) * rotated * rotated
    direction = (
        new_first
        / (1.0 - beta_one**STEP)
        / (jnp.sqrt(new_second / (1.0 - beta_two**STEP)) + adam_eps)
    )
    update = jnp.einsum("sia,sab->sib", left_rows, direction, precision=highest)
    update = jnp.einsum("sib,sjb->sij", update, right_rows, precision=highest)
    old_master = master[0]
    new_master = old_master - slot_rates[:, None, None] * (update + weight_decay * old_master)
    gain_terms = jnp.stack(
        [
            jnp.sum(grad_normed_one * residual * scale_one, 0),
            jnp.sum(grad_normed_two * middle * scale_two, 0),
        ]
    )
    square_terms = jnp.stack(
        [jnp.sum(residual * residual), jnp.sum(middle * middle), jnp.sum(block_out * block_out)]
    )
    sums = jnp.concatenate([gain_terms.reshape(-1), square_terms])
    sums = add_all(add_all(sums, "rep"), "fsdp")
    gain_grad, square_total = sums[: 2 * D].reshape(2, D), sums[2 * D :]
    new_gain_first = beta_one * gain_first + (1.0 - beta_one) * gain_grad
    new_gain_second = beta_two * gain_second + (1.0 - beta_two) * gain_grad * gain_grad
    gain_step = (
        new_gain_first
        / (1.0 - beta_one**STEP)
        / (jnp.sqrt(new_gain_second / (1.0 - beta_two**STEP)) + adam_eps)
    )
    new_gains = gains - gain_rate * gain_step
    rms_stats = jnp.sqrt(square_total / (rep_total * band_total * tok_count * D))
    return (
        block_out[None],
        grad_input[None],
        new_first[None],
        new_second[None],
        new_master[None],
        new_master.astype(jnp.bfloat16)[None],
        new_gain_first,
        new_gain_second,
        new_gains,
        rms_stats,
    )


def solution(mesh):
    in_specs = (
        P("rep", "fsdp", None),
        P("rep", "fsdp", None),
        P("rep", None, "fsdp"),
        P("fsdp", None),
        P("fsdp", "rep", None, None),
        P("fsdp", "rep", None, None),
        P("fsdp", "rep", None, None),
        P("fsdp", "rep", None, None),
        P("fsdp", "rep", None, None),
        P(),
        P(),
        P(),
    )
    out_specs = (
        P("rep", "fsdp", None),
        P("rep", "fsdp", None),
        P("fsdp", "rep", None, None),
        P("fsdp", "rep", None, None),
        P("fsdp", "rep", None, None),
        P("fsdp", "rep", None, None),
        P(),
        P(),
        P(),
        P(),
    )
    return jax.shard_map(
        per_device, mesh=mesh, in_specs=in_specs, out_specs=out_specs, check_vma=False
    )
```

```python
import functools

import jax
import jax.numpy as jnp
import numpy as np
from jax import lax
from jax.experimental import pallas as pl
from jax.experimental.pallas import tpu as pltpu
from jax.sharding import PartitionSpec as P

D = 2048
H = 32
KVH = 8
HD = 64
FF = 8192
WINDOW = 512
BLK = 128
STEP = 10


norm_eps = 1e-05
rope_theta = 500000.0
beta_one = 0.5
beta_two = 0.5
adam_eps = 1e-08
weight_decay = 0.1
gain_rate = 0.5
masked_value = -1e30


def matrix_shapes():
    kv_width = KVH * HD
    return [(D, D), (D, kv_width), (D, kv_width), (D, D), (D, FF), (D, FF), (FF, D)]


def kind_rates(band_total):
    rate_list = [
        D ** (-0.5),
        D ** (-0.5),
        D ** (-0.5),
        (D * 8 // WINDOW) ** (-0.5),
        D ** (-0.5),
        D ** (-0.5),
        FF ** (-0.5),
    ]
    pieces = []
    for (row_total, col_total), rate_value in zip(matrix_shapes(), rate_list):
        tile_count = row_total // band_total // BLK * (col_total // BLK)
        pieces.append(jnp.full((tile_count,), rate_value, jnp.float32))
    return jnp.concatenate(pieces)


def band_matrices(tiles, band_total):
    matrices = []
    offset = 0
    for row_total, col_total in matrix_shapes():
        band_rows = row_total // band_total
        tile_count = band_rows // BLK * (col_total // BLK)
        segment = tiles[offset : offset + tile_count].reshape(
            band_rows // BLK, col_total // BLK, BLK, BLK
        )
        matrices.append(segment.transpose(0, 2, 1, 3).reshape(band_rows, col_total))
        offset += tile_count
    return matrices


def band_tiles(matrices):
    pieces = []
    for matrix in matrices:
        row_count, col_count = matrix.shape
        segment = matrix.reshape(row_count // BLK, BLK, col_count // BLK, BLK).transpose(0, 2, 1, 3)
        pieces.append(segment.reshape(-1, BLK, BLK))
    return jnp.concatenate(pieces, 0)


def rope_tables(position):
    halves = jnp.arange(HD // 2, dtype=jnp.float32) * (2.0 / HD)
    frequency = rope_theta ** (-halves)
    angles = position.astype(jnp.float32)[:, None] * frequency[None, :]
    angles = jnp.concatenate([angles, angles], 1)
    return (jnp.cos(angles), jnp.sin(angles))


def rotate(vectors, cosine_table, sine_table):
    half_width = vectors.shape[-1] // 2
    turned = jnp.concatenate([-vectors[..., half_width:], vectors[..., :half_width]], -1)
    return vectors * cosine_table[:, None, :] + turned * sine_table[:, None, :]


def rotate_back(grad_rows, cosine_table, sine_table):
    half_width = grad_rows.shape[-1] // 2
    scaled = grad_rows * sine_table[:, None, :]
    turned = jnp.concatenate([scaled[..., half_width:], -scaled[..., :half_width]], -1)
    return grad_rows * cosine_table[:, None, :] + turned


def norm_back(values, row_scale, gain_row, grad_rows):
    weighted = grad_rows * gain_row
    return row_scale * weighted - values * row_scale**3 * jnp.mean(
        weighted * values, -1, keepdims=True
    )


def to_rep(block, distance):
    route = [(i, i ^ distance) for i in range(lax.axis_size("rep"))]
    return lax.ppermute(block, "rep", route)


def square():
    return lax.axis_size("rep") == 4


def square_pieces(block):
    cut = block.shape[0] // 2
    near = to_rep(block, 1)
    far = to_rep(block, 2)
    return block, near, far, to_rep(near[:cut], 2), to_rep(far[cut:], 1)


def rep_gather(block):
    if not square():
        return lax.all_gather(block, "rep", axis=0)
    own, near, far, low, high = square_pieces(block)
    return jnp.concatenate([own, near, far, low, high], 0).reshape((4,) + block.shape)


def rep_of(entry):
    place = lax.axis_index("rep")
    return place ^ entry if square() else entry


def rep_scatter(parts):
    if not square():
        flat = parts.reshape(-1, parts.shape[-1])
        return lax.psum_scatter(flat, "rep", scatter_dimension=0, tiled=True).astype(jnp.float32)
    half = parts.shape[-1] // 2
    totals = []
    for side, (first, second) in ((parts[..., :half], (1, 2)), (parts[..., half:], (2, 1))):
        away = to_rep(jnp.stack([side[first], side[3]], 0), first)
        other = (side[second].astype(jnp.float32) + away[1].astype(jnp.float32)).astype(parts.dtype)
        own = side[0].astype(jnp.float32) + away[0].astype(jnp.float32)
        totals.append(own + to_rep(other, second).astype(jnp.float32))
    return jnp.concatenate(totals, -1)


def add_all(value, axis):
    total = value.astype(jnp.float32)
    distance = 1
    while distance < lax.axis_size(axis):
        route = [(i, i ^ distance) for i in range(lax.axis_size(axis))]
        total = total + lax.ppermute(total.astype(value.dtype), axis, route).astype(jnp.float32)
        distance *= 2
    return total


def shifted(block, axis, distance):
    devices = range(lax.axis_size(axis))
    route = [(i - distance, i) for i in devices if i - distance in devices]
    return lax.ppermute(block, axis, route)


def tile_offsets(band_total):
    offsets = [0]
    for row_total, col_total in matrix_shapes():
        offsets.append(offsets[-1] + row_total // band_total // BLK * (col_total // BLK))
    return offsets


def whole_tiles(band_total, rep_total):
    return KVH * HD // rep_total % BLK == 0 and FF // band_total // rep_total % BLK == 0


def slice_layout(band_total, rep_total):
    offsets = tile_offsets(band_total)
    layout = []
    for kind, (row_total, col_total) in enumerate(matrix_shapes()):
        rows, cols = row_total // band_total // BLK, col_total // BLK
        grid = offsets[kind] + np.arange(rows * cols).reshape(rows, cols)
        if kind == 6:
            layout.append(grid.reshape(rep_total, rows // rep_total, cols))
        elif kind in (4, 5):
            cut = grid.reshape(rows, band_total, rep_total, -1).transpose(2, 0, 1, 3)
            layout.append(cut.reshape(rep_total, rows, -1))
        else:
            layout.append(grid.reshape(rows, rep_total, -1).transpose(1, 0, 2))
    return layout


def tiles_to_matrix(tiles):
    rows, cols = tiles.shape[:2]
    return tiles.transpose(0, 2, 1, 3).reshape(rows * BLK, cols * BLK)


def matrix_to_tiles(matrix):
    rows, cols = matrix.shape
    cut = matrix.reshape(rows // BLK, BLK, cols // BLK, BLK)
    return cut.transpose(0, 2, 1, 3).reshape(-1, BLK, BLK)


def cut_slices(matrices, band_total, rep_total):
    place = lax.axis_index("rep")
    slices = []
    for kind, matrix in enumerate(matrices):
        rows, cols = matrix.shape
        if kind == 3:
            slices.append(matrix)
        elif kind == 6:
            slices.append(lax.dynamic_slice_in_dim(matrix, place * (rows // rep_total), rows // rep_total, 0))
        elif kind in (4, 5):
            cut = matrix.reshape(rows, band_total, rep_total, -1)
            slices.append(lax.dynamic_index_in_dim(cut, place, 2, False).reshape(rows, -1))
        else:
            slices.append(lax.dynamic_slice_in_dim(matrix, place * (cols // rep_total), cols // rep_total, 1))
    return slices


def join_slices(stacks, band_total, rep_total):
    matrices = []
    for kind, stack in enumerate(stacks):
        rows, cols = stack.shape[1:]
        if kind == 3:
            matrices.append(stack[0])
        elif kind == 6:
            matrices.append(stack.reshape(-1, cols))
        elif kind in (4, 5):
            cut = stack.reshape(rep_total, rows, band_total, -1).transpose(1, 2, 0, 3)
            matrices.append(cut.reshape(rows, -1))
        else:
            matrices.append(stack.transpose(1, 0, 2).reshape(rows, -1))
    return matrices


def gather_kernel(shapes, meta, *refs):
    source_total = len(refs) - len(shapes) - 1
    sources, targets, done = refs[:source_total], refs[source_total:-1], refs[-1]
    start = 0
    for place, (target, (rows, cols)) in enumerate(zip(targets, shapes)):

        def one(tile, carry, target=target, cols=cols, start=start, place=place):
            kind = meta[0, start + tile]
            row = meta[1, start + tile]
            top = pl.multiple_of(tile // cols * BLK, BLK)
            left = pl.multiple_of(tile % cols * BLK, BLK)
            for number, source in enumerate(sources):

                @pl.when(kind == number)
                def _(source=source):
                    pltpu.make_async_copy(
                        source.at[row],
                        target.at[pl.ds(top, BLK), pl.ds(left, BLK)],
                        done.at[place],
                    ).start()

            return carry

        lax.fori_loop(0, rows * cols, one, 0)
        start += rows * cols
    for place, target in enumerate(targets):
        pltpu.make_async_copy(target, target, done.at[place]).wait()


def gather_matrices(sources, meta, shapes):
    anywhere = pl.BlockSpec(memory_space=pl.ANY)
    moved = sum(2 * rows * cols * BLK * BLK * 2 for rows, cols in shapes)
    return pl.pallas_call(
        functools.partial(gather_kernel, shapes),
        out_shape=[jax.ShapeDtypeStruct((rows * BLK, cols * BLK), jnp.bfloat16) for rows, cols in shapes],
        grid_spec=pltpu.PrefetchScalarGridSpec(
            num_scalar_prefetch=1,
            grid=(1,),
            in_specs=[anywhere] * len(sources),
            out_specs=[anywhere] * len(shapes),
            scratch_shapes=[pltpu.SemaphoreType.DMA((len(shapes),))],
        ),
        cost_estimate=pl.CostEstimate(flops=0, bytes_accessed=moved, transcendentals=0),
    )(meta, *sources)


def half_turn(values):
    lane = lax.broadcasted_iota(jnp.int32, values.shape, 1)
    lanes = values.shape[1]
    first = lane % HD < HD // 2
    return first, jnp.where(
        first, pltpu.roll(values, lanes - HD // 2, 1), pltpu.roll(values, HD // 2, 1)
    )


def rope_kernel(q_width, kv_width, x_ref, cos_ref, sin_ref, *outs):
    width = x_ref.shape[-1]
    for start in range(0, width, BLK):
        values = x_ref[0, :, start : start + BLK]
        first, turned = half_turn(values)
        sines = sin_ref[0]
        turned_rows = values * cos_ref[0] + turned * jnp.where(first, -sines, sines)
        if start + BLK > q_width + kv_width:
            column = lax.broadcasted_iota(jnp.int32, values.shape, 1) + start
            turned_rows = jnp.where(column >= q_width + kv_width, values, turned_rows)
        if start < q_width:
            outs[0][0, :, start : start + BLK] = (turned_rows * HD ** (-0.5)).astype(jnp.bfloat16)
        else:
            outs[-1][0, :, start - q_width : start - q_width + BLK] = turned_rows.astype(jnp.bfloat16)


def rope_rows(inner, q_width, kv_width, cosines, sines):
    seqs, rows, width = inner.shape
    shared = cosines.shape[0] == 1
    table = pl.BlockSpec((1, rows, BLK), lambda s: (0 if shared else s, 0, 0))
    widths = [w for w in (q_width, 2 * kv_width) if w]
    return pl.pallas_call(
        functools.partial(rope_kernel, q_width, kv_width),
        out_shape=[jax.ShapeDtypeStruct((seqs, rows, w), jnp.bfloat16) for w in widths],
        grid=(seqs,),
        in_specs=[pl.BlockSpec((1, rows, width), lambda s: (s, 0, 0)), table, table],
        out_specs=[pl.BlockSpec((1, rows, w), lambda s: (s, 0, 0)) for w in widths],
        cost_estimate=pl.CostEstimate(
            flops=6 * inner.size, bytes_accessed=6 * inner.size, transcendentals=0
        ),
    )(inner, cosines, sines)


def fill_bias(band_ref, gpos_ref, bias_ref, rows, window_len):
    band = band_ref[0]

    @pl.when(pl.program_id(0) == 0)
    def _():
        key = lax.broadcasted_iota(jnp.int32, (window_len, rows), 0) + (
            band * rows - (window_len - rows)
        )
        query = lax.broadcasted_iota(jnp.int32, (window_len, rows), 1) + band * rows
        inside = (key > query - WINDOW) & (key <= query) & (key >= 0)
        bias_ref[:window_len] = jnp.where(inside, 0.0, masked_value)

    glob_total = gpos_ref.shape[1]
    query = lax.broadcasted_iota(jnp.int32, (glob_total, rows), 1) + (band * rows - WINDOW)
    spot = jnp.broadcast_to(gpos_ref[0][:, :1], (glob_total, rows))
    bias_ref[window_len:] = jnp.where(spot <= query.astype(jnp.float32), 0.0, masked_value)


def over_last(left, right):
    return lax.dot_general(left, right, (((1,), (1,)), ((), ())), preferred_element_type=jnp.float32)


def over_first(left, right):
    return lax.dot_general(left, right, (((0,), (0,)), ((), ())), preferred_element_type=jnp.float32)


def attend_kernel(block_total, band_ref, gpos_ref, q_ref, *refs):
    blocks, (out_ref, lse_ref, bias_ref) = refs[:block_total], refs[block_total:]
    rows, q_width = q_ref.shape[1:]
    kv_width = blocks[0].shape[2] // 2
    heads, group = q_width // HD, q_width // kv_width
    window_len = rows * (block_total - 1)
    fill_bias(band_ref, gpos_ref, bias_ref, rows, window_len)
    starts = [rows * number for number in range(block_total)]
    pending = []
    for head in range(heads):
        left = head // group * HD
        queries = q_ref[0, :, head * HD : (head + 1) * HD]
        scores = [
            over_last(block[0, :, left : left + HD], queries)
            + bias_ref[start : start + block.shape[1]]
            for block, start in zip(blocks, starts)
        ]
        top = functools.reduce(jnp.maximum, [jnp.max(part, 0, keepdims=True) for part in scores])
        total = 0.0
        mixed = 0.0
        for block, part in zip(blocks, scores):
            weights = jnp.exp(part - top)
            total = total + jnp.sum(weights, 0, keepdims=True)
            mixed = mixed + over_first(
                block[0, :, kv_width + left : kv_width + left + HD], weights.astype(jnp.bfloat16)
            )
        lse_ref[0, head : head + 1, :] = top + jnp.log(total)
        pending.append(mixed / total)
        if len(pending) * HD == BLK or head == heads - 1:
            stop = (head + 1) * HD
            both = jnp.concatenate(pending, 0).T
            out_ref[0, :, stop - both.shape[1] : stop] = both.astype(jnp.bfloat16)
            pending = []


def attend(band, gpos, queries, blocks):
    seqs, rows, q_width = queries.shape
    heads = q_width // HD
    key_total = sum(block.shape[1] for block in blocks)

    def whole(array):
        return pl.BlockSpec((1,) + array.shape[1:], lambda s, *_: (s, 0, 0))

    out_shape = [
        jax.ShapeDtypeStruct((seqs, rows, q_width), jnp.bfloat16),
        jax.ShapeDtypeStruct((seqs, heads, rows), jnp.float32),
    ]
    return pl.pallas_call(
        functools.partial(attend_kernel, len(blocks)),
        out_shape=out_shape,
        grid_spec=pltpu.PrefetchScalarGridSpec(
            num_scalar_prefetch=1,
            grid=(seqs,),
            in_specs=[whole(array) for array in (gpos, queries, *blocks)],
            out_specs=[whole(array) for array in out_shape],
            scratch_shapes=[pltpu.VMEM((key_total, rows), jnp.float32)],
        ),
        compiler_params=pltpu.CompilerParams(vmem_limit_bytes=48 * 2**20),
        cost_estimate=pl.CostEstimate(
            flops=16 * seqs * heads * rows * key_total * HD,
            bytes_accessed=4 * queries.size,
            transcendentals=seqs * heads * rows * key_total,
        ),
    )(band, gpos, queries, *blocks)


def attend_back_kernel(block_total, band_ref, gpos_ref, cos_ref, sin_ref, q_ref, grad_ref, lse_ref, *refs):
    blocks = refs[:block_total]
    dq_ref = refs[block_total]
    out_refs = refs[block_total + 1 : 2 * block_total + 1]
    bias_ref = refs[-1]
    rows, q_width = q_ref.shape[1:]
    kv_width = blocks[0].shape[2] // 2
    heads, group = q_width // HD, q_width // kv_width
    window_len = rows * (block_total - 1)
    fill_bias(band_ref, gpos_ref, bias_ref, rows, window_len)
    starts = [rows * number for number in range(block_total)]
    pending = []
    for kv_head in range(kv_width // HD):
        left = kv_head * HD
        key_sums = [0.0] * block_total
        value_sums = [0.0] * block_total
        for head in range(kv_head * group, (kv_head + 1) * group):
            queries = q_ref[0, :, head * HD : (head + 1) * HD]
            grads = grad_ref[0, :, head * HD : (head + 1) * HD]
            lse = lse_ref[0, head : head + 1, :]
            soft, soft_grads = [], []
            inner = 0.0
            for number, (block, start) in enumerate(zip(blocks, starts)):
                part = over_last(block[0, :, left : left + HD], queries)
                part = jnp.exp(part + bias_ref[start : start + block.shape[1]] - lse)
                slope = over_last(block[0, :, kv_width + left : kv_width + left + HD], grads)
                inner = inner + jnp.sum(part * slope, 0, keepdims=True)
                soft.append(part)
                soft_grads.append(slope)
            turned = 0.0
            for number, block in enumerate(blocks):
                score_grads = (soft[number] * (soft_grads[number] - inner)).astype(jnp.bfloat16)
                value_sums[number] = value_sums[number] + jnp.dot(
                    soft[number].astype(jnp.bfloat16), grads, preferred_element_type=jnp.float32
                )
                key_sums[number] = key_sums[number] + jnp.dot(
                    score_grads, queries, preferred_element_type=jnp.float32
                )
                turned = turned + over_first(block[0, :, left : left + HD], score_grads)
            pending.append(turned)
            if len(pending) * HD == BLK or head == heads - 1:
                stop = (head + 1) * HD
                both = jnp.concatenate(pending, 0).T * HD ** (-0.5)
                pending = []
                first, other = half_turn(both * sin_ref[0])
                both = both * cos_ref[0] + jnp.where(first, other, -other)
                dq_ref[0, :, stop - both.shape[1] : stop] = both.astype(jnp.bfloat16)
        for number, out_ref in enumerate(out_refs):
            out_ref[0, :, left : left + HD] = key_sums[number].astype(out_ref.dtype)
            out_ref[0, :, kv_width + left : kv_width + left + HD] = value_sums[number].astype(
                out_ref.dtype
            )


def attend_back(band, gpos, cosines, sines, queries, grads, lse, blocks):
    seqs, rows, q_width = queries.shape
    heads = q_width // HD
    key_total = sum(block.shape[1] for block in blocks)

    def whole(array):
        return pl.BlockSpec((1,) + array.shape[1:], lambda s, *_: (s, 0, 0))

    table = pl.BlockSpec((1, rows, BLK), lambda s, *_: (0, 0, 0))
    out_shape = [jax.ShapeDtypeStruct(queries.shape, jnp.bfloat16)]
    for number, block in enumerate(blocks):
        own = number == len(blocks) - 2
        out_shape.append(jax.ShapeDtypeStruct(block.shape, jnp.float32 if own else jnp.bfloat16))
    return pl.pallas_call(
        functools.partial(attend_back_kernel, len(blocks)),
        out_shape=out_shape,
        grid_spec=pltpu.PrefetchScalarGridSpec(
            num_scalar_prefetch=1,
            grid=(seqs,),
            in_specs=[whole(gpos), table, table]
            + [whole(array) for array in (queries, grads, lse, *blocks)],
            out_specs=[whole(array) for array in out_shape],
            scratch_shapes=[pltpu.VMEM((key_total, rows), jnp.float32)],
        ),
        compiler_params=pltpu.CompilerParams(vmem_limit_bytes=48 * 2**20),
        cost_estimate=pl.CostEstimate(
            flops=40 * seqs * heads * rows * key_total * HD,
            bytes_accessed=8 * queries.size,
            transcendentals=seqs * heads * rows * key_total,
        ),
    )(band, gpos, cosines, sines, queries, grads, lse, *blocks)


def join_kernel(q_width, kv_width, dq_ref, own_ref, pick_ref, glob_ref, cos_ref, sin_ref, *refs):
    back_refs, out_ref = refs[:-1], refs[-1]
    out_ref[0, :, :q_width] = dq_ref[0]
    picked = lax.dot_general(
        pick_ref[0].astype(jnp.float32),
        glob_ref[0],
        (((0,), (0,)), ((), ())),
        precision=lax.Precision.HIGHEST,
        preferred_element_type=jnp.float32,
    )
    for start in range(0, 2 * kv_width, BLK):
        lanes = slice(start, start + BLK)
        total = own_ref[0, :, lanes] + picked[:, lanes]
        for back_ref in back_refs:
            total = total + back_ref[0, :, lanes].astype(jnp.float32)
        first, other = half_turn(total * sin_ref[0])
        turned = total * cos_ref[0] + jnp.where(first, other, -other)
        column = lax.broadcasted_iota(jnp.int32, total.shape, 1) + start
        turned = jnp.where(column >= kv_width, total, turned)
        out_ref[0, :, q_width + start : q_width + start + BLK] = turned.astype(jnp.bfloat16)


def join_grads(dq, own, picks, globs, cosines, sines, backs):
    seqs, rows, q_width = dq.shape
    kv_width = own.shape[2] // 2

    def whole(array):
        return pl.BlockSpec((1,) + array.shape[1:], lambda s: (s, 0, 0))

    table = pl.BlockSpec((1, rows, BLK), lambda s: (0, 0, 0))
    out_shape = jax.ShapeDtypeStruct((seqs, rows, q_width + 2 * kv_width), jnp.bfloat16)
    return pl.pallas_call(
        functools.partial(join_kernel, q_width, kv_width),
        out_shape=out_shape,
        grid=(seqs,),
        in_specs=[whole(dq), whole(own), whole(picks), whole(globs), table, table]
        + [whole(back) for back in backs],
        out_specs=whole(out_shape),
        cost_estimate=pl.CostEstimate(
            flops=20 * own.size, bytes_accessed=4 * dq.size + 12 * own.size, transcendentals=0
        ),
    )(dq, own, picks, globs, cosines, sines, *backs)


def adam_kernel(batch, meta, rates, *refs):
    master_ref, first_ref, second_ref, left_ref, right_ref = refs[:5]
    sources = refs[5:-6]
    new_first_ref, new_second_ref, new_master_ref, copy_ref, tiles, arrived = refs[-6:]
    step, steps = pl.program_id(0), pl.num_programs(0)
    slot = step % 2

    def fetch(at_step, at_slot):
        for place in range(batch):
            tile = at_step * batch + place
            for number, source in enumerate(sources):

                @pl.when(meta[0, tile] == number)
                def _(source=source, tile=tile, place=place):
                    top = pl.multiple_of(meta[2, tile], BLK)
                    left = pl.multiple_of(meta[3, tile], BLK)
                    pltpu.make_async_copy(
                        source.at[meta[1, tile], pl.ds(top, BLK), pl.ds(left, BLK)],
                        tiles.at[at_slot, place],
                        arrived.at[at_slot],
                    ).start()

    @pl.when(step == 0)
    def _():
        fetch(0, 0)

    @pl.when(step + 1 < steps)
    def _():
        fetch(step + 1, 1 - slot)

    pltpu.make_async_copy(tiles.at[slot], tiles.at[slot], arrived.at[slot]).wait()
    for place in range(batch):
        left = left_ref[place].astype(jnp.bfloat16)
        right = right_ref[place].astype(jnp.bfloat16)
        rotated = over_first(left, tiles[slot, place])
        rotated = jnp.dot(rotated.astype(jnp.bfloat16), right, preferred_element_type=jnp.float32)
        new_first = beta_one * first_ref[place] + (1.0 - beta_one) * rotated
        new_second = beta_two * second_ref[place] + (1.0 - beta_two) * rotated * rotated
        direction = (
            new_first
            / (1.0 - beta_one**STEP)
            / (jnp.sqrt(new_second / (1.0 - beta_two**STEP)) + adam_eps)
        )
        update = jnp.dot(left, direction.astype(jnp.bfloat16), preferred_element_type=jnp.float32)
        update = over_last(update.astype(jnp.bfloat16), right)
        old = master_ref[place]
        new_master = old - rates[step * batch + place] * (update + weight_decay * old)
        new_first_ref[place] = new_first
        new_second_ref[place] = new_second
        new_master_ref[place] = new_master
        copy_ref[place] = new_master.astype(jnp.bfloat16)


def adam(meta, rates, state, sources):
    count = state[0].shape[0]
    batch = max(size for size in (1, 2, 4) if count % size == 0)
    block = pl.BlockSpec((batch, BLK, BLK), lambda s, *_: (s, 0, 0))
    anywhere = pl.BlockSpec(memory_space=pl.ANY)
    shape = (count, BLK, BLK)
    return pl.pallas_call(
        functools.partial(adam_kernel, batch),
        out_shape=[jax.ShapeDtypeStruct(shape, jnp.float32)] * 3
        + [jax.ShapeDtypeStruct(shape, jnp.bfloat16)],
        grid_spec=pltpu.PrefetchScalarGridSpec(
            num_scalar_prefetch=2,
            grid=(count // batch,),
            in_specs=[block] * 5 + [anywhere] * len(sources),
            out_specs=[block] * 4,
            scratch_shapes=[
                pltpu.VMEM((2, batch, BLK, BLK), jnp.bfloat16),
                pltpu.SemaphoreType.DMA((2,)),
            ],
        ),
        compiler_params=pltpu.CompilerParams(vmem_limit_bytes=32 * 2**20),
        cost_estimate=pl.CostEstimate(
            flops=8 * count * BLK**3, bytes_accessed=36 * count * BLK**2, transcendentals=0
        ),
    )(meta, rates, *state, *sources)


def per_device(
    block_input,
    cotangent,
    glob_select,
    assignment,
    master,
    first_moment,
    second_moment,
    left_basis,
    right_basis,
    gains,
    gain_first,
    gain_second,
):
    band_total = lax.axis_size("fsdp")
    rep_total = lax.axis_size("rep")
    place = lax.axis_index("rep")
    band = lax.axis_index("fsdp")
    heads = H // rep_total
    kv_heads = KVH // rep_total
    q_width = heads * HD
    kv_width = kv_heads * HD
    tok_count = block_input.shape[1]
    own_count = master.shape[1]
    tile_total = own_count * rep_total
    aligned = square() and whole_tiles(band_total, rep_total)
    tile_order = assignment[0]

    owned_copy = master[0].astype(jnp.bfloat16)
    if aligned:
        slots = square_pieces(owned_copy)

    residual = block_input[0].astype(jnp.float32)
    grad_top = cotangent[0]
    position = band * tok_count + jnp.arange(tok_count, dtype=jnp.int32)
    cosine_table, sine_table = rope_tables(position)
    scale_one = lax.rsqrt(jnp.mean(residual * residual, -1, keepdims=True) + norm_eps)
    normed_one = (residual * scale_one * gains[0]).astype(jnp.bfloat16)
    normed_one_all = rep_gather(normed_one).reshape(-1, D)
    pick_rows = glob_select[0]
    selector = pick_rows.astype(jnp.bfloat16)
    glob_pos_part = jnp.sum(pick_rows * position[None, :], 1)
    digits = jnp.stack([glob_pos_part // 256, glob_pos_part % 256], 1).astype(jnp.bfloat16)
    digits = jnp.pad(digits, ((0, 0), (0, BLK - 2)))
    glob_part = jnp.concatenate(
        [jnp.dot(selector, normed_one, preferred_element_type=jnp.float32).astype(jnp.bfloat16), digits], 1
    )
    glob_rows_all = rep_gather(add_all(glob_part, "fsdp").astype(jnp.bfloat16))
    selector_all = rep_gather(selector)
    glob_normed = glob_rows_all[..., :D].reshape(-1, D)
    glob_digits = glob_rows_all[..., D : D + 2].astype(jnp.float32)
    glob_place = glob_digits[..., 0] * 256.0 + glob_digits[..., 1]
    glob_total = glob_place.shape[1]
    grad_top_all = rep_gather(grad_top).reshape(-1, D)

    if aligned:
        layout = slice_layout(band_total, rep_total)
        grids = []
        for kind, grid in enumerate(layout):
            if kind == 3:
                grids.append(jnp.asarray(grid.transpose(1, 0, 2).reshape(grid.shape[1], -1)))
            else:
                grids.append(lax.dynamic_index_in_dim(jnp.asarray(grid), place, 0, False))
        grids = [jnp.concatenate(grids[:3], 1)] + grids[3:]
        wanted_slots = jnp.take(
            tile_order, jnp.concatenate([grid.reshape(-1) for grid in grids]), mode="clip"
        )
        entry, row = (wanted_slots // own_count) ^ place, wanted_slots % own_count
        cut = own_count // 2
        high = (entry == 3) & (row >= cut)
        meta = jnp.stack([jnp.where(high, 4, entry), jnp.where(high, row - cut, row)], 0)
        inner_part, output_part, gate_part, up_part, down_part = gather_matrices(
            slots, meta.astype(jnp.int32), [grid.shape for grid in grids]
        )
    else:
        slots = lax.all_gather(owned_copy, "rep", axis=0, tiled=True)
        tiles = jnp.take(slots, tile_order, axis=0, mode="clip")
        slices = cut_slices(band_matrices(tiles, band_total), band_total, rep_total)
        inner_part = jnp.concatenate(slices[0:3], 1)
        output_part, gate_part, up_part, down_part = slices[3:]

    def over_bands(slice_rows):
        return lax.all_gather(slice_rows, "fsdp", axis=0, tiled=True)

    w_inner = over_bands(inner_part)
    per_rep = band_total // rep_total
    lanes = (jnp.arange(per_rep) + place * per_rep == band)[:, None, None]
    w_output = lax.psum(jnp.where(lanes, output_part[None], 0), "fsdp").reshape(q_width, D)
    w_gate = over_bands(gate_part)
    w_up = over_bands(up_part)
    w_down = over_bands(down_part)

    def mul(rows, weight):
        return jnp.dot(rows, weight, preferred_element_type=jnp.float32)

    def mul_back(rows, weight):
        return lax.dot_general(rows, weight, (((1,), (1,)), ((), ())), preferred_element_type=jnp.float32)

    def weight_grad(rows, grad_rows):
        return lax.dot_general(
            rows, grad_rows, (((0,), (0,)), ((), ())), preferred_element_type=jnp.float32
        ).astype(jnp.bfloat16)

    def own_sum(partial):
        return rep_scatter(partial.astype(jnp.bfloat16).reshape(rep_total, tok_count, D))

    inner_rows = mul(normed_one_all, w_inner).reshape(rep_total, tok_count, -1)
    wide_cosine = jnp.concatenate([cosine_table, cosine_table], 1)[None]
    wide_sine = jnp.concatenate([sine_table, sine_table], 1)[None]
    queries, own_pairs = rope_rows(inner_rows, q_width, kv_width, wide_cosine, wide_sine)
    glob_inner = mul(glob_normed, w_inner[:, q_width:]).reshape(rep_total, glob_total, -1)
    glob_cosine, glob_sine = rope_tables(glob_place.reshape(-1))
    glob_cosine = jnp.concatenate([glob_cosine, glob_cosine], 1).reshape(rep_total, glob_total, -1)
    glob_sine = jnp.concatenate([glob_sine, glob_sine], 1).reshape(rep_total, glob_total, -1)
    (glob_pairs,) = rope_rows(glob_inner, 0, kv_width, glob_cosine, glob_sine)
    back_count = (WINDOW + tok_count - 2) // tok_count
    pair_blocks = [shifted(own_pairs, "fsdp", distance) for distance in range(back_count, 0, -1)]
    pair_blocks = pair_blocks + [own_pairs, glob_pairs]
    glob_spots = jnp.broadcast_to(glob_place[:, :, None], (rep_total, glob_total, BLK))
    band_number = band.astype(jnp.int32).reshape(1)
    attended_low, lse = attend(band_number, glob_spots, queries, pair_blocks)
    attended_low = attended_low.reshape(-1, q_width)
    middle = residual + own_sum(mul(attended_low, w_output))
    scale_two = lax.rsqrt(jnp.mean(middle * middle, -1, keepdims=True) + norm_eps)
    normed_two = (middle * scale_two * gains[1]).astype(jnp.bfloat16)
    normed_two_all = rep_gather(normed_two).reshape(-1, D)

    gate_rows = mul(normed_two_all, w_gate)
    up_rows = mul(normed_two_all, w_up)
    sigmoid_gate = jax.nn.sigmoid(gate_rows)
    silu_gate = gate_rows * sigmoid_gate
    activation = (silu_gate * up_rows).astype(jnp.bfloat16)
    g_down = weight_grad(activation, grad_top_all)
    grad_top_all, g_down = lax.optimization_barrier((grad_top_all, g_down))
    grad_act = mul_back(grad_top_all, w_down)
    grad_gate = (
        grad_act * up_rows * sigmoid_gate * (1.0 + gate_rows * (1.0 - sigmoid_gate))
    ).astype(jnp.bfloat16)
    grad_up = (grad_act * silu_gate).astype(jnp.bfloat16)
    grad_normed_two = own_sum(mul_back(grad_gate, w_gate) + mul_back(grad_up, w_up))
    g_gate = weight_grad(normed_two_all, grad_gate)
    g_up = weight_grad(normed_two_all, grad_up)
    grad_normed_two, g_gate, g_up = lax.optimization_barrier((grad_normed_two, g_gate, g_up))
    block_out = middle + own_sum(mul(activation, w_down))

    def over_tokens(partial):
        return lax.psum_scatter(partial, "fsdp", scatter_dimension=0, tiled=True)

    s_down = over_tokens(g_down)
    s_gate = over_tokens(g_gate)
    s_up = over_tokens(g_up)

    grad_middle = grad_top.astype(jnp.float32) + norm_back(middle, scale_two, gains[1], grad_normed_two)
    grad_branch_all = rep_gather(grad_middle.astype(jnp.bfloat16)).reshape(-1, D)
    grad_attended = mul_back(grad_branch_all, w_output).astype(jnp.bfloat16)
    g_output = lax.psum(weight_grad(attended_low, grad_branch_all), "fsdp")
    grad_attended = grad_attended.reshape(rep_total, tok_count, q_width)
    grad_queries, *grad_blocks = attend_back(
        band_number, glob_spots, wide_cosine, wide_sine, queries, grad_attended, lse, pair_blocks
    )
    returned = [
        shifted(grad_blocks[back_count - distance], "fsdp", -distance)
        for distance in range(1, back_count + 1)
    ]
    glob_grads = add_all(grad_blocks[-1], "fsdp")
    grad_inner = join_grads(
        grad_queries, grad_blocks[-2], selector_all, glob_grads, wide_cosine, wide_sine, returned
    ).reshape(-1, q_width + 2 * kv_width)
    s_inner = over_tokens(weight_grad(normed_one_all, grad_inner))
    grad_normed_one = own_sum(mul_back(grad_inner, w_inner))
    grad_input = grad_middle + norm_back(residual, scale_one, gains[0], grad_normed_one)

    source = band // per_rep
    mine = lax.dynamic_index_in_dim(g_output.reshape(per_rep, D // band_total, D), band % per_rep, 0, False)
    out_entry = source ^ place if square() else source
    out_band = lax.dynamic_index_in_dim(rep_gather(mine), out_entry, 0, False)
    slot_ids = jnp.arange(tile_total, dtype=jnp.int32)
    inverse = jnp.sum(jnp.where(tile_order[None, :] == slot_ids[:, None], slot_ids[None, :], 0), 1)
    own_slots = place * own_count + jnp.arange(own_count, dtype=jnp.int32)
    owned_tiles = jnp.take(inverse, own_slots, mode="clip")
    if aligned:
        sources = [rep_gather(s_inner), out_band[None], rep_gather(s_gate), rep_gather(s_up), rep_gather(s_down)]
        where = np.zeros((4, rep_total, tile_total), np.int32)
        for kind, grid in enumerate(layout):
            first_col = (0, q_width, q_width + kv_width)[kind] if kind < 3 else 0
            for there in range(rep_total):
                rows, cols = grid.shape[1:]
                numbers = grid[there].reshape(-1)
                at = np.arange(rows * cols)
                left = at % cols * BLK + first_col + (there * cols * BLK if kind == 3 else 0)
                where[0, :, numbers] = max(kind - 2, 0)
                where[2, :, numbers] = (at // cols * BLK)[:, None]
                where[3, :, numbers] = left[:, None]
                for here in range(rep_total):
                    where[1, here, numbers] = 0 if kind == 3 else here ^ there
        tile_spots = lax.dynamic_index_in_dim(jnp.asarray(where), place, 1, False)
        meta = jnp.take(tile_spots, owned_tiles, axis=1, mode="clip")
    else:
        stacks = [
            None if piece is None else lax.all_gather(piece, "rep", axis=0)
            for piece in (
                s_inner[:, :q_width],
                s_inner[:, q_width : q_width + kv_width],
                s_inner[:, q_width + kv_width :],
                None,
                s_gate,
                s_up,
                s_down,
            )
        ]
        stacks[3] = out_band[None]
        sources = [band_tiles(join_slices(stacks, band_total, rep_total))]
        meta = jnp.stack([0 * owned_tiles, owned_tiles, 0 * owned_tiles, 0 * owned_tiles], 0)
    slot_rates = jnp.take(kind_rates(band_total), owned_tiles, mode="clip")
    new_first, new_second, new_master, master_copy = adam(
        meta,
        slot_rates,
        (master[0], first_moment[0], second_moment[0], left_basis[0], right_basis[0]),
        sources,
    )
    gain_terms = jnp.stack(
        [
            jnp.sum(grad_normed_one * residual * scale_one, 0),
            jnp.sum(grad_normed_two * middle * scale_two, 0),
        ]
    )
    square_terms = jnp.stack(
        [jnp.sum(residual * residual), jnp.sum(middle * middle), jnp.sum(block_out * block_out)]
    )
    sums = jnp.concatenate([gain_terms.reshape(-1), square_terms])
    sums = add_all(add_all(sums, "rep"), "fsdp")
    gain_grad, square_total = sums[: 2 * D].reshape(2, D), sums[2 * D :]
    new_gain_first = beta_one * gain_first + (1.0 - beta_one) * gain_grad
    new_gain_second = beta_two * gain_second + (1.0 - beta_two) * gain_grad * gain_grad
    gain_step = (
        new_gain_first
        / (1.0 - beta_one**STEP)
        / (jnp.sqrt(new_gain_second / (1.0 - beta_two**STEP)) + adam_eps)
    )
    new_gains = gains - gain_rate * gain_step
    rms_stats = jnp.sqrt(square_total / (rep_total * band_total * tok_count * D))
    return (
        block_out[None],
        grad_input[None],
        new_first[None],
        new_second[None],
        new_master[None],
        master_copy[None],
        new_gain_first,
        new_gain_second,
        new_gains,
        rms_stats,
    )


def solution(mesh):
    in_specs = (
        P("rep", "fsdp", None),
        P("rep", "fsdp", None),
        P("rep", None, "fsdp"),
        P("fsdp", None),
        P("fsdp", "rep", None, None),
        P("fsdp", "rep", None, None),
        P("fsdp", "rep", None, None),
        P("fsdp", "rep", None, None),
        P("fsdp", "rep", None, None),
        P(),
        P(),
        P(),
    )
    out_specs = (
        P("rep", "fsdp", None),
        P("rep", "fsdp", None),
        P("fsdp", "rep", None, None),
        P("fsdp", "rep", None, None),
        P("fsdp", "rep", None, None),
        P("fsdp", "rep", None, None),
        P(),
        P(),
        P(),
        P(),
    )
    return jax.shard_map(
        per_device, mesh=mesh, in_specs=in_specs, out_specs=out_specs, check_vma=False
    )
```

```python
import functools

import jax
import jax.numpy as jnp
import numpy as np
from jax import lax
from jax.experimental import pallas as pl
from jax.experimental.pallas import tpu as pltpu
from jax.sharding import PartitionSpec as P

D = 2048
H = 32
KVH = 8
HD = 64
FF = 8192
WINDOW = 512
BLK = 128
STEP = 10


norm_eps = 1e-05
rope_theta = 500000.0
beta_one = 0.5
beta_two = 0.5
adam_eps = 1e-08
weight_decay = 0.1
gain_rate = 0.5
masked_value = -1e30


def matrix_shapes():
    kv_width = KVH * HD
    return [(D, D), (D, kv_width), (D, kv_width), (D, D), (D, FF), (D, FF), (FF, D)]


def kind_rates(band_total):
    rate_list = [
        D ** (-0.5),
        D ** (-0.5),
        D ** (-0.5),
        (D * 8 // WINDOW) ** (-0.5),
        D ** (-0.5),
        D ** (-0.5),
        FF ** (-0.5),
    ]
    pieces = []
    for (row_total, col_total), rate_value in zip(matrix_shapes(), rate_list):
        tile_count = row_total // band_total // BLK * (col_total // BLK)
        pieces.append(jnp.full((tile_count,), rate_value, jnp.float32))
    return jnp.concatenate(pieces)


def band_matrices(tiles, band_total):
    matrices = []
    offset = 0
    for row_total, col_total in matrix_shapes():
        band_rows = row_total // band_total
        tile_count = band_rows // BLK * (col_total // BLK)
        segment = tiles[offset : offset + tile_count].reshape(
            band_rows // BLK, col_total // BLK, BLK, BLK
        )
        matrices.append(segment.transpose(0, 2, 1, 3).reshape(band_rows, col_total))
        offset += tile_count
    return matrices


def band_tiles(matrices):
    pieces = []
    for matrix in matrices:
        row_count, col_count = matrix.shape
        segment = matrix.reshape(row_count // BLK, BLK, col_count // BLK, BLK).transpose(0, 2, 1, 3)
        pieces.append(segment.reshape(-1, BLK, BLK))
    return jnp.concatenate(pieces, 0)


def rope_tables(position):
    halves = jnp.arange(HD // 2, dtype=jnp.float32) * (2.0 / HD)
    frequency = rope_theta ** (-halves)
    angles = position.astype(jnp.float32)[:, None] * frequency[None, :]
    angles = jnp.concatenate([angles, angles], 1)
    return (jnp.cos(angles), jnp.sin(angles))


def rotate(vectors, cosine_table, sine_table):
    half_width = vectors.shape[-1] // 2
    turned = jnp.concatenate([-vectors[..., half_width:], vectors[..., :half_width]], -1)
    return vectors * cosine_table[:, None, :] + turned * sine_table[:, None, :]


def rotate_back(grad_rows, cosine_table, sine_table):
    half_width = grad_rows.shape[-1] // 2
    scaled = grad_rows * sine_table[:, None, :]
    turned = jnp.concatenate([scaled[..., half_width:], -scaled[..., :half_width]], -1)
    return grad_rows * cosine_table[:, None, :] + turned


def norm_back(values, row_scale, gain_row, grad_rows):
    weighted = grad_rows * gain_row
    return row_scale * weighted - values * row_scale**3 * jnp.mean(
        weighted * values, -1, keepdims=True
    )


def to_rep(block, distance):
    route = [(i, i ^ distance) for i in range(lax.axis_size("rep"))]
    return lax.ppermute(block, "rep", route)


def square():
    return lax.axis_size("rep") == 4


def square_pieces(block):
    cut = block.shape[0] // 2
    near = to_rep(block, 1)
    far = to_rep(block, 2)
    return block, near, far, to_rep(near[:cut], 2), to_rep(far[cut:], 1)


def rep_gather(block):
    if not square():
        return lax.all_gather(block, "rep", axis=0)
    own, near, far, low, high = square_pieces(block)
    return jnp.concatenate([own, near, far, low, high], 0).reshape((4,) + block.shape)


def rep_of(entry):
    place = lax.axis_index("rep")
    return place ^ entry if square() else entry


def rep_scatter(parts):
    if not square():
        flat = parts.reshape(-1, parts.shape[-1])
        return lax.psum_scatter(flat, "rep", scatter_dimension=0, tiled=True).astype(jnp.float32)
    half = parts.shape[-1] // 2
    totals = []
    for side, (first, second) in ((parts[..., :half], (1, 2)), (parts[..., half:], (2, 1))):
        away = to_rep(jnp.stack([side[first], side[3]], 0), first)
        other = (side[second].astype(jnp.float32) + away[1].astype(jnp.float32)).astype(parts.dtype)
        own = side[0].astype(jnp.float32) + away[0].astype(jnp.float32)
        totals.append(own + to_rep(other, second).astype(jnp.float32))
    return jnp.concatenate(totals, -1)


def add_all(value, axis):
    total = value.astype(jnp.float32)
    distance = 1
    while distance < lax.axis_size(axis):
        route = [(i, i ^ distance) for i in range(lax.axis_size(axis))]
        total = total + lax.ppermute(total.astype(value.dtype), axis, route).astype(jnp.float32)
        distance *= 2
    return total


def line_route(distance, step):
    chips = lax.axis_size("fsdp") // 2
    width = 2 * chips
    route = []
    for rep in range(lax.axis_size("rep")):
        start, stop = rep + distance, rep + distance + step
        if 0 <= start < chips and 0 <= stop < chips:
            route += [(rep * width + 2 * start + core, rep * width + 2 * stop + core) for core in range(2)]
    return route


def along_line(block, distance, step):
    return lax.ppermute(block, ("rep", "fsdp"), line_route(distance, step))


def to_core(block):
    return lax.ppermute(block, "fsdp", [(i, i ^ 1) for i in range(lax.axis_size("fsdp"))])


def line_case():
    return lax.axis_size("fsdp") == 2 * lax.axis_size("rep") == 8


def spread_output(part):
    per_rep = lax.axis_size("fsdp") // lax.axis_size("rep")
    band = lax.axis_index("fsdp")
    lanes = (jnp.arange(per_rep) + lax.axis_index("rep") * per_rep == band)[:, None, None]
    if not line_case():
        return lax.psum(jnp.where(lanes, part[None], 0), "fsdp").reshape(-1, D)
    total = jnp.where(jnp.any(lanes), part, 0)
    up = down = part
    for distance in range(lax.axis_size("rep") - 1):
        up = along_line(up, distance, 1)
        down = along_line(down, -distance, -1)
        total = total + up + down
    other = to_core(total)
    first = band % 2 == 0
    return jnp.concatenate([jnp.where(first, total, other), jnp.where(first, other, total)], 0)


def collect_output(partial):
    per_rep = lax.axis_size("fsdp") // lax.axis_size("rep")
    spot = lax.axis_index("fsdp") % per_rep
    parts = partial.reshape(per_rep, -1, D)
    if not line_case():
        return lax.dynamic_index_in_dim(lax.psum(parts, "fsdp"), spot, 0, False)
    mine = lax.dynamic_index_in_dim(parts, spot, 0, False)
    other = lax.dynamic_index_in_dim(parts, 1 - spot, 0, False)
    total = mine.astype(jnp.float32) + to_core(other).astype(jnp.float32)
    for distance in range(lax.axis_size("rep") - 1, 0, -1):
        low = total.astype(jnp.bfloat16)
        total = total + along_line(low, distance, -1).astype(jnp.float32)
        total = total + along_line(low, -distance, 1).astype(jnp.float32)
    return total.astype(jnp.bfloat16)


def shifted(block, axis, distance):
    devices = range(lax.axis_size(axis))
    route = [(i - distance, i) for i in devices if i - distance in devices]
    return lax.ppermute(block, axis, route)


def tile_offsets(band_total):
    offsets = [0]
    for row_total, col_total in matrix_shapes():
        offsets.append(offsets[-1] + row_total // band_total // BLK * (col_total // BLK))
    return offsets


def whole_tiles(band_total, rep_total):
    return KVH * HD // rep_total % BLK == 0 and FF // band_total // rep_total % BLK == 0


def slice_layout(band_total, rep_total):
    offsets = tile_offsets(band_total)
    layout = []
    for kind, (row_total, col_total) in enumerate(matrix_shapes()):
        rows, cols = row_total // band_total // BLK, col_total // BLK
        grid = offsets[kind] + np.arange(rows * cols).reshape(rows, cols)
        if kind == 6:
            layout.append(grid.reshape(rep_total, rows // rep_total, cols))
        elif kind in (4, 5):
            cut = grid.reshape(rows, band_total, rep_total, -1).transpose(2, 0, 1, 3)
            layout.append(cut.reshape(rep_total, rows, -1))
        else:
            layout.append(grid.reshape(rows, rep_total, -1).transpose(1, 0, 2))
    return layout


def tiles_to_matrix(tiles):
    rows, cols = tiles.shape[:2]
    return tiles.transpose(0, 2, 1, 3).reshape(rows * BLK, cols * BLK)


def matrix_to_tiles(matrix):
    rows, cols = matrix.shape
    cut = matrix.reshape(rows // BLK, BLK, cols // BLK, BLK)
    return cut.transpose(0, 2, 1, 3).reshape(-1, BLK, BLK)


def cut_slices(matrices, band_total, rep_total):
    place = lax.axis_index("rep")
    slices = []
    for kind, matrix in enumerate(matrices):
        rows, cols = matrix.shape
        if kind == 3:
            slices.append(matrix)
        elif kind == 6:
            slices.append(lax.dynamic_slice_in_dim(matrix, place * (rows // rep_total), rows // rep_total, 0))
        elif kind in (4, 5):
            cut = matrix.reshape(rows, band_total, rep_total, -1)
            slices.append(lax.dynamic_index_in_dim(cut, place, 2, False).reshape(rows, -1))
        else:
            slices.append(lax.dynamic_slice_in_dim(matrix, place * (cols // rep_total), cols // rep_total, 1))
    return slices


def join_slices(stacks, band_total, rep_total):
    matrices = []
    for kind, stack in enumerate(stacks):
        rows, cols = stack.shape[1:]
        if kind == 3:
            matrices.append(stack[0])
        elif kind == 6:
            matrices.append(stack.reshape(-1, cols))
        elif kind in (4, 5):
            cut = stack.reshape(rep_total, rows, band_total, -1).transpose(1, 2, 0, 3)
            matrices.append(cut.reshape(rows, -1))
        else:
            matrices.append(stack.transpose(1, 0, 2).reshape(rows, -1))
    return matrices


def gather_kernel(plans, meta, *refs):
    source_total = len(refs) - len(plans) - 1
    sources, targets, done = refs[:source_total], refs[source_total:-1], refs[-1]
    piece_total = source_total // max(len(parts) for _, _, parts in plans)
    start = 0
    for place, (target, (rows, cols, parts)) in enumerate(zip(targets, plans)):
        height = sources[0].shape[1]

        def one(tile, carry, target=target, cols=cols, parts=parts, start=start, place=place, height=height):
            kind = meta[0, start + tile]
            row = meta[1, start + tile]
            top = tile // cols * (height * len(parts))
            left = pl.multiple_of(tile % cols * BLK, BLK)
            for number in range(piece_total):

                @pl.when(kind == number)
                def _(number=number):
                    for order, part in enumerate(parts):
                        first = pl.multiple_of(top + order * height, height)
                        pltpu.make_async_copy(
                            sources[part * piece_total + number].at[row],
                            target.at[pl.ds(first, height), pl.ds(left, BLK)],
                            done.at[place],
                        ).start()

            return carry

        lax.fori_loop(0, rows * cols, one, 0)
        start += rows * cols
    for place, target in enumerate(targets):
        pltpu.make_async_copy(target, target, done.at[place]).wait()


def gather_matrices(sources, meta, plans):
    anywhere = pl.BlockSpec(memory_space=pl.ANY)
    height = sources[0].shape[1]
    out_shape = [
        jax.ShapeDtypeStruct((rows * height * len(parts), cols * BLK), jnp.bfloat16)
        for rows, cols, parts in plans
    ]
    moved = sum(4 * shape.size for shape in out_shape)
    return pl.pallas_call(
        functools.partial(gather_kernel, plans),
        out_shape=out_shape,
        grid_spec=pltpu.PrefetchScalarGridSpec(
            num_scalar_prefetch=1,
            grid=(1,),
            in_specs=[anywhere] * len(sources),
            out_specs=[pl.BlockSpec(shape.shape, lambda i, *_: (0, 0)) for shape in out_shape],
            scratch_shapes=[pltpu.SemaphoreType.DMA((len(plans),))],
        ),
        compiler_params=pltpu.CompilerParams(vmem_limit_bytes=32 * 2**20),
        cost_estimate=pl.CostEstimate(flops=0, bytes_accessed=moved, transcendentals=0),
    )(meta, *sources)


def half_turn(values):
    lane = lax.broadcasted_iota(jnp.int32, values.shape, 1)
    lanes = values.shape[1]
    first = lane % HD < HD // 2
    return first, jnp.where(
        first, pltpu.roll(values, lanes - HD // 2, 1), pltpu.roll(values, HD // 2, 1)
    )


def rope_kernel(q_width, kv_width, x_ref, cos_ref, sin_ref, *outs):
    width = x_ref.shape[-1]
    for start in range(0, width, BLK):
        values = x_ref[0, :, start : start + BLK]
        first, turned = half_turn(values)
        sines = sin_ref[0]
        turned_rows = values * cos_ref[0] + turned * jnp.where(first, -sines, sines)
        if start + BLK > q_width + kv_width:
            column = lax.broadcasted_iota(jnp.int32, values.shape, 1) + start
            turned_rows = jnp.where(column >= q_width + kv_width, values, turned_rows)
        if start < q_width:
            outs[0][0, :, start : start + BLK] = (turned_rows * HD ** (-0.5)).astype(jnp.bfloat16)
        else:
            outs[-1][0, :, start - q_width : start - q_width + BLK] = turned_rows.astype(jnp.bfloat16)


def rope_rows(inner, q_width, kv_width, cosines, sines):
    seqs, rows, width = inner.shape
    shared = cosines.shape[0] == 1
    table = pl.BlockSpec((1, rows, BLK), lambda s: (0 if shared else s, 0, 0))
    widths = [w for w in (q_width, 2 * kv_width) if w]
    return pl.pallas_call(
        functools.partial(rope_kernel, q_width, kv_width),
        out_shape=[jax.ShapeDtypeStruct((seqs, rows, w), jnp.bfloat16) for w in widths],
        grid=(seqs,),
        in_specs=[pl.BlockSpec((1, rows, width), lambda s: (s, 0, 0)), table, table],
        out_specs=[pl.BlockSpec((1, rows, w), lambda s: (s, 0, 0)) for w in widths],
        cost_estimate=pl.CostEstimate(
            flops=6 * inner.size, bytes_accessed=6 * inner.size, transcendentals=0
        ),
    )(inner, cosines, sines)


def fill_bias(band_ref, gpos_ref, bias_ref, rows, window_len):
    band = band_ref[0]

    @pl.when(pl.program_id(0) == 0)
    def _():
        key = lax.broadcasted_iota(jnp.int32, (window_len, rows), 0) + (
            band * rows - (window_len - rows)
        )
        query = lax.broadcasted_iota(jnp.int32, (window_len, rows), 1) + band * rows
        inside = (key > query - WINDOW) & (key <= query) & (key >= 0)
        bias_ref[:window_len] = jnp.where(inside, 0.0, masked_value)

    glob_total = gpos_ref.shape[1]
    query = lax.broadcasted_iota(jnp.int32, (glob_total, rows), 1) + (band * rows - WINDOW)
    spot = jnp.broadcast_to(gpos_ref[0][:, :1], (glob_total, rows))
    bias_ref[window_len:] = jnp.where(spot <= query.astype(jnp.float32), 0.0, masked_value)


def over_last(left, right):
    return lax.dot_general(left, right, (((1,), (1,)), ((), ())), preferred_element_type=jnp.float32)


def over_first(left, right):
    return lax.dot_general(left, right, (((0,), (0,)), ((), ())), preferred_element_type=jnp.float32)


def attend_kernel(block_total, band_ref, gpos_ref, q_ref, *refs):
    blocks, (out_ref, lse_ref, bias_ref) = refs[:block_total], refs[block_total:]
    rows, q_width = q_ref.shape[1:]
    kv_width = blocks[0].shape[2] // 2
    heads, group = q_width // HD, q_width // kv_width
    window_len = rows * (block_total - 1)
    fill_bias(band_ref, gpos_ref, bias_ref, rows, window_len)
    starts = [rows * number for number in range(block_total)]
    pending = []
    for head in range(heads):
        left = head // group * HD
        queries = q_ref[0, :, head * HD : (head + 1) * HD]
        scores = [
            over_last(block[0, :, left : left + HD], queries)
            + bias_ref[start : start + block.shape[1]]
            for block, start in zip(blocks, starts)
        ]
        top = functools.reduce(jnp.maximum, [jnp.max(part, 0, keepdims=True) for part in scores])
        total = 0.0
        mixed = 0.0
        for block, part in zip(blocks, scores):
            weights = jnp.exp(part - top)
            total = total + jnp.sum(weights, 0, keepdims=True)
            mixed = mixed + over_first(
                block[0, :, kv_width + left : kv_width + left + HD], weights.astype(jnp.bfloat16)
            )
        lse_ref[0, head : head + 1, :] = top + jnp.log(total)
        pending.append(mixed / total)
        if len(pending) * HD == BLK or head == heads - 1:
            stop = (head + 1) * HD
            both = jnp.concatenate(pending, 0).T
            out_ref[0, :, stop - both.shape[1] : stop] = both.astype(jnp.bfloat16)
            pending = []


def attend(band, gpos, queries, blocks):
    seqs, rows, q_width = queries.shape
    heads = q_width // HD
    key_total = sum(block.shape[1] for block in blocks)

    def whole(array):
        return pl.BlockSpec((1,) + array.shape[1:], lambda s, *_: (s, 0, 0))

    out_shape = [
        jax.ShapeDtypeStruct((seqs, rows, q_width), jnp.bfloat16),
        jax.ShapeDtypeStruct((seqs, heads, rows), jnp.float32),
    ]
    return pl.pallas_call(
        functools.partial(attend_kernel, len(blocks)),
        out_shape=out_shape,
        grid_spec=pltpu.PrefetchScalarGridSpec(
            num_scalar_prefetch=1,
            grid=(seqs,),
            in_specs=[whole(array) for array in (gpos, queries, *blocks)],
            out_specs=[whole(array) for array in out_shape],
            scratch_shapes=[pltpu.VMEM((key_total, rows), jnp.float32)],
        ),
        compiler_params=pltpu.CompilerParams(vmem_limit_bytes=48 * 2**20),
        cost_estimate=pl.CostEstimate(
            flops=16 * seqs * heads * rows * key_total * HD,
            bytes_accessed=4 * queries.size,
            transcendentals=seqs * heads * rows * key_total,
        ),
    )(band, gpos, queries, *blocks)


def attend_back_kernel(block_total, band_ref, gpos_ref, cos_ref, sin_ref, q_ref, grad_ref, lse_ref, *refs):
    blocks = refs[:block_total]
    dq_ref = refs[block_total]
    out_refs = refs[block_total + 1 : 2 * block_total + 1]
    bias_ref = refs[-1]
    rows, q_width = q_ref.shape[1:]
    kv_width = blocks[0].shape[2] // 2
    heads, group = q_width // HD, q_width // kv_width
    window_len = rows * (block_total - 1)
    fill_bias(band_ref, gpos_ref, bias_ref, rows, window_len)
    starts = [rows * number for number in range(block_total)]
    pending = []
    for kv_head in range(kv_width // HD):
        left = kv_head * HD
        key_sums = [0.0] * block_total
        value_sums = [0.0] * block_total
        for head in range(kv_head * group, (kv_head + 1) * group):
            queries = q_ref[0, :, head * HD : (head + 1) * HD]
            grads = grad_ref[0, :, head * HD : (head + 1) * HD]
            lse = lse_ref[0, head : head + 1, :]
            soft, soft_grads = [], []
            inner = 0.0
            for number, (block, start) in enumerate(zip(blocks, starts)):
                part = over_last(block[0, :, left : left + HD], queries)
                part = jnp.exp(part + bias_ref[start : start + block.shape[1]] - lse)
                slope = over_last(block[0, :, kv_width + left : kv_width + left + HD], grads)
                inner = inner + jnp.sum(part * slope, 0, keepdims=True)
                soft.append(part)
                soft_grads.append(slope)
            turned = 0.0
            for number, block in enumerate(blocks):
                score_grads = (soft[number] * (soft_grads[number] - inner)).astype(jnp.bfloat16)
                value_sums[number] = value_sums[number] + jnp.dot(
                    soft[number].astype(jnp.bfloat16), grads, preferred_element_type=jnp.float32
                )
                key_sums[number] = key_sums[number] + jnp.dot(
                    score_grads, queries, preferred_element_type=jnp.float32
                )
                turned = turned + over_first(block[0, :, left : left + HD], score_grads)
            pending.append(turned)
            if len(pending) * HD == BLK or head == heads - 1:
                stop = (head + 1) * HD
                both = jnp.concatenate(pending, 0).T * HD ** (-0.5)
                pending = []
                first, other = half_turn(both * sin_ref[0])
                both = both * cos_ref[0] + jnp.where(first, other, -other)
                dq_ref[0, :, stop - both.shape[1] : stop] = both.astype(jnp.bfloat16)
        for number, out_ref in enumerate(out_refs):
            out_ref[0, :, left : left + HD] = key_sums[number].astype(out_ref.dtype)
            out_ref[0, :, kv_width + left : kv_width + left + HD] = value_sums[number].astype(
                out_ref.dtype
            )


def attend_back(band, gpos, cosines, sines, queries, grads, lse, blocks):
    seqs, rows, q_width = queries.shape
    heads = q_width // HD
    key_total = sum(block.shape[1] for block in blocks)

    def whole(array):
        return pl.BlockSpec((1,) + array.shape[1:], lambda s, *_: (s, 0, 0))

    table = pl.BlockSpec((1, rows, BLK), lambda s, *_: (0, 0, 0))
    out_shape = [jax.ShapeDtypeStruct(queries.shape, jnp.bfloat16)]
    for number, block in enumerate(blocks):
        own = number == len(blocks) - 2
        out_shape.append(jax.ShapeDtypeStruct(block.shape, jnp.float32 if own else jnp.bfloat16))
    return pl.pallas_call(
        functools.partial(attend_back_kernel, len(blocks)),
        out_shape=out_shape,
        grid_spec=pltpu.PrefetchScalarGridSpec(
            num_scalar_prefetch=1,
            grid=(seqs,),
            in_specs=[whole(gpos), table, table]
            + [whole(array) for array in (queries, grads, lse, *blocks)],
            out_specs=[whole(array) for array in out_shape],
            scratch_shapes=[pltpu.VMEM((key_total, rows), jnp.float32)],
        ),
        compiler_params=pltpu.CompilerParams(vmem_limit_bytes=48 * 2**20),
        cost_estimate=pl.CostEstimate(
            flops=40 * seqs * heads * rows * key_total * HD,
            bytes_accessed=8 * queries.size,
            transcendentals=seqs * heads * rows * key_total,
        ),
    )(band, gpos, cosines, sines, queries, grads, lse, *blocks)


def join_kernel(q_width, kv_width, dq_ref, own_ref, pick_ref, glob_ref, cos_ref, sin_ref, *refs):
    back_refs, out_ref = refs[:-1], refs[-1]
    out_ref[0, :, :q_width] = dq_ref[0]
    picked = lax.dot_general(
        pick_ref[0].astype(jnp.float32),
        glob_ref[0],
        (((0,), (0,)), ((), ())),
        precision=lax.Precision.HIGHEST,
        preferred_element_type=jnp.float32,
    )
    for start in range(0, 2 * kv_width, BLK):
        lanes = slice(start, start + BLK)
        total = own_ref[0, :, lanes] + picked[:, lanes]
        for back_ref in back_refs:
            total = total + back_ref[0, :, lanes].astype(jnp.float32)
        first, other = half_turn(total * sin_ref[0])
        turned = total * cos_ref[0] + jnp.where(first, other, -other)
        column = lax.broadcasted_iota(jnp.int32, total.shape, 1) + start
        turned = jnp.where(column >= kv_width, total, turned)
        out_ref[0, :, q_width + start : q_width + start + BLK] = turned.astype(jnp.bfloat16)


def join_grads(dq, own, picks, globs, cosines, sines, backs):
    seqs, rows, q_width = dq.shape
    kv_width = own.shape[2] // 2

    def whole(array):
        return pl.BlockSpec((1,) + array.shape[1:], lambda s: (s, 0, 0))

    table = pl.BlockSpec((1, rows, BLK), lambda s: (0, 0, 0))
    out_shape = jax.ShapeDtypeStruct((seqs, rows, q_width + 2 * kv_width), jnp.bfloat16)
    return pl.pallas_call(
        functools.partial(join_kernel, q_width, kv_width),
        out_shape=out_shape,
        grid=(seqs,),
        in_specs=[whole(dq), whole(own), whole(picks), whole(globs), table, table]
        + [whole(back) for back in backs],
        out_specs=whole(out_shape),
        cost_estimate=pl.CostEstimate(
            flops=20 * own.size, bytes_accessed=4 * dq.size + 12 * own.size, transcendentals=0
        ),
    )(dq, own, picks, globs, cosines, sines, *backs)


def adam_kernel(batch, meta, rates, *refs):
    master_ref, first_ref, second_ref, left_ref, right_ref = refs[:5]
    sources = refs[5:-6]
    new_first_ref, new_second_ref, new_master_ref, copy_ref, tiles, arrived = refs[-6:]
    step, steps = pl.program_id(0), pl.num_programs(0)
    slot = step % 2

    def fetch(at_step, at_slot):
        for place in range(batch):
            tile = at_step * batch + place
            for number, source in enumerate(sources):

                @pl.when(meta[0, tile] == number)
                def _(source=source, tile=tile, place=place):
                    top = pl.multiple_of(meta[2, tile], BLK)
                    left = pl.multiple_of(meta[3, tile], BLK)
                    pltpu.make_async_copy(
                        source.at[meta[1, tile], pl.ds(top, BLK), pl.ds(left, BLK)],
                        tiles.at[at_slot, place],
                        arrived.at[at_slot],
                    ).start()

    @pl.when(step == 0)
    def _():
        fetch(0, 0)

    @pl.when(step + 1 < steps)
    def _():
        fetch(step + 1, 1 - slot)

    pltpu.make_async_copy(tiles.at[slot], tiles.at[slot], arrived.at[slot]).wait()
    places = range(batch)
    lefts = [left_ref[place].astype(jnp.bfloat16) for place in places]
    rights = [right_ref[place].astype(jnp.bfloat16) for place in places]
    turned = [over_first(lefts[place], tiles[slot, place]).astype(jnp.bfloat16) for place in places]
    rotated = [
        jnp.dot(turned[place], rights[place], preferred_element_type=jnp.float32) for place in places
    ]
    directions = []
    for place in places:
        new_first = beta_one * first_ref[place] + (1.0 - beta_one) * rotated[place]
        new_second = beta_two * second_ref[place] + (1.0 - beta_two) * rotated[place] * rotated[place]
        direction = (
            new_first
            / (1.0 - beta_one**STEP)
            / (jnp.sqrt(new_second / (1.0 - beta_two**STEP)) + adam_eps)
        )
        new_first_ref[place] = new_first
        new_second_ref[place] = new_second
        directions.append(direction.astype(jnp.bfloat16))
    updates = [
        jnp.dot(lefts[place], directions[place], preferred_element_type=jnp.float32) for place in places
    ]
    updates = [over_last(updates[place].astype(jnp.bfloat16), rights[place]) for place in places]
    for place in places:
        old = master_ref[place]
        new_master = old - rates[step * batch + place] * (updates[place] + weight_decay * old)
        new_master_ref[place] = new_master
        copy_ref[place] = new_master.astype(jnp.bfloat16)


def adam(meta, rates, state, sources):
    count = state[0].shape[0]
    batch = max(size for size in (1, 2, 4) if count % size == 0)
    block = pl.BlockSpec((batch, BLK, BLK), lambda s, *_: (s, 0, 0))
    anywhere = pl.BlockSpec(memory_space=pl.ANY)
    shape = (count, BLK, BLK)
    return pl.pallas_call(
        functools.partial(adam_kernel, batch),
        out_shape=[jax.ShapeDtypeStruct(shape, jnp.float32)] * 3
        + [jax.ShapeDtypeStruct(shape, jnp.bfloat16)],
        grid_spec=pltpu.PrefetchScalarGridSpec(
            num_scalar_prefetch=2,
            grid=(count // batch,),
            in_specs=[block] * 5 + [anywhere] * len(sources),
            out_specs=[block] * 4,
            scratch_shapes=[
                pltpu.VMEM((2, batch, BLK, BLK), jnp.bfloat16),
                pltpu.SemaphoreType.DMA((2,)),
            ],
        ),
        compiler_params=pltpu.CompilerParams(vmem_limit_bytes=32 * 2**20),
        cost_estimate=pl.CostEstimate(
            flops=8 * count * BLK**3, bytes_accessed=36 * count * BLK**2, transcendentals=0
        ),
    )(meta, rates, *state, *sources)


def per_device(
    block_input,
    cotangent,
    glob_select,
    assignment,
    master,
    first_moment,
    second_moment,
    left_basis,
    right_basis,
    gains,
    gain_first,
    gain_second,
):
    band_total = lax.axis_size("fsdp")
    rep_total = lax.axis_size("rep")
    place = lax.axis_index("rep")
    band = lax.axis_index("fsdp")
    heads = H // rep_total
    kv_heads = KVH // rep_total
    q_width = heads * HD
    kv_width = kv_heads * HD
    tok_count = block_input.shape[1]
    own_count = master.shape[1]
    tile_total = own_count * rep_total
    aligned = square() and whole_tiles(band_total, rep_total)
    tile_order = assignment[0]

    if aligned:
        half = BLK // 2
        slots = square_pieces(master[0, :, :half].astype(jnp.bfloat16))
        *slots, later = lax.optimization_barrier((*slots, master[0, :, half:].astype(jnp.bfloat16)))
        later_slots = square_pieces(later)

    residual = block_input[0].astype(jnp.float32)
    grad_top = cotangent[0]
    position = band * tok_count + jnp.arange(tok_count, dtype=jnp.int32)
    cosine_table, sine_table = rope_tables(position)
    scale_one = lax.rsqrt(jnp.mean(residual * residual, -1, keepdims=True) + norm_eps)
    normed_one = (residual * scale_one * gains[0]).astype(jnp.bfloat16)
    normed_one_all = rep_gather(normed_one).reshape(-1, D)
    pick_rows = glob_select[0]
    selector = pick_rows.astype(jnp.bfloat16)
    glob_pos_part = jnp.sum(pick_rows * position[None, :], 1)
    digits = jnp.stack([glob_pos_part // 256, glob_pos_part % 256], 1).astype(jnp.bfloat16)
    digits = jnp.pad(digits, ((0, 0), (0, BLK - 2)))
    glob_part = jnp.concatenate(
        [jnp.dot(selector, normed_one, preferred_element_type=jnp.float32).astype(jnp.bfloat16), digits], 1
    )
    glob_rows_all = rep_gather(add_all(glob_part, "fsdp").astype(jnp.bfloat16))
    selector_all = rep_gather(selector)
    glob_normed = glob_rows_all[..., :D].reshape(-1, D)
    glob_digits = glob_rows_all[..., D : D + 2].astype(jnp.float32)
    glob_place = glob_digits[..., 0] * 256.0 + glob_digits[..., 1]
    glob_total = glob_place.shape[1]

    def over_bands(slice_rows):
        return lax.all_gather(slice_rows, "fsdp", axis=0, tiled=True)

    if aligned:
        layout = slice_layout(band_total, rep_total)
        grids = []
        for kind, grid in enumerate(layout):
            if kind == 3:
                grids.append(jnp.asarray(grid.transpose(1, 0, 2).reshape(grid.shape[1], -1)))
            else:
                grids.append(lax.dynamic_index_in_dim(jnp.asarray(grid), place, 0, False))
        inner_grid = jnp.concatenate(grids[:3], 1)

        def find(wanted):
            wanted = jnp.take(tile_order, jnp.concatenate([grid.reshape(-1) for grid in wanted]), mode="clip")
            entry, row = (wanted // own_count) ^ place, wanted % own_count
            cut = own_count // 2
            high = (entry == 3) & (row >= cut)
            found = jnp.stack([jnp.where(high, 4, entry), jnp.where(high, row - cut, row)], 0)
            return found.astype(jnp.int32)

        def plan(grid, parts):
            return (*grid.shape, parts)

        inner_part, gate_part = gather_matrices(
            slots, find([inner_grid, grids[4]]), [plan(inner_grid, (0,)), plan(grids[4], (0,))]
        )
        early_inner, early_gate = over_bands(inner_part), over_bands(gate_part)
        *later_slots, early_inner, early_gate = lax.optimization_barrier(
            (*later_slots, early_inner, early_gate)
        )
        inner_part, output_part, gate_part, up_part, down_part = gather_matrices(
            (*slots, *later_slots),
            find([inner_grid, *grids[3:]]),
            [plan(inner_grid, (1,)), plan(grids[3], (0, 1)), plan(grids[4], (1,))]
            + [plan(grid, (0, 1)) for grid in grids[5:]],
        )

        def woven(early, late):
            rows, cols = early.shape
            both = jnp.stack([early.reshape(-1, half, cols), late.reshape(-1, half, cols)], 1)
            return both.reshape(2 * rows, cols)

        w_inner = woven(early_inner, over_bands(inner_part))
        w_gate = woven(early_gate, over_bands(gate_part))
    else:
        slots = lax.all_gather(master[0].astype(jnp.bfloat16), "rep", axis=0, tiled=True)
        tiles = jnp.take(slots, tile_order, axis=0, mode="clip")
        slices = cut_slices(band_matrices(tiles, band_total), band_total, rep_total)
        output_part, _, up_part, down_part = slices[3:]
        w_inner = over_bands(jnp.concatenate(slices[0:3], 1))
        w_gate = over_bands(slices[4])

    per_rep = band_total // rep_total
    w_output = spread_output(output_part)
    w_up = over_bands(up_part)
    w_down = over_bands(down_part)

    def mul(rows, weight):
        return jnp.dot(rows, weight, preferred_element_type=jnp.float32)

    def mul_back(rows, weight):
        return lax.dot_general(rows, weight, (((1,), (1,)), ((), ())), preferred_element_type=jnp.float32)

    def weight_grad(rows, grad_rows):
        return lax.dot_general(
            rows, grad_rows, (((0,), (0,)), ((), ())), preferred_element_type=jnp.float32
        ).astype(jnp.bfloat16)

    def own_sum(partial):
        return rep_scatter(partial.astype(jnp.bfloat16).reshape(rep_total, tok_count, D))

    grad_top_now, w_inner = lax.optimization_barrier((grad_top, w_inner))
    grad_top_all = rep_gather(grad_top_now).reshape(-1, D)

    inner_rows = mul(normed_one_all, w_inner).reshape(rep_total, tok_count, -1)
    wide_cosine = jnp.concatenate([cosine_table, cosine_table], 1)[None]
    wide_sine = jnp.concatenate([sine_table, sine_table], 1)[None]
    queries, own_pairs = rope_rows(inner_rows, q_width, kv_width, wide_cosine, wide_sine)
    glob_inner = mul(glob_normed, w_inner[:, q_width:]).reshape(rep_total, glob_total, -1)
    glob_cosine, glob_sine = rope_tables(glob_place.reshape(-1))
    glob_cosine = jnp.concatenate([glob_cosine, glob_cosine], 1).reshape(rep_total, glob_total, -1)
    glob_sine = jnp.concatenate([glob_sine, glob_sine], 1).reshape(rep_total, glob_total, -1)
    (glob_pairs,) = rope_rows(glob_inner, 0, kv_width, glob_cosine, glob_sine)
    back_count = (WINDOW + tok_count - 2) // tok_count
    pair_blocks = [shifted(own_pairs, "fsdp", distance) for distance in range(back_count, 0, -1)]
    pair_blocks = pair_blocks + [own_pairs, glob_pairs]
    glob_spots = jnp.broadcast_to(glob_place[:, :, None], (rep_total, glob_total, BLK))
    band_number = band.astype(jnp.int32).reshape(1)
    attended_low, lse = attend(band_number, glob_spots, queries, pair_blocks)
    attended_low = attended_low.reshape(-1, q_width)
    middle = residual + own_sum(mul(attended_low, w_output))
    scale_two = lax.rsqrt(jnp.mean(middle * middle, -1, keepdims=True) + norm_eps)
    normed_two = (middle * scale_two * gains[1]).astype(jnp.bfloat16)
    normed_two_all = rep_gather(normed_two).reshape(-1, D)

    gate_rows = mul(normed_two_all, w_gate)
    up_rows = mul(normed_two_all, w_up)
    sigmoid_gate = jax.nn.sigmoid(gate_rows)
    silu_gate = gate_rows * sigmoid_gate
    activation = (silu_gate * up_rows).astype(jnp.bfloat16)
    g_down = weight_grad(activation, grad_top_all)
    grad_top_all, g_down = lax.optimization_barrier((grad_top_all, g_down))
    grad_act = mul_back(grad_top_all, w_down)
    grad_gate = (
        grad_act * up_rows * sigmoid_gate * (1.0 + gate_rows * (1.0 - sigmoid_gate))
    ).astype(jnp.bfloat16)
    grad_up = (grad_act * silu_gate).astype(jnp.bfloat16)
    grad_normed_two = own_sum(mul_back(grad_gate, w_gate) + mul_back(grad_up, w_up))
    g_gate = weight_grad(normed_two_all, grad_gate)
    g_up = weight_grad(normed_two_all, grad_up)
    grad_normed_two, g_gate, g_up = lax.optimization_barrier((grad_normed_two, g_gate, g_up))
    block_out = middle + own_sum(mul(activation, w_down))

    def over_tokens(partial):
        return lax.psum_scatter(partial, "fsdp", scatter_dimension=0, tiled=True)

    s_down = over_tokens(g_down)
    s_gate = over_tokens(g_gate)
    s_up = over_tokens(g_up)

    grad_middle = grad_top.astype(jnp.float32) + norm_back(middle, scale_two, gains[1], grad_normed_two)
    grad_branch_all = rep_gather(grad_middle.astype(jnp.bfloat16)).reshape(-1, D)
    grad_attended = mul_back(grad_branch_all, w_output).astype(jnp.bfloat16)
    grad_attended, s_down = lax.optimization_barrier((grad_attended, s_down))
    mine = collect_output(weight_grad(attended_low, grad_branch_all))
    grad_attended = grad_attended.reshape(rep_total, tok_count, q_width)
    grad_queries, *grad_blocks = attend_back(
        band_number, glob_spots, wide_cosine, wide_sine, queries, grad_attended, lse, pair_blocks
    )
    returned = [
        shifted(grad_blocks[back_count - distance], "fsdp", -distance)
        for distance in range(1, back_count + 1)
    ]
    glob_grads = add_all(grad_blocks[-1], "fsdp")
    glob_grads, s_gate = lax.optimization_barrier((glob_grads, s_gate))
    grad_inner = join_grads(
        grad_queries, grad_blocks[-2], selector_all, glob_grads, wide_cosine, wide_sine, returned
    ).reshape(-1, q_width + 2 * kv_width)
    g_inner, s_up = lax.optimization_barrier((weight_grad(normed_one_all, grad_inner), s_up))
    s_inner = over_tokens(g_inner)
    grad_normed_one = own_sum(mul_back(grad_inner, w_inner))
    grad_input = grad_middle + norm_back(residual, scale_one, gains[0], grad_normed_one)

    source = band // per_rep
    out_entry = source ^ place if square() else source
    out_band = lax.dynamic_index_in_dim(rep_gather(mine), out_entry, 0, False)
    slot_ids = jnp.arange(tile_total, dtype=jnp.int32)
    inverse = jnp.sum(jnp.where(tile_order[None, :] == slot_ids[:, None], slot_ids[None, :], 0), 1)
    own_slots = place * own_count + jnp.arange(own_count, dtype=jnp.int32)
    owned_tiles = jnp.take(inverse, own_slots, mode="clip")
    if aligned:
        sources = [rep_gather(s_inner), out_band[None], rep_gather(s_gate), rep_gather(s_up), rep_gather(s_down)]
        where = np.zeros((4, rep_total, tile_total), np.int32)
        for kind, grid in enumerate(layout):
            first_col = (0, q_width, q_width + kv_width)[kind] if kind < 3 else 0
            for there in range(rep_total):
                rows, cols = grid.shape[1:]
                numbers = grid[there].reshape(-1)
                at = np.arange(rows * cols)
                left = at % cols * BLK + first_col + (there * cols * BLK if kind == 3 else 0)
                where[0, :, numbers] = max(kind - 2, 0)
                where[2, :, numbers] = (at // cols * BLK)[:, None]
                where[3, :, numbers] = left[:, None]
                for here in range(rep_total):
                    where[1, here, numbers] = 0 if kind == 3 else here ^ there
        tile_spots = lax.dynamic_index_in_dim(jnp.asarray(where), place, 1, False)
        meta = jnp.take(tile_spots, owned_tiles, axis=1, mode="clip")
    else:
        stacks = [
            None if piece is None else lax.all_gather(piece, "rep", axis=0)
            for piece in (
                s_inner[:, :q_width],
                s_inner[:, q_width : q_width + kv_width],
                s_inner[:, q_width + kv_width :],
                None,
                s_gate,
                s_up,
                s_down,
            )
        ]
        stacks[3] = out_band[None]
        sources = [band_tiles(join_slices(stacks, band_total, rep_total))]
        meta = jnp.stack([0 * owned_tiles, owned_tiles, 0 * owned_tiles, 0 * owned_tiles], 0)
    slot_rates = jnp.take(kind_rates(band_total), owned_tiles, mode="clip")
    new_first, new_second, new_master, master_copy = adam(
        meta,
        slot_rates,
        (master[0], first_moment[0], second_moment[0], left_basis[0], right_basis[0]),
        sources,
    )
    gain_terms = jnp.stack(
        [
            jnp.sum(grad_normed_one * residual * scale_one, 0),
            jnp.sum(grad_normed_two * middle * scale_two, 0),
        ]
    )
    square_terms = jnp.stack(
        [jnp.sum(residual * residual), jnp.sum(middle * middle), jnp.sum(block_out * block_out)]
    )
    sums = jnp.concatenate([gain_terms.reshape(-1), square_terms])
    sums = add_all(add_all(sums, "rep"), "fsdp")
    gain_grad, square_total = sums[: 2 * D].reshape(2, D), sums[2 * D :]
    new_gain_first = beta_one * gain_first + (1.0 - beta_one) * gain_grad
    new_gain_second = beta_two * gain_second + (1.0 - beta_two) * gain_grad * gain_grad
    gain_step = (
        new_gain_first
        / (1.0 - beta_one**STEP)
        / (jnp.sqrt(new_gain_second / (1.0 - beta_two**STEP)) + adam_eps)
    )
    new_gains = gains - gain_rate * gain_step
    rms_stats = jnp.sqrt(square_total / (rep_total * band_total * tok_count * D))
    return (
        block_out[None],
        grad_input[None],
        new_first[None],
        new_second[None],
        new_master[None],
        master_copy[None],
        new_gain_first,
        new_gain_second,
        new_gains,
        rms_stats,
    )


def solution(mesh):
    in_specs = (
        P("rep", "fsdp", None),
        P("rep", "fsdp", None),
        P("rep", None, "fsdp"),
        P("fsdp", None),
        P("fsdp", "rep", None, None),
        P("fsdp", "rep", None, None),
        P("fsdp", "rep", None, None),
        P("fsdp", "rep", None, None),
        P("fsdp", "rep", None, None),
        P(),
        P(),
        P(),
    )
    out_specs = (
        P("rep", "fsdp", None),
        P("rep", "fsdp", None),
        P("fsdp", "rep", None, None),
        P("fsdp", "rep", None, None),
        P("fsdp", "rep", None, None),
        P("fsdp", "rep", None, None),
        P(),
        P(),
        P(),
        P(),
    )
    return jax.shard_map(
        per_device, mesh=mesh, in_specs=in_specs, out_specs=out_specs, check_vma=False
    )
```

```python
import functools

import jax
import jax.numpy as jnp
import numpy as np
from jax import lax
from jax.experimental import pallas as pl
from jax.experimental.pallas import tpu as pltpu
from jax.sharding import PartitionSpec as P

D = 2048
H = 32
KVH = 8
HD = 64
FF = 8192
WINDOW = 512
BLK = 128
STEP = 10


norm_eps = 1e-05
rope_theta = 500000.0
beta_one = 0.5
beta_two = 0.5
adam_eps = 1e-08
weight_decay = 0.1
gain_rate = 0.5
masked_value = -1e30


def matrix_shapes():
    kv_width = KVH * HD
    return [(D, D), (D, kv_width), (D, kv_width), (D, D), (D, FF), (D, FF), (FF, D)]


def kind_rates(band_total):
    rate_list = [
        D ** (-0.5),
        D ** (-0.5),
        D ** (-0.5),
        (D * 8 // WINDOW) ** (-0.5),
        D ** (-0.5),
        D ** (-0.5),
        FF ** (-0.5),
    ]
    pieces = []
    for (row_total, col_total), rate_value in zip(matrix_shapes(), rate_list):
        tile_count = row_total // band_total // BLK * (col_total // BLK)
        pieces.append(jnp.full((tile_count,), rate_value, jnp.float32))
    return jnp.concatenate(pieces)


def band_matrices(tiles, band_total):
    matrices = []
    offset = 0
    for row_total, col_total in matrix_shapes():
        band_rows = row_total // band_total
        tile_count = band_rows // BLK * (col_total // BLK)
        segment = tiles[offset : offset + tile_count].reshape(
            band_rows // BLK, col_total // BLK, BLK, BLK
        )
        matrices.append(segment.transpose(0, 2, 1, 3).reshape(band_rows, col_total))
        offset += tile_count
    return matrices


def band_tiles(matrices):
    pieces = []
    for matrix in matrices:
        row_count, col_count = matrix.shape
        segment = matrix.reshape(row_count // BLK, BLK, col_count // BLK, BLK).transpose(0, 2, 1, 3)
        pieces.append(segment.reshape(-1, BLK, BLK))
    return jnp.concatenate(pieces, 0)


def rope_tables(position):
    halves = jnp.arange(HD // 2, dtype=jnp.float32) * (2.0 / HD)
    frequency = rope_theta ** (-halves)
    angles = position.astype(jnp.float32)[:, None] * frequency[None, :]
    angles = jnp.concatenate([angles, angles], 1)
    return (jnp.cos(angles), jnp.sin(angles))


def rotate(vectors, cosine_table, sine_table):
    half_width = vectors.shape[-1] // 2
    turned = jnp.concatenate([-vectors[..., half_width:], vectors[..., :half_width]], -1)
    return vectors * cosine_table[:, None, :] + turned * sine_table[:, None, :]


def rotate_back(grad_rows, cosine_table, sine_table):
    half_width = grad_rows.shape[-1] // 2
    scaled = grad_rows * sine_table[:, None, :]
    turned = jnp.concatenate([scaled[..., half_width:], -scaled[..., :half_width]], -1)
    return grad_rows * cosine_table[:, None, :] + turned


def norm_back(values, row_scale, gain_row, grad_rows):
    weighted = grad_rows * gain_row
    return row_scale * weighted - values * row_scale**3 * jnp.mean(
        weighted * values, -1, keepdims=True
    )


def to_rep(block, distance):
    route = [(i, i ^ distance) for i in range(lax.axis_size("rep"))]
    return lax.ppermute(block, "rep", route)


def square():
    return lax.axis_size("rep") == 4


def square_pieces(block):
    cut = block.shape[0] // 2
    near = to_rep(block, 1)
    far = to_rep(block, 2)
    return block, near, far, to_rep(near[:cut], 2), to_rep(far[cut:], 1)


def rep_gather(block):
    if not square():
        return lax.all_gather(block, "rep", axis=0)
    own, near, far, low, high = square_pieces(block)
    return jnp.concatenate([own, near, far, low, high], 0).reshape((4,) + block.shape)


def rep_of(entry):
    place = lax.axis_index("rep")
    return place ^ entry if square() else entry


def rep_scatter(parts):
    if not square():
        flat = parts.reshape(-1, parts.shape[-1])
        return lax.psum_scatter(flat, "rep", scatter_dimension=0, tiled=True).astype(jnp.float32)
    half = parts.shape[-1] // 2
    totals = []
    for side, (first, second) in ((parts[..., :half], (1, 2)), (parts[..., half:], (2, 1))):
        away = to_rep(jnp.stack([side[first], side[3]], 0), first)
        other = (side[second].astype(jnp.float32) + away[1].astype(jnp.float32)).astype(parts.dtype)
        own = side[0].astype(jnp.float32) + away[0].astype(jnp.float32)
        totals.append(own + to_rep(other, second).astype(jnp.float32))
    return jnp.concatenate(totals, -1)


def add_all(value, axis):
    total = value.astype(jnp.float32)
    distance = 1
    while distance < lax.axis_size(axis):
        route = [(i, i ^ distance) for i in range(lax.axis_size(axis))]
        total = total + lax.ppermute(total.astype(value.dtype), axis, route).astype(jnp.float32)
        distance *= 2
    return total


def rep_features(block):
    if not square():
        return lax.all_gather(block, "rep", axis=2, tiled=True)
    own, near, far, low, high = square_pieces(block)
    return jnp.concatenate(
        [
            own,
            jnp.stack([near[1], near[0], near[3], near[2]], 0),
            jnp.stack([far[2], far[3], far[0], far[1]], 0),
            jnp.stack([high[1], high[0], low[1], low[0]], 0),
        ],
        2,
    )


def rep_features_sum(block):
    reps, rows, width = block.shape
    parts = block.reshape(reps, rows, reps, width // reps)
    if square():
        swapped = [
            jnp.stack([parts[there ^ entry, :, entry] for there in range(reps)], 0) for entry in range(reps)
        ]
    else:
        swapped = [parts[:, :, entry] for entry in range(reps)]
    total = rep_scatter(jnp.stack(swapped, 0).reshape(reps, reps * rows, -1))
    return total.reshape(reps, rows, -1)


def rep_exchange(parts):
    if not square():
        return lax.all_to_all(parts, "rep", 0, 0)
    return jnp.stack([parts[0]] + [to_rep(parts[entry], entry) for entry in (1, 2, 3)], 0)


def by_place(parts):
    entries = [rep_of(entry) for entry in range(parts.shape[0])]
    return jnp.stack([lax.dynamic_index_in_dim(parts, entry, 0, False) for entry in entries], 0)


def shifted(block, axis, distance):
    devices = range(lax.axis_size(axis))
    route = [(i - distance, i) for i in devices if i - distance in devices]
    return lax.ppermute(block, axis, route)


def tile_offsets(band_total):
    offsets = [0]
    for row_total, col_total in matrix_shapes():
        offsets.append(offsets[-1] + row_total // band_total // BLK * (col_total // BLK))
    return offsets


def whole_tiles(band_total, rep_total):
    return KVH * HD // rep_total % BLK == 0 and FF // band_total // rep_total % BLK == 0


def slice_layout(band_total, rep_total):
    offsets = tile_offsets(band_total)
    layout = []
    for kind, (row_total, col_total) in enumerate(matrix_shapes()):
        rows, cols = row_total // band_total // BLK, col_total // BLK
        grid = offsets[kind] + np.arange(rows * cols).reshape(rows, cols)
        if kind == 6:
            layout.append(grid.reshape(rep_total, rows // rep_total, cols))
        elif kind in (4, 5):
            cut = grid.reshape(rows, band_total, rep_total, -1).transpose(2, 0, 1, 3)
            layout.append(cut.reshape(rep_total, rows, -1))
        else:
            layout.append(grid.reshape(rows, rep_total, -1).transpose(1, 0, 2))
    return layout


def tiles_to_matrix(tiles):
    rows, cols = tiles.shape[:2]
    return tiles.transpose(0, 2, 1, 3).reshape(rows * BLK, cols * BLK)


def matrix_to_tiles(matrix):
    rows, cols = matrix.shape
    cut = matrix.reshape(rows // BLK, BLK, cols // BLK, BLK)
    return cut.transpose(0, 2, 1, 3).reshape(-1, BLK, BLK)


def cut_slices(matrices, band_total, rep_total):
    place = lax.axis_index("rep")
    slices = []
    for kind, matrix in enumerate(matrices):
        rows, cols = matrix.shape
        if kind == 6:
            slices.append(lax.dynamic_slice_in_dim(matrix, place * (rows // rep_total), rows // rep_total, 0))
        elif kind in (4, 5):
            cut = matrix.reshape(rows, band_total, rep_total, -1)
            slices.append(lax.dynamic_index_in_dim(cut, place, 2, False).reshape(rows, -1))
        else:
            slices.append(lax.dynamic_slice_in_dim(matrix, place * (cols // rep_total), cols // rep_total, 1))
    return slices


def join_slices(stacks, band_total, rep_total):
    matrices = []
    for kind, stack in enumerate(stacks):
        rows, cols = stack.shape[1:]
        if kind == 6:
            matrices.append(stack.reshape(-1, cols))
        elif kind in (4, 5):
            cut = stack.reshape(rep_total, rows, band_total, -1).transpose(1, 2, 0, 3)
            matrices.append(cut.reshape(rows, -1))
        else:
            matrices.append(stack.transpose(1, 0, 2).reshape(rows, -1))
    return matrices


def gather_kernel(plans, meta, *refs):
    source_total = len(refs) - len(plans) - 1
    sources, targets, done = refs[:source_total], refs[source_total:-1], refs[-1]
    piece_total = source_total // max(len(parts) for _, _, parts in plans)
    start = 0
    for place, (target, (rows, cols, parts)) in enumerate(zip(targets, plans)):
        height = sources[0].shape[1]

        def one(tile, carry, target=target, cols=cols, parts=parts, start=start, place=place, height=height):
            kind = meta[0, start + tile]
            row = meta[1, start + tile]
            top = tile // cols * (height * len(parts))
            left = pl.multiple_of(tile % cols * BLK, BLK)
            for number in range(piece_total):

                @pl.when(kind == number)
                def _(number=number):
                    for order, part in enumerate(parts):
                        first = pl.multiple_of(top + order * height, height)
                        pltpu.make_async_copy(
                            sources[part * piece_total + number].at[row],
                            target.at[pl.ds(first, height), pl.ds(left, BLK)],
                            done.at[place],
                        ).start()

            return carry

        lax.fori_loop(0, rows * cols, one, 0)
        start += rows * cols
    for place, target in enumerate(targets):
        pltpu.make_async_copy(target, target, done.at[place]).wait()


def gather_matrices(sources, meta, plans):
    anywhere = pl.BlockSpec(memory_space=pl.ANY)
    height = sources[0].shape[1]
    out_shape = [
        jax.ShapeDtypeStruct((rows * height * len(parts), cols * BLK), jnp.bfloat16)
        for rows, cols, parts in plans
    ]
    moved = sum(4 * shape.size for shape in out_shape)
    return pl.pallas_call(
        functools.partial(gather_kernel, plans),
        out_shape=out_shape,
        grid_spec=pltpu.PrefetchScalarGridSpec(
            num_scalar_prefetch=1,
            grid=(1,),
            in_specs=[anywhere] * len(sources),
            out_specs=[pl.BlockSpec(shape.shape, lambda i, *_: (0, 0)) for shape in out_shape],
            scratch_shapes=[pltpu.SemaphoreType.DMA((len(plans),))],
        ),
        compiler_params=pltpu.CompilerParams(vmem_limit_bytes=32 * 2**20),
        cost_estimate=pl.CostEstimate(flops=0, bytes_accessed=moved, transcendentals=0),
    )(meta, *sources)


def half_turn(values):
    lane = lax.broadcasted_iota(jnp.int32, values.shape, 1)
    lanes = values.shape[1]
    first = lane % HD < HD // 2
    return first, jnp.where(
        first, pltpu.roll(values, lanes - HD // 2, 1), pltpu.roll(values, HD // 2, 1)
    )


def rope_kernel(q_width, kv_width, x_ref, cos_ref, sin_ref, *outs):
    width = x_ref.shape[-1]
    for start in range(0, width, BLK):
        values = x_ref[0, :, start : start + BLK]
        first, turned = half_turn(values)
        sines = sin_ref[0]
        turned_rows = values * cos_ref[0] + turned * jnp.where(first, -sines, sines)
        if start + BLK > q_width + kv_width:
            column = lax.broadcasted_iota(jnp.int32, values.shape, 1) + start
            turned_rows = jnp.where(column >= q_width + kv_width, values, turned_rows)
        if start < q_width:
            outs[0][0, :, start : start + BLK] = (turned_rows * HD ** (-0.5)).astype(jnp.bfloat16)
        else:
            outs[-1][0, :, start - q_width : start - q_width + BLK] = turned_rows.astype(jnp.bfloat16)


def rope_rows(inner, rows, row_block, q_width, kv_width, cosines, sines, with_queries=True):
    seqs, _, width = inner.shape
    shared = cosines.shape[0] == 1
    table = pl.BlockSpec((1, rows, BLK), lambda s: (0 if shared else s, 0, 0))
    widths = [q_width, 2 * kv_width]
    column_block = 0
    if not with_queries:
        width, column_block = 2 * kv_width, q_width // (2 * kv_width)
        widths, q_width = widths[1:], 0
    return pl.pallas_call(
        functools.partial(rope_kernel, q_width, kv_width),
        out_shape=[jax.ShapeDtypeStruct((seqs, rows, w), jnp.bfloat16) for w in widths],
        grid=(seqs,),
        in_specs=[pl.BlockSpec((1, rows, width), lambda s: (s, row_block, column_block)), table, table],
        out_specs=[pl.BlockSpec((1, rows, w), lambda s: (s, 0, 0)) for w in widths],
        cost_estimate=pl.CostEstimate(
            flops=6 * seqs * rows * width, bytes_accessed=6 * seqs * rows * width, transcendentals=0
        ),
    )(inner, cosines, sines)


def fill_bias(band_ref, gpos_ref, bias_ref, rows, window_len):
    band = band_ref[0]

    @pl.when(pl.program_id(0) == 0)
    def _():
        key = lax.broadcasted_iota(jnp.int32, (window_len, rows), 0) + (
            band * rows - (window_len - rows)
        )
        query = lax.broadcasted_iota(jnp.int32, (window_len, rows), 1) + band * rows
        inside = (key > query - WINDOW) & (key <= query) & (key >= 0)
        bias_ref[:window_len] = jnp.where(inside, 0.0, masked_value)

    glob_total = gpos_ref.shape[1]
    query = lax.broadcasted_iota(jnp.int32, (glob_total, rows), 1) + (band * rows - WINDOW)
    spot = jnp.broadcast_to(gpos_ref[0][:, :1], (glob_total, rows))
    bias_ref[window_len:] = jnp.where(spot <= query.astype(jnp.float32), 0.0, masked_value)


def over_last(left, right):
    return lax.dot_general(left, right, (((1,), (1,)), ((), ())), preferred_element_type=jnp.float32)


def over_first(left, right):
    return lax.dot_general(left, right, (((0,), (0,)), ((), ())), preferred_element_type=jnp.float32)


def attend_kernel(block_total, band_ref, gpos_ref, q_ref, *refs):
    blocks, (out_ref, lse_ref, bias_ref) = refs[:block_total], refs[block_total:]
    rows, q_width = q_ref.shape[1:]
    kv_width = blocks[0].shape[2] // 2
    heads, group = q_width // HD, q_width // kv_width
    window_len = rows * (block_total - 1)
    fill_bias(band_ref, gpos_ref, bias_ref, rows, window_len)
    starts = [rows * number for number in range(block_total)]
    pending = []
    for head in range(heads):
        left = head // group * HD
        queries = q_ref[0, :, head * HD : (head + 1) * HD]
        scores = [
            over_last(block[0, :, left : left + HD], queries)
            + bias_ref[start : start + block.shape[1]]
            for block, start in zip(blocks, starts)
        ]
        top = functools.reduce(jnp.maximum, [jnp.max(part, 0, keepdims=True) for part in scores])
        total = 0.0
        mixed = 0.0
        for block, part in zip(blocks, scores):
            weights = jnp.exp(part - top)
            total = total + jnp.sum(weights, 0, keepdims=True)
            mixed = mixed + over_first(
                block[0, :, kv_width + left : kv_width + left + HD], weights.astype(jnp.bfloat16)
            )
        lse_ref[0, head : head + 1, :] = top + jnp.log(total)
        pending.append(mixed / total)
        if len(pending) * HD == BLK or head == heads - 1:
            stop = (head + 1) * HD
            both = jnp.concatenate(pending, 0).T
            out_ref[0, :, stop - both.shape[1] : stop] = both.astype(jnp.bfloat16)
            pending = []


def attend(band, gpos, queries, blocks):
    seqs, rows, q_width = queries.shape
    heads = q_width // HD
    key_total = sum(block.shape[1] for block in blocks)

    def whole(array):
        return pl.BlockSpec((1,) + array.shape[1:], lambda s, *_: (s, 0, 0))

    out_shape = [
        jax.ShapeDtypeStruct((seqs, rows, q_width), jnp.bfloat16),
        jax.ShapeDtypeStruct((seqs, heads, rows), jnp.float32),
    ]
    return pl.pallas_call(
        functools.partial(attend_kernel, len(blocks)),
        out_shape=out_shape,
        grid_spec=pltpu.PrefetchScalarGridSpec(
            num_scalar_prefetch=1,
            grid=(seqs,),
            in_specs=[whole(array) for array in (gpos, queries, *blocks)],
            out_specs=[whole(array) for array in out_shape],
            scratch_shapes=[pltpu.VMEM((key_total, rows), jnp.float32)],
        ),
        compiler_params=pltpu.CompilerParams(vmem_limit_bytes=48 * 2**20),
        cost_estimate=pl.CostEstimate(
            flops=16 * seqs * heads * rows * key_total * HD,
            bytes_accessed=4 * queries.size,
            transcendentals=seqs * heads * rows * key_total,
        ),
    )(band, gpos, queries, *blocks)


def attend_back_kernel(block_total, band_ref, gpos_ref, cos_ref, sin_ref, q_ref, grad_ref, lse_ref, *refs):
    blocks = refs[:block_total]
    dq_ref = refs[block_total]
    out_refs = refs[block_total + 1 : 2 * block_total + 1]
    bias_ref = refs[-1]
    rows, q_width = q_ref.shape[1:]
    kv_width = blocks[0].shape[2] // 2
    heads, group = q_width // HD, q_width // kv_width
    window_len = rows * (block_total - 1)
    fill_bias(band_ref, gpos_ref, bias_ref, rows, window_len)
    starts = [rows * number for number in range(block_total)]
    pending = []
    for kv_head in range(kv_width // HD):
        left = kv_head * HD
        key_sums = [0.0] * block_total
        value_sums = [0.0] * block_total
        for head in range(kv_head * group, (kv_head + 1) * group):
            queries = q_ref[0, :, head * HD : (head + 1) * HD]
            grads = grad_ref[0, :, head * HD : (head + 1) * HD]
            lse = lse_ref[0, head : head + 1, :]
            soft, soft_grads = [], []
            inner = 0.0
            for number, (block, start) in enumerate(zip(blocks, starts)):
                part = over_last(block[0, :, left : left + HD], queries)
                part = jnp.exp(part + bias_ref[start : start + block.shape[1]] - lse)
                slope = over_last(block[0, :, kv_width + left : kv_width + left + HD], grads)
                inner = inner + jnp.sum(part * slope, 0, keepdims=True)
                soft.append(part)
                soft_grads.append(slope)
            turned = 0.0
            for number, block in enumerate(blocks):
                score_grads = (soft[number] * (soft_grads[number] - inner)).astype(jnp.bfloat16)
                value_sums[number] = value_sums[number] + jnp.dot(
                    soft[number].astype(jnp.bfloat16), grads, preferred_element_type=jnp.float32
                )
                key_sums[number] = key_sums[number] + jnp.dot(
                    score_grads, queries, preferred_element_type=jnp.float32
                )
                turned = turned + over_first(block[0, :, left : left + HD], score_grads)
            pending.append(turned)
            if len(pending) * HD == BLK or head == heads - 1:
                stop = (head + 1) * HD
                both = jnp.concatenate(pending, 0).T * HD ** (-0.5)
                pending = []
                first, other = half_turn(both * sin_ref[0])
                both = both * cos_ref[0] + jnp.where(first, other, -other)
                dq_ref[0, :, stop - both.shape[1] : stop] = both.astype(jnp.bfloat16)
        for number, out_ref in enumerate(out_refs):
            out_ref[0, :, left : left + HD] = key_sums[number].astype(out_ref.dtype)
            out_ref[0, :, kv_width + left : kv_width + left + HD] = value_sums[number].astype(
                out_ref.dtype
            )


def attend_back(band, gpos, cosines, sines, queries, grads, lse, blocks):
    seqs, rows, q_width = queries.shape
    heads = q_width // HD
    key_total = sum(block.shape[1] for block in blocks)

    def whole(array):
        return pl.BlockSpec((1,) + array.shape[1:], lambda s, *_: (s, 0, 0))

    table = pl.BlockSpec((1, rows, BLK), lambda s, *_: (0, 0, 0))
    out_shape = [jax.ShapeDtypeStruct(queries.shape, jnp.bfloat16)]
    for number, block in enumerate(blocks):
        own = number == len(blocks) - 2
        out_shape.append(jax.ShapeDtypeStruct(block.shape, jnp.float32 if own else jnp.bfloat16))
    return pl.pallas_call(
        functools.partial(attend_back_kernel, len(blocks)),
        out_shape=out_shape,
        grid_spec=pltpu.PrefetchScalarGridSpec(
            num_scalar_prefetch=1,
            grid=(seqs,),
            in_specs=[whole(gpos), table, table]
            + [whole(array) for array in (queries, grads, lse, *blocks)],
            out_specs=[whole(array) for array in out_shape],
            scratch_shapes=[pltpu.VMEM((key_total, rows), jnp.float32)],
        ),
        compiler_params=pltpu.CompilerParams(vmem_limit_bytes=48 * 2**20),
        cost_estimate=pl.CostEstimate(
            flops=40 * seqs * heads * rows * key_total * HD,
            bytes_accessed=8 * queries.size,
            transcendentals=seqs * heads * rows * key_total,
        ),
    )(band, gpos, cosines, sines, queries, grads, lse, *blocks)


def join_kernel(q_width, kv_width, dq_ref, own_ref, pick_ref, glob_ref, cos_ref, sin_ref, *refs):
    back_refs, out_ref = refs[:-1], refs[-1]
    out_ref[0, :, :q_width] = dq_ref[0]
    picked = lax.dot_general(
        pick_ref[0].astype(jnp.float32),
        glob_ref[0],
        (((0,), (0,)), ((), ())),
        precision=lax.Precision.HIGHEST,
        preferred_element_type=jnp.float32,
    )
    for start in range(0, 2 * kv_width, BLK):
        lanes = slice(start, start + BLK)
        total = own_ref[0, :, lanes] + picked[:, lanes]
        for back_ref in back_refs:
            total = total + back_ref[0, :, lanes].astype(jnp.float32)
        first, other = half_turn(total * sin_ref[0])
        turned = total * cos_ref[0] + jnp.where(first, other, -other)
        column = lax.broadcasted_iota(jnp.int32, total.shape, 1) + start
        turned = jnp.where(column >= kv_width, total, turned)
        out_ref[0, :, q_width + start : q_width + start + BLK] = turned.astype(jnp.bfloat16)


def join_grads(dq, own, picks, globs, cosines, sines, backs):
    seqs, rows, q_width = dq.shape
    kv_width = own.shape[2] // 2

    def whole(array):
        return pl.BlockSpec((1,) + array.shape[1:], lambda s: (s, 0, 0))

    table = pl.BlockSpec((1, rows, BLK), lambda s: (0, 0, 0))
    out_shape = jax.ShapeDtypeStruct((seqs, rows, q_width + 2 * kv_width), jnp.bfloat16)
    return pl.pallas_call(
        functools.partial(join_kernel, q_width, kv_width),
        out_shape=out_shape,
        grid=(seqs,),
        in_specs=[whole(dq), whole(own), whole(picks), whole(globs), table, table]
        + [whole(back) for back in backs],
        out_specs=whole(out_shape),
        cost_estimate=pl.CostEstimate(
            flops=20 * own.size, bytes_accessed=4 * dq.size + 12 * own.size, transcendentals=0
        ),
    )(dq, own, picks, globs, cosines, sines, *backs)


def adam_kernel(batch, meta, rates, *refs):
    master_ref, first_ref, second_ref, left_ref, right_ref = refs[:5]
    sources = refs[5:-6]
    new_first_ref, new_second_ref, new_master_ref, copy_ref, tiles, arrived = refs[-6:]
    step, steps = pl.program_id(0), pl.num_programs(0)
    slot = step % 2

    def fetch(at_step, at_slot):
        for place in range(batch):
            tile = at_step * batch + place
            for number, source in enumerate(sources):

                @pl.when(meta[0, tile] == number)
                def _(source=source, tile=tile, place=place):
                    top = pl.multiple_of(meta[2, tile], BLK)
                    left = pl.multiple_of(meta[3, tile], BLK)
                    pltpu.make_async_copy(
                        source.at[meta[1, tile], pl.ds(top, BLK), pl.ds(left, BLK)],
                        tiles.at[at_slot, place],
                        arrived.at[at_slot],
                    ).start()

    @pl.when(step == 0)
    def _():
        fetch(0, 0)

    @pl.when(step + 1 < steps)
    def _():
        fetch(step + 1, 1 - slot)

    pltpu.make_async_copy(tiles.at[slot], tiles.at[slot], arrived.at[slot]).wait()
    places = range(batch)
    lefts = [left_ref[place].astype(jnp.bfloat16) for place in places]
    rights = [right_ref[place].astype(jnp.bfloat16) for place in places]
    turned = [over_first(lefts[place], tiles[slot, place]).astype(jnp.bfloat16) for place in places]
    rotated = [
        jnp.dot(turned[place], rights[place], preferred_element_type=jnp.float32) for place in places
    ]
    directions = []
    for place in places:
        new_first = beta_one * first_ref[place] + (1.0 - beta_one) * rotated[place]
        new_second = beta_two * second_ref[place] + (1.0 - beta_two) * rotated[place] * rotated[place]
        direction = (
            new_first
            / (1.0 - beta_one**STEP)
            / (jnp.sqrt(new_second / (1.0 - beta_two**STEP)) + adam_eps)
        )
        new_first_ref[place] = new_first
        new_second_ref[place] = new_second
        directions.append(direction.astype(jnp.bfloat16))
    updates = [
        jnp.dot(lefts[place], directions[place], preferred_element_type=jnp.float32) for place in places
    ]
    updates = [over_last(updates[place].astype(jnp.bfloat16), rights[place]) for place in places]
    for place in places:
        old = master_ref[place]
        new_master = old - rates[step * batch + place] * (updates[place] + weight_decay * old)
        new_master_ref[place] = new_master
        copy_ref[place] = new_master.astype(jnp.bfloat16)


def adam(meta, rates, state, sources):
    count = state[0].shape[0]
    batch = max(size for size in (1, 2, 4) if count % size == 0)
    block = pl.BlockSpec((batch, BLK, BLK), lambda s, *_: (s, 0, 0))
    anywhere = pl.BlockSpec(memory_space=pl.ANY)
    shape = (count, BLK, BLK)
    return pl.pallas_call(
        functools.partial(adam_kernel, batch),
        out_shape=[jax.ShapeDtypeStruct(shape, jnp.float32)] * 3
        + [jax.ShapeDtypeStruct(shape, jnp.bfloat16)],
        grid_spec=pltpu.PrefetchScalarGridSpec(
            num_scalar_prefetch=2,
            grid=(count // batch,),
            in_specs=[block] * 5 + [anywhere] * len(sources),
            out_specs=[block] * 4,
            scratch_shapes=[
                pltpu.VMEM((2, batch, BLK, BLK), jnp.bfloat16),
                pltpu.SemaphoreType.DMA((2,)),
            ],
        ),
        compiler_params=pltpu.CompilerParams(vmem_limit_bytes=32 * 2**20),
        cost_estimate=pl.CostEstimate(
            flops=8 * count * BLK**3, bytes_accessed=36 * count * BLK**2, transcendentals=0
        ),
    )(meta, rates, *state, *sources)


def per_device(
    block_input,
    cotangent,
    glob_select,
    assignment,
    master,
    first_moment,
    second_moment,
    left_basis,
    right_basis,
    gains,
    gain_first,
    gain_second,
):
    band_total = lax.axis_size("fsdp")
    rep_total = lax.axis_size("rep")
    place = lax.axis_index("rep")
    band = lax.axis_index("fsdp")
    heads = H // rep_total
    kv_heads = KVH // rep_total
    q_width = heads * HD
    kv_width = kv_heads * HD
    tok_count = block_input.shape[1]
    own_count = master.shape[1]
    tile_total = own_count * rep_total
    aligned = square() and whole_tiles(band_total, rep_total)
    tile_order = assignment[0]

    residual = block_input[0].astype(jnp.float32)
    grad_top = cotangent[0]
    position = band * tok_count + jnp.arange(tok_count, dtype=jnp.int32)
    cosine_table, sine_table = rope_tables(position)
    wide_cosine = jnp.concatenate([cosine_table, cosine_table], 1)[None]
    wide_sine = jnp.concatenate([sine_table, sine_table], 1)[None]
    scale_one = lax.rsqrt(jnp.mean(residual * residual, -1, keepdims=True) + norm_eps)
    normed_one = (residual * scale_one * gains[0]).astype(jnp.bfloat16)
    pick_rows = glob_select[0]
    glob_total = pick_rows.shape[0]
    selector = pick_rows.astype(jnp.bfloat16)
    glob_pos_part = jnp.sum(pick_rows * position[None, :], 1)
    digits = jnp.concatenate([glob_pos_part // 256, glob_pos_part % 256]).astype(jnp.bfloat16)
    digits = jnp.pad(digits[None], ((0, 7), (0, D - 2 * glob_total)))
    glob_rows = jnp.dot(selector, normed_one, preferred_element_type=jnp.float32).astype(jnp.bfloat16)
    glob_rows = add_all(jnp.concatenate([glob_rows, digits], 0), "fsdp").astype(jnp.bfloat16)
    packed = [normed_one, glob_rows, selector.reshape(-1, D)]
    packed = jnp.concatenate(packed, 0)
    packed = jnp.pad(packed, ((0, -packed.shape[0] % 32), (0, 0)))

    if aligned:
        half = BLK // 2
        slots = square_pieces(master[0, :, :half].astype(jnp.bfloat16))
        *slots, packed = lax.optimization_barrier((*slots, packed))
    packed_all = rep_gather(packed)
    if aligned:
        packed_all, later = lax.optimization_barrier((packed_all, master[0, :, half:].astype(jnp.bfloat16)))
        later_slots = square_pieces(later)
    normed_one_all = packed_all[:, :tok_count].reshape(-1, D)
    at = tok_count + glob_total
    glob_digits = packed_all[:, at, : 2 * glob_total].astype(jnp.float32)
    glob_place = glob_digits[:, :glob_total] * 256.0 + glob_digits[:, glob_total:]
    at += 8
    selector_all = packed_all[:, at : at + selector.size // D].reshape(rep_total, glob_total, tok_count)

    def over_bands(slice_rows):
        return lax.all_gather(slice_rows, "fsdp", axis=0, tiled=True)

    if aligned:
        layout = slice_layout(band_total, rep_total)
        grids = [lax.dynamic_index_in_dim(jnp.asarray(grid), place, 0, False) for grid in layout]
        attn_grid = jnp.concatenate(grids[:4], 1)

        def find(wanted):
            wanted = jnp.take(tile_order, jnp.concatenate([grid.reshape(-1) for grid in wanted]), mode="clip")
            entry, row = (wanted // own_count) ^ place, wanted % own_count
            cut = own_count // 2
            high = (entry == 3) & (row >= cut)
            found = jnp.stack([jnp.where(high, 4, entry), jnp.where(high, row - cut, row)], 0)
            return found.astype(jnp.int32)

        def plan(grid, parts):
            return (*grid.shape, parts)

        first_grid = jnp.concatenate([attn_grid, grids[4]], 1)
        last_grid = jnp.concatenate(grids[4:6], 1)
        first_part, up_part = gather_matrices(
            slots, find([first_grid, grids[5]]), [plan(first_grid, (0,)), plan(grids[5], (0,))]
        )
        early, early_up = over_bands(first_part), over_bands(up_part)
        *later_slots, early = lax.optimization_barrier((*later_slots, early))
        attn_part, last_part, down_part = gather_matrices(
            (*slots, *later_slots),
            find([attn_grid, last_grid, grids[6]]),
            [plan(attn_grid, (1,)), plan(last_grid, (1,)), plan(grids[6], (0, 1))],
        )
        late_attn, late = over_bands(attn_part), over_bands(last_part)

        def woven(early, late):
            rows, cols = early.shape
            both = jnp.stack([early.reshape(-1, half, cols), late.reshape(-1, half, cols)], 1)
            return both.reshape(2 * rows, cols)

        in_width = q_width + 2 * kv_width
        attn_width = late_attn.shape[1]
        w_inner = woven(early[:, :in_width], late_attn[:, :in_width])
        w_output = woven(early[:, in_width:attn_width], late_attn[:, in_width:])
        w_gate = woven(early[:, attn_width:], late[:, : late.shape[1] // 2])
        w_up = woven(early_up, late[:, late.shape[1] // 2 :])
    else:
        slots = lax.all_gather(master[0].astype(jnp.bfloat16), "rep", axis=0, tiled=True)
        tiles = jnp.take(slots, tile_order, axis=0, mode="clip")
        slices = cut_slices(band_matrices(tiles, band_total), band_total, rep_total)
        down_part = slices[6]
        w_inner = over_bands(jnp.concatenate(slices[0:3], 1))
        w_output = over_bands(slices[3])
        w_gate = over_bands(slices[4])
        w_up = over_bands(slices[5])

    w_down = over_bands(down_part)
    w_output = by_place(w_output.reshape(rep_total, q_width, -1)).reshape(D, -1)

    def mul(rows, weight):
        return jnp.dot(rows, weight, preferred_element_type=jnp.float32)

    def mul_back(rows, weight):
        return lax.dot_general(rows, weight, (((1,), (1,)), ((), ())), preferred_element_type=jnp.float32)

    def weight_grad(rows, grad_rows):
        return lax.dot_general(
            rows, grad_rows, (((0,), (0,)), ((), ())), preferred_element_type=jnp.float32
        ).astype(jnp.bfloat16)

    def own_sum(partial):
        return rep_scatter(partial.astype(jnp.bfloat16).reshape(rep_total, tok_count, D))

    grad_top_now, w_inner = lax.optimization_barrier((grad_top, w_inner))
    grad_top_all = rep_gather(grad_top_now).reshape(-1, D)

    inner_rows = mul(packed_all.reshape(-1, D), w_inner).reshape(rep_total, -1, w_inner.shape[1])
    queries, own_pairs = rope_rows(inner_rows, tok_count, 0, q_width, kv_width, wide_cosine, wide_sine)
    glob_cosine, glob_sine = rope_tables(glob_place.reshape(-1))
    glob_cosine = jnp.concatenate([glob_cosine, glob_cosine], 1).reshape(rep_total, glob_total, -1)
    glob_sine = jnp.concatenate([glob_sine, glob_sine], 1).reshape(rep_total, glob_total, -1)
    (glob_pairs,) = rope_rows(
        inner_rows, glob_total, tok_count // glob_total, q_width, kv_width, glob_cosine, glob_sine, False
    )
    back_count = (WINDOW + tok_count - 2) // tok_count
    pair_blocks = [shifted(own_pairs, "fsdp", distance) for distance in range(back_count, 0, -1)]
    pair_blocks = pair_blocks + [own_pairs, glob_pairs]
    glob_spots = jnp.broadcast_to(glob_place[:, :, None], (rep_total, glob_total, BLK))
    band_number = band.astype(jnp.int32).reshape(1)
    queries, grad_top_all = lax.optimization_barrier((queries, grad_top_all))
    attended_low, lse = attend(band_number, glob_spots, queries, pair_blocks)
    attended_all = rep_features(attended_low).reshape(-1, D)
    columns = mul(attended_all, w_output).astype(jnp.bfloat16).reshape(rep_total, tok_count, -1)
    branch = by_place(rep_exchange(columns)).transpose(1, 0, 2).reshape(tok_count, D)
    middle = residual + branch.astype(jnp.float32)
    scale_two = lax.rsqrt(jnp.mean(middle * middle, -1, keepdims=True) + norm_eps)
    normed_two = (middle * scale_two * gains[1]).astype(jnp.bfloat16)
    normed_two_all = rep_gather(normed_two).reshape(-1, D)

    gate_rows = mul(normed_two_all, w_gate)
    up_rows = mul(normed_two_all, w_up)
    sigmoid_gate = jax.nn.sigmoid(gate_rows)
    silu_gate = gate_rows * sigmoid_gate
    activation = (silu_gate * up_rows).astype(jnp.bfloat16)
    g_down = weight_grad(activation, grad_top_all)
    grad_top_all, g_down = lax.optimization_barrier((grad_top_all, g_down))
    grad_act = mul_back(grad_top_all, w_down)
    grad_gate = (
        grad_act * up_rows * sigmoid_gate * (1.0 + gate_rows * (1.0 - sigmoid_gate))
    ).astype(jnp.bfloat16)
    grad_up = (grad_act * silu_gate).astype(jnp.bfloat16)
    grad_normed_two = own_sum(mul_back(grad_gate, w_gate) + mul_back(grad_up, w_up))
    g_gate = weight_grad(normed_two_all, grad_gate)
    g_up = weight_grad(normed_two_all, grad_up)
    grad_normed_two, g_gate, g_up = lax.optimization_barrier((grad_normed_two, g_gate, g_up))
    def over_tokens(partial):
        return lax.psum_scatter(partial, "fsdp", scatter_dimension=0, tiled=True)

    s_down = rep_gather(over_tokens(g_down))
    s_gate = rep_gather(over_tokens(g_gate))
    s_up = over_tokens(g_up)

    grad_middle = grad_top.astype(jnp.float32) + norm_back(middle, scale_two, gains[1], grad_normed_two)
    grad_parts = grad_middle.astype(jnp.bfloat16).reshape(tok_count, rep_total, -1).transpose(1, 0, 2)
    grad_columns = rep_exchange(by_place(grad_parts)).reshape(rep_total * tok_count, -1)
    grad_attended = mul_back(grad_columns, w_output).astype(jnp.bfloat16)
    grad_attended = rep_features_sum(grad_attended.reshape(rep_total, tok_count, D)).astype(jnp.bfloat16)
    g_output = weight_grad(attended_all, grad_columns)
    g_output = by_place(g_output.reshape(rep_total, q_width, -1)).reshape(D, -1)
    grad_attended, s_down = lax.optimization_barrier((grad_attended, s_down))
    grad_queries, *grad_blocks = attend_back(
        band_number, glob_spots, wide_cosine, wide_sine, queries, grad_attended, lse, pair_blocks
    )
    returned = [
        shifted(grad_blocks[back_count - distance], "fsdp", -distance)
        for distance in range(1, back_count + 1)
    ]
    glob_grads = add_all(grad_blocks[-1], "fsdp")
    glob_grads, s_gate, activation = lax.optimization_barrier((glob_grads, s_gate, activation))
    block_out = middle + own_sum(mul(activation, w_down))
    grad_inner = join_grads(
        grad_queries, grad_blocks[-2], selector_all, glob_grads, wide_cosine, wide_sine, returned
    ).reshape(-1, q_width + 2 * kv_width)
    g_inner, s_up = lax.optimization_barrier((weight_grad(normed_one_all, grad_inner), s_up))
    s_attn = over_tokens(jnp.concatenate([g_inner, g_output], 1))
    grad_normed_one = own_sum(mul_back(grad_inner, w_inner))
    grad_input = grad_middle + norm_back(residual, scale_one, gains[0], grad_normed_one)

    slot_ids = jnp.arange(tile_total, dtype=jnp.int32)
    inverse = jnp.sum(jnp.where(tile_order[None, :] == slot_ids[:, None], slot_ids[None, :], 0), 1)
    own_slots = place * own_count + jnp.arange(own_count, dtype=jnp.int32)
    owned_tiles = jnp.take(inverse, own_slots, mode="clip")
    if aligned:
        sources = [rep_gather(s_attn), s_gate, rep_gather(s_up), s_down]
        where = np.zeros((4, rep_total, tile_total), np.int32)
        first_col = 0
        for kind, grid in enumerate(layout):
            rows, cols = grid.shape[1:]
            first_col = 0 if kind >= 4 else first_col
            for there in range(rep_total):
                numbers = grid[there].reshape(-1)
                at = np.arange(rows * cols)
                where[0, :, numbers] = max(kind - 3, 0)
                where[2, :, numbers] = (at // cols * BLK)[:, None]
                where[3, :, numbers] = (at % cols * BLK + first_col)[:, None]
                for here in range(rep_total):
                    where[1, here, numbers] = here ^ there
            first_col += cols * BLK
        tile_spots = lax.dynamic_index_in_dim(jnp.asarray(where), place, 1, False)
        meta = jnp.take(tile_spots, owned_tiles, axis=1, mode="clip")
    else:
        splits = [0, q_width, q_width + kv_width, q_width + 2 * kv_width, s_attn.shape[1]]
        stacks = [rep_gather(s_attn[:, low:high]) for low, high in zip(splits, splits[1:])]
        stacks += [s_gate, rep_gather(s_up), s_down]
        sources = [band_tiles(join_slices(stacks, band_total, rep_total))]
        meta = jnp.stack([0 * owned_tiles, owned_tiles, 0 * owned_tiles, 0 * owned_tiles], 0)
    slot_rates = jnp.take(kind_rates(band_total), owned_tiles, mode="clip")
    new_first, new_second, new_master, master_copy = adam(
        meta,
        slot_rates,
        (master[0], first_moment[0], second_moment[0], left_basis[0], right_basis[0]),
        sources,
    )
    gain_terms = jnp.stack(
        [
            jnp.sum(grad_normed_one * residual * scale_one, 0),
            jnp.sum(grad_normed_two * middle * scale_two, 0),
        ]
    )
    square_terms = jnp.stack(
        [jnp.sum(residual * residual), jnp.sum(middle * middle), jnp.sum(block_out * block_out)]
    )
    sums = jnp.concatenate([gain_terms.reshape(-1), square_terms])
    sums = add_all(add_all(sums, "rep"), "fsdp")
    gain_grad, square_total = sums[: 2 * D].reshape(2, D), sums[2 * D :]
    new_gain_first = beta_one * gain_first + (1.0 - beta_one) * gain_grad
    new_gain_second = beta_two * gain_second + (1.0 - beta_two) * gain_grad * gain_grad
    gain_step = (
        new_gain_first
        / (1.0 - beta_one**STEP)
        / (jnp.sqrt(new_gain_second / (1.0 - beta_two**STEP)) + adam_eps)
    )
    new_gains = gains - gain_rate * gain_step
    rms_stats = jnp.sqrt(square_total / (rep_total * band_total * tok_count * D))
    return (
        block_out[None],
        grad_input[None],
        new_first[None],
        new_second[None],
        new_master[None],
        master_copy[None],
        new_gain_first,
        new_gain_second,
        new_gains,
        rms_stats,
    )


def solution(mesh):
    in_specs = (
        P("rep", "fsdp", None),
        P("rep", "fsdp", None),
        P("rep", None, "fsdp"),
        P("fsdp", None),
        P("fsdp", "rep", None, None),
        P("fsdp", "rep", None, None),
        P("fsdp", "rep", None, None),
        P("fsdp", "rep", None, None),
        P("fsdp", "rep", None, None),
        P(),
        P(),
        P(),
    )
    out_specs = (
        P("rep", "fsdp", None),
        P("rep", "fsdp", None),
        P("fsdp", "rep", None, None),
        P("fsdp", "rep", None, None),
        P("fsdp", "rep", None, None),
        P("fsdp", "rep", None, None),
        P(),
        P(),
        P(),
        P(),
    )
    return jax.shard_map(
        per_device, mesh=mesh, in_specs=in_specs, out_specs=out_specs, check_vma=False
    )
```

```python
import functools

import jax
import jax.numpy as jnp
import numpy as np
from jax import lax
from jax.experimental import pallas as pl
from jax.experimental.pallas import tpu as pltpu
from jax.sharding import PartitionSpec as P

D = 2048
H = 32
KVH = 8
HD = 64
FF = 8192
WINDOW = 512
BLK = 128
STEP = 10


norm_eps = 1e-05
rope_theta = 500000.0
beta_one = 0.5
beta_two = 0.5
adam_eps = 1e-08
weight_decay = 0.1
gain_rate = 0.5
masked_value = -1e30


def matrix_shapes():
    kv_width = KVH * HD
    return [(D, D), (D, kv_width), (D, kv_width), (D, D), (D, FF), (D, FF), (FF, D)]


def kind_rates(band_total):
    rate_list = [
        D ** (-0.5),
        D ** (-0.5),
        D ** (-0.5),
        (D * 8 // WINDOW) ** (-0.5),
        D ** (-0.5),
        D ** (-0.5),
        FF ** (-0.5),
    ]
    pieces = []
    for (row_total, col_total), rate_value in zip(matrix_shapes(), rate_list):
        tile_count = row_total // band_total // BLK * (col_total // BLK)
        pieces.append(jnp.full((tile_count,), rate_value, jnp.float32))
    return jnp.concatenate(pieces)


def band_matrices(tiles, band_total):
    matrices = []
    offset = 0
    for row_total, col_total in matrix_shapes():
        band_rows = row_total // band_total
        tile_count = band_rows // BLK * (col_total // BLK)
        segment = tiles[offset : offset + tile_count].reshape(
            band_rows // BLK, col_total // BLK, BLK, BLK
        )
        matrices.append(segment.transpose(0, 2, 1, 3).reshape(band_rows, col_total))
        offset += tile_count
    return matrices


def band_tiles(matrices):
    pieces = []
    for matrix in matrices:
        row_count, col_count = matrix.shape
        segment = matrix.reshape(row_count // BLK, BLK, col_count // BLK, BLK).transpose(0, 2, 1, 3)
        pieces.append(segment.reshape(-1, BLK, BLK))
    return jnp.concatenate(pieces, 0)


def rope_tables(position):
    halves = jnp.arange(HD // 2, dtype=jnp.float32) * (2.0 / HD)
    frequency = rope_theta ** (-halves)
    angles = position.astype(jnp.float32)[:, None] * frequency[None, :]
    angles = jnp.concatenate([angles, angles], 1)
    return (jnp.cos(angles), jnp.sin(angles))


def rotate(vectors, cosine_table, sine_table):
    half_width = vectors.shape[-1] // 2
    turned = jnp.concatenate([-vectors[..., half_width:], vectors[..., :half_width]], -1)
    return vectors * cosine_table[:, None, :] + turned * sine_table[:, None, :]


def rotate_back(grad_rows, cosine_table, sine_table):
    half_width = grad_rows.shape[-1] // 2
    scaled = grad_rows * sine_table[:, None, :]
    turned = jnp.concatenate([scaled[..., half_width:], -scaled[..., :half_width]], -1)
    return grad_rows * cosine_table[:, None, :] + turned


def norm_back(values, row_scale, gain_row, grad_rows):
    weighted = grad_rows * gain_row
    return row_scale * weighted - values * row_scale**3 * jnp.mean(
        weighted * values, -1, keepdims=True
    )


def to_rep(block, distance):
    route = [(i, i ^ distance) for i in range(lax.axis_size("rep"))]
    return lax.ppermute(block, "rep", route)


def square():
    return lax.axis_size("rep") == 4


def square_pieces(block):
    cut = block.shape[0] // 2
    near = to_rep(block, 1)
    far = to_rep(block, 2)
    return block, near, far, to_rep(near[:cut], 2), to_rep(far[cut:], 1)


def rep_gather(block):
    if not square():
        return lax.all_gather(block, "rep", axis=0)
    own, near, far, low, high = square_pieces(block)
    return jnp.concatenate([own, near, far, low, high], 0).reshape((4,) + block.shape)


def rep_of(entry):
    place = lax.axis_index("rep")
    return place ^ entry if square() else entry


def rep_scatter(parts):
    if not square():
        flat = parts.reshape(-1, parts.shape[-1])
        return lax.psum_scatter(flat, "rep", scatter_dimension=0, tiled=True).astype(jnp.float32)
    half = parts.shape[-1] // 2
    totals = []
    for side, (first, second) in ((parts[..., :half], (1, 2)), (parts[..., half:], (2, 1))):
        away = to_rep(jnp.stack([side[first], side[3]], 0), first)
        other = (side[second].astype(jnp.float32) + away[1].astype(jnp.float32)).astype(parts.dtype)
        own = side[0].astype(jnp.float32) + away[0].astype(jnp.float32)
        totals.append(own + to_rep(other, second).astype(jnp.float32))
    return jnp.concatenate(totals, -1)


def add_all(value, axis):
    size = lax.axis_size(axis)
    total = value.astype(jnp.float32)
    distance = 1
    while distance < size:
        count = 2 if (size // distance).bit_length() % 2 == 0 else 4
        low = total.astype(value.dtype)
        others = []
        for step in range(1, count):
            route = [(i, i ^ (step * distance)) for i in range(size)]
            others.append(lax.ppermute(low, axis, route).astype(jnp.float32))
        total = total + others[0]
        if count == 4:
            total = total + (others[1] + others[2])
        distance *= count
    return total


def rep_features(block):
    if not square():
        return lax.all_gather(block, "rep", axis=2, tiled=True)
    own, near, far, low, high = square_pieces(block)
    return jnp.concatenate(
        [
            own,
            jnp.stack([near[1], near[0], near[3], near[2]], 0),
            jnp.stack([far[2], far[3], far[0], far[1]], 0),
            jnp.stack([high[1], high[0], low[1], low[0]], 0),
        ],
        2,
    )


def swapped_kernel(x_ref, w_ref, out_ref):
    out_ref[0, 0] = over_last(x_ref[0], w_ref[...]).astype(jnp.bfloat16)


def rep_features_sum(columns, weight):
    reps, rows, depth = columns.shape
    width = weight.shape[0] // reps
    if square():
        swapped = pl.pallas_call(
            swapped_kernel,
            out_shape=jax.ShapeDtypeStruct((reps, reps, rows, width), jnp.bfloat16),
            grid=(reps, reps),
            in_specs=[
                pl.BlockSpec((1, rows, depth), lambda q, p: (p ^ q, 0, 0)),
                pl.BlockSpec((width, depth), lambda q, p: (q, 0)),
            ],
            out_specs=pl.BlockSpec((1, 1, rows, width), lambda q, p: (q, p, 0, 0)),
            cost_estimate=pl.CostEstimate(
                flops=2 * reps * columns.size * width,
                bytes_accessed=10 * columns.size,
                transcendentals=0,
            ),
        )(columns, weight)
    else:
        product = over_last(columns.reshape(-1, depth), weight).astype(jnp.bfloat16)
        swapped = product.reshape(reps, rows, reps, width).transpose(2, 0, 1, 3)
    total = rep_scatter(swapped.reshape(reps, reps * rows, width))
    return total.reshape(reps, rows, width)


def rep_exchange(parts):
    if not square():
        return lax.all_to_all(parts, "rep", 0, 0)
    return jnp.stack([parts[0]] + [to_rep(parts[entry], entry) for entry in (1, 2, 3)], 0)


def by_place(parts):
    entries = [rep_of(entry) for entry in range(parts.shape[0])]
    return jnp.stack([lax.dynamic_index_in_dim(parts, entry, 0, False) for entry in entries], 0)


def shifted(block, axis, distance):
    devices = range(lax.axis_size(axis))
    route = [(i - distance, i) for i in devices if i - distance in devices]
    return lax.ppermute(block, axis, route)


def tile_offsets(band_total):
    offsets = [0]
    for row_total, col_total in matrix_shapes():
        offsets.append(offsets[-1] + row_total // band_total // BLK * (col_total // BLK))
    return offsets


def whole_tiles(band_total, rep_total):
    return KVH * HD // rep_total % BLK == 0 and FF // band_total // rep_total % BLK == 0


def slice_layout(band_total, rep_total):
    offsets = tile_offsets(band_total)
    layout = []
    for kind, (row_total, col_total) in enumerate(matrix_shapes()):
        rows, cols = row_total // band_total // BLK, col_total // BLK
        grid = offsets[kind] + np.arange(rows * cols).reshape(rows, cols)
        if kind == 6:
            layout.append(grid.reshape(rep_total, rows // rep_total, cols))
        elif kind in (4, 5):
            cut = grid.reshape(rows, band_total, rep_total, -1).transpose(2, 0, 1, 3)
            layout.append(cut.reshape(rep_total, rows, -1))
        else:
            layout.append(grid.reshape(rows, rep_total, -1).transpose(1, 0, 2))
    return layout


def tiles_to_matrix(tiles):
    rows, cols = tiles.shape[:2]
    return tiles.transpose(0, 2, 1, 3).reshape(rows * BLK, cols * BLK)


def matrix_to_tiles(matrix):
    rows, cols = matrix.shape
    cut = matrix.reshape(rows // BLK, BLK, cols // BLK, BLK)
    return cut.transpose(0, 2, 1, 3).reshape(-1, BLK, BLK)


def cut_slices(matrices, band_total, rep_total):
    place = lax.axis_index("rep")
    slices = []
    for kind, matrix in enumerate(matrices):
        rows, cols = matrix.shape
        if kind == 6:
            slices.append(lax.dynamic_slice_in_dim(matrix, place * (rows // rep_total), rows // rep_total, 0))
        elif kind in (4, 5):
            cut = matrix.reshape(rows, band_total, rep_total, -1)
            slices.append(lax.dynamic_index_in_dim(cut, place, 2, False).reshape(rows, -1))
        else:
            slices.append(lax.dynamic_slice_in_dim(matrix, place * (cols // rep_total), cols // rep_total, 1))
    return slices


def join_slices(stacks, band_total, rep_total):
    matrices = []
    for kind, stack in enumerate(stacks):
        rows, cols = stack.shape[1:]
        if kind == 6:
            matrices.append(stack.reshape(-1, cols))
        elif kind in (4, 5):
            cut = stack.reshape(rep_total, rows, band_total, -1).transpose(1, 2, 0, 3)
            matrices.append(cut.reshape(rows, -1))
        else:
            matrices.append(stack.transpose(1, 0, 2).reshape(rows, -1))
    return matrices


def gather_kernel(plans, meta, *refs):
    source_total = len(refs) - len(plans) - 1
    sources, targets, done = refs[:source_total], refs[source_total:-1], refs[-1]
    piece_total = source_total // max(len(parts) for _, _, parts in plans)
    start = 0
    for place, (target, (rows, cols, parts)) in enumerate(zip(targets, plans)):
        height = sources[0].shape[1]

        def one(tile, carry, target=target, cols=cols, parts=parts, start=start, place=place, height=height):
            kind = meta[0, start + tile]
            row = meta[1, start + tile]
            top = tile // cols * (height * len(parts))
            left = pl.multiple_of(tile % cols * BLK, BLK)
            for number in range(piece_total):

                @pl.when(kind == number)
                def _(number=number):
                    for order, part in enumerate(parts):
                        first = pl.multiple_of(top + order * height, height)
                        pltpu.make_async_copy(
                            sources[part * piece_total + number].at[row],
                            target.at[pl.ds(first, height), pl.ds(left, BLK)],
                            done.at[place],
                        ).start()

            return carry

        lax.fori_loop(0, rows * cols, one, 0)
        start += rows * cols
    for place, target in enumerate(targets):
        pltpu.make_async_copy(target, target, done.at[place]).wait()


def gather_matrices(sources, meta, plans):
    anywhere = pl.BlockSpec(memory_space=pl.ANY)
    height = sources[0].shape[1]
    out_shape = [
        jax.ShapeDtypeStruct((rows * height * len(parts), cols * BLK), jnp.bfloat16)
        for rows, cols, parts in plans
    ]
    moved = sum(4 * shape.size for shape in out_shape)
    return pl.pallas_call(
        functools.partial(gather_kernel, plans),
        out_shape=out_shape,
        grid_spec=pltpu.PrefetchScalarGridSpec(
            num_scalar_prefetch=1,
            grid=(1,),
            in_specs=[anywhere] * len(sources),
            out_specs=[pl.BlockSpec(shape.shape, lambda i, *_: (0, 0)) for shape in out_shape],
            scratch_shapes=[pltpu.SemaphoreType.DMA((len(plans),))],
        ),
        compiler_params=pltpu.CompilerParams(vmem_limit_bytes=32 * 2**20),
        cost_estimate=pl.CostEstimate(flops=0, bytes_accessed=moved, transcendentals=0),
    )(meta, *sources)


def place_kernel(entries, rows, cols, meta, low, high, out_ref, done):
    out_ref[...] = jnp.zeros_like(out_ref)
    height = low.shape[1]

    def copies(tile):
        entry, rest = tile // (rows * cols), tile % (rows * cols)
        top = rest // cols * (2 * height)
        left = pl.multiple_of(rest % cols * BLK, BLK)
        return [
            pltpu.make_async_copy(
                half.at[meta[1, tile]],
                out_ref.at[entry, pl.ds(pl.multiple_of(top + part * height, height), height), pl.ds(left, BLK)],
                done.at[part],
            )
            for part, half in enumerate((low, high))
        ]

    def begin(tile, carry):
        @pl.when(meta[0, tile] == 1)
        def _():
            for copy in copies(tile):
                copy.start()

        return carry

    def finish(tile, carry):
        @pl.when(meta[0, tile] == 1)
        def _():
            for copy in copies(tile):
                copy.wait()

        return carry

    lax.fori_loop(0, entries * rows * cols, begin, 0)
    lax.fori_loop(0, entries * rows * cols, finish, 0)


def place_tiles(low, high, meta, entries, rows, cols):
    shape = (entries, rows * BLK, cols * BLK)
    anywhere = pl.BlockSpec(memory_space=pl.ANY)
    return pl.pallas_call(
        functools.partial(place_kernel, entries, rows, cols),
        out_shape=jax.ShapeDtypeStruct(shape, jnp.bfloat16),
        grid_spec=pltpu.PrefetchScalarGridSpec(
            num_scalar_prefetch=1,
            grid=(1,),
            in_specs=[anywhere, anywhere],
            out_specs=pl.BlockSpec(shape, lambda i, *_: (0, 0, 0)),
            scratch_shapes=[pltpu.SemaphoreType.DMA((2,))],
        ),
        compiler_params=pltpu.CompilerParams(vmem_limit_bytes=32 * 2**20),
        cost_estimate=pl.CostEstimate(
            flops=0, bytes_accessed=4 * entries * rows * cols * BLK * BLK, transcendentals=0
        ),
    )(meta, low, high)


def half_turn(values):
    lane = lax.broadcasted_iota(jnp.int32, values.shape, 1)
    lanes = values.shape[1]
    first = lane % HD < HD // 2
    return first, jnp.where(
        first, pltpu.roll(values, lanes - HD // 2, 1), pltpu.roll(values, HD // 2, 1)
    )


def rope_kernel(q_width, kv_width, x_ref, cos_ref, sin_ref, *outs):
    width = x_ref.shape[-1]
    for start in range(0, width, BLK):
        values = x_ref[0, :, start : start + BLK]
        first, turned = half_turn(values)
        sines = sin_ref[0]
        turned_rows = values * cos_ref[0] + turned * jnp.where(first, -sines, sines)
        if start + BLK > q_width + kv_width:
            column = lax.broadcasted_iota(jnp.int32, values.shape, 1) + start
            turned_rows = jnp.where(column >= q_width + kv_width, values, turned_rows)
        if start < q_width:
            outs[0][0, :, start : start + BLK] = (turned_rows * HD ** (-0.5)).astype(jnp.bfloat16)
        else:
            outs[-1][0, :, start - q_width : start - q_width + BLK] = turned_rows.astype(jnp.bfloat16)


def rope_rows(inner, rows, row_block, q_width, kv_width, cosines, sines, with_queries=True):
    seqs, _, width = inner.shape
    shared = cosines.shape[0] == 1
    table = pl.BlockSpec((1, rows, BLK), lambda s: (0 if shared else s, 0, 0))
    widths = [q_width, 2 * kv_width]
    column_block = 0
    if not with_queries:
        width, column_block = 2 * kv_width, q_width // (2 * kv_width)
        widths, q_width = widths[1:], 0
    return pl.pallas_call(
        functools.partial(rope_kernel, q_width, kv_width),
        out_shape=[jax.ShapeDtypeStruct((seqs, rows, w), jnp.bfloat16) for w in widths],
        grid=(seqs,),
        in_specs=[pl.BlockSpec((1, rows, width), lambda s: (s, row_block, column_block)), table, table],
        out_specs=[pl.BlockSpec((1, rows, w), lambda s: (s, 0, 0)) for w in widths],
        cost_estimate=pl.CostEstimate(
            flops=6 * seqs * rows * width, bytes_accessed=6 * seqs * rows * width, transcendentals=0
        ),
    )(inner, cosines, sines)


def fill_bias(band_ref, gpos_ref, bias_ref, rows, window_len):
    band = band_ref[0]

    @pl.when(pl.program_id(0) == 0)
    def _():
        key = lax.broadcasted_iota(jnp.int32, (window_len, rows), 0) + (
            band * rows - (window_len - rows)
        )
        query = lax.broadcasted_iota(jnp.int32, (window_len, rows), 1) + band * rows
        inside = (key > query - WINDOW) & (key <= query) & (key >= 0)
        bias_ref[:window_len] = jnp.where(inside, 0.0, masked_value)

    glob_total = gpos_ref.shape[1]
    query = lax.broadcasted_iota(jnp.int32, (glob_total, rows), 1) + (band * rows - WINDOW)
    spot = jnp.broadcast_to(gpos_ref[0][:, :1], (glob_total, rows))
    bias_ref[window_len:] = jnp.where(spot <= query.astype(jnp.float32), 0.0, masked_value)


def over_last(left, right):
    return lax.dot_general(left, right, (((1,), (1,)), ((), ())), preferred_element_type=jnp.float32)


def over_first(left, right):
    return lax.dot_general(left, right, (((0,), (0,)), ((), ())), preferred_element_type=jnp.float32)


def attend_kernel(block_total, band_ref, gpos_ref, q_ref, *refs):
    blocks, (out_ref, lse_ref, bias_ref) = refs[:block_total], refs[block_total:]
    rows, q_width = q_ref.shape[1:]
    kv_width = blocks[0].shape[2] // 2
    heads, group = q_width // HD, q_width // kv_width
    window_len = rows * (block_total - 1)
    fill_bias(band_ref, gpos_ref, bias_ref, rows, window_len)
    starts = [rows * number for number in range(block_total)]
    pending = []
    for head in range(heads):
        left = head // group * HD
        queries = q_ref[0, :, head * HD : (head + 1) * HD]
        scores = [
            over_last(block[0, :, left : left + HD], queries)
            + bias_ref[start : start + block.shape[1]]
            for block, start in zip(blocks, starts)
        ]
        top = functools.reduce(jnp.maximum, [jnp.max(part, 0, keepdims=True) for part in scores])
        total = 0.0
        mixed = 0.0
        for block, part in zip(blocks, scores):
            weights = jnp.exp(part - top)
            total = total + jnp.sum(weights, 0, keepdims=True)
            mixed = mixed + over_first(
                block[0, :, kv_width + left : kv_width + left + HD], weights.astype(jnp.bfloat16)
            )
        lse_ref[0, head : head + 1, :] = top + jnp.log(total)
        pending.append(mixed / total)
        if len(pending) * HD == BLK or head == heads - 1:
            stop = (head + 1) * HD
            both = jnp.concatenate(pending, 0).T
            out_ref[0, :, stop - both.shape[1] : stop] = both.astype(jnp.bfloat16)
            pending = []


def attend(band, gpos, queries, blocks):
    seqs, rows, q_width = queries.shape
    heads = q_width // HD
    key_total = sum(block.shape[1] for block in blocks)

    def whole(array):
        return pl.BlockSpec((1,) + array.shape[1:], lambda s, *_: (s, 0, 0))

    out_shape = [
        jax.ShapeDtypeStruct((seqs, rows, q_width), jnp.bfloat16),
        jax.ShapeDtypeStruct((seqs, heads, rows), jnp.float32),
    ]
    return pl.pallas_call(
        functools.partial(attend_kernel, len(blocks)),
        out_shape=out_shape,
        grid_spec=pltpu.PrefetchScalarGridSpec(
            num_scalar_prefetch=1,
            grid=(seqs,),
            in_specs=[whole(array) for array in (gpos, queries, *blocks)],
            out_specs=[whole(array) for array in out_shape],
            scratch_shapes=[pltpu.VMEM((key_total, rows), jnp.float32)],
        ),
        compiler_params=pltpu.CompilerParams(vmem_limit_bytes=48 * 2**20),
        cost_estimate=pl.CostEstimate(
            flops=16 * seqs * heads * rows * key_total * HD,
            bytes_accessed=4 * queries.size,
            transcendentals=seqs * heads * rows * key_total,
        ),
    )(band, gpos, queries, *blocks)


def attend_back_kernel(block_total, band_ref, gpos_ref, cos_ref, sin_ref, q_ref, grad_ref, lse_ref, *refs):
    blocks = refs[:block_total]
    dq_ref = refs[block_total]
    out_refs = refs[block_total + 1 : 2 * block_total + 1]
    bias_ref = refs[-1]
    rows, q_width = q_ref.shape[1:]
    kv_width = blocks[0].shape[2] // 2
    heads, group = q_width // HD, q_width // kv_width
    window_len = rows * (block_total - 1)
    fill_bias(band_ref, gpos_ref, bias_ref, rows, window_len)
    starts = [rows * number for number in range(block_total)]
    pending = []
    for kv_head in range(kv_width // HD):
        left = kv_head * HD
        key_sums = [0.0] * block_total
        value_sums = [0.0] * block_total
        for head in range(kv_head * group, (kv_head + 1) * group):
            queries = q_ref[0, :, head * HD : (head + 1) * HD]
            grads = grad_ref[0, :, head * HD : (head + 1) * HD]
            lse = lse_ref[0, head : head + 1, :]
            soft, soft_grads = [], []
            inner = 0.0
            for number, (block, start) in enumerate(zip(blocks, starts)):
                part = over_last(block[0, :, left : left + HD], queries)
                part = jnp.exp(part + bias_ref[start : start + block.shape[1]] - lse)
                slope = over_last(block[0, :, kv_width + left : kv_width + left + HD], grads)
                inner = inner + jnp.sum(part * slope, 0, keepdims=True)
                soft.append(part)
                soft_grads.append(slope)
            turned = 0.0
            for number, block in enumerate(blocks):
                score_grads = (soft[number] * (soft_grads[number] - inner)).astype(jnp.bfloat16)
                value_sums[number] = value_sums[number] + jnp.dot(
                    soft[number].astype(jnp.bfloat16), grads, preferred_element_type=jnp.float32
                )
                key_sums[number] = key_sums[number] + jnp.dot(
                    score_grads, queries, preferred_element_type=jnp.float32
                )
                turned = turned + over_first(block[0, :, left : left + HD], score_grads)
            pending.append(turned)
            if len(pending) * HD == BLK or head == heads - 1:
                stop = (head + 1) * HD
                both = jnp.concatenate(pending, 0).T * HD ** (-0.5)
                pending = []
                first, other = half_turn(both * sin_ref[0])
                both = both * cos_ref[0] + jnp.where(first, other, -other)
                dq_ref[0, :, stop - both.shape[1] : stop] = both.astype(jnp.bfloat16)
        for number, out_ref in enumerate(out_refs):
            out_ref[0, :, left : left + HD] = key_sums[number].astype(out_ref.dtype)
            out_ref[0, :, kv_width + left : kv_width + left + HD] = value_sums[number].astype(
                out_ref.dtype
            )


def attend_back(band, gpos, cosines, sines, queries, grads, lse, blocks):
    seqs, rows, q_width = queries.shape
    heads = q_width // HD
    key_total = sum(block.shape[1] for block in blocks)

    def whole(array):
        return pl.BlockSpec((1,) + array.shape[1:], lambda s, *_: (s, 0, 0))

    table = pl.BlockSpec((1, rows, BLK), lambda s, *_: (0, 0, 0))
    out_shape = [jax.ShapeDtypeStruct(queries.shape, jnp.bfloat16)]
    for number, block in enumerate(blocks):
        own = number == len(blocks) - 2
        out_shape.append(jax.ShapeDtypeStruct(block.shape, jnp.float32 if own else jnp.bfloat16))
    return pl.pallas_call(
        functools.partial(attend_back_kernel, len(blocks)),
        out_shape=out_shape,
        grid_spec=pltpu.PrefetchScalarGridSpec(
            num_scalar_prefetch=1,
            grid=(seqs,),
            in_specs=[whole(gpos), table, table]
            + [whole(array) for array in (queries, grads, lse, *blocks)],
            out_specs=[whole(array) for array in out_shape],
            scratch_shapes=[pltpu.VMEM((key_total, rows), jnp.float32)],
        ),
        compiler_params=pltpu.CompilerParams(vmem_limit_bytes=48 * 2**20),
        cost_estimate=pl.CostEstimate(
            flops=40 * seqs * heads * rows * key_total * HD,
            bytes_accessed=8 * queries.size,
            transcendentals=seqs * heads * rows * key_total,
        ),
    )(band, gpos, cosines, sines, queries, grads, lse, *blocks)


def join_kernel(q_width, kv_width, dq_ref, own_ref, pick_ref, glob_ref, cos_ref, sin_ref, *refs):
    back_refs, out_ref = refs[:-1], refs[-1]
    out_ref[0, :, :q_width] = dq_ref[0]
    picked = lax.dot_general(
        pick_ref[0].astype(jnp.float32),
        glob_ref[0],
        (((0,), (0,)), ((), ())),
        precision=lax.Precision.HIGHEST,
        preferred_element_type=jnp.float32,
    )
    for start in range(0, 2 * kv_width, BLK):
        lanes = slice(start, start + BLK)
        total = own_ref[0, :, lanes] + picked[:, lanes]
        for back_ref in back_refs:
            total = total + back_ref[0, :, lanes].astype(jnp.float32)
        first, other = half_turn(total * sin_ref[0])
        turned = total * cos_ref[0] + jnp.where(first, other, -other)
        column = lax.broadcasted_iota(jnp.int32, total.shape, 1) + start
        turned = jnp.where(column >= kv_width, total, turned)
        out_ref[0, :, q_width + start : q_width + start + BLK] = turned.astype(jnp.bfloat16)


def join_grads(dq, own, picks, globs, cosines, sines, backs):
    seqs, rows, q_width = dq.shape
    kv_width = own.shape[2] // 2

    def whole(array):
        return pl.BlockSpec((1,) + array.shape[1:], lambda s: (s, 0, 0))

    table = pl.BlockSpec((1, rows, BLK), lambda s: (0, 0, 0))
    out_shape = jax.ShapeDtypeStruct((seqs, rows, q_width + 2 * kv_width), jnp.bfloat16)
    return pl.pallas_call(
        functools.partial(join_kernel, q_width, kv_width),
        out_shape=out_shape,
        grid=(seqs,),
        in_specs=[whole(dq), whole(own), whole(picks), whole(globs), table, table]
        + [whole(back) for back in backs],
        out_specs=whole(out_shape),
        cost_estimate=pl.CostEstimate(
            flops=20 * own.size, bytes_accessed=4 * dq.size + 12 * own.size, transcendentals=0
        ),
    )(dq, own, picks, globs, cosines, sines, *backs)


def adam_kernel(batch, meta, rates, *refs):
    master_ref, first_ref, second_ref, left_ref, right_ref = refs[:5]
    sources = refs[5:-6]
    new_first_ref, new_second_ref, new_master_ref, copy_ref, tiles, arrived = refs[-6:]
    step, steps = pl.program_id(0), pl.num_programs(0)
    slot = step % 2

    def fetch(at_step, at_slot):
        for place in range(batch):
            tile = at_step * batch + place
            for number, source in enumerate(sources):

                @pl.when(meta[0, tile] == number)
                def _(source=source, tile=tile, place=place):
                    top = pl.multiple_of(meta[2, tile], BLK)
                    left = pl.multiple_of(meta[3, tile], BLK)
                    pltpu.make_async_copy(
                        source.at[meta[1, tile], pl.ds(top, BLK), pl.ds(left, BLK)],
                        tiles.at[at_slot, place],
                        arrived.at[at_slot],
                    ).start()

    @pl.when(step == 0)
    def _():
        fetch(0, 0)

    @pl.when(step + 1 < steps)
    def _():
        fetch(step + 1, 1 - slot)

    pltpu.make_async_copy(tiles.at[slot], tiles.at[slot], arrived.at[slot]).wait()
    places = range(batch)
    lefts = [left_ref[place].astype(jnp.bfloat16) for place in places]
    rights = [right_ref[place].astype(jnp.bfloat16) for place in places]
    turned = [over_first(lefts[place], tiles[slot, place]).astype(jnp.bfloat16) for place in places]
    rotated = [
        jnp.dot(turned[place], rights[place], preferred_element_type=jnp.float32) for place in places
    ]
    directions = []
    for place in places:
        new_first = beta_one * first_ref[place] + (1.0 - beta_one) * rotated[place]
        new_second = beta_two * second_ref[place] + (1.0 - beta_two) * rotated[place] * rotated[place]
        direction = (
            new_first
            / (1.0 - beta_one**STEP)
            / (jnp.sqrt(new_second / (1.0 - beta_two**STEP)) + adam_eps)
        )
        new_first_ref[place] = new_first
        new_second_ref[place] = new_second
        directions.append(direction.astype(jnp.bfloat16))
    updates = [
        jnp.dot(lefts[place], directions[place], preferred_element_type=jnp.float32) for place in places
    ]
    updates = [over_last(updates[place].astype(jnp.bfloat16), rights[place]) for place in places]
    for place in places:
        old = master_ref[place]
        new_master = old - rates[step * batch + place] * (updates[place] + weight_decay * old)
        new_master_ref[place] = new_master
        copy_ref[place] = new_master.astype(jnp.bfloat16)


def adam(meta, rates, state, sources):
    count = state[0].shape[0]
    batch = max(size for size in (1, 2, 4) if count % size == 0)
    block = pl.BlockSpec((batch, BLK, BLK), lambda s, *_: (s, 0, 0))
    anywhere = pl.BlockSpec(memory_space=pl.ANY)
    shape = (count, BLK, BLK)
    return pl.pallas_call(
        functools.partial(adam_kernel, batch),
        out_shape=[jax.ShapeDtypeStruct(shape, jnp.float32)] * 3
        + [jax.ShapeDtypeStruct(shape, jnp.bfloat16)],
        grid_spec=pltpu.PrefetchScalarGridSpec(
            num_scalar_prefetch=2,
            grid=(count // batch,),
            in_specs=[block] * 5 + [anywhere] * len(sources),
            out_specs=[block] * 4,
            scratch_shapes=[
                pltpu.VMEM((2, batch, BLK, BLK), jnp.bfloat16),
                pltpu.SemaphoreType.DMA((2,)),
            ],
        ),
        compiler_params=pltpu.CompilerParams(vmem_limit_bytes=32 * 2**20),
        cost_estimate=pl.CostEstimate(
            flops=8 * count * BLK**3, bytes_accessed=36 * count * BLK**2, transcendentals=0
        ),
    )(meta, rates, *state, *sources)


def per_device(
    block_input,
    cotangent,
    glob_select,
    assignment,
    master,
    first_moment,
    second_moment,
    left_basis,
    right_basis,
    gains,
    gain_first,
    gain_second,
):
    band_total = lax.axis_size("fsdp")
    rep_total = lax.axis_size("rep")
    place = lax.axis_index("rep")
    band = lax.axis_index("fsdp")
    heads = H // rep_total
    kv_heads = KVH // rep_total
    q_width = heads * HD
    kv_width = kv_heads * HD
    tok_count = block_input.shape[1]
    own_count = master.shape[1]
    tile_total = own_count * rep_total
    aligned = square() and whole_tiles(band_total, rep_total)
    tile_order = assignment[0]

    residual = block_input[0].astype(jnp.float32)
    grad_top = cotangent[0]
    position = band * tok_count + jnp.arange(tok_count, dtype=jnp.int32)
    cosine_table, sine_table = rope_tables(position)
    wide_cosine = jnp.concatenate([cosine_table, cosine_table], 1)[None]
    wide_sine = jnp.concatenate([sine_table, sine_table], 1)[None]
    scale_one = lax.rsqrt(jnp.mean(residual * residual, -1, keepdims=True) + norm_eps)
    normed_one = (residual * scale_one * gains[0]).astype(jnp.bfloat16)
    pick_rows = glob_select[0]
    glob_total = pick_rows.shape[0]
    selector = pick_rows.astype(jnp.bfloat16)
    glob_pos_part = jnp.sum(pick_rows * position[None, :], 1)
    digits = jnp.concatenate([glob_pos_part // 256, glob_pos_part % 256]).astype(jnp.bfloat16)
    digits = jnp.pad(digits[None], ((0, 7), (0, D - 2 * glob_total)))
    glob_rows = jnp.dot(selector, normed_one, preferred_element_type=jnp.float32).astype(jnp.bfloat16)
    glob_rows = add_all(jnp.concatenate([glob_rows, digits], 0), "fsdp").astype(jnp.bfloat16)
    packed = [normed_one, glob_rows, selector.reshape(-1, D)]
    packed = jnp.concatenate(packed, 0)
    packed = jnp.pad(packed, ((0, -packed.shape[0] % 32), (0, 0)))

    if aligned:
        half = BLK // 2
        low, high = (master[0, :, rows].astype(jnp.bfloat16) for rows in (slice(0, half), slice(half, BLK)))
        layout = slice_layout(band_total, rep_total)
        attn_layout = jnp.asarray(np.concatenate(layout[:4], 2))
        wanted = jnp.take(tile_order, by_place(attn_layout).reshape(-1), mode="clip")
        meta = jnp.stack([wanted // own_count == place, wanted % own_count], 0).astype(jnp.int32)
        attn_part = place_tiles(low, high, meta, *attn_layout.shape)
        attn_part = rep_scatter(attn_part).astype(jnp.bfloat16)
        low, attn_part = lax.optimization_barrier((low, attn_part))
        slots = square_pieces(low)
        *slots, packed = lax.optimization_barrier((*slots, packed))
    packed_all = rep_gather(packed)
    if aligned:
        packed_all, high = lax.optimization_barrier((packed_all, high))
        later_slots = square_pieces(high)
    normed_one_all = packed_all[:, :tok_count].reshape(-1, D)
    at = tok_count + glob_total
    glob_digits = packed_all[:, at, : 2 * glob_total].astype(jnp.float32)
    glob_place = glob_digits[:, :glob_total] * 256.0 + glob_digits[:, glob_total:]
    at += 8
    selector_all = packed_all[:, at : at + selector.size // D].reshape(rep_total, glob_total, tok_count)

    def over_bands(slice_rows):
        return lax.all_gather(slice_rows, "fsdp", axis=0, tiled=True)

    if aligned:
        grids = [lax.dynamic_index_in_dim(jnp.asarray(grid), place, 0, False) for grid in layout]

        def find(wanted):
            wanted = jnp.take(tile_order, jnp.concatenate([grid.reshape(-1) for grid in wanted]), mode="clip")
            entry, row = (wanted // own_count) ^ place, wanted % own_count
            cut = own_count // 2
            high = (entry == 3) & (row >= cut)
            found = jnp.stack([jnp.where(high, 4, entry), jnp.where(high, row - cut, row)], 0)
            return found.astype(jnp.int32)

        def plan(grid, parts):
            return (*grid.shape, parts)

        first_grid = jnp.concatenate(grids[4:6], 1)
        attn = over_bands(attn_part)
        first_part, down_part = gather_matrices(
            slots, find([first_grid, grids[6]]), [plan(first_grid, (0,)), plan(grids[6], (0,))]
        )
        down_rows, down_cols = down_part.shape
        first_part = jnp.concatenate([first_part, down_part.reshape(first_part.shape[0], -1)], 1)
        early = over_bands(first_part)
        *later_slots, early = lax.optimization_barrier((*later_slots, early))
        last_part, down_part = gather_matrices(
            later_slots, find([first_grid, grids[6]]), [plan(first_grid, (0,)), plan(grids[6], (0,))]
        )
        late, late_down = over_bands(last_part), over_bands(down_part)

        def woven(early, late):
            rows, cols = early.shape
            both = jnp.stack([early.reshape(-1, half, cols), late.reshape(-1, half, cols)], 1)
            return both.reshape(2 * rows, cols)

        in_width = q_width + 2 * kv_width
        w_inner, w_output = attn[:, :in_width], attn[:, in_width:]
        width = late.shape[1] // 2
        w_gate = woven(early[:, :width], late[:, :width])
        w_up = woven(early[:, width : 2 * width], late[:, width:])
        w_down = woven(early[:, 2 * width :].reshape(-1, down_cols), late_down)
    else:
        slots = lax.all_gather(master[0].astype(jnp.bfloat16), "rep", axis=0, tiled=True)
        tiles = jnp.take(slots, tile_order, axis=0, mode="clip")
        slices = cut_slices(band_matrices(tiles, band_total), band_total, rep_total)
        w_inner = over_bands(jnp.concatenate(slices[0:3], 1))
        w_output = over_bands(slices[3])
        w_gate = over_bands(slices[4])
        w_up = over_bands(slices[5])
        w_down = over_bands(slices[6])

    w_output = by_place(w_output.reshape(rep_total, q_width, -1)).reshape(D, -1)

    def mul(rows, weight):
        return jnp.dot(rows, weight, preferred_element_type=jnp.float32)

    def mul_back(rows, weight):
        return lax.dot_general(rows, weight, (((1,), (1,)), ((), ())), preferred_element_type=jnp.float32)

    def weight_grad(rows, grad_rows):
        return lax.dot_general(
            rows, grad_rows, (((0,), (0,)), ((), ())), preferred_element_type=jnp.float32
        ).astype(jnp.bfloat16)

    def own_sum(partial):
        return rep_scatter(partial.astype(jnp.bfloat16).reshape(rep_total, tok_count, D))

    inner_rows = mul(packed_all.reshape(-1, D), w_inner).reshape(rep_total, -1, w_inner.shape[1])
    queries, own_pairs = rope_rows(inner_rows, tok_count, 0, q_width, kv_width, wide_cosine, wide_sine)
    glob_cosine, glob_sine = rope_tables(glob_place.reshape(-1))
    glob_cosine = jnp.concatenate([glob_cosine, glob_cosine], 1).reshape(rep_total, glob_total, -1)
    glob_sine = jnp.concatenate([glob_sine, glob_sine], 1).reshape(rep_total, glob_total, -1)
    (glob_pairs,) = rope_rows(
        inner_rows, glob_total, tok_count // glob_total, q_width, kv_width, glob_cosine, glob_sine, False
    )
    back_count = (WINDOW + tok_count - 2) // tok_count
    pair_blocks = [shifted(own_pairs, "fsdp", distance) for distance in range(back_count, 0, -1)]
    pair_blocks = pair_blocks + [own_pairs, glob_pairs]
    glob_spots = jnp.broadcast_to(glob_place[:, :, None], (rep_total, glob_total, BLK))
    band_number = band.astype(jnp.int32).reshape(1)
    attended_low, lse = attend(band_number, glob_spots, queries, pair_blocks)
    attended_all = rep_features(attended_low).reshape(-1, D)
    attended_all, grad_top_now = lax.optimization_barrier((attended_all, grad_top))
    grad_top_all = rep_gather(grad_top_now).reshape(-1, D)
    columns = mul(attended_all, w_output).astype(jnp.bfloat16).reshape(rep_total, tok_count, -1)
    branch = by_place(rep_exchange(columns)).transpose(1, 0, 2).reshape(tok_count, D)
    middle = residual + branch.astype(jnp.float32)
    scale_two = lax.rsqrt(jnp.mean(middle * middle, -1, keepdims=True) + norm_eps)
    normed_two = (middle * scale_two * gains[1]).astype(jnp.bfloat16)
    normed_two_all = rep_gather(normed_two).reshape(-1, D)
    normed_two_all, grad_top_all = lax.optimization_barrier((normed_two_all, grad_top_all))

    gate_rows = mul(normed_two_all, w_gate)
    up_rows = mul(normed_two_all, w_up)
    sigmoid_gate = jax.nn.sigmoid(gate_rows)
    silu_gate = gate_rows * sigmoid_gate
    activation = (silu_gate * up_rows).astype(jnp.bfloat16)
    g_down = weight_grad(activation, grad_top_all)
    grad_top_all, g_down = lax.optimization_barrier((grad_top_all, g_down))
    grad_act = mul_back(grad_top_all, w_down)
    grad_gate = (
        grad_act * up_rows * sigmoid_gate * (1.0 + gate_rows * (1.0 - sigmoid_gate))
    ).astype(jnp.bfloat16)
    grad_up = (grad_act * silu_gate).astype(jnp.bfloat16)
    grad_normed_two = own_sum(mul_back(grad_gate, w_gate) + mul_back(grad_up, w_up))
    g_gate = weight_grad(normed_two_all, grad_gate)
    g_up = weight_grad(normed_two_all, grad_up)
    grad_normed_two, g_gate, g_up = lax.optimization_barrier((grad_normed_two, g_gate, g_up))
    def over_tokens(partial):
        return lax.psum_scatter(partial, "fsdp", scatter_dimension=0, tiled=True)

    s_down = rep_gather(over_tokens(g_down))
    s_gate = rep_gather(over_tokens(g_gate))
    s_up = over_tokens(g_up)

    grad_middle = grad_top.astype(jnp.float32) + norm_back(middle, scale_two, gains[1], grad_normed_two)
    grad_parts = grad_middle.astype(jnp.bfloat16).reshape(tok_count, rep_total, -1).transpose(1, 0, 2)
    grad_columns = rep_exchange(by_place(grad_parts)).reshape(rep_total * tok_count, -1)
    grad_attended = rep_features_sum(
        grad_columns.reshape(rep_total, tok_count, -1), w_output
    ).astype(jnp.bfloat16)
    g_output = weight_grad(attended_all, grad_columns)
    g_output = by_place(g_output.reshape(rep_total, q_width, -1)).reshape(D, -1)
    grad_attended, s_down = lax.optimization_barrier((grad_attended, s_down))
    grad_queries, *grad_blocks = attend_back(
        band_number, glob_spots, wide_cosine, wide_sine, queries, grad_attended, lse, pair_blocks
    )
    returned = [
        shifted(grad_blocks[back_count - distance], "fsdp", -distance)
        for distance in range(1, back_count + 1)
    ]
    glob_grads = add_all(grad_blocks[-1], "fsdp")
    glob_grads, s_gate = lax.optimization_barrier((glob_grads, s_gate))
    grad_queries, activation = lax.optimization_barrier((grad_queries, activation))
    block_out = middle + own_sum(mul(activation, w_down))
    grad_inner = join_grads(
        grad_queries, grad_blocks[-2], selector_all, glob_grads, wide_cosine, wide_sine, returned
    ).reshape(-1, q_width + 2 * kv_width)
    g_inner, s_up = lax.optimization_barrier((weight_grad(normed_one_all, grad_inner), s_up))
    s_up = rep_gather(s_up)
    s_attn = over_tokens(jnp.concatenate([g_inner, g_output], 1))
    grad_normed_one = own_sum(mul_back(grad_inner, w_inner))
    grad_normed_one, s_up = lax.optimization_barrier((grad_normed_one, s_up))
    grad_input = grad_middle + norm_back(residual, scale_one, gains[0], grad_normed_one)

    slot_ids = jnp.arange(tile_total, dtype=jnp.int32)
    inverse = jnp.sum(jnp.where(tile_order[None, :] == slot_ids[:, None], slot_ids[None, :], 0), 1)
    own_slots = place * own_count + jnp.arange(own_count, dtype=jnp.int32)
    owned_tiles = jnp.take(inverse, own_slots, mode="clip")
    if aligned:
        sources = [rep_gather(s_attn), s_gate, s_up, s_down]
        where = np.zeros((4, rep_total, tile_total), np.int32)
        first_col = 0
        for kind, grid in enumerate(layout):
            rows, cols = grid.shape[1:]
            first_col = 0 if kind >= 4 else first_col
            for there in range(rep_total):
                numbers = grid[there].reshape(-1)
                at = np.arange(rows * cols)
                where[0, :, numbers] = max(kind - 3, 0)
                where[2, :, numbers] = (at // cols * BLK)[:, None]
                where[3, :, numbers] = (at % cols * BLK + first_col)[:, None]
                for here in range(rep_total):
                    where[1, here, numbers] = here ^ there
            first_col += cols * BLK
        tile_spots = lax.dynamic_index_in_dim(jnp.asarray(where), place, 1, False)
        meta = jnp.take(tile_spots, owned_tiles, axis=1, mode="clip")
    else:
        splits = [0, q_width, q_width + kv_width, q_width + 2 * kv_width, s_attn.shape[1]]
        stacks = [rep_gather(s_attn[:, low:high]) for low, high in zip(splits, splits[1:])]
        stacks += [s_gate, s_up, s_down]
        sources = [band_tiles(join_slices(stacks, band_total, rep_total))]
        meta = jnp.stack([0 * owned_tiles, owned_tiles, 0 * owned_tiles, 0 * owned_tiles], 0)
    slot_rates = jnp.take(kind_rates(band_total), owned_tiles, mode="clip")
    new_first, new_second, new_master, master_copy = adam(
        meta,
        slot_rates,
        (master[0], first_moment[0], second_moment[0], left_basis[0], right_basis[0]),
        sources,
    )
    gain_terms = jnp.stack(
        [
            jnp.sum(grad_normed_one * residual * scale_one, 0),
            jnp.sum(grad_normed_two * middle * scale_two, 0),
        ]
    )
    square_terms = jnp.stack(
        [jnp.sum(residual * residual), jnp.sum(middle * middle), jnp.sum(block_out * block_out)]
    )
    sums = jnp.concatenate([gain_terms.reshape(-1), square_terms])
    sums = add_all(add_all(sums, "rep"), "fsdp")
    gain_grad, square_total = sums[: 2 * D].reshape(2, D), sums[2 * D :]
    new_gain_first = beta_one * gain_first + (1.0 - beta_one) * gain_grad
    new_gain_second = beta_two * gain_second + (1.0 - beta_two) * gain_grad * gain_grad
    gain_step = (
        new_gain_first
        / (1.0 - beta_one**STEP)
        / (jnp.sqrt(new_gain_second / (1.0 - beta_two**STEP)) + adam_eps)
    )
    new_gains = gains - gain_rate * gain_step
    rms_stats = jnp.sqrt(square_total / (rep_total * band_total * tok_count * D))
    return (
        block_out[None],
        grad_input[None],
        new_first[None],
        new_second[None],
        new_master[None],
        master_copy[None],
        new_gain_first,
        new_gain_second,
        new_gains,
        rms_stats,
    )


def solution(mesh):
    in_specs = (
        P("rep", "fsdp", None),
        P("rep", "fsdp", None),
        P("rep", None, "fsdp"),
        P("fsdp", None),
        P("fsdp", "rep", None, None),
        P("fsdp", "rep", None, None),
        P("fsdp", "rep", None, None),
        P("fsdp", "rep", None, None),
        P("fsdp", "rep", None, None),
        P(),
        P(),
        P(),
    )
    out_specs = (
        P("rep", "fsdp", None),
        P("rep", "fsdp", None),
        P("fsdp", "rep", None, None),
        P("fsdp", "rep", None, None),
        P("fsdp", "rep", None, None),
        P("fsdp", "rep", None, None),
        P(),
        P(),
        P(),
        P(),
    )
    return jax.shard_map(
        per_device, mesh=mesh, in_specs=in_specs, out_specs=out_specs, check_vma=False
    )
```

```python
import functools

import jax
import jax.numpy as jnp
import numpy as np
from jax import lax
from jax.experimental import pallas as pl
from jax.experimental.pallas import tpu as pltpu
from jax.sharding import PartitionSpec as P

D = 2048
H = 32
KVH = 8
HD = 64
FF = 8192
WINDOW = 512
BLK = 128
STEP = 10


norm_eps = 1e-05
rope_theta = 500000.0
beta_one = 0.5
beta_two = 0.5
adam_eps = 1e-08
weight_decay = 0.1
gain_rate = 0.5
masked_value = -1e30


def matrix_shapes():
    kv_width = KVH * HD
    return [(D, D), (D, kv_width), (D, kv_width), (D, D), (D, FF), (D, FF), (FF, D)]


def kind_rates(band_total):
    rate_list = [
        D ** (-0.5),
        D ** (-0.5),
        D ** (-0.5),
        (D * 8 // WINDOW) ** (-0.5),
        D ** (-0.5),
        D ** (-0.5),
        FF ** (-0.5),
    ]
    pieces = []
    for (row_total, col_total), rate_value in zip(matrix_shapes(), rate_list):
        tile_count = row_total // band_total // BLK * (col_total // BLK)
        pieces.append(jnp.full((tile_count,), rate_value, jnp.float32))
    return jnp.concatenate(pieces)


def band_matrices(tiles, band_total):
    matrices = []
    offset = 0
    for row_total, col_total in matrix_shapes():
        band_rows = row_total // band_total
        tile_count = band_rows // BLK * (col_total // BLK)
        segment = tiles[offset : offset + tile_count].reshape(
            band_rows // BLK, col_total // BLK, BLK, BLK
        )
        matrices.append(segment.transpose(0, 2, 1, 3).reshape(band_rows, col_total))
        offset += tile_count
    return matrices


def band_tiles(matrices):
    pieces = []
    for matrix in matrices:
        row_count, col_count = matrix.shape
        segment = matrix.reshape(row_count // BLK, BLK, col_count // BLK, BLK).transpose(0, 2, 1, 3)
        pieces.append(segment.reshape(-1, BLK, BLK))
    return jnp.concatenate(pieces, 0)


def rope_tables(position):
    halves = jnp.arange(HD // 2, dtype=jnp.float32) * (2.0 / HD)
    frequency = rope_theta ** (-halves)
    angles = position.astype(jnp.float32)[:, None] * frequency[None, :]
    angles = jnp.concatenate([angles, angles], 1)
    return (jnp.cos(angles), jnp.sin(angles))


def rotate(vectors, cosine_table, sine_table):
    half_width = vectors.shape[-1] // 2
    turned = jnp.concatenate([-vectors[..., half_width:], vectors[..., :half_width]], -1)
    return vectors * cosine_table[:, None, :] + turned * sine_table[:, None, :]


def rotate_back(grad_rows, cosine_table, sine_table):
    half_width = grad_rows.shape[-1] // 2
    scaled = grad_rows * sine_table[:, None, :]
    turned = jnp.concatenate([scaled[..., half_width:], -scaled[..., :half_width]], -1)
    return grad_rows * cosine_table[:, None, :] + turned


def norm_back(values, row_scale, gain_row, grad_rows):
    weighted = grad_rows * gain_row
    return row_scale * weighted - values * row_scale**3 * jnp.mean(
        weighted * values, -1, keepdims=True
    )


def to_rep(block, distance):
    route = [(i, i ^ distance) for i in range(lax.axis_size("rep"))]
    return lax.ppermute(block, "rep", route)


def square():
    return lax.axis_size("rep") == 4


def square_pieces(block):
    cut = block.shape[0] // 2
    near = to_rep(block, 1)
    far = to_rep(block, 2)
    return block, near, far, to_rep(near[:cut], 2), to_rep(far[cut:], 1)


def rep_gather(block):
    if not square():
        return lax.all_gather(block, "rep", axis=0)
    own, near, far, low, high = square_pieces(block)
    return jnp.concatenate([own, near, far, low, high], 0).reshape((4,) + block.shape)


def rep_of(entry):
    place = lax.axis_index("rep")
    return place ^ entry if square() else entry


def rep_scatter(parts):
    if not square():
        flat = parts.reshape(-1, parts.shape[-1])
        return lax.psum_scatter(flat, "rep", scatter_dimension=0, tiled=True).astype(jnp.float32)
    half = parts.shape[-1] // 2
    low, high = parts[..., :half], parts[..., half:]
    return sum_pieces(
        jnp.stack([low[0], low[2]], 0), jnp.stack([low[1], low[3]], 0), high[:2], high[2:]
    )


def sum_pieces(low_kept, low_sent, high_kept, high_sent):
    totals = []
    for kept, sent, first, second in ((low_kept, low_sent, 1, 2), (high_kept, high_sent, 2, 1)):
        came = to_rep(sent, first)
        other = (kept[1].astype(jnp.float32) + came[1].astype(jnp.float32)).astype(kept.dtype)
        own = kept[0].astype(jnp.float32) + came[0].astype(jnp.float32)
        totals.append(own + to_rep(other, second).astype(jnp.float32))
    return jnp.concatenate(totals, -1)


def add_all(value, axis):
    size = lax.axis_size(axis)
    total = value.astype(jnp.float32)
    distance = 1
    while distance < size:
        count = 2 if (size // distance).bit_length() % 2 == 0 else 4
        low = total.astype(value.dtype)
        others = []
        for step in range(1, count):
            route = [(i, i ^ (step * distance)) for i in range(size)]
            others.append(lax.ppermute(low, axis, route).astype(jnp.float32))
        total = total + others[0]
        if count == 4:
            total = total + (others[1] + others[2])
        distance *= count
    return total


def rep_features(block):
    if not square():
        return lax.all_gather(block, "rep", axis=2, tiled=True)
    own, near, far, low, high = square_pieces(block)
    return jnp.concatenate(
        [
            own,
            jnp.stack([near[1], near[0], near[3], near[2]], 0),
            jnp.stack([far[2], far[3], far[0], far[1]], 0),
            jnp.stack([high[1], high[0], low[1], low[0]], 0),
        ],
        2,
    )


def write_pieces(entry, rows, values, refs):
    low_kept, low_sent, high_kept, high_sent = refs
    half = low_kept.shape[-1]
    values = values.astype(jnp.bfloat16)
    (low_sent if entry % 2 else low_kept)[entry // 2, rows] = values[:, :half]
    (high_sent if entry // 2 else high_kept)[entry % 2, rows] = values[:, half:]


def swapped_kernel(x_ref, w_ref, *refs):
    reps, rows, _ = x_ref.shape
    width = w_ref.shape[0] // reps
    for entry in range(reps):
        weight = w_ref[entry * width : (entry + 1) * width]
        for there in range(reps):
            product = over_last(x_ref[there ^ entry], weight)
            write_pieces(entry, slice(there * rows, (there + 1) * rows), product, refs)


def rep_features_sum(columns, weight):
    reps, rows, depth = columns.shape
    width = weight.shape[0] // reps
    if square():
        pieces = pl.pallas_call(
            swapped_kernel,
            out_shape=[jax.ShapeDtypeStruct((2, reps * rows, width // 2), jnp.bfloat16)] * 4,
            compiler_params=pltpu.CompilerParams(vmem_limit_bytes=32 * 2**20),
            cost_estimate=pl.CostEstimate(
                flops=2 * reps * columns.size * width,
                bytes_accessed=10 * columns.size,
                transcendentals=0,
            ),
        )(columns, weight)
        total = sum_pieces(*pieces)
    else:
        product = over_last(columns.reshape(-1, depth), weight).astype(jnp.bfloat16)
        swapped = product.reshape(reps, rows, reps, width).transpose(2, 0, 1, 3)
        total = rep_scatter(swapped.reshape(reps, reps * rows, width))
    return total.reshape(reps, rows, width)


def rep_exchange(parts):
    if not square():
        return lax.all_to_all(parts, "rep", 0, 0)
    return jnp.stack([parts[0]] + [to_rep(parts[entry], entry) for entry in (1, 2, 3)], 0)


def by_place(parts):
    entries = [rep_of(entry) for entry in range(parts.shape[0])]
    return jnp.stack([lax.dynamic_index_in_dim(parts, entry, 0, False) for entry in entries], 0)


def shifted(block, axis, distance):
    devices = range(lax.axis_size(axis))
    route = [(i - distance, i) for i in devices if i - distance in devices]
    return lax.ppermute(block, axis, route)


def tile_offsets(band_total):
    offsets = [0]
    for row_total, col_total in matrix_shapes():
        offsets.append(offsets[-1] + row_total // band_total // BLK * (col_total // BLK))
    return offsets


def whole_tiles(band_total, rep_total):
    return KVH * HD // rep_total % BLK == 0 and FF // band_total // rep_total % BLK == 0


def slice_layout(band_total, rep_total):
    offsets = tile_offsets(band_total)
    layout = []
    for kind, (row_total, col_total) in enumerate(matrix_shapes()):
        rows, cols = row_total // band_total // BLK, col_total // BLK
        grid = offsets[kind] + np.arange(rows * cols).reshape(rows, cols)
        if kind == 6:
            layout.append(grid.reshape(rep_total, rows // rep_total, cols))
        elif kind in (4, 5):
            cut = grid.reshape(rows, band_total, rep_total, -1).transpose(2, 0, 1, 3)
            layout.append(cut.reshape(rep_total, rows, -1))
        else:
            layout.append(grid.reshape(rows, rep_total, -1).transpose(1, 0, 2))
    return layout


def tiles_to_matrix(tiles):
    rows, cols = tiles.shape[:2]
    return tiles.transpose(0, 2, 1, 3).reshape(rows * BLK, cols * BLK)


def matrix_to_tiles(matrix):
    rows, cols = matrix.shape
    cut = matrix.reshape(rows // BLK, BLK, cols // BLK, BLK)
    return cut.transpose(0, 2, 1, 3).reshape(-1, BLK, BLK)


def cut_slices(matrices, band_total, rep_total):
    place = lax.axis_index("rep")
    slices = []
    for kind, matrix in enumerate(matrices):
        rows, cols = matrix.shape
        if kind == 6:
            slices.append(lax.dynamic_slice_in_dim(matrix, place * (rows // rep_total), rows // rep_total, 0))
        elif kind in (4, 5):
            cut = matrix.reshape(rows, band_total, rep_total, -1)
            slices.append(lax.dynamic_index_in_dim(cut, place, 2, False).reshape(rows, -1))
        else:
            slices.append(lax.dynamic_slice_in_dim(matrix, place * (cols // rep_total), cols // rep_total, 1))
    return slices


def join_slices(stacks, band_total, rep_total):
    matrices = []
    for kind, stack in enumerate(stacks):
        rows, cols = stack.shape[1:]
        if kind == 6:
            matrices.append(stack.reshape(-1, cols))
        elif kind in (4, 5):
            cut = stack.reshape(rep_total, rows, band_total, -1).transpose(1, 2, 0, 3)
            matrices.append(cut.reshape(rows, -1))
        else:
            matrices.append(stack.transpose(1, 0, 2).reshape(rows, -1))
    return matrices


def gather_kernel(plans, meta, *refs):
    source_total = len(refs) - len(plans) - 1
    sources, targets, done = refs[:source_total], refs[source_total:-1], refs[-1]
    piece_total = source_total // max(len(parts) for _, _, parts in plans)
    start = 0
    for place, (target, (rows, cols, parts)) in enumerate(zip(targets, plans)):
        height = sources[0].shape[1]

        def one(tile, carry, target=target, cols=cols, parts=parts, start=start, place=place, height=height):
            kind = meta[0, start + tile]
            row = meta[1, start + tile]
            top = tile // cols * (height * len(parts))
            left = pl.multiple_of(tile % cols * BLK, BLK)
            for number in range(piece_total):

                @pl.when(kind == number)
                def _(number=number):
                    for order, part in enumerate(parts):
                        first = pl.multiple_of(top + order * height, height)
                        pltpu.make_async_copy(
                            sources[part * piece_total + number].at[row],
                            target.at[pl.ds(first, height), pl.ds(left, BLK)],
                            done.at[place],
                        ).start()

            return carry

        lax.fori_loop(0, rows * cols, one, 0)
        start += rows * cols
    for place, target in enumerate(targets):
        pltpu.make_async_copy(target, target, done.at[place]).wait()


def gather_matrices(sources, meta, plans):
    anywhere = pl.BlockSpec(memory_space=pl.ANY)
    height = sources[0].shape[1]
    out_shape = [
        jax.ShapeDtypeStruct((rows * height * len(parts), cols * BLK), jnp.bfloat16)
        for rows, cols, parts in plans
    ]
    moved = sum(4 * shape.size for shape in out_shape)
    return pl.pallas_call(
        functools.partial(gather_kernel, plans),
        out_shape=out_shape,
        grid_spec=pltpu.PrefetchScalarGridSpec(
            num_scalar_prefetch=1,
            grid=(1,),
            in_specs=[anywhere] * len(sources),
            out_specs=[pl.BlockSpec(shape.shape, lambda i, *_: (0, 0)) for shape in out_shape],
            scratch_shapes=[pltpu.SemaphoreType.DMA((len(plans),))],
        ),
        compiler_params=pltpu.CompilerParams(vmem_limit_bytes=32 * 2**20),
        cost_estimate=pl.CostEstimate(flops=0, bytes_accessed=moved, transcendentals=0),
    )(meta, *sources)


def place_kernel(entries, rows, cols, meta, low, high, out_ref, done):
    out_ref[...] = jnp.zeros_like(out_ref)
    height = low.shape[1]

    def copies(tile):
        entry, rest = tile // (rows * cols), tile % (rows * cols)
        top = rest // cols * (2 * height)
        left = pl.multiple_of(rest % cols * BLK, BLK)
        return [
            pltpu.make_async_copy(
                half.at[meta[1, tile]],
                out_ref.at[entry, pl.ds(pl.multiple_of(top + part * height, height), height), pl.ds(left, BLK)],
                done.at[part],
            )
            for part, half in enumerate((low, high))
        ]

    def begin(tile, carry):
        @pl.when(meta[0, tile] == 1)
        def _():
            for copy in copies(tile):
                copy.start()

        return carry

    def finish(tile, carry):
        @pl.when(meta[0, tile] == 1)
        def _():
            for copy in copies(tile):
                copy.wait()

        return carry

    lax.fori_loop(0, entries * rows * cols, begin, 0)
    lax.fori_loop(0, entries * rows * cols, finish, 0)


def place_tiles(low, high, meta, entries, rows, cols):
    shape = (entries, rows * BLK, cols * BLK)
    anywhere = pl.BlockSpec(memory_space=pl.ANY)
    return pl.pallas_call(
        functools.partial(place_kernel, entries, rows, cols),
        out_shape=jax.ShapeDtypeStruct(shape, jnp.bfloat16),
        grid_spec=pltpu.PrefetchScalarGridSpec(
            num_scalar_prefetch=1,
            grid=(1,),
            in_specs=[anywhere, anywhere],
            out_specs=pl.BlockSpec(shape, lambda i, *_: (0, 0, 0)),
            scratch_shapes=[pltpu.SemaphoreType.DMA((2,))],
        ),
        compiler_params=pltpu.CompilerParams(vmem_limit_bytes=32 * 2**20),
        cost_estimate=pl.CostEstimate(
            flops=0, bytes_accessed=4 * entries * rows * cols * BLK * BLK, transcendentals=0
        ),
    )(meta, low, high)


def half_turn(values):
    lane = lax.broadcasted_iota(jnp.int32, values.shape, 1)
    lanes = values.shape[1]
    first = lane % HD < HD // 2
    return first, jnp.where(
        first, pltpu.roll(values, lanes - HD // 2, 1), pltpu.roll(values, HD // 2, 1)
    )


def fetch_columns(early, late, start, width, target, done):
    pltpu.make_async_copy(early.at[:, :, pl.ds(start, width)], target.at[:, 0], done.at[0]).start()
    pltpu.make_async_copy(late.at[:, :, pl.ds(start, width)], target.at[:, 1], done.at[1]).start()


def wait_columns(target, done):
    pltpu.make_async_copy(target.at[:, 0], target.at[:, 0], done.at[0]).wait()
    pltpu.make_async_copy(target.at[:, 1], target.at[:, 1], done.at[1]).wait()


def forward_kernel(width, x_ref, early, late, gate_ref, up_ref, act_ref, weights, done):
    step, steps = pl.program_id(0), pl.num_programs(0)
    slot = step % 2

    def fetch(at_step, at_slot):
        for number in range(2):
            start = pl.multiple_of(number * (steps * width) + at_step * width, BLK)
            fetch_columns(early, late, start, width, weights.at[number, at_slot], done.at[number, at_slot])

    @pl.when(step == 0)
    def _():
        fetch(0, 0)

    @pl.when(step + 1 < steps)
    def _():
        fetch(step + 1, 1 - slot)

    products = []
    for number in range(2):
        wait_columns(weights.at[number, slot], done.at[number, slot])
        weight = weights[number, slot].reshape(-1, width)
        products.append(jnp.dot(x_ref[...], weight, preferred_element_type=jnp.float32))
    gate, up = products
    gate_ref[...] = gate.astype(jnp.bfloat16)
    up_ref[...] = up.astype(jnp.bfloat16)
    act_ref[...] = (gate * jax.nn.sigmoid(gate) * up).astype(jnp.bfloat16)


def forward_products(rows, early, late, columns):
    tokens, depth = rows.shape
    width = 2 * BLK
    tiles, half = early.shape[:2]
    block = pl.BlockSpec((tokens, width), lambda n: (0, n))
    anywhere = pl.BlockSpec(memory_space=pl.ANY)
    return pl.pallas_call(
        functools.partial(forward_kernel, width),
        out_shape=[jax.ShapeDtypeStruct((tokens, columns), jnp.bfloat16)] * 3,
        grid=(columns // width,),
        in_specs=[pl.BlockSpec(rows.shape, lambda n: (0, 0)), anywhere, anywhere],
        out_specs=[block] * 3,
        scratch_shapes=[
            pltpu.VMEM((2, 2, tiles, 2, half, width), jnp.bfloat16),
            pltpu.SemaphoreType.DMA((2, 2, 2)),
        ],
        compiler_params=pltpu.CompilerParams(vmem_limit_bytes=48 * 2**20),
        cost_estimate=pl.CostEstimate(
            flops=tokens * depth * columns // 8, bytes_accessed=2 * rows.size, transcendentals=0
        ),
    )(rows, early, late)


def backward_kernel(
    width, down_start, top_ref, gate_ref, up_ref, act_ref, early, late, late_down, *refs
):
    dgate_ref, dup_ref = refs[:2]
    pieces, branch_pieces = refs[2:6], refs[6:10]
    weights, downs, total, branch, done, down_done = refs[10:]
    step, steps = pl.program_id(0), pl.num_programs(0)
    slot = step % 2
    tiles = downs.shape[1]

    def down_copies(at_step, at_slot):
        first = at_step * tiles
        depth = late_down.shape[2]
        return [
            pltpu.make_async_copy(
                early.at[pl.ds(first, tiles), :, pl.ds(down_start, depth)],
                downs.at[at_slot, :, 0],
                down_done.at[at_slot, 0],
            ),
            pltpu.make_async_copy(
                late_down.at[pl.ds(first, tiles)], downs.at[at_slot, :, 1], down_done.at[at_slot, 1]
            ),
        ]

    def fetch(at_step, at_slot):
        for copy in down_copies(at_step, at_slot):
            copy.start()
        for number in range(2):
            start = pl.multiple_of(number * (steps * width) + at_step * width, BLK)
            fetch_columns(early, late, start, width, weights.at[number, at_slot], done.at[number, at_slot])

    @pl.when(step == 0)
    def _():
        fetch(0, 0)
        total[...] = jnp.zeros_like(total)
        branch[...] = jnp.zeros_like(branch)

    @pl.when(step + 1 < steps)
    def _():
        fetch(step + 1, 1 - slot)

    for copy in down_copies(step, slot):
        copy.wait()
    down = downs[slot].reshape(width, -1)
    grad_act = over_last(top_ref[...], down)
    gate = gate_ref[...].astype(jnp.float32)
    up = up_ref[...].astype(jnp.float32)
    sigmoid_gate = jax.nn.sigmoid(gate)
    grad_gate = (grad_act * up * sigmoid_gate * (1.0 + gate * (1.0 - sigmoid_gate))).astype(jnp.bfloat16)
    grad_up = (grad_act * (gate * sigmoid_gate)).astype(jnp.bfloat16)
    dgate_ref[...] = grad_gate
    dup_ref[...] = grad_up
    branch[...] += jnp.dot(act_ref[...], down, preferred_element_type=jnp.float32)
    for number, grads in enumerate((grad_gate, grad_up)):
        wait_columns(weights.at[number, slot], done.at[number, slot])
        total[...] += over_last(grads, weights[number, slot].reshape(-1, width))

    @pl.when(step == steps - 1)
    def _():
        rows = total.shape[0] // 4
        for entry in range(4):
            part = slice(entry * rows, (entry + 1) * rows)
            write_pieces(entry, slice(0, rows), total[part], pieces)
            write_pieces(entry, slice(0, rows), branch[part], branch_pieces)


def backward_products(top, gate, up, act, early, late, late_down):
    tokens, depth = top.shape
    columns = gate.shape[1]
    width = 2 * BLK
    tiles, half = early.shape[:2]
    block = pl.BlockSpec((tokens, width), lambda n: (0, n))
    anywhere = pl.BlockSpec(memory_space=pl.ANY)
    piece = jax.ShapeDtypeStruct((2, tokens // 4, depth // 2), jnp.bfloat16)
    grads = jax.ShapeDtypeStruct((tokens, columns), jnp.bfloat16)
    outs = pl.pallas_call(
        functools.partial(backward_kernel, width, 2 * columns),
        out_shape=[grads] * 2 + [piece] * 8,
        grid=(columns // width,),
        in_specs=[pl.BlockSpec(top.shape, lambda n: (0, 0))] + [block] * 3 + [anywhere] * 3,
        out_specs=[block] * 2 + [pl.BlockSpec(piece.shape, lambda n: (0, 0, 0))] * 8,
        scratch_shapes=[
            pltpu.VMEM((2, 2, tiles, 2, half, width), jnp.bfloat16),
            pltpu.VMEM((2, width // BLK, 2, half, depth), jnp.bfloat16),
            pltpu.VMEM((tokens, depth), jnp.float32),
            pltpu.VMEM((tokens, depth), jnp.float32),
            pltpu.SemaphoreType.DMA((2, 2, 2)),
            pltpu.SemaphoreType.DMA((2, 2)),
        ],
        compiler_params=pltpu.CompilerParams(vmem_limit_bytes=60 * 2**20),
        cost_estimate=pl.CostEstimate(
            flops=8 * tokens * depth * columns, bytes_accessed=8 * columns * depth, transcendentals=0
        ),
    )(top, gate, up, act, early, late, late_down)
    return outs[0], outs[1], outs[2:6], outs[6:10]


def rope_kernel(q_width, kv_width, x_ref, cos_ref, sin_ref, *outs):
    width = x_ref.shape[-1]
    for start in range(0, width, BLK):
        values = x_ref[0, :, start : start + BLK]
        first, turned = half_turn(values)
        sines = sin_ref[0]
        turned_rows = values * cos_ref[0] + turned * jnp.where(first, -sines, sines)
        if start + BLK > q_width + kv_width:
            column = lax.broadcasted_iota(jnp.int32, values.shape, 1) + start
            turned_rows = jnp.where(column >= q_width + kv_width, values, turned_rows)
        if start < q_width:
            outs[0][0, :, start : start + BLK] = (turned_rows * HD ** (-0.5)).astype(jnp.bfloat16)
        else:
            outs[-1][0, :, start - q_width : start - q_width + BLK] = turned_rows.astype(jnp.bfloat16)


def rope_rows(inner, rows, row_block, q_width, kv_width, cosines, sines, with_queries=True):
    seqs, _, width = inner.shape
    shared = cosines.shape[0] == 1
    table = pl.BlockSpec((1, rows, BLK), lambda s: (0 if shared else s, 0, 0))
    widths = [q_width, 2 * kv_width]
    column_block = 0
    if not with_queries:
        width, column_block = 2 * kv_width, q_width // (2 * kv_width)
        widths, q_width = widths[1:], 0
    return pl.pallas_call(
        functools.partial(rope_kernel, q_width, kv_width),
        out_shape=[jax.ShapeDtypeStruct((seqs, rows, w), jnp.bfloat16) for w in widths],
        grid=(seqs,),
        in_specs=[pl.BlockSpec((1, rows, width), lambda s: (s, row_block, column_block)), table, table],
        out_specs=[pl.BlockSpec((1, rows, w), lambda s: (s, 0, 0)) for w in widths],
        cost_estimate=pl.CostEstimate(
            flops=6 * seqs * rows * width, bytes_accessed=6 * seqs * rows * width, transcendentals=0
        ),
    )(inner, cosines, sines)


def fill_bias(band_ref, gpos_ref, bias_ref, rows, window_len):
    band = band_ref[0]

    @pl.when(pl.program_id(0) == 0)
    def _():
        key = lax.broadcasted_iota(jnp.int32, (window_len, rows), 0) + (
            band * rows - (window_len - rows)
        )
        query = lax.broadcasted_iota(jnp.int32, (window_len, rows), 1) + band * rows
        inside = (key > query - WINDOW) & (key <= query) & (key >= 0)
        bias_ref[:window_len] = jnp.where(inside, 0.0, masked_value)

    glob_total = gpos_ref.shape[1]
    query = lax.broadcasted_iota(jnp.int32, (glob_total, rows), 1) + (band * rows - WINDOW)
    spot = jnp.broadcast_to(gpos_ref[0][:, :1], (glob_total, rows))
    bias_ref[window_len:] = jnp.where(spot <= query.astype(jnp.float32), 0.0, masked_value)


def over_last(left, right):
    return lax.dot_general(left, right, (((1,), (1,)), ((), ())), preferred_element_type=jnp.float32)


def over_first(left, right):
    return lax.dot_general(left, right, (((0,), (0,)), ((), ())), preferred_element_type=jnp.float32)


def attend_kernel(block_total, band_ref, gpos_ref, q_ref, *refs):
    blocks, (out_ref, lse_ref, bias_ref) = refs[:block_total], refs[block_total:]
    rows, q_width = q_ref.shape[1:]
    kv_width = blocks[0].shape[2] // 2
    heads, group = q_width // HD, q_width // kv_width
    window_len = rows * (block_total - 1)
    fill_bias(band_ref, gpos_ref, bias_ref, rows, window_len)
    starts = [rows * number for number in range(block_total)]
    pending = []
    for head in range(heads):
        left = head // group * HD
        queries = q_ref[0, :, head * HD : (head + 1) * HD]
        scores = [
            over_last(block[0, :, left : left + HD], queries)
            + bias_ref[start : start + block.shape[1]]
            for block, start in zip(blocks, starts)
        ]
        top = functools.reduce(jnp.maximum, [jnp.max(part, 0, keepdims=True) for part in scores])
        total = 0.0
        mixed = 0.0
        for block, part in zip(blocks, scores):
            weights = jnp.exp(part - top)
            total = total + jnp.sum(weights, 0, keepdims=True)
            mixed = mixed + over_first(
                block[0, :, kv_width + left : kv_width + left + HD], weights.astype(jnp.bfloat16)
            )
        lse_ref[0, head : head + 1, :] = top + jnp.log(total)
        pending.append(mixed / total)
        if len(pending) * HD == BLK or head == heads - 1:
            stop = (head + 1) * HD
            both = jnp.concatenate(pending, 0).T
            out_ref[0, :, stop - both.shape[1] : stop] = both.astype(jnp.bfloat16)
            pending = []


def attend(band, gpos, queries, blocks):
    seqs, rows, q_width = queries.shape
    heads = q_width // HD
    key_total = sum(block.shape[1] for block in blocks)

    def whole(array):
        return pl.BlockSpec((1,) + array.shape[1:], lambda s, *_: (s, 0, 0))

    out_shape = [
        jax.ShapeDtypeStruct((seqs, rows, q_width), jnp.bfloat16),
        jax.ShapeDtypeStruct((seqs, heads, rows), jnp.float32),
    ]
    return pl.pallas_call(
        functools.partial(attend_kernel, len(blocks)),
        out_shape=out_shape,
        grid_spec=pltpu.PrefetchScalarGridSpec(
            num_scalar_prefetch=1,
            grid=(seqs,),
            in_specs=[whole(array) for array in (gpos, queries, *blocks)],
            out_specs=[whole(array) for array in out_shape],
            scratch_shapes=[pltpu.VMEM((key_total, rows), jnp.float32)],
        ),
        compiler_params=pltpu.CompilerParams(vmem_limit_bytes=48 * 2**20),
        cost_estimate=pl.CostEstimate(
            flops=16 * seqs * heads * rows * key_total * HD,
            bytes_accessed=4 * queries.size,
            transcendentals=seqs * heads * rows * key_total,
        ),
    )(band, gpos, queries, *blocks)


def attend_back_kernel(block_total, band_ref, gpos_ref, cos_ref, sin_ref, q_ref, grad_ref, lse_ref, *refs):
    blocks = refs[:block_total]
    dq_ref = refs[block_total]
    out_refs = refs[block_total + 1 : 2 * block_total + 1]
    bias_ref = refs[-1]
    rows, q_width = q_ref.shape[1:]
    kv_width = blocks[0].shape[2] // 2
    heads, group = q_width // HD, q_width // kv_width
    window_len = rows * (block_total - 1)
    fill_bias(band_ref, gpos_ref, bias_ref, rows, window_len)
    starts = [rows * number for number in range(block_total)]
    pending = []
    for kv_head in range(kv_width // HD):
        left = kv_head * HD
        key_sums = [0.0] * block_total
        value_sums = [0.0] * block_total
        for head in range(kv_head * group, (kv_head + 1) * group):
            queries = q_ref[0, :, head * HD : (head + 1) * HD]
            grads = grad_ref[0, :, head * HD : (head + 1) * HD]
            lse = lse_ref[0, head : head + 1, :]
            soft, soft_grads = [], []
            inner = 0.0
            for number, (block, start) in enumerate(zip(blocks, starts)):
                part = over_last(block[0, :, left : left + HD], queries)
                part = jnp.exp(part + bias_ref[start : start + block.shape[1]] - lse)
                slope = over_last(block[0, :, kv_width + left : kv_width + left + HD], grads)
                inner = inner + jnp.sum(part * slope, 0, keepdims=True)
                soft.append(part)
                soft_grads.append(slope)
            turned = 0.0
            for number, block in enumerate(blocks):
                score_grads = (soft[number] * (soft_grads[number] - inner)).astype(jnp.bfloat16)
                value_sums[number] = value_sums[number] + jnp.dot(
                    soft[number].astype(jnp.bfloat16), grads, preferred_element_type=jnp.float32
                )
                key_sums[number] = key_sums[number] + jnp.dot(
                    score_grads, queries, preferred_element_type=jnp.float32
                )
                turned = turned + over_first(block[0, :, left : left + HD], score_grads)
            pending.append(turned)
            if len(pending) * HD == BLK or head == heads - 1:
                stop = (head + 1) * HD
                both = jnp.concatenate(pending, 0).T * HD ** (-0.5)
                pending = []
                first, other = half_turn(both * sin_ref[0])
                both = both * cos_ref[0] + jnp.where(first, other, -other)
                dq_ref[0, :, stop - both.shape[1] : stop] = both.astype(jnp.bfloat16)
        for number, out_ref in enumerate(out_refs):
            out_ref[0, :, left : left + HD] = key_sums[number].astype(out_ref.dtype)
            out_ref[0, :, kv_width + left : kv_width + left + HD] = value_sums[number].astype(
                out_ref.dtype
            )


def attend_back(band, gpos, cosines, sines, queries, grads, lse, blocks):
    seqs, rows, q_width = queries.shape
    heads = q_width // HD
    key_total = sum(block.shape[1] for block in blocks)

    def whole(array):
        return pl.BlockSpec((1,) + array.shape[1:], lambda s, *_: (s, 0, 0))

    table = pl.BlockSpec((1, rows, BLK), lambda s, *_: (0, 0, 0))
    out_shape = [jax.ShapeDtypeStruct(queries.shape, jnp.bfloat16)]
    for number, block in enumerate(blocks):
        own = number == len(blocks) - 2
        out_shape.append(jax.ShapeDtypeStruct(block.shape, jnp.float32 if own else jnp.bfloat16))
    return pl.pallas_call(
        functools.partial(attend_back_kernel, len(blocks)),
        out_shape=out_shape,
        grid_spec=pltpu.PrefetchScalarGridSpec(
            num_scalar_prefetch=1,
            grid=(seqs,),
            in_specs=[whole(gpos), table, table]
            + [whole(array) for array in (queries, grads, lse, *blocks)],
            out_specs=[whole(array) for array in out_shape],
            scratch_shapes=[pltpu.VMEM((key_total, rows), jnp.float32)],
        ),
        compiler_params=pltpu.CompilerParams(vmem_limit_bytes=48 * 2**20),
        cost_estimate=pl.CostEstimate(
            flops=40 * seqs * heads * rows * key_total * HD,
            bytes_accessed=8 * queries.size,
            transcendentals=seqs * heads * rows * key_total,
        ),
    )(band, gpos, cosines, sines, queries, grads, lse, *blocks)


def join_kernel(q_width, kv_width, dq_ref, own_ref, pick_ref, glob_ref, cos_ref, sin_ref, *refs):
    back_refs, out_ref = refs[:-1], refs[-1]
    out_ref[0, :, :q_width] = dq_ref[0]
    picked = lax.dot_general(
        pick_ref[0].astype(jnp.float32),
        glob_ref[0],
        (((0,), (0,)), ((), ())),
        precision=lax.Precision.HIGHEST,
        preferred_element_type=jnp.float32,
    )
    for start in range(0, 2 * kv_width, BLK):
        lanes = slice(start, start + BLK)
        total = own_ref[0, :, lanes] + picked[:, lanes]
        for back_ref in back_refs:
            total = total + back_ref[0, :, lanes].astype(jnp.float32)
        first, other = half_turn(total * sin_ref[0])
        turned = total * cos_ref[0] + jnp.where(first, other, -other)
        column = lax.broadcasted_iota(jnp.int32, total.shape, 1) + start
        turned = jnp.where(column >= kv_width, total, turned)
        out_ref[0, :, q_width + start : q_width + start + BLK] = turned.astype(jnp.bfloat16)


def join_grads(dq, own, picks, globs, cosines, sines, backs):
    seqs, rows, q_width = dq.shape
    kv_width = own.shape[2] // 2

    def whole(array):
        return pl.BlockSpec((1,) + array.shape[1:], lambda s: (s, 0, 0))

    table = pl.BlockSpec((1, rows, BLK), lambda s: (0, 0, 0))
    out_shape = jax.ShapeDtypeStruct((seqs, rows, q_width + 2 * kv_width), jnp.bfloat16)
    return pl.pallas_call(
        functools.partial(join_kernel, q_width, kv_width),
        out_shape=out_shape,
        grid=(seqs,),
        in_specs=[whole(dq), whole(own), whole(picks), whole(globs), table, table]
        + [whole(back) for back in backs],
        out_specs=whole(out_shape),
        cost_estimate=pl.CostEstimate(
            flops=20 * own.size, bytes_accessed=4 * dq.size + 12 * own.size, transcendentals=0
        ),
    )(dq, own, picks, globs, cosines, sines, *backs)


def adam_kernel(batch, meta, rates, *refs):
    master_ref, first_ref, second_ref, left_ref, right_ref = refs[:5]
    sources = refs[5:-6]
    new_first_ref, new_second_ref, new_master_ref, copy_ref, tiles, arrived = refs[-6:]
    step, steps = pl.program_id(0), pl.num_programs(0)
    slot = step % 2

    def fetch(at_step, at_slot):
        for place in range(batch):
            tile = at_step * batch + place
            for number, source in enumerate(sources):

                @pl.when(meta[0, tile] == number)
                def _(source=source, tile=tile, place=place):
                    top = pl.multiple_of(meta[2, tile], BLK)
                    left = pl.multiple_of(meta[3, tile], BLK)
                    pltpu.make_async_copy(
                        source.at[meta[1, tile], pl.ds(top, BLK), pl.ds(left, BLK)],
                        tiles.at[at_slot, place],
                        arrived.at[at_slot],
                    ).start()

    @pl.when(step == 0)
    def _():
        fetch(0, 0)

    @pl.when(step + 1 < steps)
    def _():
        fetch(step + 1, 1 - slot)

    pltpu.make_async_copy(tiles.at[slot], tiles.at[slot], arrived.at[slot]).wait()
    places = range(batch)
    lefts = [left_ref[place].astype(jnp.bfloat16) for place in places]
    rights = [right_ref[place].astype(jnp.bfloat16) for place in places]
    turned = [over_first(lefts[place], tiles[slot, place]).astype(jnp.bfloat16) for place in places]
    rotated = [
        jnp.dot(turned[place], rights[place], preferred_element_type=jnp.float32) for place in places
    ]
    directions = []
    for place in places:
        new_first = beta_one * first_ref[place] + (1.0 - beta_one) * rotated[place]
        new_second = beta_two * second_ref[place] + (1.0 - beta_two) * rotated[place] * rotated[place]
        direction = (new_first * (1.0 / (1.0 - beta_one**STEP))) / (
            jnp.sqrt(new_second * (1.0 / (1.0 - beta_two**STEP))) + adam_eps
        )
        new_first_ref[place] = new_first
        new_second_ref[place] = new_second
        directions.append(direction.astype(jnp.bfloat16))
    updates = [
        jnp.dot(lefts[place], directions[place], preferred_element_type=jnp.float32) for place in places
    ]
    updates = [over_last(updates[place].astype(jnp.bfloat16), rights[place]) for place in places]
    for place in places:
        old = master_ref[place]
        new_master = old - rates[step * batch + place] * (updates[place] + weight_decay * old)
        new_master_ref[place] = new_master
        copy_ref[place] = new_master.astype(jnp.bfloat16)


def adam(meta, rates, state, sources):
    count = state[0].shape[0]
    batch = max(size for size in (1, 2, 4) if count % size == 0)
    block = pl.BlockSpec((batch, BLK, BLK), lambda s, *_: (s, 0, 0))
    anywhere = pl.BlockSpec(memory_space=pl.ANY)
    shape = (count, BLK, BLK)
    return pl.pallas_call(
        functools.partial(adam_kernel, batch),
        out_shape=[jax.ShapeDtypeStruct(shape, jnp.float32)] * 3
        + [jax.ShapeDtypeStruct(shape, jnp.bfloat16)],
        grid_spec=pltpu.PrefetchScalarGridSpec(
            num_scalar_prefetch=2,
            grid=(count // batch,),
            in_specs=[block] * 5 + [anywhere] * len(sources),
            out_specs=[block] * 4,
            scratch_shapes=[
                pltpu.VMEM((2, batch, BLK, BLK), jnp.bfloat16),
                pltpu.SemaphoreType.DMA((2,)),
            ],
        ),
        compiler_params=pltpu.CompilerParams(vmem_limit_bytes=32 * 2**20),
        cost_estimate=pl.CostEstimate(
            flops=8 * count * BLK**3, bytes_accessed=36 * count * BLK**2, transcendentals=0
        ),
    )(meta, rates, *state, *sources)


def per_device(
    block_input,
    cotangent,
    glob_select,
    assignment,
    master,
    first_moment,
    second_moment,
    left_basis,
    right_basis,
    gains,
    gain_first,
    gain_second,
):
    band_total = lax.axis_size("fsdp")
    rep_total = lax.axis_size("rep")
    place = lax.axis_index("rep")
    band = lax.axis_index("fsdp")
    heads = H // rep_total
    kv_heads = KVH // rep_total
    q_width = heads * HD
    kv_width = kv_heads * HD
    tok_count = block_input.shape[1]
    own_count = master.shape[1]
    tile_total = own_count * rep_total
    aligned = square() and whole_tiles(band_total, rep_total)
    tile_order = assignment[0]

    residual = block_input[0].astype(jnp.float32)
    grad_top = cotangent[0]
    position = band * tok_count + jnp.arange(tok_count, dtype=jnp.int32)
    cosine_table, sine_table = rope_tables(position)
    wide_cosine = jnp.concatenate([cosine_table, cosine_table], 1)[None]
    wide_sine = jnp.concatenate([sine_table, sine_table], 1)[None]
    scale_one = lax.rsqrt(jnp.mean(residual * residual, -1, keepdims=True) + norm_eps)
    normed_one = (residual * scale_one * gains[0]).astype(jnp.bfloat16)
    pick_rows = glob_select[0]
    glob_total = pick_rows.shape[0]
    selector = pick_rows.astype(jnp.bfloat16)
    glob_pos_part = jnp.sum(pick_rows * position[None, :], 1)
    digits = jnp.concatenate([glob_pos_part // 256, glob_pos_part % 256]).astype(jnp.bfloat16)
    digits = jnp.pad(digits[None], ((0, 7), (0, D - 2 * glob_total)))
    glob_rows = jnp.dot(selector, normed_one, preferred_element_type=jnp.float32).astype(jnp.bfloat16)
    glob_rows = add_all(jnp.concatenate([glob_rows, digits], 0), "fsdp").astype(jnp.bfloat16)
    packed = [normed_one, glob_rows, selector.reshape(-1, D)]
    packed = jnp.concatenate(packed, 0)
    packed = jnp.pad(packed, ((0, -packed.shape[0] % 32), (0, 0)))

    if aligned:
        half = BLK // 2
        low, high = (master[0, :, rows].astype(jnp.bfloat16) for rows in (slice(0, half), slice(half, BLK)))
        layout = slice_layout(band_total, rep_total)
        attn_layout = jnp.asarray(np.concatenate(layout[:4], 2))
        wanted = jnp.take(tile_order, by_place(attn_layout).reshape(-1), mode="clip")
        meta = jnp.stack([wanted // own_count == place, wanted % own_count], 0).astype(jnp.int32)
        attn_part = place_tiles(low, high, meta, *attn_layout.shape)
        attn_part = rep_scatter(attn_part).astype(jnp.bfloat16)
        low, attn_part = lax.optimization_barrier((low, attn_part))
        slots = square_pieces(low)
        *slots, packed = lax.optimization_barrier((*slots, packed))
    packed_all = rep_gather(packed)
    if aligned:
        packed_all, high = lax.optimization_barrier((packed_all, high))
        later_slots = square_pieces(high)
    normed_one_all = packed_all[:, :tok_count].reshape(-1, D)
    at = tok_count + glob_total
    glob_digits = packed_all[:, at, : 2 * glob_total].astype(jnp.float32)
    glob_place = glob_digits[:, :glob_total] * 256.0 + glob_digits[:, glob_total:]
    at += 8
    selector_all = packed_all[:, at : at + selector.size // D].reshape(rep_total, glob_total, tok_count)

    def over_bands(slice_rows):
        return lax.all_gather(slice_rows, "fsdp", axis=0, tiled=True)

    if aligned:
        grids = [lax.dynamic_index_in_dim(jnp.asarray(grid), place, 0, False) for grid in layout]

        def find(wanted):
            wanted = jnp.take(tile_order, jnp.concatenate([grid.reshape(-1) for grid in wanted]), mode="clip")
            entry, row = (wanted // own_count) ^ place, wanted % own_count
            cut = own_count // 2
            high = (entry == 3) & (row >= cut)
            found = jnp.stack([jnp.where(high, 4, entry), jnp.where(high, row - cut, row)], 0)
            return found.astype(jnp.int32)

        def plan(grid, parts):
            return (*grid.shape, parts)

        first_grid = jnp.concatenate(grids[4:6], 1)
        attn = over_bands(attn_part)
        *slots, attn = lax.optimization_barrier((*slots, attn))
        first_part, down_part = gather_matrices(
            slots, find([first_grid, grids[6]]), [plan(first_grid, (0,)), plan(grids[6], (0,))]
        )
        down_rows, down_cols = down_part.shape
        first_part = jnp.concatenate([first_part, down_part.reshape(first_part.shape[0], -1)], 1)
        in_width = q_width + 2 * kv_width
        w_inner, w_output = attn[:, :in_width], attn[:, in_width:]
    else:
        slots = lax.all_gather(master[0].astype(jnp.bfloat16), "rep", axis=0, tiled=True)
        tiles = jnp.take(slots, tile_order, axis=0, mode="clip")
        slices = cut_slices(band_matrices(tiles, band_total), band_total, rep_total)
        w_inner = over_bands(jnp.concatenate(slices[0:3], 1))
        w_output = over_bands(slices[3])
        w_gate = over_bands(slices[4])
        w_up = over_bands(slices[5])
        w_down = over_bands(slices[6])

    w_output = by_place(w_output.reshape(rep_total, q_width, -1)).reshape(D, -1)

    def mul(rows, weight):
        return jnp.dot(rows, weight, preferred_element_type=jnp.float32)

    def mul_back(rows, weight):
        return lax.dot_general(rows, weight, (((1,), (1,)), ((), ())), preferred_element_type=jnp.float32)

    def weight_grad(rows, grad_rows):
        return lax.dot_general(
            rows, grad_rows, (((0,), (0,)), ((), ())), preferred_element_type=jnp.float32
        ).astype(jnp.bfloat16)

    def own_sum(partial):
        return rep_scatter(partial.astype(jnp.bfloat16).reshape(rep_total, tok_count, D))

    if aligned:
        packed_all, first_part = lax.optimization_barrier((packed_all, first_part))
        early = over_bands(first_part)
    inner_rows = mul(packed_all.reshape(-1, D), w_inner).reshape(rep_total, -1, w_inner.shape[1])
    queries, own_pairs = rope_rows(inner_rows, tok_count, 0, q_width, kv_width, wide_cosine, wide_sine)
    glob_cosine, glob_sine = rope_tables(glob_place.reshape(-1))
    glob_cosine = jnp.concatenate([glob_cosine, glob_cosine], 1).reshape(rep_total, glob_total, -1)
    glob_sine = jnp.concatenate([glob_sine, glob_sine], 1).reshape(rep_total, glob_total, -1)
    (glob_pairs,) = rope_rows(
        inner_rows, glob_total, tok_count // glob_total, q_width, kv_width, glob_cosine, glob_sine, False
    )
    back_count = (WINDOW + tok_count - 2) // tok_count
    pair_blocks = [shifted(own_pairs, "fsdp", distance) for distance in range(back_count, 0, -1)]
    pair_blocks = pair_blocks + [own_pairs, glob_pairs]
    glob_spots = jnp.broadcast_to(glob_place[:, :, None], (rep_total, glob_total, BLK))
    band_number = band.astype(jnp.int32).reshape(1)
    attended_low, lse = attend(band_number, glob_spots, queries, pair_blocks)
    if aligned:
        *later_slots, attended_low, early = lax.optimization_barrier((*later_slots, attended_low, early))
        last_part, down_part = gather_matrices(
            later_slots, find([first_grid, grids[6]]), [plan(first_grid, (0,)), plan(grids[6], (0,))]
        )
        late, late_down = over_bands(last_part), over_bands(down_part)
        early = early.reshape(-1, half, early.shape[1])
        late = late.reshape(-1, half, late.shape[1])
        late_down = late_down.reshape(-1, half, D)
    attended_all = rep_features(attended_low).reshape(-1, D)
    attended_all, grad_top_now = lax.optimization_barrier((attended_all, grad_top))
    grad_top_all = rep_gather(grad_top_now).reshape(-1, D)
    columns = mul(attended_all, w_output).astype(jnp.bfloat16).reshape(rep_total, tok_count, -1)
    branch = by_place(rep_exchange(columns)).transpose(1, 0, 2).reshape(tok_count, D)
    middle = residual + branch.astype(jnp.float32)
    scale_two = lax.rsqrt(jnp.mean(middle * middle, -1, keepdims=True) + norm_eps)
    normed_two = (middle * scale_two * gains[1]).astype(jnp.bfloat16)
    normed_two_all = rep_gather(normed_two).reshape(-1, D)
    normed_two_all, grad_top_all = lax.optimization_barrier((normed_two_all, grad_top_all))

    if aligned:
        gate_rows, up_rows, activation = forward_products(normed_two_all, early, late, late.shape[2] // 2)
        g_down = weight_grad(activation, grad_top_all)
        grad_top_all, g_down = lax.optimization_barrier((grad_top_all, g_down))
        grad_gate, grad_up, pieces, branch_pieces = backward_products(
            grad_top_all, gate_rows, up_rows, activation, early, late, late_down
        )
        grad_normed_two = sum_pieces(*pieces)
    else:
        gate_rows = mul(normed_two_all, w_gate)
        up_rows = mul(normed_two_all, w_up)
        sigmoid_gate = jax.nn.sigmoid(gate_rows)
        silu_gate = gate_rows * sigmoid_gate
        activation = (silu_gate * up_rows).astype(jnp.bfloat16)
        g_down = weight_grad(activation, grad_top_all)
        grad_act = mul_back(grad_top_all, w_down)
        grad_gate = (
            grad_act * up_rows * sigmoid_gate * (1.0 + gate_rows * (1.0 - sigmoid_gate))
        ).astype(jnp.bfloat16)
        grad_up = (grad_act * silu_gate).astype(jnp.bfloat16)
        grad_normed_two = own_sum(mul_back(grad_gate, w_gate) + mul_back(grad_up, w_up))
        branch_pieces = (mul(activation, w_down),)
    g_gate = weight_grad(normed_two_all, grad_gate)
    g_up = weight_grad(normed_two_all, grad_up)
    grad_normed_two, g_gate, g_up = lax.optimization_barrier((grad_normed_two, g_gate, g_up))

    def over_tokens(partial):
        return lax.psum_scatter(partial, "fsdp", scatter_dimension=0, tiled=True)

    s_down = over_tokens(g_down)
    s_gate = over_tokens(g_gate)
    s_up = over_tokens(g_up)

    grad_middle = grad_top.astype(jnp.float32) + norm_back(middle, scale_two, gains[1], grad_normed_two)
    grad_parts = grad_middle.astype(jnp.bfloat16).reshape(tok_count, rep_total, -1).transpose(1, 0, 2)
    grad_columns = rep_exchange(by_place(grad_parts)).reshape(rep_total * tok_count, -1)
    grad_attended = rep_features_sum(
        grad_columns.reshape(rep_total, tok_count, -1), w_output
    ).astype(jnp.bfloat16)
    g_output = weight_grad(attended_all, grad_columns)
    g_output = by_place(g_output.reshape(rep_total, q_width, -1)).reshape(D, -1)
    grad_attended, s_down, *branch_pieces = lax.optimization_barrier((grad_attended, s_down, *branch_pieces))
    s_down = rep_gather(s_down)
    branch = sum_pieces(*branch_pieces) if aligned else own_sum(branch_pieces[0])
    block_out = middle + branch
    grad_queries, *grad_blocks = attend_back(
        band_number, glob_spots, wide_cosine, wide_sine, queries, grad_attended, lse, pair_blocks
    )
    returned = [
        shifted(grad_blocks[back_count - distance], "fsdp", -distance)
        for distance in range(1, back_count + 1)
    ]
    glob_grads = add_all(grad_blocks[-1], "fsdp")
    glob_grads, s_gate, s_down, block_out = lax.optimization_barrier(
        (glob_grads, s_gate, s_down, block_out)
    )
    s_gate = rep_gather(s_gate)
    grad_inner = join_grads(
        grad_queries, grad_blocks[-2], selector_all, glob_grads, wide_cosine, wide_sine, returned
    ).reshape(-1, q_width + 2 * kv_width)
    g_inner, s_up = lax.optimization_barrier((weight_grad(normed_one_all, grad_inner), s_up))
    s_up = rep_gather(s_up)
    s_attn = over_tokens(jnp.concatenate([g_inner, g_output], 1))
    grad_normed_one = own_sum(mul_back(grad_inner, w_inner))
    grad_normed_one, s_up, s_gate = lax.optimization_barrier((grad_normed_one, s_up, s_gate))
    grad_input = grad_middle + norm_back(residual, scale_one, gains[0], grad_normed_one)

    gain_terms = jnp.stack(
        [
            jnp.sum(grad_normed_one * residual * scale_one, 0),
            jnp.sum(grad_normed_two * middle * scale_two, 0),
        ]
    )
    square_terms = jnp.stack(
        [jnp.sum(residual * residual), jnp.sum(middle * middle), jnp.sum(block_out * block_out)]
    )
    sums, s_attn = lax.optimization_barrier((jnp.concatenate([gain_terms.reshape(-1), square_terms]), s_attn))

    slot_ids = jnp.arange(tile_total, dtype=jnp.int32)
    inverse = jnp.sum(jnp.where(tile_order[None, :] == slot_ids[:, None], slot_ids[None, :], 0), 1)
    own_slots = place * own_count + jnp.arange(own_count, dtype=jnp.int32)
    owned_tiles = jnp.take(inverse, own_slots, mode="clip")
    if aligned:
        sources = [rep_gather(s_attn), s_gate, s_up, s_down]
        where = np.zeros((4, rep_total, tile_total), np.int32)
        first_col = 0
        for kind, grid in enumerate(layout):
            rows, cols = grid.shape[1:]
            first_col = 0 if kind >= 4 else first_col
            for there in range(rep_total):
                numbers = grid[there].reshape(-1)
                at = np.arange(rows * cols)
                where[0, :, numbers] = max(kind - 3, 0)
                where[2, :, numbers] = (at // cols * BLK)[:, None]
                where[3, :, numbers] = (at % cols * BLK + first_col)[:, None]
                for here in range(rep_total):
                    where[1, here, numbers] = here ^ there
            first_col += cols * BLK
        tile_spots = lax.dynamic_index_in_dim(jnp.asarray(where), place, 1, False)
        meta = jnp.take(tile_spots, owned_tiles, axis=1, mode="clip")
    else:
        splits = [0, q_width, q_width + kv_width, q_width + 2 * kv_width, s_attn.shape[1]]
        stacks = [rep_gather(s_attn[:, low:high]) for low, high in zip(splits, splits[1:])]
        stacks += [s_gate, s_up, s_down]
        sources = [band_tiles(join_slices(stacks, band_total, rep_total))]
        meta = jnp.stack([0 * owned_tiles, owned_tiles, 0 * owned_tiles, 0 * owned_tiles], 0)
    slot_rates = jnp.take(kind_rates(band_total), owned_tiles, mode="clip")
    new_first, new_second, new_master, master_copy = adam(
        meta,
        slot_rates,
        (master[0], first_moment[0], second_moment[0], left_basis[0], right_basis[0]),
        sources,
    )
    sums = add_all(add_all(sums, "rep"), "fsdp")
    gain_grad, square_total = sums[: 2 * D].reshape(2, D), sums[2 * D :]
    new_gain_first = beta_one * gain_first + (1.0 - beta_one) * gain_grad
    new_gain_second = beta_two * gain_second + (1.0 - beta_two) * gain_grad * gain_grad
    gain_step = (
        new_gain_first
        / (1.0 - beta_one**STEP)
        / (jnp.sqrt(new_gain_second / (1.0 - beta_two**STEP)) + adam_eps)
    )
    new_gains = gains - gain_rate * gain_step
    rms_stats = jnp.sqrt(square_total / (rep_total * band_total * tok_count * D))
    return (
        block_out[None],
        grad_input[None],
        new_first[None],
        new_second[None],
        new_master[None],
        master_copy[None],
        new_gain_first,
        new_gain_second,
        new_gains,
        rms_stats,
    )


def solution(mesh):
    in_specs = (
        P("rep", "fsdp", None),
        P("rep", "fsdp", None),
        P("rep", None, "fsdp"),
        P("fsdp", None),
        P("fsdp", "rep", None, None),
        P("fsdp", "rep", None, None),
        P("fsdp", "rep", None, None),
        P("fsdp", "rep", None, None),
        P("fsdp", "rep", None, None),
        P(),
        P(),
        P(),
    )
    out_specs = (
        P("rep", "fsdp", None),
        P("rep", "fsdp", None),
        P("fsdp", "rep", None, None),
        P("fsdp", "rep", None, None),
        P("fsdp", "rep", None, None),
        P("fsdp", "rep", None, None),
        P(),
        P(),
        P(),
        P(),
    )
    return jax.shard_map(
        per_device, mesh=mesh, in_specs=in_specs, out_specs=out_specs, check_vma=False
    )
```

```python
import functools

import jax
import jax.numpy as jnp
import numpy as np
from jax import lax
from jax.experimental import pallas as pl
from jax.experimental.pallas import tpu as pltpu
from jax.sharding import PartitionSpec as P

D = 2048
H = 32
KVH = 8
HD = 64
FF = 8192
WINDOW = 512
BLK = 128
STEP = 10


norm_eps = 1e-05
rope_theta = 500000.0
beta_one = 0.5
beta_two = 0.5
adam_eps = 1e-08
weight_decay = 0.1
gain_rate = 0.5
masked_value = -1e30


def matrix_shapes():
    kv_width = KVH * HD
    return [(D, D), (D, kv_width), (D, kv_width), (D, D), (D, FF), (D, FF), (FF, D)]


def kind_rates(band_total):
    rate_list = [
        D ** (-0.5),
        D ** (-0.5),
        D ** (-0.5),
        (D * 8 // WINDOW) ** (-0.5),
        D ** (-0.5),
        D ** (-0.5),
        FF ** (-0.5),
    ]
    pieces = []
    for (row_total, col_total), rate_value in zip(matrix_shapes(), rate_list):
        tile_count = row_total // band_total // BLK * (col_total // BLK)
        pieces.append(jnp.full((tile_count,), rate_value, jnp.float32))
    return jnp.concatenate(pieces)


def band_matrices(tiles, band_total):
    matrices = []
    offset = 0
    for row_total, col_total in matrix_shapes():
        band_rows = row_total // band_total
        tile_count = band_rows // BLK * (col_total // BLK)
        segment = tiles[offset : offset + tile_count].reshape(
            band_rows // BLK, col_total // BLK, BLK, BLK
        )
        matrices.append(segment.transpose(0, 2, 1, 3).reshape(band_rows, col_total))
        offset += tile_count
    return matrices


def band_tiles(matrices):
    pieces = []
    for matrix in matrices:
        row_count, col_count = matrix.shape
        segment = matrix.reshape(row_count // BLK, BLK, col_count // BLK, BLK).transpose(0, 2, 1, 3)
        pieces.append(segment.reshape(-1, BLK, BLK))
    return jnp.concatenate(pieces, 0)


def rope_tables(position):
    halves = jnp.arange(HD // 2, dtype=jnp.float32) * (2.0 / HD)
    frequency = rope_theta ** (-halves)
    angles = position.astype(jnp.float32)[:, None] * frequency[None, :]
    angles = jnp.concatenate([angles, angles], 1)
    return (jnp.cos(angles), jnp.sin(angles))


def rotate(vectors, cosine_table, sine_table):
    half_width = vectors.shape[-1] // 2
    turned = jnp.concatenate([-vectors[..., half_width:], vectors[..., :half_width]], -1)
    return vectors * cosine_table[:, None, :] + turned * sine_table[:, None, :]


def rotate_back(grad_rows, cosine_table, sine_table):
    half_width = grad_rows.shape[-1] // 2
    scaled = grad_rows * sine_table[:, None, :]
    turned = jnp.concatenate([scaled[..., half_width:], -scaled[..., :half_width]], -1)
    return grad_rows * cosine_table[:, None, :] + turned


def norm_back(values, row_scale, gain_row, grad_rows):
    weighted = grad_rows * gain_row
    return row_scale * weighted - values * row_scale**3 * jnp.mean(
        weighted * values, -1, keepdims=True
    )


def to_rep(block, distance):
    route = [(i, i ^ distance) for i in range(lax.axis_size("rep"))]
    return lax.ppermute(block, "rep", route)


def square():
    return lax.axis_size("rep") == 4


def square_pieces(block):
    cut = block.shape[0] // 2
    near = to_rep(block, 1)
    far = to_rep(block, 2)
    return block, near, far, to_rep(near[:cut], 2), to_rep(far[cut:], 1)


def rep_gather(block):
    if not square():
        return lax.all_gather(block, "rep", axis=0)
    own, near, far, low, high = square_pieces(block)
    return jnp.concatenate([own, near, far, low, high], 0).reshape((4,) + block.shape)


def rep_of(entry):
    place = lax.axis_index("rep")
    return place ^ entry if square() else entry


def rep_scatter(parts):
    if not square():
        flat = parts.reshape(-1, parts.shape[-1])
        return lax.psum_scatter(flat, "rep", scatter_dimension=0, tiled=True).astype(jnp.float32)
    half = parts.shape[-1] // 2
    low, high = parts[..., :half], parts[..., half:]
    return sum_pieces(
        jnp.stack([low[0], low[2]], 0), jnp.stack([low[1], low[3]], 0), high[:2], high[2:]
    )


def sum_pieces(low_kept, low_sent, high_kept, high_sent):
    totals = []
    for kept, sent, first, second in ((low_kept, low_sent, 1, 2), (high_kept, high_sent, 2, 1)):
        came = to_rep(sent, first)
        other = (kept[1].astype(jnp.float32) + came[1].astype(jnp.float32)).astype(kept.dtype)
        own = kept[0].astype(jnp.float32) + came[0].astype(jnp.float32)
        totals.append(own + to_rep(other, second).astype(jnp.float32))
    return jnp.concatenate(totals, -1)


def add_all(value, axis):
    size = lax.axis_size(axis)
    total = value.astype(jnp.float32)
    distance = 1
    while distance < size:
        count = 2 if (size // distance).bit_length() % 2 == 0 else 4
        low = total.astype(value.dtype)
        others = []
        for step in range(1, count):
            route = [(i, i ^ (step * distance)) for i in range(size)]
            others.append(lax.ppermute(low, axis, route).astype(jnp.float32))
        total = total + others[0]
        if count == 4:
            total = total + (others[1] + others[2])
        distance *= count
    return total


def rep_features(block):
    if not square():
        return lax.all_gather(block, "rep", axis=2, tiled=True)
    own, near, far, low, high = square_pieces(block)
    return jnp.concatenate(
        [
            own,
            jnp.stack([near[1], near[0], near[3], near[2]], 0),
            jnp.stack([far[2], far[3], far[0], far[1]], 0),
            jnp.stack([high[1], high[0], low[1], low[0]], 0),
        ],
        2,
    )


def write_pieces(entry, rows, values, refs):
    low_kept, low_sent, high_kept, high_sent = refs
    half = low_kept.shape[-1]
    values = values.astype(jnp.bfloat16)
    (low_sent if entry % 2 else low_kept)[entry // 2, rows] = values[:, :half]
    (high_sent if entry // 2 else high_kept)[entry % 2, rows] = values[:, half:]


def swapped_kernel(x_ref, w_ref, *refs):
    reps, rows, _ = x_ref.shape
    width = w_ref.shape[0] // reps
    for entry in range(reps):
        weight = w_ref[entry * width : (entry + 1) * width]
        for there in range(reps):
            product = over_last(x_ref[there ^ entry], weight)
            write_pieces(entry, slice(there * rows, (there + 1) * rows), product, refs)


def rep_features_sum(columns, weight):
    reps, rows, depth = columns.shape
    width = weight.shape[0] // reps
    if square():
        pieces = pl.pallas_call(
            swapped_kernel,
            out_shape=[jax.ShapeDtypeStruct((2, reps * rows, width // 2), jnp.bfloat16)] * 4,
            compiler_params=pltpu.CompilerParams(vmem_limit_bytes=32 * 2**20),
            cost_estimate=pl.CostEstimate(
                flops=2 * reps * columns.size * width,
                bytes_accessed=10 * columns.size,
                transcendentals=0,
            ),
        )(columns, weight)
        total = sum_pieces(*pieces)
    else:
        product = over_last(columns.reshape(-1, depth), weight).astype(jnp.bfloat16)
        swapped = product.reshape(reps, rows, reps, width).transpose(2, 0, 1, 3)
        total = rep_scatter(swapped.reshape(reps, reps * rows, width))
    return total.reshape(reps, rows, width)


def rep_exchange(parts):
    if not square():
        return lax.all_to_all(parts, "rep", 0, 0)
    return jnp.stack([parts[0]] + [to_rep(parts[entry], entry) for entry in (1, 2, 3)], 0)


def by_place(parts):
    entries = [rep_of(entry) for entry in range(parts.shape[0])]
    return jnp.stack([lax.dynamic_index_in_dim(parts, entry, 0, False) for entry in entries], 0)


def shifted(block, axis, distance):
    devices = range(lax.axis_size(axis))
    route = [(i - distance, i) for i in devices if i - distance in devices]
    return lax.ppermute(block, axis, route)


def tile_offsets(band_total):
    offsets = [0]
    for row_total, col_total in matrix_shapes():
        offsets.append(offsets[-1] + row_total // band_total // BLK * (col_total // BLK))
    return offsets


def whole_tiles(band_total, rep_total):
    return KVH * HD // rep_total % BLK == 0 and FF // band_total // rep_total % BLK == 0


def slice_layout(band_total, rep_total):
    offsets = tile_offsets(band_total)
    layout = []
    for kind, (row_total, col_total) in enumerate(matrix_shapes()):
        rows, cols = row_total // band_total // BLK, col_total // BLK
        grid = offsets[kind] + np.arange(rows * cols).reshape(rows, cols)
        if kind == 6:
            layout.append(grid.reshape(rep_total, rows // rep_total, cols))
        elif kind in (4, 5):
            cut = grid.reshape(rows, band_total, rep_total, -1).transpose(2, 0, 1, 3)
            layout.append(cut.reshape(rep_total, rows, -1))
        else:
            layout.append(grid.reshape(rows, rep_total, -1).transpose(1, 0, 2))
    return layout


def tiles_to_matrix(tiles):
    rows, cols = tiles.shape[:2]
    return tiles.transpose(0, 2, 1, 3).reshape(rows * BLK, cols * BLK)


def matrix_to_tiles(matrix):
    rows, cols = matrix.shape
    cut = matrix.reshape(rows // BLK, BLK, cols // BLK, BLK)
    return cut.transpose(0, 2, 1, 3).reshape(-1, BLK, BLK)


def cut_slices(matrices, band_total, rep_total):
    place = lax.axis_index("rep")
    slices = []
    for kind, matrix in enumerate(matrices):
        rows, cols = matrix.shape
        if kind == 6:
            slices.append(lax.dynamic_slice_in_dim(matrix, place * (rows // rep_total), rows // rep_total, 0))
        elif kind in (4, 5):
            cut = matrix.reshape(rows, band_total, rep_total, -1)
            slices.append(lax.dynamic_index_in_dim(cut, place, 2, False).reshape(rows, -1))
        else:
            slices.append(lax.dynamic_slice_in_dim(matrix, place * (cols // rep_total), cols // rep_total, 1))
    return slices


def join_slices(stacks, band_total, rep_total):
    matrices = []
    for kind, stack in enumerate(stacks):
        rows, cols = stack.shape[1:]
        if kind == 6:
            matrices.append(stack.reshape(-1, cols))
        elif kind in (4, 5):
            cut = stack.reshape(rep_total, rows, band_total, -1).transpose(1, 2, 0, 3)
            matrices.append(cut.reshape(rows, -1))
        else:
            matrices.append(stack.transpose(1, 0, 2).reshape(rows, -1))
    return matrices


def gather_kernel(grids, meta, *refs):
    source_total = len(refs) - len(grids) - 1
    sources, targets, done = refs[:source_total], refs[source_total:-1], refs[-1]
    height = sources[0].shape[1]
    start = 0
    for place, (target, (rows, cols)) in enumerate(zip(targets, grids)):

        def one(tile, carry, target=target, rows=rows, cols=cols, start=start, place=place):
            kind = meta[0, start + tile]
            row = meta[1, start + tile]
            across = tile % cols
            top = pl.multiple_of((across // 2 * rows + tile // cols) * height, height)
            left = pl.multiple_of(across % 2 * BLK, BLK)
            for number, source in enumerate(sources):

                @pl.when(kind == number)
                def _(source=source):
                    pltpu.make_async_copy(
                        source.at[row], target.at[pl.ds(top, height), pl.ds(left, BLK)], done.at[place]
                    ).start()

            return carry

        lax.fori_loop(0, rows * cols, one, 0)
        start += rows * cols
    for place, target in enumerate(targets):
        pltpu.make_async_copy(target, target, done.at[place]).wait()


def gather_strips(sources, meta, grids):
    anywhere = pl.BlockSpec(memory_space=pl.ANY)
    height = sources[0].shape[1]
    out_shape = [
        jax.ShapeDtypeStruct((cols // 2 * rows * height, 2 * BLK), jnp.bfloat16) for rows, cols in grids
    ]
    return pl.pallas_call(
        functools.partial(gather_kernel, grids),
        out_shape=out_shape,
        grid_spec=pltpu.PrefetchScalarGridSpec(
            num_scalar_prefetch=1,
            grid=(1,),
            in_specs=[anywhere] * len(sources),
            out_specs=[pl.BlockSpec(shape.shape, lambda i, *_: (0, 0)) for shape in out_shape],
            scratch_shapes=[pltpu.SemaphoreType.DMA((len(grids),))],
        ),
        compiler_params=pltpu.CompilerParams(vmem_limit_bytes=32 * 2**20),
        cost_estimate=pl.CostEstimate(
            flops=0, bytes_accessed=sum(4 * shape.size for shape in out_shape), transcendentals=0
        ),
    )(meta, *sources)


def place_kernel(entries, rows, cols, meta, low, high, out_ref, done):
    out_ref[...] = jnp.zeros_like(out_ref)
    height = low.shape[1]

    def copies(tile):
        entry, rest = tile // (rows * cols), tile % (rows * cols)
        top = rest // cols * (2 * height)
        left = pl.multiple_of(rest % cols * BLK, BLK)
        return [
            pltpu.make_async_copy(
                half.at[meta[1, tile]],
                out_ref.at[entry, pl.ds(pl.multiple_of(top + part * height, height), height), pl.ds(left, BLK)],
                done.at[part],
            )
            for part, half in enumerate((low, high))
        ]

    def begin(tile, carry):
        @pl.when(meta[0, tile] == 1)
        def _():
            for copy in copies(tile):
                copy.start()

        return carry

    def finish(tile, carry):
        @pl.when(meta[0, tile] == 1)
        def _():
            for copy in copies(tile):
                copy.wait()

        return carry

    lax.fori_loop(0, entries * rows * cols, begin, 0)
    lax.fori_loop(0, entries * rows * cols, finish, 0)


def place_tiles(low, high, meta, entries, rows, cols):
    shape = (entries, rows * BLK, cols * BLK)
    anywhere = pl.BlockSpec(memory_space=pl.ANY)
    return pl.pallas_call(
        functools.partial(place_kernel, entries, rows, cols),
        out_shape=jax.ShapeDtypeStruct(shape, jnp.bfloat16),
        grid_spec=pltpu.PrefetchScalarGridSpec(
            num_scalar_prefetch=1,
            grid=(1,),
            in_specs=[anywhere, anywhere],
            out_specs=pl.BlockSpec(shape, lambda i, *_: (0, 0, 0)),
            scratch_shapes=[pltpu.SemaphoreType.DMA((2,))],
        ),
        compiler_params=pltpu.CompilerParams(vmem_limit_bytes=32 * 2**20),
        cost_estimate=pl.CostEstimate(
            flops=0, bytes_accessed=4 * entries * rows * cols * BLK * BLK, transcendentals=0
        ),
    )(meta, low, high)


def half_turn(values):
    lane = lax.broadcasted_iota(jnp.int32, values.shape, 1)
    lanes = values.shape[1]
    first = lane % HD < HD // 2
    return first, jnp.where(
        first, pltpu.roll(values, lanes - HD // 2, 1), pltpu.roll(values, HD // 2, 1)
    )


def strip_copies(early, late, target, done):
    return [
        pltpu.make_async_copy(half, target.at[:, :, number], done.at[number])
        for number, half in enumerate((early, late))
    ]


def forward_kernel(x_ref, early, late, gate_ref, up_ref, act_ref, weights, done):
    step, steps = pl.program_id(0), pl.num_programs(0)
    slot = step % 2
    width = weights.shape[-1]

    def copies(number, at_step, at_slot):
        strip = number * steps + at_step
        return strip_copies(
            early.at[:, strip], late.at[:, strip], weights.at[number, at_slot], done.at[number, at_slot]
        )

    def fetch(at_step, at_slot):
        for number in range(2):
            for copy in copies(number, at_step, at_slot):
                copy.start()

    @pl.when(step == 0)
    def _():
        fetch(0, 0)

    @pl.when(step + 1 < steps)
    def _():
        fetch(step + 1, 1 - slot)

    products = []
    for number in range(2):
        for copy in copies(number, step, slot):
            copy.wait()
        weight = weights[number, slot].reshape(-1, width)
        products.append(jnp.dot(x_ref[...], weight, preferred_element_type=jnp.float32))
    gate, up = products
    gate_ref[...] = gate.astype(jnp.bfloat16)
    up_ref[...] = up.astype(jnp.bfloat16)
    act_ref[...] = (gate * jax.nn.sigmoid(gate) * up).astype(jnp.bfloat16)


def forward_products(rows, early, late, columns):
    tokens, depth = rows.shape
    bands, _, tiles, half, width = early.shape
    block = pl.BlockSpec((tokens, width), lambda n: (0, n))
    anywhere = pl.BlockSpec(memory_space=pl.ANY)
    return pl.pallas_call(
        forward_kernel,
        out_shape=[jax.ShapeDtypeStruct((tokens, columns), jnp.bfloat16)] * 3,
        grid=(columns // width,),
        in_specs=[pl.BlockSpec(rows.shape, lambda n: (0, 0)), anywhere, anywhere],
        out_specs=[block] * 3,
        scratch_shapes=[
            pltpu.VMEM((2, 2, bands, tiles, 2, half, width), jnp.bfloat16),
            pltpu.SemaphoreType.DMA((2, 2, 2)),
        ],
        compiler_params=pltpu.CompilerParams(vmem_limit_bytes=48 * 2**20),
        cost_estimate=pl.CostEstimate(
            flops=tokens * depth * columns // 8, bytes_accessed=2 * rows.size, transcendentals=0
        ),
    )(rows, early, late)


def backward_kernel(top_ref, gate_ref, up_ref, act_ref, early, late, late_down, *refs):
    dgate_ref, dup_ref = refs[:2]
    pieces, branch_pieces = refs[2:6], refs[6:10]
    weights, downs, total, branch, done, down_done = refs[10:]
    step, steps = pl.program_id(0), pl.num_programs(0)
    slot = step % 2
    strips, width = downs.shape[1], downs.shape[-1]

    def down_copies(at_step, at_slot):
        return strip_copies(
            early.at[at_step, pl.ds(2 * steps, strips)],
            late_down.at[at_step],
            downs.at[at_slot],
            down_done.at[at_slot],
        )

    def copies(number, at_step, at_slot):
        strip = number * steps + at_step
        return strip_copies(
            early.at[:, strip], late.at[:, strip], weights.at[number, at_slot], done.at[number, at_slot]
        )

    def fetch(at_step, at_slot):
        for copy in down_copies(at_step, at_slot):
            copy.start()
        for number in range(2):
            for copy in copies(number, at_step, at_slot):
                copy.start()

    @pl.when(step == 0)
    def _():
        fetch(0, 0)
        total[...] = jnp.zeros_like(total)
        branch[...] = jnp.zeros_like(branch)

    @pl.when(step + 1 < steps)
    def _():
        fetch(step + 1, 1 - slot)

    for copy in down_copies(step, slot):
        copy.wait()
    grad_act = 0.0
    for strip in range(strips):
        lanes = slice(strip * width, (strip + 1) * width)
        down = downs[slot, strip].reshape(-1, width)
        grad_act = grad_act + over_last(top_ref[:, lanes], down)
        branch[:, lanes] += jnp.dot(act_ref[...], down, preferred_element_type=jnp.float32)
    gate = gate_ref[...].astype(jnp.float32)
    up = up_ref[...].astype(jnp.float32)
    sigmoid_gate = jax.nn.sigmoid(gate)
    grad_gate = (grad_act * up * sigmoid_gate * (1.0 + gate * (1.0 - sigmoid_gate))).astype(jnp.bfloat16)
    grad_up = (grad_act * (gate * sigmoid_gate)).astype(jnp.bfloat16)
    dgate_ref[...] = grad_gate
    dup_ref[...] = grad_up
    for number, grads in enumerate((grad_gate, grad_up)):
        for copy in copies(number, step, slot):
            copy.wait()
        total[...] += over_last(grads, weights[number, slot].reshape(-1, width))

    @pl.when(step == steps - 1)
    def _():
        rows = total.shape[0] // 4
        for entry in range(4):
            part = slice(entry * rows, (entry + 1) * rows)
            write_pieces(entry, slice(0, rows), total[part], pieces)
            write_pieces(entry, slice(0, rows), branch[part], branch_pieces)


def backward_products(top, gate, up, act, early, late, late_down):
    tokens, depth = top.shape
    columns = gate.shape[1]
    bands, _, tiles, half, width = early.shape
    strips = late_down.shape[1]
    block = pl.BlockSpec((tokens, width), lambda n: (0, n))
    anywhere = pl.BlockSpec(memory_space=pl.ANY)
    piece = jax.ShapeDtypeStruct((2, tokens // 4, depth // 2), jnp.bfloat16)
    grads = jax.ShapeDtypeStruct((tokens, columns), jnp.bfloat16)
    outs = pl.pallas_call(
        backward_kernel,
        out_shape=[grads] * 2 + [piece] * 8,
        grid=(columns // width,),
        in_specs=[pl.BlockSpec(top.shape, lambda n: (0, 0))] + [block] * 3 + [anywhere] * 3,
        out_specs=[block] * 2 + [pl.BlockSpec(piece.shape, lambda n: (0, 0, 0))] * 8,
        scratch_shapes=[
            pltpu.VMEM((2, 2, bands, tiles, 2, half, width), jnp.bfloat16),
            pltpu.VMEM((2, strips, tiles, 2, half, width), jnp.bfloat16),
            pltpu.VMEM((tokens, depth), jnp.float32),
            pltpu.VMEM((tokens, depth), jnp.float32),
            pltpu.SemaphoreType.DMA((2, 2, 2)),
            pltpu.SemaphoreType.DMA((2, 2)),
        ],
        compiler_params=pltpu.CompilerParams(vmem_limit_bytes=60 * 2**20),
        cost_estimate=pl.CostEstimate(
            flops=8 * tokens * depth * columns, bytes_accessed=8 * columns * depth, transcendentals=0
        ),
    )(top, gate, up, act, early, late, late_down)
    return outs[0], outs[1], outs[2:6], outs[6:10]


def rope_kernel(q_width, kv_width, x_ref, cos_ref, sin_ref, *outs):
    width = x_ref.shape[-1]
    for start in range(0, width, BLK):
        values = x_ref[0, :, start : start + BLK]
        first, turned = half_turn(values)
        sines = sin_ref[0]
        turned_rows = values * cos_ref[0] + turned * jnp.where(first, -sines, sines)
        if start + BLK > q_width + kv_width:
            column = lax.broadcasted_iota(jnp.int32, values.shape, 1) + start
            turned_rows = jnp.where(column >= q_width + kv_width, values, turned_rows)
        if start < q_width:
            outs[0][0, :, start : start + BLK] = (turned_rows * HD ** (-0.5)).astype(jnp.bfloat16)
        else:
            outs[-1][0, :, start - q_width : start - q_width + BLK] = turned_rows.astype(jnp.bfloat16)


def rope_rows(inner, rows, row_block, q_width, kv_width, cosines, sines, with_queries=True):
    seqs, _, width = inner.shape
    shared = cosines.shape[0] == 1
    table = pl.BlockSpec((1, rows, BLK), lambda s: (0 if shared else s, 0, 0))
    widths = [q_width, 2 * kv_width]
    column_block = 0
    if not with_queries:
        width, column_block = 2 * kv_width, q_width // (2 * kv_width)
        widths, q_width = widths[1:], 0
    return pl.pallas_call(
        functools.partial(rope_kernel, q_width, kv_width),
        out_shape=[jax.ShapeDtypeStruct((seqs, rows, w), jnp.bfloat16) for w in widths],
        grid=(seqs,),
        in_specs=[pl.BlockSpec((1, rows, width), lambda s: (s, row_block, column_block)), table, table],
        out_specs=[pl.BlockSpec((1, rows, w), lambda s: (s, 0, 0)) for w in widths],
        cost_estimate=pl.CostEstimate(
            flops=6 * seqs * rows * width, bytes_accessed=6 * seqs * rows * width, transcendentals=0
        ),
    )(inner, cosines, sines)


def fill_bias(band_ref, gpos_ref, bias_ref, rows, window_len):
    band = band_ref[0]

    @pl.when(pl.program_id(0) == 0)
    def _():
        key = lax.broadcasted_iota(jnp.int32, (window_len, rows), 0) + (
            band * rows - (window_len - rows)
        )
        query = lax.broadcasted_iota(jnp.int32, (window_len, rows), 1) + band * rows
        inside = (key > query - WINDOW) & (key <= query) & (key >= 0)
        bias_ref[:window_len] = jnp.where(inside, 0.0, masked_value)

    glob_total = gpos_ref.shape[1]
    query = lax.broadcasted_iota(jnp.int32, (glob_total, rows), 1) + (band * rows - WINDOW)
    spot = jnp.broadcast_to(gpos_ref[0][:, :1], (glob_total, rows))
    bias_ref[window_len:] = jnp.where(spot <= query.astype(jnp.float32), 0.0, masked_value)


def over_last(left, right):
    return lax.dot_general(left, right, (((1,), (1,)), ((), ())), preferred_element_type=jnp.float32)


def over_first(left, right):
    return lax.dot_general(left, right, (((0,), (0,)), ((), ())), preferred_element_type=jnp.float32)


def attend_kernel(block_total, band_ref, gpos_ref, q_ref, *refs):
    blocks, (out_ref, lse_ref, bias_ref) = refs[:block_total], refs[block_total:]
    rows, q_width = q_ref.shape[1:]
    kv_width = blocks[0].shape[2] // 2
    heads, group = q_width // HD, q_width // kv_width
    window_len = rows * (block_total - 1)
    fill_bias(band_ref, gpos_ref, bias_ref, rows, window_len)
    starts = [rows * number for number in range(block_total)]
    pending = []
    for head in range(heads):
        left = head // group * HD
        queries = q_ref[0, :, head * HD : (head + 1) * HD]
        scores = [
            over_last(block[0, :, left : left + HD], queries)
            + bias_ref[start : start + block.shape[1]]
            for block, start in zip(blocks, starts)
        ]
        top = functools.reduce(jnp.maximum, [jnp.max(part, 0, keepdims=True) for part in scores])
        total = 0.0
        mixed = 0.0
        for block, part in zip(blocks, scores):
            weights = jnp.exp(part - top)
            total = total + jnp.sum(weights, 0, keepdims=True)
            mixed = mixed + over_first(
                block[0, :, kv_width + left : kv_width + left + HD], weights.astype(jnp.bfloat16)
            )
        lse_ref[0, head : head + 1, :] = top + jnp.log(total)
        pending.append(mixed / total)
        if len(pending) * HD == BLK or head == heads - 1:
            stop = (head + 1) * HD
            both = jnp.concatenate(pending, 0).T
            out_ref[0, :, stop - both.shape[1] : stop] = both.astype(jnp.bfloat16)
            pending = []


def attend(band, gpos, queries, blocks):
    seqs, rows, q_width = queries.shape
    heads = q_width // HD
    key_total = sum(block.shape[1] for block in blocks)

    def whole(array):
        return pl.BlockSpec((1,) + array.shape[1:], lambda s, *_: (s, 0, 0))

    out_shape = [
        jax.ShapeDtypeStruct((seqs, rows, q_width), jnp.bfloat16),
        jax.ShapeDtypeStruct((seqs, heads, rows), jnp.float32),
    ]
    return pl.pallas_call(
        functools.partial(attend_kernel, len(blocks)),
        out_shape=out_shape,
        grid_spec=pltpu.PrefetchScalarGridSpec(
            num_scalar_prefetch=1,
            grid=(seqs,),
            in_specs=[whole(array) for array in (gpos, queries, *blocks)],
            out_specs=[whole(array) for array in out_shape],
            scratch_shapes=[pltpu.VMEM((key_total, rows), jnp.float32)],
        ),
        compiler_params=pltpu.CompilerParams(vmem_limit_bytes=48 * 2**20),
        cost_estimate=pl.CostEstimate(
            flops=16 * seqs * heads * rows * key_total * HD,
            bytes_accessed=4 * queries.size,
            transcendentals=seqs * heads * rows * key_total,
        ),
    )(band, gpos, queries, *blocks)


def attend_back_kernel(block_total, band_ref, gpos_ref, cos_ref, sin_ref, q_ref, grad_ref, lse_ref, *refs):
    blocks = refs[:block_total]
    dq_ref = refs[block_total]
    out_refs = refs[block_total + 1 : 2 * block_total + 1]
    bias_ref = refs[-1]
    rows, q_width = q_ref.shape[1:]
    kv_width = blocks[0].shape[2] // 2
    heads, group = q_width // HD, q_width // kv_width
    window_len = rows * (block_total - 1)
    fill_bias(band_ref, gpos_ref, bias_ref, rows, window_len)
    starts = [rows * number for number in range(block_total)]
    pending = []
    for kv_head in range(kv_width // HD):
        left = kv_head * HD
        key_sums = [0.0] * block_total
        value_sums = [0.0] * block_total
        for head in range(kv_head * group, (kv_head + 1) * group):
            queries = q_ref[0, :, head * HD : (head + 1) * HD]
            grads = grad_ref[0, :, head * HD : (head + 1) * HD]
            lse = lse_ref[0, head : head + 1, :]
            soft, soft_grads = [], []
            inner = 0.0
            for number, (block, start) in enumerate(zip(blocks, starts)):
                part = over_last(block[0, :, left : left + HD], queries)
                part = jnp.exp(part + bias_ref[start : start + block.shape[1]] - lse)
                slope = over_last(block[0, :, kv_width + left : kv_width + left + HD], grads)
                inner = inner + jnp.sum(part * slope, 0, keepdims=True)
                soft.append(part)
                soft_grads.append(slope)
            turned = 0.0
            for number, block in enumerate(blocks):
                score_grads = (soft[number] * (soft_grads[number] - inner)).astype(jnp.bfloat16)
                value_sums[number] = value_sums[number] + jnp.dot(
                    soft[number].astype(jnp.bfloat16), grads, preferred_element_type=jnp.float32
                )
                key_sums[number] = key_sums[number] + jnp.dot(
                    score_grads, queries, preferred_element_type=jnp.float32
                )
                turned = turned + over_first(block[0, :, left : left + HD], score_grads)
            pending.append(turned)
            if len(pending) * HD == BLK or head == heads - 1:
                stop = (head + 1) * HD
                both = jnp.concatenate(pending, 0).T * HD ** (-0.5)
                pending = []
                first, other = half_turn(both * sin_ref[0])
                both = both * cos_ref[0] + jnp.where(first, other, -other)
                dq_ref[0, :, stop - both.shape[1] : stop] = both.astype(jnp.bfloat16)
        for number, out_ref in enumerate(out_refs):
            out_ref[0, :, left : left + HD] = key_sums[number].astype(out_ref.dtype)
            out_ref[0, :, kv_width + left : kv_width + left + HD] = value_sums[number].astype(
                out_ref.dtype
            )


def attend_back(band, gpos, cosines, sines, queries, grads, lse, blocks):
    seqs, rows, q_width = queries.shape
    heads = q_width // HD
    key_total = sum(block.shape[1] for block in blocks)

    def whole(array):
        return pl.BlockSpec((1,) + array.shape[1:], lambda s, *_: (s, 0, 0))

    table = pl.BlockSpec((1, rows, BLK), lambda s, *_: (0, 0, 0))
    out_shape = [jax.ShapeDtypeStruct(queries.shape, jnp.bfloat16)]
    for number, block in enumerate(blocks):
        own = number == len(blocks) - 2
        out_shape.append(jax.ShapeDtypeStruct(block.shape, jnp.float32 if own else jnp.bfloat16))
    return pl.pallas_call(
        functools.partial(attend_back_kernel, len(blocks)),
        out_shape=out_shape,
        grid_spec=pltpu.PrefetchScalarGridSpec(
            num_scalar_prefetch=1,
            grid=(seqs,),
            in_specs=[whole(gpos), table, table]
            + [whole(array) for array in (queries, grads, lse, *blocks)],
            out_specs=[whole(array) for array in out_shape],
            scratch_shapes=[pltpu.VMEM((key_total, rows), jnp.float32)],
        ),
        compiler_params=pltpu.CompilerParams(vmem_limit_bytes=48 * 2**20),
        cost_estimate=pl.CostEstimate(
            flops=40 * seqs * heads * rows * key_total * HD,
            bytes_accessed=8 * queries.size,
            transcendentals=seqs * heads * rows * key_total,
        ),
    )(band, gpos, cosines, sines, queries, grads, lse, *blocks)


def join_kernel(q_width, kv_width, dq_ref, own_ref, pick_ref, glob_ref, cos_ref, sin_ref, *refs):
    back_refs, out_ref = refs[:-1], refs[-1]
    out_ref[0, :, :q_width] = dq_ref[0]
    picked = lax.dot_general(
        pick_ref[0].astype(jnp.float32),
        glob_ref[0],
        (((0,), (0,)), ((), ())),
        precision=lax.Precision.HIGHEST,
        preferred_element_type=jnp.float32,
    )
    for start in range(0, 2 * kv_width, BLK):
        lanes = slice(start, start + BLK)
        total = own_ref[0, :, lanes] + picked[:, lanes]
        for back_ref in back_refs:
            total = total + back_ref[0, :, lanes].astype(jnp.float32)
        first, other = half_turn(total * sin_ref[0])
        turned = total * cos_ref[0] + jnp.where(first, other, -other)
        column = lax.broadcasted_iota(jnp.int32, total.shape, 1) + start
        turned = jnp.where(column >= kv_width, total, turned)
        out_ref[0, :, q_width + start : q_width + start + BLK] = turned.astype(jnp.bfloat16)


def join_grads(dq, own, picks, globs, cosines, sines, backs):
    seqs, rows, q_width = dq.shape
    kv_width = own.shape[2] // 2

    def whole(array):
        return pl.BlockSpec((1,) + array.shape[1:], lambda s: (s, 0, 0))

    table = pl.BlockSpec((1, rows, BLK), lambda s: (0, 0, 0))
    out_shape = jax.ShapeDtypeStruct((seqs, rows, q_width + 2 * kv_width), jnp.bfloat16)
    return pl.pallas_call(
        functools.partial(join_kernel, q_width, kv_width),
        out_shape=out_shape,
        grid=(seqs,),
        in_specs=[whole(dq), whole(own), whole(picks), whole(globs), table, table]
        + [whole(back) for back in backs],
        out_specs=whole(out_shape),
        cost_estimate=pl.CostEstimate(
            flops=20 * own.size, bytes_accessed=4 * dq.size + 12 * own.size, transcendentals=0
        ),
    )(dq, own, picks, globs, cosines, sines, *backs)


def adam_kernel(batch, meta, rates, *refs):
    master_ref, first_ref, second_ref, left_ref, right_ref = refs[:5]
    sources = refs[5:-6]
    new_first_ref, new_second_ref, new_master_ref, copy_ref, tiles, arrived = refs[-6:]
    step, steps = pl.program_id(0), pl.num_programs(0)
    slot = step % 2

    def fetch(at_step, at_slot):
        for place in range(batch):
            tile = at_step * batch + place
            for number, source in enumerate(sources):

                @pl.when(meta[0, tile] == number)
                def _(source=source, tile=tile, place=place):
                    top = pl.multiple_of(meta[2, tile], BLK)
                    left = pl.multiple_of(meta[3, tile], BLK)
                    pltpu.make_async_copy(
                        source.at[meta[1, tile], pl.ds(top, BLK), pl.ds(left, BLK)],
                        tiles.at[at_slot, place],
                        arrived.at[at_slot],
                    ).start()

    @pl.when(step == 0)
    def _():
        fetch(0, 0)

    @pl.when(step + 1 < steps)
    def _():
        fetch(step + 1, 1 - slot)

    pltpu.make_async_copy(tiles.at[slot], tiles.at[slot], arrived.at[slot]).wait()
    places = range(batch)
    lefts = [left_ref[place].astype(jnp.bfloat16) for place in places]
    rights = [right_ref[place].astype(jnp.bfloat16) for place in places]
    turned = [over_first(lefts[place], tiles[slot, place]).astype(jnp.bfloat16) for place in places]
    rotated = [
        jnp.dot(turned[place], rights[place], preferred_element_type=jnp.float32) for place in places
    ]
    directions = []
    for place in places:
        new_first = beta_one * first_ref[place] + (1.0 - beta_one) * rotated[place]
        new_second = beta_two * second_ref[place] + (1.0 - beta_two) * rotated[place] * rotated[place]
        direction = (new_first * (1.0 / (1.0 - beta_one**STEP))) / (
            jnp.sqrt(new_second * (1.0 / (1.0 - beta_two**STEP))) + adam_eps
        )
        new_first_ref[place] = new_first
        new_second_ref[place] = new_second
        directions.append(direction.astype(jnp.bfloat16))
    updates = [
        jnp.dot(lefts[place], directions[place], preferred_element_type=jnp.float32) for place in places
    ]
    updates = [over_last(updates[place].astype(jnp.bfloat16), rights[place]) for place in places]
    for place in places:
        old = master_ref[place]
        new_master = old - rates[step * batch + place] * (updates[place] + weight_decay * old)
        new_master_ref[place] = new_master
        copy_ref[place] = new_master.astype(jnp.bfloat16)


def adam(meta, rates, state, sources):
    count = state[0].shape[0]
    batch = max(size for size in (1, 2, 4) if count % size == 0)
    block = pl.BlockSpec((batch, BLK, BLK), lambda s, *_: (s, 0, 0))
    anywhere = pl.BlockSpec(memory_space=pl.ANY)
    shape = (count, BLK, BLK)
    return pl.pallas_call(
        functools.partial(adam_kernel, batch),
        out_shape=[jax.ShapeDtypeStruct(shape, jnp.float32)] * 3
        + [jax.ShapeDtypeStruct(shape, jnp.bfloat16)],
        grid_spec=pltpu.PrefetchScalarGridSpec(
            num_scalar_prefetch=2,
            grid=(count // batch,),
            in_specs=[block] * 5 + [anywhere] * len(sources),
            out_specs=[block] * 4,
            scratch_shapes=[
                pltpu.VMEM((2, batch, BLK, BLK), jnp.bfloat16),
                pltpu.SemaphoreType.DMA((2,)),
            ],
        ),
        compiler_params=pltpu.CompilerParams(vmem_limit_bytes=32 * 2**20),
        cost_estimate=pl.CostEstimate(
            flops=8 * count * BLK**3, bytes_accessed=36 * count * BLK**2, transcendentals=0
        ),
    )(meta, rates, *state, *sources)


def per_device(
    block_input,
    cotangent,
    glob_select,
    assignment,
    master,
    first_moment,
    second_moment,
    left_basis,
    right_basis,
    gains,
    gain_first,
    gain_second,
):
    band_total = lax.axis_size("fsdp")
    rep_total = lax.axis_size("rep")
    place = lax.axis_index("rep")
    band = lax.axis_index("fsdp")
    heads = H // rep_total
    kv_heads = KVH // rep_total
    q_width = heads * HD
    kv_width = kv_heads * HD
    tok_count = block_input.shape[1]
    own_count = master.shape[1]
    tile_total = own_count * rep_total
    aligned = square() and whole_tiles(band_total, rep_total)
    tile_order = assignment[0]

    residual = block_input[0].astype(jnp.float32)
    grad_top = cotangent[0]
    position = band * tok_count + jnp.arange(tok_count, dtype=jnp.int32)
    cosine_table, sine_table = rope_tables(position)
    wide_cosine = jnp.concatenate([cosine_table, cosine_table], 1)[None]
    wide_sine = jnp.concatenate([sine_table, sine_table], 1)[None]
    scale_one = lax.rsqrt(jnp.mean(residual * residual, -1, keepdims=True) + norm_eps)
    normed_one = (residual * scale_one * gains[0]).astype(jnp.bfloat16)
    pick_rows = glob_select[0]
    glob_total = pick_rows.shape[0]
    selector = pick_rows.astype(jnp.bfloat16)
    glob_pos_part = jnp.sum(pick_rows * position[None, :], 1)
    digits = jnp.concatenate([glob_pos_part // 256, glob_pos_part % 256]).astype(jnp.bfloat16)
    digits = jnp.pad(digits[None], ((0, 7), (0, D - 2 * glob_total)))
    glob_rows = jnp.dot(selector, normed_one, preferred_element_type=jnp.float32).astype(jnp.bfloat16)
    glob_rows = add_all(jnp.concatenate([glob_rows, digits], 0), "fsdp").astype(jnp.bfloat16)
    packed = [normed_one, glob_rows, selector.reshape(-1, D)]
    packed = jnp.concatenate(packed, 0)
    packed = jnp.pad(packed, ((0, -packed.shape[0] % 32), (0, 0)))

    def over_bands(slice_rows):
        return lax.all_gather(slice_rows, "fsdp", axis=0, tiled=True)

    if aligned:
        half = BLK // 2
        low, high = (master[0, :, rows].astype(jnp.bfloat16) for rows in (slice(0, half), slice(half, BLK)))
        layout = slice_layout(band_total, rep_total)
        attn_layout = jnp.asarray(np.concatenate(layout[:4], 2))
        wanted = jnp.take(tile_order, by_place(attn_layout).reshape(-1), mode="clip")
        meta = jnp.stack([wanted // own_count == place, wanted % own_count], 0).astype(jnp.int32)
        attn_part = place_tiles(low, high, meta, *attn_layout.shape)
        attn_part = rep_scatter(attn_part).astype(jnp.bfloat16)
        low, attn_part = lax.optimization_barrier((low, attn_part))
        slots = square_pieces(low)
        attn = over_bands(attn_part)
        *slots, attn = lax.optimization_barrier((*slots, attn))
        grids = [lax.dynamic_index_in_dim(jnp.asarray(grid), place, 0, False) for grid in layout]

        def find(wanted):
            wanted = jnp.take(tile_order, jnp.concatenate([grid.reshape(-1) for grid in wanted]), mode="clip")
            entry, row = (wanted // own_count) ^ place, wanted % own_count
            cut = own_count // 2
            high = (entry == 3) & (row >= cut)
            found = jnp.stack([jnp.where(high, 4, entry), jnp.where(high, row - cut, row)], 0)
            return found.astype(jnp.int32)

        all_grid = jnp.concatenate(grids[4:], 1)
        (first_part,) = gather_strips(slots, find([all_grid]), [all_grid.shape])
        packed, first_part = lax.optimization_barrier((packed, first_part))
    packed_all = rep_gather(packed)
    if aligned:
        packed_all, high = lax.optimization_barrier((packed_all, high))
        later_slots = square_pieces(high)
    normed_one_all = packed_all[:, :tok_count].reshape(-1, D)
    at = tok_count + glob_total
    glob_digits = packed_all[:, at, : 2 * glob_total].astype(jnp.float32)
    glob_place = glob_digits[:, :glob_total] * 256.0 + glob_digits[:, glob_total:]
    at += 8
    selector_all = packed_all[:, at : at + selector.size // D].reshape(rep_total, glob_total, tok_count)

    if aligned:
        in_width = q_width + 2 * kv_width
        w_inner, w_output = attn[:, :in_width], attn[:, in_width:]
    else:
        slots = lax.all_gather(master[0].astype(jnp.bfloat16), "rep", axis=0, tiled=True)
        tiles = jnp.take(slots, tile_order, axis=0, mode="clip")
        slices = cut_slices(band_matrices(tiles, band_total), band_total, rep_total)
        w_inner = over_bands(jnp.concatenate(slices[0:3], 1))
        w_output = over_bands(slices[3])
        w_gate = over_bands(slices[4])
        w_up = over_bands(slices[5])
        w_down = over_bands(slices[6])

    w_output = by_place(w_output.reshape(rep_total, q_width, -1)).reshape(D, -1)

    def mul(rows, weight):
        return jnp.dot(rows, weight, preferred_element_type=jnp.float32)

    def mul_back(rows, weight):
        return lax.dot_general(rows, weight, (((1,), (1,)), ((), ())), preferred_element_type=jnp.float32)

    def weight_grad(rows, grad_rows):
        return lax.dot_general(
            rows, grad_rows, (((0,), (0,)), ((), ())), preferred_element_type=jnp.float32
        ).astype(jnp.bfloat16)

    def own_sum(partial):
        return rep_scatter(partial.astype(jnp.bfloat16).reshape(rep_total, tok_count, D))

    if aligned:
        packed_all, first_part = lax.optimization_barrier((packed_all, first_part))
        early = over_bands(first_part)
    inner_rows = mul(packed_all.reshape(-1, D), w_inner).reshape(rep_total, -1, w_inner.shape[1])
    queries, own_pairs = rope_rows(inner_rows, tok_count, 0, q_width, kv_width, wide_cosine, wide_sine)
    glob_cosine, glob_sine = rope_tables(glob_place.reshape(-1))
    glob_cosine = jnp.concatenate([glob_cosine, glob_cosine], 1).reshape(rep_total, glob_total, -1)
    glob_sine = jnp.concatenate([glob_sine, glob_sine], 1).reshape(rep_total, glob_total, -1)
    (glob_pairs,) = rope_rows(
        inner_rows, glob_total, tok_count // glob_total, q_width, kv_width, glob_cosine, glob_sine, False
    )
    back_count = (WINDOW + tok_count - 2) // tok_count
    pair_blocks = [shifted(own_pairs, "fsdp", distance) for distance in range(back_count, 0, -1)]
    pair_blocks = pair_blocks + [own_pairs, glob_pairs]
    glob_spots = jnp.broadcast_to(glob_place[:, :, None], (rep_total, glob_total, BLK))
    band_number = band.astype(jnp.int32).reshape(1)
    attended_low, lse = attend(band_number, glob_spots, queries, pair_blocks)
    if aligned:
        *later_slots, attended_low, early = lax.optimization_barrier((*later_slots, attended_low, early))
        last_grid = jnp.concatenate(grids[4:6], 1)
        last_part, down_part = gather_strips(
            later_slots, find([last_grid, grids[6]]), [last_grid.shape, grids[6].shape]
        )

        def by_strips(part):
            gathered = over_bands(part)
            return gathered.reshape(band_total, -1, last_grid.shape[0], half, gathered.shape[-1])

        early = early.reshape(band_total, -1, all_grid.shape[0], half, early.shape[-1])
        late, late_down = by_strips(last_part), by_strips(down_part)
    attended_all = rep_features(attended_low).reshape(-1, D)
    attended_all, grad_top_now = lax.optimization_barrier((attended_all, grad_top))
    grad_top_all = rep_gather(grad_top_now).reshape(-1, D)
    columns = mul(attended_all, w_output).astype(jnp.bfloat16).reshape(rep_total, tok_count, -1)
    branch = by_place(rep_exchange(columns)).transpose(1, 0, 2).reshape(tok_count, D)
    middle = residual + branch.astype(jnp.float32)
    scale_two = lax.rsqrt(jnp.mean(middle * middle, -1, keepdims=True) + norm_eps)
    normed_two = (middle * scale_two * gains[1]).astype(jnp.bfloat16)
    normed_two_all = rep_gather(normed_two).reshape(-1, D)
    normed_two_all, grad_top_all = lax.optimization_barrier((normed_two_all, grad_top_all))

    if aligned:
        gate_rows, up_rows, activation = forward_products(normed_two_all, early, late, FF // rep_total)
        g_down = weight_grad(activation, grad_top_all)
        grad_top_all, g_down = lax.optimization_barrier((grad_top_all, g_down))
        grad_gate, grad_up, pieces, branch_pieces = backward_products(
            grad_top_all, gate_rows, up_rows, activation, early, late, late_down
        )
        grad_normed_two = sum_pieces(*pieces)
    else:
        gate_rows = mul(normed_two_all, w_gate)
        up_rows = mul(normed_two_all, w_up)
        sigmoid_gate = jax.nn.sigmoid(gate_rows)
        silu_gate = gate_rows * sigmoid_gate
        activation = (silu_gate * up_rows).astype(jnp.bfloat16)
        g_down = weight_grad(activation, grad_top_all)
        grad_act = mul_back(grad_top_all, w_down)
        grad_gate = (
            grad_act * up_rows * sigmoid_gate * (1.0 + gate_rows * (1.0 - sigmoid_gate))
        ).astype(jnp.bfloat16)
        grad_up = (grad_act * silu_gate).astype(jnp.bfloat16)
        grad_normed_two = own_sum(mul_back(grad_gate, w_gate) + mul_back(grad_up, w_up))
        branch_pieces = (mul(activation, w_down),)
    g_gate = weight_grad(normed_two_all, grad_gate)
    g_up = weight_grad(normed_two_all, grad_up)
    grad_normed_two, g_gate, g_up, *branch_pieces = lax.optimization_barrier(
        (grad_normed_two, g_gate, g_up, *branch_pieces)
    )
    block_out = middle + (sum_pieces(*branch_pieces) if aligned else own_sum(branch_pieces[0]))

    def over_tokens(partial):
        return lax.psum_scatter(partial, "fsdp", scatter_dimension=0, tiled=True)

    s_down = over_tokens(g_down)
    s_gate = over_tokens(g_gate)
    s_up = over_tokens(g_up)

    grad_middle = grad_top.astype(jnp.float32) + norm_back(middle, scale_two, gains[1], grad_normed_two)
    grad_parts = grad_middle.astype(jnp.bfloat16).reshape(tok_count, rep_total, -1).transpose(1, 0, 2)
    grad_columns = rep_exchange(by_place(grad_parts)).reshape(rep_total * tok_count, -1)
    grad_attended = rep_features_sum(
        grad_columns.reshape(rep_total, tok_count, -1), w_output
    ).astype(jnp.bfloat16)
    g_output = weight_grad(attended_all, grad_columns)
    g_output = by_place(g_output.reshape(rep_total, q_width, -1)).reshape(D, -1)
    grad_attended, s_down, block_out = lax.optimization_barrier((grad_attended, s_down, block_out))
    s_down = rep_gather(s_down)
    grad_queries, *grad_blocks = attend_back(
        band_number, glob_spots, wide_cosine, wide_sine, queries, grad_attended, lse, pair_blocks
    )
    returned = [
        shifted(grad_blocks[back_count - distance], "fsdp", -distance)
        for distance in range(1, back_count + 1)
    ]
    glob_grads = add_all(grad_blocks[-1], "fsdp")
    s_gate = rep_gather(s_gate)
    glob_grads, s_gate, s_down = lax.optimization_barrier((glob_grads, s_gate, s_down))
    grad_inner = join_grads(
        grad_queries, grad_blocks[-2], selector_all, glob_grads, wide_cosine, wide_sine, returned
    ).reshape(-1, q_width + 2 * kv_width)
    g_inner, s_up = lax.optimization_barrier((weight_grad(normed_one_all, grad_inner), s_up))
    s_up = rep_gather(s_up)
    s_attn = over_tokens(jnp.concatenate([g_inner, g_output], 1))
    grad_normed_one = own_sum(mul_back(grad_inner, w_inner))
    grad_normed_one, s_up = lax.optimization_barrier((grad_normed_one, s_up))
    grad_input = grad_middle + norm_back(residual, scale_one, gains[0], grad_normed_one)

    gain_terms = jnp.stack(
        [
            jnp.sum(grad_normed_one * residual * scale_one, 0),
            jnp.sum(grad_normed_two * middle * scale_two, 0),
        ]
    )
    square_terms = jnp.stack(
        [jnp.sum(residual * residual), jnp.sum(middle * middle), jnp.sum(block_out * block_out)]
    )
    sums, s_attn = lax.optimization_barrier((jnp.concatenate([gain_terms.reshape(-1), square_terms]), s_attn))

    slot_ids = jnp.arange(tile_total, dtype=jnp.int32)
    inverse = jnp.sum(jnp.where(tile_order[None, :] == slot_ids[:, None], slot_ids[None, :], 0), 1)
    own_slots = place * own_count + jnp.arange(own_count, dtype=jnp.int32)
    owned_tiles = jnp.take(inverse, own_slots, mode="clip")
    if aligned:
        sources = [rep_gather(s_attn), s_gate, s_up, s_down]
        where = np.zeros((4, rep_total, tile_total), np.int32)
        first_col = 0
        for kind, grid in enumerate(layout):
            rows, cols = grid.shape[1:]
            first_col = 0 if kind >= 4 else first_col
            for there in range(rep_total):
                numbers = grid[there].reshape(-1)
                at = np.arange(rows * cols)
                where[0, :, numbers] = max(kind - 3, 0)
                where[2, :, numbers] = (at // cols * BLK)[:, None]
                where[3, :, numbers] = (at % cols * BLK + first_col)[:, None]
                for here in range(rep_total):
                    where[1, here, numbers] = here ^ there
            first_col += cols * BLK
        tile_spots = lax.dynamic_index_in_dim(jnp.asarray(where), place, 1, False)
        meta = jnp.take(tile_spots, owned_tiles, axis=1, mode="clip")
    else:
        splits = [0, q_width, q_width + kv_width, q_width + 2 * kv_width, s_attn.shape[1]]
        stacks = [rep_gather(s_attn[:, low:high]) for low, high in zip(splits, splits[1:])]
        stacks += [s_gate, s_up, s_down]
        sources = [band_tiles(join_slices(stacks, band_total, rep_total))]
        meta = jnp.stack([0 * owned_tiles, owned_tiles, 0 * owned_tiles, 0 * owned_tiles], 0)
    slot_rates = jnp.take(kind_rates(band_total), owned_tiles, mode="clip")
    new_first, new_second, new_master, master_copy = adam(
        meta,
        slot_rates,
        (master[0], first_moment[0], second_moment[0], left_basis[0], right_basis[0]),
        sources,
    )
    sums = add_all(add_all(sums, "rep"), "fsdp")
    gain_grad, square_total = sums[: 2 * D].reshape(2, D), sums[2 * D :]
    new_gain_first = beta_one * gain_first + (1.0 - beta_one) * gain_grad
    new_gain_second = beta_two * gain_second + (1.0 - beta_two) * gain_grad * gain_grad
    gain_step = (
        new_gain_first
        / (1.0 - beta_one**STEP)
        / (jnp.sqrt(new_gain_second / (1.0 - beta_two**STEP)) + adam_eps)
    )
    new_gains = gains - gain_rate * gain_step
    rms_stats = jnp.sqrt(square_total / (rep_total * band_total * tok_count * D))
    return (
        block_out[None],
        grad_input[None],
        new_first[None],
        new_second[None],
        new_master[None],
        master_copy[None],
        new_gain_first,
        new_gain_second,
        new_gains,
        rms_stats,
    )


def solution(mesh):
    in_specs = (
        P("rep", "fsdp", None),
        P("rep", "fsdp", None),
        P("rep", None, "fsdp"),
        P("fsdp", None),
        P("fsdp", "rep", None, None),
        P("fsdp", "rep", None, None),
        P("fsdp", "rep", None, None),
        P("fsdp", "rep", None, None),
        P("fsdp", "rep", None, None),
        P(),
        P(),
        P(),
    )
    out_specs = (
        P("rep", "fsdp", None),
        P("rep", "fsdp", None),
        P("fsdp", "rep", None, None),
        P("fsdp", "rep", None, None),
        P("fsdp", "rep", None, None),
        P("fsdp", "rep", None, None),
        P(),
        P(),
        P(),
        P(),
    )
    return jax.shard_map(
        per_device, mesh=mesh, in_specs=in_specs, out_specs=out_specs, check_vma=False
    )
```

```python
import functools

import jax
import jax.numpy as jnp
import numpy as np
from jax import lax
from jax.experimental import pallas as pl
from jax.experimental.pallas import tpu as pltpu
from jax.sharding import PartitionSpec as P

D = 2048
H = 32
KVH = 8
HD = 64
FF = 8192
WINDOW = 512
BLK = 128
STEP = 10


norm_eps = 1e-05
rope_theta = 500000.0
beta_one = 0.5
beta_two = 0.5
adam_eps = 1e-08
weight_decay = 0.1
gain_rate = 0.5
masked_value = -1e30


def matrix_shapes():
    kv_width = KVH * HD
    return [(D, D), (D, kv_width), (D, kv_width), (D, D), (D, FF), (D, FF), (FF, D)]


def kind_rates(band_total):
    rate_list = [
        D ** (-0.5),
        D ** (-0.5),
        D ** (-0.5),
        (D * 8 // WINDOW) ** (-0.5),
        D ** (-0.5),
        D ** (-0.5),
        FF ** (-0.5),
    ]
    pieces = []
    for (row_total, col_total), rate_value in zip(matrix_shapes(), rate_list):
        tile_count = row_total // band_total // BLK * (col_total // BLK)
        pieces.append(jnp.full((tile_count,), rate_value, jnp.float32))
    return jnp.concatenate(pieces)


def band_matrices(tiles, band_total):
    matrices = []
    offset = 0
    for row_total, col_total in matrix_shapes():
        band_rows = row_total // band_total
        tile_count = band_rows // BLK * (col_total // BLK)
        segment = tiles[offset : offset + tile_count].reshape(
            band_rows // BLK, col_total // BLK, BLK, BLK
        )
        matrices.append(segment.transpose(0, 2, 1, 3).reshape(band_rows, col_total))
        offset += tile_count
    return matrices


def band_tiles(matrices):
    pieces = []
    for matrix in matrices:
        row_count, col_count = matrix.shape
        segment = matrix.reshape(row_count // BLK, BLK, col_count // BLK, BLK).transpose(0, 2, 1, 3)
        pieces.append(segment.reshape(-1, BLK, BLK))
    return jnp.concatenate(pieces, 0)


def rope_tables(position):
    halves = jnp.arange(HD // 2, dtype=jnp.float32) * (2.0 / HD)
    frequency = rope_theta ** (-halves)
    angles = position.astype(jnp.float32)[:, None] * frequency[None, :]
    angles = jnp.concatenate([angles, angles], 1)
    return (jnp.cos(angles), jnp.sin(angles))


def rotate(vectors, cosine_table, sine_table):
    half_width = vectors.shape[-1] // 2
    turned = jnp.concatenate([-vectors[..., half_width:], vectors[..., :half_width]], -1)
    return vectors * cosine_table[:, None, :] + turned * sine_table[:, None, :]


def rotate_back(grad_rows, cosine_table, sine_table):
    half_width = grad_rows.shape[-1] // 2
    scaled = grad_rows * sine_table[:, None, :]
    turned = jnp.concatenate([scaled[..., half_width:], -scaled[..., :half_width]], -1)
    return grad_rows * cosine_table[:, None, :] + turned


def norm_back(values, row_scale, gain_row, grad_rows):
    weighted = grad_rows * gain_row
    return row_scale * weighted - values * row_scale**3 * jnp.mean(
        weighted * values, -1, keepdims=True
    )


def to_rep(block, distance):
    route = [(i, i ^ distance) for i in range(lax.axis_size("rep"))]
    return lax.ppermute(block, "rep", route)


def square():
    return lax.axis_size("rep") == 4


def square_pieces(block):
    cut = block.shape[0] // 2
    near = to_rep(block, 1)
    far = to_rep(block, 2)
    return block, near, far, to_rep(near[:cut], 2), to_rep(far[cut:], 1)


def rep_gather(block):
    if not square():
        return lax.all_gather(block, "rep", axis=0)
    own, near, far, low, high = square_pieces(block)
    return jnp.concatenate([own, near, far, low, high], 0).reshape((4,) + block.shape)


def rep_of(entry):
    place = lax.axis_index("rep")
    return place ^ entry if square() else entry


def rep_scatter(parts):
    if not square():
        flat = parts.reshape(-1, parts.shape[-1])
        return lax.psum_scatter(flat, "rep", scatter_dimension=0, tiled=True).astype(jnp.float32)
    half = parts.shape[-1] // 2
    low, high = parts[..., :half], parts[..., half:]
    return sum_pieces(
        jnp.stack([low[0], low[2]], 0), jnp.stack([low[1], low[3]], 0), high[:2], high[2:]
    )


def sum_pieces(low_kept, low_sent, high_kept, high_sent):
    totals = []
    for kept, sent, first, second in ((low_kept, low_sent, 1, 2), (high_kept, high_sent, 2, 1)):
        came = to_rep(sent, first)
        other = (kept[1].astype(jnp.float32) + came[1].astype(jnp.float32)).astype(kept.dtype)
        own = kept[0].astype(jnp.float32) + came[0].astype(jnp.float32)
        totals.append(own + to_rep(other, second).astype(jnp.float32))
    return jnp.concatenate(totals, -1)


def add_all(value, axis):
    size = lax.axis_size(axis)
    total = value.astype(jnp.float32)
    distance = 1
    while distance < size:
        count = 2 if (size // distance).bit_length() % 2 == 0 else 4
        low = total.astype(value.dtype)
        others = []
        for step in range(1, count):
            route = [(i, i ^ (step * distance)) for i in range(size)]
            others.append(lax.ppermute(low, axis, route).astype(jnp.float32))
        total = total + others[0]
        if count == 4:
            total = total + (others[1] + others[2])
        distance *= count
    return total


def rep_features(block):
    if not square():
        return lax.all_gather(block, "rep", axis=2, tiled=True)
    own, near, far, low, high = square_pieces(block)
    return jnp.concatenate(
        [
            own,
            jnp.stack([near[1], near[0], near[3], near[2]], 0),
            jnp.stack([far[2], far[3], far[0], far[1]], 0),
            jnp.stack([high[1], high[0], low[1], low[0]], 0),
        ],
        2,
    )


def write_pieces(entry, rows, values, refs):
    low_kept, low_sent, high_kept, high_sent = refs
    half = low_kept.shape[-1]
    values = values.astype(jnp.bfloat16)
    (low_sent if entry % 2 else low_kept)[entry // 2, rows] = values[:, :half]
    (high_sent if entry // 2 else high_kept)[entry % 2, rows] = values[:, half:]


def swapped_kernel(x_ref, w_ref, *refs):
    reps, rows, _ = x_ref.shape
    width = w_ref.shape[0] // reps
    for entry in range(reps):
        weight = w_ref[entry * width : (entry + 1) * width]
        for there in range(reps):
            product = over_last(x_ref[there ^ entry], weight)
            write_pieces(entry, slice(there * rows, (there + 1) * rows), product, refs)


def rep_features_sum(columns, weight):
    reps, rows, depth = columns.shape
    width = weight.shape[0] // reps
    if square():
        pieces = pl.pallas_call(
            swapped_kernel,
            out_shape=[jax.ShapeDtypeStruct((2, reps * rows, width // 2), jnp.bfloat16)] * 4,
            compiler_params=pltpu.CompilerParams(vmem_limit_bytes=32 * 2**20),
            cost_estimate=pl.CostEstimate(
                flops=2 * reps * columns.size * width,
                bytes_accessed=10 * columns.size,
                transcendentals=0,
            ),
        )(columns, weight)
        total = sum_pieces(*pieces)
    else:
        product = over_last(columns.reshape(-1, depth), weight).astype(jnp.bfloat16)
        swapped = product.reshape(reps, rows, reps, width).transpose(2, 0, 1, 3)
        total = rep_scatter(swapped.reshape(reps, reps * rows, width))
    return total.reshape(reps, rows, width)


def rep_exchange(parts):
    if not square():
        return lax.all_to_all(parts, "rep", 0, 0)
    return jnp.stack([parts[0]] + [to_rep(parts[entry], entry) for entry in (1, 2, 3)], 0)


def by_place(parts):
    entries = [rep_of(entry) for entry in range(parts.shape[0])]
    return jnp.stack([lax.dynamic_index_in_dim(parts, entry, 0, False) for entry in entries], 0)


def shifted(block, axis, distance):
    devices = range(lax.axis_size(axis))
    route = [(i - distance, i) for i in devices if i - distance in devices]
    return lax.ppermute(block, axis, route)


def tile_offsets(band_total):
    offsets = [0]
    for row_total, col_total in matrix_shapes():
        offsets.append(offsets[-1] + row_total // band_total // BLK * (col_total // BLK))
    return offsets


def whole_tiles(band_total, rep_total):
    return KVH * HD // rep_total % BLK == 0 and FF // band_total // rep_total % BLK == 0


def slice_layout(band_total, rep_total):
    offsets = tile_offsets(band_total)
    layout = []
    for kind, (row_total, col_total) in enumerate(matrix_shapes()):
        rows, cols = row_total // band_total // BLK, col_total // BLK
        grid = offsets[kind] + np.arange(rows * cols).reshape(rows, cols)
        if kind == 6:
            layout.append(grid.reshape(rep_total, rows // rep_total, cols))
        elif kind in (4, 5):
            cut = grid.reshape(rows, band_total, rep_total, -1).transpose(2, 0, 1, 3)
            layout.append(cut.reshape(rep_total, rows, -1))
        else:
            layout.append(grid.reshape(rows, rep_total, -1).transpose(1, 0, 2))
    return layout


def tiles_to_matrix(tiles):
    rows, cols = tiles.shape[:2]
    return tiles.transpose(0, 2, 1, 3).reshape(rows * BLK, cols * BLK)


def matrix_to_tiles(matrix):
    rows, cols = matrix.shape
    cut = matrix.reshape(rows // BLK, BLK, cols // BLK, BLK)
    return cut.transpose(0, 2, 1, 3).reshape(-1, BLK, BLK)


def cut_slices(matrices, band_total, rep_total):
    place = lax.axis_index("rep")
    slices = []
    for kind, matrix in enumerate(matrices):
        rows, cols = matrix.shape
        if kind == 6:
            slices.append(lax.dynamic_slice_in_dim(matrix, place * (rows // rep_total), rows // rep_total, 0))
        elif kind in (4, 5):
            cut = matrix.reshape(rows, band_total, rep_total, -1)
            slices.append(lax.dynamic_index_in_dim(cut, place, 2, False).reshape(rows, -1))
        else:
            slices.append(lax.dynamic_slice_in_dim(matrix, place * (cols // rep_total), cols // rep_total, 1))
    return slices


def join_slices(stacks, band_total, rep_total):
    matrices = []
    for kind, stack in enumerate(stacks):
        rows, cols = stack.shape[1:]
        if kind == 6:
            matrices.append(stack.reshape(-1, cols))
        elif kind in (4, 5):
            cut = stack.reshape(rep_total, rows, band_total, -1).transpose(1, 2, 0, 3)
            matrices.append(cut.reshape(rows, -1))
        else:
            matrices.append(stack.transpose(1, 0, 2).reshape(rows, -1))
    return matrices


def gather_kernel(grids, meta, *refs):
    source_total = len(refs) - len(grids) - 1
    sources, targets, done = refs[:source_total], refs[source_total:-1], refs[-1]
    height = sources[0].shape[1]
    start = 0
    for place, (target, (rows, cols)) in enumerate(zip(targets, grids)):

        def one(tile, carry, target=target, rows=rows, cols=cols, start=start, place=place):
            kind = meta[0, start + tile]
            row = meta[1, start + tile]
            across = tile % cols
            top = pl.multiple_of((across // 2 * rows + tile // cols) * height, height)
            left = pl.multiple_of(across % 2 * BLK, BLK)
            for number, source in enumerate(sources):

                @pl.when(kind == number)
                def _(source=source):
                    pltpu.make_async_copy(
                        source.at[row], target.at[pl.ds(top, height), pl.ds(left, BLK)], done.at[place]
                    ).start()

            return carry

        lax.fori_loop(0, rows * cols, one, 0)
        start += rows * cols
    for place, target in enumerate(targets):
        pltpu.make_async_copy(target, target, done.at[place]).wait()


def gather_strips(sources, meta, grids):
    anywhere = pl.BlockSpec(memory_space=pl.ANY)
    height = sources[0].shape[1]
    out_shape = [
        jax.ShapeDtypeStruct((cols // 2 * rows * height, 2 * BLK), jnp.bfloat16) for rows, cols in grids
    ]
    return pl.pallas_call(
        functools.partial(gather_kernel, grids),
        out_shape=out_shape,
        grid_spec=pltpu.PrefetchScalarGridSpec(
            num_scalar_prefetch=1,
            grid=(1,),
            in_specs=[anywhere] * len(sources),
            out_specs=[pl.BlockSpec(shape.shape, lambda i, *_: (0, 0)) for shape in out_shape],
            scratch_shapes=[pltpu.SemaphoreType.DMA((len(grids),))],
        ),
        compiler_params=pltpu.CompilerParams(vmem_limit_bytes=32 * 2**20),
        cost_estimate=pl.CostEstimate(
            flops=0, bytes_accessed=sum(4 * shape.size for shape in out_shape), transcendentals=0
        ),
    )(meta, *sources)


def place_kernel(entries, rows, cols, meta, low, high, out_ref, done):
    out_ref[...] = jnp.zeros_like(out_ref)
    height = low.shape[1]

    def copies(tile):
        entry, rest = tile // (rows * cols), tile % (rows * cols)
        top = rest // cols * (2 * height)
        left = pl.multiple_of(rest % cols * BLK, BLK)
        return [
            pltpu.make_async_copy(
                half.at[meta[1, tile]],
                out_ref.at[entry, pl.ds(pl.multiple_of(top + part * height, height), height), pl.ds(left, BLK)],
                done.at[part],
            )
            for part, half in enumerate((low, high))
        ]

    def begin(tile, carry):
        @pl.when(meta[0, tile] == 1)
        def _():
            for copy in copies(tile):
                copy.start()

        return carry

    def finish(tile, carry):
        @pl.when(meta[0, tile] == 1)
        def _():
            for copy in copies(tile):
                copy.wait()

        return carry

    lax.fori_loop(0, entries * rows * cols, begin, 0)
    lax.fori_loop(0, entries * rows * cols, finish, 0)


def place_tiles(low, high, meta, entries, rows, cols):
    shape = (entries, rows * BLK, cols * BLK)
    anywhere = pl.BlockSpec(memory_space=pl.ANY)
    return pl.pallas_call(
        functools.partial(place_kernel, entries, rows, cols),
        out_shape=jax.ShapeDtypeStruct(shape, jnp.bfloat16),
        grid_spec=pltpu.PrefetchScalarGridSpec(
            num_scalar_prefetch=1,
            grid=(1,),
            in_specs=[anywhere, anywhere],
            out_specs=pl.BlockSpec(shape, lambda i, *_: (0, 0, 0)),
            scratch_shapes=[pltpu.SemaphoreType.DMA((2,))],
        ),
        compiler_params=pltpu.CompilerParams(vmem_limit_bytes=32 * 2**20),
        cost_estimate=pl.CostEstimate(
            flops=0, bytes_accessed=4 * entries * rows * cols * BLK * BLK, transcendentals=0
        ),
    )(meta, low, high)


def half_turn(values):
    lane = lax.broadcasted_iota(jnp.int32, values.shape, 1)
    lanes = values.shape[1]
    first = lane % HD < HD // 2
    return first, jnp.where(
        first, pltpu.roll(values, lanes - HD // 2, 1), pltpu.roll(values, HD // 2, 1)
    )


def strip_copies(early, late, target, done):
    return [
        pltpu.make_async_copy(half, target.at[:, :, number], done.at[number])
        for number, half in enumerate((early, late))
    ]


def forward_kernel(x_ref, early, late, gate_ref, up_ref, act_ref, weights, done):
    step, steps = pl.program_id(0), pl.num_programs(0)
    slot = step % 2
    width = weights.shape[-1]

    def copies(number, at_step, at_slot):
        strip = number * steps + at_step
        return strip_copies(
            early.at[:, strip], late.at[:, strip], weights.at[number, at_slot], done.at[number, at_slot]
        )

    def fetch(at_step, at_slot):
        for number in range(2):
            for copy in copies(number, at_step, at_slot):
                copy.start()

    @pl.when(step == 0)
    def _():
        fetch(0, 0)

    @pl.when(step + 1 < steps)
    def _():
        fetch(step + 1, 1 - slot)

    for number in range(2):
        for copy in copies(number, step, slot):
            copy.wait()
    gate_weight, up_weight = (weights[number, slot].reshape(-1, width) for number in range(2))
    chunk = min(2 * BLK, x_ref.shape[0])
    for first in range(0, x_ref.shape[0], chunk):
        rows = slice(first, first + chunk)
        gate = jnp.dot(x_ref[rows], gate_weight, preferred_element_type=jnp.float32)
        up = jnp.dot(x_ref[rows], up_weight, preferred_element_type=jnp.float32)
        gate_ref[rows] = gate.astype(jnp.bfloat16)
        up_ref[rows] = up.astype(jnp.bfloat16)
        act_ref[rows] = (gate * jax.nn.sigmoid(gate) * up).astype(jnp.bfloat16)


def forward_products(rows, early, late, columns):
    tokens, depth = rows.shape
    bands, _, tiles, half, width = early.shape
    block = pl.BlockSpec((tokens, width), lambda n: (0, n))
    anywhere = pl.BlockSpec(memory_space=pl.ANY)
    return pl.pallas_call(
        forward_kernel,
        out_shape=[jax.ShapeDtypeStruct((tokens, columns), jnp.bfloat16)] * 3,
        grid=(columns // width,),
        in_specs=[pl.BlockSpec(rows.shape, lambda n: (0, 0)), anywhere, anywhere],
        out_specs=[block] * 3,
        scratch_shapes=[
            pltpu.VMEM((2, 2, bands, tiles, 2, half, width), jnp.bfloat16),
            pltpu.SemaphoreType.DMA((2, 2, 2)),
        ],
        compiler_params=pltpu.CompilerParams(vmem_limit_bytes=48 * 2**20),
        cost_estimate=pl.CostEstimate(
            flops=tokens * depth * columns // 8, bytes_accessed=2 * rows.size, transcendentals=0
        ),
    )(rows, early, late)


def backward_kernel(top_ref, gate_ref, up_ref, act_ref, early, late, late_down, *refs):
    dgate_ref, dup_ref = refs[:2]
    pieces, branch_pieces = refs[2:6], refs[6:10]
    weights, downs, total, branch, done, down_done = refs[10:]
    step, steps = pl.program_id(0), pl.num_programs(0)
    slot = step % 2
    strips, width = downs.shape[1], downs.shape[-1]

    def down_copies(at_step, at_slot):
        return strip_copies(
            early.at[at_step, pl.ds(2 * steps, strips)],
            late_down.at[at_step],
            downs.at[at_slot],
            down_done.at[at_slot],
        )

    def copies(number, at_step, at_slot):
        strip = number * steps + at_step
        return strip_copies(
            early.at[:, strip], late.at[:, strip], weights.at[number, at_slot], done.at[number, at_slot]
        )

    def fetch(at_step, at_slot):
        for copy in down_copies(at_step, at_slot):
            copy.start()
        for number in range(2):
            for copy in copies(number, at_step, at_slot):
                copy.start()

    @pl.when(step == 0)
    def _():
        fetch(0, 0)
        total[...] = jnp.zeros_like(total)
        branch[...] = jnp.zeros_like(branch)

    @pl.when(step + 1 < steps)
    def _():
        fetch(step + 1, 1 - slot)

    for copy in down_copies(step, slot):
        copy.wait()
    for number in range(2):
        for copy in copies(number, step, slot):
            copy.wait()
    gate_weight, up_weight = (weights[number, slot].reshape(-1, width) for number in range(2))
    chunk = min(4 * BLK, top_ref.shape[0])
    for first in range(0, top_ref.shape[0], chunk):
        rows = slice(first, first + chunk)
        grad_act = 0.0
        for strip in range(strips):
            lanes = slice(strip * width, (strip + 1) * width)
            down = downs[slot, strip].reshape(-1, width)
            grad_act = grad_act + over_last(top_ref[rows, lanes], down)
            branch[rows, lanes] += jnp.dot(act_ref[rows], down, preferred_element_type=jnp.float32)
        gate = gate_ref[rows].astype(jnp.float32)
        up = up_ref[rows].astype(jnp.float32)
        sigmoid_gate = jax.nn.sigmoid(gate)
        grad_gate = grad_act * up * sigmoid_gate * (1.0 + gate * (1.0 - sigmoid_gate))
        grad_gate = grad_gate.astype(jnp.bfloat16)
        grad_up = (grad_act * (gate * sigmoid_gate)).astype(jnp.bfloat16)
        dgate_ref[rows] = grad_gate
        dup_ref[rows] = grad_up
        total[rows] += over_last(grad_gate, gate_weight) + over_last(grad_up, up_weight)

    @pl.when(step == steps - 1)
    def _():
        rows = total.shape[0] // 4
        for entry in range(4):
            part = slice(entry * rows, (entry + 1) * rows)
            write_pieces(entry, slice(0, rows), total[part], pieces)
            write_pieces(entry, slice(0, rows), branch[part], branch_pieces)


def backward_products(top, gate, up, act, early, late, late_down):
    tokens, depth = top.shape
    columns = gate.shape[1]
    bands, _, tiles, half, width = early.shape
    strips = late_down.shape[1]
    block = pl.BlockSpec((tokens, width), lambda n: (0, n))
    anywhere = pl.BlockSpec(memory_space=pl.ANY)
    piece = jax.ShapeDtypeStruct((2, tokens // 4, depth // 2), jnp.bfloat16)
    grads = jax.ShapeDtypeStruct((tokens, columns), jnp.bfloat16)
    outs = pl.pallas_call(
        backward_kernel,
        out_shape=[grads] * 2 + [piece] * 8,
        grid=(columns // width,),
        in_specs=[pl.BlockSpec(top.shape, lambda n: (0, 0))] + [block] * 3 + [anywhere] * 3,
        out_specs=[block] * 2 + [pl.BlockSpec(piece.shape, lambda n: (0, 0, 0))] * 8,
        scratch_shapes=[
            pltpu.VMEM((2, 2, bands, tiles, 2, half, width), jnp.bfloat16),
            pltpu.VMEM((2, strips, tiles, 2, half, width), jnp.bfloat16),
            pltpu.VMEM((tokens, depth), jnp.float32),
            pltpu.VMEM((tokens, depth), jnp.float32),
            pltpu.SemaphoreType.DMA((2, 2, 2)),
            pltpu.SemaphoreType.DMA((2, 2)),
        ],
        compiler_params=pltpu.CompilerParams(vmem_limit_bytes=60 * 2**20),
        cost_estimate=pl.CostEstimate(
            flops=8 * tokens * depth * columns, bytes_accessed=8 * columns * depth, transcendentals=0
        ),
    )(top, gate, up, act, early, late, late_down)
    return outs[0], outs[1], outs[2:6], outs[6:10]


def rope_kernel(q_width, kv_width, x_ref, cos_ref, sin_ref, *outs):
    width = x_ref.shape[-1]
    for start in range(0, width, BLK):
        values = x_ref[0, :, start : start + BLK]
        first, turned = half_turn(values)
        sines = sin_ref[0]
        turned_rows = values * cos_ref[0] + turned * jnp.where(first, -sines, sines)
        if start + BLK > q_width + kv_width:
            column = lax.broadcasted_iota(jnp.int32, values.shape, 1) + start
            turned_rows = jnp.where(column >= q_width + kv_width, values, turned_rows)
        if start < q_width:
            outs[0][0, :, start : start + BLK] = (turned_rows * HD ** (-0.5)).astype(jnp.bfloat16)
        else:
            outs[-1][0, :, start - q_width : start - q_width + BLK] = turned_rows.astype(jnp.bfloat16)


def rope_rows(inner, rows, row_block, q_width, kv_width, cosines, sines, with_queries=True):
    seqs, _, width = inner.shape
    shared = cosines.shape[0] == 1
    table = pl.BlockSpec((1, rows, BLK), lambda s: (0 if shared else s, 0, 0))
    widths = [q_width, 2 * kv_width]
    column_block = 0
    if not with_queries:
        width, column_block = 2 * kv_width, q_width // (2 * kv_width)
        widths, q_width = widths[1:], 0
    return pl.pallas_call(
        functools.partial(rope_kernel, q_width, kv_width),
        out_shape=[jax.ShapeDtypeStruct((seqs, rows, w), jnp.bfloat16) for w in widths],
        grid=(seqs,),
        in_specs=[pl.BlockSpec((1, rows, width), lambda s: (s, row_block, column_block)), table, table],
        out_specs=[pl.BlockSpec((1, rows, w), lambda s: (s, 0, 0)) for w in widths],
        cost_estimate=pl.CostEstimate(
            flops=6 * seqs * rows * width, bytes_accessed=6 * seqs * rows * width, transcendentals=0
        ),
    )(inner, cosines, sines)


def fill_bias(band_ref, gpos_ref, bias_ref, rows, window_len):
    band = band_ref[0]

    @pl.when(pl.program_id(0) == 0)
    def _():
        key = lax.broadcasted_iota(jnp.int32, (window_len, rows), 0) + (
            band * rows - (window_len - rows)
        )
        query = lax.broadcasted_iota(jnp.int32, (window_len, rows), 1) + band * rows
        inside = (key > query - WINDOW) & (key <= query) & (key >= 0)
        bias_ref[:window_len] = jnp.where(inside, 0.0, masked_value)

    glob_total = gpos_ref.shape[1]
    query = lax.broadcasted_iota(jnp.int32, (glob_total, rows), 1) + (band * rows - WINDOW)
    spot = jnp.broadcast_to(gpos_ref[0][:, :1], (glob_total, rows))
    bias_ref[window_len:] = jnp.where(spot <= query.astype(jnp.float32), 0.0, masked_value)


def over_last(left, right):
    return lax.dot_general(left, right, (((1,), (1,)), ((), ())), preferred_element_type=jnp.float32)


def over_first(left, right):
    return lax.dot_general(left, right, (((0,), (0,)), ((), ())), preferred_element_type=jnp.float32)


def attend_kernel(block_total, band_ref, gpos_ref, q_ref, *refs):
    blocks, (out_ref, lse_ref, bias_ref) = refs[:block_total], refs[block_total:]
    rows, q_width = q_ref.shape[1:]
    kv_width = blocks[0].shape[2] // 2
    heads, group = q_width // HD, q_width // kv_width
    window_len = rows * (block_total - 1)
    fill_bias(band_ref, gpos_ref, bias_ref, rows, window_len)
    starts = [rows * number for number in range(block_total)]
    pending = []
    for head in range(heads):
        left = head // group * HD
        queries = q_ref[0, :, head * HD : (head + 1) * HD]
        scores = [
            over_last(block[0, :, left : left + HD], queries)
            + bias_ref[start : start + block.shape[1]]
            for block, start in zip(blocks, starts)
        ]
        top = functools.reduce(jnp.maximum, [jnp.max(part, 0, keepdims=True) for part in scores])
        total = 0.0
        mixed = 0.0
        for block, part in zip(blocks, scores):
            weights = jnp.exp(part - top)
            total = total + jnp.sum(weights, 0, keepdims=True)
            mixed = mixed + over_first(
                block[0, :, kv_width + left : kv_width + left + HD], weights.astype(jnp.bfloat16)
            )
        lse_ref[0, head : head + 1, :] = top + jnp.log(total)
        pending.append(mixed / total)
        if len(pending) * HD == BLK or head == heads - 1:
            stop = (head + 1) * HD
            both = jnp.concatenate(pending, 0).T
            out_ref[0, :, stop - both.shape[1] : stop] = both.astype(jnp.bfloat16)
            pending = []


def attend(band, gpos, queries, blocks):
    seqs, rows, q_width = queries.shape
    heads = q_width // HD
    key_total = sum(block.shape[1] for block in blocks)

    def whole(array):
        return pl.BlockSpec((1,) + array.shape[1:], lambda s, *_: (s, 0, 0))

    out_shape = [
        jax.ShapeDtypeStruct((seqs, rows, q_width), jnp.bfloat16),
        jax.ShapeDtypeStruct((seqs, heads, rows), jnp.float32),
    ]
    return pl.pallas_call(
        functools.partial(attend_kernel, len(blocks)),
        out_shape=out_shape,
        grid_spec=pltpu.PrefetchScalarGridSpec(
            num_scalar_prefetch=1,
            grid=(seqs,),
            in_specs=[whole(array) for array in (gpos, queries, *blocks)],
            out_specs=[whole(array) for array in out_shape],
            scratch_shapes=[pltpu.VMEM((key_total, rows), jnp.float32)],
        ),
        compiler_params=pltpu.CompilerParams(vmem_limit_bytes=48 * 2**20),
        cost_estimate=pl.CostEstimate(
            flops=16 * seqs * heads * rows * key_total * HD,
            bytes_accessed=4 * queries.size,
            transcendentals=seqs * heads * rows * key_total,
        ),
    )(band, gpos, queries, *blocks)


def attend_back_kernel(block_total, band_ref, gpos_ref, cos_ref, sin_ref, q_ref, grad_ref, lse_ref, *refs):
    blocks = refs[:block_total]
    dq_ref = refs[block_total]
    out_refs = refs[block_total + 1 : 2 * block_total + 1]
    bias_ref = refs[-1]
    rows, q_width = q_ref.shape[1:]
    kv_width = blocks[0].shape[2] // 2
    heads, group = q_width // HD, q_width // kv_width
    window_len = rows * (block_total - 1)
    fill_bias(band_ref, gpos_ref, bias_ref, rows, window_len)
    starts = [rows * number for number in range(block_total)]
    pending = []
    for kv_head in range(kv_width // HD):
        left = kv_head * HD
        key_sums = [0.0] * block_total
        value_sums = [0.0] * block_total
        for head in range(kv_head * group, (kv_head + 1) * group):
            queries = q_ref[0, :, head * HD : (head + 1) * HD]
            grads = grad_ref[0, :, head * HD : (head + 1) * HD]
            lse = lse_ref[0, head : head + 1, :]
            soft, soft_grads = [], []
            inner = 0.0
            for number, (block, start) in enumerate(zip(blocks, starts)):
                part = over_last(block[0, :, left : left + HD], queries)
                part = jnp.exp(part + bias_ref[start : start + block.shape[1]] - lse)
                slope = over_last(block[0, :, kv_width + left : kv_width + left + HD], grads)
                inner = inner + jnp.sum(part * slope, 0, keepdims=True)
                soft.append(part)
                soft_grads.append(slope)
            turned = 0.0
            for number, block in enumerate(blocks):
                score_grads = (soft[number] * (soft_grads[number] - inner)).astype(jnp.bfloat16)
                value_sums[number] = value_sums[number] + jnp.dot(
                    soft[number].astype(jnp.bfloat16), grads, preferred_element_type=jnp.float32
                )
                key_sums[number] = key_sums[number] + jnp.dot(
                    score_grads, queries, preferred_element_type=jnp.float32
                )
                turned = turned + over_first(block[0, :, left : left + HD], score_grads)
            pending.append(turned)
            if len(pending) * HD == BLK or head == heads - 1:
                stop = (head + 1) * HD
                both = jnp.concatenate(pending, 0).T * HD ** (-0.5)
                pending = []
                first, other = half_turn(both * sin_ref[0])
                both = both * cos_ref[0] + jnp.where(first, other, -other)
                dq_ref[0, :, stop - both.shape[1] : stop] = both.astype(jnp.bfloat16)
        for number, out_ref in enumerate(out_refs):
            out_ref[0, :, left : left + HD] = key_sums[number].astype(out_ref.dtype)
            out_ref[0, :, kv_width + left : kv_width + left + HD] = value_sums[number].astype(
                out_ref.dtype
            )


def attend_back(band, gpos, cosines, sines, queries, grads, lse, blocks):
    seqs, rows, q_width = queries.shape
    heads = q_width // HD
    key_total = sum(block.shape[1] for block in blocks)

    def whole(array):
        return pl.BlockSpec((1,) + array.shape[1:], lambda s, *_: (s, 0, 0))

    table = pl.BlockSpec((1, rows, BLK), lambda s, *_: (0, 0, 0))
    out_shape = [jax.ShapeDtypeStruct(queries.shape, jnp.bfloat16)]
    for number, block in enumerate(blocks):
        own = number == len(blocks) - 2
        out_shape.append(jax.ShapeDtypeStruct(block.shape, jnp.float32 if own else jnp.bfloat16))
    return pl.pallas_call(
        functools.partial(attend_back_kernel, len(blocks)),
        out_shape=out_shape,
        grid_spec=pltpu.PrefetchScalarGridSpec(
            num_scalar_prefetch=1,
            grid=(seqs,),
            in_specs=[whole(gpos), table, table]
            + [whole(array) for array in (queries, grads, lse, *blocks)],
            out_specs=[whole(array) for array in out_shape],
            scratch_shapes=[pltpu.VMEM((key_total, rows), jnp.float32)],
        ),
        compiler_params=pltpu.CompilerParams(vmem_limit_bytes=48 * 2**20),
        cost_estimate=pl.CostEstimate(
            flops=40 * seqs * heads * rows * key_total * HD,
            bytes_accessed=8 * queries.size,
            transcendentals=seqs * heads * rows * key_total,
        ),
    )(band, gpos, cosines, sines, queries, grads, lse, *blocks)


def join_kernel(q_width, kv_width, dq_ref, own_ref, pick_ref, glob_ref, cos_ref, sin_ref, *refs):
    back_refs, out_ref = refs[:-1], refs[-1]
    out_ref[0, :, :q_width] = dq_ref[0]
    picked = lax.dot_general(
        pick_ref[0].astype(jnp.float32),
        glob_ref[0],
        (((0,), (0,)), ((), ())),
        precision=lax.Precision.HIGHEST,
        preferred_element_type=jnp.float32,
    )
    for start in range(0, 2 * kv_width, BLK):
        lanes = slice(start, start + BLK)
        total = own_ref[0, :, lanes] + picked[:, lanes]
        for back_ref in back_refs:
            total = total + back_ref[0, :, lanes].astype(jnp.float32)
        first, other = half_turn(total * sin_ref[0])
        turned = total * cos_ref[0] + jnp.where(first, other, -other)
        column = lax.broadcasted_iota(jnp.int32, total.shape, 1) + start
        turned = jnp.where(column >= kv_width, total, turned)
        out_ref[0, :, q_width + start : q_width + start + BLK] = turned.astype(jnp.bfloat16)


def join_grads(dq, own, picks, globs, cosines, sines, backs):
    seqs, rows, q_width = dq.shape
    kv_width = own.shape[2] // 2

    def whole(array):
        return pl.BlockSpec((1,) + array.shape[1:], lambda s: (s, 0, 0))

    table = pl.BlockSpec((1, rows, BLK), lambda s: (0, 0, 0))
    out_shape = jax.ShapeDtypeStruct((seqs, rows, q_width + 2 * kv_width), jnp.bfloat16)
    return pl.pallas_call(
        functools.partial(join_kernel, q_width, kv_width),
        out_shape=out_shape,
        grid=(seqs,),
        in_specs=[whole(dq), whole(own), whole(picks), whole(globs), table, table]
        + [whole(back) for back in backs],
        out_specs=whole(out_shape),
        cost_estimate=pl.CostEstimate(
            flops=20 * own.size, bytes_accessed=4 * dq.size + 12 * own.size, transcendentals=0
        ),
    )(dq, own, picks, globs, cosines, sines, *backs)


def adam_kernel(batch, meta, rates, *refs):
    master_ref, first_ref, second_ref, left_ref, right_ref = refs[:5]
    sources = refs[5:-6]
    new_first_ref, new_second_ref, new_master_ref, copy_ref, tiles, arrived = refs[-6:]
    step, steps = pl.program_id(0), pl.num_programs(0)
    slot = step % 2

    def fetch(at_step, at_slot):
        for place in range(batch):
            tile = at_step * batch + place
            for number, source in enumerate(sources):

                @pl.when(meta[0, tile] == number)
                def _(source=source, tile=tile, place=place):
                    top = pl.multiple_of(meta[2, tile], BLK)
                    left = pl.multiple_of(meta[3, tile], BLK)
                    pltpu.make_async_copy(
                        source.at[meta[1, tile], pl.ds(top, BLK), pl.ds(left, BLK)],
                        tiles.at[at_slot, place],
                        arrived.at[at_slot],
                    ).start()

    @pl.when(step == 0)
    def _():
        fetch(0, 0)

    @pl.when(step + 1 < steps)
    def _():
        fetch(step + 1, 1 - slot)

    pltpu.make_async_copy(tiles.at[slot], tiles.at[slot], arrived.at[slot]).wait()
    places = range(batch)
    lefts = [left_ref[place].astype(jnp.bfloat16) for place in places]
    rights = [right_ref[place].astype(jnp.bfloat16) for place in places]
    turned = [over_first(lefts[place], tiles[slot, place]).astype(jnp.bfloat16) for place in places]
    rotated = [
        jnp.dot(turned[place], rights[place], preferred_element_type=jnp.float32) for place in places
    ]
    directions = []
    for place in places:
        new_first = beta_one * first_ref[place] + (1.0 - beta_one) * rotated[place]
        new_second = beta_two * second_ref[place] + (1.0 - beta_two) * rotated[place] * rotated[place]
        direction = (new_first * (1.0 / (1.0 - beta_one**STEP))) / (
            jnp.sqrt(new_second * (1.0 / (1.0 - beta_two**STEP))) + adam_eps
        )
        new_first_ref[place] = new_first
        new_second_ref[place] = new_second
        directions.append(direction.astype(jnp.bfloat16))
    updates = [
        jnp.dot(lefts[place], directions[place], preferred_element_type=jnp.float32) for place in places
    ]
    updates = [over_last(updates[place].astype(jnp.bfloat16), rights[place]) for place in places]
    for place in places:
        old = master_ref[place]
        new_master = old - rates[step * batch + place] * (updates[place] + weight_decay * old)
        new_master_ref[place] = new_master
        copy_ref[place] = new_master.astype(jnp.bfloat16)


def adam(meta, rates, state, sources):
    count = state[0].shape[0]
    batch = max(size for size in range(1, 33) if count % size == 0)
    block = pl.BlockSpec((batch, BLK, BLK), lambda s, *_: (s, 0, 0))
    anywhere = pl.BlockSpec(memory_space=pl.ANY)
    shape = (count, BLK, BLK)
    return pl.pallas_call(
        functools.partial(adam_kernel, batch),
        out_shape=[jax.ShapeDtypeStruct(shape, jnp.float32)] * 3
        + [jax.ShapeDtypeStruct(shape, jnp.bfloat16)],
        grid_spec=pltpu.PrefetchScalarGridSpec(
            num_scalar_prefetch=2,
            grid=(count // batch,),
            in_specs=[block] * 5 + [anywhere] * len(sources),
            out_specs=[block] * 4,
            scratch_shapes=[
                pltpu.VMEM((2, batch, BLK, BLK), jnp.bfloat16),
                pltpu.SemaphoreType.DMA((2,)),
            ],
        ),
        compiler_params=pltpu.CompilerParams(vmem_limit_bytes=56 * 2**20),
        cost_estimate=pl.CostEstimate(
            flops=8 * count * BLK**3, bytes_accessed=36 * count * BLK**2, transcendentals=0
        ),
    )(meta, rates, *state, *sources)


def per_device(
    block_input,
    cotangent,
    glob_select,
    assignment,
    master,
    first_moment,
    second_moment,
    left_basis,
    right_basis,
    gains,
    gain_first,
    gain_second,
):
    band_total = lax.axis_size("fsdp")
    rep_total = lax.axis_size("rep")
    place = lax.axis_index("rep")
    band = lax.axis_index("fsdp")
    heads = H // rep_total
    kv_heads = KVH // rep_total
    q_width = heads * HD
    kv_width = kv_heads * HD
    tok_count = block_input.shape[1]
    own_count = master.shape[1]
    tile_total = own_count * rep_total
    aligned = square() and whole_tiles(band_total, rep_total)
    tile_order = assignment[0]

    residual = block_input[0].astype(jnp.float32)
    grad_top = cotangent[0]
    position = band * tok_count + jnp.arange(tok_count, dtype=jnp.int32)
    cosine_table, sine_table = rope_tables(position)
    wide_cosine = jnp.concatenate([cosine_table, cosine_table], 1)[None]
    wide_sine = jnp.concatenate([sine_table, sine_table], 1)[None]
    scale_one = lax.rsqrt(jnp.mean(residual * residual, -1, keepdims=True) + norm_eps)
    normed_one = (residual * scale_one * gains[0]).astype(jnp.bfloat16)
    pick_rows = glob_select[0]
    glob_total = pick_rows.shape[0]
    selector = pick_rows.astype(jnp.bfloat16)
    glob_pos_part = jnp.sum(pick_rows * position[None, :], 1)
    digits = jnp.concatenate([glob_pos_part // 256, glob_pos_part % 256]).astype(jnp.bfloat16)
    digits = jnp.pad(digits[None], ((0, 7), (0, D - 2 * glob_total)))
    glob_rows = jnp.dot(selector, normed_one, preferred_element_type=jnp.float32).astype(jnp.bfloat16)
    glob_rows = add_all(jnp.concatenate([glob_rows, digits], 0), "fsdp").astype(jnp.bfloat16)
    packed = [normed_one, glob_rows, selector.reshape(-1, D)]
    packed = jnp.concatenate(packed, 0)
    packed = jnp.pad(packed, ((0, -packed.shape[0] % 32), (0, 0)))

    def over_bands(slice_rows):
        return lax.all_gather(slice_rows, "fsdp", axis=0, tiled=True)

    if aligned:
        half = BLK // 2
        low, high = (master[0, :, rows].astype(jnp.bfloat16) for rows in (slice(0, half), slice(half, BLK)))
        layout = slice_layout(band_total, rep_total)
        attn_layout = jnp.asarray(np.concatenate(layout[:4], 2))
        wanted = jnp.take(tile_order, by_place(attn_layout).reshape(-1), mode="clip")
        meta = jnp.stack([wanted // own_count == place, wanted % own_count], 0).astype(jnp.int32)
        attn_part = place_tiles(low, high, meta, *attn_layout.shape)
        attn_part = rep_scatter(attn_part).astype(jnp.bfloat16)
        low, attn_part = lax.optimization_barrier((low, attn_part))
        slots = square_pieces(low)
        attn = over_bands(attn_part)
        *slots, attn = lax.optimization_barrier((*slots, attn))
        grids = [lax.dynamic_index_in_dim(jnp.asarray(grid), place, 0, False) for grid in layout]

        def find(wanted):
            wanted = jnp.take(tile_order, jnp.concatenate([grid.reshape(-1) for grid in wanted]), mode="clip")
            entry, row = (wanted // own_count) ^ place, wanted % own_count
            cut = own_count // 2
            high = (entry == 3) & (row >= cut)
            found = jnp.stack([jnp.where(high, 4, entry), jnp.where(high, row - cut, row)], 0)
            return found.astype(jnp.int32)

        all_grid = jnp.concatenate(grids[4:], 1)
        (first_part,) = gather_strips(slots, find([all_grid]), [all_grid.shape])
        packed, first_part = lax.optimization_barrier((packed, first_part))
        early = over_bands(first_part)
    packed_all = rep_gather(packed)
    packed_all, grad_top_now = lax.optimization_barrier((packed_all, grad_top))
    grad_top_all = rep_gather(grad_top_now).reshape(-1, D)
    if aligned:
        grad_top_all, high = lax.optimization_barrier((grad_top_all, high))
        later_slots = square_pieces(high)
    normed_one_all = packed_all[:, :tok_count].reshape(-1, D)
    at = tok_count + glob_total
    glob_digits = packed_all[:, at, : 2 * glob_total].astype(jnp.float32)
    glob_place = glob_digits[:, :glob_total] * 256.0 + glob_digits[:, glob_total:]
    at += 8
    selector_all = packed_all[:, at : at + selector.size // D].reshape(rep_total, glob_total, tok_count)

    if aligned:
        in_width = q_width + 2 * kv_width
        w_inner, w_output = attn[:, :in_width], attn[:, in_width:]
    else:
        slots = lax.all_gather(master[0].astype(jnp.bfloat16), "rep", axis=0, tiled=True)
        tiles = jnp.take(slots, tile_order, axis=0, mode="clip")
        slices = cut_slices(band_matrices(tiles, band_total), band_total, rep_total)
        w_inner = over_bands(jnp.concatenate(slices[0:3], 1))
        w_output = over_bands(slices[3])
        w_gate = over_bands(slices[4])
        w_up = over_bands(slices[5])
        w_down = over_bands(slices[6])

    w_output = by_place(w_output.reshape(rep_total, q_width, -1)).reshape(D, -1)

    def mul(rows, weight):
        return jnp.dot(rows, weight, preferred_element_type=jnp.float32)

    def mul_back(rows, weight):
        return lax.dot_general(rows, weight, (((1,), (1,)), ((), ())), preferred_element_type=jnp.float32)

    def weight_grad(rows, grad_rows):
        return lax.dot_general(
            rows, grad_rows, (((0,), (0,)), ((), ())), preferred_element_type=jnp.float32
        ).astype(jnp.bfloat16)

    def own_sum(partial):
        return rep_scatter(partial.astype(jnp.bfloat16).reshape(rep_total, tok_count, D))

    inner_rows = mul(packed_all.reshape(-1, D), w_inner).reshape(rep_total, -1, w_inner.shape[1])
    packed_all, normed_one_all = lax.optimization_barrier((packed_all, normed_one_all))
    queries, own_pairs = rope_rows(inner_rows, tok_count, 0, q_width, kv_width, wide_cosine, wide_sine)
    glob_cosine, glob_sine = rope_tables(glob_place.reshape(-1))
    glob_cosine = jnp.concatenate([glob_cosine, glob_cosine], 1).reshape(rep_total, glob_total, -1)
    glob_sine = jnp.concatenate([glob_sine, glob_sine], 1).reshape(rep_total, glob_total, -1)
    (glob_pairs,) = rope_rows(
        inner_rows, glob_total, tok_count // glob_total, q_width, kv_width, glob_cosine, glob_sine, False
    )
    back_count = (WINDOW + tok_count - 2) // tok_count
    pair_blocks = [shifted(own_pairs, "fsdp", distance) for distance in range(back_count, 0, -1)]
    pair_blocks = pair_blocks + [own_pairs, glob_pairs]
    glob_spots = jnp.broadcast_to(glob_place[:, :, None], (rep_total, glob_total, BLK))
    band_number = band.astype(jnp.int32).reshape(1)
    attended_low, lse = attend(band_number, glob_spots, queries, pair_blocks)
    if aligned:
        *later_slots, attended_low, early = lax.optimization_barrier((*later_slots, attended_low, early))
        last_grid = jnp.concatenate(grids[4:6], 1)
        last_part, down_part = gather_strips(
            later_slots, find([last_grid, grids[6]]), [last_grid.shape, grids[6].shape]
        )

        def by_strips(part):
            gathered = over_bands(part)
            return gathered.reshape(band_total, -1, last_grid.shape[0], half, gathered.shape[-1])

        early = early.reshape(band_total, -1, all_grid.shape[0], half, early.shape[-1])
        late, late_down = by_strips(last_part), by_strips(down_part)
    attended_all = rep_features(attended_low).reshape(-1, D)
    columns = mul(attended_all, w_output).astype(jnp.bfloat16).reshape(rep_total, tok_count, -1)
    branch = by_place(rep_exchange(columns)).transpose(1, 0, 2).reshape(tok_count, D)
    middle = residual + branch.astype(jnp.float32)
    scale_two = lax.rsqrt(jnp.mean(middle * middle, -1, keepdims=True) + norm_eps)
    normed_two = (middle * scale_two * gains[1]).astype(jnp.bfloat16)
    normed_two_all = rep_gather(normed_two).reshape(-1, D)
    normed_two_all, grad_top_all = lax.optimization_barrier((normed_two_all, grad_top_all))

    if aligned:
        gate_rows, up_rows, activation = forward_products(normed_two_all, early, late, FF // rep_total)
        g_down = weight_grad(activation, grad_top_all)
        grad_top_all, g_down = lax.optimization_barrier((grad_top_all, g_down))
        grad_gate, grad_up, pieces, branch_pieces = backward_products(
            grad_top_all, gate_rows, up_rows, activation, early, late, late_down
        )
        grad_normed_two = sum_pieces(*pieces)
    else:
        gate_rows = mul(normed_two_all, w_gate)
        up_rows = mul(normed_two_all, w_up)
        sigmoid_gate = jax.nn.sigmoid(gate_rows)
        silu_gate = gate_rows * sigmoid_gate
        activation = (silu_gate * up_rows).astype(jnp.bfloat16)
        g_down = weight_grad(activation, grad_top_all)
        grad_act = mul_back(grad_top_all, w_down)
        grad_gate = (
            grad_act * up_rows * sigmoid_gate * (1.0 + gate_rows * (1.0 - sigmoid_gate))
        ).astype(jnp.bfloat16)
        grad_up = (grad_act * silu_gate).astype(jnp.bfloat16)
        grad_normed_two = own_sum(mul_back(grad_gate, w_gate) + mul_back(grad_up, w_up))
        branch_pieces = (mul(activation, w_down),)
    g_gate = weight_grad(normed_two_all, grad_gate)
    g_up = weight_grad(normed_two_all, grad_up)
    grad_normed_two, g_gate, g_up = lax.optimization_barrier((grad_normed_two, g_gate, g_up))

    def over_tokens(partial):
        return lax.psum_scatter(partial, "fsdp", scatter_dimension=0, tiled=True)

    s_down = over_tokens(g_down)
    s_gate = over_tokens(g_gate)
    s_up = over_tokens(g_up)

    grad_middle = grad_top.astype(jnp.float32) + norm_back(middle, scale_two, gains[1], grad_normed_two)
    grad_parts = grad_middle.astype(jnp.bfloat16).reshape(tok_count, rep_total, -1).transpose(1, 0, 2)
    grad_columns = rep_exchange(by_place(grad_parts)).reshape(rep_total * tok_count, -1)
    grad_attended = rep_features_sum(
        grad_columns.reshape(rep_total, tok_count, -1), w_output
    ).astype(jnp.bfloat16)
    g_output = weight_grad(attended_all, grad_columns)
    g_output = by_place(g_output.reshape(rep_total, q_width, -1)).reshape(D, -1)
    grad_attended, s_down, *branch_pieces = lax.optimization_barrier((grad_attended, s_down, *branch_pieces))
    s_down = rep_gather(s_down)
    block_out = middle + (sum_pieces(*branch_pieces) if aligned else own_sum(branch_pieces[0]))
    grad_queries, *grad_blocks = attend_back(
        band_number, glob_spots, wide_cosine, wide_sine, queries, grad_attended, lse, pair_blocks
    )
    returned = [
        shifted(grad_blocks[back_count - distance], "fsdp", -distance)
        for distance in range(1, back_count + 1)
    ]
    glob_grads = add_all(grad_blocks[-1], "fsdp")
    s_gate = rep_gather(s_gate)
    glob_grads, s_gate, s_down, block_out = lax.optimization_barrier(
        (glob_grads, s_gate, s_down, block_out)
    )
    grad_inner = join_grads(
        grad_queries, grad_blocks[-2], selector_all, glob_grads, wide_cosine, wide_sine, returned
    ).reshape(-1, q_width + 2 * kv_width)
    g_inner, s_up = lax.optimization_barrier((weight_grad(normed_one_all, grad_inner), s_up))
    s_up = rep_gather(s_up)
    s_attn = over_tokens(jnp.concatenate([g_inner, g_output], 1))
    grad_normed_one = own_sum(mul_back(grad_inner, w_inner))
    grad_normed_one, s_up = lax.optimization_barrier((grad_normed_one, s_up))
    grad_input = grad_middle + norm_back(residual, scale_one, gains[0], grad_normed_one)

    gain_terms = jnp.stack(
        [
            jnp.sum(grad_normed_one * residual * scale_one, 0),
            jnp.sum(grad_normed_two * middle * scale_two, 0),
        ]
    )
    square_terms = jnp.stack(
        [jnp.sum(residual * residual), jnp.sum(middle * middle), jnp.sum(block_out * block_out)]
    )
    sums, s_attn = lax.optimization_barrier((jnp.concatenate([gain_terms.reshape(-1), square_terms]), s_attn))

    slot_ids = jnp.arange(tile_total, dtype=jnp.int32)
    inverse = jnp.sum(jnp.where(tile_order[None, :] == slot_ids[:, None], slot_ids[None, :], 0), 1)
    own_slots = place * own_count + jnp.arange(own_count, dtype=jnp.int32)
    owned_tiles = jnp.take(inverse, own_slots, mode="clip")
    if aligned:
        sources = [rep_gather(s_attn), s_gate, s_up, s_down]
        where = np.zeros((4, rep_total, tile_total), np.int32)
        first_col = 0
        for kind, grid in enumerate(layout):
            rows, cols = grid.shape[1:]
            first_col = 0 if kind >= 4 else first_col
            for there in range(rep_total):
                numbers = grid[there].reshape(-1)
                at = np.arange(rows * cols)
                where[0, :, numbers] = max(kind - 3, 0)
                where[2, :, numbers] = (at // cols * BLK)[:, None]
                where[3, :, numbers] = (at % cols * BLK + first_col)[:, None]
                for here in range(rep_total):
                    where[1, here, numbers] = here ^ there
            first_col += cols * BLK
        tile_spots = lax.dynamic_index_in_dim(jnp.asarray(where), place, 1, False)
        meta = jnp.take(tile_spots, owned_tiles, axis=1, mode="clip")
    else:
        splits = [0, q_width, q_width + kv_width, q_width + 2 * kv_width, s_attn.shape[1]]
        stacks = [rep_gather(s_attn[:, low:high]) for low, high in zip(splits, splits[1:])]
        stacks += [s_gate, s_up, s_down]
        sources = [band_tiles(join_slices(stacks, band_total, rep_total))]
        meta = jnp.stack([0 * owned_tiles, owned_tiles, 0 * owned_tiles, 0 * owned_tiles], 0)
    slot_rates = jnp.take(kind_rates(band_total), owned_tiles, mode="clip")
    new_first, new_second, new_master, master_copy = adam(
        meta,
        slot_rates,
        (master[0], first_moment[0], second_moment[0], left_basis[0], right_basis[0]),
        sources,
    )
    sums = add_all(add_all(sums, "rep"), "fsdp")
    gain_grad, square_total = sums[: 2 * D].reshape(2, D), sums[2 * D :]
    new_gain_first = beta_one * gain_first + (1.0 - beta_one) * gain_grad
    new_gain_second = beta_two * gain_second + (1.0 - beta_two) * gain_grad * gain_grad
    gain_step = (
        new_gain_first
        / (1.0 - beta_one**STEP)
        / (jnp.sqrt(new_gain_second / (1.0 - beta_two**STEP)) + adam_eps)
    )
    new_gains = gains - gain_rate * gain_step
    rms_stats = jnp.sqrt(square_total / (rep_total * band_total * tok_count * D))
    return (
        block_out[None],
        grad_input[None],
        new_first[None],
        new_second[None],
        new_master[None],
        master_copy[None],
        new_gain_first,
        new_gain_second,
        new_gains,
        rms_stats,
    )


def solution(mesh):
    in_specs = (
        P("rep", "fsdp", None),
        P("rep", "fsdp", None),
        P("rep", None, "fsdp"),
        P("fsdp", None),
        P("fsdp", "rep", None, None),
        P("fsdp", "rep", None, None),
        P("fsdp", "rep", None, None),
        P("fsdp", "rep", None, None),
        P("fsdp", "rep", None, None),
        P(),
        P(),
        P(),
    )
    out_specs = (
        P("rep", "fsdp", None),
        P("rep", "fsdp", None),
        P("fsdp", "rep", None, None),
        P("fsdp", "rep", None, None),
        P("fsdp", "rep", None, None),
        P("fsdp", "rep", None, None),
        P(),
        P(),
        P(),
        P(),
    )
    return jax.shard_map(
        per_device, mesh=mesh, in_specs=in_specs, out_specs=out_specs, check_vma=False
    )
```

```python
import functools

import jax
import jax.numpy as jnp
import numpy as np
from jax import lax
from jax.experimental import pallas as pl
from jax.experimental.pallas import tpu as pltpu
from jax.sharding import PartitionSpec as P

D = 2048
H = 32
KVH = 8
HD = 64
FF = 8192
WINDOW = 512
BLK = 128
STEP = 10


norm_eps = 1e-05
rope_theta = 500000.0
beta_one = 0.5
beta_two = 0.5
adam_eps = 1e-08
weight_decay = 0.1
gain_rate = 0.5
masked_value = -1e30


def matrix_shapes():
    kv_width = KVH * HD
    return [(D, D), (D, kv_width), (D, kv_width), (D, D), (D, FF), (D, FF), (FF, D)]


def kind_rates(band_total):
    rate_list = [
        D ** (-0.5),
        D ** (-0.5),
        D ** (-0.5),
        (D * 8 // WINDOW) ** (-0.5),
        D ** (-0.5),
        D ** (-0.5),
        FF ** (-0.5),
    ]
    pieces = []
    for (row_total, col_total), rate_value in zip(matrix_shapes(), rate_list):
        tile_count = row_total // band_total // BLK * (col_total // BLK)
        pieces.append(jnp.full((tile_count,), rate_value, jnp.float32))
    return jnp.concatenate(pieces)


def band_matrices(tiles, band_total):
    matrices = []
    offset = 0
    for row_total, col_total in matrix_shapes():
        band_rows = row_total // band_total
        tile_count = band_rows // BLK * (col_total // BLK)
        segment = tiles[offset : offset + tile_count].reshape(
            band_rows // BLK, col_total // BLK, BLK, BLK
        )
        matrices.append(segment.transpose(0, 2, 1, 3).reshape(band_rows, col_total))
        offset += tile_count
    return matrices


def band_tiles(matrices):
    pieces = []
    for matrix in matrices:
        row_count, col_count = matrix.shape
        segment = matrix.reshape(row_count // BLK, BLK, col_count // BLK, BLK).transpose(0, 2, 1, 3)
        pieces.append(segment.reshape(-1, BLK, BLK))
    return jnp.concatenate(pieces, 0)


def rope_tables(position):
    halves = jnp.arange(HD // 2, dtype=jnp.float32) * (2.0 / HD)
    frequency = rope_theta ** (-halves)
    angles = position.astype(jnp.float32)[:, None] * frequency[None, :]
    angles = jnp.concatenate([angles, angles], 1)
    return (jnp.cos(angles), jnp.sin(angles))


def rotate(vectors, cosine_table, sine_table):
    half_width = vectors.shape[-1] // 2
    turned = jnp.concatenate([-vectors[..., half_width:], vectors[..., :half_width]], -1)
    return vectors * cosine_table[:, None, :] + turned * sine_table[:, None, :]


def rotate_back(grad_rows, cosine_table, sine_table):
    half_width = grad_rows.shape[-1] // 2
    scaled = grad_rows * sine_table[:, None, :]
    turned = jnp.concatenate([scaled[..., half_width:], -scaled[..., :half_width]], -1)
    return grad_rows * cosine_table[:, None, :] + turned


def norm_back(values, row_scale, gain_row, grad_rows):
    weighted = grad_rows * gain_row
    return row_scale * weighted - values * row_scale**3 * jnp.mean(
        weighted * values, -1, keepdims=True
    )


def to_rep(block, distance):
    route = [(i, i ^ distance) for i in range(lax.axis_size("rep"))]
    return lax.ppermute(block, "rep", route)


def square():
    return lax.axis_size("rep") == 4


def square_pieces(block):
    cut = block.shape[0] // 2
    near = to_rep(block, 1)
    far = to_rep(block, 2)
    return block, near, far, to_rep(near[:cut], 2), to_rep(far[cut:], 1)


def rep_gather(block):
    if not square():
        return lax.all_gather(block, "rep", axis=0)
    own, near, far, low, high = square_pieces(block)
    return jnp.concatenate([own, near, far, low, high], 0).reshape((4,) + block.shape)


def rep_of(entry):
    place = lax.axis_index("rep")
    return place ^ entry if square() else entry


def rep_scatter(parts):
    if not square():
        flat = parts.reshape(-1, parts.shape[-1])
        return lax.psum_scatter(flat, "rep", scatter_dimension=0, tiled=True).astype(jnp.float32)
    half = parts.shape[-1] // 2
    low, high = parts[..., :half], parts[..., half:]
    return sum_pieces(
        jnp.stack([low[0], low[2]], 0), jnp.stack([low[1], low[3]], 0), high[:2], high[2:]
    )


def sum_pieces(low_kept, low_sent, high_kept, high_sent):
    totals = []
    for kept, sent, first, second in ((low_kept, low_sent, 1, 2), (high_kept, high_sent, 2, 1)):
        came = to_rep(sent, first)
        other = (kept[1].astype(jnp.float32) + came[1].astype(jnp.float32)).astype(kept.dtype)
        own = kept[0].astype(jnp.float32) + came[0].astype(jnp.float32)
        totals.append(own + to_rep(other, second).astype(jnp.float32))
    return jnp.concatenate(totals, -1)


def add_all(value, axis):
    size = lax.axis_size(axis)
    total = value.astype(jnp.float32)
    distance = 1
    while distance < size:
        count = 2 if (size // distance).bit_length() % 2 == 0 else 4
        low = total.astype(value.dtype)
        others = []
        for step in range(1, count):
            route = [(i, i ^ (step * distance)) for i in range(size)]
            others.append(lax.ppermute(low, axis, route).astype(jnp.float32))
        total = total + others[0]
        if count == 4:
            total = total + (others[1] + others[2])
        distance *= count
    return total


def rep_features(block):
    if not square():
        return lax.all_gather(block, "rep", axis=2, tiled=True)
    own, near, far, low, high = square_pieces(block)
    return jnp.concatenate(
        [
            own,
            jnp.stack([near[1], near[0], near[3], near[2]], 0),
            jnp.stack([far[2], far[3], far[0], far[1]], 0),
            jnp.stack([high[1], high[0], low[1], low[0]], 0),
        ],
        2,
    )


def write_pieces(entry, rows, values, refs):
    low_kept, low_sent, high_kept, high_sent = refs
    half = low_kept.shape[-1]
    values = values.astype(jnp.bfloat16)
    (low_sent if entry % 2 else low_kept)[entry // 2, rows] = values[:, :half]
    (high_sent if entry // 2 else high_kept)[entry % 2, rows] = values[:, half:]


def swapped_kernel(x_ref, w_ref, *refs):
    reps, rows, _ = x_ref.shape
    width = w_ref.shape[0] // reps
    for entry in range(reps):
        weight = w_ref[entry * width : (entry + 1) * width]
        for there in range(reps):
            product = over_last(x_ref[there ^ entry], weight)
            write_pieces(entry, slice(there * rows, (there + 1) * rows), product, refs)


def rep_features_sum(columns, weight):
    reps, rows, depth = columns.shape
    width = weight.shape[0] // reps
    if square():
        pieces = pl.pallas_call(
            swapped_kernel,
            out_shape=[jax.ShapeDtypeStruct((2, reps * rows, width // 2), jnp.bfloat16)] * 4,
            compiler_params=pltpu.CompilerParams(vmem_limit_bytes=32 * 2**20),
            cost_estimate=pl.CostEstimate(
                flops=2 * reps * columns.size * width,
                bytes_accessed=10 * columns.size,
                transcendentals=0,
            ),
        )(columns, weight)
        total = sum_pieces(*pieces)
    else:
        product = over_last(columns.reshape(-1, depth), weight).astype(jnp.bfloat16)
        swapped = product.reshape(reps, rows, reps, width).transpose(2, 0, 1, 3)
        total = rep_scatter(swapped.reshape(reps, reps * rows, width))
    return total.reshape(reps, rows, width)


def rep_exchange(parts):
    if not square():
        return lax.all_to_all(parts, "rep", 0, 0)
    return jnp.stack([parts[0]] + [to_rep(parts[entry], entry) for entry in (1, 2, 3)], 0)


def by_place(parts):
    entries = [rep_of(entry) for entry in range(parts.shape[0])]
    return jnp.stack([lax.dynamic_index_in_dim(parts, entry, 0, False) for entry in entries], 0)


def shifted(block, axis, distance):
    devices = range(lax.axis_size(axis))
    route = [(i - distance, i) for i in devices if i - distance in devices]
    return lax.ppermute(block, axis, route)


def tile_offsets(band_total):
    offsets = [0]
    for row_total, col_total in matrix_shapes():
        offsets.append(offsets[-1] + row_total // band_total // BLK * (col_total // BLK))
    return offsets


def whole_tiles(band_total, rep_total):
    return KVH * HD // rep_total % BLK == 0 and FF // band_total // rep_total % BLK == 0


def slice_layout(band_total, rep_total):
    offsets = tile_offsets(band_total)
    layout = []
    for kind, (row_total, col_total) in enumerate(matrix_shapes()):
        rows, cols = row_total // band_total // BLK, col_total // BLK
        grid = offsets[kind] + np.arange(rows * cols).reshape(rows, cols)
        if kind == 6:
            layout.append(grid.reshape(rep_total, rows // rep_total, cols))
        elif kind in (4, 5):
            cut = grid.reshape(rows, band_total, rep_total, -1).transpose(2, 0, 1, 3)
            layout.append(cut.reshape(rep_total, rows, -1))
        else:
            layout.append(grid.reshape(rows, rep_total, -1).transpose(1, 0, 2))
    return layout


def tiles_to_matrix(tiles):
    rows, cols = tiles.shape[:2]
    return tiles.transpose(0, 2, 1, 3).reshape(rows * BLK, cols * BLK)


def matrix_to_tiles(matrix):
    rows, cols = matrix.shape
    cut = matrix.reshape(rows // BLK, BLK, cols // BLK, BLK)
    return cut.transpose(0, 2, 1, 3).reshape(-1, BLK, BLK)


def cut_slices(matrices, band_total, rep_total):
    place = lax.axis_index("rep")
    slices = []
    for kind, matrix in enumerate(matrices):
        rows, cols = matrix.shape
        if kind == 6:
            slices.append(lax.dynamic_slice_in_dim(matrix, place * (rows // rep_total), rows // rep_total, 0))
        elif kind in (4, 5):
            cut = matrix.reshape(rows, band_total, rep_total, -1)
            slices.append(lax.dynamic_index_in_dim(cut, place, 2, False).reshape(rows, -1))
        else:
            slices.append(lax.dynamic_slice_in_dim(matrix, place * (cols // rep_total), cols // rep_total, 1))
    return slices


def join_slices(stacks, band_total, rep_total):
    matrices = []
    for kind, stack in enumerate(stacks):
        rows, cols = stack.shape[1:]
        if kind == 6:
            matrices.append(stack.reshape(-1, cols))
        elif kind in (4, 5):
            cut = stack.reshape(rep_total, rows, band_total, -1).transpose(1, 2, 0, 3)
            matrices.append(cut.reshape(rows, -1))
        else:
            matrices.append(stack.transpose(1, 0, 2).reshape(rows, -1))
    return matrices


def gather_kernel(grids, meta, *refs):
    source_total = len(refs) - len(grids) - 1
    sources, targets, done = refs[:source_total], refs[source_total:-1], refs[-1]
    height = sources[0].shape[1]
    start = 0
    for place, (target, (rows, cols)) in enumerate(zip(targets, grids)):

        def one(tile, carry, target=target, rows=rows, cols=cols, start=start, place=place):
            kind = meta[0, start + tile]
            row = meta[1, start + tile]
            across = tile % cols
            top = pl.multiple_of((across // 2 * rows + tile // cols) * height, height)
            left = pl.multiple_of(across % 2 * BLK, BLK)
            for number, source in enumerate(sources):

                @pl.when(kind == number)
                def _(source=source):
                    pltpu.make_async_copy(
                        source.at[row], target.at[pl.ds(top, height), pl.ds(left, BLK)], done.at[place]
                    ).start()

            return carry

        lax.fori_loop(0, rows * cols, one, 0)
        start += rows * cols
    for place, target in enumerate(targets):
        pltpu.make_async_copy(target, target, done.at[place]).wait()


def gather_strips(sources, meta, grids):
    anywhere = pl.BlockSpec(memory_space=pl.ANY)
    height = sources[0].shape[1]
    out_shape = [
        jax.ShapeDtypeStruct((cols // 2 * rows * height, 2 * BLK), jnp.bfloat16) for rows, cols in grids
    ]
    return pl.pallas_call(
        functools.partial(gather_kernel, grids),
        out_shape=out_shape,
        grid_spec=pltpu.PrefetchScalarGridSpec(
            num_scalar_prefetch=1,
            grid=(1,),
            in_specs=[anywhere] * len(sources),
            out_specs=[pl.BlockSpec(shape.shape, lambda i, *_: (0, 0)) for shape in out_shape],
            scratch_shapes=[pltpu.SemaphoreType.DMA((len(grids),))],
        ),
        compiler_params=pltpu.CompilerParams(vmem_limit_bytes=32 * 2**20),
        cost_estimate=pl.CostEstimate(
            flops=0, bytes_accessed=sum(4 * shape.size for shape in out_shape), transcendentals=0
        ),
    )(meta, *sources)


def place_kernel(entries, rows, cols, meta, low, high, out_ref, done):
    out_ref[...] = jnp.zeros_like(out_ref)
    height = low.shape[1]

    def copies(tile):
        entry, rest = tile // (rows * cols), tile % (rows * cols)
        top = rest // cols * (2 * height)
        left = pl.multiple_of(rest % cols * BLK, BLK)
        return [
            pltpu.make_async_copy(
                half.at[meta[1, tile]],
                out_ref.at[entry, pl.ds(pl.multiple_of(top + part * height, height), height), pl.ds(left, BLK)],
                done.at[part],
            )
            for part, half in enumerate((low, high))
        ]

    def begin(tile, carry):
        @pl.when(meta[0, tile] == 1)
        def _():
            for copy in copies(tile):
                copy.start()

        return carry

    def finish(tile, carry):
        @pl.when(meta[0, tile] == 1)
        def _():
            for copy in copies(tile):
                copy.wait()

        return carry

    lax.fori_loop(0, entries * rows * cols, begin, 0)
    lax.fori_loop(0, entries * rows * cols, finish, 0)


def place_tiles(low, high, meta, entries, rows, cols):
    shape = (entries, rows * BLK, cols * BLK)
    anywhere = pl.BlockSpec(memory_space=pl.ANY)
    return pl.pallas_call(
        functools.partial(place_kernel, entries, rows, cols),
        out_shape=jax.ShapeDtypeStruct(shape, jnp.bfloat16),
        grid_spec=pltpu.PrefetchScalarGridSpec(
            num_scalar_prefetch=1,
            grid=(1,),
            in_specs=[anywhere, anywhere],
            out_specs=pl.BlockSpec(shape, lambda i, *_: (0, 0, 0)),
            scratch_shapes=[pltpu.SemaphoreType.DMA((2,))],
        ),
        compiler_params=pltpu.CompilerParams(vmem_limit_bytes=32 * 2**20),
        cost_estimate=pl.CostEstimate(
            flops=0, bytes_accessed=4 * entries * rows * cols * BLK * BLK, transcendentals=0
        ),
    )(meta, low, high)


def half_turn(values):
    lane = lax.broadcasted_iota(jnp.int32, values.shape, 1)
    lanes = values.shape[1]
    first = lane % HD < HD // 2
    return first, jnp.where(
        first, pltpu.roll(values, lanes - HD // 2, 1), pltpu.roll(values, HD // 2, 1)
    )


def strip_copies(early, late, target, done):
    return [
        pltpu.make_async_copy(half, target.at[:, :, number], done.at[number])
        for number, half in enumerate((early, late))
    ]


def forward_kernel(x_ref, early, late, gate_ref, up_ref, act_ref, weights, done):
    step, steps = pl.program_id(0), pl.num_programs(0)
    slot = step % 2
    width = weights.shape[-1]

    def copies(number, at_step, at_slot):
        strip = number * steps + at_step
        return strip_copies(
            early.at[:, strip], late.at[:, strip], weights.at[number, at_slot], done.at[number, at_slot]
        )

    def fetch(at_step, at_slot):
        for number in range(2):
            for copy in copies(number, at_step, at_slot):
                copy.start()

    @pl.when(step == 0)
    def _():
        fetch(0, 0)

    @pl.when(step + 1 < steps)
    def _():
        fetch(step + 1, 1 - slot)

    for number in range(2):
        for copy in copies(number, step, slot):
            copy.wait()
    gate_weight, up_weight = (weights[number, slot].reshape(-1, width) for number in range(2))
    chunk = min(2 * BLK, x_ref.shape[0])
    for first in range(0, x_ref.shape[0], chunk):
        rows = slice(first, first + chunk)
        gate = jnp.dot(x_ref[rows], gate_weight, preferred_element_type=jnp.float32)
        up = jnp.dot(x_ref[rows], up_weight, preferred_element_type=jnp.float32)
        gate_ref[rows] = gate.astype(jnp.bfloat16)
        up_ref[rows] = up.astype(jnp.bfloat16)
        act_ref[rows] = (gate * jax.nn.sigmoid(gate) * up).astype(jnp.bfloat16)


def forward_products(rows, early, late, columns):
    tokens, depth = rows.shape
    bands, _, tiles, half, width = early.shape
    block = pl.BlockSpec((tokens, width), lambda n: (0, n))
    anywhere = pl.BlockSpec(memory_space=pl.ANY)
    return pl.pallas_call(
        forward_kernel,
        out_shape=[jax.ShapeDtypeStruct((tokens, columns), jnp.bfloat16)] * 3,
        grid=(columns // width,),
        in_specs=[pl.BlockSpec(rows.shape, lambda n: (0, 0)), anywhere, anywhere],
        out_specs=[block] * 3,
        scratch_shapes=[
            pltpu.VMEM((2, 2, bands, tiles, 2, half, width), jnp.bfloat16),
            pltpu.SemaphoreType.DMA((2, 2, 2)),
        ],
        compiler_params=pltpu.CompilerParams(vmem_limit_bytes=48 * 2**20),
        cost_estimate=pl.CostEstimate(
            flops=tokens * depth * columns // 8, bytes_accessed=2 * rows.size, transcendentals=0
        ),
    )(rows, early, late)


def backward_kernel(top_ref, gate_ref, up_ref, act_ref, early, late, late_down, *refs):
    dgate_ref, dup_ref = refs[:2]
    pieces, branch_pieces = refs[2:6], refs[6:10]
    weights, downs, total, branch, done, down_done = refs[10:]
    step, steps = pl.program_id(0), pl.num_programs(0)
    slot = step % 2
    strips, width = downs.shape[1], downs.shape[-1]

    def down_copies(at_step, at_slot):
        return strip_copies(
            early.at[at_step, pl.ds(2 * steps, strips)],
            late_down.at[at_step],
            downs.at[at_slot],
            down_done.at[at_slot],
        )

    def copies(number, at_step, at_slot):
        strip = number * steps + at_step
        return strip_copies(
            early.at[:, strip], late.at[:, strip], weights.at[number, at_slot], done.at[number, at_slot]
        )

    def fetch(at_step, at_slot):
        for copy in down_copies(at_step, at_slot):
            copy.start()
        for number in range(2):
            for copy in copies(number, at_step, at_slot):
                copy.start()

    @pl.when(step == 0)
    def _():
        fetch(0, 0)
        total[...] = jnp.zeros_like(total)
        branch[...] = jnp.zeros_like(branch)

    @pl.when(step + 1 < steps)
    def _():
        fetch(step + 1, 1 - slot)

    for copy in down_copies(step, slot):
        copy.wait()
    for number in range(2):
        for copy in copies(number, step, slot):
            copy.wait()
    gate_weight, up_weight = (weights[number, slot].reshape(-1, width) for number in range(2))
    chunk = min(2 * BLK, top_ref.shape[0])
    for first in range(0, top_ref.shape[0], chunk):
        rows = slice(first, first + chunk)
        grad_act = 0.0
        for strip in range(strips):
            lanes = slice(strip * width, (strip + 1) * width)
            down = downs[slot, strip].reshape(-1, width)
            grad_act = grad_act + over_last(top_ref[rows, lanes], down)
            branch[rows, lanes] += jnp.dot(act_ref[rows], down, preferred_element_type=jnp.float32)
        gate = gate_ref[rows].astype(jnp.float32)
        up = up_ref[rows].astype(jnp.float32)
        sigmoid_gate = jax.nn.sigmoid(gate)
        grad_gate = grad_act * up * sigmoid_gate * (1.0 + gate * (1.0 - sigmoid_gate))
        grad_gate = grad_gate.astype(jnp.bfloat16)
        grad_up = (grad_act * (gate * sigmoid_gate)).astype(jnp.bfloat16)
        dgate_ref[rows] = grad_gate
        dup_ref[rows] = grad_up
        total[rows] += over_last(grad_gate, gate_weight) + over_last(grad_up, up_weight)

    @pl.when(step == steps - 1)
    def _():
        rows = total.shape[0] // 4
        for entry in range(4):
            part = slice(entry * rows, (entry + 1) * rows)
            write_pieces(entry, slice(0, rows), total[part], pieces)
            write_pieces(entry, slice(0, rows), branch[part], branch_pieces)


def backward_products(top, gate, up, act, early, late, late_down):
    tokens, depth = top.shape
    columns = gate.shape[1]
    bands, _, tiles, half, width = early.shape
    strips = late_down.shape[1]
    block = pl.BlockSpec((tokens, width), lambda n: (0, n))
    anywhere = pl.BlockSpec(memory_space=pl.ANY)
    piece = jax.ShapeDtypeStruct((2, tokens // 4, depth // 2), jnp.bfloat16)
    grads = jax.ShapeDtypeStruct((tokens, columns), jnp.bfloat16)
    outs = pl.pallas_call(
        backward_kernel,
        out_shape=[grads] * 2 + [piece] * 8,
        grid=(columns // width,),
        in_specs=[pl.BlockSpec(top.shape, lambda n: (0, 0))] + [block] * 3 + [anywhere] * 3,
        out_specs=[block] * 2 + [pl.BlockSpec(piece.shape, lambda n: (0, 0, 0))] * 8,
        scratch_shapes=[
            pltpu.VMEM((2, 2, bands, tiles, 2, half, width), jnp.bfloat16),
            pltpu.VMEM((2, strips, tiles, 2, half, width), jnp.bfloat16),
            pltpu.VMEM((tokens, depth), jnp.float32),
            pltpu.VMEM((tokens, depth), jnp.float32),
            pltpu.SemaphoreType.DMA((2, 2, 2)),
            pltpu.SemaphoreType.DMA((2, 2)),
        ],
        compiler_params=pltpu.CompilerParams(vmem_limit_bytes=60 * 2**20),
        cost_estimate=pl.CostEstimate(
            flops=8 * tokens * depth * columns, bytes_accessed=8 * columns * depth, transcendentals=0
        ),
    )(top, gate, up, act, early, late, late_down)
    return outs[0], outs[1], outs[2:6], outs[6:10]


def rope_kernel(q_width, kv_width, x_ref, cos_ref, sin_ref, *outs):
    width = x_ref.shape[-1]
    for start in range(0, width, BLK):
        values = x_ref[0, :, start : start + BLK]
        first, turned = half_turn(values)
        sines = sin_ref[0]
        turned_rows = values * cos_ref[0] + turned * jnp.where(first, -sines, sines)
        if start + BLK > q_width + kv_width:
            column = lax.broadcasted_iota(jnp.int32, values.shape, 1) + start
            turned_rows = jnp.where(column >= q_width + kv_width, values, turned_rows)
        if start < q_width:
            outs[0][0, :, start : start + BLK] = (turned_rows * HD ** (-0.5)).astype(jnp.bfloat16)
        else:
            outs[-1][0, :, start - q_width : start - q_width + BLK] = turned_rows.astype(jnp.bfloat16)


def rope_rows(inner, rows, row_block, q_width, kv_width, cosines, sines, with_queries=True):
    seqs, _, width = inner.shape
    shared = cosines.shape[0] == 1
    table = pl.BlockSpec((1, rows, BLK), lambda s: (0 if shared else s, 0, 0))
    widths = [q_width, 2 * kv_width]
    column_block = 0
    if not with_queries:
        width, column_block = 2 * kv_width, q_width // (2 * kv_width)
        widths, q_width = widths[1:], 0
    return pl.pallas_call(
        functools.partial(rope_kernel, q_width, kv_width),
        out_shape=[jax.ShapeDtypeStruct((seqs, rows, w), jnp.bfloat16) for w in widths],
        grid=(seqs,),
        in_specs=[pl.BlockSpec((1, rows, width), lambda s: (s, row_block, column_block)), table, table],
        out_specs=[pl.BlockSpec((1, rows, w), lambda s: (s, 0, 0)) for w in widths],
        cost_estimate=pl.CostEstimate(
            flops=6 * seqs * rows * width, bytes_accessed=6 * seqs * rows * width, transcendentals=0
        ),
    )(inner, cosines, sines)


def fill_bias(band_ref, gpos_ref, bias_ref, rows, window_len):
    band = band_ref[0]

    @pl.when(pl.program_id(0) == 0)
    def _():
        key = lax.broadcasted_iota(jnp.int32, (window_len, rows), 0) + (
            band * rows - (window_len - rows)
        )
        query = lax.broadcasted_iota(jnp.int32, (window_len, rows), 1) + band * rows
        inside = (key > query - WINDOW) & (key <= query) & (key >= 0)
        bias_ref[:window_len] = jnp.where(inside, 0.0, masked_value)

    glob_total = gpos_ref.shape[1]
    query = lax.broadcasted_iota(jnp.int32, (glob_total, rows), 1) + (band * rows - WINDOW)
    spot = jnp.broadcast_to(gpos_ref[0][:, :1], (glob_total, rows))
    bias_ref[window_len:] = jnp.where(spot <= query.astype(jnp.float32), 0.0, masked_value)


def over_last(left, right):
    return lax.dot_general(left, right, (((1,), (1,)), ((), ())), preferred_element_type=jnp.float32)


def over_first(left, right):
    return lax.dot_general(left, right, (((0,), (0,)), ((), ())), preferred_element_type=jnp.float32)


def attend_kernel(block_total, band_ref, gpos_ref, q_ref, *refs):
    blocks, (out_ref, lse_ref, bias_ref) = refs[:block_total], refs[block_total:]
    rows, q_width = q_ref.shape[1:]
    kv_width = blocks[0].shape[2] // 2
    heads, group = q_width // HD, q_width // kv_width
    window_len = rows * (block_total - 1)
    fill_bias(band_ref, gpos_ref, bias_ref, rows, window_len)
    starts = [rows * number for number in range(block_total)]
    pending = []
    for head in range(heads):
        left = head // group * HD
        queries = q_ref[0, :, head * HD : (head + 1) * HD]
        scores = [
            over_last(block[0, :, left : left + HD], queries)
            + bias_ref[start : start + block.shape[1]]
            for block, start in zip(blocks, starts)
        ]
        top = functools.reduce(jnp.maximum, [jnp.max(part, 0, keepdims=True) for part in scores])
        total = 0.0
        mixed = 0.0
        for block, part in zip(blocks, scores):
            weights = jnp.exp(part - top)
            total = total + jnp.sum(weights, 0, keepdims=True)
            mixed = mixed + over_first(
                block[0, :, kv_width + left : kv_width + left + HD], weights.astype(jnp.bfloat16)
            )
        lse_ref[0, head : head + 1, :] = top + jnp.log(total)
        pending.append(mixed / total)
        if len(pending) * HD == BLK or head == heads - 1:
            stop = (head + 1) * HD
            both = jnp.concatenate(pending, 0).T
            out_ref[0, :, stop - both.shape[1] : stop] = both.astype(jnp.bfloat16)
            pending = []


def attend(band, gpos, queries, blocks):
    seqs, rows, q_width = queries.shape
    heads = q_width // HD
    key_total = sum(block.shape[1] for block in blocks)

    def whole(array):
        return pl.BlockSpec((1,) + array.shape[1:], lambda s, *_: (s, 0, 0))

    out_shape = [
        jax.ShapeDtypeStruct((seqs, rows, q_width), jnp.bfloat16),
        jax.ShapeDtypeStruct((seqs, heads, rows), jnp.float32),
    ]
    return pl.pallas_call(
        functools.partial(attend_kernel, len(blocks)),
        out_shape=out_shape,
        grid_spec=pltpu.PrefetchScalarGridSpec(
            num_scalar_prefetch=1,
            grid=(seqs,),
            in_specs=[whole(array) for array in (gpos, queries, *blocks)],
            out_specs=[whole(array) for array in out_shape],
            scratch_shapes=[pltpu.VMEM((key_total, rows), jnp.float32)],
        ),
        compiler_params=pltpu.CompilerParams(vmem_limit_bytes=48 * 2**20),
        cost_estimate=pl.CostEstimate(
            flops=16 * seqs * heads * rows * key_total * HD,
            bytes_accessed=4 * queries.size,
            transcendentals=seqs * heads * rows * key_total,
        ),
    )(band, gpos, queries, *blocks)


def attend_back_kernel(block_total, band_ref, gpos_ref, cos_ref, sin_ref, q_ref, grad_ref, lse_ref, *refs):
    blocks = refs[:block_total]
    dq_ref = refs[block_total]
    out_refs = refs[block_total + 1 : 2 * block_total + 1]
    bias_ref = refs[-1]
    rows, q_width = q_ref.shape[1:]
    kv_width = blocks[0].shape[2] // 2
    heads, group = q_width // HD, q_width // kv_width
    window_len = rows * (block_total - 1)
    fill_bias(band_ref, gpos_ref, bias_ref, rows, window_len)
    starts = [rows * number for number in range(block_total)]
    pending = []
    for kv_head in range(kv_width // HD):
        left = kv_head * HD
        key_sums = [0.0] * block_total
        value_sums = [0.0] * block_total
        for head in range(kv_head * group, (kv_head + 1) * group):
            queries = q_ref[0, :, head * HD : (head + 1) * HD]
            grads = grad_ref[0, :, head * HD : (head + 1) * HD]
            lse = lse_ref[0, head : head + 1, :]
            soft, soft_grads = [], []
            inner = 0.0
            for number, (block, start) in enumerate(zip(blocks, starts)):
                part = over_last(block[0, :, left : left + HD], queries)
                part = jnp.exp(part + bias_ref[start : start + block.shape[1]] - lse)
                slope = over_last(block[0, :, kv_width + left : kv_width + left + HD], grads)
                inner = inner + jnp.sum(part * slope, 0, keepdims=True)
                soft.append(part)
                soft_grads.append(slope)
            turned = 0.0
            for number, block in enumerate(blocks):
                score_grads = (soft[number] * (soft_grads[number] - inner)).astype(jnp.bfloat16)
                value_sums[number] = value_sums[number] + jnp.dot(
                    soft[number].astype(jnp.bfloat16), grads, preferred_element_type=jnp.float32
                )
                key_sums[number] = key_sums[number] + jnp.dot(
                    score_grads, queries, preferred_element_type=jnp.float32
                )
                turned = turned + over_first(block[0, :, left : left + HD], score_grads)
            pending.append(turned)
            if len(pending) * HD == BLK or head == heads - 1:
                stop = (head + 1) * HD
                both = jnp.concatenate(pending, 0).T * HD ** (-0.5)
                pending = []
                first, other = half_turn(both * sin_ref[0])
                both = both * cos_ref[0] + jnp.where(first, other, -other)
                dq_ref[0, :, stop - both.shape[1] : stop] = both.astype(jnp.bfloat16)
        for number, out_ref in enumerate(out_refs):
            out_ref[0, :, left : left + HD] = key_sums[number].astype(out_ref.dtype)
            out_ref[0, :, kv_width + left : kv_width + left + HD] = value_sums[number].astype(
                out_ref.dtype
            )


def attend_back(band, gpos, cosines, sines, queries, grads, lse, blocks):
    seqs, rows, q_width = queries.shape
    heads = q_width // HD
    key_total = sum(block.shape[1] for block in blocks)

    def whole(array):
        return pl.BlockSpec((1,) + array.shape[1:], lambda s, *_: (s, 0, 0))

    table = pl.BlockSpec((1, rows, BLK), lambda s, *_: (0, 0, 0))
    out_shape = [jax.ShapeDtypeStruct(queries.shape, jnp.bfloat16)]
    for number, block in enumerate(blocks):
        own = number == len(blocks) - 2
        out_shape.append(jax.ShapeDtypeStruct(block.shape, jnp.float32 if own else jnp.bfloat16))
    return pl.pallas_call(
        functools.partial(attend_back_kernel, len(blocks)),
        out_shape=out_shape,
        grid_spec=pltpu.PrefetchScalarGridSpec(
            num_scalar_prefetch=1,
            grid=(seqs,),
            in_specs=[whole(gpos), table, table]
            + [whole(array) for array in (queries, grads, lse, *blocks)],
            out_specs=[whole(array) for array in out_shape],
            scratch_shapes=[pltpu.VMEM((key_total, rows), jnp.float32)],
        ),
        compiler_params=pltpu.CompilerParams(vmem_limit_bytes=48 * 2**20),
        cost_estimate=pl.CostEstimate(
            flops=40 * seqs * heads * rows * key_total * HD,
            bytes_accessed=8 * queries.size,
            transcendentals=seqs * heads * rows * key_total,
        ),
    )(band, gpos, cosines, sines, queries, grads, lse, *blocks)


def join_kernel(q_width, kv_width, dq_ref, own_ref, pick_ref, glob_ref, cos_ref, sin_ref, *refs):
    back_refs, out_ref = refs[:-1], refs[-1]
    out_ref[0, :, :q_width] = dq_ref[0]
    picked = lax.dot_general(
        pick_ref[0].astype(jnp.float32),
        glob_ref[0],
        (((0,), (0,)), ((), ())),
        precision=lax.Precision.HIGHEST,
        preferred_element_type=jnp.float32,
    )
    for start in range(0, 2 * kv_width, BLK):
        lanes = slice(start, start + BLK)
        total = own_ref[0, :, lanes] + picked[:, lanes]
        for back_ref in back_refs:
            total = total + back_ref[0, :, lanes].astype(jnp.float32)
        first, other = half_turn(total * sin_ref[0])
        turned = total * cos_ref[0] + jnp.where(first, other, -other)
        column = lax.broadcasted_iota(jnp.int32, total.shape, 1) + start
        turned = jnp.where(column >= kv_width, total, turned)
        out_ref[0, :, q_width + start : q_width + start + BLK] = turned.astype(jnp.bfloat16)


def join_grads(dq, own, picks, globs, cosines, sines, backs):
    seqs, rows, q_width = dq.shape
    kv_width = own.shape[2] // 2

    def whole(array):
        return pl.BlockSpec((1,) + array.shape[1:], lambda s: (s, 0, 0))

    table = pl.BlockSpec((1, rows, BLK), lambda s: (0, 0, 0))
    out_shape = jax.ShapeDtypeStruct((seqs, rows, q_width + 2 * kv_width), jnp.bfloat16)
    return pl.pallas_call(
        functools.partial(join_kernel, q_width, kv_width),
        out_shape=out_shape,
        grid=(seqs,),
        in_specs=[whole(dq), whole(own), whole(picks), whole(globs), table, table]
        + [whole(back) for back in backs],
        out_specs=whole(out_shape),
        cost_estimate=pl.CostEstimate(
            flops=20 * own.size, bytes_accessed=4 * dq.size + 12 * own.size, transcendentals=0
        ),
    )(dq, own, picks, globs, cosines, sines, *backs)


def adam_kernel(batch, meta, rates, *refs):
    master_ref, first_ref, second_ref, left_ref, right_ref = refs[:5]
    sources = refs[5:-6]
    new_first_ref, new_second_ref, new_master_ref, copy_ref, tiles, arrived = refs[-6:]
    step, steps = pl.program_id(0), pl.num_programs(0)
    slot = step % 2

    def fetch(at_step, at_slot):
        for place in range(batch):
            tile = at_step * batch + place
            for number, source in enumerate(sources):

                @pl.when(meta[0, tile] == number)
                def _(source=source, tile=tile, place=place):
                    top = pl.multiple_of(meta[2, tile], BLK)
                    left = pl.multiple_of(meta[3, tile], BLK)
                    pltpu.make_async_copy(
                        source.at[meta[1, tile], pl.ds(top, BLK), pl.ds(left, BLK)],
                        tiles.at[at_slot, place],
                        arrived.at[at_slot],
                    ).start()

    @pl.when(step == 0)
    def _():
        fetch(0, 0)

    @pl.when(step + 1 < steps)
    def _():
        fetch(step + 1, 1 - slot)

    pltpu.make_async_copy(tiles.at[slot], tiles.at[slot], arrived.at[slot]).wait()
    places = range(batch)
    lefts = [left_ref[place].astype(jnp.bfloat16) for place in places]
    rights = [right_ref[place].astype(jnp.bfloat16) for place in places]
    turned = [over_first(lefts[place], tiles[slot, place]).astype(jnp.bfloat16) for place in places]
    rotated = [
        jnp.dot(turned[place], rights[place], preferred_element_type=jnp.float32) for place in places
    ]
    directions = []
    for place in places:
        new_first = beta_one * first_ref[place] + (1.0 - beta_one) * rotated[place]
        new_second = beta_two * second_ref[place] + (1.0 - beta_two) * rotated[place] * rotated[place]
        direction = (new_first * (1.0 / (1.0 - beta_one**STEP))) / (
            jnp.sqrt(new_second * (1.0 / (1.0 - beta_two**STEP))) + adam_eps
        )
        new_first_ref[place] = new_first
        new_second_ref[place] = new_second
        directions.append(direction.astype(jnp.bfloat16))
    updates = [
        jnp.dot(lefts[place], directions[place], preferred_element_type=jnp.float32) for place in places
    ]
    updates = [over_last(updates[place].astype(jnp.bfloat16), rights[place]) for place in places]
    for place in places:
        old = master_ref[place]
        new_master = old - rates[step * batch + place] * (updates[place] + weight_decay * old)
        new_master_ref[place] = new_master
        copy_ref[place] = new_master.astype(jnp.bfloat16)


def adam(meta, rates, state, sources):
    count = state[0].shape[0]
    batch = max(size for size in range(1, 33) if count % size == 0)
    block = pl.BlockSpec((batch, BLK, BLK), lambda s, *_: (s, 0, 0))
    anywhere = pl.BlockSpec(memory_space=pl.ANY)
    shape = (count, BLK, BLK)
    return pl.pallas_call(
        functools.partial(adam_kernel, batch),
        out_shape=[jax.ShapeDtypeStruct(shape, jnp.float32)] * 3
        + [jax.ShapeDtypeStruct(shape, jnp.bfloat16)],
        grid_spec=pltpu.PrefetchScalarGridSpec(
            num_scalar_prefetch=2,
            grid=(count // batch,),
            in_specs=[block] * 5 + [anywhere] * len(sources),
            out_specs=[block] * 4,
            scratch_shapes=[
                pltpu.VMEM((2, batch, BLK, BLK), jnp.bfloat16),
                pltpu.SemaphoreType.DMA((2,)),
            ],
        ),
        compiler_params=pltpu.CompilerParams(vmem_limit_bytes=56 * 2**20),
        cost_estimate=pl.CostEstimate(
            flops=8 * count * BLK**3, bytes_accessed=36 * count * BLK**2, transcendentals=0
        ),
    )(meta, rates, *state, *sources)


def per_device(
    block_input,
    cotangent,
    glob_select,
    assignment,
    master,
    first_moment,
    second_moment,
    left_basis,
    right_basis,
    gains,
    gain_first,
    gain_second,
):
    band_total = lax.axis_size("fsdp")
    rep_total = lax.axis_size("rep")
    place = lax.axis_index("rep")
    band = lax.axis_index("fsdp")
    heads = H // rep_total
    kv_heads = KVH // rep_total
    q_width = heads * HD
    kv_width = kv_heads * HD
    tok_count = block_input.shape[1]
    own_count = master.shape[1]
    tile_total = own_count * rep_total
    aligned = square() and whole_tiles(band_total, rep_total)
    tile_order = assignment[0]

    residual = block_input[0].astype(jnp.float32)
    grad_top = cotangent[0]
    position = band * tok_count + jnp.arange(tok_count, dtype=jnp.int32)
    cosine_table, sine_table = rope_tables(position)
    wide_cosine = jnp.concatenate([cosine_table, cosine_table], 1)[None]
    wide_sine = jnp.concatenate([sine_table, sine_table], 1)[None]
    scale_one = lax.rsqrt(jnp.mean(residual * residual, -1, keepdims=True) + norm_eps)
    normed_one = (residual * scale_one * gains[0]).astype(jnp.bfloat16)
    pick_rows = glob_select[0]
    glob_total = pick_rows.shape[0]
    selector = pick_rows.astype(jnp.bfloat16)
    glob_pos_part = jnp.sum(pick_rows * position[None, :], 1)
    digits = jnp.concatenate([glob_pos_part // 256, glob_pos_part % 256]).astype(jnp.bfloat16)
    digits = jnp.pad(digits[None], ((0, 7), (0, D - 2 * glob_total)))
    glob_rows = jnp.dot(selector, normed_one, preferred_element_type=jnp.float32).astype(jnp.bfloat16)
    glob_rows = add_all(jnp.concatenate([glob_rows, digits], 0), "fsdp").astype(jnp.bfloat16)
    packed = [normed_one, glob_rows, selector.reshape(-1, D)]
    packed = jnp.concatenate(packed, 0)
    packed = jnp.pad(packed, ((0, -packed.shape[0] % 32), (0, 0)))

    def over_bands(slice_rows):
        return lax.all_gather(slice_rows, "fsdp", axis=0, tiled=True)

    if aligned:
        half = BLK // 2
        low, high = (master[0, :, rows].astype(jnp.bfloat16) for rows in (slice(0, half), slice(half, BLK)))
        layout = slice_layout(band_total, rep_total)
        attn_layout = jnp.asarray(np.concatenate(layout[:4], 2))
        wanted = jnp.take(tile_order, by_place(attn_layout).reshape(-1), mode="clip")
        meta = jnp.stack([wanted // own_count == place, wanted % own_count], 0).astype(jnp.int32)
        attn_part = place_tiles(low, high, meta, *attn_layout.shape)
        attn_part = rep_scatter(attn_part).astype(jnp.bfloat16)
        low, attn_part = lax.optimization_barrier((low, attn_part))
        slots = square_pieces(low)
        packed, attn_part = lax.optimization_barrier((packed, attn_part))
        attn = over_bands(attn_part)
        *slots, attn = lax.optimization_barrier((*slots, attn))
        grids = [lax.dynamic_index_in_dim(jnp.asarray(grid), place, 0, False) for grid in layout]

        def find(wanted):
            wanted = jnp.take(tile_order, jnp.concatenate([grid.reshape(-1) for grid in wanted]), mode="clip")
            entry, row = (wanted // own_count) ^ place, wanted % own_count
            cut = own_count // 2
            high = (entry == 3) & (row >= cut)
            found = jnp.stack([jnp.where(high, 4, entry), jnp.where(high, row - cut, row)], 0)
            return found.astype(jnp.int32)

        all_grid = jnp.concatenate(grids[4:], 1)
        (first_part,) = gather_strips(slots, find([all_grid]), [all_grid.shape])
        packed, first_part = lax.optimization_barrier((packed, first_part))
        early = over_bands(first_part)
    packed_all = rep_gather(packed)
    if aligned:
        packed_all, high = lax.optimization_barrier((packed_all, high))
        later_slots = square_pieces(high)
    normed_one_all = packed_all[:, :tok_count].reshape(-1, D)
    at = tok_count + glob_total
    glob_digits = packed_all[:, at, : 2 * glob_total].astype(jnp.float32)
    glob_place = glob_digits[:, :glob_total] * 256.0 + glob_digits[:, glob_total:]
    at += 8
    selector_all = packed_all[:, at : at + selector.size // D].reshape(rep_total, glob_total, tok_count)

    if aligned:
        in_width = q_width + 2 * kv_width
        w_inner, w_output = attn[:, :in_width], attn[:, in_width:]
    else:
        slots = lax.all_gather(master[0].astype(jnp.bfloat16), "rep", axis=0, tiled=True)
        tiles = jnp.take(slots, tile_order, axis=0, mode="clip")
        slices = cut_slices(band_matrices(tiles, band_total), band_total, rep_total)
        w_inner = over_bands(jnp.concatenate(slices[0:3], 1))
        w_output = over_bands(slices[3])
        w_gate = over_bands(slices[4])
        w_up = over_bands(slices[5])
        w_down = over_bands(slices[6])

    w_output = by_place(w_output.reshape(rep_total, q_width, -1)).reshape(D, -1)

    def mul(rows, weight):
        return jnp.dot(rows, weight, preferred_element_type=jnp.float32)

    def mul_back(rows, weight):
        return lax.dot_general(rows, weight, (((1,), (1,)), ((), ())), preferred_element_type=jnp.float32)

    def weight_grad(rows, grad_rows):
        return lax.dot_general(
            rows, grad_rows, (((0,), (0,)), ((), ())), preferred_element_type=jnp.float32
        ).astype(jnp.bfloat16)

    def own_sum(partial):
        return rep_scatter(partial.astype(jnp.bfloat16).reshape(rep_total, tok_count, D))

    inner_rows = mul(packed_all.reshape(-1, D), w_inner).reshape(rep_total, -1, w_inner.shape[1])
    packed_all, normed_one_all = lax.optimization_barrier((packed_all, normed_one_all))
    queries, own_pairs = rope_rows(inner_rows, tok_count, 0, q_width, kv_width, wide_cosine, wide_sine)
    glob_cosine, glob_sine = rope_tables(glob_place.reshape(-1))
    glob_cosine = jnp.concatenate([glob_cosine, glob_cosine], 1).reshape(rep_total, glob_total, -1)
    glob_sine = jnp.concatenate([glob_sine, glob_sine], 1).reshape(rep_total, glob_total, -1)
    (glob_pairs,) = rope_rows(
        inner_rows, glob_total, tok_count // glob_total, q_width, kv_width, glob_cosine, glob_sine, False
    )
    back_count = (WINDOW + tok_count - 2) // tok_count
    pair_blocks = [shifted(own_pairs, "fsdp", distance) for distance in range(back_count, 0, -1)]
    pair_blocks = pair_blocks + [own_pairs, glob_pairs]
    glob_spots = jnp.broadcast_to(glob_place[:, :, None], (rep_total, glob_total, BLK))
    band_number = band.astype(jnp.int32).reshape(1)
    attended_low, lse = attend(band_number, glob_spots, queries, pair_blocks)
    if aligned:
        *later_slots, attended_low, early = lax.optimization_barrier((*later_slots, attended_low, early))
        last_grid = jnp.concatenate(grids[4:6], 1)
        last_part, down_part = gather_strips(
            later_slots, find([last_grid, grids[6]]), [last_grid.shape, grids[6].shape]
        )

        def by_strips(part):
            gathered = over_bands(part)
            return gathered.reshape(band_total, -1, last_grid.shape[0], half, gathered.shape[-1])

        early = early.reshape(band_total, -1, all_grid.shape[0], half, early.shape[-1])
        late, late_down = by_strips(last_part), by_strips(down_part)
    attended_all = rep_features(attended_low).reshape(-1, D)
    attended_all, grad_top_now = lax.optimization_barrier((attended_all, grad_top))
    grad_top_all = rep_gather(grad_top_now).reshape(-1, D)
    columns = mul(attended_all, w_output).astype(jnp.bfloat16).reshape(rep_total, tok_count, -1)
    branch = by_place(rep_exchange(columns)).transpose(1, 0, 2).reshape(tok_count, D)
    middle = residual + branch.astype(jnp.float32)
    scale_two = lax.rsqrt(jnp.mean(middle * middle, -1, keepdims=True) + norm_eps)
    normed_two = (middle * scale_two * gains[1]).astype(jnp.bfloat16)
    normed_two, grad_top_all = lax.optimization_barrier((normed_two, grad_top_all))
    normed_two_all = rep_gather(normed_two).reshape(-1, D)

    if aligned:
        gate_rows, up_rows, activation = forward_products(normed_two_all, early, late, FF // rep_total)
        g_down = weight_grad(activation, grad_top_all)
        grad_top_all, g_down = lax.optimization_barrier((grad_top_all, g_down))
        grad_gate, grad_up, pieces, branch_pieces = backward_products(
            grad_top_all, gate_rows, up_rows, activation, early, late, late_down
        )
        grad_normed_two = sum_pieces(*pieces)
    else:
        gate_rows = mul(normed_two_all, w_gate)
        up_rows = mul(normed_two_all, w_up)
        sigmoid_gate = jax.nn.sigmoid(gate_rows)
        silu_gate = gate_rows * sigmoid_gate
        activation = (silu_gate * up_rows).astype(jnp.bfloat16)
        g_down = weight_grad(activation, grad_top_all)
        grad_act = mul_back(grad_top_all, w_down)
        grad_gate = (
            grad_act * up_rows * sigmoid_gate * (1.0 + gate_rows * (1.0 - sigmoid_gate))
        ).astype(jnp.bfloat16)
        grad_up = (grad_act * silu_gate).astype(jnp.bfloat16)
        grad_normed_two = own_sum(mul_back(grad_gate, w_gate) + mul_back(grad_up, w_up))
        branch_pieces = (mul(activation, w_down),)
    g_gate = weight_grad(normed_two_all, grad_gate)
    g_up = weight_grad(normed_two_all, grad_up)
    grad_normed_two, g_gate, g_up = lax.optimization_barrier((grad_normed_two, g_gate, g_up))

    def over_tokens(partial):
        return lax.psum_scatter(partial, "fsdp", scatter_dimension=0, tiled=True)

    s_down = over_tokens(g_down)
    s_gate = over_tokens(g_gate)
    s_up = over_tokens(g_up)

    grad_middle = grad_top.astype(jnp.float32) + norm_back(middle, scale_two, gains[1], grad_normed_two)
    grad_parts = grad_middle.astype(jnp.bfloat16).reshape(tok_count, rep_total, -1).transpose(1, 0, 2)
    grad_columns = rep_exchange(by_place(grad_parts)).reshape(rep_total * tok_count, -1)
    grad_attended = rep_features_sum(
        grad_columns.reshape(rep_total, tok_count, -1), w_output
    ).astype(jnp.bfloat16)
    g_output = weight_grad(attended_all, grad_columns)
    g_output = by_place(g_output.reshape(rep_total, q_width, -1)).reshape(D, -1)
    grad_attended, s_down, *branch_pieces = lax.optimization_barrier((grad_attended, s_down, *branch_pieces))
    s_down = rep_gather(s_down)
    block_out = middle + (sum_pieces(*branch_pieces) if aligned else own_sum(branch_pieces[0]))
    grad_queries, *grad_blocks = attend_back(
        band_number, glob_spots, wide_cosine, wide_sine, queries, grad_attended, lse, pair_blocks
    )
    returned = [
        shifted(grad_blocks[back_count - distance], "fsdp", -distance)
        for distance in range(1, back_count + 1)
    ]
    glob_grads = add_all(grad_blocks[-1], "fsdp")
    grad_inner = join_grads(
        grad_queries, grad_blocks[-2], selector_all, glob_grads, wide_cosine, wide_sine, returned
    ).reshape(-1, q_width + 2 * kv_width)
    g_inner, s_down, block_out = lax.optimization_barrier(
        (weight_grad(normed_one_all, grad_inner), s_down, block_out)
    )
    s_gate = rep_gather(s_gate)
    g_attn, s_gate, s_up = lax.optimization_barrier(
        (jnp.concatenate([g_inner, g_output], 1), s_gate, s_up)
    )
    s_up = rep_gather(s_up)
    s_attn = over_tokens(g_attn)
    grad_normed_one = own_sum(mul_back(grad_inner, w_inner))
    grad_input = grad_middle + norm_back(residual, scale_one, gains[0], grad_normed_one)

    gain_terms = jnp.stack(
        [
            jnp.sum(grad_normed_one * residual * scale_one, 0),
            jnp.sum(grad_normed_two * middle * scale_two, 0),
        ]
    )
    square_terms = jnp.stack(
        [jnp.sum(residual * residual), jnp.sum(middle * middle), jnp.sum(block_out * block_out)]
    )
    sums = jnp.concatenate([gain_terms.reshape(-1), square_terms])

    slot_ids = jnp.arange(tile_total, dtype=jnp.int32)
    inverse = jnp.sum(jnp.where(tile_order[None, :] == slot_ids[:, None], slot_ids[None, :], 0), 1)
    own_slots = place * own_count + jnp.arange(own_count, dtype=jnp.int32)
    owned_tiles = jnp.take(inverse, own_slots, mode="clip")
    if aligned:
        sources = [rep_gather(s_attn), s_gate, s_up, s_down]
        where = np.zeros((4, rep_total, tile_total), np.int32)
        first_col = 0
        for kind, grid in enumerate(layout):
            rows, cols = grid.shape[1:]
            first_col = 0 if kind >= 4 else first_col
            for there in range(rep_total):
                numbers = grid[there].reshape(-1)
                at = np.arange(rows * cols)
                where[0, :, numbers] = max(kind - 3, 0)
                where[2, :, numbers] = (at // cols * BLK)[:, None]
                where[3, :, numbers] = (at % cols * BLK + first_col)[:, None]
                for here in range(rep_total):
                    where[1, here, numbers] = here ^ there
            first_col += cols * BLK
        tile_spots = lax.dynamic_index_in_dim(jnp.asarray(where), place, 1, False)
        meta = jnp.take(tile_spots, owned_tiles, axis=1, mode="clip")
    else:
        splits = [0, q_width, q_width + kv_width, q_width + 2 * kv_width, s_attn.shape[1]]
        stacks = [rep_gather(s_attn[:, low:high]) for low, high in zip(splits, splits[1:])]
        stacks += [s_gate, s_up, s_down]
        sources = [band_tiles(join_slices(stacks, band_total, rep_total))]
        meta = jnp.stack([0 * owned_tiles, owned_tiles, 0 * owned_tiles, 0 * owned_tiles], 0)
    slot_rates = jnp.take(kind_rates(band_total), owned_tiles, mode="clip")
    new_first, new_second, new_master, master_copy = adam(
        meta,
        slot_rates,
        (master[0], first_moment[0], second_moment[0], left_basis[0], right_basis[0]),
        sources,
    )
    sums = add_all(add_all(sums, "rep"), "fsdp")
    gain_grad, square_total = sums[: 2 * D].reshape(2, D), sums[2 * D :]
    new_gain_first = beta_one * gain_first + (1.0 - beta_one) * gain_grad
    new_gain_second = beta_two * gain_second + (1.0 - beta_two) * gain_grad * gain_grad
    gain_step = (
        new_gain_first
        / (1.0 - beta_one**STEP)
        / (jnp.sqrt(new_gain_second / (1.0 - beta_two**STEP)) + adam_eps)
    )
    new_gains = gains - gain_rate * gain_step
    rms_stats = jnp.sqrt(square_total / (rep_total * band_total * tok_count * D))
    return (
        block_out[None],
        grad_input[None],
        new_first[None],
        new_second[None],
        new_master[None],
        master_copy[None],
        new_gain_first,
        new_gain_second,
        new_gains,
        rms_stats,
    )


def solution(mesh):
    in_specs = (
        P("rep", "fsdp", None),
        P("rep", "fsdp", None),
        P("rep", None, "fsdp"),
        P("fsdp", None),
        P("fsdp", "rep", None, None),
        P("fsdp", "rep", None, None),
        P("fsdp", "rep", None, None),
        P("fsdp", "rep", None, None),
        P("fsdp", "rep", None, None),
        P(),
        P(),
        P(),
    )
    out_specs = (
        P("rep", "fsdp", None),
        P("rep", "fsdp", None),
        P("fsdp", "rep", None, None),
        P("fsdp", "rep", None, None),
        P("fsdp", "rep", None, None),
        P("fsdp", "rep", None, None),
        P(),
        P(),
        P(),
        P(),
    )
    return jax.shard_map(
        per_device, mesh=mesh, in_specs=in_specs, out_specs=out_specs, check_vma=False
    )
```

```python
import functools

import jax
import jax.numpy as jnp
import numpy as np
from jax import lax
from jax.experimental import pallas as pl
from jax.experimental.layout import Layout, with_layout_constraint
from jax.experimental.pallas import tpu as pltpu
from jax.sharding import PartitionSpec as P

D = 2048
H = 32
KVH = 8
HD = 64
FF = 8192
WINDOW = 512
BLK = 128
STEP = 10


norm_eps = 1e-05
rope_theta = 500000.0
beta_one = 0.5
beta_two = 0.5
adam_eps = 1e-08
weight_decay = 0.1
gain_rate = 0.5
masked_value = -1e30


def matrix_shapes():
    kv_width = KVH * HD
    return [(D, D), (D, kv_width), (D, kv_width), (D, D), (D, FF), (D, FF), (FF, D)]


def kind_rates(band_total):
    rate_list = [
        D ** (-0.5),
        D ** (-0.5),
        D ** (-0.5),
        (D * 8 // WINDOW) ** (-0.5),
        D ** (-0.5),
        D ** (-0.5),
        FF ** (-0.5),
    ]
    pieces = []
    for (row_total, col_total), rate_value in zip(matrix_shapes(), rate_list):
        tile_count = row_total // band_total // BLK * (col_total // BLK)
        pieces.append(jnp.full((tile_count,), rate_value, jnp.float32))
    return jnp.concatenate(pieces)


def band_matrices(tiles, band_total):
    matrices = []
    offset = 0
    for row_total, col_total in matrix_shapes():
        band_rows = row_total // band_total
        tile_count = band_rows // BLK * (col_total // BLK)
        segment = tiles[offset : offset + tile_count].reshape(
            band_rows // BLK, col_total // BLK, BLK, BLK
        )
        matrices.append(segment.transpose(0, 2, 1, 3).reshape(band_rows, col_total))
        offset += tile_count
    return matrices


def band_tiles(matrices):
    pieces = []
    for matrix in matrices:
        row_count, col_count = matrix.shape
        segment = matrix.reshape(row_count // BLK, BLK, col_count // BLK, BLK).transpose(0, 2, 1, 3)
        pieces.append(segment.reshape(-1, BLK, BLK))
    return jnp.concatenate(pieces, 0)


def rope_tables(position):
    halves = jnp.arange(HD // 2, dtype=jnp.float32) * (2.0 / HD)
    frequency = rope_theta ** (-halves)
    angles = position.astype(jnp.float32)[:, None] * frequency[None, :]
    angles = jnp.concatenate([angles, angles], 1)
    return (jnp.cos(angles), jnp.sin(angles))


def rotate(vectors, cosine_table, sine_table):
    half_width = vectors.shape[-1] // 2
    turned = jnp.concatenate([-vectors[..., half_width:], vectors[..., :half_width]], -1)
    return vectors * cosine_table[:, None, :] + turned * sine_table[:, None, :]


def rotate_back(grad_rows, cosine_table, sine_table):
    half_width = grad_rows.shape[-1] // 2
    scaled = grad_rows * sine_table[:, None, :]
    turned = jnp.concatenate([scaled[..., half_width:], -scaled[..., :half_width]], -1)
    return grad_rows * cosine_table[:, None, :] + turned


def norm_back(values, row_scale, gain_row, grad_rows):
    weighted = grad_rows * gain_row
    return row_scale * weighted - values * row_scale**3 * jnp.mean(
        weighted * values, -1, keepdims=True
    )


def to_rep(block, distance):
    route = [(i, i ^ distance) for i in range(lax.axis_size("rep"))]
    return lax.ppermute(block, "rep", route)


def square():
    return lax.axis_size("rep") == 4


def gather_first(block):
    if not square():
        return (lax.all_gather(block, "rep", axis=0),)
    return block, to_rep(block, 1), to_rep(block, 2)


def gather_second(first):
    if not square():
        return first
    block, near, far = first
    cut = block.shape[0] // 2
    return block, near, far, to_rep(near[:cut], 2), to_rep(far[cut:], 1)


def gather_join(pieces):
    if not square():
        return pieces[0]
    return jnp.concatenate(pieces, 0).reshape((4,) + pieces[0].shape)


def square_pieces(block):
    return gather_second(gather_first(block))


def rep_gather(block):
    return gather_join(gather_second(gather_first(block)))


def after(values, *others):
    count = len(values)
    tied = lax.optimization_barrier((*values, *others))
    return tuple(tied[:count]), *tied[count:]


def rep_of(entry):
    place = lax.axis_index("rep")
    return place ^ entry if square() else entry


def rep_scatter(parts):
    if not square():
        flat = parts.reshape(-1, parts.shape[-1])
        return lax.psum_scatter(flat, "rep", scatter_dimension=0, tiled=True).astype(jnp.float32)
    return sum_pieces(*split_pieces(parts))


def split_pieces(parts):
    half = parts.shape[-1] // 2
    low, high = parts[..., :half], parts[..., half:]
    return jnp.stack([low[0], low[2]], 0), jnp.stack([low[1], low[3]], 0), high[:2], high[2:]


def sum_first(pieces):
    low_kept, low_sent, high_kept, high_sent = pieces
    parts = []
    for kept, sent, first in ((low_kept, low_sent, 1), (high_kept, high_sent, 2)):
        came = to_rep(sent, first)
        parts.append(kept[0].astype(jnp.float32) + came[0].astype(jnp.float32))
        parts.append((kept[1].astype(jnp.float32) + came[1].astype(jnp.float32)).astype(kept.dtype))
    return tuple(parts)


def sum_second(parts):
    low, low_other, high, high_other = parts
    low = low + to_rep(low_other, 2).astype(jnp.float32)
    high = high + to_rep(high_other, 1).astype(jnp.float32)
    return jnp.concatenate([low, high], -1)


def sum_pieces(*pieces):
    return sum_second(sum_first(pieces))


def add_all(value, axis):
    size = lax.axis_size(axis)
    total = value.astype(jnp.float32)
    distance = 1
    while distance < size:
        count = 2 if (size // distance).bit_length() % 2 == 0 else 4
        low = total.astype(value.dtype)
        others = []
        for step in range(1, count):
            route = [(i, i ^ (step * distance)) for i in range(size)]
            others.append(lax.ppermute(low, axis, route).astype(jnp.float32))
        total = total + others[0]
        if count == 4:
            total = total + (others[1] + others[2])
        distance *= count
    return total


def rep_features(block):
    if not square():
        return lax.all_gather(block, "rep", axis=2, tiled=True)
    own, near, far, low, high = square_pieces(block)
    return jnp.concatenate(
        [
            own,
            jnp.stack([near[1], near[0], near[3], near[2]], 0),
            jnp.stack([far[2], far[3], far[0], far[1]], 0),
            jnp.stack([high[1], high[0], low[1], low[0]], 0),
        ],
        2,
    )


def write_pieces(entry, rows, values, refs):
    low_kept, low_sent, high_kept, high_sent = refs
    half = low_kept.shape[-1]
    values = values.astype(jnp.bfloat16)
    (low_sent if entry % 2 else low_kept)[entry // 2, rows] = values[:, :half]
    (high_sent if entry // 2 else high_kept)[entry % 2, rows] = values[:, half:]


def swapped_kernel(x_ref, w_ref, *refs):
    reps, rows, _ = x_ref.shape
    width = w_ref.shape[0] // reps
    for entry in range(reps):
        weight = w_ref[entry * width : (entry + 1) * width]
        for there in range(reps):
            product = over_last(x_ref[there ^ entry], weight)
            write_pieces(entry, slice(there * rows, (there + 1) * rows), product, refs)


def rep_features_sum(columns, weight):
    reps, rows, depth = columns.shape
    width = weight.shape[0] // reps
    if square():
        pieces = pl.pallas_call(
            swapped_kernel,
            out_shape=[jax.ShapeDtypeStruct((2, reps * rows, width // 2), jnp.bfloat16)] * 4,
            compiler_params=pltpu.CompilerParams(vmem_limit_bytes=32 * 2**20),
            cost_estimate=pl.CostEstimate(
                flops=2 * reps * columns.size * width,
                bytes_accessed=10 * columns.size,
                transcendentals=0,
            ),
        )(columns, weight)
        total = sum_pieces(*pieces)
    else:
        product = over_last(columns.reshape(-1, depth), weight).astype(jnp.bfloat16)
        swapped = product.reshape(reps, rows, reps, width).transpose(2, 0, 1, 3)
        total = rep_scatter(swapped.reshape(reps, reps * rows, width))
    return total.reshape(reps, rows, width)


def rep_exchange(parts):
    if not square():
        return lax.all_to_all(parts, "rep", 0, 0)
    return jnp.stack([parts[0]] + [to_rep(parts[entry], entry) for entry in (1, 2, 3)], 0)


def by_place(parts):
    entries = [rep_of(entry) for entry in range(parts.shape[0])]
    return jnp.stack([lax.dynamic_index_in_dim(parts, entry, 0, False) for entry in entries], 0)


def shifted(block, axis, distance):
    devices = range(lax.axis_size(axis))
    route = [(i - distance, i) for i in devices if i - distance in devices]
    return lax.ppermute(block, axis, route)


def tile_offsets(band_total):
    offsets = [0]
    for row_total, col_total in matrix_shapes():
        offsets.append(offsets[-1] + row_total // band_total // BLK * (col_total // BLK))
    return offsets


def whole_tiles(band_total, rep_total):
    return KVH * HD // rep_total % BLK == 0 and FF // band_total // rep_total % BLK == 0


def slice_layout(band_total, rep_total):
    offsets = tile_offsets(band_total)
    layout = []
    for kind, (row_total, col_total) in enumerate(matrix_shapes()):
        rows, cols = row_total // band_total // BLK, col_total // BLK
        grid = offsets[kind] + np.arange(rows * cols).reshape(rows, cols)
        if kind == 6:
            layout.append(grid.reshape(rep_total, rows // rep_total, cols))
        elif kind in (4, 5):
            cut = grid.reshape(rows, band_total, rep_total, -1).transpose(2, 0, 1, 3)
            layout.append(cut.reshape(rep_total, rows, -1))
        else:
            layout.append(grid.reshape(rows, rep_total, -1).transpose(1, 0, 2))
    return layout


def tiles_to_matrix(tiles):
    rows, cols = tiles.shape[:2]
    return tiles.transpose(0, 2, 1, 3).reshape(rows * BLK, cols * BLK)


def matrix_to_tiles(matrix):
    rows, cols = matrix.shape
    cut = matrix.reshape(rows // BLK, BLK, cols // BLK, BLK)
    return cut.transpose(0, 2, 1, 3).reshape(-1, BLK, BLK)


def cut_slices(matrices, band_total, rep_total):
    place = lax.axis_index("rep")
    slices = []
    for kind, matrix in enumerate(matrices):
        rows, cols = matrix.shape
        if kind == 6:
            slices.append(lax.dynamic_slice_in_dim(matrix, place * (rows // rep_total), rows // rep_total, 0))
        elif kind in (4, 5):
            cut = matrix.reshape(rows, band_total, rep_total, -1)
            slices.append(lax.dynamic_index_in_dim(cut, place, 2, False).reshape(rows, -1))
        else:
            slices.append(lax.dynamic_slice_in_dim(matrix, place * (cols // rep_total), cols // rep_total, 1))
    return slices


def join_slices(stacks, band_total, rep_total):
    matrices = []
    for kind, stack in enumerate(stacks):
        rows, cols = stack.shape[1:]
        if kind == 6:
            matrices.append(stack.reshape(-1, cols))
        elif kind in (4, 5):
            cut = stack.reshape(rep_total, rows, band_total, -1).transpose(1, 2, 0, 3)
            matrices.append(cut.reshape(rows, -1))
        else:
            matrices.append(stack.transpose(1, 0, 2).reshape(rows, -1))
    return matrices


def gather_kernel(grids, meta, *refs):
    source_total = len(refs) - len(grids) - 1
    sources, targets, done = refs[:source_total], refs[source_total:-1], refs[-1]
    height = sources[0].shape[1]
    start = 0
    for place, (target, (rows, cols)) in enumerate(zip(targets, grids)):

        def one(tile, carry, target=target, rows=rows, cols=cols, start=start, place=place):
            kind = meta[0, start + tile]
            row = meta[1, start + tile]
            across = tile % cols
            top = pl.multiple_of((across // 2 * rows + tile // cols) * height, height)
            left = pl.multiple_of(across % 2 * BLK, BLK)
            for number, source in enumerate(sources):

                @pl.when(kind == number)
                def _(source=source):
                    pltpu.make_async_copy(
                        source.at[row], target.at[pl.ds(top, height), pl.ds(left, BLK)], done.at[place]
                    ).start()

            return carry

        lax.fori_loop(0, rows * cols, one, 0)
        start += rows * cols
    for place, target in enumerate(targets):
        pltpu.make_async_copy(target, target, done.at[place]).wait()


def gather_strips(sources, meta, grids):
    anywhere = pl.BlockSpec(memory_space=pl.ANY)
    height = sources[0].shape[1]
    out_shape = [
        jax.ShapeDtypeStruct((cols // 2 * rows * height, 2 * BLK), jnp.bfloat16) for rows, cols in grids
    ]
    return pl.pallas_call(
        functools.partial(gather_kernel, grids),
        out_shape=out_shape,
        grid_spec=pltpu.PrefetchScalarGridSpec(
            num_scalar_prefetch=1,
            grid=(1,),
            in_specs=[anywhere] * len(sources),
            out_specs=[pl.BlockSpec(shape.shape, lambda i, *_: (0, 0)) for shape in out_shape],
            scratch_shapes=[pltpu.SemaphoreType.DMA((len(grids),))],
        ),
        compiler_params=pltpu.CompilerParams(vmem_limit_bytes=32 * 2**20),
        cost_estimate=pl.CostEstimate(
            flops=0, bytes_accessed=sum(4 * shape.size for shape in out_shape), transcendentals=0
        ),
    )(meta, *sources)


def place_kernel(entries, rows, cols, meta, low, high, out_ref, done):
    out_ref[...] = jnp.zeros_like(out_ref)
    height = low.shape[1]

    def copies(tile):
        entry, rest = tile // (rows * cols), tile % (rows * cols)
        top = rest // cols * (2 * height)
        left = pl.multiple_of(rest % cols * BLK, BLK)
        return [
            pltpu.make_async_copy(
                half.at[meta[1, tile]],
                out_ref.at[entry, pl.ds(pl.multiple_of(top + part * height, height), height), pl.ds(left, BLK)],
                done.at[part],
            )
            for part, half in enumerate((low, high))
        ]

    def begin(tile, carry):
        @pl.when(meta[0, tile] == 1)
        def _():
            for copy in copies(tile):
                copy.start()

        return carry

    def finish(tile, carry):
        @pl.when(meta[0, tile] == 1)
        def _():
            for copy in copies(tile):
                copy.wait()

        return carry

    lax.fori_loop(0, entries * rows * cols, begin, 0)
    lax.fori_loop(0, entries * rows * cols, finish, 0)


def place_tiles(low, high, meta, entries, rows, cols):
    shape = (entries, rows * BLK, cols * BLK)
    anywhere = pl.BlockSpec(memory_space=pl.ANY)
    return pl.pallas_call(
        functools.partial(place_kernel, entries, rows, cols),
        out_shape=jax.ShapeDtypeStruct(shape, jnp.bfloat16),
        grid_spec=pltpu.PrefetchScalarGridSpec(
            num_scalar_prefetch=1,
            grid=(1,),
            in_specs=[anywhere, anywhere],
            out_specs=pl.BlockSpec(shape, lambda i, *_: (0, 0, 0)),
            scratch_shapes=[pltpu.SemaphoreType.DMA((2,))],
        ),
        compiler_params=pltpu.CompilerParams(vmem_limit_bytes=32 * 2**20),
        cost_estimate=pl.CostEstimate(
            flops=0, bytes_accessed=4 * entries * rows * cols * BLK * BLK, transcendentals=0
        ),
    )(meta, low, high)


def half_turn(values):
    lane = lax.broadcasted_iota(jnp.int32, values.shape, 1)
    lanes = values.shape[1]
    first = lane % HD < HD // 2
    return first, jnp.where(
        first, pltpu.roll(values, lanes - HD // 2, 1), pltpu.roll(values, HD // 2, 1)
    )


def strip_copies(early, late, target, done):
    return [
        pltpu.make_async_copy(half, target.at[:, :, number], done.at[number])
        for number, half in enumerate((early, late))
    ]


def forward_kernel(x_ref, early, late, gate_ref, up_ref, act_ref, weights, done):
    step, steps = pl.program_id(0), pl.num_programs(0)
    slot = step % 2
    width = weights.shape[-1]

    def copies(number, at_step, at_slot):
        strip = number * steps + at_step
        return strip_copies(
            early.at[:, strip], late.at[:, strip], weights.at[number, at_slot], done.at[number, at_slot]
        )

    def fetch(at_step, at_slot):
        for number in range(2):
            for copy in copies(number, at_step, at_slot):
                copy.start()

    @pl.when(step == 0)
    def _():
        fetch(0, 0)

    @pl.when(step + 1 < steps)
    def _():
        fetch(step + 1, 1 - slot)

    for number in range(2):
        for copy in copies(number, step, slot):
            copy.wait()
    gate_weight, up_weight = (weights[number, slot].reshape(-1, width) for number in range(2))
    chunk = min(2 * BLK, x_ref.shape[0])
    for first in range(0, x_ref.shape[0], chunk):
        rows = slice(first, first + chunk)
        gate = jnp.dot(x_ref[rows], gate_weight, preferred_element_type=jnp.float32)
        up = jnp.dot(x_ref[rows], up_weight, preferred_element_type=jnp.float32)
        gate_ref[rows] = gate.astype(jnp.bfloat16)
        up_ref[rows] = up.astype(jnp.bfloat16)
        act_ref[rows] = (gate * jax.nn.sigmoid(gate) * up).astype(jnp.bfloat16)


def forward_products(rows, early, late, columns):
    tokens, depth = rows.shape
    bands, _, tiles, half, width = early.shape
    block = pl.BlockSpec((tokens, width), lambda n: (0, n))
    anywhere = pl.BlockSpec(memory_space=pl.ANY)
    return pl.pallas_call(
        forward_kernel,
        out_shape=[jax.ShapeDtypeStruct((tokens, columns), jnp.bfloat16)] * 3,
        grid=(columns // width,),
        in_specs=[pl.BlockSpec(rows.shape, lambda n: (0, 0)), anywhere, anywhere],
        out_specs=[block] * 3,
        scratch_shapes=[
            pltpu.VMEM((2, 2, bands, tiles, 2, half, width), jnp.bfloat16),
            pltpu.SemaphoreType.DMA((2, 2, 2)),
        ],
        compiler_params=pltpu.CompilerParams(vmem_limit_bytes=48 * 2**20),
        cost_estimate=pl.CostEstimate(
            flops=tokens * depth * columns // 8, bytes_accessed=2 * rows.size, transcendentals=0
        ),
    )(rows, early, late)


def backward_kernel(top_ref, gate_ref, up_ref, act_ref, early, late, late_down, *refs):
    dgate_ref, dup_ref = refs[:2]
    pieces, branch_pieces = refs[2:6], refs[6:10]
    weights, downs, total, branch, done, down_done = refs[10:]
    step, steps = pl.program_id(0), pl.num_programs(0)
    slot = step % 2
    strips, width = downs.shape[1], downs.shape[-1]

    def down_copies(at_step, at_slot):
        return strip_copies(
            early.at[at_step, pl.ds(2 * steps, strips)],
            late_down.at[at_step],
            downs.at[at_slot],
            down_done.at[at_slot],
        )

    def copies(number, at_step, at_slot):
        strip = number * steps + at_step
        return strip_copies(
            early.at[:, strip], late.at[:, strip], weights.at[number, at_slot], done.at[number, at_slot]
        )

    def fetch(at_step, at_slot):
        for copy in down_copies(at_step, at_slot):
            copy.start()
        for number in range(2):
            for copy in copies(number, at_step, at_slot):
                copy.start()

    @pl.when(step == 0)
    def _():
        fetch(0, 0)
        total[...] = jnp.zeros_like(total)
        branch[...] = jnp.zeros_like(branch)

    @pl.when(step + 1 < steps)
    def _():
        fetch(step + 1, 1 - slot)

    for copy in down_copies(step, slot):
        copy.wait()
    for number in range(2):
        for copy in copies(number, step, slot):
            copy.wait()
    gate_weight, up_weight = (weights[number, slot].reshape(-1, width) for number in range(2))
    chunk = min(4 * BLK, top_ref.shape[0])
    for first in range(0, top_ref.shape[0], chunk):
        rows = slice(first, first + chunk)
        grad_act = 0.0
        for strip in range(strips):
            lanes = slice(strip * width, (strip + 1) * width)
            down = downs[slot, strip].reshape(-1, width)
            grad_act = grad_act + over_last(top_ref[rows, lanes], down)
            branch[rows, lanes] += jnp.dot(act_ref[rows], down, preferred_element_type=jnp.float32)
        gate = gate_ref[rows].astype(jnp.float32)
        up = up_ref[rows].astype(jnp.float32)
        sigmoid_gate = jax.nn.sigmoid(gate)
        grad_gate = grad_act * up * sigmoid_gate * (1.0 + gate * (1.0 - sigmoid_gate))
        grad_gate = grad_gate.astype(jnp.bfloat16)
        grad_up = (grad_act * (gate * sigmoid_gate)).astype(jnp.bfloat16)
        dgate_ref[rows] = grad_gate
        dup_ref[rows] = grad_up
        total[rows] += over_last(grad_gate, gate_weight) + over_last(grad_up, up_weight)

    @pl.when(step == steps - 1)
    def _():
        rows = total.shape[0] // 4
        for entry in range(4):
            part = slice(entry * rows, (entry + 1) * rows)
            write_pieces(entry, slice(0, rows), total[part], pieces)
            write_pieces(entry, slice(0, rows), branch[part], branch_pieces)


def backward_products(top, gate, up, act, early, late, late_down):
    tokens, depth = top.shape
    columns = gate.shape[1]
    bands, _, tiles, half, width = early.shape
    strips = late_down.shape[1]
    block = pl.BlockSpec((tokens, width), lambda n: (0, n))
    anywhere = pl.BlockSpec(memory_space=pl.ANY)
    piece = jax.ShapeDtypeStruct((2, tokens // 4, depth // 2), jnp.bfloat16)
    grads = jax.ShapeDtypeStruct((tokens, columns), jnp.bfloat16)
    outs = pl.pallas_call(
        backward_kernel,
        out_shape=[grads] * 2 + [piece] * 8,
        grid=(columns // width,),
        in_specs=[pl.BlockSpec(top.shape, lambda n: (0, 0))] + [block] * 3 + [anywhere] * 3,
        out_specs=[block] * 2 + [pl.BlockSpec(piece.shape, lambda n: (0, 0, 0))] * 8,
        scratch_shapes=[
            pltpu.VMEM((2, 2, bands, tiles, 2, half, width), jnp.bfloat16),
            pltpu.VMEM((2, strips, tiles, 2, half, width), jnp.bfloat16),
            pltpu.VMEM((tokens, depth), jnp.float32),
            pltpu.VMEM((tokens, depth), jnp.float32),
            pltpu.SemaphoreType.DMA((2, 2, 2)),
            pltpu.SemaphoreType.DMA((2, 2)),
        ],
        compiler_params=pltpu.CompilerParams(vmem_limit_bytes=60 * 2**20),
        cost_estimate=pl.CostEstimate(
            flops=8 * tokens * depth * columns, bytes_accessed=8 * columns * depth, transcendentals=0
        ),
    )(top, gate, up, act, early, late, late_down)
    return outs[0], outs[1], outs[2:6], outs[6:10]


def rope_kernel(q_width, kv_width, x_ref, cos_ref, sin_ref, *outs):
    width = x_ref.shape[-1]
    for start in range(0, width, BLK):
        values = x_ref[0, :, start : start + BLK]
        first, turned = half_turn(values)
        sines = sin_ref[0]
        turned_rows = values * cos_ref[0] + turned * jnp.where(first, -sines, sines)
        if start + BLK > q_width + kv_width:
            column = lax.broadcasted_iota(jnp.int32, values.shape, 1) + start
            turned_rows = jnp.where(column >= q_width + kv_width, values, turned_rows)
        if start < q_width:
            outs[0][0, :, start : start + BLK] = (turned_rows * HD ** (-0.5)).astype(jnp.bfloat16)
        else:
            outs[-1][0, :, start - q_width : start - q_width + BLK] = turned_rows.astype(jnp.bfloat16)


def rope_rows(inner, rows, row_block, q_width, kv_width, cosines, sines, with_queries=True):
    seqs, _, width = inner.shape
    shared = cosines.shape[0] == 1
    table = pl.BlockSpec((1, rows, BLK), lambda s: (0 if shared else s, 0, 0))
    widths = [q_width, 2 * kv_width]
    column_block = 0
    if not with_queries:
        width, column_block = 2 * kv_width, q_width // (2 * kv_width)
        widths, q_width = widths[1:], 0
    return pl.pallas_call(
        functools.partial(rope_kernel, q_width, kv_width),
        out_shape=[jax.ShapeDtypeStruct((seqs, rows, w), jnp.bfloat16) for w in widths],
        grid=(seqs,),
        in_specs=[pl.BlockSpec((1, rows, width), lambda s: (s, row_block, column_block)), table, table],
        out_specs=[pl.BlockSpec((1, rows, w), lambda s: (s, 0, 0)) for w in widths],
        cost_estimate=pl.CostEstimate(
            flops=6 * seqs * rows * width, bytes_accessed=6 * seqs * rows * width, transcendentals=0
        ),
    )(inner, cosines, sines)


def fill_bias(band_ref, gpos_ref, bias_ref, rows, window_len):
    band = band_ref[0]

    @pl.when(pl.program_id(0) == 0)
    def _():
        key = lax.broadcasted_iota(jnp.int32, (window_len, rows), 0) + (
            band * rows - (window_len - rows)
        )
        query = lax.broadcasted_iota(jnp.int32, (window_len, rows), 1) + band * rows
        inside = (key > query - WINDOW) & (key <= query) & (key >= 0)
        bias_ref[:window_len] = jnp.where(inside, 0.0, masked_value)

    glob_total = gpos_ref.shape[1]
    query = lax.broadcasted_iota(jnp.int32, (glob_total, rows), 1) + (band * rows - WINDOW)
    spot = jnp.broadcast_to(gpos_ref[0][:, :1], (glob_total, rows))
    bias_ref[window_len:] = jnp.where(spot <= query.astype(jnp.float32), 0.0, masked_value)


def over_last(left, right):
    return lax.dot_general(left, right, (((1,), (1,)), ((), ())), preferred_element_type=jnp.float32)


def over_first(left, right):
    return lax.dot_general(left, right, (((0,), (0,)), ((), ())), preferred_element_type=jnp.float32)


def attend_kernel(block_total, band_ref, gpos_ref, q_ref, *refs):
    blocks, (out_ref, lse_ref, bias_ref) = refs[:block_total], refs[block_total:]
    rows, q_width = q_ref.shape[1:]
    kv_width = blocks[0].shape[2] // 2
    heads, group = q_width // HD, q_width // kv_width
    window_len = rows * (block_total - 1)
    fill_bias(band_ref, gpos_ref, bias_ref, rows, window_len)
    starts = [rows * number for number in range(block_total)]
    pending = []
    for head in range(heads):
        left = head // group * HD
        queries = q_ref[0, :, head * HD : (head + 1) * HD]
        scores = [
            over_last(block[0, :, left : left + HD], queries)
            + bias_ref[start : start + block.shape[1]]
            for block, start in zip(blocks, starts)
        ]
        top = functools.reduce(jnp.maximum, [jnp.max(part, 0, keepdims=True) for part in scores])
        total = 0.0
        mixed = 0.0
        for block, part in zip(blocks, scores):
            weights = jnp.exp(part - top)
            total = total + jnp.sum(weights, 0, keepdims=True)
            mixed = mixed + over_first(
                block[0, :, kv_width + left : kv_width + left + HD], weights.astype(jnp.bfloat16)
            )
        lse_ref[0, head : head + 1, :] = top + jnp.log(total)
        pending.append(mixed / total)
        if len(pending) * HD == BLK or head == heads - 1:
            stop = (head + 1) * HD
            both = jnp.concatenate(pending, 0).T
            out_ref[0, :, stop - both.shape[1] : stop] = both.astype(jnp.bfloat16)
            pending = []


def attend(band, gpos, queries, blocks):
    seqs, rows, q_width = queries.shape
    heads = q_width // HD
    key_total = sum(block.shape[1] for block in blocks)

    def whole(array):
        return pl.BlockSpec((1,) + array.shape[1:], lambda s, *_: (s, 0, 0))

    out_shape = [
        jax.ShapeDtypeStruct((seqs, rows, q_width), jnp.bfloat16),
        jax.ShapeDtypeStruct((seqs, heads, rows), jnp.float32),
    ]
    return pl.pallas_call(
        functools.partial(attend_kernel, len(blocks)),
        out_shape=out_shape,
        grid_spec=pltpu.PrefetchScalarGridSpec(
            num_scalar_prefetch=1,
            grid=(seqs,),
            in_specs=[whole(array) for array in (gpos, queries, *blocks)],
            out_specs=[whole(array) for array in out_shape],
            scratch_shapes=[pltpu.VMEM((key_total, rows), jnp.float32)],
        ),
        compiler_params=pltpu.CompilerParams(vmem_limit_bytes=48 * 2**20),
        cost_estimate=pl.CostEstimate(
            flops=16 * seqs * heads * rows * key_total * HD,
            bytes_accessed=4 * queries.size,
            transcendentals=seqs * heads * rows * key_total,
        ),
    )(band, gpos, queries, *blocks)


def attend_back_kernel(block_total, band_ref, gpos_ref, cos_ref, sin_ref, q_ref, grad_ref, lse_ref, *refs):
    blocks = refs[:block_total]
    dq_ref = refs[block_total]
    out_refs = refs[block_total + 1 : 2 * block_total + 1]
    bias_ref = refs[-1]
    rows, q_width = q_ref.shape[1:]
    kv_width = blocks[0].shape[2] // 2
    heads, group = q_width // HD, q_width // kv_width
    window_len = rows * (block_total - 1)
    fill_bias(band_ref, gpos_ref, bias_ref, rows, window_len)
    starts = [rows * number for number in range(block_total)]
    pending = []
    for kv_head in range(kv_width // HD):
        left = kv_head * HD
        key_sums = [0.0] * block_total
        value_sums = [0.0] * block_total
        for head in range(kv_head * group, (kv_head + 1) * group):
            queries = q_ref[0, :, head * HD : (head + 1) * HD]
            grads = grad_ref[0, :, head * HD : (head + 1) * HD]
            lse = lse_ref[0, head : head + 1, :]
            soft, soft_grads = [], []
            inner = 0.0
            for number, (block, start) in enumerate(zip(blocks, starts)):
                part = over_last(block[0, :, left : left + HD], queries)
                part = jnp.exp(part + bias_ref[start : start + block.shape[1]] - lse)
                slope = over_last(block[0, :, kv_width + left : kv_width + left + HD], grads)
                inner = inner + jnp.sum(part * slope, 0, keepdims=True)
                soft.append(part)
                soft_grads.append(slope)
            turned = 0.0
            for number, block in enumerate(blocks):
                score_grads = (soft[number] * (soft_grads[number] - inner)).astype(jnp.bfloat16)
                value_sums[number] = value_sums[number] + jnp.dot(
                    soft[number].astype(jnp.bfloat16), grads, preferred_element_type=jnp.float32
                )
                key_sums[number] = key_sums[number] + jnp.dot(
                    score_grads, queries, preferred_element_type=jnp.float32
                )
                turned = turned + over_first(block[0, :, left : left + HD], score_grads)
            pending.append(turned)
            if len(pending) * HD == BLK or head == heads - 1:
                stop = (head + 1) * HD
                both = jnp.concatenate(pending, 0).T * HD ** (-0.5)
                pending = []
                first, other = half_turn(both * sin_ref[0])
                both = both * cos_ref[0] + jnp.where(first, other, -other)
                dq_ref[0, :, stop - both.shape[1] : stop] = both.astype(jnp.bfloat16)
        for number, out_ref in enumerate(out_refs):
            out_ref[0, :, left : left + HD] = key_sums[number].astype(out_ref.dtype)
            out_ref[0, :, kv_width + left : kv_width + left + HD] = value_sums[number].astype(
                out_ref.dtype
            )


def attend_back(band, gpos, cosines, sines, queries, grads, lse, blocks):
    seqs, rows, q_width = queries.shape
    heads = q_width // HD
    key_total = sum(block.shape[1] for block in blocks)

    def whole(array):
        return pl.BlockSpec((1,) + array.shape[1:], lambda s, *_: (s, 0, 0))

    table = pl.BlockSpec((1, rows, BLK), lambda s, *_: (0, 0, 0))
    out_shape = [jax.ShapeDtypeStruct(queries.shape, jnp.bfloat16)]
    for number, block in enumerate(blocks):
        own = number == len(blocks) - 2
        out_shape.append(jax.ShapeDtypeStruct(block.shape, jnp.float32 if own else jnp.bfloat16))
    return pl.pallas_call(
        functools.partial(attend_back_kernel, len(blocks)),
        out_shape=out_shape,
        grid_spec=pltpu.PrefetchScalarGridSpec(
            num_scalar_prefetch=1,
            grid=(seqs,),
            in_specs=[whole(gpos), table, table]
            + [whole(array) for array in (queries, grads, lse, *blocks)],
            out_specs=[whole(array) for array in out_shape],
            scratch_shapes=[pltpu.VMEM((key_total, rows), jnp.float32)],
        ),
        compiler_params=pltpu.CompilerParams(vmem_limit_bytes=48 * 2**20),
        cost_estimate=pl.CostEstimate(
            flops=40 * seqs * heads * rows * key_total * HD,
            bytes_accessed=8 * queries.size,
            transcendentals=seqs * heads * rows * key_total,
        ),
    )(band, gpos, cosines, sines, queries, grads, lse, *blocks)


def join_kernel(q_width, kv_width, dq_ref, own_ref, pick_ref, glob_ref, cos_ref, sin_ref, *refs):
    back_refs, out_ref = refs[:-1], refs[-1]
    out_ref[0, :, :q_width] = dq_ref[0]
    picked = lax.dot_general(
        pick_ref[0].astype(jnp.float32),
        glob_ref[0],
        (((0,), (0,)), ((), ())),
        precision=lax.Precision.HIGHEST,
        preferred_element_type=jnp.float32,
    )
    for start in range(0, 2 * kv_width, BLK):
        lanes = slice(start, start + BLK)
        total = own_ref[0, :, lanes] + picked[:, lanes]
        for back_ref in back_refs:
            total = total + back_ref[0, :, lanes].astype(jnp.float32)
        first, other = half_turn(total * sin_ref[0])
        turned = total * cos_ref[0] + jnp.where(first, other, -other)
        column = lax.broadcasted_iota(jnp.int32, total.shape, 1) + start
        turned = jnp.where(column >= kv_width, total, turned)
        out_ref[0, :, q_width + start : q_width + start + BLK] = turned.astype(jnp.bfloat16)


def join_grads(dq, own, picks, globs, cosines, sines, backs):
    seqs, rows, q_width = dq.shape
    kv_width = own.shape[2] // 2

    def whole(array):
        return pl.BlockSpec((1,) + array.shape[1:], lambda s: (s, 0, 0))

    table = pl.BlockSpec((1, rows, BLK), lambda s: (0, 0, 0))
    out_shape = jax.ShapeDtypeStruct((seqs, rows, q_width + 2 * kv_width), jnp.bfloat16)
    return pl.pallas_call(
        functools.partial(join_kernel, q_width, kv_width),
        out_shape=out_shape,
        grid=(seqs,),
        in_specs=[whole(dq), whole(own), whole(picks), whole(globs), table, table]
        + [whole(back) for back in backs],
        out_specs=whole(out_shape),
        cost_estimate=pl.CostEstimate(
            flops=20 * own.size, bytes_accessed=4 * dq.size + 12 * own.size, transcendentals=0
        ),
    )(dq, own, picks, globs, cosines, sines, *backs)


def adam_kernel(batch, meta, rates, *refs):
    master_ref, first_ref, second_ref, left_ref, right_ref = refs[:5]
    sources = refs[5:-6]
    new_first_ref, new_second_ref, new_master_ref, copy_ref, tiles, arrived = refs[-6:]
    step, steps = pl.program_id(0), pl.num_programs(0)
    slot = step % 2

    def fetch(at_step, at_slot):
        for place in range(batch):
            tile = at_step * batch + place
            for number, source in enumerate(sources):

                @pl.when(meta[0, tile] == number)
                def _(source=source, tile=tile, place=place):
                    top = pl.multiple_of(meta[2, tile], BLK)
                    left = pl.multiple_of(meta[3, tile], BLK)
                    pltpu.make_async_copy(
                        source.at[meta[1, tile], pl.ds(top, BLK), pl.ds(left, BLK)],
                        tiles.at[at_slot, place],
                        arrived.at[at_slot],
                    ).start()

    @pl.when(step == 0)
    def _():
        fetch(0, 0)

    @pl.when(step + 1 < steps)
    def _():
        fetch(step + 1, 1 - slot)

    pltpu.make_async_copy(tiles.at[slot], tiles.at[slot], arrived.at[slot]).wait()
    places = range(batch)
    lefts = [left_ref[place].astype(jnp.bfloat16) for place in places]
    rights = [right_ref[place].astype(jnp.bfloat16) for place in places]
    turned = [over_first(lefts[place], tiles[slot, place]).astype(jnp.bfloat16) for place in places]
    rotated = [
        jnp.dot(turned[place], rights[place], preferred_element_type=jnp.float32) for place in places
    ]
    directions = []
    for place in places:
        new_first = beta_one * first_ref[place] + (1.0 - beta_one) * rotated[place]
        new_second = beta_two * second_ref[place] + (1.0 - beta_two) * rotated[place] * rotated[place]
        direction = (new_first * (1.0 / (1.0 - beta_one**STEP))) / (
            jnp.sqrt(new_second * (1.0 / (1.0 - beta_two**STEP))) + adam_eps
        )
        new_first_ref[place] = new_first
        new_second_ref[place] = new_second
        directions.append(direction.astype(jnp.bfloat16))
    updates = [
        jnp.dot(lefts[place], directions[place], preferred_element_type=jnp.float32) for place in places
    ]
    updates = [over_last(updates[place].astype(jnp.bfloat16), rights[place]) for place in places]
    for place in places:
        old = master_ref[place]
        new_master = old - rates[step * batch + place] * (updates[place] + weight_decay * old)
        new_master_ref[place] = new_master
        copy_ref[place] = new_master.astype(jnp.bfloat16)


def adam(meta, rates, state, sources):
    count = state[0].shape[0]
    batch = max(size for size in range(1, 33) if count % size == 0)
    block = pl.BlockSpec((batch, BLK, BLK), lambda s, *_: (s, 0, 0))
    anywhere = pl.BlockSpec(memory_space=pl.ANY)
    shape = (count, BLK, BLK)
    return pl.pallas_call(
        functools.partial(adam_kernel, batch),
        out_shape=[jax.ShapeDtypeStruct(shape, jnp.float32)] * 3
        + [jax.ShapeDtypeStruct(shape, jnp.bfloat16)],
        grid_spec=pltpu.PrefetchScalarGridSpec(
            num_scalar_prefetch=2,
            grid=(count // batch,),
            in_specs=[block] * 5 + [anywhere] * len(sources),
            out_specs=[block] * 4,
            scratch_shapes=[
                pltpu.VMEM((2, batch, BLK, BLK), jnp.bfloat16),
                pltpu.SemaphoreType.DMA((2,)),
            ],
        ),
        compiler_params=pltpu.CompilerParams(vmem_limit_bytes=56 * 2**20),
        cost_estimate=pl.CostEstimate(
            flops=8 * count * BLK**3, bytes_accessed=36 * count * BLK**2, transcendentals=0
        ),
    )(meta, rates, *state, *sources)


def per_device(
    block_input,
    cotangent,
    glob_select,
    assignment,
    master,
    first_moment,
    second_moment,
    left_basis,
    right_basis,
    gains,
    gain_first,
    gain_second,
):
    band_total = lax.axis_size("fsdp")
    rep_total = lax.axis_size("rep")
    place = lax.axis_index("rep")
    band = lax.axis_index("fsdp")
    heads = H // rep_total
    kv_heads = KVH // rep_total
    q_width = heads * HD
    kv_width = kv_heads * HD
    tok_count = block_input.shape[1]
    own_count = master.shape[1]
    tile_total = own_count * rep_total
    aligned = square() and whole_tiles(band_total, rep_total)
    tile_order = assignment[0]

    residual = block_input[0].astype(jnp.float32)
    grad_top = cotangent[0]
    position = band * tok_count + jnp.arange(tok_count, dtype=jnp.int32)
    cosine_table, sine_table = rope_tables(position)
    wide_cosine = jnp.concatenate([cosine_table, cosine_table], 1)[None]
    wide_sine = jnp.concatenate([sine_table, sine_table], 1)[None]
    scale_one = lax.rsqrt(jnp.mean(residual * residual, -1, keepdims=True) + norm_eps)
    normed_one = (residual * scale_one * gains[0]).astype(jnp.bfloat16)
    pick_rows = glob_select[0]
    glob_total = pick_rows.shape[0]
    selector = pick_rows.astype(jnp.bfloat16)
    glob_pos_part = jnp.sum(pick_rows * position[None, :], 1)
    digits = jnp.concatenate([glob_pos_part // 256, glob_pos_part % 256]).astype(jnp.bfloat16)
    digits = jnp.pad(digits[None], ((0, 7), (0, D - 2 * glob_total)))
    glob_rows = jnp.dot(selector, normed_one, preferred_element_type=jnp.float32).astype(jnp.bfloat16)
    glob_rows = add_all(jnp.concatenate([glob_rows, digits], 0), "fsdp").astype(jnp.bfloat16)
    packed = [normed_one, glob_rows, selector.reshape(-1, D)]
    packed = jnp.concatenate(packed, 0)
    packed = jnp.pad(packed, ((0, -packed.shape[0] % 32), (0, 0)))

    def over_bands(slice_rows):
        return lax.all_gather(slice_rows, "fsdp", axis=0, tiled=True)

    if aligned:
        half = BLK // 2
        low, high = (master[0, :, rows].astype(jnp.bfloat16) for rows in (slice(0, half), slice(half, BLK)))
        layout = slice_layout(band_total, rep_total)
        attn_layout = jnp.asarray(np.concatenate(layout[:4], 2))
        wanted = jnp.take(tile_order, by_place(attn_layout).reshape(-1), mode="clip")
        meta = jnp.stack([wanted // own_count == place, wanted % own_count], 0).astype(jnp.int32)
        attn_part = place_tiles(low, high, meta, *attn_layout.shape)
        attn_part = rep_scatter(attn_part).astype(jnp.bfloat16)
        low, attn_part = lax.optimization_barrier((low, attn_part))
        slots = square_pieces(low)
        attn = over_bands(attn_part)
        *slots, attn = lax.optimization_barrier((*slots, attn))
        grids = [lax.dynamic_index_in_dim(jnp.asarray(grid), place, 0, False) for grid in layout]

        def find(wanted):
            wanted = jnp.take(tile_order, jnp.concatenate([grid.reshape(-1) for grid in wanted]), mode="clip")
            entry, row = (wanted // own_count) ^ place, wanted % own_count
            cut = own_count // 2
            high = (entry == 3) & (row >= cut)
            found = jnp.stack([jnp.where(high, 4, entry), jnp.where(high, row - cut, row)], 0)
            return found.astype(jnp.int32)

        all_grid = jnp.concatenate(grids[4:], 1)
        (first_part,) = gather_strips(slots, find([all_grid]), [all_grid.shape])
        packed, first_part = lax.optimization_barrier((packed, first_part))
        early = over_bands(first_part)
    packed_all = rep_gather(packed)
    if aligned:
        packed_all, high = lax.optimization_barrier((packed_all, high))
        later_slots = square_pieces(high)
    normed_one_all = packed_all[:, :tok_count].reshape(-1, D)
    at = tok_count + glob_total
    glob_digits = packed_all[:, at, : 2 * glob_total].astype(jnp.float32)
    glob_place = glob_digits[:, :glob_total] * 256.0 + glob_digits[:, glob_total:]
    at += 8
    selector_all = packed_all[:, at : at + selector.size // D].reshape(rep_total, glob_total, tok_count)

    if aligned:
        in_width = q_width + 2 * kv_width
        w_inner, w_output = attn[:, :in_width], attn[:, in_width:]
    else:
        slots = lax.all_gather(master[0].astype(jnp.bfloat16), "rep", axis=0, tiled=True)
        tiles = jnp.take(slots, tile_order, axis=0, mode="clip")
        slices = cut_slices(band_matrices(tiles, band_total), band_total, rep_total)
        w_inner = over_bands(jnp.concatenate(slices[0:3], 1))
        w_output = over_bands(slices[3])
        w_gate = over_bands(slices[4])
        w_up = over_bands(slices[5])
        w_down = over_bands(slices[6])

    w_output = by_place(w_output.reshape(rep_total, q_width, -1)).reshape(D, -1)

    def mul(rows, weight):
        return jnp.dot(rows, weight, preferred_element_type=jnp.float32)

    def mul_back(rows, weight):
        return lax.dot_general(rows, weight, (((1,), (1,)), ((), ())), preferred_element_type=jnp.float32)

    def weight_grad(rows, grad_rows):
        return lax.dot_general(
            rows, grad_rows, (((0,), (0,)), ((), ())), preferred_element_type=jnp.float32
        ).astype(jnp.bfloat16)

    def own_sum(partial):
        return rep_scatter(partial.astype(jnp.bfloat16).reshape(rep_total, tok_count, D))

    inner_rows = mul(packed_all.reshape(-1, D), w_inner).reshape(rep_total, -1, w_inner.shape[1])
    packed_all, normed_one_all = lax.optimization_barrier((packed_all, normed_one_all))
    queries, own_pairs = rope_rows(inner_rows, tok_count, 0, q_width, kv_width, wide_cosine, wide_sine)
    glob_cosine, glob_sine = rope_tables(glob_place.reshape(-1))
    glob_cosine = jnp.concatenate([glob_cosine, glob_cosine], 1).reshape(rep_total, glob_total, -1)
    glob_sine = jnp.concatenate([glob_sine, glob_sine], 1).reshape(rep_total, glob_total, -1)
    (glob_pairs,) = rope_rows(
        inner_rows, glob_total, tok_count // glob_total, q_width, kv_width, glob_cosine, glob_sine, False
    )
    back_count = (WINDOW + tok_count - 2) // tok_count
    pair_blocks = [shifted(own_pairs, "fsdp", distance) for distance in range(back_count, 0, -1)]
    pair_blocks = pair_blocks + [own_pairs, glob_pairs]
    glob_spots = jnp.broadcast_to(glob_place[:, :, None], (rep_total, glob_total, BLK))
    band_number = band.astype(jnp.int32).reshape(1)
    attended_low, lse = attend(band_number, glob_spots, queries, pair_blocks)
    if aligned:
        *later_slots, attended_low, early = lax.optimization_barrier((*later_slots, attended_low, early))
        last_grid = jnp.concatenate(grids[4:6], 1)
        last_part, down_part = gather_strips(
            later_slots, find([last_grid, grids[6]]), [last_grid.shape, grids[6].shape]
        )

        def by_strips(part):
            gathered = over_bands(part)
            return gathered.reshape(band_total, -1, last_grid.shape[0], half, gathered.shape[-1])

        early = early.reshape(band_total, -1, all_grid.shape[0], half, early.shape[-1])
        late, late_down = by_strips(last_part), by_strips(down_part)
    attended_all = rep_features(attended_low).reshape(-1, D)
    attended_all, grad_top_now = lax.optimization_barrier((attended_all, grad_top))
    top_first = gather_first(grad_top_now)
    columns = mul(attended_all, w_output).astype(jnp.bfloat16).reshape(rep_total, tok_count, -1)
    branch = by_place(rep_exchange(columns)).transpose(1, 0, 2).reshape(tok_count, D)
    middle = residual + branch.astype(jnp.float32)
    scale_two = lax.rsqrt(jnp.mean(middle * middle, -1, keepdims=True) + norm_eps)
    normed_two = (middle * scale_two * gains[1]).astype(jnp.bfloat16)
    top_first, normed_two = after(top_first, normed_two)
    normed_two_all = rep_gather(normed_two).reshape(-1, D)
    top_first, normed_two_all = after(top_first, normed_two_all)
    grad_top_all = gather_join(gather_second(top_first)).reshape(-1, D)

    if aligned:
        gate_rows, up_rows, activation = forward_products(normed_two_all, early, late, FF // rep_total)
        g_down = weight_grad(activation, grad_top_all)
        grad_top_all, g_down = lax.optimization_barrier((grad_top_all, g_down))
        grad_gate, grad_up, pieces, branch_pieces = backward_products(
            grad_top_all, gate_rows, up_rows, activation, early, late, late_down
        )
        grad_normed_two = sum_pieces(*pieces)
    else:
        gate_rows = mul(normed_two_all, w_gate)
        up_rows = mul(normed_two_all, w_up)
        sigmoid_gate = jax.nn.sigmoid(gate_rows)
        silu_gate = gate_rows * sigmoid_gate
        activation = (silu_gate * up_rows).astype(jnp.bfloat16)
        g_down = weight_grad(activation, grad_top_all)
        grad_act = mul_back(grad_top_all, w_down)
        grad_gate = (
            grad_act * up_rows * sigmoid_gate * (1.0 + gate_rows * (1.0 - sigmoid_gate))
        ).astype(jnp.bfloat16)
        grad_up = (grad_act * silu_gate).astype(jnp.bfloat16)
        grad_normed_two = own_sum(mul_back(grad_gate, w_gate) + mul_back(grad_up, w_up))
        branch_pieces = (mul(activation, w_down),)
    g_gate = weight_grad(normed_two_all, grad_gate)
    g_up = weight_grad(normed_two_all, grad_up)
    grad_normed_two, g_gate, g_up = lax.optimization_barrier((grad_normed_two, g_gate, g_up))

    def over_tokens(partial):
        return lax.psum_scatter(partial, "fsdp", scatter_dimension=0, tiled=True)

    s_down = over_tokens(g_down)
    s_gate = over_tokens(g_gate)
    s_up = over_tokens(g_up)

    grad_middle = grad_top.astype(jnp.float32) + norm_back(middle, scale_two, gains[1], grad_normed_two)
    grad_parts = grad_middle.astype(jnp.bfloat16).reshape(tok_count, rep_total, -1).transpose(1, 0, 2)
    grad_columns = rep_exchange(by_place(grad_parts)).reshape(rep_total * tok_count, -1)
    grad_attended = rep_features_sum(
        grad_columns.reshape(rep_total, tok_count, -1), w_output
    ).astype(jnp.bfloat16)
    g_output = weight_grad(attended_all, grad_columns)
    g_output = by_place(g_output.reshape(rep_total, q_width, -1)).reshape(D, -1)
    (s_down,), grad_attended = after((s_down,), grad_attended)
    down_first = gather_first(s_down)
    grad_queries, *grad_blocks = attend_back(
        band_number, glob_spots, wide_cosine, wide_sine, queries, grad_attended, lse, pair_blocks
    )
    down_first, *grad_blocks = after(down_first, *grad_blocks)
    down_second = gather_second(down_first)
    branch_pieces, *grad_blocks = after(tuple(branch_pieces), *grad_blocks)
    branch_first = sum_first(branch_pieces) if aligned else (own_sum(branch_pieces[0]),)
    returned = [
        shifted(grad_blocks[back_count - distance], "fsdp", -distance)
        for distance in range(1, back_count + 1)
    ]
    glob_grads = add_all(grad_blocks[-1], "fsdp")
    grad_inner = join_grads(
        grad_queries, grad_blocks[-2], selector_all, glob_grads, wide_cosine, wide_sine, returned
    ).reshape(-1, q_width + 2 * kv_width)
    branch_first, grad_inner = after(branch_first, grad_inner)
    down_second, grad_inner = after(down_second, grad_inner)
    s_down = gather_join(down_second)
    block_out = middle + (sum_second(branch_first) if aligned else branch_first[0])
    (s_gate,), grad_inner = after((s_gate,), grad_inner)
    gate_first = gather_first(s_gate)
    g_inner = weight_grad(normed_one_all, grad_inner)
    gate_first, grad_normed_parts, block_out = after(
        gate_first, mul_back(grad_inner, w_inner).astype(jnp.bfloat16), block_out
    )
    gate_second = gather_second(gate_first)
    grad_normed_parts = grad_normed_parts.reshape(rep_total, tok_count, D)
    if square():
        normed_first = sum_first(split_pieces(grad_normed_parts))
    else:
        normed_first = (rep_scatter(grad_normed_parts),)
    g_attn = with_layout_constraint(jnp.concatenate([g_inner, g_output], 1), Layout((0, 1)))
    normed_first, s_up, g_attn, *gate_second = after(normed_first, s_up, g_attn, *gate_second)
    s_gate = gather_join(gate_second)
    grad_normed_one = sum_second(normed_first) if square() else normed_first[0]
    s_up = rep_gather(s_up)
    s_attn = over_tokens(g_attn)
    grad_input = grad_middle + norm_back(residual, scale_one, gains[0], grad_normed_one)

    gain_terms = jnp.stack(
        [
            jnp.sum(grad_normed_one * residual * scale_one, 0),
            jnp.sum(grad_normed_two * middle * scale_two, 0),
        ]
    )
    square_terms = jnp.stack(
        [jnp.sum(residual * residual), jnp.sum(middle * middle), jnp.sum(block_out * block_out)]
    )
    sums = jnp.concatenate([gain_terms.reshape(-1), square_terms])

    sums = add_all(add_all(sums, "rep"), "fsdp")
    sums, s_attn, s_up = lax.optimization_barrier((sums, s_attn, s_up))
    gain_grad, square_total = sums[: 2 * D].reshape(2, D), sums[2 * D :]

    slot_ids = jnp.arange(tile_total, dtype=jnp.int32)
    inverse = jnp.sum(jnp.where(tile_order[None, :] == slot_ids[:, None], slot_ids[None, :], 0), 1)
    own_slots = place * own_count + jnp.arange(own_count, dtype=jnp.int32)
    owned_tiles = jnp.take(inverse, own_slots, mode="clip")
    if aligned:
        sources = [rep_gather(s_attn), s_gate, s_up, s_down]
        where = np.zeros((4, rep_total, tile_total), np.int32)
        first_col = 0
        for kind, grid in enumerate(layout):
            rows, cols = grid.shape[1:]
            first_col = 0 if kind >= 4 else first_col
            for there in range(rep_total):
                numbers = grid[there].reshape(-1)
                at = np.arange(rows * cols)
                where[0, :, numbers] = max(kind - 3, 0)
                where[2, :, numbers] = (at // cols * BLK)[:, None]
                where[3, :, numbers] = (at % cols * BLK + first_col)[:, None]
                for here in range(rep_total):
                    where[1, here, numbers] = here ^ there
            first_col += cols * BLK
        tile_spots = lax.dynamic_index_in_dim(jnp.asarray(where), place, 1, False)
        meta = jnp.take(tile_spots, owned_tiles, axis=1, mode="clip")
    else:
        splits = [0, q_width, q_width + kv_width, q_width + 2 * kv_width, s_attn.shape[1]]
        stacks = [rep_gather(s_attn[:, low:high]) for low, high in zip(splits, splits[1:])]
        stacks += [s_gate, s_up, s_down]
        sources = [band_tiles(join_slices(stacks, band_total, rep_total))]
        meta = jnp.stack([0 * owned_tiles, owned_tiles, 0 * owned_tiles, 0 * owned_tiles], 0)
    slot_rates = jnp.take(kind_rates(band_total), owned_tiles, mode="clip")
    new_first, new_second, new_master, master_copy = adam(
        meta,
        slot_rates,
        (master[0], first_moment[0], second_moment[0], left_basis[0], right_basis[0]),
        sources,
    )
    new_gain_first = beta_one * gain_first + (1.0 - beta_one) * gain_grad
    new_gain_second = beta_two * gain_second + (1.0 - beta_two) * gain_grad * gain_grad
    gain_step = (
        new_gain_first
        / (1.0 - beta_one**STEP)
        / (jnp.sqrt(new_gain_second / (1.0 - beta_two**STEP)) + adam_eps)
    )
    new_gains = gains - gain_rate * gain_step
    rms_stats = jnp.sqrt(square_total / (rep_total * band_total * tok_count * D))
    return (
        block_out[None],
        grad_input[None],
        new_first[None],
        new_second[None],
        new_master[None],
        master_copy[None],
        new_gain_first,
        new_gain_second,
        new_gains,
        rms_stats,
    )


def solution(mesh):
    in_specs = (
        P("rep", "fsdp", None),
        P("rep", "fsdp", None),
        P("rep", None, "fsdp"),
        P("fsdp", None),
        P("fsdp", "rep", None, None),
        P("fsdp", "rep", None, None),
        P("fsdp", "rep", None, None),
        P("fsdp", "rep", None, None),
        P("fsdp", "rep", None, None),
        P(),
        P(),
        P(),
    )
    out_specs = (
        P("rep", "fsdp", None),
        P("rep", "fsdp", None),
        P("fsdp", "rep", None, None),
        P("fsdp", "rep", None, None),
        P("fsdp", "rep", None, None),
        P("fsdp", "rep", None, None),
        P(),
        P(),
        P(),
        P(),
    )
    return jax.shard_map(
        per_device, mesh=mesh, in_specs=in_specs, out_specs=out_specs, check_vma=False
    )
```

```python
import functools

import jax
import jax.numpy as jnp
import numpy as np
from jax import lax
from jax.experimental import pallas as pl
from jax.experimental.layout import Layout, with_layout_constraint
from jax.experimental.pallas import tpu as pltpu
from jax.sharding import PartitionSpec as P

D = 2048
H = 32
KVH = 8
HD = 64
FF = 8192
WINDOW = 512
BLK = 128
STEP = 10


norm_eps = 1e-05
rope_theta = 500000.0
beta_one = 0.5
beta_two = 0.5
adam_eps = 1e-08
weight_decay = 0.1
gain_rate = 0.5
masked_value = -1e30


def matrix_shapes():
    kv_width = KVH * HD
    return [(D, D), (D, kv_width), (D, kv_width), (D, D), (D, FF), (D, FF), (FF, D)]


def kind_rates(band_total):
    rate_list = [
        D ** (-0.5),
        D ** (-0.5),
        D ** (-0.5),
        (D * 8 // WINDOW) ** (-0.5),
        D ** (-0.5),
        D ** (-0.5),
        FF ** (-0.5),
    ]
    pieces = []
    for (row_total, col_total), rate_value in zip(matrix_shapes(), rate_list):
        tile_count = row_total // band_total // BLK * (col_total // BLK)
        pieces.append(jnp.full((tile_count,), rate_value, jnp.float32))
    return jnp.concatenate(pieces)


def band_matrices(tiles, band_total):
    matrices = []
    offset = 0
    for row_total, col_total in matrix_shapes():
        band_rows = row_total // band_total
        tile_count = band_rows // BLK * (col_total // BLK)
        segment = tiles[offset : offset + tile_count].reshape(
            band_rows // BLK, col_total // BLK, BLK, BLK
        )
        matrices.append(segment.transpose(0, 2, 1, 3).reshape(band_rows, col_total))
        offset += tile_count
    return matrices


def band_tiles(matrices):
    pieces = []
    for matrix in matrices:
        row_count, col_count = matrix.shape
        segment = matrix.reshape(row_count // BLK, BLK, col_count // BLK, BLK).transpose(0, 2, 1, 3)
        pieces.append(segment.reshape(-1, BLK, BLK))
    return jnp.concatenate(pieces, 0)


def rope_tables(position):
    halves = jnp.arange(HD // 2, dtype=jnp.float32) * (2.0 / HD)
    frequency = rope_theta ** (-halves)
    angles = position.astype(jnp.float32)[:, None] * frequency[None, :]
    angles = jnp.concatenate([angles, angles], 1)
    return (jnp.cos(angles), jnp.sin(angles))


def rotate(vectors, cosine_table, sine_table):
    half_width = vectors.shape[-1] // 2
    turned = jnp.concatenate([-vectors[..., half_width:], vectors[..., :half_width]], -1)
    return vectors * cosine_table[:, None, :] + turned * sine_table[:, None, :]


def rotate_back(grad_rows, cosine_table, sine_table):
    half_width = grad_rows.shape[-1] // 2
    scaled = grad_rows * sine_table[:, None, :]
    turned = jnp.concatenate([scaled[..., half_width:], -scaled[..., :half_width]], -1)
    return grad_rows * cosine_table[:, None, :] + turned


def norm_back(values, row_scale, gain_row, grad_rows):
    weighted = grad_rows * gain_row
    return row_scale * weighted - values * row_scale**3 * jnp.mean(
        weighted * values, -1, keepdims=True
    )


def to_rep(block, distance):
    route = [(i, i ^ distance) for i in range(lax.axis_size("rep"))]
    return lax.ppermute(block, "rep", route)


def square():
    return lax.axis_size("rep") == 4


def gather_first(block):
    if not square():
        return (lax.all_gather(block, "rep", axis=0),)
    return block, to_rep(block, 1), to_rep(block, 2)


def gather_second(first):
    if not square():
        return first
    block, near, far = first
    cut = block.shape[0] // 2
    return block, near, far, to_rep(near[:cut], 2), to_rep(far[cut:], 1)


def gather_join(pieces):
    if not square():
        return pieces[0]
    return jnp.concatenate(pieces, 0).reshape((4,) + pieces[0].shape)


def square_pieces(block):
    return gather_second(gather_first(block))


def rep_gather(block):
    return gather_join(gather_second(gather_first(block)))


def after(values, *others):
    count = len(values)
    tied = lax.optimization_barrier((*values, *others))
    return tuple(tied[:count]), *tied[count:]


def rep_of(entry):
    place = lax.axis_index("rep")
    return place ^ entry if square() else entry


def rep_scatter(parts):
    if not square():
        flat = parts.reshape(-1, parts.shape[-1])
        return lax.psum_scatter(flat, "rep", scatter_dimension=0, tiled=True).astype(jnp.float32)
    return sum_pieces(*split_pieces(parts))


def split_pieces(parts):
    half = parts.shape[-1] // 2
    low, high = parts[..., :half], parts[..., half:]
    return jnp.stack([low[0], low[2]], 0), jnp.stack([low[1], low[3]], 0), high[:2], high[2:]


def sum_first(pieces):
    low_kept, low_sent, high_kept, high_sent = pieces
    parts = []
    for kept, sent, first in ((low_kept, low_sent, 1), (high_kept, high_sent, 2)):
        came = to_rep(sent, first)
        parts.append(kept[0].astype(jnp.float32) + came[0].astype(jnp.float32))
        parts.append((kept[1].astype(jnp.float32) + came[1].astype(jnp.float32)).astype(kept.dtype))
    return tuple(parts)


def sum_second(parts):
    low, low_other, high, high_other = parts
    low = low + to_rep(low_other, 2).astype(jnp.float32)
    high = high + to_rep(high_other, 1).astype(jnp.float32)
    return jnp.concatenate([low, high], -1)


def sum_pieces(*pieces):
    return sum_second(sum_first(pieces))


def add_all(value, axis):
    size = lax.axis_size(axis)
    total = value.astype(jnp.float32)
    distance = 1
    while distance < size:
        count = 2 if (size // distance).bit_length() % 2 == 0 else 4
        low = total.astype(value.dtype)
        others = []
        for step in range(1, count):
            route = [(i, i ^ (step * distance)) for i in range(size)]
            others.append(lax.ppermute(low, axis, route).astype(jnp.float32))
        total = total + others[0]
        if count == 4:
            total = total + (others[1] + others[2])
        distance *= count
    return total


def rep_features(block):
    if not square():
        return lax.all_gather(block, "rep", axis=2, tiled=True)
    own, near, far, low, high = square_pieces(block)
    return jnp.concatenate(
        [
            own,
            jnp.stack([near[1], near[0], near[3], near[2]], 0),
            jnp.stack([far[2], far[3], far[0], far[1]], 0),
            jnp.stack([high[1], high[0], low[1], low[0]], 0),
        ],
        2,
    )


def write_pieces(entry, rows, values, refs):
    low_kept, low_sent, high_kept, high_sent = refs
    half = low_kept.shape[-1]
    values = values.astype(jnp.bfloat16)
    (low_sent if entry % 2 else low_kept)[entry // 2, rows] = values[:, :half]
    (high_sent if entry // 2 else high_kept)[entry % 2, rows] = values[:, half:]


def swapped_kernel(x_ref, w_ref, *refs):
    reps, rows, _ = x_ref.shape
    width = w_ref.shape[0] // reps
    for entry in range(reps):
        weight = w_ref[entry * width : (entry + 1) * width]
        for there in range(reps):
            product = over_last(x_ref[there ^ entry], weight)
            write_pieces(entry, slice(there * rows, (there + 1) * rows), product, refs)


def rep_features_sum(columns, weight):
    reps, rows, depth = columns.shape
    width = weight.shape[0] // reps
    if square():
        pieces = pl.pallas_call(
            swapped_kernel,
            out_shape=[jax.ShapeDtypeStruct((2, reps * rows, width // 2), jnp.bfloat16)] * 4,
            compiler_params=pltpu.CompilerParams(vmem_limit_bytes=32 * 2**20),
            cost_estimate=pl.CostEstimate(
                flops=2 * reps * columns.size * width,
                bytes_accessed=10 * columns.size,
                transcendentals=0,
            ),
        )(columns, weight)
        total = sum_pieces(*pieces)
    else:
        product = over_last(columns.reshape(-1, depth), weight).astype(jnp.bfloat16)
        swapped = product.reshape(reps, rows, reps, width).transpose(2, 0, 1, 3)
        total = rep_scatter(swapped.reshape(reps, reps * rows, width))
    return total.reshape(reps, rows, width)


def rep_exchange(parts):
    if not square():
        return lax.all_to_all(parts, "rep", 0, 0)
    return jnp.stack([parts[0]] + [to_rep(parts[entry], entry) for entry in (1, 2, 3)], 0)


def by_place(parts):
    entries = [rep_of(entry) for entry in range(parts.shape[0])]
    return jnp.stack([lax.dynamic_index_in_dim(parts, entry, 0, False) for entry in entries], 0)


def to_core(block):
    return lax.ppermute(block, "fsdp", [(i, i ^ 1) for i in range(lax.axis_size("fsdp"))])


def shifted(block, axis, distance):
    devices = range(lax.axis_size(axis))
    route = [(i - distance, i) for i in devices if i - distance in devices]
    return lax.ppermute(block, axis, route)


def tile_offsets(band_total):
    offsets = [0]
    for row_total, col_total in matrix_shapes():
        offsets.append(offsets[-1] + row_total // band_total // BLK * (col_total // BLK))
    return offsets


def whole_tiles(band_total, rep_total):
    return KVH * HD // rep_total % BLK == 0 and FF // band_total // rep_total % BLK == 0


def slice_layout(band_total, rep_total):
    offsets = tile_offsets(band_total)
    layout = []
    for kind, (row_total, col_total) in enumerate(matrix_shapes()):
        rows, cols = row_total // band_total // BLK, col_total // BLK
        grid = offsets[kind] + np.arange(rows * cols).reshape(rows, cols)
        if kind == 6:
            layout.append(grid.reshape(rep_total, rows // rep_total, cols))
        elif kind in (4, 5):
            cut = grid.reshape(rows, band_total, rep_total, -1).transpose(2, 0, 1, 3)
            layout.append(cut.reshape(rep_total, rows, -1))
        else:
            layout.append(grid.reshape(rows, rep_total, -1).transpose(1, 0, 2))
    return layout


def tiles_to_matrix(tiles):
    rows, cols = tiles.shape[:2]
    return tiles.transpose(0, 2, 1, 3).reshape(rows * BLK, cols * BLK)


def matrix_to_tiles(matrix):
    rows, cols = matrix.shape
    cut = matrix.reshape(rows // BLK, BLK, cols // BLK, BLK)
    return cut.transpose(0, 2, 1, 3).reshape(-1, BLK, BLK)


def cut_slices(matrices, band_total, rep_total):
    place = lax.axis_index("rep")
    slices = []
    for kind, matrix in enumerate(matrices):
        rows, cols = matrix.shape
        if kind == 6:
            slices.append(lax.dynamic_slice_in_dim(matrix, place * (rows // rep_total), rows // rep_total, 0))
        elif kind in (4, 5):
            cut = matrix.reshape(rows, band_total, rep_total, -1)
            slices.append(lax.dynamic_index_in_dim(cut, place, 2, False).reshape(rows, -1))
        else:
            slices.append(lax.dynamic_slice_in_dim(matrix, place * (cols // rep_total), cols // rep_total, 1))
    return slices


def join_slices(stacks, band_total, rep_total):
    matrices = []
    for kind, stack in enumerate(stacks):
        rows, cols = stack.shape[1:]
        if kind == 6:
            matrices.append(stack.reshape(-1, cols))
        elif kind in (4, 5):
            cut = stack.reshape(rep_total, rows, band_total, -1).transpose(1, 2, 0, 3)
            matrices.append(cut.reshape(rows, -1))
        else:
            matrices.append(stack.transpose(1, 0, 2).reshape(rows, -1))
    return matrices


def gather_kernel(grids, meta, *refs):
    source_total = len(refs) - len(grids) - 1
    sources, targets, done = refs[:source_total], refs[source_total:-1], refs[-1]
    height = sources[0].shape[1]
    start = 0
    for place, (target, (rows, cols)) in enumerate(zip(targets, grids)):

        def one(tile, carry, target=target, rows=rows, cols=cols, start=start, place=place):
            kind = meta[0, start + tile]
            row = meta[1, start + tile]
            across = tile % cols
            top = pl.multiple_of((across // 2 * rows + tile // cols) * height, height)
            left = pl.multiple_of(across % 2 * BLK, BLK)
            for number, source in enumerate(sources):

                @pl.when(kind == number)
                def _(source=source):
                    pltpu.make_async_copy(
                        source.at[row], target.at[pl.ds(top, height), pl.ds(left, BLK)], done.at[place]
                    ).start()

            return carry

        lax.fori_loop(0, rows * cols, one, 0)
        start += rows * cols
    for place, target in enumerate(targets):
        pltpu.make_async_copy(target, target, done.at[place]).wait()


def gather_strips(sources, meta, grids):
    anywhere = pl.BlockSpec(memory_space=pl.ANY)
    height = sources[0].shape[1]
    out_shape = [
        jax.ShapeDtypeStruct((cols // 2 * rows * height, 2 * BLK), jnp.bfloat16) for rows, cols in grids
    ]
    return pl.pallas_call(
        functools.partial(gather_kernel, grids),
        out_shape=out_shape,
        grid_spec=pltpu.PrefetchScalarGridSpec(
            num_scalar_prefetch=1,
            grid=(1,),
            in_specs=[anywhere] * len(sources),
            out_specs=[pl.BlockSpec(shape.shape, lambda i, *_: (0, 0)) for shape in out_shape],
            scratch_shapes=[pltpu.SemaphoreType.DMA((len(grids),))],
        ),
        compiler_params=pltpu.CompilerParams(vmem_limit_bytes=32 * 2**20),
        cost_estimate=pl.CostEstimate(
            flops=0, bytes_accessed=sum(4 * shape.size for shape in out_shape), transcendentals=0
        ),
    )(meta, *sources)


def place_kernel(entries, rows, cols, meta, low, high, out_ref, done):
    out_ref[...] = jnp.zeros_like(out_ref)
    height = low.shape[1]

    def copies(tile):
        entry, rest = tile // (rows * cols), tile % (rows * cols)
        top = rest // cols * (2 * height)
        left = pl.multiple_of(rest % cols * BLK, BLK)
        return [
            pltpu.make_async_copy(
                half.at[meta[1, tile]],
                out_ref.at[entry, pl.ds(pl.multiple_of(top + part * height, height), height), pl.ds(left, BLK)],
                done.at[part],
            )
            for part, half in enumerate((low, high))
        ]

    def begin(tile, carry):
        @pl.when(meta[0, tile] == 1)
        def _():
            for copy in copies(tile):
                copy.start()

        return carry

    def finish(tile, carry):
        @pl.when(meta[0, tile] == 1)
        def _():
            for copy in copies(tile):
                copy.wait()

        return carry

    lax.fori_loop(0, entries * rows * cols, begin, 0)
    lax.fori_loop(0, entries * rows * cols, finish, 0)


def place_tiles(low, high, meta, entries, rows, cols):
    shape = (entries, rows * BLK, cols * BLK)
    anywhere = pl.BlockSpec(memory_space=pl.ANY)
    return pl.pallas_call(
        functools.partial(place_kernel, entries, rows, cols),
        out_shape=jax.ShapeDtypeStruct(shape, jnp.bfloat16),
        grid_spec=pltpu.PrefetchScalarGridSpec(
            num_scalar_prefetch=1,
            grid=(1,),
            in_specs=[anywhere, anywhere],
            out_specs=pl.BlockSpec(shape, lambda i, *_: (0, 0, 0)),
            scratch_shapes=[pltpu.SemaphoreType.DMA((2,))],
        ),
        compiler_params=pltpu.CompilerParams(vmem_limit_bytes=32 * 2**20),
        cost_estimate=pl.CostEstimate(
            flops=0, bytes_accessed=4 * entries * rows * cols * BLK * BLK, transcendentals=0
        ),
    )(meta, low, high)


def half_turn(values):
    lane = lax.broadcasted_iota(jnp.int32, values.shape, 1)
    lanes = values.shape[1]
    first = lane % HD < HD // 2
    return first, jnp.where(
        first, pltpu.roll(values, lanes - HD // 2, 1), pltpu.roll(values, HD // 2, 1)
    )


def strip_copies(early, late, target, done):
    return [
        pltpu.make_async_copy(half, target.at[:, :, number], done.at[number])
        for number, half in enumerate((early, late))
    ]


def forward_kernel(x_ref, early, late, gate_ref, up_ref, act_ref, weights, done):
    step, steps = pl.program_id(0), pl.num_programs(0)
    slot = step % 2
    width = weights.shape[-1]

    def copies(number, at_step, at_slot):
        strip = number * steps + at_step
        return strip_copies(
            early.at[:, strip], late.at[:, strip], weights.at[number, at_slot], done.at[number, at_slot]
        )

    def fetch(at_step, at_slot):
        for number in range(2):
            for copy in copies(number, at_step, at_slot):
                copy.start()

    @pl.when(step == 0)
    def _():
        fetch(0, 0)

    @pl.when(step + 1 < steps)
    def _():
        fetch(step + 1, 1 - slot)

    for number in range(2):
        for copy in copies(number, step, slot):
            copy.wait()
    gate_weight, up_weight = (weights[number, slot].reshape(-1, width) for number in range(2))
    chunk = min(2 * BLK, x_ref.shape[0])
    for first in range(0, x_ref.shape[0], chunk):
        rows = slice(first, first + chunk)
        gate = jnp.dot(x_ref[rows], gate_weight, preferred_element_type=jnp.float32)
        up = jnp.dot(x_ref[rows], up_weight, preferred_element_type=jnp.float32)
        gate_ref[rows] = gate.astype(jnp.bfloat16)
        up_ref[rows] = up.astype(jnp.bfloat16)
        act_ref[rows] = (gate * jax.nn.sigmoid(gate) * up).astype(jnp.bfloat16)


def forward_products(rows, early, late, columns):
    tokens, depth = rows.shape
    bands, _, tiles, half, width = early.shape
    block = pl.BlockSpec((tokens, width), lambda n: (0, n))
    anywhere = pl.BlockSpec(memory_space=pl.ANY)
    return pl.pallas_call(
        forward_kernel,
        out_shape=[jax.ShapeDtypeStruct((tokens, columns), jnp.bfloat16)] * 3,
        grid=(columns // width,),
        in_specs=[pl.BlockSpec(rows.shape, lambda n: (0, 0)), anywhere, anywhere],
        out_specs=[block] * 3,
        scratch_shapes=[
            pltpu.VMEM((2, 2, bands, tiles, 2, half, width), jnp.bfloat16),
            pltpu.SemaphoreType.DMA((2, 2, 2)),
        ],
        compiler_params=pltpu.CompilerParams(vmem_limit_bytes=48 * 2**20),
        cost_estimate=pl.CostEstimate(
            flops=tokens * depth * columns // 8, bytes_accessed=2 * rows.size, transcendentals=0
        ),
    )(rows, early, late)


def backward_kernel(top_ref, gate_ref, up_ref, act_ref, early, late, *refs):
    dgate_ref, dup_ref = refs[:2]
    pieces, branch_pieces = refs[2:6], refs[6:10]
    weights, downs, total, branch, done, down_done = refs[10:]
    step, steps = pl.program_id(0), pl.num_programs(0)
    slot = step % 2
    strips, width = downs.shape[1], downs.shape[-1]

    def down_copies(at_step, at_slot):
        wanted = pl.ds(2 * steps, strips)
        return strip_copies(
            early.at[at_step, wanted], late.at[at_step, wanted], downs.at[at_slot], down_done.at[at_slot]
        )

    def copies(number, at_step, at_slot):
        strip = number * steps + at_step
        return strip_copies(
            early.at[:, strip], late.at[:, strip], weights.at[number, at_slot], done.at[number, at_slot]
        )

    def fetch(at_step, at_slot):
        for copy in down_copies(at_step, at_slot):
            copy.start()
        for number in range(2):
            for copy in copies(number, at_step, at_slot):
                copy.start()

    @pl.when(step == 0)
    def _():
        fetch(0, 0)
        total[...] = jnp.zeros_like(total)
        branch[...] = jnp.zeros_like(branch)

    @pl.when(step + 1 < steps)
    def _():
        fetch(step + 1, 1 - slot)

    for copy in down_copies(step, slot):
        copy.wait()
    for number in range(2):
        for copy in copies(number, step, slot):
            copy.wait()
    gate_weight, up_weight = (weights[number, slot].reshape(-1, width) for number in range(2))
    chunk = min(4 * BLK, top_ref.shape[0])
    for first in range(0, top_ref.shape[0], chunk):
        rows = slice(first, first + chunk)
        grad_act = 0.0
        for strip in range(strips):
            lanes = slice(strip * width, (strip + 1) * width)
            down = downs[slot, strip].reshape(-1, width)
            grad_act = grad_act + over_last(top_ref[rows, lanes], down)
            branch[rows, lanes] += jnp.dot(act_ref[rows], down, preferred_element_type=jnp.float32)
        gate = gate_ref[rows].astype(jnp.float32)
        up = up_ref[rows].astype(jnp.float32)
        sigmoid_gate = jax.nn.sigmoid(gate)
        grad_gate = grad_act * up * sigmoid_gate * (1.0 + gate * (1.0 - sigmoid_gate))
        grad_gate = grad_gate.astype(jnp.bfloat16)
        grad_up = (grad_act * (gate * sigmoid_gate)).astype(jnp.bfloat16)
        dgate_ref[rows] = grad_gate
        dup_ref[rows] = grad_up
        total[rows] += over_last(grad_gate, gate_weight) + over_last(grad_up, up_weight)

    @pl.when(step == steps - 1)
    def _():
        rows = total.shape[0] // 4
        for entry in range(4):
            part = slice(entry * rows, (entry + 1) * rows)
            write_pieces(entry, slice(0, rows), total[part], pieces)
            write_pieces(entry, slice(0, rows), branch[part], branch_pieces)


def backward_products(top, gate, up, act, early, late):
    tokens, depth = top.shape
    columns = gate.shape[1]
    bands, _, tiles, half, width = early.shape
    strips = depth // width
    block = pl.BlockSpec((tokens, width), lambda n: (0, n))
    anywhere = pl.BlockSpec(memory_space=pl.ANY)
    piece = jax.ShapeDtypeStruct((2, tokens // 4, depth // 2), jnp.bfloat16)
    grads = jax.ShapeDtypeStruct((tokens, columns), jnp.bfloat16)
    outs = pl.pallas_call(
        backward_kernel,
        out_shape=[grads] * 2 + [piece] * 8,
        grid=(columns // width,),
        in_specs=[pl.BlockSpec(top.shape, lambda n: (0, 0))] + [block] * 3 + [anywhere] * 2,
        out_specs=[block] * 2 + [pl.BlockSpec(piece.shape, lambda n: (0, 0, 0))] * 8,
        scratch_shapes=[
            pltpu.VMEM((2, 2, bands, tiles, 2, half, width), jnp.bfloat16),
            pltpu.VMEM((2, strips, tiles, 2, half, width), jnp.bfloat16),
            pltpu.VMEM((tokens, depth), jnp.float32),
            pltpu.VMEM((tokens, depth), jnp.float32),
            pltpu.SemaphoreType.DMA((2, 2, 2)),
            pltpu.SemaphoreType.DMA((2, 2)),
        ],
        compiler_params=pltpu.CompilerParams(vmem_limit_bytes=60 * 2**20),
        cost_estimate=pl.CostEstimate(
            flops=8 * tokens * depth * columns, bytes_accessed=8 * columns * depth, transcendentals=0
        ),
    )(top, gate, up, act, early, late)
    return outs[0], outs[1], outs[2:6], outs[6:10]


def rope_kernel(q_width, kv_width, x_ref, cos_ref, sin_ref, *outs):
    width = x_ref.shape[-1]
    for start in range(0, width, BLK):
        values = x_ref[0, :, start : start + BLK]
        first, turned = half_turn(values)
        sines = sin_ref[0]
        turned_rows = values * cos_ref[0] + turned * jnp.where(first, -sines, sines)
        if start + BLK > q_width + kv_width:
            column = lax.broadcasted_iota(jnp.int32, values.shape, 1) + start
            turned_rows = jnp.where(column >= q_width + kv_width, values, turned_rows)
        if start < q_width:
            outs[0][0, :, start : start + BLK] = (turned_rows * HD ** (-0.5)).astype(jnp.bfloat16)
        else:
            outs[-1][0, :, start - q_width : start - q_width + BLK] = turned_rows.astype(jnp.bfloat16)


def rope_rows(inner, rows, row_block, q_width, kv_width, cosines, sines, with_queries=True):
    seqs, _, width = inner.shape
    shared = cosines.shape[0] == 1
    table = pl.BlockSpec((1, rows, BLK), lambda s: (0 if shared else s, 0, 0))
    widths = [q_width, 2 * kv_width]
    column_block = 0
    if not with_queries:
        width, column_block = 2 * kv_width, q_width // (2 * kv_width)
        widths, q_width = widths[1:], 0
    return pl.pallas_call(
        functools.partial(rope_kernel, q_width, kv_width),
        out_shape=[jax.ShapeDtypeStruct((seqs, rows, w), jnp.bfloat16) for w in widths],
        grid=(seqs,),
        in_specs=[pl.BlockSpec((1, rows, width), lambda s: (s, row_block, column_block)), table, table],
        out_specs=[pl.BlockSpec((1, rows, w), lambda s: (s, 0, 0)) for w in widths],
        cost_estimate=pl.CostEstimate(
            flops=6 * seqs * rows * width, bytes_accessed=6 * seqs * rows * width, transcendentals=0
        ),
    )(inner, cosines, sines)


def fill_bias(band_ref, gpos_ref, bias_ref, rows, window_len):
    band = band_ref[0]

    @pl.when(pl.program_id(0) == 0)
    def _():
        key = lax.broadcasted_iota(jnp.int32, (window_len, rows), 0) + (
            band * rows - (window_len - rows)
        )
        query = lax.broadcasted_iota(jnp.int32, (window_len, rows), 1) + band * rows
        inside = (key > query - WINDOW) & (key <= query) & (key >= 0)
        bias_ref[:window_len] = jnp.where(inside, 0.0, masked_value)

    glob_total = gpos_ref.shape[1]
    query = lax.broadcasted_iota(jnp.int32, (glob_total, rows), 1) + (band * rows - WINDOW)
    spot = jnp.broadcast_to(gpos_ref[0][:, :1], (glob_total, rows))
    bias_ref[window_len:] = jnp.where(spot <= query.astype(jnp.float32), 0.0, masked_value)


def over_last(left, right):
    return lax.dot_general(left, right, (((1,), (1,)), ((), ())), preferred_element_type=jnp.float32)


def over_first(left, right):
    return lax.dot_general(left, right, (((0,), (0,)), ((), ())), preferred_element_type=jnp.float32)


def attend_kernel(block_total, band_ref, gpos_ref, q_ref, *refs):
    blocks, (out_ref, lse_ref, bias_ref) = refs[:block_total], refs[block_total:]
    rows, q_width = q_ref.shape[1:]
    kv_width = blocks[0].shape[2] // 2
    heads, group = q_width // HD, q_width // kv_width
    window_len = rows * (block_total - 1)
    fill_bias(band_ref, gpos_ref, bias_ref, rows, window_len)
    starts = [rows * number for number in range(block_total)]
    pending = []
    for head in range(heads):
        left = head // group * HD
        queries = q_ref[0, :, head * HD : (head + 1) * HD]
        scores = [
            over_last(block[0, :, left : left + HD], queries)
            + bias_ref[start : start + block.shape[1]]
            for block, start in zip(blocks, starts)
        ]
        top = functools.reduce(jnp.maximum, [jnp.max(part, 0, keepdims=True) for part in scores])
        total = 0.0
        mixed = 0.0
        for block, part in zip(blocks, scores):
            weights = jnp.exp(part - top)
            total = total + jnp.sum(weights, 0, keepdims=True)
            mixed = mixed + over_first(
                block[0, :, kv_width + left : kv_width + left + HD], weights.astype(jnp.bfloat16)
            )
        lse_ref[0, head : head + 1, :] = top + jnp.log(total)
        pending.append(mixed / total)
        if len(pending) * HD == BLK or head == heads - 1:
            stop = (head + 1) * HD
            both = jnp.concatenate(pending, 0).T
            out_ref[0, :, stop - both.shape[1] : stop] = both.astype(jnp.bfloat16)
            pending = []


def attend(band, gpos, queries, blocks):
    seqs, rows, q_width = queries.shape
    heads = q_width // HD
    key_total = sum(block.shape[1] for block in blocks)

    def whole(array):
        return pl.BlockSpec((1,) + array.shape[1:], lambda s, *_: (s, 0, 0))

    out_shape = [
        jax.ShapeDtypeStruct((seqs, rows, q_width), jnp.bfloat16),
        jax.ShapeDtypeStruct((seqs, heads, rows), jnp.float32),
    ]
    return pl.pallas_call(
        functools.partial(attend_kernel, len(blocks)),
        out_shape=out_shape,
        grid_spec=pltpu.PrefetchScalarGridSpec(
            num_scalar_prefetch=1,
            grid=(seqs,),
            in_specs=[whole(array) for array in (gpos, queries, *blocks)],
            out_specs=[whole(array) for array in out_shape],
            scratch_shapes=[pltpu.VMEM((key_total, rows), jnp.float32)],
        ),
        compiler_params=pltpu.CompilerParams(vmem_limit_bytes=48 * 2**20),
        cost_estimate=pl.CostEstimate(
            flops=16 * seqs * heads * rows * key_total * HD,
            bytes_accessed=4 * queries.size,
            transcendentals=seqs * heads * rows * key_total,
        ),
    )(band, gpos, queries, *blocks)


def attend_back_kernel(block_total, band_ref, gpos_ref, cos_ref, sin_ref, q_ref, grad_ref, lse_ref, *refs):
    blocks = refs[:block_total]
    dq_ref = refs[block_total]
    out_refs = refs[block_total + 1 : 2 * block_total + 1]
    bias_ref = refs[-1]
    rows, q_width = q_ref.shape[1:]
    kv_width = blocks[0].shape[2] // 2
    heads, group = q_width // HD, q_width // kv_width
    window_len = rows * (block_total - 1)
    fill_bias(band_ref, gpos_ref, bias_ref, rows, window_len)
    starts = [rows * number for number in range(block_total)]
    pending = []
    for kv_head in range(kv_width // HD):
        left = kv_head * HD
        key_sums = [0.0] * block_total
        value_sums = [0.0] * block_total
        for head in range(kv_head * group, (kv_head + 1) * group):
            queries = q_ref[0, :, head * HD : (head + 1) * HD]
            grads = grad_ref[0, :, head * HD : (head + 1) * HD]
            lse = lse_ref[0, head : head + 1, :]
            soft, soft_grads = [], []
            inner = 0.0
            for number, (block, start) in enumerate(zip(blocks, starts)):
                part = over_last(block[0, :, left : left + HD], queries)
                part = jnp.exp(part + bias_ref[start : start + block.shape[1]] - lse)
                slope = over_last(block[0, :, kv_width + left : kv_width + left + HD], grads)
                inner = inner + jnp.sum(part * slope, 0, keepdims=True)
                soft.append(part)
                soft_grads.append(slope)
            turned = 0.0
            for number, block in enumerate(blocks):
                score_grads = (soft[number] * (soft_grads[number] - inner)).astype(jnp.bfloat16)
                value_sums[number] = value_sums[number] + jnp.dot(
                    soft[number].astype(jnp.bfloat16), grads, preferred_element_type=jnp.float32
                )
                key_sums[number] = key_sums[number] + jnp.dot(
                    score_grads, queries, preferred_element_type=jnp.float32
                )
                turned = turned + over_first(block[0, :, left : left + HD], score_grads)
            pending.append(turned)
            if len(pending) * HD == BLK or head == heads - 1:
                stop = (head + 1) * HD
                both = jnp.concatenate(pending, 0).T * HD ** (-0.5)
                pending = []
                first, other = half_turn(both * sin_ref[0])
                both = both * cos_ref[0] + jnp.where(first, other, -other)
                dq_ref[0, :, stop - both.shape[1] : stop] = both.astype(jnp.bfloat16)
        for number, out_ref in enumerate(out_refs):
            out_ref[0, :, left : left + HD] = key_sums[number].astype(out_ref.dtype)
            out_ref[0, :, kv_width + left : kv_width + left + HD] = value_sums[number].astype(
                out_ref.dtype
            )


def attend_back(band, gpos, cosines, sines, queries, grads, lse, blocks):
    seqs, rows, q_width = queries.shape
    heads = q_width // HD
    key_total = sum(block.shape[1] for block in blocks)

    def whole(array):
        return pl.BlockSpec((1,) + array.shape[1:], lambda s, *_: (s, 0, 0))

    table = pl.BlockSpec((1, rows, BLK), lambda s, *_: (0, 0, 0))
    out_shape = [jax.ShapeDtypeStruct(queries.shape, jnp.bfloat16)]
    for number, block in enumerate(blocks):
        own = number == len(blocks) - 2
        out_shape.append(jax.ShapeDtypeStruct(block.shape, jnp.float32 if own else jnp.bfloat16))
    return pl.pallas_call(
        functools.partial(attend_back_kernel, len(blocks)),
        out_shape=out_shape,
        grid_spec=pltpu.PrefetchScalarGridSpec(
            num_scalar_prefetch=1,
            grid=(seqs,),
            in_specs=[whole(gpos), table, table]
            + [whole(array) for array in (queries, grads, lse, *blocks)],
            out_specs=[whole(array) for array in out_shape],
            scratch_shapes=[pltpu.VMEM((key_total, rows), jnp.float32)],
        ),
        compiler_params=pltpu.CompilerParams(vmem_limit_bytes=48 * 2**20),
        cost_estimate=pl.CostEstimate(
            flops=40 * seqs * heads * rows * key_total * HD,
            bytes_accessed=8 * queries.size,
            transcendentals=seqs * heads * rows * key_total,
        ),
    )(band, gpos, cosines, sines, queries, grads, lse, *blocks)


def join_kernel(q_width, kv_width, dq_ref, own_ref, pick_ref, glob_ref, cos_ref, sin_ref, *refs):
    back_refs, out_ref = refs[:-1], refs[-1]
    out_ref[0, :, :q_width] = dq_ref[0]
    picked = lax.dot_general(
        pick_ref[0].astype(jnp.float32),
        glob_ref[0],
        (((0,), (0,)), ((), ())),
        precision=lax.Precision.HIGHEST,
        preferred_element_type=jnp.float32,
    )
    for start in range(0, 2 * kv_width, BLK):
        lanes = slice(start, start + BLK)
        total = own_ref[0, :, lanes] + picked[:, lanes]
        for back_ref in back_refs:
            total = total + back_ref[0, :, lanes].astype(jnp.float32)
        first, other = half_turn(total * sin_ref[0])
        turned = total * cos_ref[0] + jnp.where(first, other, -other)
        column = lax.broadcasted_iota(jnp.int32, total.shape, 1) + start
        turned = jnp.where(column >= kv_width, total, turned)
        out_ref[0, :, q_width + start : q_width + start + BLK] = turned.astype(jnp.bfloat16)


def join_grads(dq, own, picks, globs, cosines, sines, backs):
    seqs, rows, q_width = dq.shape
    kv_width = own.shape[2] // 2

    def whole(array):
        return pl.BlockSpec((1,) + array.shape[1:], lambda s: (s, 0, 0))

    table = pl.BlockSpec((1, rows, BLK), lambda s: (0, 0, 0))
    out_shape = jax.ShapeDtypeStruct((seqs, rows, q_width + 2 * kv_width), jnp.bfloat16)
    return pl.pallas_call(
        functools.partial(join_kernel, q_width, kv_width),
        out_shape=out_shape,
        grid=(seqs,),
        in_specs=[whole(dq), whole(own), whole(picks), whole(globs), table, table]
        + [whole(back) for back in backs],
        out_specs=whole(out_shape),
        cost_estimate=pl.CostEstimate(
            flops=20 * own.size, bytes_accessed=4 * dq.size + 12 * own.size, transcendentals=0
        ),
    )(dq, own, picks, globs, cosines, sines, *backs)


def adam_kernel(batch, meta, rates, *refs):
    master_ref, first_ref, second_ref, left_ref, right_ref = refs[:5]
    sources = refs[5:-6]
    new_first_ref, new_second_ref, new_master_ref, copy_ref, tiles, arrived = refs[-6:]
    step, steps = pl.program_id(0), pl.num_programs(0)
    slot = step % 2

    def fetch(at_step, at_slot):
        for place in range(batch):
            tile = at_step * batch + place
            for number, source in enumerate(sources):

                @pl.when(meta[0, tile] == number)
                def _(source=source, tile=tile, place=place):
                    top = pl.multiple_of(meta[2, tile], BLK)
                    left = pl.multiple_of(meta[3, tile], BLK)
                    pltpu.make_async_copy(
                        source.at[meta[1, tile], pl.ds(top, BLK), pl.ds(left, BLK)],
                        tiles.at[at_slot, place],
                        arrived.at[at_slot],
                    ).start()

    @pl.when(step == 0)
    def _():
        fetch(0, 0)

    @pl.when(step + 1 < steps)
    def _():
        fetch(step + 1, 1 - slot)

    pltpu.make_async_copy(tiles.at[slot], tiles.at[slot], arrived.at[slot]).wait()
    places = range(batch)
    lefts = [left_ref[place].astype(jnp.bfloat16) for place in places]
    rights = [right_ref[place].astype(jnp.bfloat16) for place in places]
    turned = [over_first(lefts[place], tiles[slot, place]).astype(jnp.bfloat16) for place in places]
    rotated = [
        jnp.dot(turned[place], rights[place], preferred_element_type=jnp.float32) for place in places
    ]
    directions = []
    for place in places:
        new_first = beta_one * first_ref[place] + (1.0 - beta_one) * rotated[place]
        new_second = beta_two * second_ref[place] + (1.0 - beta_two) * rotated[place] * rotated[place]
        direction = (new_first * (1.0 / (1.0 - beta_one**STEP))) / (
            jnp.sqrt(new_second * (1.0 / (1.0 - beta_two**STEP))) + adam_eps
        )
        new_first_ref[place] = new_first
        new_second_ref[place] = new_second
        directions.append(direction.astype(jnp.bfloat16))
    updates = [
        jnp.dot(lefts[place], directions[place], preferred_element_type=jnp.float32) for place in places
    ]
    updates = [over_last(updates[place].astype(jnp.bfloat16), rights[place]) for place in places]
    for place in places:
        old = master_ref[place]
        new_master = old - rates[step * batch + place] * (updates[place] + weight_decay * old)
        new_master_ref[place] = new_master
        copy_ref[place] = new_master.astype(jnp.bfloat16)


def adam(meta, rates, state, sources):
    count = state[0].shape[0]
    batch = max(size for size in range(1, 33) if count % size == 0)
    block = pl.BlockSpec((batch, BLK, BLK), lambda s, *_: (s, 0, 0))
    anywhere = pl.BlockSpec(memory_space=pl.ANY)
    shape = (count, BLK, BLK)
    return pl.pallas_call(
        functools.partial(adam_kernel, batch),
        out_shape=[jax.ShapeDtypeStruct(shape, jnp.float32)] * 3
        + [jax.ShapeDtypeStruct(shape, jnp.bfloat16)],
        grid_spec=pltpu.PrefetchScalarGridSpec(
            num_scalar_prefetch=2,
            grid=(count // batch,),
            in_specs=[block] * 5 + [anywhere] * len(sources),
            out_specs=[block] * 4,
            scratch_shapes=[
                pltpu.VMEM((2, batch, BLK, BLK), jnp.bfloat16),
                pltpu.SemaphoreType.DMA((2,)),
            ],
        ),
        compiler_params=pltpu.CompilerParams(vmem_limit_bytes=56 * 2**20),
        cost_estimate=pl.CostEstimate(
            flops=8 * count * BLK**3, bytes_accessed=36 * count * BLK**2, transcendentals=0
        ),
    )(meta, rates, *state, *sources)


def per_device(
    block_input,
    cotangent,
    glob_select,
    assignment,
    master,
    first_moment,
    second_moment,
    left_basis,
    right_basis,
    gains,
    gain_first,
    gain_second,
):
    band_total = lax.axis_size("fsdp")
    rep_total = lax.axis_size("rep")
    place = lax.axis_index("rep")
    band = lax.axis_index("fsdp")
    heads = H // rep_total
    kv_heads = KVH // rep_total
    q_width = heads * HD
    kv_width = kv_heads * HD
    tok_count = block_input.shape[1]
    own_count = master.shape[1]
    tile_total = own_count * rep_total
    aligned = square() and whole_tiles(band_total, rep_total)
    tile_order = assignment[0]

    residual = block_input[0].astype(jnp.float32)
    grad_top = cotangent[0]
    position = band * tok_count + jnp.arange(tok_count, dtype=jnp.int32)
    cosine_table, sine_table = rope_tables(position)
    wide_cosine = jnp.concatenate([cosine_table, cosine_table], 1)[None]
    wide_sine = jnp.concatenate([sine_table, sine_table], 1)[None]
    scale_one = lax.rsqrt(jnp.mean(residual * residual, -1, keepdims=True) + norm_eps)
    normed_one = (residual * scale_one * gains[0]).astype(jnp.bfloat16)
    pick_rows = glob_select[0]
    glob_total = pick_rows.shape[0]
    selector = pick_rows.astype(jnp.bfloat16)
    glob_pos_part = jnp.sum(pick_rows * position[None, :], 1)
    digits = jnp.concatenate([glob_pos_part // 256, glob_pos_part % 256]).astype(jnp.bfloat16)
    digits = jnp.pad(digits[None], ((0, 7), (0, D - 2 * glob_total)))
    glob_rows = jnp.dot(selector, normed_one, preferred_element_type=jnp.float32).astype(jnp.bfloat16)
    glob_rows = add_all(jnp.concatenate([glob_rows, digits], 0), "fsdp").astype(jnp.bfloat16)
    packed = [normed_one, glob_rows, selector.reshape(-1, D)]
    packed = jnp.concatenate(packed, 0)
    packed = jnp.pad(packed, ((0, -packed.shape[0] % 32), (0, 0)))

    def over_bands(slice_rows):
        return lax.all_gather(slice_rows, "fsdp", axis=0, tiled=True)

    if aligned:
        half = BLK // 2
        low, high = (master[0, :, rows].astype(jnp.bfloat16) for rows in (slice(0, half), slice(half, BLK)))
        layout = slice_layout(band_total, rep_total)
        attn_layout = jnp.asarray(np.concatenate(layout[:4], 2))
        wanted = jnp.take(tile_order, by_place(attn_layout).reshape(-1), mode="clip")
        meta = jnp.stack([wanted // own_count == place, wanted % own_count], 0).astype(jnp.int32)
        attn_part = place_tiles(low, high, meta, *attn_layout.shape)
        attn_part = rep_scatter(attn_part).astype(jnp.bfloat16)
        low, attn_part = lax.optimization_barrier((low, attn_part))
        slots = square_pieces(low)
        attn = over_bands(attn_part)
        *slots, attn = lax.optimization_barrier((*slots, attn))
        grids = [lax.dynamic_index_in_dim(jnp.asarray(grid), place, 0, False) for grid in layout]

        def find(wanted):
            wanted = jnp.take(tile_order, jnp.concatenate([grid.reshape(-1) for grid in wanted]), mode="clip")
            entry, row = (wanted // own_count) ^ place, wanted % own_count
            cut = own_count // 2
            high = (entry == 3) & (row >= cut)
            found = jnp.stack([jnp.where(high, 4, entry), jnp.where(high, row - cut, row)], 0)
            return found.astype(jnp.int32)

        all_grid = jnp.concatenate(grids[4:], 1)
        (first_part,) = gather_strips(slots, find([all_grid]), [all_grid.shape])
        packed, first_part = lax.optimization_barrier((packed, first_part))
        early = over_bands(first_part)
    packed_all = rep_gather(packed)
    if aligned:
        packed_all, high = lax.optimization_barrier((packed_all, high))
        later_slots = square_pieces(high)
    normed_one_all = packed_all[:, :tok_count].reshape(-1, D)
    at = tok_count + glob_total
    glob_digits = packed_all[:, at, : 2 * glob_total].astype(jnp.float32)
    glob_place = glob_digits[:, :glob_total] * 256.0 + glob_digits[:, glob_total:]
    at += 8
    selector_all = packed_all[:, at : at + selector.size // D].reshape(rep_total, glob_total, tok_count)

    if aligned:
        in_width = q_width + 2 * kv_width
        w_inner, w_output = attn[:, :in_width], attn[:, in_width:]
    else:
        slots = lax.all_gather(master[0].astype(jnp.bfloat16), "rep", axis=0, tiled=True)
        tiles = jnp.take(slots, tile_order, axis=0, mode="clip")
        slices = cut_slices(band_matrices(tiles, band_total), band_total, rep_total)
        w_inner = over_bands(jnp.concatenate(slices[0:3], 1))
        w_output = over_bands(slices[3])
        w_gate = over_bands(slices[4])
        w_up = over_bands(slices[5])
        w_down = over_bands(slices[6])

    w_output = by_place(w_output.reshape(rep_total, q_width, -1)).reshape(D, -1)

    def mul(rows, weight):
        return jnp.dot(rows, weight, preferred_element_type=jnp.float32)

    def mul_back(rows, weight):
        return lax.dot_general(rows, weight, (((1,), (1,)), ((), ())), preferred_element_type=jnp.float32)

    def weight_grad(rows, grad_rows):
        return lax.dot_general(
            rows, grad_rows, (((0,), (0,)), ((), ())), preferred_element_type=jnp.float32
        ).astype(jnp.bfloat16)

    def own_sum(partial):
        return rep_scatter(partial.astype(jnp.bfloat16).reshape(rep_total, tok_count, D))

    inner_rows = mul(packed_all.reshape(-1, D), w_inner).reshape(rep_total, -1, w_inner.shape[1])
    packed_all, normed_one_all = lax.optimization_barrier((packed_all, normed_one_all))
    queries, own_pairs = rope_rows(inner_rows, tok_count, 0, q_width, kv_width, wide_cosine, wide_sine)
    glob_cosine, glob_sine = rope_tables(glob_place.reshape(-1))
    glob_cosine = jnp.concatenate([glob_cosine, glob_cosine], 1).reshape(rep_total, glob_total, -1)
    glob_sine = jnp.concatenate([glob_sine, glob_sine], 1).reshape(rep_total, glob_total, -1)
    (glob_pairs,) = rope_rows(
        inner_rows, glob_total, tok_count // glob_total, q_width, kv_width, glob_cosine, glob_sine, False
    )
    back_count = (WINDOW + tok_count - 2) // tok_count
    odd = band % 2 == 1
    by_chip = back_count == 2 and band_total % 2 == 0
    if by_chip:
        two_back = shifted(own_pairs, "fsdp", 2)
        pair_blocks = [two_back, to_core(jnp.where(odd, two_back, own_pairs))]
    else:
        pair_blocks = [shifted(own_pairs, "fsdp", distance) for distance in range(back_count, 0, -1)]
    pair_blocks = pair_blocks + [own_pairs, glob_pairs]
    glob_spots = jnp.broadcast_to(glob_place[:, :, None], (rep_total, glob_total, BLK))
    band_number = band.astype(jnp.int32).reshape(1)
    attended_low, lse = attend(band_number, glob_spots, queries, pair_blocks)
    if aligned:
        *later_slots, attended_low, early = lax.optimization_barrier((*later_slots, attended_low, early))
        (last_part,) = gather_strips(later_slots, find([all_grid]), [all_grid.shape])

        def by_strips(gathered):
            return gathered.reshape(band_total, -1, all_grid.shape[0], half, gathered.shape[-1])

        early, late = by_strips(early), by_strips(over_bands(last_part))
    attended_all = rep_features(attended_low).reshape(-1, D)
    attended_all, grad_top_now = lax.optimization_barrier((attended_all, grad_top))
    top_first = gather_first(grad_top_now)
    columns = mul(attended_all, w_output).astype(jnp.bfloat16).reshape(rep_total, tok_count, -1)
    branch = by_place(rep_exchange(columns)).transpose(1, 0, 2).reshape(tok_count, D)
    middle = residual + branch.astype(jnp.float32)
    scale_two = lax.rsqrt(jnp.mean(middle * middle, -1, keepdims=True) + norm_eps)
    normed_two = (middle * scale_two * gains[1]).astype(jnp.bfloat16)
    top_first, normed_two = after(top_first, normed_two)
    normed_two_all = rep_gather(normed_two).reshape(-1, D)
    top_first, normed_two_all = after(top_first, normed_two_all)
    top_second = gather_second(top_first)

    if aligned:
        gate_rows, up_rows, activation = forward_products(normed_two_all, early, late, FF // rep_total)
        top_second, activation = after(top_second, activation)
        grad_top_all = gather_join(top_second).reshape(-1, D)
        g_down = weight_grad(activation, grad_top_all)
        grad_top_all, g_down = lax.optimization_barrier((grad_top_all, g_down))
        grad_gate, grad_up, pieces, branch_pieces = backward_products(
            grad_top_all, gate_rows, up_rows, activation, early, late
        )
        grad_normed_two = sum_pieces(*pieces)
    else:
        gate_rows = mul(normed_two_all, w_gate)
        up_rows = mul(normed_two_all, w_up)
        sigmoid_gate = jax.nn.sigmoid(gate_rows)
        silu_gate = gate_rows * sigmoid_gate
        activation = (silu_gate * up_rows).astype(jnp.bfloat16)
        grad_top_all = gather_join(top_second).reshape(-1, D)
        g_down = weight_grad(activation, grad_top_all)
        grad_act = mul_back(grad_top_all, w_down)
        grad_gate = (
            grad_act * up_rows * sigmoid_gate * (1.0 + gate_rows * (1.0 - sigmoid_gate))
        ).astype(jnp.bfloat16)
        grad_up = (grad_act * silu_gate).astype(jnp.bfloat16)
        grad_normed_two = own_sum(mul_back(grad_gate, w_gate) + mul_back(grad_up, w_up))
        branch_pieces = (mul(activation, w_down),)
    g_gate = weight_grad(normed_two_all, grad_gate)
    g_up = weight_grad(normed_two_all, grad_up)
    grad_normed_two, g_gate, g_up = lax.optimization_barrier((grad_normed_two, g_gate, g_up))

    def over_tokens(partial):
        return lax.psum_scatter(partial, "fsdp", scatter_dimension=0, tiled=True)

    s_down = over_tokens(g_down)
    s_gate = over_tokens(g_gate)

    grad_middle = grad_top.astype(jnp.float32) + norm_back(middle, scale_two, gains[1], grad_normed_two)
    grad_parts = grad_middle.astype(jnp.bfloat16).reshape(tok_count, rep_total, -1).transpose(1, 0, 2)
    grad_columns = rep_exchange(by_place(grad_parts)).reshape(rep_total * tok_count, -1)
    grad_attended = rep_features_sum(
        grad_columns.reshape(rep_total, tok_count, -1), w_output
    ).astype(jnp.bfloat16)
    g_output = weight_grad(attended_all, grad_columns)
    g_output = by_place(g_output.reshape(rep_total, q_width, -1)).reshape(D, -1)
    (s_down,), grad_attended = after((s_down,), grad_attended)
    down_first = gather_first(s_down)
    grad_queries, *grad_blocks = attend_back(
        band_number, glob_spots, wide_cosine, wide_sine, queries, grad_attended, lse, pair_blocks
    )
    down_first, *grad_blocks = after(down_first, *grad_blocks)
    down_second = gather_second(down_first)
    branch_pieces, *grad_blocks = after(tuple(branch_pieces), *grad_blocks)
    branch_first = sum_first(branch_pieces) if aligned else (own_sum(branch_pieces[0]),)
    if by_chip:
        came = to_core(grad_blocks[1])
        total = grad_blocks[0].astype(jnp.float32) + came.astype(jnp.float32)
        sent = jnp.where(odd, total.astype(jnp.bfloat16), grad_blocks[0])
        returned = [shifted(sent, "fsdp", -2), jnp.where(odd, jnp.zeros_like(came), came)]
    else:
        returned = [
            shifted(grad_blocks[back_count - distance], "fsdp", -distance)
            for distance in range(1, back_count + 1)
        ]
    glob_grads = add_all(grad_blocks[-1], "fsdp")
    g_up, glob_grads, *returned = lax.optimization_barrier((g_up, glob_grads, *returned))
    s_up = over_tokens(g_up)
    grad_inner = join_grads(
        grad_queries, grad_blocks[-2], selector_all, glob_grads, wide_cosine, wide_sine, returned
    ).reshape(-1, q_width + 2 * kv_width)
    branch_first, grad_inner = after(branch_first, grad_inner)
    down_second, grad_inner = after(down_second, grad_inner)
    s_down = gather_join(down_second)
    block_out = middle + (sum_second(branch_first) if aligned else branch_first[0])
    (s_gate,), grad_inner = after((s_gate,), grad_inner)
    gate_first = gather_first(s_gate)
    g_inner = weight_grad(normed_one_all, grad_inner)
    gate_first, grad_normed_parts, block_out = after(
        gate_first, mul_back(grad_inner, w_inner).astype(jnp.bfloat16), block_out
    )
    gate_second = gather_second(gate_first)
    grad_normed_parts = grad_normed_parts.reshape(rep_total, tok_count, D)
    if square():
        normed_first = sum_first(split_pieces(grad_normed_parts))
    else:
        normed_first = (rep_scatter(grad_normed_parts),)
    g_attn = with_layout_constraint(jnp.concatenate([g_inner, g_output], 1), Layout((0, 1)))
    normed_first, s_up, g_attn, *gate_second = after(normed_first, s_up, g_attn, *gate_second)
    s_gate = gather_join(gate_second)
    grad_normed_one = sum_second(normed_first) if square() else normed_first[0]
    s_up = rep_gather(s_up)
    s_attn = over_tokens(g_attn)
    grad_input = grad_middle + norm_back(residual, scale_one, gains[0], grad_normed_one)

    gain_terms = jnp.stack(
        [
            jnp.sum(grad_normed_one * residual * scale_one, 0),
            jnp.sum(grad_normed_two * middle * scale_two, 0),
        ]
    )
    square_terms = jnp.stack(
        [jnp.sum(residual * residual), jnp.sum(middle * middle), jnp.sum(block_out * block_out)]
    )
    sums = jnp.concatenate([gain_terms.reshape(-1), square_terms])

    sums = add_all(add_all(sums, "rep"), "fsdp")
    sums, s_attn, s_up = lax.optimization_barrier((sums, s_attn, s_up))
    gain_grad, square_total = sums[: 2 * D].reshape(2, D), sums[2 * D :]

    slot_ids = jnp.arange(tile_total, dtype=jnp.int32)
    inverse = jnp.sum(jnp.where(tile_order[None, :] == slot_ids[:, None], slot_ids[None, :], 0), 1)
    own_slots = place * own_count + jnp.arange(own_count, dtype=jnp.int32)
    owned_tiles = jnp.take(inverse, own_slots, mode="clip")
    if aligned:
        sources = [rep_gather(s_attn), s_gate, s_up, s_down]
        where = np.zeros((4, rep_total, tile_total), np.int32)
        first_col = 0
        for kind, grid in enumerate(layout):
            rows, cols = grid.shape[1:]
            first_col = 0 if kind >= 4 else first_col
            for there in range(rep_total):
                numbers = grid[there].reshape(-1)
                at = np.arange(rows * cols)
                where[0, :, numbers] = max(kind - 3, 0)
                where[2, :, numbers] = (at // cols * BLK)[:, None]
                where[3, :, numbers] = (at % cols * BLK + first_col)[:, None]
                for here in range(rep_total):
                    where[1, here, numbers] = here ^ there
            first_col += cols * BLK
        tile_spots = lax.dynamic_index_in_dim(jnp.asarray(where), place, 1, False)
        meta = jnp.take(tile_spots, owned_tiles, axis=1, mode="clip")
    else:
        splits = [0, q_width, q_width + kv_width, q_width + 2 * kv_width, s_attn.shape[1]]
        stacks = [rep_gather(s_attn[:, low:high]) for low, high in zip(splits, splits[1:])]
        stacks += [s_gate, s_up, s_down]
        sources = [band_tiles(join_slices(stacks, band_total, rep_total))]
        meta = jnp.stack([0 * owned_tiles, owned_tiles, 0 * owned_tiles, 0 * owned_tiles], 0)
    slot_rates = jnp.take(kind_rates(band_total), owned_tiles, mode="clip")
    new_first, new_second, new_master, master_copy = adam(
        meta,
        slot_rates,
        (master[0], first_moment[0], second_moment[0], left_basis[0], right_basis[0]),
        sources,
    )
    new_gain_first = beta_one * gain_first + (1.0 - beta_one) * gain_grad
    new_gain_second = beta_two * gain_second + (1.0 - beta_two) * gain_grad * gain_grad
    gain_step = (
        new_gain_first
        / (1.0 - beta_one**STEP)
        / (jnp.sqrt(new_gain_second / (1.0 - beta_two**STEP)) + adam_eps)
    )
    new_gains = gains - gain_rate * gain_step
    rms_stats = jnp.sqrt(square_total / (rep_total * band_total * tok_count * D))
    return (
        block_out[None],
        grad_input[None],
        new_first[None],
        new_second[None],
        new_master[None],
        master_copy[None],
        new_gain_first,
        new_gain_second,
        new_gains,
        rms_stats,
    )


def solution(mesh):
    in_specs = (
        P("rep", "fsdp", None),
        P("rep", "fsdp", None),
        P("rep", None, "fsdp"),
        P("fsdp", None),
        P("fsdp", "rep", None, None),
        P("fsdp", "rep", None, None),
        P("fsdp", "rep", None, None),
        P("fsdp", "rep", None, None),
        P("fsdp", "rep", None, None),
        P(),
        P(),
        P(),
    )
    out_specs = (
        P("rep", "fsdp", None),
        P("rep", "fsdp", None),
        P("fsdp", "rep", None, None),
        P("fsdp", "rep", None, None),
        P("fsdp", "rep", None, None),
        P("fsdp", "rep", None, None),
        P(),
        P(),
        P(),
        P(),
    )
    return jax.shard_map(
        per_device, mesh=mesh, in_specs=in_specs, out_specs=out_specs, check_vma=False
    )
```

```python
import functools

import jax
import jax.numpy as jnp
import numpy as np
from jax import lax
from jax.experimental import pallas as pl
from jax.experimental.layout import Layout, with_layout_constraint
from jax.experimental.pallas import tpu as pltpu
from jax.sharding import PartitionSpec as P

D = 2048
H = 32
KVH = 8
HD = 64
FF = 8192
WINDOW = 512
BLK = 128
STEP = 10


norm_eps = 1e-05
rope_theta = 500000.0
beta_one = 0.5
beta_two = 0.5
adam_eps = 1e-08
weight_decay = 0.1
gain_rate = 0.5
masked_value = -1e30


def matrix_shapes():
    kv_width = KVH * HD
    return [(D, D), (D, kv_width), (D, kv_width), (D, D), (D, FF), (D, FF), (FF, D)]


def kind_rates(band_total):
    rate_list = [
        D ** (-0.5),
        D ** (-0.5),
        D ** (-0.5),
        (D * 8 // WINDOW) ** (-0.5),
        D ** (-0.5),
        D ** (-0.5),
        FF ** (-0.5),
    ]
    pieces = []
    for (row_total, col_total), rate_value in zip(matrix_shapes(), rate_list):
        tile_count = row_total // band_total // BLK * (col_total // BLK)
        pieces.append(jnp.full((tile_count,), rate_value, jnp.float32))
    return jnp.concatenate(pieces)


def band_matrices(tiles, band_total):
    matrices = []
    offset = 0
    for row_total, col_total in matrix_shapes():
        band_rows = row_total // band_total
        tile_count = band_rows // BLK * (col_total // BLK)
        segment = tiles[offset : offset + tile_count].reshape(
            band_rows // BLK, col_total // BLK, BLK, BLK
        )
        matrices.append(segment.transpose(0, 2, 1, 3).reshape(band_rows, col_total))
        offset += tile_count
    return matrices


def band_tiles(matrices):
    pieces = []
    for matrix in matrices:
        row_count, col_count = matrix.shape
        segment = matrix.reshape(row_count // BLK, BLK, col_count // BLK, BLK).transpose(0, 2, 1, 3)
        pieces.append(segment.reshape(-1, BLK, BLK))
    return jnp.concatenate(pieces, 0)


def rope_tables(position):
    halves = jnp.arange(HD // 2, dtype=jnp.float32) * (2.0 / HD)
    frequency = rope_theta ** (-halves)
    angles = position.astype(jnp.float32)[:, None] * frequency[None, :]
    angles = jnp.concatenate([angles, angles], 1)
    return (jnp.cos(angles), jnp.sin(angles))


def rotate(vectors, cosine_table, sine_table):
    half_width = vectors.shape[-1] // 2
    turned = jnp.concatenate([-vectors[..., half_width:], vectors[..., :half_width]], -1)
    return vectors * cosine_table[:, None, :] + turned * sine_table[:, None, :]


def rotate_back(grad_rows, cosine_table, sine_table):
    half_width = grad_rows.shape[-1] // 2
    scaled = grad_rows * sine_table[:, None, :]
    turned = jnp.concatenate([scaled[..., half_width:], -scaled[..., :half_width]], -1)
    return grad_rows * cosine_table[:, None, :] + turned


def norm_back(values, row_scale, gain_row, grad_rows):
    weighted = grad_rows * gain_row
    return row_scale * weighted - values * row_scale**3 * jnp.mean(
        weighted * values, -1, keepdims=True
    )


def to_rep(block, distance):
    route = [(i, i ^ distance) for i in range(lax.axis_size("rep"))]
    return lax.ppermute(block, "rep", route)


def square():
    return lax.axis_size("rep") == 4


def gather_first(block):
    if not square():
        return (lax.all_gather(block, "rep", axis=0),)
    return block, to_rep(block, 1), to_rep(block, 2)


def gather_second(first):
    if not square():
        return first
    block, near, far = first
    cut = block.shape[0] // 2
    return block, near, far, to_rep(near[:cut], 2), to_rep(far[cut:], 1)


def gather_join(pieces):
    if not square():
        return pieces[0]
    return jnp.concatenate(pieces, 0).reshape((4,) + pieces[0].shape)


def square_pieces(block):
    return gather_second(gather_first(block))


def rep_gather(block):
    return gather_join(gather_second(gather_first(block)))


def after(values, *others):
    count = len(values)
    tied = lax.optimization_barrier((*values, *others))
    return tuple(tied[:count]), *tied[count:]


def rep_of(entry):
    place = lax.axis_index("rep")
    return place ^ entry if square() else entry


def rep_scatter(parts):
    if not square():
        flat = parts.reshape(-1, parts.shape[-1])
        return lax.psum_scatter(flat, "rep", scatter_dimension=0, tiled=True).astype(jnp.float32)
    return sum_pieces(*split_pieces(parts))


def split_pieces(parts):
    half = parts.shape[-1] // 2
    low, high = parts[..., :half], parts[..., half:]
    return jnp.stack([low[0], low[2]], 0), jnp.stack([low[1], low[3]], 0), high[:2], high[2:]


def sum_first(pieces):
    low_kept, low_sent, high_kept, high_sent = pieces
    parts = []
    for kept, sent, first in ((low_kept, low_sent, 1), (high_kept, high_sent, 2)):
        came = to_rep(sent, first)
        parts.append(kept[0].astype(jnp.float32) + came[0].astype(jnp.float32))
        parts.append((kept[1].astype(jnp.float32) + came[1].astype(jnp.float32)).astype(kept.dtype))
    return tuple(parts)


def sum_second(parts):
    low, low_other, high, high_other = parts
    low = low + to_rep(low_other, 2).astype(jnp.float32)
    high = high + to_rep(high_other, 1).astype(jnp.float32)
    return jnp.concatenate([low, high], -1)


def sum_pieces(*pieces):
    return sum_second(sum_first(pieces))


def add_all(value, axis):
    size = lax.axis_size(axis)
    total = value.astype(jnp.float32)
    distance = 1
    while distance < size:
        count = 2 if (size // distance).bit_length() % 2 == 0 else 4
        low = total.astype(value.dtype)
        others = []
        for step in range(1, count):
            route = [(i, i ^ (step * distance)) for i in range(size)]
            others.append(lax.ppermute(low, axis, route).astype(jnp.float32))
        total = total + others[0]
        if count == 4:
            total = total + (others[1] + others[2])
        distance *= count
    return total


def rep_features(block):
    if not square():
        return lax.all_gather(block, "rep", axis=2, tiled=True)
    own, near, far, low, high = square_pieces(block)
    return jnp.concatenate(
        [
            own,
            jnp.stack([near[1], near[0], near[3], near[2]], 0),
            jnp.stack([far[2], far[3], far[0], far[1]], 0),
            jnp.stack([high[1], high[0], low[1], low[0]], 0),
        ],
        2,
    )


def write_pieces(entry, rows, values, refs):
    low_kept, low_sent, high_kept, high_sent = refs
    half = low_kept.shape[-1]
    values = values.astype(jnp.bfloat16)
    (low_sent if entry % 2 else low_kept)[entry // 2, rows] = values[:, :half]
    (high_sent if entry // 2 else high_kept)[entry % 2, rows] = values[:, half:]


def swapped_kernel(x_ref, w_ref, *refs):
    reps, rows, _ = x_ref.shape
    width = w_ref.shape[0] // reps
    for entry in range(reps):
        weight = w_ref[entry * width : (entry + 1) * width]
        for there in range(reps):
            product = over_last(x_ref[there ^ entry], weight)
            write_pieces(entry, slice(there * rows, (there + 1) * rows), product, refs)


def rep_features_sum(columns, weight):
    reps, rows, depth = columns.shape
    width = weight.shape[0] // reps
    if square():
        pieces = pl.pallas_call(
            swapped_kernel,
            out_shape=[jax.ShapeDtypeStruct((2, reps * rows, width // 2), jnp.bfloat16)] * 4,
            compiler_params=pltpu.CompilerParams(vmem_limit_bytes=32 * 2**20),
            cost_estimate=pl.CostEstimate(
                flops=2 * reps * columns.size * width,
                bytes_accessed=10 * columns.size,
                transcendentals=0,
            ),
        )(columns, weight)
        total = sum_pieces(*pieces)
    else:
        product = over_last(columns.reshape(-1, depth), weight).astype(jnp.bfloat16)
        swapped = product.reshape(reps, rows, reps, width).transpose(2, 0, 1, 3)
        total = rep_scatter(swapped.reshape(reps, reps * rows, width))
    return total.reshape(reps, rows, width)


def rep_exchange(parts):
    if not square():
        return lax.all_to_all(parts, "rep", 0, 0)
    return jnp.stack([parts[0]] + [to_rep(parts[entry], entry) for entry in (1, 2, 3)], 0)


def by_place(parts):
    entries = [rep_of(entry) for entry in range(parts.shape[0])]
    return jnp.stack([lax.dynamic_index_in_dim(parts, entry, 0, False) for entry in entries], 0)


def to_core(block):
    return lax.ppermute(block, "fsdp", [(i, i ^ 1) for i in range(lax.axis_size("fsdp"))])


def shifted(block, axis, distance):
    devices = range(lax.axis_size(axis))
    route = [(i - distance, i) for i in devices if i - distance in devices]
    return lax.ppermute(block, axis, route)


def tile_offsets(band_total):
    offsets = [0]
    for row_total, col_total in matrix_shapes():
        offsets.append(offsets[-1] + row_total // band_total // BLK * (col_total // BLK))
    return offsets


def whole_tiles(band_total, rep_total):
    return KVH * HD // rep_total % BLK == 0 and FF // band_total // rep_total % BLK == 0


def slice_layout(band_total, rep_total):
    offsets = tile_offsets(band_total)
    layout = []
    for kind, (row_total, col_total) in enumerate(matrix_shapes()):
        rows, cols = row_total // band_total // BLK, col_total // BLK
        grid = offsets[kind] + np.arange(rows * cols).reshape(rows, cols)
        if kind == 6:
            layout.append(grid.reshape(rep_total, rows // rep_total, cols))
        elif kind in (4, 5):
            cut = grid.reshape(rows, band_total, rep_total, -1).transpose(2, 0, 1, 3)
            layout.append(cut.reshape(rep_total, rows, -1))
        else:
            layout.append(grid.reshape(rows, rep_total, -1).transpose(1, 0, 2))
    return layout


def tiles_to_matrix(tiles):
    rows, cols = tiles.shape[:2]
    return tiles.transpose(0, 2, 1, 3).reshape(rows * BLK, cols * BLK)


def matrix_to_tiles(matrix):
    rows, cols = matrix.shape
    cut = matrix.reshape(rows // BLK, BLK, cols // BLK, BLK)
    return cut.transpose(0, 2, 1, 3).reshape(-1, BLK, BLK)


def cut_slices(matrices, band_total, rep_total):
    place = lax.axis_index("rep")
    slices = []
    for kind, matrix in enumerate(matrices):
        rows, cols = matrix.shape
        if kind == 6:
            slices.append(lax.dynamic_slice_in_dim(matrix, place * (rows // rep_total), rows // rep_total, 0))
        elif kind in (4, 5):
            cut = matrix.reshape(rows, band_total, rep_total, -1)
            slices.append(lax.dynamic_index_in_dim(cut, place, 2, False).reshape(rows, -1))
        else:
            slices.append(lax.dynamic_slice_in_dim(matrix, place * (cols // rep_total), cols // rep_total, 1))
    return slices


def join_slices(stacks, band_total, rep_total):
    matrices = []
    for kind, stack in enumerate(stacks):
        rows, cols = stack.shape[1:]
        if kind == 6:
            matrices.append(stack.reshape(-1, cols))
        elif kind in (4, 5):
            cut = stack.reshape(rep_total, rows, band_total, -1).transpose(1, 2, 0, 3)
            matrices.append(cut.reshape(rows, -1))
        else:
            matrices.append(stack.transpose(1, 0, 2).reshape(rows, -1))
    return matrices


def gather_kernel(grids, meta, *refs):
    source_total = len(refs) - len(grids) - 1
    sources, targets, done = refs[:source_total], refs[source_total:-1], refs[-1]
    height = sources[0].shape[1]
    start = 0
    for place, (target, (rows, cols)) in enumerate(zip(targets, grids)):

        def one(tile, carry, target=target, rows=rows, cols=cols, start=start, place=place):
            kind = meta[0, start + tile]
            row = meta[1, start + tile]
            across = tile % cols
            top = pl.multiple_of((across // 2 * rows + tile // cols) * height, height)
            left = pl.multiple_of(across % 2 * BLK, BLK)
            for number, source in enumerate(sources):

                @pl.when(kind == number)
                def _(source=source):
                    pltpu.make_async_copy(
                        source.at[row], target.at[pl.ds(top, height), pl.ds(left, BLK)], done.at[place]
                    ).start()

            return carry

        lax.fori_loop(0, rows * cols, one, 0)
        start += rows * cols
    for place, target in enumerate(targets):
        pltpu.make_async_copy(target, target, done.at[place]).wait()


def gather_strips(sources, meta, grids):
    anywhere = pl.BlockSpec(memory_space=pl.ANY)
    height = sources[0].shape[1]
    out_shape = [
        jax.ShapeDtypeStruct((cols // 2 * rows * height, 2 * BLK), jnp.bfloat16) for rows, cols in grids
    ]
    return pl.pallas_call(
        functools.partial(gather_kernel, grids),
        out_shape=out_shape,
        grid_spec=pltpu.PrefetchScalarGridSpec(
            num_scalar_prefetch=1,
            grid=(1,),
            in_specs=[anywhere] * len(sources),
            out_specs=[pl.BlockSpec(shape.shape, lambda i, *_: (0, 0)) for shape in out_shape],
            scratch_shapes=[pltpu.SemaphoreType.DMA((len(grids),))],
        ),
        compiler_params=pltpu.CompilerParams(vmem_limit_bytes=32 * 2**20),
        cost_estimate=pl.CostEstimate(
            flops=0, bytes_accessed=sum(4 * shape.size for shape in out_shape), transcendentals=0
        ),
    )(meta, *sources)


def place_kernel(entries, rows, cols, meta, low, high, out_ref, done):
    out_ref[...] = jnp.zeros_like(out_ref)
    height = low.shape[1]

    def copies(tile):
        entry, rest = tile // (rows * cols), tile % (rows * cols)
        top = rest // cols * (2 * height)
        left = pl.multiple_of(rest % cols * BLK, BLK)
        return [
            pltpu.make_async_copy(
                half.at[meta[1, tile]],
                out_ref.at[entry, pl.ds(pl.multiple_of(top + part * height, height), height), pl.ds(left, BLK)],
                done.at[part],
            )
            for part, half in enumerate((low, high))
        ]

    def begin(tile, carry):
        @pl.when(meta[0, tile] == 1)
        def _():
            for copy in copies(tile):
                copy.start()

        return carry

    def finish(tile, carry):
        @pl.when(meta[0, tile] == 1)
        def _():
            for copy in copies(tile):
                copy.wait()

        return carry

    lax.fori_loop(0, entries * rows * cols, begin, 0)
    lax.fori_loop(0, entries * rows * cols, finish, 0)


def place_tiles(low, high, meta, entries, rows, cols):
    shape = (entries, rows * BLK, cols * BLK)
    anywhere = pl.BlockSpec(memory_space=pl.ANY)
    return pl.pallas_call(
        functools.partial(place_kernel, entries, rows, cols),
        out_shape=jax.ShapeDtypeStruct(shape, jnp.bfloat16),
        grid_spec=pltpu.PrefetchScalarGridSpec(
            num_scalar_prefetch=1,
            grid=(1,),
            in_specs=[anywhere, anywhere],
            out_specs=pl.BlockSpec(shape, lambda i, *_: (0, 0, 0)),
            scratch_shapes=[pltpu.SemaphoreType.DMA((2,))],
        ),
        compiler_params=pltpu.CompilerParams(vmem_limit_bytes=32 * 2**20),
        cost_estimate=pl.CostEstimate(
            flops=0, bytes_accessed=4 * entries * rows * cols * BLK * BLK, transcendentals=0
        ),
    )(meta, low, high)


def half_turn(values):
    lane = lax.broadcasted_iota(jnp.int32, values.shape, 1)
    lanes = values.shape[1]
    first = lane % HD < HD // 2
    return first, jnp.where(
        first, pltpu.roll(values, lanes - HD // 2, 1), pltpu.roll(values, HD // 2, 1)
    )


def strip_copies(early, late, target, done):
    return [
        pltpu.make_async_copy(half, target.at[:, :, number], done.at[number])
        for number, half in enumerate((early, late))
    ]


def forward_kernel(x_ref, early, late, gate_ref, up_ref, act_ref, weights, done):
    step, steps = pl.program_id(0), pl.num_programs(0)
    slot = step % 2
    width = weights.shape[-1]

    def copies(number, at_step, at_slot):
        strip = number * steps + at_step
        return strip_copies(
            early.at[:, strip], late.at[:, strip], weights.at[number, at_slot], done.at[number, at_slot]
        )

    def fetch(at_step, at_slot):
        for number in range(2):
            for copy in copies(number, at_step, at_slot):
                copy.start()

    @pl.when(step == 0)
    def _():
        fetch(0, 0)

    @pl.when(step + 1 < steps)
    def _():
        fetch(step + 1, 1 - slot)

    for number in range(2):
        for copy in copies(number, step, slot):
            copy.wait()
    gate_weight, up_weight = (weights[number, slot].reshape(-1, width) for number in range(2))
    chunk = min(2 * BLK, x_ref.shape[0])
    for first in range(0, x_ref.shape[0], chunk):
        rows = slice(first, first + chunk)
        gate = jnp.dot(x_ref[rows], gate_weight, preferred_element_type=jnp.float32)
        up = jnp.dot(x_ref[rows], up_weight, preferred_element_type=jnp.float32)
        gate_ref[rows] = gate.astype(jnp.bfloat16)
        up_ref[rows] = up.astype(jnp.bfloat16)
        act_ref[rows] = (gate * jax.nn.sigmoid(gate) * up).astype(jnp.bfloat16)


def forward_products(rows, early, late, columns):
    tokens, depth = rows.shape
    bands, _, tiles, half, width = early.shape
    block = pl.BlockSpec((tokens, width), lambda n: (0, n))
    anywhere = pl.BlockSpec(memory_space=pl.ANY)
    return pl.pallas_call(
        forward_kernel,
        out_shape=[jax.ShapeDtypeStruct((tokens, columns), jnp.bfloat16)] * 3,
        grid=(columns // width,),
        in_specs=[pl.BlockSpec(rows.shape, lambda n: (0, 0)), anywhere, anywhere],
        out_specs=[block] * 3,
        scratch_shapes=[
            pltpu.VMEM((2, 2, bands, tiles, 2, half, width), jnp.bfloat16),
            pltpu.SemaphoreType.DMA((2, 2, 2)),
        ],
        compiler_params=pltpu.CompilerParams(vmem_limit_bytes=48 * 2**20),
        cost_estimate=pl.CostEstimate(
            flops=tokens * depth * columns // 8, bytes_accessed=2 * rows.size, transcendentals=0
        ),
    )(rows, early, late)


def backward_kernel(top_ref, gate_ref, up_ref, act_ref, early, late, late_down, *refs):
    dgate_ref, dup_ref = refs[:2]
    pieces, branch_pieces = refs[2:6], refs[6:10]
    weights, downs, total, branch, done, down_done = refs[10:]
    step, steps = pl.program_id(0), pl.num_programs(0)
    slot = step % 2
    strips, width = downs.shape[1], downs.shape[-1]

    def down_copies(at_step, at_slot):
        wanted = pl.ds(2 * steps, strips)
        return strip_copies(
            early.at[at_step, wanted], late_down.at[at_step], downs.at[at_slot], down_done.at[at_slot]
        )

    def copies(number, at_step, at_slot):
        strip = number * steps + at_step
        return strip_copies(
            early.at[:, strip], late.at[:, strip], weights.at[number, at_slot], done.at[number, at_slot]
        )

    def fetch(at_step, at_slot):
        for copy in down_copies(at_step, at_slot):
            copy.start()
        for number in range(2):
            for copy in copies(number, at_step, at_slot):
                copy.start()

    @pl.when(step == 0)
    def _():
        fetch(0, 0)
        total[...] = jnp.zeros_like(total)
        branch[...] = jnp.zeros_like(branch)

    @pl.when(step + 1 < steps)
    def _():
        fetch(step + 1, 1 - slot)

    for copy in down_copies(step, slot):
        copy.wait()
    for number in range(2):
        for copy in copies(number, step, slot):
            copy.wait()
    gate_weight, up_weight = (weights[number, slot].reshape(-1, width) for number in range(2))
    chunk = min(4 * BLK, top_ref.shape[0])
    for first in range(0, top_ref.shape[0], chunk):
        rows = slice(first, first + chunk)
        grad_act = 0.0
        for strip in range(strips):
            lanes = slice(strip * width, (strip + 1) * width)
            down = downs[slot, strip].reshape(-1, width)
            grad_act = grad_act + over_last(top_ref[rows, lanes], down)
            branch[rows, lanes] += jnp.dot(act_ref[rows], down, preferred_element_type=jnp.float32)
        gate = gate_ref[rows].astype(jnp.float32)
        up = up_ref[rows].astype(jnp.float32)
        sigmoid_gate = jax.nn.sigmoid(gate)
        grad_gate = grad_act * up * sigmoid_gate * (1.0 + gate * (1.0 - sigmoid_gate))
        grad_gate = grad_gate.astype(jnp.bfloat16)
        grad_up = (grad_act * (gate * sigmoid_gate)).astype(jnp.bfloat16)
        dgate_ref[rows] = grad_gate
        dup_ref[rows] = grad_up
        total[rows] += over_last(grad_gate, gate_weight) + over_last(grad_up, up_weight)

    @pl.when(step == steps - 1)
    def _():
        rows = total.shape[0] // 4
        for entry in range(4):
            part = slice(entry * rows, (entry + 1) * rows)
            write_pieces(entry, slice(0, rows), total[part], pieces)
            write_pieces(entry, slice(0, rows), branch[part], branch_pieces)


def backward_products(top, gate, up, act, early, late, late_down):
    tokens, depth = top.shape
    columns = gate.shape[1]
    bands, _, tiles, half, width = early.shape
    strips = depth // width
    block = pl.BlockSpec((tokens, width), lambda n: (0, n))
    anywhere = pl.BlockSpec(memory_space=pl.ANY)
    piece = jax.ShapeDtypeStruct((2, tokens // 4, depth // 2), jnp.bfloat16)
    grads = jax.ShapeDtypeStruct((tokens, columns), jnp.bfloat16)
    outs = pl.pallas_call(
        backward_kernel,
        out_shape=[grads] * 2 + [piece] * 8,
        grid=(columns // width,),
        in_specs=[pl.BlockSpec(top.shape, lambda n: (0, 0))] + [block] * 3 + [anywhere] * 3,
        out_specs=[block] * 2 + [pl.BlockSpec(piece.shape, lambda n: (0, 0, 0))] * 8,
        scratch_shapes=[
            pltpu.VMEM((2, 2, bands, tiles, 2, half, width), jnp.bfloat16),
            pltpu.VMEM((2, strips, tiles, 2, half, width), jnp.bfloat16),
            pltpu.VMEM((tokens, depth), jnp.float32),
            pltpu.VMEM((tokens, depth), jnp.float32),
            pltpu.SemaphoreType.DMA((2, 2, 2)),
            pltpu.SemaphoreType.DMA((2, 2)),
        ],
        compiler_params=pltpu.CompilerParams(vmem_limit_bytes=60 * 2**20),
        cost_estimate=pl.CostEstimate(
            flops=8 * tokens * depth * columns, bytes_accessed=8 * columns * depth, transcendentals=0
        ),
    )(top, gate, up, act, early, late, late_down)
    return outs[0], outs[1], outs[2:6], outs[6:10]


def rope_kernel(q_width, kv_width, x_ref, cos_ref, sin_ref, *outs):
    width = x_ref.shape[-1]
    for start in range(0, width, BLK):
        values = x_ref[0, :, start : start + BLK]
        first, turned = half_turn(values)
        sines = sin_ref[0]
        turned_rows = values * cos_ref[0] + turned * jnp.where(first, -sines, sines)
        if start + BLK > q_width + kv_width:
            column = lax.broadcasted_iota(jnp.int32, values.shape, 1) + start
            turned_rows = jnp.where(column >= q_width + kv_width, values, turned_rows)
        if start < q_width:
            outs[0][0, :, start : start + BLK] = (turned_rows * HD ** (-0.5)).astype(jnp.bfloat16)
        else:
            outs[-1][0, :, start - q_width : start - q_width + BLK] = turned_rows.astype(jnp.bfloat16)


def rope_rows(inner, rows, row_block, q_width, kv_width, cosines, sines, with_queries=True):
    seqs, _, width = inner.shape
    shared = cosines.shape[0] == 1
    table = pl.BlockSpec((1, rows, BLK), lambda s: (0 if shared else s, 0, 0))
    widths = [q_width, 2 * kv_width]
    column_block = 0
    if not with_queries:
        width, column_block = 2 * kv_width, q_width // (2 * kv_width)
        widths, q_width = widths[1:], 0
    return pl.pallas_call(
        functools.partial(rope_kernel, q_width, kv_width),
        out_shape=[jax.ShapeDtypeStruct((seqs, rows, w), jnp.bfloat16) for w in widths],
        grid=(seqs,),
        in_specs=[pl.BlockSpec((1, rows, width), lambda s: (s, row_block, column_block)), table, table],
        out_specs=[pl.BlockSpec((1, rows, w), lambda s: (s, 0, 0)) for w in widths],
        cost_estimate=pl.CostEstimate(
            flops=6 * seqs * rows * width, bytes_accessed=6 * seqs * rows * width, transcendentals=0
        ),
    )(inner, cosines, sines)


def fill_bias(band_ref, gpos_ref, bias_ref, rows, window_len):
    band = band_ref[0]

    @pl.when(pl.program_id(0) == 0)
    def _():
        key = lax.broadcasted_iota(jnp.int32, (window_len, rows), 0) + (
            band * rows - (window_len - rows)
        )
        query = lax.broadcasted_iota(jnp.int32, (window_len, rows), 1) + band * rows
        inside = (key > query - WINDOW) & (key <= query) & (key >= 0)
        bias_ref[:window_len] = jnp.where(inside, 0.0, masked_value)

    glob_total = gpos_ref.shape[1]
    query = lax.broadcasted_iota(jnp.int32, (glob_total, rows), 1) + (band * rows - WINDOW)
    spot = jnp.broadcast_to(gpos_ref[0][:, :1], (glob_total, rows))
    bias_ref[window_len:] = jnp.where(spot <= query.astype(jnp.float32), 0.0, masked_value)


def over_last(left, right):
    return lax.dot_general(left, right, (((1,), (1,)), ((), ())), preferred_element_type=jnp.float32)


def over_first(left, right):
    return lax.dot_general(left, right, (((0,), (0,)), ((), ())), preferred_element_type=jnp.float32)


def attend_kernel(block_total, band_ref, gpos_ref, q_ref, *refs):
    blocks, (out_ref, lse_ref, bias_ref) = refs[:block_total], refs[block_total:]
    rows, q_width = q_ref.shape[1:]
    kv_width = blocks[0].shape[2] // 2
    heads, group = q_width // HD, q_width // kv_width
    window_len = rows * (block_total - 1)
    fill_bias(band_ref, gpos_ref, bias_ref, rows, window_len)
    starts = [rows * number for number in range(block_total)]
    pending = []
    for head in range(heads):
        left = head // group * HD
        queries = q_ref[0, :, head * HD : (head + 1) * HD]
        scores = [
            over_last(block[0, :, left : left + HD], queries)
            + bias_ref[start : start + block.shape[1]]
            for block, start in zip(blocks, starts)
        ]
        top = functools.reduce(jnp.maximum, [jnp.max(part, 0, keepdims=True) for part in scores])
        total = 0.0
        mixed = 0.0
        for block, part in zip(blocks, scores):
            weights = jnp.exp(part - top)
            total = total + jnp.sum(weights, 0, keepdims=True)
            mixed = mixed + over_first(
                block[0, :, kv_width + left : kv_width + left + HD], weights.astype(jnp.bfloat16)
            )
        lse_ref[0, head : head + 1, :] = top + jnp.log(total)
        pending.append(mixed / total)
        if len(pending) * HD == BLK or head == heads - 1:
            stop = (head + 1) * HD
            both = jnp.concatenate(pending, 0).T
            out_ref[0, :, stop - both.shape[1] : stop] = both.astype(jnp.bfloat16)
            pending = []


def attend(band, gpos, queries, blocks):
    seqs, rows, q_width = queries.shape
    heads = q_width // HD
    key_total = sum(block.shape[1] for block in blocks)

    def whole(array):
        return pl.BlockSpec((1,) + array.shape[1:], lambda s, *_: (s, 0, 0))

    out_shape = [
        jax.ShapeDtypeStruct((seqs, rows, q_width), jnp.bfloat16),
        jax.ShapeDtypeStruct((seqs, heads, rows), jnp.float32),
    ]
    return pl.pallas_call(
        functools.partial(attend_kernel, len(blocks)),
        out_shape=out_shape,
        grid_spec=pltpu.PrefetchScalarGridSpec(
            num_scalar_prefetch=1,
            grid=(seqs,),
            in_specs=[whole(array) for array in (gpos, queries, *blocks)],
            out_specs=[whole(array) for array in out_shape],
            scratch_shapes=[pltpu.VMEM((key_total, rows), jnp.float32)],
        ),
        compiler_params=pltpu.CompilerParams(vmem_limit_bytes=48 * 2**20),
        cost_estimate=pl.CostEstimate(
            flops=16 * seqs * heads * rows * key_total * HD,
            bytes_accessed=4 * queries.size,
            transcendentals=seqs * heads * rows * key_total,
        ),
    )(band, gpos, queries, *blocks)


def attend_back_kernel(block_total, band_ref, gpos_ref, cos_ref, sin_ref, q_ref, grad_ref, lse_ref, *refs):
    blocks = refs[:block_total]
    dq_ref = refs[block_total]
    out_refs = refs[block_total + 1 : 2 * block_total + 1]
    bias_ref = refs[-1]
    rows, q_width = q_ref.shape[1:]
    kv_width = blocks[0].shape[2] // 2
    heads, group = q_width // HD, q_width // kv_width
    window_len = rows * (block_total - 1)
    fill_bias(band_ref, gpos_ref, bias_ref, rows, window_len)
    starts = [rows * number for number in range(block_total)]
    pending = []
    for kv_head in range(kv_width // HD):
        left = kv_head * HD
        key_sums = [0.0] * block_total
        value_sums = [0.0] * block_total
        for head in range(kv_head * group, (kv_head + 1) * group):
            queries = q_ref[0, :, head * HD : (head + 1) * HD]
            grads = grad_ref[0, :, head * HD : (head + 1) * HD]
            lse = lse_ref[0, head : head + 1, :]
            soft, soft_grads = [], []
            inner = 0.0
            for number, (block, start) in enumerate(zip(blocks, starts)):
                part = over_last(block[0, :, left : left + HD], queries)
                part = jnp.exp(part + bias_ref[start : start + block.shape[1]] - lse)
                slope = over_last(block[0, :, kv_width + left : kv_width + left + HD], grads)
                inner = inner + jnp.sum(part * slope, 0, keepdims=True)
                soft.append(part)
                soft_grads.append(slope)
            turned = 0.0
            for number, block in enumerate(blocks):
                score_grads = (soft[number] * (soft_grads[number] - inner)).astype(jnp.bfloat16)
                value_sums[number] = value_sums[number] + jnp.dot(
                    soft[number].astype(jnp.bfloat16), grads, preferred_element_type=jnp.float32
                )
                key_sums[number] = key_sums[number] + jnp.dot(
                    score_grads, queries, preferred_element_type=jnp.float32
                )
                turned = turned + over_first(block[0, :, left : left + HD], score_grads)
            pending.append(turned)
            if len(pending) * HD == BLK or head == heads - 1:
                stop = (head + 1) * HD
                both = jnp.concatenate(pending, 0).T * HD ** (-0.5)
                pending = []
                first, other = half_turn(both * sin_ref[0])
                both = both * cos_ref[0] + jnp.where(first, other, -other)
                dq_ref[0, :, stop - both.shape[1] : stop] = both.astype(jnp.bfloat16)
        for number, out_ref in enumerate(out_refs):
            out_ref[0, :, left : left + HD] = key_sums[number].astype(out_ref.dtype)
            out_ref[0, :, kv_width + left : kv_width + left + HD] = value_sums[number].astype(
                out_ref.dtype
            )


def attend_back(band, gpos, cosines, sines, queries, grads, lse, blocks):
    seqs, rows, q_width = queries.shape
    heads = q_width // HD
    key_total = sum(block.shape[1] for block in blocks)

    def whole(array):
        return pl.BlockSpec((1,) + array.shape[1:], lambda s, *_: (s, 0, 0))

    table = pl.BlockSpec((1, rows, BLK), lambda s, *_: (0, 0, 0))
    out_shape = [jax.ShapeDtypeStruct(queries.shape, jnp.bfloat16)]
    for number, block in enumerate(blocks):
        own = number == len(blocks) - 2
        out_shape.append(jax.ShapeDtypeStruct(block.shape, jnp.float32 if own else jnp.bfloat16))
    return pl.pallas_call(
        functools.partial(attend_back_kernel, len(blocks)),
        out_shape=out_shape,
        grid_spec=pltpu.PrefetchScalarGridSpec(
            num_scalar_prefetch=1,
            grid=(seqs,),
            in_specs=[whole(gpos), table, table]
            + [whole(array) for array in (queries, grads, lse, *blocks)],
            out_specs=[whole(array) for array in out_shape],
            scratch_shapes=[pltpu.VMEM((key_total, rows), jnp.float32)],
        ),
        compiler_params=pltpu.CompilerParams(vmem_limit_bytes=48 * 2**20),
        cost_estimate=pl.CostEstimate(
            flops=40 * seqs * heads * rows * key_total * HD,
            bytes_accessed=8 * queries.size,
            transcendentals=seqs * heads * rows * key_total,
        ),
    )(band, gpos, cosines, sines, queries, grads, lse, *blocks)


def join_kernel(q_width, kv_width, dq_ref, own_ref, pick_ref, glob_ref, cos_ref, sin_ref, *refs):
    back_refs, out_ref = refs[:-1], refs[-1]
    out_ref[0, :, :q_width] = dq_ref[0]
    picked = lax.dot_general(
        pick_ref[0].astype(jnp.float32),
        glob_ref[0],
        (((0,), (0,)), ((), ())),
        precision=lax.Precision.HIGHEST,
        preferred_element_type=jnp.float32,
    )
    for start in range(0, 2 * kv_width, BLK):
        lanes = slice(start, start + BLK)
        total = own_ref[0, :, lanes] + picked[:, lanes]
        for back_ref in back_refs:
            total = total + back_ref[0, :, lanes].astype(jnp.float32)
        first, other = half_turn(total * sin_ref[0])
        turned = total * cos_ref[0] + jnp.where(first, other, -other)
        column = lax.broadcasted_iota(jnp.int32, total.shape, 1) + start
        turned = jnp.where(column >= kv_width, total, turned)
        out_ref[0, :, q_width + start : q_width + start + BLK] = turned.astype(jnp.bfloat16)


def join_grads(dq, own, picks, globs, cosines, sines, backs):
    seqs, rows, q_width = dq.shape
    kv_width = own.shape[2] // 2

    def whole(array):
        return pl.BlockSpec((1,) + array.shape[1:], lambda s: (s, 0, 0))

    table = pl.BlockSpec((1, rows, BLK), lambda s: (0, 0, 0))
    out_shape = jax.ShapeDtypeStruct((seqs, rows, q_width + 2 * kv_width), jnp.bfloat16)
    return pl.pallas_call(
        functools.partial(join_kernel, q_width, kv_width),
        out_shape=out_shape,
        grid=(seqs,),
        in_specs=[whole(dq), whole(own), whole(picks), whole(globs), table, table]
        + [whole(back) for back in backs],
        out_specs=whole(out_shape),
        cost_estimate=pl.CostEstimate(
            flops=20 * own.size, bytes_accessed=4 * dq.size + 12 * own.size, transcendentals=0
        ),
    )(dq, own, picks, globs, cosines, sines, *backs)


def adam_kernel(batch, meta, rates, *refs):
    master_ref, first_ref, second_ref, left_ref, right_ref = refs[:5]
    sources = refs[5:-6]
    new_first_ref, new_second_ref, new_master_ref, copy_ref, tiles, arrived = refs[-6:]
    step, steps = pl.program_id(0), pl.num_programs(0)
    slot = step % 2

    def fetch(at_step, at_slot):
        for place in range(batch):
            tile = at_step * batch + place
            for number, source in enumerate(sources):

                @pl.when(meta[0, tile] == number)
                def _(source=source, tile=tile, place=place):
                    top = pl.multiple_of(meta[2, tile], BLK)
                    left = pl.multiple_of(meta[3, tile], BLK)
                    pltpu.make_async_copy(
                        source.at[meta[1, tile], pl.ds(top, BLK), pl.ds(left, BLK)],
                        tiles.at[at_slot, place],
                        arrived.at[at_slot],
                    ).start()

    @pl.when(step == 0)
    def _():
        fetch(0, 0)

    @pl.when(step + 1 < steps)
    def _():
        fetch(step + 1, 1 - slot)

    pltpu.make_async_copy(tiles.at[slot], tiles.at[slot], arrived.at[slot]).wait()
    places = range(batch)
    lefts = [left_ref[place].astype(jnp.bfloat16) for place in places]
    rights = [right_ref[place].astype(jnp.bfloat16) for place in places]
    turned = [over_first(lefts[place], tiles[slot, place]).astype(jnp.bfloat16) for place in places]
    rotated = [
        jnp.dot(turned[place], rights[place], preferred_element_type=jnp.float32) for place in places
    ]
    directions = []
    for place in places:
        new_first = beta_one * first_ref[place] + (1.0 - beta_one) * rotated[place]
        new_second = beta_two * second_ref[place] + (1.0 - beta_two) * rotated[place] * rotated[place]
        direction = (new_first * (1.0 / (1.0 - beta_one**STEP))) / (
            jnp.sqrt(new_second * (1.0 / (1.0 - beta_two**STEP))) + adam_eps
        )
        new_first_ref[place] = new_first
        new_second_ref[place] = new_second
        directions.append(direction.astype(jnp.bfloat16))
    updates = [
        jnp.dot(lefts[place], directions[place], preferred_element_type=jnp.float32) for place in places
    ]
    updates = [over_last(updates[place].astype(jnp.bfloat16), rights[place]) for place in places]
    for place in places:
        old = master_ref[place]
        new_master = old - rates[step * batch + place] * (updates[place] + weight_decay * old)
        new_master_ref[place] = new_master
        copy_ref[place] = new_master.astype(jnp.bfloat16)


def adam(meta, rates, state, sources):
    count = state[0].shape[0]
    batch = max(size for size in range(1, 33) if count % size == 0)
    block = pl.BlockSpec((batch, BLK, BLK), lambda s, *_: (s, 0, 0))
    anywhere = pl.BlockSpec(memory_space=pl.ANY)
    shape = (count, BLK, BLK)
    return pl.pallas_call(
        functools.partial(adam_kernel, batch),
        out_shape=[jax.ShapeDtypeStruct(shape, jnp.float32)] * 3
        + [jax.ShapeDtypeStruct(shape, jnp.bfloat16)],
        grid_spec=pltpu.PrefetchScalarGridSpec(
            num_scalar_prefetch=2,
            grid=(count // batch,),
            in_specs=[block] * 5 + [anywhere] * len(sources),
            out_specs=[block] * 4,
            scratch_shapes=[
                pltpu.VMEM((2, batch, BLK, BLK), jnp.bfloat16),
                pltpu.SemaphoreType.DMA((2,)),
            ],
        ),
        compiler_params=pltpu.CompilerParams(vmem_limit_bytes=56 * 2**20),
        cost_estimate=pl.CostEstimate(
            flops=8 * count * BLK**3, bytes_accessed=36 * count * BLK**2, transcendentals=0
        ),
    )(meta, rates, *state, *sources)


def per_device(
    block_input,
    cotangent,
    glob_select,
    assignment,
    master,
    first_moment,
    second_moment,
    left_basis,
    right_basis,
    gains,
    gain_first,
    gain_second,
):
    band_total = lax.axis_size("fsdp")
    rep_total = lax.axis_size("rep")
    place = lax.axis_index("rep")
    band = lax.axis_index("fsdp")
    heads = H // rep_total
    kv_heads = KVH // rep_total
    q_width = heads * HD
    kv_width = kv_heads * HD
    tok_count = block_input.shape[1]
    own_count = master.shape[1]
    tile_total = own_count * rep_total
    aligned = square() and whole_tiles(band_total, rep_total)
    tile_order = assignment[0]

    residual = block_input[0].astype(jnp.float32)
    grad_top = cotangent[0]
    position = band * tok_count + jnp.arange(tok_count, dtype=jnp.int32)
    cosine_table, sine_table = rope_tables(position)
    wide_cosine = jnp.concatenate([cosine_table, cosine_table], 1)[None]
    wide_sine = jnp.concatenate([sine_table, sine_table], 1)[None]
    scale_one = lax.rsqrt(jnp.mean(residual * residual, -1, keepdims=True) + norm_eps)
    normed_one = (residual * scale_one * gains[0]).astype(jnp.bfloat16)
    pick_rows = glob_select[0]
    glob_total = pick_rows.shape[0]
    selector = pick_rows.astype(jnp.bfloat16)
    glob_pos_part = jnp.sum(pick_rows * position[None, :], 1)
    digits = jnp.concatenate([glob_pos_part // 256, glob_pos_part % 256]).astype(jnp.bfloat16)
    digits = jnp.pad(digits[None], ((0, 7), (0, D - 2 * glob_total)))
    glob_rows = jnp.dot(selector, normed_one, preferred_element_type=jnp.float32).astype(jnp.bfloat16)
    glob_rows = add_all(jnp.concatenate([glob_rows, digits], 0), "fsdp").astype(jnp.bfloat16)
    packed = [normed_one, glob_rows, selector.reshape(-1, D)]
    packed = jnp.concatenate(packed, 0)
    packed = jnp.pad(packed, ((0, -packed.shape[0] % 32), (0, 0)))

    def over_bands(slice_rows):
        return lax.all_gather(slice_rows, "fsdp", axis=0, tiled=True)

    if aligned:
        half = BLK // 2
        low, high = (master[0, :, rows].astype(jnp.bfloat16) for rows in (slice(0, half), slice(half, BLK)))
        layout = slice_layout(band_total, rep_total)
        attn_layout = jnp.asarray(np.concatenate(layout[:4], 2))
        wanted = jnp.take(tile_order, by_place(attn_layout).reshape(-1), mode="clip")
        meta = jnp.stack([wanted // own_count == place, wanted % own_count], 0).astype(jnp.int32)
        attn_part = place_tiles(low, high, meta, *attn_layout.shape)
        attn_part = rep_scatter(attn_part).astype(jnp.bfloat16)
        low, attn_part = lax.optimization_barrier((low, attn_part))
        slots = square_pieces(low)
        attn = over_bands(attn_part)
        *slots, attn = lax.optimization_barrier((*slots, attn))
        grids = [lax.dynamic_index_in_dim(jnp.asarray(grid), place, 0, False) for grid in layout]

        def find(wanted):
            wanted = jnp.take(tile_order, jnp.concatenate([grid.reshape(-1) for grid in wanted]), mode="clip")
            entry, row = (wanted // own_count) ^ place, wanted % own_count
            cut = own_count // 2
            high = (entry == 3) & (row >= cut)
            found = jnp.stack([jnp.where(high, 4, entry), jnp.where(high, row - cut, row)], 0)
            return found.astype(jnp.int32)

        all_grid = jnp.concatenate(grids[4:], 1)
        (first_part,) = gather_strips(slots, find([all_grid]), [all_grid.shape])
        packed, first_part = lax.optimization_barrier((packed, first_part))
        early = over_bands(first_part)
    packed_all = rep_gather(packed)
    if aligned:
        packed_all, high = lax.optimization_barrier((packed_all, high))
        later_slots = square_pieces(high)
    normed_one_all = packed_all[:, :tok_count].reshape(-1, D)
    at = tok_count + glob_total
    glob_digits = packed_all[:, at, : 2 * glob_total].astype(jnp.float32)
    glob_place = glob_digits[:, :glob_total] * 256.0 + glob_digits[:, glob_total:]
    at += 8
    selector_all = packed_all[:, at : at + selector.size // D].reshape(rep_total, glob_total, tok_count)

    if aligned:
        in_width = q_width + 2 * kv_width
        w_inner, w_output = attn[:, :in_width], attn[:, in_width:]
    else:
        slots = lax.all_gather(master[0].astype(jnp.bfloat16), "rep", axis=0, tiled=True)
        tiles = jnp.take(slots, tile_order, axis=0, mode="clip")
        slices = cut_slices(band_matrices(tiles, band_total), band_total, rep_total)
        w_inner = over_bands(jnp.concatenate(slices[0:3], 1))
        w_output = over_bands(slices[3])
        w_gate = over_bands(slices[4])
        w_up = over_bands(slices[5])
        w_down = over_bands(slices[6])

    w_output = by_place(w_output.reshape(rep_total, q_width, -1)).reshape(D, -1)

    def mul(rows, weight):
        return jnp.dot(rows, weight, preferred_element_type=jnp.float32)

    def mul_back(rows, weight):
        return lax.dot_general(rows, weight, (((1,), (1,)), ((), ())), preferred_element_type=jnp.float32)

    def weight_grad(rows, grad_rows):
        return lax.dot_general(
            rows, grad_rows, (((0,), (0,)), ((), ())), preferred_element_type=jnp.float32
        ).astype(jnp.bfloat16)

    def own_sum(partial):
        return rep_scatter(partial.astype(jnp.bfloat16).reshape(rep_total, tok_count, D))

    inner_rows = mul(packed_all.reshape(-1, D), w_inner).reshape(rep_total, -1, w_inner.shape[1])
    packed_all, normed_one_all = lax.optimization_barrier((packed_all, normed_one_all))
    queries, own_pairs = rope_rows(inner_rows, tok_count, 0, q_width, kv_width, wide_cosine, wide_sine)
    glob_cosine, glob_sine = rope_tables(glob_place.reshape(-1))
    glob_cosine = jnp.concatenate([glob_cosine, glob_cosine], 1).reshape(rep_total, glob_total, -1)
    glob_sine = jnp.concatenate([glob_sine, glob_sine], 1).reshape(rep_total, glob_total, -1)
    (glob_pairs,) = rope_rows(
        inner_rows, glob_total, tok_count // glob_total, q_width, kv_width, glob_cosine, glob_sine, False
    )
    back_count = (WINDOW + tok_count - 2) // tok_count
    odd = band % 2 == 1
    by_chip = back_count == 2 and band_total % 2 == 0
    if by_chip:
        two_back = shifted(own_pairs, "fsdp", 2)
        pair_blocks = [two_back, to_core(jnp.where(odd, two_back, own_pairs))]
    else:
        pair_blocks = [shifted(own_pairs, "fsdp", distance) for distance in range(back_count, 0, -1)]
    pair_blocks = pair_blocks + [own_pairs, glob_pairs]
    glob_spots = jnp.broadcast_to(glob_place[:, :, None], (rep_total, glob_total, BLK))
    band_number = band.astype(jnp.int32).reshape(1)
    attended_low, lse = attend(band_number, glob_spots, queries, pair_blocks)
    if aligned:
        *later_slots, attended_low, early = lax.optimization_barrier((*later_slots, attended_low, early))
        last_grid = jnp.concatenate(grids[4:6], 1)
        last_part, down_part = gather_strips(
            later_slots, find([last_grid, grids[6]]), [last_grid.shape, grids[6].shape]
        )

        def by_strips(gathered):
            return gathered.reshape(band_total, -1, all_grid.shape[0], half, gathered.shape[-1])

        early, late, late_down = by_strips(early), by_strips(over_bands(last_part)), by_strips(over_bands(down_part))
    attended_all = rep_features(attended_low).reshape(-1, D)
    columns = mul(attended_all, w_output).astype(jnp.bfloat16).reshape(rep_total, tok_count, -1)
    branch = by_place(rep_exchange(columns)).transpose(1, 0, 2).reshape(tok_count, D)
    middle = residual + branch.astype(jnp.float32)
    scale_two = lax.rsqrt(jnp.mean(middle * middle, -1, keepdims=True) + norm_eps)
    normed_two = (middle * scale_two * gains[1]).astype(jnp.bfloat16)
    normed_two_all = rep_gather(normed_two).reshape(-1, D)
    normed_two_all, grad_top_now = lax.optimization_barrier((normed_two_all, grad_top))
    top_first = gather_first(grad_top_now)

    if aligned:
        gate_rows, up_rows, activation = forward_products(normed_two_all, early, late, FF // rep_total)
        top_first, activation = after(top_first, activation)
        grad_top_all = gather_join(gather_second(top_first)).reshape(-1, D)
        g_down = weight_grad(activation, grad_top_all)
        grad_top_all, g_down = lax.optimization_barrier((grad_top_all, g_down))
        grad_gate, grad_up, pieces, branch_pieces = backward_products(
            grad_top_all, gate_rows, up_rows, activation, early, late, late_down
        )
        grad_normed_two = sum_pieces(*pieces)
    else:
        gate_rows = mul(normed_two_all, w_gate)
        up_rows = mul(normed_two_all, w_up)
        sigmoid_gate = jax.nn.sigmoid(gate_rows)
        silu_gate = gate_rows * sigmoid_gate
        activation = (silu_gate * up_rows).astype(jnp.bfloat16)
        grad_top_all = gather_join(gather_second(top_first)).reshape(-1, D)
        g_down = weight_grad(activation, grad_top_all)
        grad_act = mul_back(grad_top_all, w_down)
        grad_gate = (
            grad_act * up_rows * sigmoid_gate * (1.0 + gate_rows * (1.0 - sigmoid_gate))
        ).astype(jnp.bfloat16)
        grad_up = (grad_act * silu_gate).astype(jnp.bfloat16)
        grad_normed_two = own_sum(mul_back(grad_gate, w_gate) + mul_back(grad_up, w_up))
        branch_pieces = (mul(activation, w_down),)
    g_gate = weight_grad(normed_two_all, grad_gate)
    grad_normed_two, g_gate = lax.optimization_barrier((grad_normed_two, g_gate))

    def over_tokens(partial):
        return lax.psum_scatter(partial, "fsdp", scatter_dimension=0, tiled=True)

    s_down = over_tokens(g_down)
    s_gate = over_tokens(g_gate)

    grad_middle = grad_top.astype(jnp.float32) + norm_back(middle, scale_two, gains[1], grad_normed_two)
    grad_parts = grad_middle.astype(jnp.bfloat16).reshape(tok_count, rep_total, -1).transpose(1, 0, 2)
    grad_columns = rep_exchange(by_place(grad_parts)).reshape(rep_total * tok_count, -1)
    grad_columns, grad_up = lax.optimization_barrier((grad_columns, grad_up))
    g_up = weight_grad(normed_two_all, grad_up)
    grad_attended = rep_features_sum(
        grad_columns.reshape(rep_total, tok_count, -1), w_output
    ).astype(jnp.bfloat16)
    (s_down, g_up), grad_attended = after((s_down, g_up), grad_attended)
    down_first = gather_first(s_down)
    grad_queries, *grad_blocks = attend_back(
        band_number, glob_spots, wide_cosine, wide_sine, queries, grad_attended, lse, pair_blocks
    )
    down_first, *grad_blocks = after(down_first, *grad_blocks)
    down_second = gather_second(down_first)
    branch_pieces, *grad_blocks = after(tuple(branch_pieces), *grad_blocks)
    branch_first = sum_first(branch_pieces) if aligned else (own_sum(branch_pieces[0]),)
    if by_chip:
        came = to_core(grad_blocks[1])
        total = grad_blocks[0].astype(jnp.float32) + came.astype(jnp.float32)
        sent = jnp.where(odd, total.astype(jnp.bfloat16), grad_blocks[0])
        returned = [shifted(sent, "fsdp", -2), jnp.where(odd, jnp.zeros_like(came), came)]
    else:
        returned = [
            shifted(grad_blocks[back_count - distance], "fsdp", -distance)
            for distance in range(1, back_count + 1)
        ]
    glob_grads = add_all(grad_blocks[-1], "fsdp")
    g_up, glob_grads, *returned = lax.optimization_barrier((g_up, glob_grads, *returned))
    s_up = over_tokens(g_up)
    grad_inner = join_grads(
        grad_queries, grad_blocks[-2], selector_all, glob_grads, wide_cosine, wide_sine, returned
    ).reshape(-1, q_width + 2 * kv_width)
    branch_first, grad_inner = after(branch_first, grad_inner)
    down_second, grad_inner = after(down_second, grad_inner)
    s_down = gather_join(down_second)
    block_out = middle + (sum_second(branch_first) if aligned else branch_first[0])
    (s_gate,), grad_inner = after((s_gate,), grad_inner)
    gate_first = gather_first(s_gate)
    g_inner = weight_grad(normed_one_all, grad_inner)
    attended_all, g_inner = lax.optimization_barrier((attended_all, g_inner))
    g_output = weight_grad(attended_all, grad_columns)
    g_output = by_place(g_output.reshape(rep_total, q_width, -1)).reshape(D, -1)
    g_attn = with_layout_constraint(jnp.concatenate([g_inner, g_output], 1), Layout((0, 1)))
    grad_inner, g_attn = lax.optimization_barrier((grad_inner, g_attn))
    grad_normed_parts = mul_back(grad_inner, w_inner).astype(jnp.bfloat16).reshape(rep_total, tok_count, D)
    if square():
        normed_first = sum_first(split_pieces(grad_normed_parts))
    else:
        normed_first = (rep_scatter(grad_normed_parts),)
    (s_up, *gate_first), g_attn, block_out = after((s_up, *gate_first), g_attn, block_out)
    s_attn = over_tokens(g_attn)
    s_gate = gather_join(gather_second(gate_first))
    normed_first, s_up = after(normed_first, s_up)
    grad_normed_one = sum_second(normed_first) if square() else normed_first[0]
    s_up = rep_gather(s_up)
    grad_input = grad_middle + norm_back(residual, scale_one, gains[0], grad_normed_one)

    gain_terms = jnp.stack(
        [
            jnp.sum(grad_normed_one * residual * scale_one, 0),
            jnp.sum(grad_normed_two * middle * scale_two, 0),
        ]
    )
    square_terms = jnp.stack(
        [jnp.sum(residual * residual), jnp.sum(middle * middle), jnp.sum(block_out * block_out)]
    )
    sums = jnp.concatenate([gain_terms.reshape(-1), square_terms])

    sums = add_all(add_all(sums, "rep"), "fsdp")
    sums, s_attn, s_up = lax.optimization_barrier((sums, s_attn, s_up))
    gain_grad, square_total = sums[: 2 * D].reshape(2, D), sums[2 * D :]

    slot_ids = jnp.arange(tile_total, dtype=jnp.int32)
    inverse = jnp.sum(jnp.where(tile_order[None, :] == slot_ids[:, None], slot_ids[None, :], 0), 1)
    own_slots = place * own_count + jnp.arange(own_count, dtype=jnp.int32)
    owned_tiles = jnp.take(inverse, own_slots, mode="clip")
    if aligned:
        sources = [rep_gather(s_attn), s_gate, s_up, s_down]
        where = np.zeros((4, rep_total, tile_total), np.int32)
        first_col = 0
        for kind, grid in enumerate(layout):
            rows, cols = grid.shape[1:]
            first_col = 0 if kind >= 4 else first_col
            for there in range(rep_total):
                numbers = grid[there].reshape(-1)
                at = np.arange(rows * cols)
                where[0, :, numbers] = max(kind - 3, 0)
                where[2, :, numbers] = (at // cols * BLK)[:, None]
                where[3, :, numbers] = (at % cols * BLK + first_col)[:, None]
                for here in range(rep_total):
                    where[1, here, numbers] = here ^ there
            first_col += cols * BLK
        tile_spots = lax.dynamic_index_in_dim(jnp.asarray(where), place, 1, False)
        meta = jnp.take(tile_spots, owned_tiles, axis=1, mode="clip")
    else:
        splits = [0, q_width, q_width + kv_width, q_width + 2 * kv_width, s_attn.shape[1]]
        stacks = [rep_gather(s_attn[:, low:high]) for low, high in zip(splits, splits[1:])]
        stacks += [s_gate, s_up, s_down]
        sources = [band_tiles(join_slices(stacks, band_total, rep_total))]
        meta = jnp.stack([0 * owned_tiles, owned_tiles, 0 * owned_tiles, 0 * owned_tiles], 0)
    slot_rates = jnp.take(kind_rates(band_total), owned_tiles, mode="clip")
    new_first, new_second, new_master, master_copy = adam(
        meta,
        slot_rates,
        (master[0], first_moment[0], second_moment[0], left_basis[0], right_basis[0]),
        sources,
    )
    new_gain_first = beta_one * gain_first + (1.0 - beta_one) * gain_grad
    new_gain_second = beta_two * gain_second + (1.0 - beta_two) * gain_grad * gain_grad
    gain_step = (
        new_gain_first
        / (1.0 - beta_one**STEP)
        / (jnp.sqrt(new_gain_second / (1.0 - beta_two**STEP)) + adam_eps)
    )
    new_gains = gains - gain_rate * gain_step
    rms_stats = jnp.sqrt(square_total / (rep_total * band_total * tok_count * D))
    return (
        block_out[None],
        grad_input[None],
        new_first[None],
        new_second[None],
        new_master[None],
        master_copy[None],
        new_gain_first,
        new_gain_second,
        new_gains,
        rms_stats,
    )


def solution(mesh):
    in_specs = (
        P("rep", "fsdp", None),
        P("rep", "fsdp", None),
        P("rep", None, "fsdp"),
        P("fsdp", None),
        P("fsdp", "rep", None, None),
        P("fsdp", "rep", None, None),
        P("fsdp", "rep", None, None),
        P("fsdp", "rep", None, None),
        P("fsdp", "rep", None, None),
        P(),
        P(),
        P(),
    )
    out_specs = (
        P("rep", "fsdp", None),
        P("rep", "fsdp", None),
        P("fsdp", "rep", None, None),
        P("fsdp", "rep", None, None),
        P("fsdp", "rep", None, None),
        P("fsdp", "rep", None, None),
        P(),
        P(),
        P(),
        P(),
    )
    return jax.shard_map(
        per_device, mesh=mesh, in_specs=in_specs, out_specs=out_specs, check_vma=False
    )
```

```python
import functools

import jax
import jax.numpy as jnp
import numpy as np
from jax import lax
from jax.experimental import pallas as pl
from jax.experimental.layout import Layout, with_layout_constraint
from jax.experimental.pallas import tpu as pltpu
from jax.sharding import PartitionSpec as P

D = 2048
H = 32
KVH = 8
HD = 64
FF = 8192
WINDOW = 512
BLK = 128
STEP = 10


norm_eps = 1e-05
rope_theta = 500000.0
beta_one = 0.5
beta_two = 0.5
adam_eps = 1e-08
weight_decay = 0.1
gain_rate = 0.5
masked_value = -1e30


def matrix_shapes():
    kv_width = KVH * HD
    return [(D, D), (D, kv_width), (D, kv_width), (D, D), (D, FF), (D, FF), (FF, D)]


def kind_rates(band_total):
    rate_list = [
        D ** (-0.5),
        D ** (-0.5),
        D ** (-0.5),
        (D * 8 // WINDOW) ** (-0.5),
        D ** (-0.5),
        D ** (-0.5),
        FF ** (-0.5),
    ]
    pieces = []
    for (row_total, col_total), rate_value in zip(matrix_shapes(), rate_list):
        tile_count = row_total // band_total // BLK * (col_total // BLK)
        pieces.append(jnp.full((tile_count,), rate_value, jnp.float32))
    return jnp.concatenate(pieces)


def band_matrices(tiles, band_total):
    matrices = []
    offset = 0
    for row_total, col_total in matrix_shapes():
        band_rows = row_total // band_total
        tile_count = band_rows // BLK * (col_total // BLK)
        segment = tiles[offset : offset + tile_count].reshape(
            band_rows // BLK, col_total // BLK, BLK, BLK
        )
        matrices.append(segment.transpose(0, 2, 1, 3).reshape(band_rows, col_total))
        offset += tile_count
    return matrices


def band_tiles(matrices):
    pieces = []
    for matrix in matrices:
        row_count, col_count = matrix.shape
        segment = matrix.reshape(row_count // BLK, BLK, col_count // BLK, BLK).transpose(0, 2, 1, 3)
        pieces.append(segment.reshape(-1, BLK, BLK))
    return jnp.concatenate(pieces, 0)


def rope_tables(position):
    halves = jnp.arange(HD // 2, dtype=jnp.float32) * (2.0 / HD)
    frequency = rope_theta ** (-halves)
    angles = position.astype(jnp.float32)[:, None] * frequency[None, :]
    angles = jnp.concatenate([angles, angles], 1)
    return (jnp.cos(angles), jnp.sin(angles))


def rotate(vectors, cosine_table, sine_table):
    half_width = vectors.shape[-1] // 2
    turned = jnp.concatenate([-vectors[..., half_width:], vectors[..., :half_width]], -1)
    return vectors * cosine_table[:, None, :] + turned * sine_table[:, None, :]


def rotate_back(grad_rows, cosine_table, sine_table):
    half_width = grad_rows.shape[-1] // 2
    scaled = grad_rows * sine_table[:, None, :]
    turned = jnp.concatenate([scaled[..., half_width:], -scaled[..., :half_width]], -1)
    return grad_rows * cosine_table[:, None, :] + turned


def norm_back(values, row_scale, gain_row, grad_rows):
    weighted = grad_rows * gain_row
    return row_scale * weighted - values * row_scale**3 * jnp.mean(
        weighted * values, -1, keepdims=True
    )


def to_rep(block, distance):
    route = [(i, i ^ distance) for i in range(lax.axis_size("rep"))]
    return lax.ppermute(block, "rep", route)


def square():
    return lax.axis_size("rep") == 4


def gather_first(block):
    if not square():
        return (lax.all_gather(block, "rep", axis=0),)
    return block, to_rep(block, 1), to_rep(block, 2)


def gather_second(first):
    if not square():
        return first
    block, near, far = first
    cut = block.shape[0] // 2
    return block, near, far, to_rep(near[:cut], 2), to_rep(far[cut:], 1)


def gather_join(pieces):
    if not square():
        return pieces[0]
    return jnp.concatenate(pieces, 0).reshape((4,) + pieces[0].shape)


def square_pieces(block):
    return gather_second(gather_first(block))


def rep_gather(block):
    return gather_join(gather_second(gather_first(block)))


def after(values, *others):
    count = len(values)
    tied = lax.optimization_barrier((*values, *others))
    return tuple(tied[:count]), *tied[count:]


def rep_of(entry):
    place = lax.axis_index("rep")
    return place ^ entry if square() else entry


def rep_scatter(parts):
    if not square():
        flat = parts.reshape(-1, parts.shape[-1])
        return lax.psum_scatter(flat, "rep", scatter_dimension=0, tiled=True).astype(jnp.float32)
    return sum_pieces(*split_pieces(parts))


def split_pieces(parts):
    half = parts.shape[-1] // 2
    low, high = parts[..., :half], parts[..., half:]
    return jnp.stack([low[0], low[2]], 0), jnp.stack([low[1], low[3]], 0), high[:2], high[2:]


def sum_first(pieces):
    low_kept, low_sent, high_kept, high_sent = pieces
    parts = []
    for kept, sent, first in ((low_kept, low_sent, 1), (high_kept, high_sent, 2)):
        came = to_rep(sent, first)
        parts.append(kept[0].astype(jnp.float32) + came[0].astype(jnp.float32))
        parts.append((kept[1].astype(jnp.float32) + came[1].astype(jnp.float32)).astype(kept.dtype))
    return tuple(parts)


def sum_second(parts):
    low, low_other, high, high_other = parts
    low = low + to_rep(low_other, 2).astype(jnp.float32)
    high = high + to_rep(high_other, 1).astype(jnp.float32)
    return jnp.concatenate([low, high], -1)


def sum_pieces(*pieces):
    return sum_second(sum_first(pieces))


def add_all(value, axis):
    size = lax.axis_size(axis)
    total = value.astype(jnp.float32)
    distance = 1
    while distance < size:
        count = 2 if (size // distance).bit_length() % 2 == 0 else 4
        low = total.astype(value.dtype)
        others = []
        for step in range(1, count):
            route = [(i, i ^ (step * distance)) for i in range(size)]
            others.append(lax.ppermute(low, axis, route).astype(jnp.float32))
        total = total + others[0]
        if count == 4:
            total = total + (others[1] + others[2])
        distance *= count
    return total


def rep_features(block):
    if not square():
        return lax.all_gather(block, "rep", axis=2, tiled=True)
    own, near, far, low, high = square_pieces(block)
    return jnp.concatenate(
        [
            own,
            jnp.stack([near[1], near[0], near[3], near[2]], 0),
            jnp.stack([far[2], far[3], far[0], far[1]], 0),
            jnp.stack([high[1], high[0], low[1], low[0]], 0),
        ],
        2,
    )


def write_pieces(entry, rows, values, refs):
    low_kept, low_sent, high_kept, high_sent = refs
    half = low_kept.shape[-1]
    values = values.astype(jnp.bfloat16)
    (low_sent if entry % 2 else low_kept)[entry // 2, rows] = values[:, :half]
    (high_sent if entry // 2 else high_kept)[entry % 2, rows] = values[:, half:]


def swapped_kernel(x_ref, w_ref, *refs):
    reps, rows, _ = x_ref.shape
    width = w_ref.shape[0] // reps
    for entry in range(reps):
        weight = w_ref[entry * width : (entry + 1) * width]
        for there in range(reps):
            product = over_last(x_ref[there ^ entry], weight)
            write_pieces(entry, slice(there * rows, (there + 1) * rows), product, refs)


def rep_features_sum(columns, weight, meanwhile):
    reps, rows, depth = columns.shape
    width = weight.shape[0] // reps
    if square():
        pieces = pl.pallas_call(
            swapped_kernel,
            out_shape=[jax.ShapeDtypeStruct((2, reps * rows, width // 2), jnp.bfloat16)] * 4,
            compiler_params=pltpu.CompilerParams(vmem_limit_bytes=32 * 2**20),
            cost_estimate=pl.CostEstimate(
                flops=2 * reps * columns.size * width,
                bytes_accessed=10 * columns.size,
                transcendentals=0,
            ),
        )(columns, weight)
        first = sum_first(pieces)
        first, other = after(first, meanwhile())
        total = sum_second(first)
    else:
        other = meanwhile()
        product = over_last(columns.reshape(-1, depth), weight).astype(jnp.bfloat16)
        swapped = product.reshape(reps, rows, reps, width).transpose(2, 0, 1, 3)
        total = rep_scatter(swapped.reshape(reps, reps * rows, width))
    return total.reshape(reps, rows, width), other


def rep_exchange(parts):
    if not square():
        return lax.all_to_all(parts, "rep", 0, 0)
    return jnp.stack([parts[0]] + [to_rep(parts[entry], entry) for entry in (1, 2, 3)], 0)


def by_place(parts):
    entries = [rep_of(entry) for entry in range(parts.shape[0])]
    return jnp.stack([lax.dynamic_index_in_dim(parts, entry, 0, False) for entry in entries], 0)


def to_core(block):
    return lax.ppermute(block, "fsdp", [(i, i ^ 1) for i in range(lax.axis_size("fsdp"))])


def shifted(block, axis, distance):
    devices = range(lax.axis_size(axis))
    route = [(i - distance, i) for i in devices if i - distance in devices]
    return lax.ppermute(block, axis, route)


def tile_offsets(band_total):
    offsets = [0]
    for row_total, col_total in matrix_shapes():
        offsets.append(offsets[-1] + row_total // band_total // BLK * (col_total // BLK))
    return offsets


def whole_tiles(band_total, rep_total):
    return KVH * HD // rep_total % BLK == 0 and FF // band_total // rep_total % BLK == 0


def slice_layout(band_total, rep_total):
    offsets = tile_offsets(band_total)
    layout = []
    for kind, (row_total, col_total) in enumerate(matrix_shapes()):
        rows, cols = row_total // band_total // BLK, col_total // BLK
        grid = offsets[kind] + np.arange(rows * cols).reshape(rows, cols)
        if kind == 6:
            layout.append(grid.reshape(rep_total, rows // rep_total, cols))
        elif kind in (4, 5):
            cut = grid.reshape(rows, band_total, rep_total, -1).transpose(2, 0, 1, 3)
            layout.append(cut.reshape(rep_total, rows, -1))
        else:
            layout.append(grid.reshape(rows, rep_total, -1).transpose(1, 0, 2))
    return layout


def tiles_to_matrix(tiles):
    rows, cols = tiles.shape[:2]
    return tiles.transpose(0, 2, 1, 3).reshape(rows * BLK, cols * BLK)


def matrix_to_tiles(matrix):
    rows, cols = matrix.shape
    cut = matrix.reshape(rows // BLK, BLK, cols // BLK, BLK)
    return cut.transpose(0, 2, 1, 3).reshape(-1, BLK, BLK)


def cut_slices(matrices, band_total, rep_total):
    place = lax.axis_index("rep")
    slices = []
    for kind, matrix in enumerate(matrices):
        rows, cols = matrix.shape
        if kind == 6:
            slices.append(lax.dynamic_slice_in_dim(matrix, place * (rows // rep_total), rows // rep_total, 0))
        elif kind in (4, 5):
            cut = matrix.reshape(rows, band_total, rep_total, -1)
            slices.append(lax.dynamic_index_in_dim(cut, place, 2, False).reshape(rows, -1))
        else:
            slices.append(lax.dynamic_slice_in_dim(matrix, place * (cols // rep_total), cols // rep_total, 1))
    return slices


def join_slices(stacks, band_total, rep_total):
    matrices = []
    for kind, stack in enumerate(stacks):
        rows, cols = stack.shape[1:]
        if kind == 6:
            matrices.append(stack.reshape(-1, cols))
        elif kind in (4, 5):
            cut = stack.reshape(rep_total, rows, band_total, -1).transpose(1, 2, 0, 3)
            matrices.append(cut.reshape(rows, -1))
        else:
            matrices.append(stack.transpose(1, 0, 2).reshape(rows, -1))
    return matrices


def gather_kernel(grids, meta, *refs):
    source_total = len(refs) - len(grids) - 1
    sources, targets, done = refs[:source_total], refs[source_total:-1], refs[-1]
    height = sources[0].shape[1]
    start = 0
    for place, (target, (rows, cols)) in enumerate(zip(targets, grids)):

        def one(tile, carry, target=target, rows=rows, cols=cols, start=start, place=place):
            kind = meta[0, start + tile]
            row = meta[1, start + tile]
            across = tile % cols
            top = pl.multiple_of((across // 2 * rows + tile // cols) * height, height)
            left = pl.multiple_of(across % 2 * BLK, BLK)
            for number, source in enumerate(sources):

                @pl.when(kind == number)
                def _(source=source):
                    pltpu.make_async_copy(
                        source.at[row], target.at[pl.ds(top, height), pl.ds(left, BLK)], done.at[place]
                    ).start()

            return carry

        lax.fori_loop(0, rows * cols, one, 0)
        start += rows * cols
    for place, target in enumerate(targets):
        pltpu.make_async_copy(target, target, done.at[place]).wait()


def gather_strips(sources, meta, grids):
    anywhere = pl.BlockSpec(memory_space=pl.ANY)
    height = sources[0].shape[1]
    out_shape = [
        jax.ShapeDtypeStruct((cols // 2 * rows * height, 2 * BLK), jnp.bfloat16) for rows, cols in grids
    ]
    return pl.pallas_call(
        functools.partial(gather_kernel, grids),
        out_shape=out_shape,
        grid_spec=pltpu.PrefetchScalarGridSpec(
            num_scalar_prefetch=1,
            grid=(1,),
            in_specs=[anywhere] * len(sources),
            out_specs=[pl.BlockSpec(shape.shape, lambda i, *_: (0, 0)) for shape in out_shape],
            scratch_shapes=[pltpu.SemaphoreType.DMA((len(grids),))],
        ),
        compiler_params=pltpu.CompilerParams(vmem_limit_bytes=32 * 2**20),
        cost_estimate=pl.CostEstimate(
            flops=0, bytes_accessed=sum(4 * shape.size for shape in out_shape), transcendentals=0
        ),
    )(meta, *sources)


def place_kernel(entries, rows, cols, meta, low, high, out_ref, done):
    out_ref[...] = jnp.zeros_like(out_ref)
    height = low.shape[1]

    def copies(tile):
        entry, rest = tile // (rows * cols), tile % (rows * cols)
        top = rest // cols * (2 * height)
        left = pl.multiple_of(rest % cols * BLK, BLK)
        return [
            pltpu.make_async_copy(
                half.at[meta[1, tile]],
                out_ref.at[entry, pl.ds(pl.multiple_of(top + part * height, height), height), pl.ds(left, BLK)],
                done.at[part],
            )
            for part, half in enumerate((low, high))
        ]

    def begin(tile, carry):
        @pl.when(meta[0, tile] == 1)
        def _():
            for copy in copies(tile):
                copy.start()

        return carry

    def finish(tile, carry):
        @pl.when(meta[0, tile] == 1)
        def _():
            for copy in copies(tile):
                copy.wait()

        return carry

    lax.fori_loop(0, entries * rows * cols, begin, 0)
    lax.fori_loop(0, entries * rows * cols, finish, 0)


def place_tiles(low, high, meta, entries, rows, cols):
    shape = (entries, rows * BLK, cols * BLK)
    anywhere = pl.BlockSpec(memory_space=pl.ANY)
    return pl.pallas_call(
        functools.partial(place_kernel, entries, rows, cols),
        out_shape=jax.ShapeDtypeStruct(shape, jnp.bfloat16),
        grid_spec=pltpu.PrefetchScalarGridSpec(
            num_scalar_prefetch=1,
            grid=(1,),
            in_specs=[anywhere, anywhere],
            out_specs=pl.BlockSpec(shape, lambda i, *_: (0, 0, 0)),
            scratch_shapes=[pltpu.SemaphoreType.DMA((2,))],
        ),
        compiler_params=pltpu.CompilerParams(vmem_limit_bytes=32 * 2**20),
        cost_estimate=pl.CostEstimate(
            flops=0, bytes_accessed=4 * entries * rows * cols * BLK * BLK, transcendentals=0
        ),
    )(meta, low, high)


def half_turn(values):
    lane = lax.broadcasted_iota(jnp.int32, values.shape, 1)
    lanes = values.shape[1]
    first = lane % HD < HD // 2
    return first, jnp.where(
        first, pltpu.roll(values, lanes - HD // 2, 1), pltpu.roll(values, HD // 2, 1)
    )


def strip_copies(early, late, target, done):
    return [
        pltpu.make_async_copy(half, target.at[:, :, number], done.at[number])
        for number, half in enumerate((early, late))
    ]


def forward_kernel(x_ref, early, late, gate_ref, up_ref, act_ref, weights, done):
    step, steps = pl.program_id(0), pl.num_programs(0)
    slot = step % 2
    width = weights.shape[-1]

    def copies(number, at_step, at_slot):
        strip = number * steps + at_step
        return strip_copies(
            early.at[:, strip], late.at[:, strip], weights.at[number, at_slot], done.at[number, at_slot]
        )

    def fetch(at_step, at_slot):
        for number in range(2):
            for copy in copies(number, at_step, at_slot):
                copy.start()

    @pl.when(step == 0)
    def _():
        fetch(0, 0)

    @pl.when(step + 1 < steps)
    def _():
        fetch(step + 1, 1 - slot)

    for number in range(2):
        for copy in copies(number, step, slot):
            copy.wait()
    gate_weight, up_weight = (weights[number, slot].reshape(-1, width) for number in range(2))
    chunk = min(2 * BLK, x_ref.shape[0])
    for first in range(0, x_ref.shape[0], chunk):
        rows = slice(first, first + chunk)
        gate = jnp.dot(x_ref[rows], gate_weight, preferred_element_type=jnp.float32)
        up = jnp.dot(x_ref[rows], up_weight, preferred_element_type=jnp.float32)
        gate_ref[rows] = gate.astype(jnp.bfloat16)
        up_ref[rows] = up.astype(jnp.bfloat16)
        act_ref[rows] = (gate * jax.nn.sigmoid(gate) * up).astype(jnp.bfloat16)


def forward_products(rows, early, late, columns):
    tokens, depth = rows.shape
    bands, _, tiles, half, width = early.shape
    block = pl.BlockSpec((tokens, width), lambda n: (0, n))
    anywhere = pl.BlockSpec(memory_space=pl.ANY)
    return pl.pallas_call(
        forward_kernel,
        out_shape=[jax.ShapeDtypeStruct((tokens, columns), jnp.bfloat16)] * 3,
        grid=(columns // width,),
        in_specs=[pl.BlockSpec(rows.shape, lambda n: (0, 0)), anywhere, anywhere],
        out_specs=[block] * 3,
        scratch_shapes=[
            pltpu.VMEM((2, 2, bands, tiles, 2, half, width), jnp.bfloat16),
            pltpu.SemaphoreType.DMA((2, 2, 2)),
        ],
        compiler_params=pltpu.CompilerParams(vmem_limit_bytes=48 * 2**20),
        cost_estimate=pl.CostEstimate(
            flops=tokens * depth * columns // 8, bytes_accessed=2 * rows.size, transcendentals=0
        ),
    )(rows, early, late)


def backward_kernel(top_ref, gate_ref, up_ref, act_ref, early, late, late_down, *refs):
    dgate_ref, dup_ref = refs[:2]
    pieces, branch_pieces = refs[2:6], refs[6:10]
    weights, downs, total, branch, done, down_done = refs[10:]
    step, steps = pl.program_id(0), pl.num_programs(0)
    slot = step % 2
    strips, width = downs.shape[1], downs.shape[-1]

    def down_copies(at_step, at_slot):
        wanted = pl.ds(2 * steps, strips)
        return strip_copies(
            early.at[at_step, wanted], late_down.at[at_step], downs.at[at_slot], down_done.at[at_slot]
        )

    def copies(number, at_step, at_slot):
        strip = number * steps + at_step
        return strip_copies(
            early.at[:, strip], late.at[:, strip], weights.at[number, at_slot], done.at[number, at_slot]
        )

    def fetch(at_step, at_slot):
        for copy in down_copies(at_step, at_slot):
            copy.start()
        for number in range(2):
            for copy in copies(number, at_step, at_slot):
                copy.start()

    @pl.when(step == 0)
    def _():
        fetch(0, 0)
        total[...] = jnp.zeros_like(total)
        branch[...] = jnp.zeros_like(branch)

    @pl.when(step + 1 < steps)
    def _():
        fetch(step + 1, 1 - slot)

    for copy in down_copies(step, slot):
        copy.wait()
    for number in range(2):
        for copy in copies(number, step, slot):
            copy.wait()
    gate_weight, up_weight = (weights[number, slot].reshape(-1, width) for number in range(2))
    chunk = min(4 * BLK, top_ref.shape[0])
    for first in range(0, top_ref.shape[0], chunk):
        rows = slice(first, first + chunk)
        grad_act = 0.0
        for strip in range(strips):
            lanes = slice(strip * width, (strip + 1) * width)
            down = downs[slot, strip].reshape(-1, width)
            grad_act = grad_act + over_last(top_ref[rows, lanes], down)
            branch[rows, lanes] += jnp.dot(act_ref[rows], down, preferred_element_type=jnp.float32)
        gate = gate_ref[rows].astype(jnp.float32)
        up = up_ref[rows].astype(jnp.float32)
        sigmoid_gate = jax.nn.sigmoid(gate)
        grad_gate = grad_act * up * sigmoid_gate * (1.0 + gate * (1.0 - sigmoid_gate))
        grad_gate = grad_gate.astype(jnp.bfloat16)
        grad_up = (grad_act * (gate * sigmoid_gate)).astype(jnp.bfloat16)
        dgate_ref[rows] = grad_gate
        dup_ref[rows] = grad_up
        total[rows] += over_last(grad_gate, gate_weight) + over_last(grad_up, up_weight)

    @pl.when(step == steps - 1)
    def _():
        rows = total.shape[0] // 4
        for entry in range(4):
            part = slice(entry * rows, (entry + 1) * rows)
            write_pieces(entry, slice(0, rows), total[part], pieces)
            write_pieces(entry, slice(0, rows), branch[part], branch_pieces)


def backward_products(top, gate, up, act, early, late, late_down):
    tokens, depth = top.shape
    columns = gate.shape[1]
    bands, _, tiles, half, width = early.shape
    strips = depth // width
    block = pl.BlockSpec((tokens, width), lambda n: (0, n))
    anywhere = pl.BlockSpec(memory_space=pl.ANY)
    piece = jax.ShapeDtypeStruct((2, tokens // 4, depth // 2), jnp.bfloat16)
    grads = jax.ShapeDtypeStruct((tokens, columns), jnp.bfloat16)
    outs = pl.pallas_call(
        backward_kernel,
        out_shape=[grads] * 2 + [piece] * 8,
        grid=(columns // width,),
        in_specs=[pl.BlockSpec(top.shape, lambda n: (0, 0))] + [block] * 3 + [anywhere] * 3,
        out_specs=[block] * 2 + [pl.BlockSpec(piece.shape, lambda n: (0, 0, 0))] * 8,
        scratch_shapes=[
            pltpu.VMEM((2, 2, bands, tiles, 2, half, width), jnp.bfloat16),
            pltpu.VMEM((2, strips, tiles, 2, half, width), jnp.bfloat16),
            pltpu.VMEM((tokens, depth), jnp.float32),
            pltpu.VMEM((tokens, depth), jnp.float32),
            pltpu.SemaphoreType.DMA((2, 2, 2)),
            pltpu.SemaphoreType.DMA((2, 2)),
        ],
        compiler_params=pltpu.CompilerParams(vmem_limit_bytes=60 * 2**20),
        cost_estimate=pl.CostEstimate(
            flops=8 * tokens * depth * columns, bytes_accessed=8 * columns * depth, transcendentals=0
        ),
    )(top, gate, up, act, early, late, late_down)
    return outs[0], outs[1], outs[2:6], outs[6:10]


def rope_kernel(q_width, kv_width, x_ref, cos_ref, sin_ref, *outs):
    width = x_ref.shape[-1]
    for start in range(0, width, BLK):
        values = x_ref[0, :, start : start + BLK]
        first, turned = half_turn(values)
        sines = sin_ref[0]
        turned_rows = values * cos_ref[0] + turned * jnp.where(first, -sines, sines)
        if start + BLK > q_width + kv_width:
            column = lax.broadcasted_iota(jnp.int32, values.shape, 1) + start
            turned_rows = jnp.where(column >= q_width + kv_width, values, turned_rows)
        if start < q_width:
            outs[0][0, :, start : start + BLK] = (turned_rows * HD ** (-0.5)).astype(jnp.bfloat16)
        else:
            outs[-1][0, :, start - q_width : start - q_width + BLK] = turned_rows.astype(jnp.bfloat16)


def rope_rows(inner, rows, row_block, q_width, kv_width, cosines, sines, with_queries=True):
    seqs, _, width = inner.shape
    shared = cosines.shape[0] == 1
    table = pl.BlockSpec((1, rows, BLK), lambda s: (0 if shared else s, 0, 0))
    widths = [q_width, 2 * kv_width]
    column_block = 0
    if not with_queries:
        width, column_block = 2 * kv_width, q_width // (2 * kv_width)
        widths, q_width = widths[1:], 0
    return pl.pallas_call(
        functools.partial(rope_kernel, q_width, kv_width),
        out_shape=[jax.ShapeDtypeStruct((seqs, rows, w), jnp.bfloat16) for w in widths],
        grid=(seqs,),
        in_specs=[pl.BlockSpec((1, rows, width), lambda s: (s, row_block, column_block)), table, table],
        out_specs=[pl.BlockSpec((1, rows, w), lambda s: (s, 0, 0)) for w in widths],
        cost_estimate=pl.CostEstimate(
            flops=6 * seqs * rows * width, bytes_accessed=6 * seqs * rows * width, transcendentals=0
        ),
    )(inner, cosines, sines)


def fill_bias(band_ref, gpos_ref, bias_ref, rows, window_len):
    band = band_ref[0]

    @pl.when(pl.program_id(0) == 0)
    def _():
        key = lax.broadcasted_iota(jnp.int32, (window_len, rows), 0) + (
            band * rows - (window_len - rows)
        )
        query = lax.broadcasted_iota(jnp.int32, (window_len, rows), 1) + band * rows
        inside = (key > query - WINDOW) & (key <= query) & (key >= 0)
        bias_ref[:window_len] = jnp.where(inside, 0.0, masked_value)

    glob_total = gpos_ref.shape[1]
    query = lax.broadcasted_iota(jnp.int32, (glob_total, rows), 1) + (band * rows - WINDOW)
    spot = jnp.broadcast_to(gpos_ref[0][:, :1], (glob_total, rows))
    bias_ref[window_len:] = jnp.where(spot <= query.astype(jnp.float32), 0.0, masked_value)


def over_last(left, right):
    return lax.dot_general(left, right, (((1,), (1,)), ((), ())), preferred_element_type=jnp.float32)


def over_first(left, right):
    return lax.dot_general(left, right, (((0,), (0,)), ((), ())), preferred_element_type=jnp.float32)


def attend_kernel(block_total, band_ref, gpos_ref, q_ref, *refs):
    blocks, (out_ref, lse_ref, bias_ref) = refs[:block_total], refs[block_total:]
    rows, q_width = q_ref.shape[1:]
    kv_width = blocks[0].shape[2] // 2
    heads, group = q_width // HD, q_width // kv_width
    window_len = rows * (block_total - 1)
    fill_bias(band_ref, gpos_ref, bias_ref, rows, window_len)
    starts = [rows * number for number in range(block_total)]
    pending = []
    for head in range(heads):
        left = head // group * HD
        queries = q_ref[0, :, head * HD : (head + 1) * HD]
        scores = [
            over_last(block[0, :, left : left + HD], queries)
            + bias_ref[start : start + block.shape[1]]
            for block, start in zip(blocks, starts)
        ]
        top = functools.reduce(jnp.maximum, [jnp.max(part, 0, keepdims=True) for part in scores])
        total = 0.0
        mixed = 0.0
        for block, part in zip(blocks, scores):
            weights = jnp.exp(part - top)
            total = total + jnp.sum(weights, 0, keepdims=True)
            mixed = mixed + over_first(
                block[0, :, kv_width + left : kv_width + left + HD], weights.astype(jnp.bfloat16)
            )
        lse_ref[0, head : head + 1, :] = top + jnp.log(total)
        pending.append(mixed / total)
        if len(pending) * HD == BLK or head == heads - 1:
            stop = (head + 1) * HD
            both = jnp.concatenate(pending, 0).T
            out_ref[0, :, stop - both.shape[1] : stop] = both.astype(jnp.bfloat16)
            pending = []


def attend(band, gpos, queries, blocks):
    seqs, rows, q_width = queries.shape
    heads = q_width // HD
    key_total = sum(block.shape[1] for block in blocks)

    def whole(array):
        return pl.BlockSpec((1,) + array.shape[1:], lambda s, *_: (s, 0, 0))

    out_shape = [
        jax.ShapeDtypeStruct((seqs, rows, q_width), jnp.bfloat16),
        jax.ShapeDtypeStruct((seqs, heads, rows), jnp.float32),
    ]
    return pl.pallas_call(
        functools.partial(attend_kernel, len(blocks)),
        out_shape=out_shape,
        grid_spec=pltpu.PrefetchScalarGridSpec(
            num_scalar_prefetch=1,
            grid=(seqs,),
            in_specs=[whole(array) for array in (gpos, queries, *blocks)],
            out_specs=[whole(array) for array in out_shape],
            scratch_shapes=[pltpu.VMEM((key_total, rows), jnp.float32)],
        ),
        compiler_params=pltpu.CompilerParams(vmem_limit_bytes=48 * 2**20),
        cost_estimate=pl.CostEstimate(
            flops=16 * seqs * heads * rows * key_total * HD,
            bytes_accessed=4 * queries.size,
            transcendentals=seqs * heads * rows * key_total,
        ),
    )(band, gpos, queries, *blocks)


def attend_back_kernel(block_total, band_ref, gpos_ref, cos_ref, sin_ref, q_ref, grad_ref, lse_ref, *refs):
    blocks = refs[:block_total]
    dq_ref = refs[block_total]
    out_refs = refs[block_total + 1 : 2 * block_total + 1]
    bias_ref = refs[-1]
    rows, q_width = q_ref.shape[1:]
    kv_width = blocks[0].shape[2] // 2
    heads, group = q_width // HD, q_width // kv_width
    window_len = rows * (block_total - 1)
    fill_bias(band_ref, gpos_ref, bias_ref, rows, window_len)
    starts = [rows * number for number in range(block_total)]
    pending = []
    for kv_head in range(kv_width // HD):
        left = kv_head * HD
        key_sums = [0.0] * block_total
        value_sums = [0.0] * block_total
        for head in range(kv_head * group, (kv_head + 1) * group):
            queries = q_ref[0, :, head * HD : (head + 1) * HD]
            grads = grad_ref[0, :, head * HD : (head + 1) * HD]
            lse = lse_ref[0, head : head + 1, :]
            soft, soft_grads = [], []
            inner = 0.0
            for number, (block, start) in enumerate(zip(blocks, starts)):
                part = over_last(block[0, :, left : left + HD], queries)
                part = jnp.exp(part + bias_ref[start : start + block.shape[1]] - lse)
                slope = over_last(block[0, :, kv_width + left : kv_width + left + HD], grads)
                inner = inner + jnp.sum(part * slope, 0, keepdims=True)
                soft.append(part)
                soft_grads.append(slope)
            turned = 0.0
            for number, block in enumerate(blocks):
                score_grads = (soft[number] * (soft_grads[number] - inner)).astype(jnp.bfloat16)
                value_sums[number] = value_sums[number] + jnp.dot(
                    soft[number].astype(jnp.bfloat16), grads, preferred_element_type=jnp.float32
                )
                key_sums[number] = key_sums[number] + jnp.dot(
                    score_grads, queries, preferred_element_type=jnp.float32
                )
                turned = turned + over_first(block[0, :, left : left + HD], score_grads)
            pending.append(turned)
            if len(pending) * HD == BLK or head == heads - 1:
                stop = (head + 1) * HD
                both = jnp.concatenate(pending, 0).T * HD ** (-0.5)
                pending = []
                first, other = half_turn(both * sin_ref[0])
                both = both * cos_ref[0] + jnp.where(first, other, -other)
                dq_ref[0, :, stop - both.shape[1] : stop] = both.astype(jnp.bfloat16)
        for number, out_ref in enumerate(out_refs):
            out_ref[0, :, left : left + HD] = key_sums[number].astype(out_ref.dtype)
            out_ref[0, :, kv_width + left : kv_width + left + HD] = value_sums[number].astype(
                out_ref.dtype
            )


def attend_back(band, gpos, cosines, sines, queries, grads, lse, blocks):
    seqs, rows, q_width = queries.shape
    heads = q_width // HD
    key_total = sum(block.shape[1] for block in blocks)

    def whole(array):
        return pl.BlockSpec((1,) + array.shape[1:], lambda s, *_: (s, 0, 0))

    table = pl.BlockSpec((1, rows, BLK), lambda s, *_: (0, 0, 0))
    out_shape = [jax.ShapeDtypeStruct(queries.shape, jnp.bfloat16)]
    for number, block in enumerate(blocks):
        own = number == len(blocks) - 2
        out_shape.append(jax.ShapeDtypeStruct(block.shape, jnp.float32 if own else jnp.bfloat16))
    return pl.pallas_call(
        functools.partial(attend_back_kernel, len(blocks)),
        out_shape=out_shape,
        grid_spec=pltpu.PrefetchScalarGridSpec(
            num_scalar_prefetch=1,
            grid=(seqs,),
            in_specs=[whole(gpos), table, table]
            + [whole(array) for array in (queries, grads, lse, *blocks)],
            out_specs=[whole(array) for array in out_shape],
            scratch_shapes=[pltpu.VMEM((key_total, rows), jnp.float32)],
        ),
        compiler_params=pltpu.CompilerParams(vmem_limit_bytes=48 * 2**20),
        cost_estimate=pl.CostEstimate(
            flops=40 * seqs * heads * rows * key_total * HD,
            bytes_accessed=8 * queries.size,
            transcendentals=seqs * heads * rows * key_total,
        ),
    )(band, gpos, cosines, sines, queries, grads, lse, *blocks)


def join_kernel(q_width, kv_width, dq_ref, own_ref, pick_ref, glob_ref, cos_ref, sin_ref, *refs):
    back_refs, out_ref = refs[:-1], refs[-1]
    out_ref[0, :, :q_width] = dq_ref[0]
    picked = lax.dot_general(
        pick_ref[0].astype(jnp.float32),
        glob_ref[0],
        (((0,), (0,)), ((), ())),
        precision=lax.Precision.HIGHEST,
        preferred_element_type=jnp.float32,
    )
    for start in range(0, 2 * kv_width, BLK):
        lanes = slice(start, start + BLK)
        total = own_ref[0, :, lanes] + picked[:, lanes]
        for back_ref in back_refs:
            total = total + back_ref[0, :, lanes].astype(jnp.float32)
        first, other = half_turn(total * sin_ref[0])
        turned = total * cos_ref[0] + jnp.where(first, other, -other)
        column = lax.broadcasted_iota(jnp.int32, total.shape, 1) + start
        turned = jnp.where(column >= kv_width, total, turned)
        out_ref[0, :, q_width + start : q_width + start + BLK] = turned.astype(jnp.bfloat16)


def join_grads(dq, own, picks, globs, cosines, sines, backs):
    seqs, rows, q_width = dq.shape
    kv_width = own.shape[2] // 2

    def whole(array):
        return pl.BlockSpec((1,) + array.shape[1:], lambda s: (s, 0, 0))

    table = pl.BlockSpec((1, rows, BLK), lambda s: (0, 0, 0))
    out_shape = jax.ShapeDtypeStruct((seqs, rows, q_width + 2 * kv_width), jnp.bfloat16)
    return pl.pallas_call(
        functools.partial(join_kernel, q_width, kv_width),
        out_shape=out_shape,
        grid=(seqs,),
        in_specs=[whole(dq), whole(own), whole(picks), whole(globs), table, table]
        + [whole(back) for back in backs],
        out_specs=whole(out_shape),
        cost_estimate=pl.CostEstimate(
            flops=20 * own.size, bytes_accessed=4 * dq.size + 12 * own.size, transcendentals=0
        ),
    )(dq, own, picks, globs, cosines, sines, *backs)


def adam_kernel(batch, meta, rates, *refs):
    master_ref, first_ref, second_ref, left_ref, right_ref = refs[:5]
    sources = refs[5:-6]
    new_first_ref, new_second_ref, new_master_ref, copy_ref, tiles, arrived = refs[-6:]
    step, steps = pl.program_id(0), pl.num_programs(0)
    slot = step % 2

    def fetch(at_step, at_slot):
        for place in range(batch):
            tile = at_step * batch + place
            for number, source in enumerate(sources):

                @pl.when(meta[0, tile] == number)
                def _(source=source, tile=tile, place=place):
                    top = pl.multiple_of(meta[2, tile], BLK)
                    left = pl.multiple_of(meta[3, tile], BLK)
                    pltpu.make_async_copy(
                        source.at[meta[1, tile], pl.ds(top, BLK), pl.ds(left, BLK)],
                        tiles.at[at_slot, place],
                        arrived.at[at_slot],
                    ).start()

    @pl.when(step == 0)
    def _():
        fetch(0, 0)

    @pl.when(step + 1 < steps)
    def _():
        fetch(step + 1, 1 - slot)

    pltpu.make_async_copy(tiles.at[slot], tiles.at[slot], arrived.at[slot]).wait()
    places = range(batch)
    lefts = [left_ref[place].astype(jnp.bfloat16) for place in places]
    rights = [right_ref[place].astype(jnp.bfloat16) for place in places]
    turned = [over_first(lefts[place], tiles[slot, place]).astype(jnp.bfloat16) for place in places]
    rotated = [
        jnp.dot(turned[place], rights[place], preferred_element_type=jnp.float32) for place in places
    ]
    directions = []
    for place in places:
        new_first = beta_one * first_ref[place] + (1.0 - beta_one) * rotated[place]
        new_second = beta_two * second_ref[place] + (1.0 - beta_two) * rotated[place] * rotated[place]
        direction = (new_first * (1.0 / (1.0 - beta_one**STEP))) / (
            jnp.sqrt(new_second * (1.0 / (1.0 - beta_two**STEP))) + adam_eps
        )
        new_first_ref[place] = new_first
        new_second_ref[place] = new_second
        directions.append(direction.astype(jnp.bfloat16))
    updates = [
        jnp.dot(lefts[place], directions[place], preferred_element_type=jnp.float32) for place in places
    ]
    updates = [over_last(updates[place].astype(jnp.bfloat16), rights[place]) for place in places]
    for place in places:
        old = master_ref[place]
        new_master = old - rates[step * batch + place] * (updates[place] + weight_decay * old)
        new_master_ref[place] = new_master
        copy_ref[place] = new_master.astype(jnp.bfloat16)


def adam(meta, rates, state, sources):
    count = state[0].shape[0]
    batch = max(size for size in range(1, 33) if count % size == 0)
    block = pl.BlockSpec((batch, BLK, BLK), lambda s, *_: (s, 0, 0))
    anywhere = pl.BlockSpec(memory_space=pl.ANY)
    shape = (count, BLK, BLK)
    return pl.pallas_call(
        functools.partial(adam_kernel, batch),
        out_shape=[jax.ShapeDtypeStruct(shape, jnp.float32)] * 3
        + [jax.ShapeDtypeStruct(shape, jnp.bfloat16)],
        grid_spec=pltpu.PrefetchScalarGridSpec(
            num_scalar_prefetch=2,
            grid=(count // batch,),
            in_specs=[block] * 5 + [anywhere] * len(sources),
            out_specs=[block] * 4,
            scratch_shapes=[
                pltpu.VMEM((2, batch, BLK, BLK), jnp.bfloat16),
                pltpu.SemaphoreType.DMA((2,)),
            ],
        ),
        compiler_params=pltpu.CompilerParams(vmem_limit_bytes=56 * 2**20),
        cost_estimate=pl.CostEstimate(
            flops=8 * count * BLK**3, bytes_accessed=36 * count * BLK**2, transcendentals=0
        ),
    )(meta, rates, *state, *sources)


def per_device(
    block_input,
    cotangent,
    glob_select,
    assignment,
    master,
    first_moment,
    second_moment,
    left_basis,
    right_basis,
    gains,
    gain_first,
    gain_second,
):
    band_total = lax.axis_size("fsdp")
    rep_total = lax.axis_size("rep")
    place = lax.axis_index("rep")
    band = lax.axis_index("fsdp")
    heads = H // rep_total
    kv_heads = KVH // rep_total
    q_width = heads * HD
    kv_width = kv_heads * HD
    tok_count = block_input.shape[1]
    own_count = master.shape[1]
    tile_total = own_count * rep_total
    aligned = square() and whole_tiles(band_total, rep_total)
    tile_order = assignment[0]

    residual = block_input[0].astype(jnp.float32)
    grad_top = cotangent[0]
    position = band * tok_count + jnp.arange(tok_count, dtype=jnp.int32)
    cosine_table, sine_table = rope_tables(position)
    wide_cosine = jnp.concatenate([cosine_table, cosine_table], 1)[None]
    wide_sine = jnp.concatenate([sine_table, sine_table], 1)[None]
    scale_one = lax.rsqrt(jnp.mean(residual * residual, -1, keepdims=True) + norm_eps)
    normed_one = (residual * scale_one * gains[0]).astype(jnp.bfloat16)
    pick_rows = glob_select[0]
    glob_total = pick_rows.shape[0]
    selector = pick_rows.astype(jnp.bfloat16)
    glob_pos_part = jnp.sum(pick_rows * position[None, :], 1)
    digits = jnp.concatenate([glob_pos_part // 256, glob_pos_part % 256]).astype(jnp.bfloat16)
    digits = jnp.pad(digits[None], ((0, 7), (0, D - 2 * glob_total)))
    glob_rows = jnp.dot(selector, normed_one, preferred_element_type=jnp.float32).astype(jnp.bfloat16)
    glob_rows = add_all(jnp.concatenate([glob_rows, digits], 0), "fsdp").astype(jnp.bfloat16)
    packed = [normed_one, glob_rows, selector.reshape(-1, D)]
    packed = jnp.concatenate(packed, 0)
    packed = jnp.pad(packed, ((0, -packed.shape[0] % 32), (0, 0)))

    def over_bands(slice_rows):
        return lax.all_gather(slice_rows, "fsdp", axis=0, tiled=True)

    if aligned:
        half = BLK // 2
        low, high = (master[0, :, rows].astype(jnp.bfloat16) for rows in (slice(0, half), slice(half, BLK)))
        layout = slice_layout(band_total, rep_total)
        attn_layout = jnp.asarray(np.concatenate(layout[:4], 2))
        wanted = jnp.take(tile_order, by_place(attn_layout).reshape(-1), mode="clip")
        meta = jnp.stack([wanted // own_count == place, wanted % own_count], 0).astype(jnp.int32)
        attn_part = place_tiles(low, high, meta, *attn_layout.shape)
        attn_part = rep_scatter(attn_part).astype(jnp.bfloat16)
        low, attn_part = lax.optimization_barrier((low, attn_part))
        slots = square_pieces(low)
        attn = over_bands(attn_part)
        *slots, attn = lax.optimization_barrier((*slots, attn))
        grids = [lax.dynamic_index_in_dim(jnp.asarray(grid), place, 0, False) for grid in layout]

        def find(wanted):
            wanted = jnp.take(tile_order, jnp.concatenate([grid.reshape(-1) for grid in wanted]), mode="clip")
            entry, row = (wanted // own_count) ^ place, wanted % own_count
            cut = own_count // 2
            high = (entry == 3) & (row >= cut)
            found = jnp.stack([jnp.where(high, 4, entry), jnp.where(high, row - cut, row)], 0)
            return found.astype(jnp.int32)

        all_grid = jnp.concatenate(grids[4:], 1)
        (first_part,) = gather_strips(slots, find([all_grid]), [all_grid.shape])
        packed, first_part = lax.optimization_barrier((packed, first_part))
        early = over_bands(first_part)
    packed_all = rep_gather(packed)
    if aligned:
        packed_all, high = lax.optimization_barrier((packed_all, high))
        later_slots = square_pieces(high)
    normed_one_all = packed_all[:, :tok_count].reshape(-1, D)
    at = tok_count + glob_total
    glob_digits = packed_all[:, at, : 2 * glob_total].astype(jnp.float32)
    glob_place = glob_digits[:, :glob_total] * 256.0 + glob_digits[:, glob_total:]
    at += 8
    selector_all = packed_all[:, at : at + selector.size // D].reshape(rep_total, glob_total, tok_count)

    if aligned:
        in_width = q_width + 2 * kv_width
        w_inner, w_output = attn[:, :in_width], attn[:, in_width:]
    else:
        slots = lax.all_gather(master[0].astype(jnp.bfloat16), "rep", axis=0, tiled=True)
        tiles = jnp.take(slots, tile_order, axis=0, mode="clip")
        slices = cut_slices(band_matrices(tiles, band_total), band_total, rep_total)
        w_inner = over_bands(jnp.concatenate(slices[0:3], 1))
        w_output = over_bands(slices[3])
        w_gate = over_bands(slices[4])
        w_up = over_bands(slices[5])
        w_down = over_bands(slices[6])

    w_output = by_place(w_output.reshape(rep_total, q_width, -1)).reshape(D, -1)

    def mul(rows, weight):
        return jnp.dot(rows, weight, preferred_element_type=jnp.float32)

    def mul_back(rows, weight):
        return lax.dot_general(rows, weight, (((1,), (1,)), ((), ())), preferred_element_type=jnp.float32)

    def weight_grad(rows, grad_rows):
        return lax.dot_general(
            rows, grad_rows, (((0,), (0,)), ((), ())), preferred_element_type=jnp.float32
        ).astype(jnp.bfloat16)

    def own_sum(partial):
        return rep_scatter(partial.astype(jnp.bfloat16).reshape(rep_total, tok_count, D))

    inner_rows = mul(packed_all.reshape(-1, D), w_inner).reshape(rep_total, -1, w_inner.shape[1])
    packed_all, normed_one_all = lax.optimization_barrier((packed_all, normed_one_all))
    queries, own_pairs = rope_rows(inner_rows, tok_count, 0, q_width, kv_width, wide_cosine, wide_sine)
    glob_cosine, glob_sine = rope_tables(glob_place.reshape(-1))
    glob_cosine = jnp.concatenate([glob_cosine, glob_cosine], 1).reshape(rep_total, glob_total, -1)
    glob_sine = jnp.concatenate([glob_sine, glob_sine], 1).reshape(rep_total, glob_total, -1)
    (glob_pairs,) = rope_rows(
        inner_rows, glob_total, tok_count // glob_total, q_width, kv_width, glob_cosine, glob_sine, False
    )
    back_count = (WINDOW + tok_count - 2) // tok_count
    odd = band % 2 == 1
    by_chip = back_count == 2 and band_total % 2 == 0
    if by_chip:
        two_back = shifted(own_pairs, "fsdp", 2)
        pair_blocks = [two_back, to_core(jnp.where(odd, two_back, own_pairs))]
    else:
        pair_blocks = [shifted(own_pairs, "fsdp", distance) for distance in range(back_count, 0, -1)]
    pair_blocks = pair_blocks + [own_pairs, glob_pairs]
    glob_spots = jnp.broadcast_to(glob_place[:, :, None], (rep_total, glob_total, BLK))
    band_number = band.astype(jnp.int32).reshape(1)
    attended_low, lse = attend(band_number, glob_spots, queries, pair_blocks)
    if aligned:
        *later_slots, attended_low, early = lax.optimization_barrier((*later_slots, attended_low, early))
        last_grid = jnp.concatenate(grids[4:6], 1)
        last_part, down_part = gather_strips(
            later_slots, find([last_grid, grids[6]]), [last_grid.shape, grids[6].shape]
        )

        def by_strips(gathered):
            return gathered.reshape(band_total, -1, all_grid.shape[0], half, gathered.shape[-1])

        early, late, late_down = by_strips(early), by_strips(over_bands(last_part)), by_strips(over_bands(down_part))
    attended_all = rep_features(attended_low).reshape(-1, D)
    columns = mul(attended_all, w_output).astype(jnp.bfloat16).reshape(rep_total, tok_count, -1)
    branch = by_place(rep_exchange(columns)).transpose(1, 0, 2).reshape(tok_count, D)
    middle = residual + branch.astype(jnp.float32)
    scale_two = lax.rsqrt(jnp.mean(middle * middle, -1, keepdims=True) + norm_eps)
    normed_two = (middle * scale_two * gains[1]).astype(jnp.bfloat16)
    normed_two_all = rep_gather(normed_two).reshape(-1, D)
    normed_two_all, grad_top_now = lax.optimization_barrier((normed_two_all, grad_top))
    top_first = gather_first(grad_top_now)

    if aligned:
        gate_rows, up_rows, activation = forward_products(normed_two_all, early, late, FF // rep_total)
        top_first, activation = after(top_first, activation)
        grad_top_all = gather_join(gather_second(top_first)).reshape(-1, D)
        g_down = weight_grad(activation, grad_top_all)
        grad_top_all, g_down = lax.optimization_barrier((grad_top_all, g_down))
        grad_gate, grad_up, pieces, branch_pieces = backward_products(
            grad_top_all, gate_rows, up_rows, activation, early, late, late_down
        )
        normed_first = sum_first(pieces)
        normed_first, g_gate = after(normed_first, weight_grad(normed_two_all, grad_gate))
        grad_normed_two = sum_second(normed_first)
    else:
        gate_rows = mul(normed_two_all, w_gate)
        up_rows = mul(normed_two_all, w_up)
        sigmoid_gate = jax.nn.sigmoid(gate_rows)
        silu_gate = gate_rows * sigmoid_gate
        activation = (silu_gate * up_rows).astype(jnp.bfloat16)
        grad_top_all = gather_join(gather_second(top_first)).reshape(-1, D)
        g_down = weight_grad(activation, grad_top_all)
        grad_act = mul_back(grad_top_all, w_down)
        grad_gate = (
            grad_act * up_rows * sigmoid_gate * (1.0 + gate_rows * (1.0 - sigmoid_gate))
        ).astype(jnp.bfloat16)
        grad_up = (grad_act * silu_gate).astype(jnp.bfloat16)
        grad_normed_two = own_sum(mul_back(grad_gate, w_gate) + mul_back(grad_up, w_up))
        branch_pieces = (mul(activation, w_down),)
        g_gate = weight_grad(normed_two_all, grad_gate)
    grad_normed_two, g_gate = lax.optimization_barrier((grad_normed_two, g_gate))

    def over_tokens(partial):
        return lax.psum_scatter(partial, "fsdp", scatter_dimension=0, tiled=True)

    s_down = over_tokens(g_down)
    s_gate = over_tokens(g_gate)

    grad_middle = grad_top.astype(jnp.float32) + norm_back(middle, scale_two, gains[1], grad_normed_two)
    grad_parts = grad_middle.astype(jnp.bfloat16).reshape(tok_count, rep_total, -1).transpose(1, 0, 2)
    grad_columns = rep_exchange(by_place(grad_parts)).reshape(rep_total * tok_count, -1)
    grad_columns, grad_up = lax.optimization_barrier((grad_columns, grad_up))
    grad_attended, g_up = rep_features_sum(
        grad_columns.reshape(rep_total, tok_count, -1),
        w_output,
        lambda: weight_grad(normed_two_all, grad_up),
    )
    grad_attended = grad_attended.astype(jnp.bfloat16)
    (s_down, g_up), grad_attended = after((s_down, g_up), grad_attended)
    down_first = gather_first(s_down)
    grad_queries, *grad_blocks = attend_back(
        band_number, glob_spots, wide_cosine, wide_sine, queries, grad_attended, lse, pair_blocks
    )
    down_first, *grad_blocks = after(down_first, *grad_blocks)
    down_second = gather_second(down_first)
    branch_pieces, *grad_blocks = after(tuple(branch_pieces), *grad_blocks)
    branch_first = sum_first(branch_pieces) if aligned else (own_sum(branch_pieces[0]),)
    if by_chip:
        came = to_core(grad_blocks[1])
        total = grad_blocks[0].astype(jnp.float32) + came.astype(jnp.float32)
        sent = jnp.where(odd, total.astype(jnp.bfloat16), grad_blocks[0])
        returned = [shifted(sent, "fsdp", -2), jnp.where(odd, jnp.zeros_like(came), came)]
    else:
        returned = [
            shifted(grad_blocks[back_count - distance], "fsdp", -distance)
            for distance in range(1, back_count + 1)
        ]
    glob_grads = add_all(grad_blocks[-1], "fsdp")
    g_up, glob_grads, *returned = lax.optimization_barrier((g_up, glob_grads, *returned))
    s_up = over_tokens(g_up)
    grad_inner = join_grads(
        grad_queries, grad_blocks[-2], selector_all, glob_grads, wide_cosine, wide_sine, returned
    ).reshape(-1, q_width + 2 * kv_width)
    grad_normed_parts = mul_back(grad_inner, w_inner).astype(jnp.bfloat16).reshape(rep_total, tok_count, D)
    if square():
        normed_first = sum_first(split_pieces(grad_normed_parts))
    else:
        normed_first = (rep_scatter(grad_normed_parts),)
    grad_inner, grad_normed_parts = lax.optimization_barrier((grad_inner, grad_normed_parts))
    g_inner = weight_grad(normed_one_all, grad_inner)
    attended_all, g_inner = lax.optimization_barrier((attended_all, g_inner))
    g_output = weight_grad(attended_all, grad_columns)
    g_output = by_place(g_output.reshape(rep_total, q_width, -1)).reshape(D, -1)
    g_attn = with_layout_constraint(jnp.concatenate([g_inner, g_output], 1), Layout((0, 1)))
    branch_first, *normed_first = after(branch_first, *normed_first)
    down_second, s_gate, *normed_first = after(down_second, s_gate, *normed_first)
    s_down = gather_join(down_second)
    grad_normed_one = sum_second(normed_first) if square() else normed_first[0]
    block_out = middle + (sum_second(branch_first) if aligned else branch_first[0])
    gate_first = gather_first(s_gate)
    (s_up, *gate_first), g_attn, block_out, grad_normed_one = after(
        (s_up, *gate_first), g_attn, block_out, grad_normed_one
    )
    s_attn = over_tokens(g_attn)
    s_gate = gather_join(gather_second(gate_first))
    s_up = rep_gather(s_up)
    grad_input = grad_middle + norm_back(residual, scale_one, gains[0], grad_normed_one)

    gain_terms = jnp.stack(
        [
            jnp.sum(grad_normed_one * residual * scale_one, 0),
            jnp.sum(grad_normed_two * middle * scale_two, 0),
        ]
    )
    square_terms = jnp.stack(
        [jnp.sum(residual * residual), jnp.sum(middle * middle), jnp.sum(block_out * block_out)]
    )
    sums = jnp.concatenate([gain_terms.reshape(-1), square_terms])

    sums = add_all(add_all(sums, "rep"), "fsdp")
    sums, s_attn, s_up, s_gate = lax.optimization_barrier((sums, s_attn, s_up, s_gate))
    gain_grad, square_total = sums[: 2 * D].reshape(2, D), sums[2 * D :]

    slot_ids = jnp.arange(tile_total, dtype=jnp.int32)
    inverse = jnp.sum(jnp.where(tile_order[None, :] == slot_ids[:, None], slot_ids[None, :], 0), 1)
    own_slots = place * own_count + jnp.arange(own_count, dtype=jnp.int32)
    owned_tiles = jnp.take(inverse, own_slots, mode="clip")
    if aligned:
        sources = [rep_gather(s_attn), s_gate, s_up, s_down]
        where = np.zeros((4, rep_total, tile_total), np.int32)
        first_col = 0
        for kind, grid in enumerate(layout):
            rows, cols = grid.shape[1:]
            first_col = 0 if kind >= 4 else first_col
            for there in range(rep_total):
                numbers = grid[there].reshape(-1)
                at = np.arange(rows * cols)
                where[0, :, numbers] = max(kind - 3, 0)
                where[2, :, numbers] = (at // cols * BLK)[:, None]
                where[3, :, numbers] = (at % cols * BLK + first_col)[:, None]
                for here in range(rep_total):
                    where[1, here, numbers] = here ^ there
            first_col += cols * BLK
        tile_spots = lax.dynamic_index_in_dim(jnp.asarray(where), place, 1, False)
        meta = jnp.take(tile_spots, owned_tiles, axis=1, mode="clip")
    else:
        splits = [0, q_width, q_width + kv_width, q_width + 2 * kv_width, s_attn.shape[1]]
        stacks = [rep_gather(s_attn[:, low:high]) for low, high in zip(splits, splits[1:])]
        stacks += [s_gate, s_up, s_down]
        sources = [band_tiles(join_slices(stacks, band_total, rep_total))]
        meta = jnp.stack([0 * owned_tiles, owned_tiles, 0 * owned_tiles, 0 * owned_tiles], 0)
    slot_rates = jnp.take(kind_rates(band_total), owned_tiles, mode="clip")
    new_first, new_second, new_master, master_copy = adam(
        meta,
        slot_rates,
        (master[0], first_moment[0], second_moment[0], left_basis[0], right_basis[0]),
        sources,
    )
    new_gain_first = beta_one * gain_first + (1.0 - beta_one) * gain_grad
    new_gain_second = beta_two * gain_second + (1.0 - beta_two) * gain_grad * gain_grad
    gain_step = (
        new_gain_first
        / (1.0 - beta_one**STEP)
        / (jnp.sqrt(new_gain_second / (1.0 - beta_two**STEP)) + adam_eps)
    )
    new_gains = gains - gain_rate * gain_step
    rms_stats = jnp.sqrt(square_total / (rep_total * band_total * tok_count * D))
    return (
        block_out[None],
        grad_input[None],
        new_first[None],
        new_second[None],
        new_master[None],
        master_copy[None],
        new_gain_first,
        new_gain_second,
        new_gains,
        rms_stats,
    )


def solution(mesh):
    in_specs = (
        P("rep", "fsdp", None),
        P("rep", "fsdp", None),
        P("rep", None, "fsdp"),
        P("fsdp", None),
        P("fsdp", "rep", None, None),
        P("fsdp", "rep", None, None),
        P("fsdp", "rep", None, None),
        P("fsdp", "rep", None, None),
        P("fsdp", "rep", None, None),
        P(),
        P(),
        P(),
    )
    out_specs = (
        P("rep", "fsdp", None),
        P("rep", "fsdp", None),
        P("fsdp", "rep", None, None),
        P("fsdp", "rep", None, None),
        P("fsdp", "rep", None, None),
        P("fsdp", "rep", None, None),
        P(),
        P(),
        P(),
        P(),
    )
    return jax.shard_map(
        per_device, mesh=mesh, in_specs=in_specs, out_specs=out_specs, check_vma=False
    )
```

```python
import functools

import jax
import jax.numpy as jnp
import numpy as np
from jax import lax
from jax.experimental import pallas as pl
from jax.experimental.layout import Layout, with_layout_constraint
from jax.experimental.pallas import tpu as pltpu
from jax.sharding import PartitionSpec as P

D = 2048
H = 32
KVH = 8
HD = 64
FF = 8192
WINDOW = 512
BLK = 128
STEP = 10


norm_eps = 1e-05
rope_theta = 500000.0
beta_one = 0.5
beta_two = 0.5
adam_eps = 1e-08
weight_decay = 0.1
gain_rate = 0.5
masked_value = -1e30


def matrix_shapes():
    kv_width = KVH * HD
    return [(D, D), (D, kv_width), (D, kv_width), (D, D), (D, FF), (D, FF), (FF, D)]


def kind_rates(band_total):
    rate_list = [
        D ** (-0.5),
        D ** (-0.5),
        D ** (-0.5),
        (D * 8 // WINDOW) ** (-0.5),
        D ** (-0.5),
        D ** (-0.5),
        FF ** (-0.5),
    ]
    pieces = []
    for (row_total, col_total), rate_value in zip(matrix_shapes(), rate_list):
        tile_count = row_total // band_total // BLK * (col_total // BLK)
        pieces.append(jnp.full((tile_count,), rate_value, jnp.float32))
    return jnp.concatenate(pieces)


def band_matrices(tiles, band_total):
    matrices = []
    offset = 0
    for row_total, col_total in matrix_shapes():
        band_rows = row_total // band_total
        tile_count = band_rows // BLK * (col_total // BLK)
        segment = tiles[offset : offset + tile_count].reshape(
            band_rows // BLK, col_total // BLK, BLK, BLK
        )
        matrices.append(segment.transpose(0, 2, 1, 3).reshape(band_rows, col_total))
        offset += tile_count
    return matrices


def band_tiles(matrices):
    pieces = []
    for matrix in matrices:
        row_count, col_count = matrix.shape
        segment = matrix.reshape(row_count // BLK, BLK, col_count // BLK, BLK).transpose(0, 2, 1, 3)
        pieces.append(segment.reshape(-1, BLK, BLK))
    return jnp.concatenate(pieces, 0)


def rope_tables(position):
    halves = jnp.arange(HD // 2, dtype=jnp.float32) * (2.0 / HD)
    frequency = rope_theta ** (-halves)
    angles = position.astype(jnp.float32)[:, None] * frequency[None, :]
    angles = jnp.concatenate([angles, angles], 1)
    return (jnp.cos(angles), jnp.sin(angles))


def rotate(vectors, cosine_table, sine_table):
    half_width = vectors.shape[-1] // 2
    turned = jnp.concatenate([-vectors[..., half_width:], vectors[..., :half_width]], -1)
    return vectors * cosine_table[:, None, :] + turned * sine_table[:, None, :]


def rotate_back(grad_rows, cosine_table, sine_table):
    half_width = grad_rows.shape[-1] // 2
    scaled = grad_rows * sine_table[:, None, :]
    turned = jnp.concatenate([scaled[..., half_width:], -scaled[..., :half_width]], -1)
    return grad_rows * cosine_table[:, None, :] + turned


def norm_back(values, row_scale, gain_row, grad_rows):
    weighted = grad_rows * gain_row
    return row_scale * weighted - values * row_scale**3 * jnp.mean(
        weighted * values, -1, keepdims=True
    )


def to_rep(block, distance):
    route = [(i, i ^ distance) for i in range(lax.axis_size("rep"))]
    return lax.ppermute(block, "rep", route)


def square():
    return lax.axis_size("rep") == 4


def gather_first(block):
    if not square():
        return (lax.all_gather(block, "rep", axis=0),)
    return block, to_rep(block, 1), to_rep(block, 2)


def gather_second(first):
    if not square():
        return first
    block, near, far = first
    cut = block.shape[0] // 2
    return block, near, far, to_rep(near[:cut], 2), to_rep(far[cut:], 1)


def gather_join(pieces):
    if not square():
        return pieces[0]
    return jnp.concatenate(pieces, 0).reshape((4,) + pieces[0].shape)


def square_pieces(block):
    return gather_second(gather_first(block))


def rep_gather(block):
    return gather_join(gather_second(gather_first(block)))


def after(values, *others):
    count = len(values)
    tied = lax.optimization_barrier((*values, *others))
    return tuple(tied[:count]), *tied[count:]


def rep_of(entry):
    place = lax.axis_index("rep")
    return place ^ entry if square() else entry


def rep_scatter(parts):
    if not square():
        flat = parts.reshape(-1, parts.shape[-1])
        return lax.psum_scatter(flat, "rep", scatter_dimension=0, tiled=True).astype(jnp.float32)
    return sum_pieces(*split_pieces(parts))


def split_pieces(parts):
    half = parts.shape[-1] // 2
    low, high = parts[..., :half], parts[..., half:]
    return jnp.stack([low[0], low[2]], 0), jnp.stack([low[1], low[3]], 0), high[:2], high[2:]


def sum_first(pieces):
    low_kept, low_sent, high_kept, high_sent = pieces
    parts = []
    for kept, sent, first in ((low_kept, low_sent, 1), (high_kept, high_sent, 2)):
        came = to_rep(sent, first)
        parts.append(kept[0].astype(jnp.float32) + came[0].astype(jnp.float32))
        parts.append((kept[1].astype(jnp.float32) + came[1].astype(jnp.float32)).astype(kept.dtype))
    return tuple(parts)


def sum_second(parts):
    low, low_other, high, high_other = parts
    low = low + to_rep(low_other, 2).astype(jnp.float32)
    high = high + to_rep(high_other, 1).astype(jnp.float32)
    return jnp.concatenate([low, high], -1)


def sum_pieces(*pieces):
    return sum_second(sum_first(pieces))


def add_all(value, axis):
    size = lax.axis_size(axis)
    total = value.astype(jnp.float32)
    distance = 1
    while distance < size:
        count = 2 if (size // distance).bit_length() % 2 == 0 else 4
        low = total.astype(value.dtype)
        others = []
        for step in range(1, count):
            route = [(i, i ^ (step * distance)) for i in range(size)]
            others.append(lax.ppermute(low, axis, route).astype(jnp.float32))
        total = total + others[0]
        if count == 4:
            total = total + (others[1] + others[2])
        distance *= count
    return total


def rep_features(block):
    if not square():
        return lax.all_gather(block, "rep", axis=2, tiled=True)
    own, near, far, low, high = square_pieces(block)
    return jnp.concatenate(
        [
            own,
            jnp.stack([near[1], near[0], near[3], near[2]], 0),
            jnp.stack([far[2], far[3], far[0], far[1]], 0),
            jnp.stack([high[1], high[0], low[1], low[0]], 0),
        ],
        2,
    )


def write_pieces(entry, rows, values, refs):
    low_kept, low_sent, high_kept, high_sent = refs
    half = low_kept.shape[-1]
    values = values.astype(jnp.bfloat16)
    (low_sent if entry % 2 else low_kept)[entry // 2, rows] = values[:, :half]
    (high_sent if entry // 2 else high_kept)[entry % 2, rows] = values[:, half:]


def swapped_kernel(x_ref, w_ref, *refs):
    reps, rows, _ = x_ref.shape
    width = w_ref.shape[0] // reps
    for entry in range(reps):
        weight = w_ref[entry * width : (entry + 1) * width]
        for there in range(reps):
            product = over_last(x_ref[there ^ entry], weight)
            write_pieces(entry, slice(there * rows, (there + 1) * rows), product, refs)


def rep_features_sum(columns, weight, meanwhile):
    reps, rows, depth = columns.shape
    width = weight.shape[0] // reps
    if square():
        pieces = pl.pallas_call(
            swapped_kernel,
            out_shape=[jax.ShapeDtypeStruct((2, reps * rows, width // 2), jnp.bfloat16)] * 4,
            compiler_params=pltpu.CompilerParams(vmem_limit_bytes=32 * 2**20),
            cost_estimate=pl.CostEstimate(
                flops=2 * reps * columns.size * width,
                bytes_accessed=10 * columns.size,
                transcendentals=0,
            ),
        )(columns, weight)
        first = sum_first(pieces)
        first, other = after(first, meanwhile())
        total = sum_second(first)
    else:
        other = meanwhile()
        product = over_last(columns.reshape(-1, depth), weight).astype(jnp.bfloat16)
        swapped = product.reshape(reps, rows, reps, width).transpose(2, 0, 1, 3)
        total = rep_scatter(swapped.reshape(reps, reps * rows, width))
    return total.reshape(reps, rows, width), other


def rep_exchange(parts):
    if not square():
        return lax.all_to_all(parts, "rep", 0, 0)
    return jnp.stack([parts[0]] + [to_rep(parts[entry], entry) for entry in (1, 2, 3)], 0)


def by_place(parts):
    entries = [rep_of(entry) for entry in range(parts.shape[0])]
    return jnp.stack([lax.dynamic_index_in_dim(parts, entry, 0, False) for entry in entries], 0)


def to_core(block):
    return lax.ppermute(block, "fsdp", [(i, i ^ 1) for i in range(lax.axis_size("fsdp"))])


def shifted(block, axis, distance):
    devices = range(lax.axis_size(axis))
    route = [(i - distance, i) for i in devices if i - distance in devices]
    return lax.ppermute(block, axis, route)


def tile_offsets(band_total):
    offsets = [0]
    for row_total, col_total in matrix_shapes():
        offsets.append(offsets[-1] + row_total // band_total // BLK * (col_total // BLK))
    return offsets


def whole_tiles(band_total, rep_total):
    return KVH * HD // rep_total % BLK == 0 and FF // band_total // rep_total % BLK == 0


def slice_layout(band_total, rep_total):
    offsets = tile_offsets(band_total)
    layout = []
    for kind, (row_total, col_total) in enumerate(matrix_shapes()):
        rows, cols = row_total // band_total // BLK, col_total // BLK
        grid = offsets[kind] + np.arange(rows * cols).reshape(rows, cols)
        if kind == 6:
            layout.append(grid.reshape(rep_total, rows // rep_total, cols))
        elif kind in (4, 5):
            cut = grid.reshape(rows, band_total, rep_total, -1).transpose(2, 0, 1, 3)
            layout.append(cut.reshape(rep_total, rows, -1))
        else:
            layout.append(grid.reshape(rows, rep_total, -1).transpose(1, 0, 2))
    return layout


def tiles_to_matrix(tiles):
    rows, cols = tiles.shape[:2]
    return tiles.transpose(0, 2, 1, 3).reshape(rows * BLK, cols * BLK)


def matrix_to_tiles(matrix):
    rows, cols = matrix.shape
    cut = matrix.reshape(rows // BLK, BLK, cols // BLK, BLK)
    return cut.transpose(0, 2, 1, 3).reshape(-1, BLK, BLK)


def cut_slices(matrices, band_total, rep_total):
    place = lax.axis_index("rep")
    slices = []
    for kind, matrix in enumerate(matrices):
        rows, cols = matrix.shape
        if kind == 6:
            slices.append(lax.dynamic_slice_in_dim(matrix, place * (rows // rep_total), rows // rep_total, 0))
        elif kind in (4, 5):
            cut = matrix.reshape(rows, band_total, rep_total, -1)
            slices.append(lax.dynamic_index_in_dim(cut, place, 2, False).reshape(rows, -1))
        else:
            slices.append(lax.dynamic_slice_in_dim(matrix, place * (cols // rep_total), cols // rep_total, 1))
    return slices


def join_slices(stacks, band_total, rep_total):
    matrices = []
    for kind, stack in enumerate(stacks):
        rows, cols = stack.shape[1:]
        if kind == 6:
            matrices.append(stack.reshape(-1, cols))
        elif kind in (4, 5):
            cut = stack.reshape(rep_total, rows, band_total, -1).transpose(1, 2, 0, 3)
            matrices.append(cut.reshape(rows, -1))
        else:
            matrices.append(stack.transpose(1, 0, 2).reshape(rows, -1))
    return matrices


def gather_kernel(grids, meta, *refs):
    source_total = len(refs) - len(grids) - 1
    sources, targets, done = refs[:source_total], refs[source_total:-1], refs[-1]
    height = sources[0].shape[1]
    start = 0
    for place, (target, (rows, cols)) in enumerate(zip(targets, grids)):

        def one(tile, carry, target=target, rows=rows, cols=cols, start=start, place=place):
            kind = meta[0, start + tile]
            row = meta[1, start + tile]
            across = tile % cols
            top = pl.multiple_of((across // 2 * rows + tile // cols) * height, height)
            left = pl.multiple_of(across % 2 * BLK, BLK)
            for number, source in enumerate(sources):

                @pl.when(kind == number)
                def _(source=source):
                    pltpu.make_async_copy(
                        source.at[row], target.at[pl.ds(top, height), pl.ds(left, BLK)], done.at[place]
                    ).start()

            return carry

        lax.fori_loop(0, rows * cols, one, 0)
        start += rows * cols
    for place, target in enumerate(targets):
        pltpu.make_async_copy(target, target, done.at[place]).wait()


def gather_strips(sources, meta, grids):
    anywhere = pl.BlockSpec(memory_space=pl.ANY)
    height = sources[0].shape[1]
    out_shape = [
        jax.ShapeDtypeStruct((cols // 2 * rows * height, 2 * BLK), jnp.bfloat16) for rows, cols in grids
    ]
    return pl.pallas_call(
        functools.partial(gather_kernel, grids),
        out_shape=out_shape,
        grid_spec=pltpu.PrefetchScalarGridSpec(
            num_scalar_prefetch=1,
            grid=(1,),
            in_specs=[anywhere] * len(sources),
            out_specs=[pl.BlockSpec(shape.shape, lambda i, *_: (0, 0)) for shape in out_shape],
            scratch_shapes=[pltpu.SemaphoreType.DMA((len(grids),))],
        ),
        compiler_params=pltpu.CompilerParams(vmem_limit_bytes=32 * 2**20),
        cost_estimate=pl.CostEstimate(
            flops=0, bytes_accessed=sum(4 * shape.size for shape in out_shape), transcendentals=0
        ),
    )(meta, *sources)


def place_kernel(entries, rows, cols, meta, low, high, out_ref, done):
    out_ref[...] = jnp.zeros_like(out_ref)
    height = low.shape[1]

    def copies(tile):
        entry, rest = tile // (rows * cols), tile % (rows * cols)
        top = rest // cols * (2 * height)
        left = pl.multiple_of(rest % cols * BLK, BLK)
        return [
            pltpu.make_async_copy(
                half.at[meta[1, tile]],
                out_ref.at[entry, pl.ds(pl.multiple_of(top + part * height, height), height), pl.ds(left, BLK)],
                done.at[part],
            )
            for part, half in enumerate((low, high))
        ]

    def begin(tile, carry):
        @pl.when(meta[0, tile] == 1)
        def _():
            for copy in copies(tile):
                copy.start()

        return carry

    def finish(tile, carry):
        @pl.when(meta[0, tile] == 1)
        def _():
            for copy in copies(tile):
                copy.wait()

        return carry

    lax.fori_loop(0, entries * rows * cols, begin, 0)
    lax.fori_loop(0, entries * rows * cols, finish, 0)


def place_tiles(low, high, meta, entries, rows, cols):
    shape = (entries, rows * BLK, cols * BLK)
    anywhere = pl.BlockSpec(memory_space=pl.ANY)
    return pl.pallas_call(
        functools.partial(place_kernel, entries, rows, cols),
        out_shape=jax.ShapeDtypeStruct(shape, jnp.bfloat16),
        grid_spec=pltpu.PrefetchScalarGridSpec(
            num_scalar_prefetch=1,
            grid=(1,),
            in_specs=[anywhere, anywhere],
            out_specs=pl.BlockSpec(shape, lambda i, *_: (0, 0, 0)),
            scratch_shapes=[pltpu.SemaphoreType.DMA((2,))],
        ),
        compiler_params=pltpu.CompilerParams(vmem_limit_bytes=32 * 2**20),
        cost_estimate=pl.CostEstimate(
            flops=0, bytes_accessed=4 * entries * rows * cols * BLK * BLK, transcendentals=0
        ),
    )(meta, low, high)


def half_turn(values):
    lane = lax.broadcasted_iota(jnp.int32, values.shape, 1)
    lanes = values.shape[1]
    first = lane % HD < HD // 2
    return first, jnp.where(
        first, pltpu.roll(values, lanes - HD // 2, 1), pltpu.roll(values, HD // 2, 1)
    )


def strip_copies(early, late, target, done):
    return [
        pltpu.make_async_copy(half, target.at[:, :, number], done.at[number])
        for number, half in enumerate((early, late))
    ]


def forward_kernel(x_ref, early, late, gate_ref, up_ref, act_ref, weights, done):
    step, steps = pl.program_id(0), pl.num_programs(0)
    slot = step % 2
    width = weights.shape[-1]

    def copies(number, at_step, at_slot):
        strip = number * steps + at_step
        return strip_copies(
            early.at[:, strip], late.at[:, strip], weights.at[number, at_slot], done.at[number, at_slot]
        )

    def fetch(at_step, at_slot):
        for number in range(2):
            for copy in copies(number, at_step, at_slot):
                copy.start()

    @pl.when(step == 0)
    def _():
        fetch(0, 0)

    @pl.when(step + 1 < steps)
    def _():
        fetch(step + 1, 1 - slot)

    for number in range(2):
        for copy in copies(number, step, slot):
            copy.wait()
    gate_weight, up_weight = (weights[number, slot].reshape(-1, width) for number in range(2))
    chunk = min(2 * BLK, x_ref.shape[0])
    for first in range(0, x_ref.shape[0], chunk):
        rows = slice(first, first + chunk)
        gate = jnp.dot(x_ref[rows], gate_weight, preferred_element_type=jnp.float32)
        up = jnp.dot(x_ref[rows], up_weight, preferred_element_type=jnp.float32)
        gate_ref[rows] = gate.astype(jnp.bfloat16)
        up_ref[rows] = up.astype(jnp.bfloat16)
        act_ref[rows] = (gate * jax.nn.sigmoid(gate) * up).astype(jnp.bfloat16)


def forward_products(rows, early, late, columns):
    tokens, depth = rows.shape
    bands, _, tiles, half, width = early.shape
    block = pl.BlockSpec((tokens, width), lambda n: (0, n))
    anywhere = pl.BlockSpec(memory_space=pl.ANY)
    return pl.pallas_call(
        forward_kernel,
        out_shape=[jax.ShapeDtypeStruct((tokens, columns), jnp.bfloat16)] * 3,
        grid=(columns // width,),
        in_specs=[pl.BlockSpec(rows.shape, lambda n: (0, 0)), anywhere, anywhere],
        out_specs=[block] * 3,
        scratch_shapes=[
            pltpu.VMEM((2, 2, bands, tiles, 2, half, width), jnp.bfloat16),
            pltpu.SemaphoreType.DMA((2, 2, 2)),
        ],
        compiler_params=pltpu.CompilerParams(vmem_limit_bytes=48 * 2**20),
        cost_estimate=pl.CostEstimate(
            flops=tokens * depth * columns // 8, bytes_accessed=2 * rows.size, transcendentals=0
        ),
    )(rows, early, late)


def backward_kernel(top_ref, gate_ref, up_ref, act_ref, early, late, late_down, *refs):
    dgate_ref, dup_ref = refs[:2]
    pieces, branch_pieces = refs[2:6], refs[6:10]
    weights, downs, total, branch, done, down_done = refs[10:]
    step, steps = pl.program_id(0), pl.num_programs(0)
    slot = step % 2
    strips, width = downs.shape[1], downs.shape[-1]

    def down_copies(at_step, at_slot):
        wanted = pl.ds(2 * steps, strips)
        return strip_copies(
            early.at[at_step, wanted], late_down.at[at_step], downs.at[at_slot], down_done.at[at_slot]
        )

    def copies(number, at_step, at_slot):
        strip = number * steps + at_step
        return strip_copies(
            early.at[:, strip], late.at[:, strip], weights.at[number, at_slot], done.at[number, at_slot]
        )

    def fetch(at_step, at_slot):
        for copy in down_copies(at_step, at_slot):
            copy.start()
        for number in range(2):
            for copy in copies(number, at_step, at_slot):
                copy.start()

    @pl.when(step == 0)
    def _():
        fetch(0, 0)
        total[...] = jnp.zeros_like(total)
        branch[...] = jnp.zeros_like(branch)

    @pl.when(step + 1 < steps)
    def _():
        fetch(step + 1, 1 - slot)

    for copy in down_copies(step, slot):
        copy.wait()
    for number in range(2):
        for copy in copies(number, step, slot):
            copy.wait()
    gate_weight, up_weight = (weights[number, slot].reshape(-1, width) for number in range(2))
    chunk = min(4 * BLK, top_ref.shape[0])
    for first in range(0, top_ref.shape[0], chunk):
        rows = slice(first, first + chunk)
        grad_act = 0.0
        for strip in range(strips):
            lanes = slice(strip * width, (strip + 1) * width)
            down = downs[slot, strip].reshape(-1, width)
            grad_act = grad_act + over_last(top_ref[rows, lanes], down)
            branch[rows, lanes] += jnp.dot(act_ref[rows], down, preferred_element_type=jnp.float32)
        gate = gate_ref[rows].astype(jnp.float32)
        up = up_ref[rows].astype(jnp.float32)
        sigmoid_gate = jax.nn.sigmoid(gate)
        grad_gate = grad_act * up * sigmoid_gate * (1.0 + gate * (1.0 - sigmoid_gate))
        grad_gate = grad_gate.astype(jnp.bfloat16)
        grad_up = (grad_act * (gate * sigmoid_gate)).astype(jnp.bfloat16)
        dgate_ref[rows] = grad_gate
        dup_ref[rows] = grad_up
        total[rows] += over_last(grad_gate, gate_weight) + over_last(grad_up, up_weight)

    @pl.when(step == steps - 1)
    def _():
        rows = total.shape[0] // 4
        for entry in range(4):
            part = slice(entry * rows, (entry + 1) * rows)
            write_pieces(entry, slice(0, rows), total[part], pieces)
            write_pieces(entry, slice(0, rows), branch[part], branch_pieces)


def backward_products(top, gate, up, act, early, late, late_down):
    tokens, depth = top.shape
    columns = gate.shape[1]
    bands, _, tiles, half, width = early.shape
    strips = depth // width
    block = pl.BlockSpec((tokens, width), lambda n: (0, n))
    anywhere = pl.BlockSpec(memory_space=pl.ANY)
    piece = jax.ShapeDtypeStruct((2, tokens // 4, depth // 2), jnp.bfloat16)
    grads = jax.ShapeDtypeStruct((tokens, columns), jnp.bfloat16)
    outs = pl.pallas_call(
        backward_kernel,
        out_shape=[grads] * 2 + [piece] * 8,
        grid=(columns // width,),
        in_specs=[pl.BlockSpec(top.shape, lambda n: (0, 0))] + [block] * 3 + [anywhere] * 3,
        out_specs=[block] * 2 + [pl.BlockSpec(piece.shape, lambda n: (0, 0, 0))] * 8,
        scratch_shapes=[
            pltpu.VMEM((2, 2, bands, tiles, 2, half, width), jnp.bfloat16),
            pltpu.VMEM((2, strips, tiles, 2, half, width), jnp.bfloat16),
            pltpu.VMEM((tokens, depth), jnp.float32),
            pltpu.VMEM((tokens, depth), jnp.float32),
            pltpu.SemaphoreType.DMA((2, 2, 2)),
            pltpu.SemaphoreType.DMA((2, 2)),
        ],
        compiler_params=pltpu.CompilerParams(vmem_limit_bytes=60 * 2**20),
        cost_estimate=pl.CostEstimate(
            flops=8 * tokens * depth * columns, bytes_accessed=8 * columns * depth, transcendentals=0
        ),
    )(top, gate, up, act, early, late, late_down)
    return outs[0], outs[1], outs[2:6], outs[6:10]


def rope_kernel(q_width, kv_width, x_ref, cos_ref, sin_ref, *outs):
    width = x_ref.shape[-1]
    for start in range(0, width, BLK):
        values = x_ref[0, :, start : start + BLK]
        first, turned = half_turn(values)
        sines = sin_ref[0]
        turned_rows = values * cos_ref[0] + turned * jnp.where(first, -sines, sines)
        if start + BLK > q_width + kv_width:
            column = lax.broadcasted_iota(jnp.int32, values.shape, 1) + start
            turned_rows = jnp.where(column >= q_width + kv_width, values, turned_rows)
        if start < q_width:
            outs[0][0, :, start : start + BLK] = (turned_rows * HD ** (-0.5)).astype(jnp.bfloat16)
        else:
            outs[-1][0, :, start - q_width : start - q_width + BLK] = turned_rows.astype(jnp.bfloat16)


def rope_rows(inner, rows, row_block, q_width, kv_width, cosines, sines, with_queries=True):
    seqs, _, width = inner.shape
    shared = cosines.shape[0] == 1
    table = pl.BlockSpec((1, rows, BLK), lambda s: (0 if shared else s, 0, 0))
    widths = [q_width, 2 * kv_width]
    column_block = 0
    if not with_queries:
        width, column_block = 2 * kv_width, q_width // (2 * kv_width)
        widths, q_width = widths[1:], 0
    return pl.pallas_call(
        functools.partial(rope_kernel, q_width, kv_width),
        out_shape=[jax.ShapeDtypeStruct((seqs, rows, w), jnp.bfloat16) for w in widths],
        grid=(seqs,),
        in_specs=[pl.BlockSpec((1, rows, width), lambda s: (s, row_block, column_block)), table, table],
        out_specs=[pl.BlockSpec((1, rows, w), lambda s: (s, 0, 0)) for w in widths],
        cost_estimate=pl.CostEstimate(
            flops=6 * seqs * rows * width, bytes_accessed=6 * seqs * rows * width, transcendentals=0
        ),
    )(inner, cosines, sines)


def fill_bias(band_ref, gpos_ref, bias_ref, rows, window_len):
    band = band_ref[0]

    @pl.when(pl.program_id(0) == 0)
    def _():
        key = lax.broadcasted_iota(jnp.int32, (window_len, rows), 0) + (
            band * rows - (window_len - rows)
        )
        query = lax.broadcasted_iota(jnp.int32, (window_len, rows), 1) + band * rows
        inside = (key > query - WINDOW) & (key <= query) & (key >= 0)
        bias_ref[:window_len] = jnp.where(inside, 0.0, masked_value)

    glob_total = gpos_ref.shape[1]
    query = lax.broadcasted_iota(jnp.int32, (glob_total, rows), 1) + (band * rows - WINDOW)
    spot = jnp.broadcast_to(gpos_ref[0][:, :1], (glob_total, rows))
    bias_ref[window_len:] = jnp.where(spot <= query.astype(jnp.float32), 0.0, masked_value)


def over_last(left, right):
    return lax.dot_general(left, right, (((1,), (1,)), ((), ())), preferred_element_type=jnp.float32)


def over_first(left, right):
    return lax.dot_general(left, right, (((0,), (0,)), ((), ())), preferred_element_type=jnp.float32)


def attend_kernel(block_total, band_ref, gpos_ref, q_ref, *refs):
    blocks, (out_ref, lse_ref, bias_ref) = refs[:block_total], refs[block_total:]
    rows, q_width = q_ref.shape[1:]
    kv_width = blocks[0].shape[2] // 2
    heads, group = q_width // HD, q_width // kv_width
    window_len = rows * (block_total - 1)
    fill_bias(band_ref, gpos_ref, bias_ref, rows, window_len)
    starts = [rows * number for number in range(block_total)]
    pending = []
    for head in range(heads):
        left = head // group * HD
        queries = q_ref[0, :, head * HD : (head + 1) * HD]
        scores = [
            over_last(block[0, :, left : left + HD], queries)
            + bias_ref[start : start + block.shape[1]]
            for block, start in zip(blocks, starts)
        ]
        top = functools.reduce(jnp.maximum, [jnp.max(part, 0, keepdims=True) for part in scores])
        total = 0.0
        mixed = 0.0
        for block, part in zip(blocks, scores):
            weights = jnp.exp(part - top)
            total = total + jnp.sum(weights, 0, keepdims=True)
            mixed = mixed + over_first(
                block[0, :, kv_width + left : kv_width + left + HD], weights.astype(jnp.bfloat16)
            )
        lse_ref[0, head : head + 1, :] = top + jnp.log(total)
        pending.append(mixed / total)
        if len(pending) * HD == BLK or head == heads - 1:
            stop = (head + 1) * HD
            both = jnp.concatenate(pending, 0).T
            out_ref[0, :, stop - both.shape[1] : stop] = both.astype(jnp.bfloat16)
            pending = []


def attend(band, gpos, queries, blocks):
    seqs, rows, q_width = queries.shape
    heads = q_width // HD
    key_total = sum(block.shape[1] for block in blocks)

    def whole(array):
        return pl.BlockSpec((1,) + array.shape[1:], lambda s, *_: (s, 0, 0))

    out_shape = [
        jax.ShapeDtypeStruct((seqs, rows, q_width), jnp.bfloat16),
        jax.ShapeDtypeStruct((seqs, heads, rows), jnp.float32),
    ]
    return pl.pallas_call(
        functools.partial(attend_kernel, len(blocks)),
        out_shape=out_shape,
        grid_spec=pltpu.PrefetchScalarGridSpec(
            num_scalar_prefetch=1,
            grid=(seqs,),
            in_specs=[whole(array) for array in (gpos, queries, *blocks)],
            out_specs=[whole(array) for array in out_shape],
            scratch_shapes=[pltpu.VMEM((key_total, rows), jnp.float32)],
        ),
        compiler_params=pltpu.CompilerParams(vmem_limit_bytes=48 * 2**20),
        cost_estimate=pl.CostEstimate(
            flops=16 * seqs * heads * rows * key_total * HD,
            bytes_accessed=4 * queries.size,
            transcendentals=seqs * heads * rows * key_total,
        ),
    )(band, gpos, queries, *blocks)


def attend_back_kernel(block_total, band_ref, gpos_ref, cos_ref, sin_ref, q_ref, grad_ref, lse_ref, *refs):
    blocks = refs[:block_total]
    dq_ref = refs[block_total]
    out_refs = refs[block_total + 1 : 2 * block_total + 1]
    bias_ref = refs[-1]
    rows, q_width = q_ref.shape[1:]
    kv_width = blocks[0].shape[2] // 2
    heads, group = q_width // HD, q_width // kv_width
    window_len = rows * (block_total - 1)
    fill_bias(band_ref, gpos_ref, bias_ref, rows, window_len)
    starts = [rows * number for number in range(block_total)]
    pending = []
    for kv_head in range(kv_width // HD):
        left = kv_head * HD
        key_sums = [0.0] * block_total
        value_sums = [0.0] * block_total
        for head in range(kv_head * group, (kv_head + 1) * group):
            queries = q_ref[0, :, head * HD : (head + 1) * HD]
            grads = grad_ref[0, :, head * HD : (head + 1) * HD]
            lse = lse_ref[0, head : head + 1, :]
            soft, soft_grads = [], []
            inner = 0.0
            for number, (block, start) in enumerate(zip(blocks, starts)):
                part = over_last(block[0, :, left : left + HD], queries)
                part = jnp.exp(part + bias_ref[start : start + block.shape[1]] - lse)
                slope = over_last(block[0, :, kv_width + left : kv_width + left + HD], grads)
                inner = inner + jnp.sum(part * slope, 0, keepdims=True)
                soft.append(part)
                soft_grads.append(slope)
            turned = 0.0
            for number, block in enumerate(blocks):
                score_grads = (soft[number] * (soft_grads[number] - inner)).astype(jnp.bfloat16)
                value_sums[number] = value_sums[number] + jnp.dot(
                    soft[number].astype(jnp.bfloat16), grads, preferred_element_type=jnp.float32
                )
                key_sums[number] = key_sums[number] + jnp.dot(
                    score_grads, queries, preferred_element_type=jnp.float32
                )
                turned = turned + over_first(block[0, :, left : left + HD], score_grads)
            pending.append(turned)
            if len(pending) * HD == BLK or head == heads - 1:
                stop = (head + 1) * HD
                both = jnp.concatenate(pending, 0).T * HD ** (-0.5)
                pending = []
                first, other = half_turn(both * sin_ref[0])
                both = both * cos_ref[0] + jnp.where(first, other, -other)
                dq_ref[0, :, stop - both.shape[1] : stop] = both.astype(jnp.bfloat16)
        for number, out_ref in enumerate(out_refs):
            out_ref[0, :, left : left + HD] = key_sums[number].astype(out_ref.dtype)
            out_ref[0, :, kv_width + left : kv_width + left + HD] = value_sums[number].astype(
                out_ref.dtype
            )


def attend_back(band, gpos, cosines, sines, queries, grads, lse, blocks):
    seqs, rows, q_width = queries.shape
    heads = q_width // HD
    key_total = sum(block.shape[1] for block in blocks)

    def whole(array):
        return pl.BlockSpec((1,) + array.shape[1:], lambda s, *_: (s, 0, 0))

    table = pl.BlockSpec((1, rows, BLK), lambda s, *_: (0, 0, 0))
    out_shape = [jax.ShapeDtypeStruct(queries.shape, jnp.bfloat16)]
    for number, block in enumerate(blocks):
        own = number == len(blocks) - 2
        out_shape.append(jax.ShapeDtypeStruct(block.shape, jnp.float32 if own else jnp.bfloat16))
    return pl.pallas_call(
        functools.partial(attend_back_kernel, len(blocks)),
        out_shape=out_shape,
        grid_spec=pltpu.PrefetchScalarGridSpec(
            num_scalar_prefetch=1,
            grid=(seqs,),
            in_specs=[whole(gpos), table, table]
            + [whole(array) for array in (queries, grads, lse, *blocks)],
            out_specs=[whole(array) for array in out_shape],
            scratch_shapes=[pltpu.VMEM((key_total, rows), jnp.float32)],
        ),
        compiler_params=pltpu.CompilerParams(vmem_limit_bytes=48 * 2**20),
        cost_estimate=pl.CostEstimate(
            flops=40 * seqs * heads * rows * key_total * HD,
            bytes_accessed=8 * queries.size,
            transcendentals=seqs * heads * rows * key_total,
        ),
    )(band, gpos, cosines, sines, queries, grads, lse, *blocks)


def join_kernel(q_width, kv_width, dq_ref, own_ref, pick_ref, glob_ref, cos_ref, sin_ref, *refs):
    back_refs, out_ref = refs[:-1], refs[-1]
    out_ref[0, :, :q_width] = dq_ref[0]
    picked = lax.dot_general(
        pick_ref[0].astype(jnp.float32),
        glob_ref[0],
        (((0,), (0,)), ((), ())),
        precision=lax.Precision.HIGHEST,
        preferred_element_type=jnp.float32,
    )
    for start in range(0, 2 * kv_width, BLK):
        lanes = slice(start, start + BLK)
        total = own_ref[0, :, lanes] + picked[:, lanes]
        for back_ref in back_refs:
            total = total + back_ref[0, :, lanes].astype(jnp.float32)
        first, other = half_turn(total * sin_ref[0])
        turned = total * cos_ref[0] + jnp.where(first, other, -other)
        column = lax.broadcasted_iota(jnp.int32, total.shape, 1) + start
        turned = jnp.where(column >= kv_width, total, turned)
        out_ref[0, :, q_width + start : q_width + start + BLK] = turned.astype(jnp.bfloat16)


def join_grads(dq, own, picks, globs, cosines, sines, backs):
    seqs, rows, q_width = dq.shape
    kv_width = own.shape[2] // 2

    def whole(array):
        return pl.BlockSpec((1,) + array.shape[1:], lambda s: (s, 0, 0))

    table = pl.BlockSpec((1, rows, BLK), lambda s: (0, 0, 0))
    out_shape = jax.ShapeDtypeStruct((seqs, rows, q_width + 2 * kv_width), jnp.bfloat16)
    return pl.pallas_call(
        functools.partial(join_kernel, q_width, kv_width),
        out_shape=out_shape,
        grid=(seqs,),
        in_specs=[whole(dq), whole(own), whole(picks), whole(globs), table, table]
        + [whole(back) for back in backs],
        out_specs=whole(out_shape),
        cost_estimate=pl.CostEstimate(
            flops=20 * own.size, bytes_accessed=4 * dq.size + 12 * own.size, transcendentals=0
        ),
    )(dq, own, picks, globs, cosines, sines, *backs)


def adam_kernel(batch, meta, rates, *refs):
    master_ref, first_ref, second_ref, left_ref, right_ref = refs[:5]
    sources = refs[5:-6]
    new_first_ref, new_second_ref, new_master_ref, copy_ref, tiles, arrived = refs[-6:]
    step, steps = pl.program_id(0), pl.num_programs(0)
    slot = step % 2

    def fetch(at_step, at_slot):
        for place in range(batch):
            tile = at_step * batch + place
            for number, source in enumerate(sources):

                @pl.when(meta[0, tile] == number)
                def _(source=source, tile=tile, place=place):
                    top = pl.multiple_of(meta[2, tile], BLK)
                    left = pl.multiple_of(meta[3, tile], BLK)
                    pltpu.make_async_copy(
                        source.at[meta[1, tile], pl.ds(top, BLK), pl.ds(left, BLK)],
                        tiles.at[at_slot, place],
                        arrived.at[at_slot],
                    ).start()

    @pl.when(step == 0)
    def _():
        fetch(0, 0)

    @pl.when(step + 1 < steps)
    def _():
        fetch(step + 1, 1 - slot)

    pltpu.make_async_copy(tiles.at[slot], tiles.at[slot], arrived.at[slot]).wait()
    places = range(batch)
    lefts = [left_ref[place].astype(jnp.bfloat16) for place in places]
    rights = [right_ref[place].astype(jnp.bfloat16) for place in places]
    turned = [over_first(lefts[place], tiles[slot, place]).astype(jnp.bfloat16) for place in places]
    rotated = [
        jnp.dot(turned[place], rights[place], preferred_element_type=jnp.float32) for place in places
    ]
    directions = []
    for place in places:
        new_first = beta_one * first_ref[place] + (1.0 - beta_one) * rotated[place]
        new_second = beta_two * second_ref[place] + (1.0 - beta_two) * rotated[place] * rotated[place]
        direction = (new_first * (1.0 / (1.0 - beta_one**STEP))) / (
            jnp.sqrt(new_second * (1.0 / (1.0 - beta_two**STEP))) + adam_eps
        )
        new_first_ref[place] = new_first
        new_second_ref[place] = new_second
        directions.append(direction.astype(jnp.bfloat16))
    updates = [
        jnp.dot(lefts[place], directions[place], preferred_element_type=jnp.float32) for place in places
    ]
    updates = [over_last(updates[place].astype(jnp.bfloat16), rights[place]) for place in places]
    for place in places:
        old = master_ref[place]
        new_master = old - rates[step * batch + place] * (updates[place] + weight_decay * old)
        new_master_ref[place] = new_master
        copy_ref[place] = new_master.astype(jnp.bfloat16)


def adam(meta, rates, state, sources):
    count = state[0].shape[0]
    batch = max(size for size in range(1, 33) if count % size == 0)
    block = pl.BlockSpec((batch, BLK, BLK), lambda s, *_: (s, 0, 0))
    anywhere = pl.BlockSpec(memory_space=pl.ANY)
    shape = (count, BLK, BLK)
    return pl.pallas_call(
        functools.partial(adam_kernel, batch),
        out_shape=[jax.ShapeDtypeStruct(shape, jnp.float32)] * 3
        + [jax.ShapeDtypeStruct(shape, jnp.bfloat16)],
        grid_spec=pltpu.PrefetchScalarGridSpec(
            num_scalar_prefetch=2,
            grid=(count // batch,),
            in_specs=[block] * 5 + [anywhere] * len(sources),
            out_specs=[block] * 4,
            scratch_shapes=[
                pltpu.VMEM((2, batch, BLK, BLK), jnp.bfloat16),
                pltpu.SemaphoreType.DMA((2,)),
            ],
        ),
        compiler_params=pltpu.CompilerParams(vmem_limit_bytes=56 * 2**20),
        cost_estimate=pl.CostEstimate(
            flops=8 * count * BLK**3, bytes_accessed=36 * count * BLK**2, transcendentals=0
        ),
    )(meta, rates, *state, *sources)


def per_device(
    block_input,
    cotangent,
    glob_select,
    assignment,
    master,
    first_moment,
    second_moment,
    left_basis,
    right_basis,
    gains,
    gain_first,
    gain_second,
):
    band_total = lax.axis_size("fsdp")
    rep_total = lax.axis_size("rep")
    place = lax.axis_index("rep")
    band = lax.axis_index("fsdp")
    heads = H // rep_total
    kv_heads = KVH // rep_total
    q_width = heads * HD
    kv_width = kv_heads * HD
    tok_count = block_input.shape[1]
    own_count = master.shape[1]
    tile_total = own_count * rep_total
    aligned = square() and whole_tiles(band_total, rep_total)
    tile_order = assignment[0]

    residual = block_input[0].astype(jnp.float32)
    grad_top = cotangent[0]
    position = band * tok_count + jnp.arange(tok_count, dtype=jnp.int32)
    cosine_table, sine_table = rope_tables(position)
    wide_cosine = jnp.concatenate([cosine_table, cosine_table], 1)[None]
    wide_sine = jnp.concatenate([sine_table, sine_table], 1)[None]
    scale_one = lax.rsqrt(jnp.mean(residual * residual, -1, keepdims=True) + norm_eps)
    normed_one = (residual * scale_one * gains[0]).astype(jnp.bfloat16)
    pick_rows = glob_select[0]
    glob_total = pick_rows.shape[0]
    selector = pick_rows.astype(jnp.bfloat16)
    glob_pos_part = jnp.sum(pick_rows * position[None, :], 1)
    digits = jnp.concatenate([glob_pos_part // 256, glob_pos_part % 256]).astype(jnp.bfloat16)
    digits = jnp.pad(digits[None], ((0, 7), (0, D - 2 * glob_total)))
    glob_rows = jnp.dot(selector, normed_one, preferred_element_type=jnp.float32).astype(jnp.bfloat16)
    glob_rows = add_all(jnp.concatenate([glob_rows, digits], 0), "fsdp").astype(jnp.bfloat16)
    packed = [normed_one, glob_rows, selector.reshape(-1, D)]
    packed = jnp.concatenate(packed, 0)
    packed = jnp.pad(packed, ((0, -packed.shape[0] % 32), (0, 0)))

    def over_bands(slice_rows):
        return lax.all_gather(slice_rows, "fsdp", axis=0, tiled=True)

    if aligned:
        half = BLK // 2
        low, high = (master[0, :, rows].astype(jnp.bfloat16) for rows in (slice(0, half), slice(half, BLK)))
        layout = slice_layout(band_total, rep_total)
        attn_layout = jnp.asarray(np.concatenate(layout[:4], 2))
        wanted = jnp.take(tile_order, by_place(attn_layout).reshape(-1), mode="clip")
        meta = jnp.stack([wanted // own_count == place, wanted % own_count], 0).astype(jnp.int32)
        attn_part = place_tiles(low, high, meta, *attn_layout.shape)
        attn_part = rep_scatter(attn_part).astype(jnp.bfloat16)
        low, attn_part = lax.optimization_barrier((low, attn_part))
        slots = square_pieces(low)
        attn = over_bands(attn_part)
        grids = [lax.dynamic_index_in_dim(jnp.asarray(grid), place, 0, False) for grid in layout]

        def find(wanted):
            wanted = jnp.take(tile_order, jnp.concatenate([grid.reshape(-1) for grid in wanted]), mode="clip")
            entry, row = (wanted // own_count) ^ place, wanted % own_count
            cut = own_count // 2
            high = (entry == 3) & (row >= cut)
            found = jnp.stack([jnp.where(high, 4, entry), jnp.where(high, row - cut, row)], 0)
            return found.astype(jnp.int32)

        all_grid = jnp.concatenate(grids[4:], 1)
        (first_part,) = gather_strips(slots, find([all_grid]), [all_grid.shape])
        packed, first_part, attn = lax.optimization_barrier((packed, first_part, attn))
        early = over_bands(first_part)
    packed_all = rep_gather(packed)
    if aligned:
        packed_all, high = lax.optimization_barrier((packed_all, high))
        later_slots = square_pieces(high)
    normed_one_all = packed_all[:, :tok_count].reshape(-1, D)
    at = tok_count + glob_total
    glob_digits = packed_all[:, at, : 2 * glob_total].astype(jnp.float32)
    glob_place = glob_digits[:, :glob_total] * 256.0 + glob_digits[:, glob_total:]
    at += 8
    selector_all = packed_all[:, at : at + selector.size // D].reshape(rep_total, glob_total, tok_count)

    if aligned:
        in_width = q_width + 2 * kv_width
        w_inner, w_output = attn[:, :in_width], attn[:, in_width:]
    else:
        slots = lax.all_gather(master[0].astype(jnp.bfloat16), "rep", axis=0, tiled=True)
        tiles = jnp.take(slots, tile_order, axis=0, mode="clip")
        slices = cut_slices(band_matrices(tiles, band_total), band_total, rep_total)
        w_inner = over_bands(jnp.concatenate(slices[0:3], 1))
        w_output = over_bands(slices[3])
        w_gate = over_bands(slices[4])
        w_up = over_bands(slices[5])
        w_down = over_bands(slices[6])

    w_output = by_place(w_output.reshape(rep_total, q_width, -1)).reshape(D, -1)

    def mul(rows, weight):
        return jnp.dot(rows, weight, preferred_element_type=jnp.float32)

    def mul_back(rows, weight):
        return lax.dot_general(rows, weight, (((1,), (1,)), ((), ())), preferred_element_type=jnp.float32)

    def weight_grad(rows, grad_rows):
        return lax.dot_general(
            rows, grad_rows, (((0,), (0,)), ((), ())), preferred_element_type=jnp.float32
        ).astype(jnp.bfloat16)

    def own_sum(partial):
        return rep_scatter(partial.astype(jnp.bfloat16).reshape(rep_total, tok_count, D))

    inner_rows = mul(packed_all.reshape(-1, D), w_inner).reshape(rep_total, -1, w_inner.shape[1])
    packed_all, normed_one_all = lax.optimization_barrier((packed_all, normed_one_all))
    queries, own_pairs = rope_rows(inner_rows, tok_count, 0, q_width, kv_width, wide_cosine, wide_sine)
    glob_cosine, glob_sine = rope_tables(glob_place.reshape(-1))
    glob_cosine = jnp.concatenate([glob_cosine, glob_cosine], 1).reshape(rep_total, glob_total, -1)
    glob_sine = jnp.concatenate([glob_sine, glob_sine], 1).reshape(rep_total, glob_total, -1)
    (glob_pairs,) = rope_rows(
        inner_rows, glob_total, tok_count // glob_total, q_width, kv_width, glob_cosine, glob_sine, False
    )
    back_count = (WINDOW + tok_count - 2) // tok_count
    odd = band % 2 == 1
    by_chip = back_count == 2 and band_total % 2 == 0
    if by_chip:
        two_back = shifted(own_pairs, "fsdp", 2)
        pair_blocks = [two_back, to_core(jnp.where(odd, two_back, own_pairs))]
    else:
        pair_blocks = [shifted(own_pairs, "fsdp", distance) for distance in range(back_count, 0, -1)]
    pair_blocks = pair_blocks + [own_pairs, glob_pairs]
    glob_spots = jnp.broadcast_to(glob_place[:, :, None], (rep_total, glob_total, BLK))
    band_number = band.astype(jnp.int32).reshape(1)
    attended_low, lse = attend(band_number, glob_spots, queries, pair_blocks)
    if aligned:
        *later_slots, attended_low, early = lax.optimization_barrier((*later_slots, attended_low, early))
        last_grid = jnp.concatenate(grids[4:6], 1)
        last_part, down_part = gather_strips(
            later_slots, find([last_grid, grids[6]]), [last_grid.shape, grids[6].shape]
        )

        def by_strips(gathered):
            return gathered.reshape(band_total, -1, all_grid.shape[0], half, gathered.shape[-1])

        early, late, late_down = by_strips(early), by_strips(over_bands(last_part)), by_strips(over_bands(down_part))
    attended_all = rep_features(attended_low).reshape(-1, D)
    columns = mul(attended_all, w_output).astype(jnp.bfloat16).reshape(rep_total, tok_count, -1)
    branch = by_place(rep_exchange(columns)).transpose(1, 0, 2).reshape(tok_count, D)
    middle = residual + branch.astype(jnp.float32)
    scale_two = lax.rsqrt(jnp.mean(middle * middle, -1, keepdims=True) + norm_eps)
    normed_two = (middle * scale_two * gains[1]).astype(jnp.bfloat16)
    normed_two_all = rep_gather(normed_two).reshape(-1, D)
    normed_two_all, grad_top_now = lax.optimization_barrier((normed_two_all, grad_top))
    top_first = gather_first(grad_top_now)

    if aligned:
        gate_rows, up_rows, activation = forward_products(normed_two_all, early, late, FF // rep_total)
        top_first, activation = after(top_first, activation)
        grad_top_all = gather_join(gather_second(top_first)).reshape(-1, D)
        g_down = weight_grad(activation, grad_top_all)
        grad_top_all, g_down = lax.optimization_barrier((grad_top_all, g_down))
        grad_gate, grad_up, pieces, branch_pieces = backward_products(
            grad_top_all, gate_rows, up_rows, activation, early, late, late_down
        )
        normed_first = sum_first(pieces)
        normed_first, g_gate = after(normed_first, weight_grad(normed_two_all, grad_gate))
        grad_normed_two = sum_second(normed_first)
    else:
        gate_rows = mul(normed_two_all, w_gate)
        up_rows = mul(normed_two_all, w_up)
        sigmoid_gate = jax.nn.sigmoid(gate_rows)
        silu_gate = gate_rows * sigmoid_gate
        activation = (silu_gate * up_rows).astype(jnp.bfloat16)
        grad_top_all = gather_join(gather_second(top_first)).reshape(-1, D)
        g_down = weight_grad(activation, grad_top_all)
        grad_act = mul_back(grad_top_all, w_down)
        grad_gate = (
            grad_act * up_rows * sigmoid_gate * (1.0 + gate_rows * (1.0 - sigmoid_gate))
        ).astype(jnp.bfloat16)
        grad_up = (grad_act * silu_gate).astype(jnp.bfloat16)
        grad_normed_two = own_sum(mul_back(grad_gate, w_gate) + mul_back(grad_up, w_up))
        branch_pieces = (mul(activation, w_down),)
        g_gate = weight_grad(normed_two_all, grad_gate)
    grad_normed_two, g_gate = lax.optimization_barrier((grad_normed_two, g_gate))

    def over_tokens(partial):
        return lax.psum_scatter(partial, "fsdp", scatter_dimension=0, tiled=True)

    s_down = over_tokens(g_down)
    s_gate = over_tokens(g_gate)

    grad_middle = grad_top.astype(jnp.float32) + norm_back(middle, scale_two, gains[1], grad_normed_two)
    grad_parts = grad_middle.astype(jnp.bfloat16).reshape(tok_count, rep_total, -1).transpose(1, 0, 2)
    grad_columns = rep_exchange(by_place(grad_parts)).reshape(rep_total * tok_count, -1)
    grad_columns, grad_up = lax.optimization_barrier((grad_columns, grad_up))
    grad_attended, g_up = rep_features_sum(
        grad_columns.reshape(rep_total, tok_count, -1),
        w_output,
        lambda: weight_grad(normed_two_all, grad_up),
    )
    grad_attended = grad_attended.astype(jnp.bfloat16)
    (s_down, g_up), grad_attended = after((s_down, g_up), grad_attended)
    down_first = gather_first(s_down)
    grad_queries, *grad_blocks = attend_back(
        band_number, glob_spots, wide_cosine, wide_sine, queries, grad_attended, lse, pair_blocks
    )
    down_first, *grad_blocks = after(down_first, *grad_blocks)
    down_second = gather_second(down_first)
    branch_pieces, *grad_blocks = after(tuple(branch_pieces), *grad_blocks)
    branch_first = sum_first(branch_pieces) if aligned else (own_sum(branch_pieces[0]),)
    if by_chip:
        came = to_core(grad_blocks[1])
        total = grad_blocks[0].astype(jnp.float32) + came.astype(jnp.float32)
        sent = jnp.where(odd, total.astype(jnp.bfloat16), grad_blocks[0])
        returned = [shifted(sent, "fsdp", -2), jnp.where(odd, jnp.zeros_like(came), came)]
    else:
        returned = [
            shifted(grad_blocks[back_count - distance], "fsdp", -distance)
            for distance in range(1, back_count + 1)
        ]
    glob_grads = add_all(grad_blocks[-1], "fsdp")
    g_up, glob_grads, *returned = lax.optimization_barrier((g_up, glob_grads, *returned))
    s_up = over_tokens(g_up)
    grad_inner = join_grads(
        grad_queries, grad_blocks[-2], selector_all, glob_grads, wide_cosine, wide_sine, returned
    ).reshape(-1, q_width + 2 * kv_width)
    grad_normed_parts = mul_back(grad_inner, w_inner).astype(jnp.bfloat16).reshape(rep_total, tok_count, D)
    if square():
        normed_first = sum_first(split_pieces(grad_normed_parts))
    else:
        normed_first = (rep_scatter(grad_normed_parts),)
    grad_inner, grad_normed_parts = lax.optimization_barrier((grad_inner, grad_normed_parts))
    g_inner = weight_grad(normed_one_all, grad_inner)
    attended_all, g_inner = lax.optimization_barrier((attended_all, g_inner))
    g_output = weight_grad(attended_all, grad_columns)
    g_output = by_place(g_output.reshape(rep_total, q_width, -1)).reshape(D, -1)
    g_attn = with_layout_constraint(jnp.concatenate([g_inner, g_output], 1), Layout((0, 1)))
    branch_first, *normed_first = after(branch_first, *normed_first)
    (s_gate,), *normed_first = after((s_gate,), *normed_first)
    s_down = gather_join(down_second)
    grad_normed_one = sum_second(normed_first) if square() else normed_first[0]
    block_out = middle + (sum_second(branch_first) if aligned else branch_first[0])
    gate_first = gather_first(s_gate)
    (s_up,), g_attn, grad_normed_one = after((s_up,), g_attn, grad_normed_one)
    s_attn = over_tokens(g_attn)
    s_gate = gather_join(gather_second(gate_first))
    up_first = gather_first(s_up)
    grad_input = grad_middle + norm_back(residual, scale_one, gains[0], grad_normed_one)

    gain_terms = jnp.stack(
        [
            jnp.sum(grad_normed_one * residual * scale_one, 0),
            jnp.sum(grad_normed_two * middle * scale_two, 0),
        ]
    )
    square_terms = jnp.stack(
        [jnp.sum(residual * residual), jnp.sum(middle * middle), jnp.sum(block_out * block_out)]
    )
    sums = jnp.concatenate([gain_terms.reshape(-1), square_terms])

    up_first, sums = after(up_first, sums)
    s_up = gather_join(gather_second(up_first))
    sums = add_all(add_all(sums, "rep"), "fsdp")
    sums, s_attn, s_up, s_gate, s_down = lax.optimization_barrier((sums, s_attn, s_up, s_gate, s_down))
    gain_grad, square_total = sums[: 2 * D].reshape(2, D), sums[2 * D :]

    slot_ids = jnp.arange(tile_total, dtype=jnp.int32)
    inverse = jnp.sum(jnp.where(tile_order[None, :] == slot_ids[:, None], slot_ids[None, :], 0), 1)
    own_slots = place * own_count + jnp.arange(own_count, dtype=jnp.int32)
    owned_tiles = jnp.take(inverse, own_slots, mode="clip")
    if aligned:
        sources = [rep_gather(s_attn), s_gate, s_up, s_down]
        where = np.zeros((4, rep_total, tile_total), np.int32)
        first_col = 0
        for kind, grid in enumerate(layout):
            rows, cols = grid.shape[1:]
            first_col = 0 if kind >= 4 else first_col
            for there in range(rep_total):
                numbers = grid[there].reshape(-1)
                at = np.arange(rows * cols)
                where[0, :, numbers] = max(kind - 3, 0)
                where[2, :, numbers] = (at // cols * BLK)[:, None]
                where[3, :, numbers] = (at % cols * BLK + first_col)[:, None]
                for here in range(rep_total):
                    where[1, here, numbers] = here ^ there
            first_col += cols * BLK
        tile_spots = lax.dynamic_index_in_dim(jnp.asarray(where), place, 1, False)
        meta = jnp.take(tile_spots, owned_tiles, axis=1, mode="clip")
    else:
        splits = [0, q_width, q_width + kv_width, q_width + 2 * kv_width, s_attn.shape[1]]
        stacks = [rep_gather(s_attn[:, low:high]) for low, high in zip(splits, splits[1:])]
        stacks += [s_gate, s_up, s_down]
        sources = [band_tiles(join_slices(stacks, band_total, rep_total))]
        meta = jnp.stack([0 * owned_tiles, owned_tiles, 0 * owned_tiles, 0 * owned_tiles], 0)
    slot_rates = jnp.take(kind_rates(band_total), owned_tiles, mode="clip")
    new_first, new_second, new_master, master_copy = adam(
        meta,
        slot_rates,
        (master[0], first_moment[0], second_moment[0], left_basis[0], right_basis[0]),
        sources,
    )
    new_gain_first = beta_one * gain_first + (1.0 - beta_one) * gain_grad
    new_gain_second = beta_two * gain_second + (1.0 - beta_two) * gain_grad * gain_grad
    gain_step = (
        new_gain_first
        / (1.0 - beta_one**STEP)
        / (jnp.sqrt(new_gain_second / (1.0 - beta_two**STEP)) + adam_eps)
    )
    new_gains = gains - gain_rate * gain_step
    rms_stats = jnp.sqrt(square_total / (rep_total * band_total * tok_count * D))
    return (
        block_out[None],
        grad_input[None],
        new_first[None],
        new_second[None],
        new_master[None],
        master_copy[None],
        new_gain_first,
        new_gain_second,
        new_gains,
        rms_stats,
    )


def solution(mesh):
    in_specs = (
        P("rep", "fsdp", None),
        P("rep", "fsdp", None),
        P("rep", None, "fsdp"),
        P("fsdp", None),
        P("fsdp", "rep", None, None),
        P("fsdp", "rep", None, None),
        P("fsdp", "rep", None, None),
        P("fsdp", "rep", None, None),
        P("fsdp", "rep", None, None),
        P(),
        P(),
        P(),
    )
    out_specs = (
        P("rep", "fsdp", None),
        P("rep", "fsdp", None),
        P("fsdp", "rep", None, None),
        P("fsdp", "rep", None, None),
        P("fsdp", "rep", None, None),
        P("fsdp", "rep", None, None),
        P(),
        P(),
        P(),
        P(),
    )
    return jax.shard_map(
        per_device, mesh=mesh, in_specs=in_specs, out_specs=out_specs, check_vma=False
    )
```

```python
import functools

import jax
import jax.numpy as jnp
import numpy as np
from jax import lax
from jax.experimental import pallas as pl
from jax.experimental.layout import Layout, with_layout_constraint
from jax.experimental.pallas import tpu as pltpu
from jax.sharding import PartitionSpec as P

D = 2048
H = 32
KVH = 8
HD = 64
FF = 8192
WINDOW = 512
BLK = 128
STEP = 10


norm_eps = 1e-05
rope_theta = 500000.0
beta_one = 0.5
beta_two = 0.5
adam_eps = 1e-08
weight_decay = 0.1
gain_rate = 0.5
masked_value = -1e30


def matrix_shapes():
    kv_width = KVH * HD
    return [(D, D), (D, kv_width), (D, kv_width), (D, D), (D, FF), (D, FF), (FF, D)]


def kind_rates(band_total):
    rate_list = [
        D ** (-0.5),
        D ** (-0.5),
        D ** (-0.5),
        (D * 8 // WINDOW) ** (-0.5),
        D ** (-0.5),
        D ** (-0.5),
        FF ** (-0.5),
    ]
    pieces = []
    for (row_total, col_total), rate_value in zip(matrix_shapes(), rate_list):
        tile_count = row_total // band_total // BLK * (col_total // BLK)
        pieces.append(jnp.full((tile_count,), rate_value, jnp.float32))
    return jnp.concatenate(pieces)


def band_matrices(tiles, band_total):
    matrices = []
    offset = 0
    for row_total, col_total in matrix_shapes():
        band_rows = row_total // band_total
        tile_count = band_rows // BLK * (col_total // BLK)
        segment = tiles[offset : offset + tile_count].reshape(
            band_rows // BLK, col_total // BLK, BLK, BLK
        )
        matrices.append(segment.transpose(0, 2, 1, 3).reshape(band_rows, col_total))
        offset += tile_count
    return matrices


def band_tiles(matrices):
    pieces = []
    for matrix in matrices:
        row_count, col_count = matrix.shape
        segment = matrix.reshape(row_count // BLK, BLK, col_count // BLK, BLK).transpose(0, 2, 1, 3)
        pieces.append(segment.reshape(-1, BLK, BLK))
    return jnp.concatenate(pieces, 0)


def rope_tables(position):
    halves = jnp.arange(HD // 2, dtype=jnp.float32) * (2.0 / HD)
    frequency = rope_theta ** (-halves)
    angles = position.astype(jnp.float32)[:, None] * frequency[None, :]
    angles = jnp.concatenate([angles, angles], 1)
    return (jnp.cos(angles), jnp.sin(angles))


def rotate(vectors, cosine_table, sine_table):
    half_width = vectors.shape[-1] // 2
    turned = jnp.concatenate([-vectors[..., half_width:], vectors[..., :half_width]], -1)
    return vectors * cosine_table[:, None, :] + turned * sine_table[:, None, :]


def rotate_back(grad_rows, cosine_table, sine_table):
    half_width = grad_rows.shape[-1] // 2
    scaled = grad_rows * sine_table[:, None, :]
    turned = jnp.concatenate([scaled[..., half_width:], -scaled[..., :half_width]], -1)
    return grad_rows * cosine_table[:, None, :] + turned


def norm_back(values, row_scale, gain_row, grad_rows):
    weighted = grad_rows * gain_row
    return row_scale * weighted - values * row_scale**3 * jnp.mean(
        weighted * values, -1, keepdims=True
    )


def to_rep(block, distance):
    route = [(i, i ^ distance) for i in range(lax.axis_size("rep"))]
    return lax.ppermute(block, "rep", route)


def square():
    return lax.axis_size("rep") == 4


def gather_first(block):
    if not square():
        return (lax.all_gather(block, "rep", axis=0),)
    return block, to_rep(block, 1), to_rep(block, 2)


def gather_second(first):
    if not square():
        return first
    block, near, far = first
    cut = block.shape[0] // 2
    return block, near, far, to_rep(near[:cut], 2), to_rep(far[cut:], 1)


def gather_join(pieces):
    if not square():
        return pieces[0]
    return jnp.concatenate(pieces, 0).reshape((4,) + pieces[0].shape)


def square_pieces(block):
    return gather_second(gather_first(block))


def rep_gather(block):
    return gather_join(gather_second(gather_first(block)))


def after(values, *others):
    count = len(values)
    tied = lax.optimization_barrier((*values, *others))
    return tuple(tied[:count]), *tied[count:]


def rep_of(entry):
    place = lax.axis_index("rep")
    return place ^ entry if square() else entry


def rep_scatter(parts):
    if not square():
        flat = parts.reshape(-1, parts.shape[-1])
        return lax.psum_scatter(flat, "rep", scatter_dimension=0, tiled=True).astype(jnp.float32)
    return sum_pieces(*split_pieces(parts))


def split_pieces(parts):
    half = parts.shape[-1] // 2
    low, high = parts[..., :half], parts[..., half:]
    return jnp.stack([low[0], low[2]], 0), jnp.stack([low[1], low[3]], 0), high[:2], high[2:]


def sum_first(pieces):
    low_kept, low_sent, high_kept, high_sent = pieces
    parts = []
    for kept, sent, first in ((low_kept, low_sent, 1), (high_kept, high_sent, 2)):
        came = to_rep(sent, first)
        parts.append(kept[0].astype(jnp.float32) + came[0].astype(jnp.float32))
        parts.append((kept[1].astype(jnp.float32) + came[1].astype(jnp.float32)).astype(kept.dtype))
    return tuple(parts)


def sum_second(parts):
    low, low_other, high, high_other = parts
    low = low + to_rep(low_other, 2).astype(jnp.float32)
    high = high + to_rep(high_other, 1).astype(jnp.float32)
    return jnp.concatenate([low, high], -1)


def sum_pieces(*pieces):
    return sum_second(sum_first(pieces))


def add_all(value, axis):
    size = lax.axis_size(axis)
    total = value.astype(jnp.float32)
    distance = 1
    while distance < size:
        count = 2 if (size // distance).bit_length() % 2 == 0 else 4
        low = total.astype(value.dtype)
        others = []
        for step in range(1, count):
            route = [(i, i ^ (step * distance)) for i in range(size)]
            others.append(lax.ppermute(low, axis, route).astype(jnp.float32))
        total = total + others[0]
        if count == 4:
            total = total + (others[1] + others[2])
        distance *= count
    return total


def rep_features(block):
    if not square():
        return lax.all_gather(block, "rep", axis=2, tiled=True)
    own, near, far, low, high = square_pieces(block)
    return jnp.concatenate(
        [
            own,
            jnp.stack([near[1], near[0], near[3], near[2]], 0),
            jnp.stack([far[2], far[3], far[0], far[1]], 0),
            jnp.stack([high[1], high[0], low[1], low[0]], 0),
        ],
        2,
    )


def write_pieces(entry, rows, values, refs):
    low_kept, low_sent, high_kept, high_sent = refs
    half = low_kept.shape[-1]
    values = values.astype(jnp.bfloat16)
    (low_sent if entry % 2 else low_kept)[entry // 2, rows] = values[:, :half]
    (high_sent if entry // 2 else high_kept)[entry % 2, rows] = values[:, half:]


def swapped_kernel(x_ref, w_ref, *refs):
    reps, rows, _ = x_ref.shape
    width = w_ref.shape[0] // reps
    for entry in range(reps):
        weight = w_ref[entry * width : (entry + 1) * width]
        for there in range(reps):
            product = over_last(x_ref[there ^ entry], weight)
            write_pieces(entry, slice(there * rows, (there + 1) * rows), product, refs)


def rep_features_sum(columns, weight, meanwhile):
    reps, rows, depth = columns.shape
    width = weight.shape[0] // reps
    if square():
        pieces = pl.pallas_call(
            swapped_kernel,
            out_shape=[jax.ShapeDtypeStruct((2, reps * rows, width // 2), jnp.bfloat16)] * 4,
            compiler_params=pltpu.CompilerParams(vmem_limit_bytes=32 * 2**20),
            cost_estimate=pl.CostEstimate(
                flops=2 * reps * columns.size * width,
                bytes_accessed=10 * columns.size,
                transcendentals=0,
            ),
        )(columns, weight)
        first = sum_first(pieces)
        first, other = after(first, meanwhile())
        total = sum_second(first)
    else:
        other = meanwhile()
        product = over_last(columns.reshape(-1, depth), weight).astype(jnp.bfloat16)
        swapped = product.reshape(reps, rows, reps, width).transpose(2, 0, 1, 3)
        total = rep_scatter(swapped.reshape(reps, reps * rows, width))
    return total.reshape(reps, rows, width), other


def rep_exchange(parts):
    if not square():
        return lax.all_to_all(parts, "rep", 0, 0)
    return jnp.stack([parts[0]] + [to_rep(parts[entry], entry) for entry in (1, 2, 3)], 0)


def by_place(parts):
    entries = [rep_of(entry) for entry in range(parts.shape[0])]
    return jnp.stack([lax.dynamic_index_in_dim(parts, entry, 0, False) for entry in entries], 0)


def to_core(block):
    return lax.ppermute(block, "fsdp", [(i, i ^ 1) for i in range(lax.axis_size("fsdp"))])


def shifted(block, axis, distance):
    devices = range(lax.axis_size(axis))
    route = [(i - distance, i) for i in devices if i - distance in devices]
    return lax.ppermute(block, axis, route)


def tile_offsets(band_total):
    offsets = [0]
    for row_total, col_total in matrix_shapes():
        offsets.append(offsets[-1] + row_total // band_total // BLK * (col_total // BLK))
    return offsets


def whole_tiles(band_total, rep_total):
    return KVH * HD // rep_total % BLK == 0 and FF // band_total // rep_total % BLK == 0


def slice_layout(band_total, rep_total):
    offsets = tile_offsets(band_total)
    layout = []
    for kind, (row_total, col_total) in enumerate(matrix_shapes()):
        rows, cols = row_total // band_total // BLK, col_total // BLK
        grid = offsets[kind] + np.arange(rows * cols).reshape(rows, cols)
        if kind == 6:
            layout.append(grid.reshape(rep_total, rows // rep_total, cols))
        elif kind in (4, 5):
            cut = grid.reshape(rows, band_total, rep_total, -1).transpose(2, 0, 1, 3)
            layout.append(cut.reshape(rep_total, rows, -1))
        else:
            layout.append(grid.reshape(rows, rep_total, -1).transpose(1, 0, 2))
    return layout


def tiles_to_matrix(tiles):
    rows, cols = tiles.shape[:2]
    return tiles.transpose(0, 2, 1, 3).reshape(rows * BLK, cols * BLK)


def matrix_to_tiles(matrix):
    rows, cols = matrix.shape
    cut = matrix.reshape(rows // BLK, BLK, cols // BLK, BLK)
    return cut.transpose(0, 2, 1, 3).reshape(-1, BLK, BLK)


def cut_slices(matrices, band_total, rep_total):
    place = lax.axis_index("rep")
    slices = []
    for kind, matrix in enumerate(matrices):
        rows, cols = matrix.shape
        if kind == 6:
            slices.append(lax.dynamic_slice_in_dim(matrix, place * (rows // rep_total), rows // rep_total, 0))
        elif kind in (4, 5):
            cut = matrix.reshape(rows, band_total, rep_total, -1)
            slices.append(lax.dynamic_index_in_dim(cut, place, 2, False).reshape(rows, -1))
        else:
            slices.append(lax.dynamic_slice_in_dim(matrix, place * (cols // rep_total), cols // rep_total, 1))
    return slices


def join_slices(stacks, band_total, rep_total):
    matrices = []
    for kind, stack in enumerate(stacks):
        rows, cols = stack.shape[1:]
        if kind == 6:
            matrices.append(stack.reshape(-1, cols))
        elif kind in (4, 5):
            cut = stack.reshape(rep_total, rows, band_total, -1).transpose(1, 2, 0, 3)
            matrices.append(cut.reshape(rows, -1))
        else:
            matrices.append(stack.transpose(1, 0, 2).reshape(rows, -1))
    return matrices


def gather_kernel(grids, meta, *refs):
    source_total = len(refs) - len(grids) - 1
    sources, targets, done = refs[:source_total], refs[source_total:-1], refs[-1]
    height = sources[0].shape[1]
    start = 0
    for place, (target, (rows, cols)) in enumerate(zip(targets, grids)):

        def one(tile, carry, target=target, rows=rows, cols=cols, start=start, place=place):
            kind = meta[0, start + tile]
            row = meta[1, start + tile]
            across = tile % cols
            top = pl.multiple_of((across // 2 * rows + tile // cols) * height, height)
            left = pl.multiple_of(across % 2 * BLK, BLK)
            for number, source in enumerate(sources):

                @pl.when(kind == number)
                def _(source=source):
                    pltpu.make_async_copy(
                        source.at[row], target.at[pl.ds(top, height), pl.ds(left, BLK)], done.at[place]
                    ).start()

            return carry

        lax.fori_loop(0, rows * cols, one, 0)
        start += rows * cols
    for place, target in enumerate(targets):
        pltpu.make_async_copy(target, target, done.at[place]).wait()


def gather_strips(sources, meta, grids):
    anywhere = pl.BlockSpec(memory_space=pl.ANY)
    height = sources[0].shape[1]
    out_shape = [
        jax.ShapeDtypeStruct((cols // 2 * rows * height, 2 * BLK), jnp.bfloat16) for rows, cols in grids
    ]
    return pl.pallas_call(
        functools.partial(gather_kernel, grids),
        out_shape=out_shape,
        grid_spec=pltpu.PrefetchScalarGridSpec(
            num_scalar_prefetch=1,
            grid=(1,),
            in_specs=[anywhere] * len(sources),
            out_specs=[pl.BlockSpec(shape.shape, lambda i, *_: (0, 0)) for shape in out_shape],
            scratch_shapes=[pltpu.SemaphoreType.DMA((len(grids),))],
        ),
        compiler_params=pltpu.CompilerParams(vmem_limit_bytes=32 * 2**20),
        cost_estimate=pl.CostEstimate(
            flops=0, bytes_accessed=sum(4 * shape.size for shape in out_shape), transcendentals=0
        ),
    )(meta, *sources)


def place_kernel(entries, rows, cols, meta, low, high, out_ref, done):
    out_ref[...] = jnp.zeros_like(out_ref)
    height = low.shape[1]

    def copies(tile):
        entry, rest = tile // (rows * cols), tile % (rows * cols)
        top = rest // cols * (2 * height)
        left = pl.multiple_of(rest % cols * BLK, BLK)
        return [
            pltpu.make_async_copy(
                half.at[meta[1, tile]],
                out_ref.at[entry, pl.ds(pl.multiple_of(top + part * height, height), height), pl.ds(left, BLK)],
                done.at[part],
            )
            for part, half in enumerate((low, high))
        ]

    def begin(tile, carry):
        @pl.when(meta[0, tile] == 1)
        def _():
            for copy in copies(tile):
                copy.start()

        return carry

    def finish(tile, carry):
        @pl.when(meta[0, tile] == 1)
        def _():
            for copy in copies(tile):
                copy.wait()

        return carry

    lax.fori_loop(0, entries * rows * cols, begin, 0)
    lax.fori_loop(0, entries * rows * cols, finish, 0)


def place_tiles(low, high, meta, entries, rows, cols):
    shape = (entries, rows * BLK, cols * BLK)
    anywhere = pl.BlockSpec(memory_space=pl.ANY)
    return pl.pallas_call(
        functools.partial(place_kernel, entries, rows, cols),
        out_shape=jax.ShapeDtypeStruct(shape, jnp.bfloat16),
        grid_spec=pltpu.PrefetchScalarGridSpec(
            num_scalar_prefetch=1,
            grid=(1,),
            in_specs=[anywhere, anywhere],
            out_specs=pl.BlockSpec(shape, lambda i, *_: (0, 0, 0)),
            scratch_shapes=[pltpu.SemaphoreType.DMA((2,))],
        ),
        compiler_params=pltpu.CompilerParams(vmem_limit_bytes=32 * 2**20),
        cost_estimate=pl.CostEstimate(
            flops=0, bytes_accessed=4 * entries * rows * cols * BLK * BLK, transcendentals=0
        ),
    )(meta, low, high)


def half_turn(values):
    lane = lax.broadcasted_iota(jnp.int32, values.shape, 1)
    lanes = values.shape[1]
    first = lane % HD < HD // 2
    return first, jnp.where(
        first, pltpu.roll(values, lanes - HD // 2, 1), pltpu.roll(values, HD // 2, 1)
    )


def strip_copies(early, late, target, done):
    return [
        pltpu.make_async_copy(half, target.at[:, :, number], done.at[number])
        for number, half in enumerate((early, late))
    ]


def forward_kernel(x_ref, early, late, gate_ref, up_ref, act_ref, weights, done):
    step, steps = pl.program_id(0), pl.num_programs(0)
    slot = step % 2
    width = weights.shape[-1]

    def copies(number, at_step, at_slot):
        strip = number * steps + at_step
        return strip_copies(
            early.at[:, strip], late.at[:, strip], weights.at[number, at_slot], done.at[number, at_slot]
        )

    def fetch(at_step, at_slot):
        for number in range(2):
            for copy in copies(number, at_step, at_slot):
                copy.start()

    @pl.when(step == 0)
    def _():
        fetch(0, 0)

    @pl.when(step + 1 < steps)
    def _():
        fetch(step + 1, 1 - slot)

    for number in range(2):
        for copy in copies(number, step, slot):
            copy.wait()
    gate_weight, up_weight = (weights[number, slot].reshape(-1, width) for number in range(2))
    chunk = min(2 * BLK, x_ref.shape[0])
    for first in range(0, x_ref.shape[0], chunk):
        rows = slice(first, first + chunk)
        gate = jnp.dot(x_ref[rows], gate_weight, preferred_element_type=jnp.float32)
        up = jnp.dot(x_ref[rows], up_weight, preferred_element_type=jnp.float32)
        gate_ref[rows] = gate.astype(jnp.bfloat16)
        up_ref[rows] = up.astype(jnp.bfloat16)
        act_ref[rows] = (gate * jax.nn.sigmoid(gate) * up).astype(jnp.bfloat16)


def forward_products(rows, early, late, columns):
    tokens, depth = rows.shape
    bands, _, tiles, half, width = early.shape
    block = pl.BlockSpec((tokens, width), lambda n: (0, n))
    anywhere = pl.BlockSpec(memory_space=pl.ANY)
    return pl.pallas_call(
        forward_kernel,
        out_shape=[jax.ShapeDtypeStruct((tokens, columns), jnp.bfloat16)] * 3,
        grid=(columns // width,),
        in_specs=[pl.BlockSpec(rows.shape, lambda n: (0, 0)), anywhere, anywhere],
        out_specs=[block] * 3,
        scratch_shapes=[
            pltpu.VMEM((2, 2, bands, tiles, 2, half, width), jnp.bfloat16),
            pltpu.SemaphoreType.DMA((2, 2, 2)),
        ],
        compiler_params=pltpu.CompilerParams(vmem_limit_bytes=48 * 2**20),
        cost_estimate=pl.CostEstimate(
            flops=tokens * depth * columns // 8, bytes_accessed=2 * rows.size, transcendentals=0
        ),
    )(rows, early, late)


def backward_kernel(top_ref, gate_ref, up_ref, act_ref, early, late, late_down, *refs):
    dgate_ref, dup_ref = refs[:2]
    pieces, branch_pieces = refs[2:6], refs[6:10]
    weights, downs, total, branch, done, down_done = refs[10:]
    step, steps = pl.program_id(0), pl.num_programs(0)
    slot = step % 2
    strips, width = downs.shape[1], downs.shape[-1]

    def down_copies(at_step, at_slot):
        wanted = pl.ds(2 * steps, strips)
        return strip_copies(
            early.at[at_step, wanted], late_down.at[at_step], downs.at[at_slot], down_done.at[at_slot]
        )

    def copies(number, at_step, at_slot):
        strip = number * steps + at_step
        return strip_copies(
            early.at[:, strip], late.at[:, strip], weights.at[number, at_slot], done.at[number, at_slot]
        )

    def fetch(at_step, at_slot):
        for copy in down_copies(at_step, at_slot):
            copy.start()
        for number in range(2):
            for copy in copies(number, at_step, at_slot):
                copy.start()

    @pl.when(step == 0)
    def _():
        fetch(0, 0)
        total[...] = jnp.zeros_like(total)
        branch[...] = jnp.zeros_like(branch)

    @pl.when(step + 1 < steps)
    def _():
        fetch(step + 1, 1 - slot)

    for copy in down_copies(step, slot):
        copy.wait()
    for number in range(2):
        for copy in copies(number, step, slot):
            copy.wait()
    gate_weight, up_weight = (weights[number, slot].reshape(-1, width) for number in range(2))
    chunk = min(4 * BLK, top_ref.shape[0])
    for first in range(0, top_ref.shape[0], chunk):
        rows = slice(first, first + chunk)
        grad_act = 0.0
        for strip in range(strips):
            lanes = slice(strip * width, (strip + 1) * width)
            down = downs[slot, strip].reshape(-1, width)
            grad_act = grad_act + over_last(top_ref[rows, lanes], down)
            branch[rows, lanes] += jnp.dot(act_ref[rows], down, preferred_element_type=jnp.float32)
        gate = gate_ref[rows].astype(jnp.float32)
        up = up_ref[rows].astype(jnp.float32)
        sigmoid_gate = jax.nn.sigmoid(gate)
        grad_gate = grad_act * up * sigmoid_gate * (1.0 + gate * (1.0 - sigmoid_gate))
        grad_gate = grad_gate.astype(jnp.bfloat16)
        grad_up = (grad_act * (gate * sigmoid_gate)).astype(jnp.bfloat16)
        dgate_ref[rows] = grad_gate
        dup_ref[rows] = grad_up
        total[rows] += over_last(grad_gate, gate_weight) + over_last(grad_up, up_weight)

    @pl.when(step == steps - 1)
    def _():
        rows = total.shape[0] // 4
        for entry in range(4):
            part = slice(entry * rows, (entry + 1) * rows)
            write_pieces(entry, slice(0, rows), total[part], pieces)
            write_pieces(entry, slice(0, rows), branch[part], branch_pieces)


def backward_products(top, gate, up, act, early, late, late_down):
    tokens, depth = top.shape
    columns = gate.shape[1]
    bands, _, tiles, half, width = early.shape
    strips = depth // width
    block = pl.BlockSpec((tokens, width), lambda n: (0, n))
    anywhere = pl.BlockSpec(memory_space=pl.ANY)
    piece = jax.ShapeDtypeStruct((2, tokens // 4, depth // 2), jnp.bfloat16)
    grads = jax.ShapeDtypeStruct((tokens, columns), jnp.bfloat16)
    outs = pl.pallas_call(
        backward_kernel,
        out_shape=[grads] * 2 + [piece] * 8,
        grid=(columns // width,),
        in_specs=[pl.BlockSpec(top.shape, lambda n: (0, 0))] + [block] * 3 + [anywhere] * 3,
        out_specs=[block] * 2 + [pl.BlockSpec(piece.shape, lambda n: (0, 0, 0))] * 8,
        scratch_shapes=[
            pltpu.VMEM((2, 2, bands, tiles, 2, half, width), jnp.bfloat16),
            pltpu.VMEM((2, strips, tiles, 2, half, width), jnp.bfloat16),
            pltpu.VMEM((tokens, depth), jnp.float32),
            pltpu.VMEM((tokens, depth), jnp.float32),
            pltpu.SemaphoreType.DMA((2, 2, 2)),
            pltpu.SemaphoreType.DMA((2, 2)),
        ],
        compiler_params=pltpu.CompilerParams(vmem_limit_bytes=60 * 2**20),
        cost_estimate=pl.CostEstimate(
            flops=8 * tokens * depth * columns, bytes_accessed=8 * columns * depth, transcendentals=0
        ),
    )(top, gate, up, act, early, late, late_down)
    return outs[0], outs[1], outs[2:6], outs[6:10]


def rope_kernel(q_width, kv_width, x_ref, cos_ref, sin_ref, *outs):
    width = x_ref.shape[-1]
    for start in range(0, width, BLK):
        values = x_ref[0, :, start : start + BLK]
        first, turned = half_turn(values)
        sines = sin_ref[0]
        turned_rows = values * cos_ref[0] + turned * jnp.where(first, -sines, sines)
        if start + BLK > q_width + kv_width:
            column = lax.broadcasted_iota(jnp.int32, values.shape, 1) + start
            turned_rows = jnp.where(column >= q_width + kv_width, values, turned_rows)
        if start < q_width:
            outs[0][0, :, start : start + BLK] = (turned_rows * HD ** (-0.5)).astype(jnp.bfloat16)
        else:
            outs[-1][0, :, start - q_width : start - q_width + BLK] = turned_rows.astype(jnp.bfloat16)


def rope_rows(inner, rows, row_block, q_width, kv_width, cosines, sines, with_queries=True):
    seqs, _, width = inner.shape
    shared = cosines.shape[0] == 1
    table = pl.BlockSpec((1, rows, BLK), lambda s: (0 if shared else s, 0, 0))
    widths = [q_width, 2 * kv_width]
    column_block = 0
    if not with_queries:
        width, column_block = 2 * kv_width, q_width // (2 * kv_width)
        widths, q_width = widths[1:], 0
    return pl.pallas_call(
        functools.partial(rope_kernel, q_width, kv_width),
        out_shape=[jax.ShapeDtypeStruct((seqs, rows, w), jnp.bfloat16) for w in widths],
        grid=(seqs,),
        in_specs=[pl.BlockSpec((1, rows, width), lambda s: (s, row_block, column_block)), table, table],
        out_specs=[pl.BlockSpec((1, rows, w), lambda s: (s, 0, 0)) for w in widths],
        cost_estimate=pl.CostEstimate(
            flops=6 * seqs * rows * width, bytes_accessed=6 * seqs * rows * width, transcendentals=0
        ),
    )(inner, cosines, sines)


def fill_bias(band_ref, gpos_ref, bias_ref, rows, window_len):
    band = band_ref[0]

    @pl.when(pl.program_id(0) == 0)
    def _():
        key = lax.broadcasted_iota(jnp.int32, (window_len, rows), 0) + (
            band * rows - (window_len - rows)
        )
        query = lax.broadcasted_iota(jnp.int32, (window_len, rows), 1) + band * rows
        inside = (key > query - WINDOW) & (key <= query) & (key >= 0)
        bias_ref[:window_len] = jnp.where(inside, 0.0, masked_value)

    glob_total = gpos_ref.shape[1]
    query = lax.broadcasted_iota(jnp.int32, (glob_total, rows), 1) + (band * rows - WINDOW)
    spot = jnp.broadcast_to(gpos_ref[0][:, :1], (glob_total, rows))
    bias_ref[window_len:] = jnp.where(spot <= query.astype(jnp.float32), 0.0, masked_value)


def over_last(left, right):
    return lax.dot_general(left, right, (((1,), (1,)), ((), ())), preferred_element_type=jnp.float32)


def over_first(left, right):
    return lax.dot_general(left, right, (((0,), (0,)), ((), ())), preferred_element_type=jnp.float32)


def attend_kernel(block_total, band_ref, gpos_ref, q_ref, *refs):
    blocks, (out_ref, lse_ref, bias_ref) = refs[:block_total], refs[block_total:]
    rows, q_width = q_ref.shape[1:]
    kv_width = blocks[0].shape[2] // 2
    heads, group = q_width // HD, q_width // kv_width
    window_len = rows * (block_total - 1)
    fill_bias(band_ref, gpos_ref, bias_ref, rows, window_len)
    starts = [rows * number for number in range(block_total)]
    pending = []
    for head in range(heads):
        left = head // group * HD
        queries = q_ref[0, :, head * HD : (head + 1) * HD]
        scores = [
            over_last(block[0, :, left : left + HD], queries)
            + bias_ref[start : start + block.shape[1]]
            for block, start in zip(blocks, starts)
        ]
        top = functools.reduce(jnp.maximum, [jnp.max(part, 0, keepdims=True) for part in scores])
        total = 0.0
        mixed = 0.0
        for block, part in zip(blocks, scores):
            weights = jnp.exp(part - top)
            total = total + jnp.sum(weights, 0, keepdims=True)
            mixed = mixed + over_first(
                block[0, :, kv_width + left : kv_width + left + HD], weights.astype(jnp.bfloat16)
            )
        lse_ref[0, head : head + 1, :] = top + jnp.log(total)
        pending.append(mixed / total)
        if len(pending) * HD == BLK or head == heads - 1:
            stop = (head + 1) * HD
            both = jnp.concatenate(pending, 0).T
            out_ref[0, :, stop - both.shape[1] : stop] = both.astype(jnp.bfloat16)
            pending = []


def attend(band, gpos, queries, blocks):
    seqs, rows, q_width = queries.shape
    heads = q_width // HD
    key_total = sum(block.shape[1] for block in blocks)

    def whole(array):
        return pl.BlockSpec((1,) + array.shape[1:], lambda s, *_: (s, 0, 0))

    out_shape = [
        jax.ShapeDtypeStruct((seqs, rows, q_width), jnp.bfloat16),
        jax.ShapeDtypeStruct((seqs, heads, rows), jnp.float32),
    ]
    return pl.pallas_call(
        functools.partial(attend_kernel, len(blocks)),
        out_shape=out_shape,
        grid_spec=pltpu.PrefetchScalarGridSpec(
            num_scalar_prefetch=1,
            grid=(seqs,),
            in_specs=[whole(array) for array in (gpos, queries, *blocks)],
            out_specs=[whole(array) for array in out_shape],
            scratch_shapes=[pltpu.VMEM((key_total, rows), jnp.float32)],
        ),
        compiler_params=pltpu.CompilerParams(vmem_limit_bytes=48 * 2**20),
        cost_estimate=pl.CostEstimate(
            flops=16 * seqs * heads * rows * key_total * HD,
            bytes_accessed=4 * queries.size,
            transcendentals=seqs * heads * rows * key_total,
        ),
    )(band, gpos, queries, *blocks)


def attend_back_kernel(block_total, band_ref, gpos_ref, cos_ref, sin_ref, q_ref, grad_ref, lse_ref, *refs):
    blocks = refs[:block_total]
    dq_ref = refs[block_total]
    out_refs = refs[block_total + 1 : 2 * block_total + 1]
    bias_ref = refs[-1]
    rows, q_width = q_ref.shape[1:]
    kv_width = blocks[0].shape[2] // 2
    heads, group = q_width // HD, q_width // kv_width
    window_len = rows * (block_total - 1)
    fill_bias(band_ref, gpos_ref, bias_ref, rows, window_len)
    starts = [rows * number for number in range(block_total)]
    pending = []
    for kv_head in range(kv_width // HD):
        left = kv_head * HD
        key_sums = [0.0] * block_total
        value_sums = [0.0] * block_total
        for head in range(kv_head * group, (kv_head + 1) * group):
            queries = q_ref[0, :, head * HD : (head + 1) * HD]
            grads = grad_ref[0, :, head * HD : (head + 1) * HD]
            lse = lse_ref[0, head : head + 1, :]
            soft, soft_grads = [], []
            inner = 0.0
            for number, (block, start) in enumerate(zip(blocks, starts)):
                part = over_last(block[0, :, left : left + HD], queries)
                part = jnp.exp(part + bias_ref[start : start + block.shape[1]] - lse)
                slope = over_last(block[0, :, kv_width + left : kv_width + left + HD], grads)
                inner = inner + jnp.sum(part * slope, 0, keepdims=True)
                soft.append(part)
                soft_grads.append(slope)
            turned = 0.0
            for number, block in enumerate(blocks):
                score_grads = (soft[number] * (soft_grads[number] - inner)).astype(jnp.bfloat16)
                value_sums[number] = value_sums[number] + jnp.dot(
                    soft[number].astype(jnp.bfloat16), grads, preferred_element_type=jnp.float32
                )
                key_sums[number] = key_sums[number] + jnp.dot(
                    score_grads, queries, preferred_element_type=jnp.float32
                )
                turned = turned + over_first(block[0, :, left : left + HD], score_grads)
            pending.append(turned)
            if len(pending) * HD == BLK or head == heads - 1:
                stop = (head + 1) * HD
                both = jnp.concatenate(pending, 0).T * HD ** (-0.5)
                pending = []
                first, other = half_turn(both * sin_ref[0])
                both = both * cos_ref[0] + jnp.where(first, other, -other)
                dq_ref[0, :, stop - both.shape[1] : stop] = both.astype(jnp.bfloat16)
        for number, out_ref in enumerate(out_refs):
            out_ref[0, :, left : left + HD] = key_sums[number].astype(out_ref.dtype)
            out_ref[0, :, kv_width + left : kv_width + left + HD] = value_sums[number].astype(
                out_ref.dtype
            )


def attend_back(band, gpos, cosines, sines, queries, grads, lse, blocks):
    seqs, rows, q_width = queries.shape
    heads = q_width // HD
    key_total = sum(block.shape[1] for block in blocks)

    def whole(array):
        return pl.BlockSpec((1,) + array.shape[1:], lambda s, *_: (s, 0, 0))

    table = pl.BlockSpec((1, rows, BLK), lambda s, *_: (0, 0, 0))
    out_shape = [jax.ShapeDtypeStruct(queries.shape, jnp.bfloat16)]
    for number, block in enumerate(blocks):
        own = number == len(blocks) - 2
        out_shape.append(jax.ShapeDtypeStruct(block.shape, jnp.float32 if own else jnp.bfloat16))
    return pl.pallas_call(
        functools.partial(attend_back_kernel, len(blocks)),
        out_shape=out_shape,
        grid_spec=pltpu.PrefetchScalarGridSpec(
            num_scalar_prefetch=1,
            grid=(seqs,),
            in_specs=[whole(gpos), table, table]
            + [whole(array) for array in (queries, grads, lse, *blocks)],
            out_specs=[whole(array) for array in out_shape],
            scratch_shapes=[pltpu.VMEM((key_total, rows), jnp.float32)],
        ),
        compiler_params=pltpu.CompilerParams(vmem_limit_bytes=48 * 2**20),
        cost_estimate=pl.CostEstimate(
            flops=40 * seqs * heads * rows * key_total * HD,
            bytes_accessed=8 * queries.size,
            transcendentals=seqs * heads * rows * key_total,
        ),
    )(band, gpos, cosines, sines, queries, grads, lse, *blocks)


def join_kernel(q_width, kv_width, dq_ref, own_ref, pick_ref, glob_ref, cos_ref, sin_ref, *refs):
    back_refs, out_ref = refs[:-1], refs[-1]
    out_ref[0, :, :q_width] = dq_ref[0]
    picked = lax.dot_general(
        pick_ref[0].astype(jnp.float32),
        glob_ref[0],
        (((0,), (0,)), ((), ())),
        precision=lax.Precision.HIGHEST,
        preferred_element_type=jnp.float32,
    )
    for start in range(0, 2 * kv_width, BLK):
        lanes = slice(start, start + BLK)
        total = own_ref[0, :, lanes] + picked[:, lanes]
        for back_ref in back_refs:
            total = total + back_ref[0, :, lanes].astype(jnp.float32)
        first, other = half_turn(total * sin_ref[0])
        turned = total * cos_ref[0] + jnp.where(first, other, -other)
        column = lax.broadcasted_iota(jnp.int32, total.shape, 1) + start
        turned = jnp.where(column >= kv_width, total, turned)
        out_ref[0, :, q_width + start : q_width + start + BLK] = turned.astype(jnp.bfloat16)


def join_grads(dq, own, picks, globs, cosines, sines, backs):
    seqs, rows, q_width = dq.shape
    kv_width = own.shape[2] // 2

    def whole(array):
        return pl.BlockSpec((1,) + array.shape[1:], lambda s: (s, 0, 0))

    table = pl.BlockSpec((1, rows, BLK), lambda s: (0, 0, 0))
    out_shape = jax.ShapeDtypeStruct((seqs, rows, q_width + 2 * kv_width), jnp.bfloat16)
    return pl.pallas_call(
        functools.partial(join_kernel, q_width, kv_width),
        out_shape=out_shape,
        grid=(seqs,),
        in_specs=[whole(dq), whole(own), whole(picks), whole(globs), table, table]
        + [whole(back) for back in backs],
        out_specs=whole(out_shape),
        cost_estimate=pl.CostEstimate(
            flops=20 * own.size, bytes_accessed=4 * dq.size + 12 * own.size, transcendentals=0
        ),
    )(dq, own, picks, globs, cosines, sines, *backs)


def adam_kernel(batch, meta, rates, *refs):
    master_ref, first_ref, second_ref, left_ref, right_ref = refs[:5]
    sources = refs[5:-6]
    new_first_ref, new_second_ref, new_master_ref, copy_ref, tiles, arrived = refs[-6:]
    step, steps = pl.program_id(0), pl.num_programs(0)
    slot = step % 2

    def fetch(at_step, at_slot):
        for place in range(batch):
            tile = at_step * batch + place
            for number, source in enumerate(sources):

                @pl.when(meta[0, tile] == number)
                def _(source=source, tile=tile, place=place):
                    top = pl.multiple_of(meta[2, tile], BLK)
                    left = pl.multiple_of(meta[3, tile], BLK)
                    pltpu.make_async_copy(
                        source.at[meta[1, tile], pl.ds(top, BLK), pl.ds(left, BLK)],
                        tiles.at[at_slot, place],
                        arrived.at[at_slot],
                    ).start()

    @pl.when(step == 0)
    def _():
        fetch(0, 0)

    @pl.when(step + 1 < steps)
    def _():
        fetch(step + 1, 1 - slot)

    pltpu.make_async_copy(tiles.at[slot], tiles.at[slot], arrived.at[slot]).wait()
    places = range(batch)
    lefts = [left_ref[place].astype(jnp.bfloat16) for place in places]
    rights = [right_ref[place].astype(jnp.bfloat16) for place in places]
    turned = [over_first(lefts[place], tiles[slot, place]).astype(jnp.bfloat16) for place in places]
    rotated = [
        jnp.dot(turned[place], rights[place], preferred_element_type=jnp.float32) for place in places
    ]
    directions = []
    for place in places:
        new_first = beta_one * first_ref[place] + (1.0 - beta_one) * rotated[place]
        new_second = beta_two * second_ref[place] + (1.0 - beta_two) * rotated[place] * rotated[place]
        direction = (new_first * (1.0 / (1.0 - beta_one**STEP))) / (
            jnp.sqrt(new_second * (1.0 / (1.0 - beta_two**STEP))) + adam_eps
        )
        new_first_ref[place] = new_first
        new_second_ref[place] = new_second
        directions.append(direction.astype(jnp.bfloat16))
    updates = [
        jnp.dot(lefts[place], directions[place], preferred_element_type=jnp.float32) for place in places
    ]
    updates = [over_last(updates[place].astype(jnp.bfloat16), rights[place]) for place in places]
    for place in places:
        old = master_ref[place]
        new_master = old - rates[step * batch + place] * (updates[place] + weight_decay * old)
        new_master_ref[place] = new_master
        copy_ref[place] = new_master.astype(jnp.bfloat16)


def adam(meta, rates, state, sources):
    count = state[0].shape[0]
    batch = max(size for size in range(1, 33) if count % size == 0)
    block = pl.BlockSpec((batch, BLK, BLK), lambda s, *_: (s, 0, 0))
    anywhere = pl.BlockSpec(memory_space=pl.ANY)
    shape = (count, BLK, BLK)
    return pl.pallas_call(
        functools.partial(adam_kernel, batch),
        out_shape=[jax.ShapeDtypeStruct(shape, jnp.float32)] * 3
        + [jax.ShapeDtypeStruct(shape, jnp.bfloat16)],
        grid_spec=pltpu.PrefetchScalarGridSpec(
            num_scalar_prefetch=2,
            grid=(count // batch,),
            in_specs=[block] * 5 + [anywhere] * len(sources),
            out_specs=[block] * 4,
            scratch_shapes=[
                pltpu.VMEM((2, batch, BLK, BLK), jnp.bfloat16),
                pltpu.SemaphoreType.DMA((2,)),
            ],
        ),
        compiler_params=pltpu.CompilerParams(vmem_limit_bytes=56 * 2**20),
        cost_estimate=pl.CostEstimate(
            flops=8 * count * BLK**3, bytes_accessed=36 * count * BLK**2, transcendentals=0
        ),
    )(meta, rates, *state, *sources)


def per_device(
    block_input,
    cotangent,
    glob_select,
    assignment,
    master,
    first_moment,
    second_moment,
    left_basis,
    right_basis,
    gains,
    gain_first,
    gain_second,
):
    band_total = lax.axis_size("fsdp")
    rep_total = lax.axis_size("rep")
    place = lax.axis_index("rep")
    band = lax.axis_index("fsdp")
    heads = H // rep_total
    kv_heads = KVH // rep_total
    q_width = heads * HD
    kv_width = kv_heads * HD
    tok_count = block_input.shape[1]
    own_count = master.shape[1]
    tile_total = own_count * rep_total
    aligned = square() and whole_tiles(band_total, rep_total)
    tile_order = assignment[0]

    residual = block_input[0].astype(jnp.float32)
    grad_top = cotangent[0]
    position = band * tok_count + jnp.arange(tok_count, dtype=jnp.int32)
    cosine_table, sine_table = rope_tables(position)
    wide_cosine = jnp.concatenate([cosine_table, cosine_table], 1)[None]
    wide_sine = jnp.concatenate([sine_table, sine_table], 1)[None]
    scale_one = lax.rsqrt(jnp.mean(residual * residual, -1, keepdims=True) + norm_eps)
    normed_one = (residual * scale_one * gains[0]).astype(jnp.bfloat16)
    pick_rows = glob_select[0]
    glob_total = pick_rows.shape[0]
    selector = pick_rows.astype(jnp.bfloat16)
    glob_pos_part = jnp.sum(pick_rows * position[None, :], 1)
    digits = jnp.concatenate([glob_pos_part // 256, glob_pos_part % 256]).astype(jnp.bfloat16)
    digits = jnp.pad(digits[None], ((0, 7), (0, D - 2 * glob_total)))
    glob_rows = jnp.dot(selector, normed_one, preferred_element_type=jnp.float32).astype(jnp.bfloat16)
    glob_rows = add_all(jnp.concatenate([glob_rows, digits], 0), "fsdp").astype(jnp.bfloat16)
    packed = [normed_one, glob_rows, selector.reshape(-1, D)]
    packed = jnp.concatenate(packed, 0)
    packed = jnp.pad(packed, ((0, -packed.shape[0] % 32), (0, 0)))

    def over_bands(slice_rows):
        return lax.all_gather(slice_rows, "fsdp", axis=0, tiled=True)

    if aligned:
        half = BLK // 2
        low, high = (master[0, :, rows].astype(jnp.bfloat16) for rows in (slice(0, half), slice(half, BLK)))
        layout = slice_layout(band_total, rep_total)
        attn_layout = jnp.asarray(np.concatenate(layout[:4], 2))
        wanted = jnp.take(tile_order, by_place(attn_layout).reshape(-1), mode="clip")
        meta = jnp.stack([wanted // own_count == place, wanted % own_count], 0).astype(jnp.int32)
        attn_part = place_tiles(low, high, meta, *attn_layout.shape)
        attn_part = rep_scatter(attn_part).astype(jnp.bfloat16)
        low, attn_part = lax.optimization_barrier((low, attn_part))
        slots = square_pieces(low)
        attn = over_bands(attn_part)
        grids = [lax.dynamic_index_in_dim(jnp.asarray(grid), place, 0, False) for grid in layout]

        def find(wanted):
            wanted = jnp.take(tile_order, jnp.concatenate([grid.reshape(-1) for grid in wanted]), mode="clip")
            entry, row = (wanted // own_count) ^ place, wanted % own_count
            cut = own_count // 2
            high = (entry == 3) & (row >= cut)
            found = jnp.stack([jnp.where(high, 4, entry), jnp.where(high, row - cut, row)], 0)
            return found.astype(jnp.int32)

        all_grid = jnp.concatenate(grids[4:], 1)
        (first_part,) = gather_strips(slots, find([all_grid]), [all_grid.shape])
        packed, first_part, attn = lax.optimization_barrier((packed, first_part, attn))
        early = over_bands(first_part)
    packed_all = rep_gather(packed)
    if aligned:
        packed_all, high = lax.optimization_barrier((packed_all, high))
        later_slots = square_pieces(high)
    normed_one_all = packed_all[:, :tok_count].reshape(-1, D)
    at = tok_count + glob_total
    glob_digits = packed_all[:, at, : 2 * glob_total].astype(jnp.float32)
    glob_place = glob_digits[:, :glob_total] * 256.0 + glob_digits[:, glob_total:]
    at += 8
    selector_all = packed_all[:, at : at + selector.size // D].reshape(rep_total, glob_total, tok_count)

    if aligned:
        in_width = q_width + 2 * kv_width
        w_inner, w_output = attn[:, :in_width], attn[:, in_width:]
    else:
        slots = lax.all_gather(master[0].astype(jnp.bfloat16), "rep", axis=0, tiled=True)
        tiles = jnp.take(slots, tile_order, axis=0, mode="clip")
        slices = cut_slices(band_matrices(tiles, band_total), band_total, rep_total)
        w_inner = over_bands(jnp.concatenate(slices[0:3], 1))
        w_output = over_bands(slices[3])
        w_gate = over_bands(slices[4])
        w_up = over_bands(slices[5])
        w_down = over_bands(slices[6])

    w_output = by_place(w_output.reshape(rep_total, q_width, -1)).reshape(D, -1)

    def mul(rows, weight):
        return jnp.dot(rows, weight, preferred_element_type=jnp.float32)

    def mul_back(rows, weight):
        return lax.dot_general(rows, weight, (((1,), (1,)), ((), ())), preferred_element_type=jnp.float32)

    def weight_grad(rows, grad_rows):
        return lax.dot_general(
            rows, grad_rows, (((0,), (0,)), ((), ())), preferred_element_type=jnp.float32
        ).astype(jnp.bfloat16)

    def own_sum(partial):
        return rep_scatter(partial.astype(jnp.bfloat16).reshape(rep_total, tok_count, D))

    inner_rows = mul(packed_all.reshape(-1, D), w_inner).reshape(rep_total, -1, w_inner.shape[1])
    packed_all, normed_one_all = lax.optimization_barrier((packed_all, normed_one_all))
    queries, own_pairs = rope_rows(inner_rows, tok_count, 0, q_width, kv_width, wide_cosine, wide_sine)
    glob_cosine, glob_sine = rope_tables(glob_place.reshape(-1))
    glob_cosine = jnp.concatenate([glob_cosine, glob_cosine], 1).reshape(rep_total, glob_total, -1)
    glob_sine = jnp.concatenate([glob_sine, glob_sine], 1).reshape(rep_total, glob_total, -1)
    (glob_pairs,) = rope_rows(
        inner_rows, glob_total, tok_count // glob_total, q_width, kv_width, glob_cosine, glob_sine, False
    )
    back_count = (WINDOW + tok_count - 2) // tok_count
    odd = band % 2 == 1
    by_chip = back_count == 2 and band_total % 2 == 0
    if by_chip:
        two_back = shifted(own_pairs, "fsdp", 2)
        pair_blocks = [two_back, to_core(jnp.where(odd, two_back, own_pairs))]
    else:
        pair_blocks = [shifted(own_pairs, "fsdp", distance) for distance in range(back_count, 0, -1)]
    pair_blocks = pair_blocks + [own_pairs, glob_pairs]
    glob_spots = jnp.broadcast_to(glob_place[:, :, None], (rep_total, glob_total, BLK))
    band_number = band.astype(jnp.int32).reshape(1)
    attended_low, lse = attend(band_number, glob_spots, queries, pair_blocks)
    if aligned:
        *later_slots, attended_low, early = lax.optimization_barrier((*later_slots, attended_low, early))
        last_grid = jnp.concatenate(grids[4:6], 1)
        last_part, down_part = gather_strips(
            later_slots, find([last_grid, grids[6]]), [last_grid.shape, grids[6].shape]
        )

        def by_strips(gathered):
            return gathered.reshape(band_total, -1, all_grid.shape[0], half, gathered.shape[-1])

        early, late, late_down = by_strips(early), by_strips(over_bands(last_part)), by_strips(over_bands(down_part))
    attended_all = rep_features(attended_low).reshape(-1, D)
    columns = mul(attended_all, w_output).astype(jnp.bfloat16).reshape(rep_total, tok_count, -1)
    branch = by_place(rep_exchange(columns)).transpose(1, 0, 2).reshape(tok_count, D)
    middle = residual + branch.astype(jnp.float32)
    scale_two = lax.rsqrt(jnp.mean(middle * middle, -1, keepdims=True) + norm_eps)
    normed_two = (middle * scale_two * gains[1]).astype(jnp.bfloat16)
    normed_two_all = rep_gather(normed_two).reshape(-1, D)
    normed_two_all, grad_top_now = lax.optimization_barrier((normed_two_all, grad_top))
    top_first = gather_first(grad_top_now)

    if aligned:
        gate_rows, up_rows, activation = forward_products(normed_two_all, early, late, FF // rep_total)
        top_first, activation = after(top_first, activation)
        grad_top_all = gather_join(gather_second(top_first)).reshape(-1, D)
        g_down = weight_grad(activation, grad_top_all)
        grad_top_all, g_down = lax.optimization_barrier((grad_top_all, g_down))
        grad_gate, grad_up, pieces, branch_pieces = backward_products(
            grad_top_all, gate_rows, up_rows, activation, early, late, late_down
        )
        normed_first = sum_first(pieces)
        normed_first, g_gate = after(normed_first, weight_grad(normed_two_all, grad_gate))
        grad_normed_two = sum_second(normed_first)
    else:
        gate_rows = mul(normed_two_all, w_gate)
        up_rows = mul(normed_two_all, w_up)
        sigmoid_gate = jax.nn.sigmoid(gate_rows)
        silu_gate = gate_rows * sigmoid_gate
        activation = (silu_gate * up_rows).astype(jnp.bfloat16)
        grad_top_all = gather_join(gather_second(top_first)).reshape(-1, D)
        g_down = weight_grad(activation, grad_top_all)
        grad_act = mul_back(grad_top_all, w_down)
        grad_gate = (
            grad_act * up_rows * sigmoid_gate * (1.0 + gate_rows * (1.0 - sigmoid_gate))
        ).astype(jnp.bfloat16)
        grad_up = (grad_act * silu_gate).astype(jnp.bfloat16)
        grad_normed_two = own_sum(mul_back(grad_gate, w_gate) + mul_back(grad_up, w_up))
        branch_pieces = (mul(activation, w_down),)
        g_gate = weight_grad(normed_two_all, grad_gate)
    grad_normed_two, g_gate = lax.optimization_barrier((grad_normed_two, g_gate))

    def over_tokens(partial):
        return lax.psum_scatter(partial, "fsdp", scatter_dimension=0, tiled=True)

    s_down = over_tokens(g_down)
    s_gate = over_tokens(g_gate)

    grad_middle = grad_top.astype(jnp.float32) + norm_back(middle, scale_two, gains[1], grad_normed_two)
    grad_parts = grad_middle.astype(jnp.bfloat16).reshape(tok_count, rep_total, -1).transpose(1, 0, 2)
    grad_columns = rep_exchange(by_place(grad_parts)).reshape(rep_total * tok_count, -1)
    grad_columns, grad_up = lax.optimization_barrier((grad_columns, grad_up))
    grad_attended, g_up = rep_features_sum(
        grad_columns.reshape(rep_total, tok_count, -1),
        w_output,
        lambda: weight_grad(normed_two_all, grad_up),
    )
    grad_attended = grad_attended.astype(jnp.bfloat16)
    (s_down, g_up), grad_attended = after((s_down, g_up), grad_attended)
    down_first = gather_first(s_down)
    grad_queries, *grad_blocks = attend_back(
        band_number, glob_spots, wide_cosine, wide_sine, queries, grad_attended, lse, pair_blocks
    )
    down_first, *grad_blocks = after(down_first, *grad_blocks)
    down_second = gather_second(down_first)
    branch_pieces, *grad_blocks = after(tuple(branch_pieces), *grad_blocks)
    branch_first = sum_first(branch_pieces) if aligned else (own_sum(branch_pieces[0]),)
    if by_chip:
        came = to_core(grad_blocks[1])
        total = grad_blocks[0].astype(jnp.float32) + came.astype(jnp.float32)
        sent = jnp.where(odd, total.astype(jnp.bfloat16), grad_blocks[0])
        returned = [shifted(sent, "fsdp", -2), jnp.where(odd, jnp.zeros_like(came), came)]
    else:
        returned = [
            shifted(grad_blocks[back_count - distance], "fsdp", -distance)
            for distance in range(1, back_count + 1)
        ]
    glob_grads = add_all(grad_blocks[-1], "fsdp")
    branch_first, down_second, g_up, glob_grads, s_gate, *returned = lax.optimization_barrier(
        (branch_first, down_second, g_up, glob_grads, s_gate, *returned)
    )
    s_up = over_tokens(g_up)
    gate_first = gather_first(s_gate)
    s_down = gather_join(down_second)
    block_out = middle + (sum_second(branch_first) if aligned else branch_first[0])
    grad_inner = join_grads(
        grad_queries, grad_blocks[-2], selector_all, glob_grads, wide_cosine, wide_sine, returned
    ).reshape(-1, q_width + 2 * kv_width)
    grad_normed_parts = mul_back(grad_inner, w_inner).astype(jnp.bfloat16).reshape(rep_total, tok_count, D)
    if square():
        normed_first = sum_first(split_pieces(grad_normed_parts))
    else:
        normed_first = (rep_scatter(grad_normed_parts),)
    grad_inner, grad_normed_parts = lax.optimization_barrier((grad_inner, grad_normed_parts))
    g_inner = weight_grad(normed_one_all, grad_inner)
    attended_all, g_inner = lax.optimization_barrier((attended_all, g_inner))
    g_output = weight_grad(attended_all, grad_columns)
    g_output = by_place(g_output.reshape(rep_total, q_width, -1)).reshape(D, -1)
    g_attn = with_layout_constraint(jnp.concatenate([g_inner, g_output], 1), Layout((0, 1)))
    gate_first, block_out, *normed_first = after(gate_first, block_out, *normed_first)
    gate_second = gather_second(gate_first)
    grad_normed_one = sum_second(normed_first) if square() else normed_first[0]
    gate_second, s_up, g_attn, grad_normed_one = after(gate_second, s_up, g_attn, grad_normed_one)
    s_attn = over_tokens(g_attn)
    s_gate = gather_join(gate_second)
    up_first = gather_first(s_up)
    grad_input = grad_middle + norm_back(residual, scale_one, gains[0], grad_normed_one)

    gain_terms = jnp.stack(
        [
            jnp.sum(grad_normed_one * residual * scale_one, 0),
            jnp.sum(grad_normed_two * middle * scale_two, 0),
        ]
    )
    square_terms = jnp.stack(
        [jnp.sum(residual * residual), jnp.sum(middle * middle), jnp.sum(block_out * block_out)]
    )
    sums = jnp.concatenate([gain_terms.reshape(-1), square_terms])

    up_first, sums = after(up_first, sums)
    s_up = gather_join(gather_second(up_first))
    sums = add_all(add_all(sums, "rep"), "fsdp")
    sums, s_attn, s_up, s_gate, s_down = lax.optimization_barrier((sums, s_attn, s_up, s_gate, s_down))
    gain_grad, square_total = sums[: 2 * D].reshape(2, D), sums[2 * D :]

    slot_ids = jnp.arange(tile_total, dtype=jnp.int32)
    inverse = jnp.sum(jnp.where(tile_order[None, :] == slot_ids[:, None], slot_ids[None, :], 0), 1)
    own_slots = place * own_count + jnp.arange(own_count, dtype=jnp.int32)
    owned_tiles = jnp.take(inverse, own_slots, mode="clip")
    if aligned:
        sources = [rep_gather(s_attn), s_gate, s_up, s_down]
        where = np.zeros((4, rep_total, tile_total), np.int32)
        first_col = 0
        for kind, grid in enumerate(layout):
            rows, cols = grid.shape[1:]
            first_col = 0 if kind >= 4 else first_col
            for there in range(rep_total):
                numbers = grid[there].reshape(-1)
                at = np.arange(rows * cols)
                where[0, :, numbers] = max(kind - 3, 0)
                where[2, :, numbers] = (at // cols * BLK)[:, None]
                where[3, :, numbers] = (at % cols * BLK + first_col)[:, None]
                for here in range(rep_total):
                    where[1, here, numbers] = here ^ there
            first_col += cols * BLK
        tile_spots = lax.dynamic_index_in_dim(jnp.asarray(where), place, 1, False)
        meta = jnp.take(tile_spots, owned_tiles, axis=1, mode="clip")
    else:
        splits = [0, q_width, q_width + kv_width, q_width + 2 * kv_width, s_attn.shape[1]]
        stacks = [rep_gather(s_attn[:, low:high]) for low, high in zip(splits, splits[1:])]
        stacks += [s_gate, s_up, s_down]
        sources = [band_tiles(join_slices(stacks, band_total, rep_total))]
        meta = jnp.stack([0 * owned_tiles, owned_tiles, 0 * owned_tiles, 0 * owned_tiles], 0)
    slot_rates = jnp.take(kind_rates(band_total), owned_tiles, mode="clip")
    new_first, new_second, new_master, master_copy = adam(
        meta,
        slot_rates,
        (master[0], first_moment[0], second_moment[0], left_basis[0], right_basis[0]),
        sources,
    )
    new_gain_first = beta_one * gain_first + (1.0 - beta_one) * gain_grad
    new_gain_second = beta_two * gain_second + (1.0 - beta_two) * gain_grad * gain_grad
    gain_step = (
        new_gain_first
        / (1.0 - beta_one**STEP)
        / (jnp.sqrt(new_gain_second / (1.0 - beta_two**STEP)) + adam_eps)
    )
    new_gains = gains - gain_rate * gain_step
    rms_stats = jnp.sqrt(square_total / (rep_total * band_total * tok_count * D))
    return (
        block_out[None],
        grad_input[None],
        new_first[None],
        new_second[None],
        new_master[None],
        master_copy[None],
        new_gain_first,
        new_gain_second,
        new_gains,
        rms_stats,
    )


def solution(mesh):
    in_specs = (
        P("rep", "fsdp", None),
        P("rep", "fsdp", None),
        P("rep", None, "fsdp"),
        P("fsdp", None),
        P("fsdp", "rep", None, None),
        P("fsdp", "rep", None, None),
        P("fsdp", "rep", None, None),
        P("fsdp", "rep", None, None),
        P("fsdp", "rep", None, None),
        P(),
        P(),
        P(),
    )
    out_specs = (
        P("rep", "fsdp", None),
        P("rep", "fsdp", None),
        P("fsdp", "rep", None, None),
        P("fsdp", "rep", None, None),
        P("fsdp", "rep", None, None),
        P("fsdp", "rep", None, None),
        P(),
        P(),
        P(),
        P(),
    )
    return jax.shard_map(
        per_device, mesh=mesh, in_specs=in_specs, out_specs=out_specs, check_vma=False
    )
```

```python
import functools

import jax
import jax.numpy as jnp
import numpy as np
from jax import lax
from jax.experimental import pallas as pl
from jax.experimental.layout import Layout, with_layout_constraint
from jax.experimental.pallas import tpu as pltpu
from jax.sharding import PartitionSpec as P

D = 2048
H = 32
KVH = 8
HD = 64
FF = 8192
WINDOW = 512
BLK = 128
STEP = 10


norm_eps = 1e-05
rope_theta = 500000.0
beta_one = 0.5
beta_two = 0.5
adam_eps = 1e-08
weight_decay = 0.1
gain_rate = 0.5
masked_value = -1e30


def matrix_shapes():
    kv_width = KVH * HD
    return [(D, D), (D, kv_width), (D, kv_width), (D, D), (D, FF), (D, FF), (FF, D)]


def kind_rates(band_total):
    rate_list = [
        D ** (-0.5),
        D ** (-0.5),
        D ** (-0.5),
        (D * 8 // WINDOW) ** (-0.5),
        D ** (-0.5),
        D ** (-0.5),
        FF ** (-0.5),
    ]
    pieces = []
    for (row_total, col_total), rate_value in zip(matrix_shapes(), rate_list):
        tile_count = row_total // band_total // BLK * (col_total // BLK)
        pieces.append(jnp.full((tile_count,), rate_value, jnp.float32))
    return jnp.concatenate(pieces)


def band_matrices(tiles, band_total):
    matrices = []
    offset = 0
    for row_total, col_total in matrix_shapes():
        band_rows = row_total // band_total
        tile_count = band_rows // BLK * (col_total // BLK)
        segment = tiles[offset : offset + tile_count].reshape(
            band_rows // BLK, col_total // BLK, BLK, BLK
        )
        matrices.append(segment.transpose(0, 2, 1, 3).reshape(band_rows, col_total))
        offset += tile_count
    return matrices


def band_tiles(matrices):
    pieces = []
    for matrix in matrices:
        row_count, col_count = matrix.shape
        segment = matrix.reshape(row_count // BLK, BLK, col_count // BLK, BLK).transpose(0, 2, 1, 3)
        pieces.append(segment.reshape(-1, BLK, BLK))
    return jnp.concatenate(pieces, 0)


def rope_tables(position):
    halves = jnp.arange(HD // 2, dtype=jnp.float32) * (2.0 / HD)
    frequency = rope_theta ** (-halves)
    angles = position.astype(jnp.float32)[:, None] * frequency[None, :]
    angles = jnp.concatenate([angles, angles], 1)
    return (jnp.cos(angles), jnp.sin(angles))


def rotate(vectors, cosine_table, sine_table):
    half_width = vectors.shape[-1] // 2
    turned = jnp.concatenate([-vectors[..., half_width:], vectors[..., :half_width]], -1)
    return vectors * cosine_table[:, None, :] + turned * sine_table[:, None, :]


def rotate_back(grad_rows, cosine_table, sine_table):
    half_width = grad_rows.shape[-1] // 2
    scaled = grad_rows * sine_table[:, None, :]
    turned = jnp.concatenate([scaled[..., half_width:], -scaled[..., :half_width]], -1)
    return grad_rows * cosine_table[:, None, :] + turned


def norm_back(values, row_scale, gain_row, grad_rows):
    weighted = grad_rows * gain_row
    return row_scale * weighted - values * row_scale**3 * jnp.mean(
        weighted * values, -1, keepdims=True
    )


def to_rep(block, distance):
    route = [(i, i ^ distance) for i in range(lax.axis_size("rep"))]
    return lax.ppermute(block, "rep", route)


def square():
    return lax.axis_size("rep") == 4


def gather_first(block):
    if not square():
        return (lax.all_gather(block, "rep", axis=0),)
    return block, to_rep(block, 1), to_rep(block, 2)


def gather_second(first):
    if not square():
        return first
    block, near, far = first
    cut = block.shape[0] // 2
    return block, near, far, to_rep(near[:cut], 2), to_rep(far[cut:], 1)


def gather_join(pieces):
    if not square():
        return pieces[0]
    return jnp.concatenate(pieces, 0).reshape((4,) + pieces[0].shape)


def square_pieces(block):
    return gather_second(gather_first(block))


def rep_gather(block):
    return gather_join(gather_second(gather_first(block)))


def after(values, *others):
    count = len(values)
    tied = lax.optimization_barrier((*values, *others))
    return tuple(tied[:count]), *tied[count:]


def rep_of(entry):
    place = lax.axis_index("rep")
    return place ^ entry if square() else entry


def rep_scatter(parts):
    if not square():
        flat = parts.reshape(-1, parts.shape[-1])
        return lax.psum_scatter(flat, "rep", scatter_dimension=0, tiled=True).astype(jnp.float32)
    return sum_pieces(*split_pieces(parts))


def split_pieces(parts):
    half = parts.shape[-1] // 2
    low, high = parts[..., :half], parts[..., half:]
    return jnp.stack([low[0], low[2]], 0), jnp.stack([low[1], low[3]], 0), high[:2], high[2:]


def sum_first(pieces):
    low_kept, low_sent, high_kept, high_sent = pieces
    parts = []
    for kept, sent, first in ((low_kept, low_sent, 1), (high_kept, high_sent, 2)):
        came = to_rep(sent, first)
        parts.append(kept[0].astype(jnp.float32) + came[0].astype(jnp.float32))
        parts.append((kept[1].astype(jnp.float32) + came[1].astype(jnp.float32)).astype(kept.dtype))
    return tuple(parts)


def sum_second(parts):
    low, low_other, high, high_other = parts
    low = low + to_rep(low_other, 2).astype(jnp.float32)
    high = high + to_rep(high_other, 1).astype(jnp.float32)
    return jnp.concatenate([low, high], -1)


def sum_pieces(*pieces):
    return sum_second(sum_first(pieces))


def add_all(value, axis, distance=1):
    size = lax.axis_size(axis)
    total = value.astype(jnp.float32)
    while distance < size:
        count = 2 if (size // distance).bit_length() % 2 == 0 else 4
        low = total.astype(value.dtype)
        others = []
        for step in range(1, count):
            route = [(i, i ^ (step * distance)) for i in range(size)]
            others.append(lax.ppermute(low, axis, route).astype(jnp.float32))
        total = total + others[0]
        if count == 4:
            total = total + (others[1] + others[2])
        distance *= count
    return total


def rep_features(block):
    if not square():
        return lax.all_gather(block, "rep", axis=2, tiled=True)
    own, near, far, low, high = square_pieces(block)
    return jnp.concatenate(
        [
            own,
            jnp.stack([near[1], near[0], near[3], near[2]], 0),
            jnp.stack([far[2], far[3], far[0], far[1]], 0),
            jnp.stack([high[1], high[0], low[1], low[0]], 0),
        ],
        2,
    )


def write_pieces(entry, rows, values, refs):
    low_kept, low_sent, high_kept, high_sent = refs
    half = low_kept.shape[-1]
    values = values.astype(jnp.bfloat16)
    (low_sent if entry % 2 else low_kept)[entry // 2, rows] = values[:, :half]
    (high_sent if entry // 2 else high_kept)[entry % 2, rows] = values[:, half:]


def swapped_kernel(x_ref, w_ref, *refs):
    reps, rows, _ = x_ref.shape
    width = w_ref.shape[0] // reps
    for entry in range(reps):
        weight = w_ref[entry * width : (entry + 1) * width]
        for there in range(reps):
            product = over_last(x_ref[there ^ entry], weight)
            write_pieces(entry, slice(there * rows, (there + 1) * rows), product, refs)


def rep_features_sum(columns, weight, meanwhile):
    reps, rows, depth = columns.shape
    width = weight.shape[0] // reps
    if square():
        pieces = pl.pallas_call(
            swapped_kernel,
            out_shape=[jax.ShapeDtypeStruct((2, reps * rows, width // 2), jnp.bfloat16)] * 4,
            compiler_params=pltpu.CompilerParams(vmem_limit_bytes=32 * 2**20),
            cost_estimate=pl.CostEstimate(
                flops=2 * reps * columns.size * width,
                bytes_accessed=10 * columns.size,
                transcendentals=0,
            ),
        )(columns, weight)
        first = sum_first(pieces)
        first, other = after(first, meanwhile())
        total = sum_second(first)
    else:
        other = meanwhile()
        product = over_last(columns.reshape(-1, depth), weight).astype(jnp.bfloat16)
        swapped = product.reshape(reps, rows, reps, width).transpose(2, 0, 1, 3)
        total = rep_scatter(swapped.reshape(reps, reps * rows, width))
    return total.reshape(reps, rows, width), other


def rep_exchange(parts):
    if not square():
        return lax.all_to_all(parts, "rep", 0, 0)
    return jnp.stack([parts[0]] + [to_rep(parts[entry], entry) for entry in (1, 2, 3)], 0)


def by_place(parts):
    entries = [rep_of(entry) for entry in range(parts.shape[0])]
    return jnp.stack([lax.dynamic_index_in_dim(parts, entry, 0, False) for entry in entries], 0)


def to_core(block):
    return lax.ppermute(block, "fsdp", [(i, i ^ 1) for i in range(lax.axis_size("fsdp"))])


def shifted(block, axis, distance):
    devices = range(lax.axis_size(axis))
    route = [(i - distance, i) for i in devices if i - distance in devices]
    return lax.ppermute(block, axis, route)


def tile_offsets(band_total):
    offsets = [0]
    for row_total, col_total in matrix_shapes():
        offsets.append(offsets[-1] + row_total // band_total // BLK * (col_total // BLK))
    return offsets


def whole_tiles(band_total, rep_total):
    return KVH * HD // rep_total % BLK == 0 and FF // band_total // rep_total % BLK == 0


def slice_layout(band_total, rep_total):
    offsets = tile_offsets(band_total)
    layout = []
    for kind, (row_total, col_total) in enumerate(matrix_shapes()):
        rows, cols = row_total // band_total // BLK, col_total // BLK
        grid = offsets[kind] + np.arange(rows * cols).reshape(rows, cols)
        if kind == 6:
            layout.append(grid.reshape(rep_total, rows // rep_total, cols))
        elif kind in (4, 5):
            cut = grid.reshape(rows, band_total, rep_total, -1).transpose(2, 0, 1, 3)
            layout.append(cut.reshape(rep_total, rows, -1))
        else:
            layout.append(grid.reshape(rows, rep_total, -1).transpose(1, 0, 2))
    return layout


def tiles_to_matrix(tiles):
    rows, cols = tiles.shape[:2]
    return tiles.transpose(0, 2, 1, 3).reshape(rows * BLK, cols * BLK)


def matrix_to_tiles(matrix):
    rows, cols = matrix.shape
    cut = matrix.reshape(rows // BLK, BLK, cols // BLK, BLK)
    return cut.transpose(0, 2, 1, 3).reshape(-1, BLK, BLK)


def cut_slices(matrices, band_total, rep_total):
    place = lax.axis_index("rep")
    slices = []
    for kind, matrix in enumerate(matrices):
        rows, cols = matrix.shape
        if kind == 6:
            slices.append(lax.dynamic_slice_in_dim(matrix, place * (rows // rep_total), rows // rep_total, 0))
        elif kind in (4, 5):
            cut = matrix.reshape(rows, band_total, rep_total, -1)
            slices.append(lax.dynamic_index_in_dim(cut, place, 2, False).reshape(rows, -1))
        else:
            slices.append(lax.dynamic_slice_in_dim(matrix, place * (cols // rep_total), cols // rep_total, 1))
    return slices


def join_slices(stacks, band_total, rep_total):
    matrices = []
    for kind, stack in enumerate(stacks):
        rows, cols = stack.shape[1:]
        if kind == 6:
            matrices.append(stack.reshape(-1, cols))
        elif kind in (4, 5):
            cut = stack.reshape(rep_total, rows, band_total, -1).transpose(1, 2, 0, 3)
            matrices.append(cut.reshape(rows, -1))
        else:
            matrices.append(stack.transpose(1, 0, 2).reshape(rows, -1))
    return matrices


def gather_kernel(grids, meta, *refs):
    source_total = len(refs) - len(grids) - 1
    sources, targets, done = refs[:source_total], refs[source_total:-1], refs[-1]
    height = sources[0].shape[1]
    start = 0
    for place, (target, (rows, cols)) in enumerate(zip(targets, grids)):

        def one(tile, carry, target=target, rows=rows, cols=cols, start=start, place=place):
            kind = meta[0, start + tile]
            row = meta[1, start + tile]
            across = tile % cols
            top = pl.multiple_of((across // 2 * rows + tile // cols) * height, height)
            left = pl.multiple_of(across % 2 * BLK, BLK)
            for number, source in enumerate(sources):

                @pl.when(kind == number)
                def _(source=source):
                    pltpu.make_async_copy(
                        source.at[row], target.at[pl.ds(top, height), pl.ds(left, BLK)], done.at[place]
                    ).start()

            return carry

        lax.fori_loop(0, rows * cols, one, 0)
        start += rows * cols
    for place, target in enumerate(targets):
        pltpu.make_async_copy(target, target, done.at[place]).wait()


def gather_strips(sources, meta, grids):
    anywhere = pl.BlockSpec(memory_space=pl.ANY)
    height = sources[0].shape[1]
    out_shape = [
        jax.ShapeDtypeStruct((cols // 2 * rows * height, 2 * BLK), jnp.bfloat16) for rows, cols in grids
    ]
    return pl.pallas_call(
        functools.partial(gather_kernel, grids),
        out_shape=out_shape,
        grid_spec=pltpu.PrefetchScalarGridSpec(
            num_scalar_prefetch=1,
            grid=(1,),
            in_specs=[anywhere] * len(sources),
            out_specs=[pl.BlockSpec(shape.shape, lambda i, *_: (0, 0)) for shape in out_shape],
            scratch_shapes=[pltpu.SemaphoreType.DMA((len(grids),))],
        ),
        compiler_params=pltpu.CompilerParams(vmem_limit_bytes=32 * 2**20),
        cost_estimate=pl.CostEstimate(
            flops=0, bytes_accessed=sum(4 * shape.size for shape in out_shape), transcendentals=0
        ),
    )(meta, *sources)


def place_kernel(entries, rows, cols, meta, low, high, out_ref, done):
    out_ref[...] = jnp.zeros_like(out_ref)
    height = low.shape[1]

    def copies(tile):
        entry, rest = tile // (rows * cols), tile % (rows * cols)
        top = rest // cols * (2 * height)
        left = pl.multiple_of(rest % cols * BLK, BLK)
        return [
            pltpu.make_async_copy(
                half.at[meta[1, tile]],
                out_ref.at[entry, pl.ds(pl.multiple_of(top + part * height, height), height), pl.ds(left, BLK)],
                done.at[part],
            )
            for part, half in enumerate((low, high))
        ]

    def begin(tile, carry):
        @pl.when(meta[0, tile] == 1)
        def _():
            for copy in copies(tile):
                copy.start()

        return carry

    def finish(tile, carry):
        @pl.when(meta[0, tile] == 1)
        def _():
            for copy in copies(tile):
                copy.wait()

        return carry

    lax.fori_loop(0, entries * rows * cols, begin, 0)
    lax.fori_loop(0, entries * rows * cols, finish, 0)


def place_tiles(low, high, meta, entries, rows, cols):
    shape = (entries, rows * BLK, cols * BLK)
    anywhere = pl.BlockSpec(memory_space=pl.ANY)
    return pl.pallas_call(
        functools.partial(place_kernel, entries, rows, cols),
        out_shape=jax.ShapeDtypeStruct(shape, jnp.bfloat16),
        grid_spec=pltpu.PrefetchScalarGridSpec(
            num_scalar_prefetch=1,
            grid=(1,),
            in_specs=[anywhere, anywhere],
            out_specs=pl.BlockSpec(shape, lambda i, *_: (0, 0, 0)),
            scratch_shapes=[pltpu.SemaphoreType.DMA((2,))],
        ),
        compiler_params=pltpu.CompilerParams(vmem_limit_bytes=32 * 2**20),
        cost_estimate=pl.CostEstimate(
            flops=0, bytes_accessed=4 * entries * rows * cols * BLK * BLK, transcendentals=0
        ),
    )(meta, low, high)


def half_turn(values):
    lane = lax.broadcasted_iota(jnp.int32, values.shape, 1)
    lanes = values.shape[1]
    first = lane % HD < HD // 2
    return first, jnp.where(
        first, pltpu.roll(values, lanes - HD // 2, 1), pltpu.roll(values, HD // 2, 1)
    )


def strip_copies(early, late, target, done):
    return [
        pltpu.make_async_copy(half, target.at[:, :, number], done.at[number])
        for number, half in enumerate((early, late))
    ]


def forward_kernel(x_ref, early, late, gate_ref, up_ref, act_ref, weights, done):
    step, steps = pl.program_id(0), pl.num_programs(0)
    slot = step % 2
    width = weights.shape[-1]

    def copies(number, at_step, at_slot):
        strip = number * steps + at_step
        return strip_copies(
            early.at[:, strip], late.at[:, strip], weights.at[number, at_slot], done.at[number, at_slot]
        )

    def fetch(at_step, at_slot):
        for number in range(2):
            for copy in copies(number, at_step, at_slot):
                copy.start()

    @pl.when(step == 0)
    def _():
        fetch(0, 0)

    @pl.when(step + 1 < steps)
    def _():
        fetch(step + 1, 1 - slot)

    for number in range(2):
        for copy in copies(number, step, slot):
            copy.wait()
    gate_weight, up_weight = (weights[number, slot].reshape(-1, width) for number in range(2))
    chunk = min(2 * BLK, x_ref.shape[0])
    for first in range(0, x_ref.shape[0], chunk):
        rows = slice(first, first + chunk)
        gate = jnp.dot(x_ref[rows], gate_weight, preferred_element_type=jnp.float32)
        up = jnp.dot(x_ref[rows], up_weight, preferred_element_type=jnp.float32)
        gate_ref[rows] = gate.astype(jnp.bfloat16)
        up_ref[rows] = up.astype(jnp.bfloat16)
        act_ref[rows] = (gate * jax.nn.sigmoid(gate) * up).astype(jnp.bfloat16)


def forward_products(rows, early, late, columns):
    tokens, depth = rows.shape
    bands, _, tiles, half, width = early.shape
    block = pl.BlockSpec((tokens, width), lambda n: (0, n))
    anywhere = pl.BlockSpec(memory_space=pl.ANY)
    return pl.pallas_call(
        forward_kernel,
        out_shape=[jax.ShapeDtypeStruct((tokens, columns), jnp.bfloat16)] * 3,
        grid=(columns // width,),
        in_specs=[pl.BlockSpec(rows.shape, lambda n: (0, 0)), anywhere, anywhere],
        out_specs=[block] * 3,
        scratch_shapes=[
            pltpu.VMEM((2, 2, bands, tiles, 2, half, width), jnp.bfloat16),
            pltpu.SemaphoreType.DMA((2, 2, 2)),
        ],
        compiler_params=pltpu.CompilerParams(vmem_limit_bytes=48 * 2**20),
        cost_estimate=pl.CostEstimate(
            flops=tokens * depth * columns // 8, bytes_accessed=2 * rows.size, transcendentals=0
        ),
    )(rows, early, late)


def backward_kernel(top_ref, gate_ref, up_ref, act_ref, early, late, late_down, *refs):
    dgate_ref, dup_ref = refs[:2]
    pieces, branch_pieces = refs[2:6], refs[6:10]
    weights, downs, total, branch, done, down_done = refs[10:]
    step, steps = pl.program_id(0), pl.num_programs(0)
    slot = step % 2
    strips, width = downs.shape[1], downs.shape[-1]

    def down_copies(at_step, at_slot):
        wanted = pl.ds(2 * steps, strips)
        return strip_copies(
            early.at[at_step, wanted], late_down.at[at_step], downs.at[at_slot], down_done.at[at_slot]
        )

    def copies(number, at_step, at_slot):
        strip = number * steps + at_step
        return strip_copies(
            early.at[:, strip], late.at[:, strip], weights.at[number, at_slot], done.at[number, at_slot]
        )

    def fetch(at_step, at_slot):
        for copy in down_copies(at_step, at_slot):
            copy.start()
        for number in range(2):
            for copy in copies(number, at_step, at_slot):
                copy.start()

    @pl.when(step == 0)
    def _():
        fetch(0, 0)
        total[...] = jnp.zeros_like(total)
        branch[...] = jnp.zeros_like(branch)

    @pl.when(step + 1 < steps)
    def _():
        fetch(step + 1, 1 - slot)

    for copy in down_copies(step, slot):
        copy.wait()
    for number in range(2):
        for copy in copies(number, step, slot):
            copy.wait()
    gate_weight, up_weight = (weights[number, slot].reshape(-1, width) for number in range(2))
    chunk = min(4 * BLK, top_ref.shape[0])
    for first in range(0, top_ref.shape[0], chunk):
        rows = slice(first, first + chunk)
        grad_act = 0.0
        for strip in range(strips):
            lanes = slice(strip * width, (strip + 1) * width)
            down = downs[slot, strip].reshape(-1, width)
            grad_act = grad_act + over_last(top_ref[rows, lanes], down)
            branch[rows, lanes] += jnp.dot(act_ref[rows], down, preferred_element_type=jnp.float32)
        gate = gate_ref[rows].astype(jnp.float32)
        up = up_ref[rows].astype(jnp.float32)
        sigmoid_gate = jax.nn.sigmoid(gate)
        grad_gate = grad_act * up * sigmoid_gate * (1.0 + gate * (1.0 - sigmoid_gate))
        grad_gate = grad_gate.astype(jnp.bfloat16)
        grad_up = (grad_act * (gate * sigmoid_gate)).astype(jnp.bfloat16)
        dgate_ref[rows] = grad_gate
        dup_ref[rows] = grad_up
        total[rows] += over_last(grad_gate, gate_weight) + over_last(grad_up, up_weight)

    @pl.when(step == steps - 1)
    def _():
        rows = total.shape[0] // 4
        for entry in range(4):
            part = slice(entry * rows, (entry + 1) * rows)
            write_pieces(entry, slice(0, rows), total[part], pieces)
            write_pieces(entry, slice(0, rows), branch[part], branch_pieces)


def backward_products(top, gate, up, act, early, late, late_down):
    tokens, depth = top.shape
    columns = gate.shape[1]
    bands, _, tiles, half, width = early.shape
    strips = depth // width
    block = pl.BlockSpec((tokens, width), lambda n: (0, n))
    anywhere = pl.BlockSpec(memory_space=pl.ANY)
    piece = jax.ShapeDtypeStruct((2, tokens // 4, depth // 2), jnp.bfloat16)
    grads = jax.ShapeDtypeStruct((tokens, columns), jnp.bfloat16)
    outs = pl.pallas_call(
        backward_kernel,
        out_shape=[grads] * 2 + [piece] * 8,
        grid=(columns // width,),
        in_specs=[pl.BlockSpec(top.shape, lambda n: (0, 0))] + [block] * 3 + [anywhere] * 3,
        out_specs=[block] * 2 + [pl.BlockSpec(piece.shape, lambda n: (0, 0, 0))] * 8,
        scratch_shapes=[
            pltpu.VMEM((2, 2, bands, tiles, 2, half, width), jnp.bfloat16),
            pltpu.VMEM((2, strips, tiles, 2, half, width), jnp.bfloat16),
            pltpu.VMEM((tokens, depth), jnp.float32),
            pltpu.VMEM((tokens, depth), jnp.float32),
            pltpu.SemaphoreType.DMA((2, 2, 2)),
            pltpu.SemaphoreType.DMA((2, 2)),
        ],
        compiler_params=pltpu.CompilerParams(vmem_limit_bytes=60 * 2**20),
        cost_estimate=pl.CostEstimate(
            flops=8 * tokens * depth * columns, bytes_accessed=8 * columns * depth, transcendentals=0
        ),
    )(top, gate, up, act, early, late, late_down)
    return outs[0], outs[1], outs[2:6], outs[6:10]


def rope_kernel(q_width, kv_width, x_ref, cos_ref, sin_ref, *outs):
    width = x_ref.shape[-1]
    for start in range(0, width, BLK):
        values = x_ref[0, :, start : start + BLK]
        first, turned = half_turn(values)
        sines = sin_ref[0]
        turned_rows = values * cos_ref[0] + turned * jnp.where(first, -sines, sines)
        if start + BLK > q_width + kv_width:
            column = lax.broadcasted_iota(jnp.int32, values.shape, 1) + start
            turned_rows = jnp.where(column >= q_width + kv_width, values, turned_rows)
        if start < q_width:
            outs[0][0, :, start : start + BLK] = (turned_rows * HD ** (-0.5)).astype(jnp.bfloat16)
        else:
            outs[-1][0, :, start - q_width : start - q_width + BLK] = turned_rows.astype(jnp.bfloat16)


def rope_rows(inner, rows, row_block, q_width, kv_width, cosines, sines, with_queries=True):
    seqs, _, width = inner.shape
    shared = cosines.shape[0] == 1
    table = pl.BlockSpec((1, rows, BLK), lambda s: (0 if shared else s, 0, 0))
    widths = [q_width, 2 * kv_width]
    column_block = 0
    if not with_queries:
        width, column_block = 2 * kv_width, q_width // (2 * kv_width)
        widths, q_width = widths[1:], 0
    return pl.pallas_call(
        functools.partial(rope_kernel, q_width, kv_width),
        out_shape=[jax.ShapeDtypeStruct((seqs, rows, w), jnp.bfloat16) for w in widths],
        grid=(seqs,),
        in_specs=[pl.BlockSpec((1, rows, width), lambda s: (s, row_block, column_block)), table, table],
        out_specs=[pl.BlockSpec((1, rows, w), lambda s: (s, 0, 0)) for w in widths],
        cost_estimate=pl.CostEstimate(
            flops=6 * seqs * rows * width, bytes_accessed=6 * seqs * rows * width, transcendentals=0
        ),
    )(inner, cosines, sines)


def fill_bias(band_ref, gpos_ref, bias_ref, rows, window_len):
    band = band_ref[0]

    @pl.when(pl.program_id(0) == 0)
    def _():
        key = lax.broadcasted_iota(jnp.int32, (window_len, rows), 0) + (
            band * rows - (window_len - rows)
        )
        query = lax.broadcasted_iota(jnp.int32, (window_len, rows), 1) + band * rows
        inside = (key > query - WINDOW) & (key <= query) & (key >= 0)
        bias_ref[:window_len] = jnp.where(inside, 0.0, masked_value)

    glob_total = gpos_ref.shape[1]
    query = lax.broadcasted_iota(jnp.int32, (glob_total, rows), 1) + (band * rows - WINDOW)
    spot = jnp.broadcast_to(gpos_ref[0][:, :1], (glob_total, rows))
    bias_ref[window_len:] = jnp.where(spot <= query.astype(jnp.float32), 0.0, masked_value)


def over_last(left, right):
    return lax.dot_general(left, right, (((1,), (1,)), ((), ())), preferred_element_type=jnp.float32)


def over_first(left, right):
    return lax.dot_general(left, right, (((0,), (0,)), ((), ())), preferred_element_type=jnp.float32)


def attend_kernel(block_total, band_ref, gpos_ref, q_ref, *refs):
    blocks, (out_ref, lse_ref, bias_ref) = refs[:block_total], refs[block_total:]
    rows, q_width = q_ref.shape[1:]
    kv_width = blocks[0].shape[2] // 2
    heads, group = q_width // HD, q_width // kv_width
    window_len = rows * (block_total - 1)
    fill_bias(band_ref, gpos_ref, bias_ref, rows, window_len)
    starts = [rows * number for number in range(block_total)]
    pending = []
    for head in range(heads):
        left = head // group * HD
        queries = q_ref[0, :, head * HD : (head + 1) * HD]
        scores = [
            over_last(block[0, :, left : left + HD], queries)
            + bias_ref[start : start + block.shape[1]]
            for block, start in zip(blocks, starts)
        ]
        top = functools.reduce(jnp.maximum, [jnp.max(part, 0, keepdims=True) for part in scores])
        total = 0.0
        mixed = 0.0
        for block, part in zip(blocks, scores):
            weights = jnp.exp(part - top)
            total = total + jnp.sum(weights, 0, keepdims=True)
            mixed = mixed + over_first(
                block[0, :, kv_width + left : kv_width + left + HD], weights.astype(jnp.bfloat16)
            )
        lse_ref[0, head : head + 1, :] = top + jnp.log(total)
        pending.append(mixed / total)
        if len(pending) * HD == BLK or head == heads - 1:
            stop = (head + 1) * HD
            both = jnp.concatenate(pending, 0).T
            out_ref[0, :, stop - both.shape[1] : stop] = both.astype(jnp.bfloat16)
            pending = []


def attend(band, gpos, queries, blocks):
    seqs, rows, q_width = queries.shape
    heads = q_width // HD
    key_total = sum(block.shape[1] for block in blocks)

    def whole(array):
        return pl.BlockSpec((1,) + array.shape[1:], lambda s, *_: (s, 0, 0))

    out_shape = [
        jax.ShapeDtypeStruct((seqs, rows, q_width), jnp.bfloat16),
        jax.ShapeDtypeStruct((seqs, heads, rows), jnp.float32),
    ]
    return pl.pallas_call(
        functools.partial(attend_kernel, len(blocks)),
        out_shape=out_shape,
        grid_spec=pltpu.PrefetchScalarGridSpec(
            num_scalar_prefetch=1,
            grid=(seqs,),
            in_specs=[whole(array) for array in (gpos, queries, *blocks)],
            out_specs=[whole(array) for array in out_shape],
            scratch_shapes=[pltpu.VMEM((key_total, rows), jnp.float32)],
        ),
        compiler_params=pltpu.CompilerParams(vmem_limit_bytes=48 * 2**20),
        cost_estimate=pl.CostEstimate(
            flops=16 * seqs * heads * rows * key_total * HD,
            bytes_accessed=4 * queries.size,
            transcendentals=seqs * heads * rows * key_total,
        ),
    )(band, gpos, queries, *blocks)


def attend_back_kernel(block_total, band_ref, gpos_ref, cos_ref, sin_ref, q_ref, grad_ref, lse_ref, *refs):
    blocks = refs[:block_total]
    dq_ref = refs[block_total]
    out_refs = refs[block_total + 1 : 2 * block_total + 1]
    bias_ref = refs[-1]
    rows, q_width = q_ref.shape[1:]
    kv_width = blocks[0].shape[2] // 2
    heads, group = q_width // HD, q_width // kv_width
    window_len = rows * (block_total - 1)
    fill_bias(band_ref, gpos_ref, bias_ref, rows, window_len)
    starts = [rows * number for number in range(block_total)]
    pending = []
    for kv_head in range(kv_width // HD):
        left = kv_head * HD
        key_sums = [0.0] * block_total
        value_sums = [0.0] * block_total
        for head in range(kv_head * group, (kv_head + 1) * group):
            queries = q_ref[0, :, head * HD : (head + 1) * HD]
            grads = grad_ref[0, :, head * HD : (head + 1) * HD]
            lse = lse_ref[0, head : head + 1, :]
            soft, soft_grads = [], []
            inner = 0.0
            for number, (block, start) in enumerate(zip(blocks, starts)):
                part = over_last(block[0, :, left : left + HD], queries)
                part = jnp.exp(part + bias_ref[start : start + block.shape[1]] - lse)
                slope = over_last(block[0, :, kv_width + left : kv_width + left + HD], grads)
                inner = inner + jnp.sum(part * slope, 0, keepdims=True)
                soft.append(part)
                soft_grads.append(slope)
            turned = 0.0
            for number, block in enumerate(blocks):
                score_grads = (soft[number] * (soft_grads[number] - inner)).astype(jnp.bfloat16)
                value_sums[number] = value_sums[number] + jnp.dot(
                    soft[number].astype(jnp.bfloat16), grads, preferred_element_type=jnp.float32
                )
                key_sums[number] = key_sums[number] + jnp.dot(
                    score_grads, queries, preferred_element_type=jnp.float32
                )
                turned = turned + over_first(block[0, :, left : left + HD], score_grads)
            pending.append(turned)
            if len(pending) * HD == BLK or head == heads - 1:
                stop = (head + 1) * HD
                both = jnp.concatenate(pending, 0).T * HD ** (-0.5)
                pending = []
                first, other = half_turn(both * sin_ref[0])
                both = both * cos_ref[0] + jnp.where(first, other, -other)
                dq_ref[0, :, stop - both.shape[1] : stop] = both.astype(jnp.bfloat16)
        for number, out_ref in enumerate(out_refs):
            out_ref[0, :, left : left + HD] = key_sums[number].astype(out_ref.dtype)
            out_ref[0, :, kv_width + left : kv_width + left + HD] = value_sums[number].astype(
                out_ref.dtype
            )


def attend_back(band, gpos, cosines, sines, queries, grads, lse, blocks):
    seqs, rows, q_width = queries.shape
    heads = q_width // HD
    key_total = sum(block.shape[1] for block in blocks)

    def whole(array):
        return pl.BlockSpec((1,) + array.shape[1:], lambda s, *_: (s, 0, 0))

    table = pl.BlockSpec((1, rows, BLK), lambda s, *_: (0, 0, 0))
    out_shape = [jax.ShapeDtypeStruct(queries.shape, jnp.bfloat16)]
    for number, block in enumerate(blocks):
        own = number == len(blocks) - 2
        out_shape.append(jax.ShapeDtypeStruct(block.shape, jnp.float32 if own else jnp.bfloat16))
    return pl.pallas_call(
        functools.partial(attend_back_kernel, len(blocks)),
        out_shape=out_shape,
        grid_spec=pltpu.PrefetchScalarGridSpec(
            num_scalar_prefetch=1,
            grid=(seqs,),
            in_specs=[whole(gpos), table, table]
            + [whole(array) for array in (queries, grads, lse, *blocks)],
            out_specs=[whole(array) for array in out_shape],
            scratch_shapes=[pltpu.VMEM((key_total, rows), jnp.float32)],
        ),
        compiler_params=pltpu.CompilerParams(vmem_limit_bytes=48 * 2**20),
        cost_estimate=pl.CostEstimate(
            flops=40 * seqs * heads * rows * key_total * HD,
            bytes_accessed=8 * queries.size,
            transcendentals=seqs * heads * rows * key_total,
        ),
    )(band, gpos, cosines, sines, queries, grads, lse, *blocks)


def join_kernel(q_width, kv_width, dq_ref, own_ref, pick_ref, glob_ref, cos_ref, sin_ref, *refs):
    back_refs, out_ref = refs[:-1], refs[-1]
    out_ref[0, :, :q_width] = dq_ref[0]
    picked = lax.dot_general(
        pick_ref[0].astype(jnp.float32),
        glob_ref[0],
        (((0,), (0,)), ((), ())),
        precision=lax.Precision.HIGHEST,
        preferred_element_type=jnp.float32,
    )
    for start in range(0, 2 * kv_width, BLK):
        lanes = slice(start, start + BLK)
        total = own_ref[0, :, lanes] + picked[:, lanes]
        for back_ref in back_refs:
            total = total + back_ref[0, :, lanes].astype(jnp.float32)
        first, other = half_turn(total * sin_ref[0])
        turned = total * cos_ref[0] + jnp.where(first, other, -other)
        column = lax.broadcasted_iota(jnp.int32, total.shape, 1) + start
        turned = jnp.where(column >= kv_width, total, turned)
        out_ref[0, :, q_width + start : q_width + start + BLK] = turned.astype(jnp.bfloat16)


def join_grads(dq, own, picks, globs, cosines, sines, backs):
    seqs, rows, q_width = dq.shape
    kv_width = own.shape[2] // 2

    def whole(array):
        return pl.BlockSpec((1,) + array.shape[1:], lambda s: (s, 0, 0))

    table = pl.BlockSpec((1, rows, BLK), lambda s: (0, 0, 0))
    out_shape = jax.ShapeDtypeStruct((seqs, rows, q_width + 2 * kv_width), jnp.bfloat16)
    return pl.pallas_call(
        functools.partial(join_kernel, q_width, kv_width),
        out_shape=out_shape,
        grid=(seqs,),
        in_specs=[whole(dq), whole(own), whole(picks), whole(globs), table, table]
        + [whole(back) for back in backs],
        out_specs=whole(out_shape),
        cost_estimate=pl.CostEstimate(
            flops=20 * own.size, bytes_accessed=4 * dq.size + 12 * own.size, transcendentals=0
        ),
    )(dq, own, picks, globs, cosines, sines, *backs)


def adam_kernel(batch, meta, rates, *refs):
    master_ref, first_ref, second_ref, left_ref, right_ref = refs[:5]
    sources = refs[5:-6]
    new_first_ref, new_second_ref, new_master_ref, copy_ref, tiles, arrived = refs[-6:]
    step, steps = pl.program_id(0), pl.num_programs(0)
    slot = step % 2

    def fetch(at_step, at_slot):
        for place in range(batch):
            tile = at_step * batch + place
            for number, source in enumerate(sources):

                @pl.when(meta[0, tile] == number)
                def _(source=source, tile=tile, place=place):
                    top = pl.multiple_of(meta[2, tile], BLK)
                    left = pl.multiple_of(meta[3, tile], BLK)
                    pltpu.make_async_copy(
                        source.at[meta[1, tile], pl.ds(top, BLK), pl.ds(left, BLK)],
                        tiles.at[at_slot, place],
                        arrived.at[at_slot],
                    ).start()

    @pl.when(step == 0)
    def _():
        fetch(0, 0)

    @pl.when(step + 1 < steps)
    def _():
        fetch(step + 1, 1 - slot)

    pltpu.make_async_copy(tiles.at[slot], tiles.at[slot], arrived.at[slot]).wait()
    places = range(batch)
    lefts = [left_ref[place].astype(jnp.bfloat16) for place in places]
    rights = [right_ref[place].astype(jnp.bfloat16) for place in places]
    turned = [over_first(lefts[place], tiles[slot, place]).astype(jnp.bfloat16) for place in places]
    rotated = [
        jnp.dot(turned[place], rights[place], preferred_element_type=jnp.float32) for place in places
    ]
    directions = []
    for place in places:
        new_first = beta_one * first_ref[place] + (1.0 - beta_one) * rotated[place]
        new_second = beta_two * second_ref[place] + (1.0 - beta_two) * rotated[place] * rotated[place]
        direction = (new_first * (1.0 / (1.0 - beta_one**STEP))) / (
            jnp.sqrt(new_second * (1.0 / (1.0 - beta_two**STEP))) + adam_eps
        )
        new_first_ref[place] = new_first
        new_second_ref[place] = new_second
        directions.append(direction.astype(jnp.bfloat16))
    updates = [
        jnp.dot(lefts[place], directions[place], preferred_element_type=jnp.float32) for place in places
    ]
    updates = [over_last(updates[place].astype(jnp.bfloat16), rights[place]) for place in places]
    for place in places:
        old = master_ref[place]
        new_master = old - rates[step * batch + place] * (updates[place] + weight_decay * old)
        new_master_ref[place] = new_master
        copy_ref[place] = new_master.astype(jnp.bfloat16)


def adam(meta, rates, state, sources):
    count = state[0].shape[0]
    batch = max(size for size in range(1, 33) if count % size == 0)
    block = pl.BlockSpec((batch, BLK, BLK), lambda s, *_: (s, 0, 0))
    anywhere = pl.BlockSpec(memory_space=pl.ANY)
    shape = (count, BLK, BLK)
    return pl.pallas_call(
        functools.partial(adam_kernel, batch),
        out_shape=[jax.ShapeDtypeStruct(shape, jnp.float32)] * 3
        + [jax.ShapeDtypeStruct(shape, jnp.bfloat16)],
        grid_spec=pltpu.PrefetchScalarGridSpec(
            num_scalar_prefetch=2,
            grid=(count // batch,),
            in_specs=[block] * 5 + [anywhere] * len(sources),
            out_specs=[block] * 4,
            scratch_shapes=[
                pltpu.VMEM((2, batch, BLK, BLK), jnp.bfloat16),
                pltpu.SemaphoreType.DMA((2,)),
            ],
        ),
        compiler_params=pltpu.CompilerParams(vmem_limit_bytes=56 * 2**20),
        cost_estimate=pl.CostEstimate(
            flops=8 * count * BLK**3, bytes_accessed=36 * count * BLK**2, transcendentals=0
        ),
    )(meta, rates, *state, *sources)


def per_device(
    block_input,
    cotangent,
    glob_select,
    assignment,
    master,
    first_moment,
    second_moment,
    left_basis,
    right_basis,
    gains,
    gain_first,
    gain_second,
):
    band_total = lax.axis_size("fsdp")
    rep_total = lax.axis_size("rep")
    place = lax.axis_index("rep")
    band = lax.axis_index("fsdp")
    heads = H // rep_total
    kv_heads = KVH // rep_total
    q_width = heads * HD
    kv_width = kv_heads * HD
    tok_count = block_input.shape[1]
    own_count = master.shape[1]
    tile_total = own_count * rep_total
    aligned = square() and whole_tiles(band_total, rep_total)
    tile_order = assignment[0]

    residual = block_input[0].astype(jnp.float32)
    grad_top = cotangent[0]
    position = band * tok_count + jnp.arange(tok_count, dtype=jnp.int32)
    cosine_table, sine_table = rope_tables(position)
    wide_cosine = jnp.concatenate([cosine_table, cosine_table], 1)[None]
    wide_sine = jnp.concatenate([sine_table, sine_table], 1)[None]
    scale_one = lax.rsqrt(jnp.mean(residual * residual, -1, keepdims=True) + norm_eps)
    normed_one = (residual * scale_one * gains[0]).astype(jnp.bfloat16)
    pick_rows = glob_select[0]
    glob_total = pick_rows.shape[0]
    selector = pick_rows.astype(jnp.bfloat16)
    glob_pos_part = jnp.sum(pick_rows * position[None, :], 1)
    digits = jnp.concatenate([glob_pos_part // 256, glob_pos_part % 256]).astype(jnp.bfloat16)
    digits = jnp.pad(digits[None], ((0, 7), (0, D - 2 * glob_total)))
    glob_rows = jnp.dot(selector, normed_one, preferred_element_type=jnp.float32).astype(jnp.bfloat16)
    glob_rows = add_all(jnp.concatenate([glob_rows, digits], 0), "fsdp").astype(jnp.bfloat16)
    packed = [normed_one, glob_rows, selector.reshape(-1, D)]
    packed = jnp.concatenate(packed, 0)
    packed = jnp.pad(packed, ((0, -packed.shape[0] % 32), (0, 0)))

    def over_bands(slice_rows):
        return lax.all_gather(slice_rows, "fsdp", axis=0, tiled=True)

    if aligned:
        half = BLK // 2
        low, high = (master[0, :, rows].astype(jnp.bfloat16) for rows in (slice(0, half), slice(half, BLK)))
        layout = slice_layout(band_total, rep_total)
        attn_layout = jnp.asarray(np.concatenate(layout[:4], 2))
        wanted = jnp.take(tile_order, by_place(attn_layout).reshape(-1), mode="clip")
        meta = jnp.stack([wanted // own_count == place, wanted % own_count], 0).astype(jnp.int32)
        attn_part = place_tiles(low, high, meta, *attn_layout.shape)
        attn_part = rep_scatter(attn_part).astype(jnp.bfloat16)
        low, attn_part = lax.optimization_barrier((low, attn_part))
        slots = square_pieces(low)
        attn = over_bands(attn_part)
        grids = [lax.dynamic_index_in_dim(jnp.asarray(grid), place, 0, False) for grid in layout]

        def find(wanted):
            wanted = jnp.take(tile_order, jnp.concatenate([grid.reshape(-1) for grid in wanted]), mode="clip")
            entry, row = (wanted // own_count) ^ place, wanted % own_count
            cut = own_count // 2
            high = (entry == 3) & (row >= cut)
            found = jnp.stack([jnp.where(high, 4, entry), jnp.where(high, row - cut, row)], 0)
            return found.astype(jnp.int32)

        all_grid = jnp.concatenate(grids[4:], 1)
        (first_part,) = gather_strips(slots, find([all_grid]), [all_grid.shape])
        packed, first_part, attn = lax.optimization_barrier((packed, first_part, attn))
        early = over_bands(first_part)
    packed_all = rep_gather(packed)
    if aligned:
        packed_all, high = lax.optimization_barrier((packed_all, high))
        later_slots = square_pieces(high)
    normed_one_all = packed_all[:, :tok_count].reshape(-1, D)
    at = tok_count + glob_total
    glob_digits = packed_all[:, at, : 2 * glob_total].astype(jnp.float32)
    glob_place = glob_digits[:, :glob_total] * 256.0 + glob_digits[:, glob_total:]
    at += 8
    selector_all = packed_all[:, at : at + selector.size // D].reshape(rep_total, glob_total, tok_count)

    if aligned:
        in_width = q_width + 2 * kv_width
        w_inner, w_output = attn[:, :in_width], attn[:, in_width:]
    else:
        slots = lax.all_gather(master[0].astype(jnp.bfloat16), "rep", axis=0, tiled=True)
        tiles = jnp.take(slots, tile_order, axis=0, mode="clip")
        slices = cut_slices(band_matrices(tiles, band_total), band_total, rep_total)
        w_inner = over_bands(jnp.concatenate(slices[0:3], 1))
        w_output = over_bands(slices[3])
        w_gate = over_bands(slices[4])
        w_up = over_bands(slices[5])
        w_down = over_bands(slices[6])

    w_output = by_place(w_output.reshape(rep_total, q_width, -1)).reshape(D, -1)

    def mul(rows, weight):
        return jnp.dot(rows, weight, preferred_element_type=jnp.float32)

    def mul_back(rows, weight):
        return lax.dot_general(rows, weight, (((1,), (1,)), ((), ())), preferred_element_type=jnp.float32)

    def weight_grad(rows, grad_rows):
        return lax.dot_general(
            rows, grad_rows, (((0,), (0,)), ((), ())), preferred_element_type=jnp.float32
        ).astype(jnp.bfloat16)

    def own_sum(partial):
        return rep_scatter(partial.astype(jnp.bfloat16).reshape(rep_total, tok_count, D))

    inner_rows = mul(packed_all.reshape(-1, D), w_inner).reshape(rep_total, -1, w_inner.shape[1])
    packed_all, normed_one_all = lax.optimization_barrier((packed_all, normed_one_all))
    queries, own_pairs = rope_rows(inner_rows, tok_count, 0, q_width, kv_width, wide_cosine, wide_sine)
    glob_cosine, glob_sine = rope_tables(glob_place.reshape(-1))
    glob_cosine = jnp.concatenate([glob_cosine, glob_cosine], 1).reshape(rep_total, glob_total, -1)
    glob_sine = jnp.concatenate([glob_sine, glob_sine], 1).reshape(rep_total, glob_total, -1)
    (glob_pairs,) = rope_rows(
        inner_rows, glob_total, tok_count // glob_total, q_width, kv_width, glob_cosine, glob_sine, False
    )
    back_count = (WINDOW + tok_count - 2) // tok_count
    odd = band % 2 == 1
    by_chip = back_count == 2 and band_total % 2 == 0
    if by_chip:
        two_back = shifted(own_pairs, "fsdp", 2)
        pair_blocks = [two_back, to_core(jnp.where(odd, two_back, own_pairs))]
    else:
        pair_blocks = [shifted(own_pairs, "fsdp", distance) for distance in range(back_count, 0, -1)]
    pair_blocks = pair_blocks + [own_pairs, glob_pairs]
    glob_spots = jnp.broadcast_to(glob_place[:, :, None], (rep_total, glob_total, BLK))
    band_number = band.astype(jnp.int32).reshape(1)
    attended_low, lse = attend(band_number, glob_spots, queries, pair_blocks)
    if aligned:
        *later_slots, attended_low, early = lax.optimization_barrier((*later_slots, attended_low, early))
        last_grid = jnp.concatenate(grids[4:6], 1)
        last_part, down_part = gather_strips(
            later_slots, find([last_grid, grids[6]]), [last_grid.shape, grids[6].shape]
        )

        def by_strips(gathered):
            return gathered.reshape(band_total, -1, all_grid.shape[0], half, gathered.shape[-1])

        early, late, late_down = by_strips(early), by_strips(over_bands(last_part)), by_strips(over_bands(down_part))
    attended_all = rep_features(attended_low).reshape(-1, D)
    columns = mul(attended_all, w_output).astype(jnp.bfloat16).reshape(rep_total, tok_count, -1)
    branch = by_place(rep_exchange(columns)).transpose(1, 0, 2).reshape(tok_count, D)
    middle = residual + branch.astype(jnp.float32)
    scale_two = lax.rsqrt(jnp.mean(middle * middle, -1, keepdims=True) + norm_eps)
    normed_two = (middle * scale_two * gains[1]).astype(jnp.bfloat16)
    normed_two_all = rep_gather(normed_two).reshape(-1, D)
    normed_two_all, grad_top_now = lax.optimization_barrier((normed_two_all, grad_top))
    top_first = gather_first(grad_top_now)

    if aligned:
        gate_rows, up_rows, activation = forward_products(normed_two_all, early, late, FF // rep_total)
        top_first, activation = after(top_first, activation)
        grad_top_all = gather_join(gather_second(top_first)).reshape(-1, D)
        g_down = weight_grad(activation, grad_top_all)
        grad_top_all, g_down = lax.optimization_barrier((grad_top_all, g_down))
        grad_gate, grad_up, pieces, branch_pieces = backward_products(
            grad_top_all, gate_rows, up_rows, activation, early, late, late_down
        )
        normed_first = sum_first(pieces)
        normed_first, g_gate = after(normed_first, weight_grad(normed_two_all, grad_gate))
        grad_normed_two = sum_second(normed_first)
    else:
        gate_rows = mul(normed_two_all, w_gate)
        up_rows = mul(normed_two_all, w_up)
        sigmoid_gate = jax.nn.sigmoid(gate_rows)
        silu_gate = gate_rows * sigmoid_gate
        activation = (silu_gate * up_rows).astype(jnp.bfloat16)
        grad_top_all = gather_join(gather_second(top_first)).reshape(-1, D)
        g_down = weight_grad(activation, grad_top_all)
        grad_act = mul_back(grad_top_all, w_down)
        grad_gate = (
            grad_act * up_rows * sigmoid_gate * (1.0 + gate_rows * (1.0 - sigmoid_gate))
        ).astype(jnp.bfloat16)
        grad_up = (grad_act * silu_gate).astype(jnp.bfloat16)
        grad_normed_two = own_sum(mul_back(grad_gate, w_gate) + mul_back(grad_up, w_up))
        branch_pieces = (mul(activation, w_down),)
        g_gate = weight_grad(normed_two_all, grad_gate)
    grad_normed_two, g_gate = lax.optimization_barrier((grad_normed_two, g_gate))

    def over_tokens(partial):
        return lax.psum_scatter(partial, "fsdp", scatter_dimension=0, tiled=True)

    s_down = over_tokens(g_down)
    s_gate = over_tokens(g_gate)

    grad_middle = grad_top.astype(jnp.float32) + norm_back(middle, scale_two, gains[1], grad_normed_two)
    grad_parts = grad_middle.astype(jnp.bfloat16).reshape(tok_count, rep_total, -1).transpose(1, 0, 2)
    grad_columns = rep_exchange(by_place(grad_parts)).reshape(rep_total * tok_count, -1)
    grad_columns, grad_up = lax.optimization_barrier((grad_columns, grad_up))
    grad_attended, g_up = rep_features_sum(
        grad_columns.reshape(rep_total, tok_count, -1),
        w_output,
        lambda: weight_grad(normed_two_all, grad_up),
    )
    grad_attended = grad_attended.astype(jnp.bfloat16)
    (s_down, g_up), grad_attended = after((s_down, g_up), grad_attended)
    down_first = gather_first(s_down)
    grad_queries, *grad_blocks = attend_back(
        band_number, glob_spots, wide_cosine, wide_sine, queries, grad_attended, lse, pair_blocks
    )
    down_first, *grad_blocks = after(down_first, *grad_blocks)
    down_second = gather_second(down_first)
    branch_pieces, *grad_blocks = after(tuple(branch_pieces), *grad_blocks)
    branch_first = sum_first(branch_pieces) if aligned else (own_sum(branch_pieces[0]),)
    if by_chip:
        came = to_core(jnp.concatenate([grad_blocks[1], grad_blocks[-1]], 1))
        came, glob_came = came[:, :tok_count], came[:, tok_count:]
        total = grad_blocks[0].astype(jnp.float32) + came.astype(jnp.float32)
        sent = jnp.where(odd, total.astype(jnp.bfloat16), grad_blocks[0])
        returned = [shifted(sent, "fsdp", -2), jnp.where(odd, jnp.zeros_like(came), came)]
    else:
        returned = [
            shifted(grad_blocks[back_count - distance], "fsdp", -distance)
            for distance in range(1, back_count + 1)
        ]
    if by_chip:
        glob_both = grad_blocks[-1].astype(jnp.float32) + glob_came.astype(jnp.float32)
        glob_grads = add_all(glob_both.astype(jnp.bfloat16), "fsdp", 2)
    else:
        glob_grads = add_all(grad_blocks[-1], "fsdp")
    branch_first, g_up, glob_grads, s_gate, *returned = lax.optimization_barrier(
        (branch_first, g_up, glob_grads, s_gate, *returned)
    )
    s_up = over_tokens(g_up)
    gate_first = gather_first(s_gate)
    block_out = middle + (sum_second(branch_first) if aligned else branch_first[0])
    grad_inner = join_grads(
        grad_queries, grad_blocks[-2], selector_all, glob_grads, wide_cosine, wide_sine, returned
    ).reshape(-1, q_width + 2 * kv_width)
    grad_normed_parts = mul_back(grad_inner, w_inner).astype(jnp.bfloat16).reshape(rep_total, tok_count, D)
    if square():
        normed_first = sum_first(split_pieces(grad_normed_parts))
    else:
        normed_first = (rep_scatter(grad_normed_parts),)
    grad_inner, grad_normed_parts = lax.optimization_barrier((grad_inner, grad_normed_parts))
    g_inner = weight_grad(normed_one_all, grad_inner)
    attended_all, g_inner = lax.optimization_barrier((attended_all, g_inner))
    g_output = weight_grad(attended_all, grad_columns)
    g_output = by_place(g_output.reshape(rep_total, q_width, -1)).reshape(D, -1)
    g_attn = with_layout_constraint(jnp.concatenate([g_inner, g_output], 1), Layout((0, 1)))
    gate_first, block_out, down_second, *normed_first = after(gate_first, block_out, down_second, *normed_first)
    s_down = gather_join(down_second)
    gate_second = gather_second(gate_first)
    grad_normed_one = sum_second(normed_first) if square() else normed_first[0]
    gate_second, s_up, g_attn, grad_normed_one = after(gate_second, s_up, g_attn, grad_normed_one)
    s_attn = over_tokens(g_attn)
    s_gate = gather_join(gate_second)
    up_first = gather_first(s_up)
    grad_input = grad_middle + norm_back(residual, scale_one, gains[0], grad_normed_one)

    gain_terms = jnp.stack(
        [
            jnp.sum(grad_normed_one * residual * scale_one, 0),
            jnp.sum(grad_normed_two * middle * scale_two, 0),
        ]
    )
    square_terms = jnp.stack(
        [jnp.sum(residual * residual), jnp.sum(middle * middle), jnp.sum(block_out * block_out)]
    )
    sums = jnp.concatenate([gain_terms.reshape(-1), square_terms])

    up_first, sums = after(up_first, sums)
    s_up = gather_join(gather_second(up_first))
    sums = add_all(add_all(sums, "rep"), "fsdp")
    sums, s_attn, s_up, s_gate, s_down = lax.optimization_barrier((sums, s_attn, s_up, s_gate, s_down))
    gain_grad, square_total = sums[: 2 * D].reshape(2, D), sums[2 * D :]

    slot_ids = jnp.arange(tile_total, dtype=jnp.int32)
    inverse = jnp.sum(jnp.where(tile_order[None, :] == slot_ids[:, None], slot_ids[None, :], 0), 1)
    own_slots = place * own_count + jnp.arange(own_count, dtype=jnp.int32)
    owned_tiles = jnp.take(inverse, own_slots, mode="clip")
    if aligned:
        sources = [rep_gather(s_attn), s_gate, s_up, s_down]
        where = np.zeros((4, rep_total, tile_total), np.int32)
        first_col = 0
        for kind, grid in enumerate(layout):
            rows, cols = grid.shape[1:]
            first_col = 0 if kind >= 4 else first_col
            for there in range(rep_total):
                numbers = grid[there].reshape(-1)
                at = np.arange(rows * cols)
                where[0, :, numbers] = max(kind - 3, 0)
                where[2, :, numbers] = (at // cols * BLK)[:, None]
                where[3, :, numbers] = (at % cols * BLK + first_col)[:, None]
                for here in range(rep_total):
                    where[1, here, numbers] = here ^ there
            first_col += cols * BLK
        tile_spots = lax.dynamic_index_in_dim(jnp.asarray(where), place, 1, False)
        meta = jnp.take(tile_spots, owned_tiles, axis=1, mode="clip")
    else:
        splits = [0, q_width, q_width + kv_width, q_width + 2 * kv_width, s_attn.shape[1]]
        stacks = [rep_gather(s_attn[:, low:high]) for low, high in zip(splits, splits[1:])]
        stacks += [s_gate, s_up, s_down]
        sources = [band_tiles(join_slices(stacks, band_total, rep_total))]
        meta = jnp.stack([0 * owned_tiles, owned_tiles, 0 * owned_tiles, 0 * owned_tiles], 0)
    slot_rates = jnp.take(kind_rates(band_total), owned_tiles, mode="clip")
    new_first, new_second, new_master, master_copy = adam(
        meta,
        slot_rates,
        (master[0], first_moment[0], second_moment[0], left_basis[0], right_basis[0]),
        sources,
    )
    new_gain_first = beta_one * gain_first + (1.0 - beta_one) * gain_grad
    new_gain_second = beta_two * gain_second + (1.0 - beta_two) * gain_grad * gain_grad
    gain_step = (
        new_gain_first
        / (1.0 - beta_one**STEP)
        / (jnp.sqrt(new_gain_second / (1.0 - beta_two**STEP)) + adam_eps)
    )
    new_gains = gains - gain_rate * gain_step
    rms_stats = jnp.sqrt(square_total / (rep_total * band_total * tok_count * D))
    return (
        block_out[None],
        grad_input[None],
        new_first[None],
        new_second[None],
        new_master[None],
        master_copy[None],
        new_gain_first,
        new_gain_second,
        new_gains,
        rms_stats,
    )


def solution(mesh):
    in_specs = (
        P("rep", "fsdp", None),
        P("rep", "fsdp", None),
        P("rep", None, "fsdp"),
        P("fsdp", None),
        P("fsdp", "rep", None, None),
        P("fsdp", "rep", None, None),
        P("fsdp", "rep", None, None),
        P("fsdp", "rep", None, None),
        P("fsdp", "rep", None, None),
        P(),
        P(),
        P(),
    )
    out_specs = (
        P("rep", "fsdp", None),
        P("rep", "fsdp", None),
        P("fsdp", "rep", None, None),
        P("fsdp", "rep", None, None),
        P("fsdp", "rep", None, None),
        P("fsdp", "rep", None, None),
        P(),
        P(),
        P(),
        P(),
    )
    return jax.shard_map(
        per_device, mesh=mesh, in_specs=in_specs, out_specs=out_specs, check_vma=False
    )
```

```python
import functools

import jax
import jax.numpy as jnp
import numpy as np
from jax import lax
from jax.experimental import pallas as pl
from jax.experimental.layout import Layout, with_layout_constraint
from jax.experimental.pallas import tpu as pltpu
from jax.sharding import PartitionSpec as P

D = 2048
H = 32
KVH = 8
HD = 64
FF = 8192
WINDOW = 512
BLK = 128
STEP = 10


norm_eps = 1e-05
rope_theta = 500000.0
beta_one = 0.5
beta_two = 0.5
adam_eps = 1e-08
weight_decay = 0.1
gain_rate = 0.5
masked_value = -1e30


def matrix_shapes():
    kv_width = KVH * HD
    return [(D, D), (D, kv_width), (D, kv_width), (D, D), (D, FF), (D, FF), (FF, D)]


def kind_rates(band_total):
    rate_list = [
        D ** (-0.5),
        D ** (-0.5),
        D ** (-0.5),
        (D * 8 // WINDOW) ** (-0.5),
        D ** (-0.5),
        D ** (-0.5),
        FF ** (-0.5),
    ]
    pieces = []
    for (row_total, col_total), rate_value in zip(matrix_shapes(), rate_list):
        tile_count = row_total // band_total // BLK * (col_total // BLK)
        pieces.append(jnp.full((tile_count,), rate_value, jnp.float32))
    return jnp.concatenate(pieces)


def band_matrices(tiles, band_total):
    matrices = []
    offset = 0
    for row_total, col_total in matrix_shapes():
        band_rows = row_total // band_total
        tile_count = band_rows // BLK * (col_total // BLK)
        segment = tiles[offset : offset + tile_count].reshape(
            band_rows // BLK, col_total // BLK, BLK, BLK
        )
        matrices.append(segment.transpose(0, 2, 1, 3).reshape(band_rows, col_total))
        offset += tile_count
    return matrices


def band_tiles(matrices):
    pieces = []
    for matrix in matrices:
        row_count, col_count = matrix.shape
        segment = matrix.reshape(row_count // BLK, BLK, col_count // BLK, BLK).transpose(0, 2, 1, 3)
        pieces.append(segment.reshape(-1, BLK, BLK))
    return jnp.concatenate(pieces, 0)


def rope_tables(position):
    halves = jnp.arange(HD // 2, dtype=jnp.float32) * (2.0 / HD)
    frequency = rope_theta ** (-halves)
    angles = position.astype(jnp.float32)[:, None] * frequency[None, :]
    angles = jnp.concatenate([angles, angles], 1)
    return (jnp.cos(angles), jnp.sin(angles))


def rotate(vectors, cosine_table, sine_table):
    half_width = vectors.shape[-1] // 2
    turned = jnp.concatenate([-vectors[..., half_width:], vectors[..., :half_width]], -1)
    return vectors * cosine_table[:, None, :] + turned * sine_table[:, None, :]


def rotate_back(grad_rows, cosine_table, sine_table):
    half_width = grad_rows.shape[-1] // 2
    scaled = grad_rows * sine_table[:, None, :]
    turned = jnp.concatenate([scaled[..., half_width:], -scaled[..., :half_width]], -1)
    return grad_rows * cosine_table[:, None, :] + turned


def norm_back(values, row_scale, gain_row, grad_rows):
    weighted = grad_rows * gain_row
    return row_scale * weighted - values * row_scale**3 * jnp.mean(
        weighted * values, -1, keepdims=True
    )


def to_rep(block, distance):
    route = [(i, i ^ distance) for i in range(lax.axis_size("rep"))]
    return lax.ppermute(block, "rep", route)


def square():
    return lax.axis_size("rep") == 4


def gather_first(block):
    if not square():
        return (lax.all_gather(block, "rep", axis=0),)
    return block, to_rep(block, 1), to_rep(block, 2)


def gather_second(first):
    if not square():
        return first
    block, near, far = first
    cut = block.shape[0] // 2
    return block, near, far, to_rep(near[:cut], 2), to_rep(far[cut:], 1)


def gather_join(pieces):
    if not square():
        return pieces[0]
    return jnp.concatenate(pieces, 0).reshape((4,) + pieces[0].shape)


def square_pieces(block):
    return gather_second(gather_first(block))


def rep_gather(block):
    return gather_join(gather_second(gather_first(block)))


def after(values, *others):
    count = len(values)
    tied = lax.optimization_barrier((*values, *others))
    return tuple(tied[:count]), *tied[count:]


def rep_of(entry):
    place = lax.axis_index("rep")
    return place ^ entry if square() else entry


def rep_scatter(parts):
    if not square():
        flat = parts.reshape(-1, parts.shape[-1])
        return lax.psum_scatter(flat, "rep", scatter_dimension=0, tiled=True).astype(jnp.float32)
    return sum_pieces(*split_pieces(parts))


def split_pieces(parts):
    half = parts.shape[-1] // 2
    low, high = parts[..., :half], parts[..., half:]
    return jnp.stack([low[0], low[2]], 0), jnp.stack([low[1], low[3]], 0), high[:2], high[2:]


def sum_first(pieces):
    low_kept, low_sent, high_kept, high_sent = pieces
    parts = []
    for kept, sent, first in ((low_kept, low_sent, 1), (high_kept, high_sent, 2)):
        came = to_rep(sent, first)
        parts.append(kept[0].astype(jnp.float32) + came[0].astype(jnp.float32))
        parts.append((kept[1].astype(jnp.float32) + came[1].astype(jnp.float32)).astype(kept.dtype))
    return tuple(parts)


def sum_second(parts):
    low, low_other, high, high_other = parts
    low = low + to_rep(low_other, 2).astype(jnp.float32)
    high = high + to_rep(high_other, 1).astype(jnp.float32)
    return jnp.concatenate([low, high], -1)


def sum_pieces(*pieces):
    return sum_second(sum_first(pieces))


def add_all(value, axis, distance=1):
    size = lax.axis_size(axis)
    total = value.astype(jnp.float32)
    while distance < size:
        count = 2 if (size // distance).bit_length() % 2 == 0 else 4
        low = total.astype(value.dtype)
        others = []
        for step in range(1, count):
            route = [(i, i ^ (step * distance)) for i in range(size)]
            others.append(lax.ppermute(low, axis, route).astype(jnp.float32))
        total = total + others[0]
        if count == 4:
            total = total + (others[1] + others[2])
        distance *= count
    return total


def rep_features(block):
    if not square():
        return lax.all_gather(block, "rep", axis=2, tiled=True)
    own, near, far, low, high = square_pieces(block)
    return jnp.concatenate(
        [
            own,
            jnp.stack([near[1], near[0], near[3], near[2]], 0),
            jnp.stack([far[2], far[3], far[0], far[1]], 0),
            jnp.stack([high[1], high[0], low[1], low[0]], 0),
        ],
        2,
    )


def write_pieces(entry, rows, values, refs):
    low_kept, low_sent, high_kept, high_sent = refs
    half = low_kept.shape[-1]
    values = values.astype(jnp.bfloat16)
    (low_sent if entry % 2 else low_kept)[entry // 2, rows] = values[:, :half]
    (high_sent if entry // 2 else high_kept)[entry % 2, rows] = values[:, half:]


def swapped_kernel(x_ref, w_ref, *refs):
    reps, rows, _ = x_ref.shape
    width = w_ref.shape[0] // reps
    for entry in range(reps):
        weight = w_ref[entry * width : (entry + 1) * width]
        for there in range(reps):
            product = over_last(x_ref[there ^ entry], weight)
            write_pieces(entry, slice(there * rows, (there + 1) * rows), product, refs)


def rep_features_sum(columns, weight, meanwhile):
    reps, rows, depth = columns.shape
    width = weight.shape[0] // reps
    if square():
        pieces = pl.pallas_call(
            swapped_kernel,
            out_shape=[jax.ShapeDtypeStruct((2, reps * rows, width // 2), jnp.bfloat16)] * 4,
            compiler_params=pltpu.CompilerParams(vmem_limit_bytes=32 * 2**20),
            cost_estimate=pl.CostEstimate(
                flops=2 * reps * columns.size * width,
                bytes_accessed=10 * columns.size,
                transcendentals=0,
            ),
        )(columns, weight)
        first = sum_first(pieces)
        first, other = after(first, meanwhile())
        total = sum_second(first)
    else:
        other = meanwhile()
        product = over_last(columns.reshape(-1, depth), weight).astype(jnp.bfloat16)
        swapped = product.reshape(reps, rows, reps, width).transpose(2, 0, 1, 3)
        total = rep_scatter(swapped.reshape(reps, reps * rows, width))
    return total.reshape(reps, rows, width), other


def rep_exchange(parts):
    if not square():
        return lax.all_to_all(parts, "rep", 0, 0)
    return jnp.stack([parts[0]] + [to_rep(parts[entry], entry) for entry in (1, 2, 3)], 0)


def by_place(parts):
    entries = [rep_of(entry) for entry in range(parts.shape[0])]
    return jnp.stack([lax.dynamic_index_in_dim(parts, entry, 0, False) for entry in entries], 0)


def to_core(block):
    return lax.ppermute(block, "fsdp", [(i, i ^ 1) for i in range(lax.axis_size("fsdp"))])


def shifted(block, axis, distance):
    devices = range(lax.axis_size(axis))
    route = [(i - distance, i) for i in devices if i - distance in devices]
    return lax.ppermute(block, axis, route)


def tile_offsets(band_total):
    offsets = [0]
    for row_total, col_total in matrix_shapes():
        offsets.append(offsets[-1] + row_total // band_total // BLK * (col_total // BLK))
    return offsets


def whole_tiles(band_total, rep_total):
    return KVH * HD // rep_total % BLK == 0 and FF // band_total // rep_total % BLK == 0


def slice_layout(band_total, rep_total):
    offsets = tile_offsets(band_total)
    layout = []
    for kind, (row_total, col_total) in enumerate(matrix_shapes()):
        rows, cols = row_total // band_total // BLK, col_total // BLK
        grid = offsets[kind] + np.arange(rows * cols).reshape(rows, cols)
        if kind == 6:
            layout.append(grid.reshape(rep_total, rows // rep_total, cols))
        elif kind in (4, 5):
            cut = grid.reshape(rows, band_total, rep_total, -1).transpose(2, 0, 1, 3)
            layout.append(cut.reshape(rep_total, rows, -1))
        else:
            layout.append(grid.reshape(rows, rep_total, -1).transpose(1, 0, 2))
    return layout


def tiles_to_matrix(tiles):
    rows, cols = tiles.shape[:2]
    return tiles.transpose(0, 2, 1, 3).reshape(rows * BLK, cols * BLK)


def matrix_to_tiles(matrix):
    rows, cols = matrix.shape
    cut = matrix.reshape(rows // BLK, BLK, cols // BLK, BLK)
    return cut.transpose(0, 2, 1, 3).reshape(-1, BLK, BLK)


def cut_slices(matrices, band_total, rep_total):
    place = lax.axis_index("rep")
    slices = []
    for kind, matrix in enumerate(matrices):
        rows, cols = matrix.shape
        if kind == 6:
            slices.append(lax.dynamic_slice_in_dim(matrix, place * (rows // rep_total), rows // rep_total, 0))
        elif kind in (4, 5):
            cut = matrix.reshape(rows, band_total, rep_total, -1)
            slices.append(lax.dynamic_index_in_dim(cut, place, 2, False).reshape(rows, -1))
        else:
            slices.append(lax.dynamic_slice_in_dim(matrix, place * (cols // rep_total), cols // rep_total, 1))
    return slices


def join_slices(stacks, band_total, rep_total):
    matrices = []
    for kind, stack in enumerate(stacks):
        rows, cols = stack.shape[1:]
        if kind == 6:
            matrices.append(stack.reshape(-1, cols))
        elif kind in (4, 5):
            cut = stack.reshape(rep_total, rows, band_total, -1).transpose(1, 2, 0, 3)
            matrices.append(cut.reshape(rows, -1))
        else:
            matrices.append(stack.transpose(1, 0, 2).reshape(rows, -1))
    return matrices


def gather_kernel(grids, meta, *refs):
    source_total = len(refs) - len(grids) - 1
    sources, targets, done = refs[:source_total], refs[source_total:-1], refs[-1]
    height = sources[0].shape[1]
    start = 0
    for place, (target, (rows, cols)) in enumerate(zip(targets, grids)):

        def one(tile, carry, target=target, rows=rows, cols=cols, start=start, place=place):
            kind = meta[0, start + tile]
            row = meta[1, start + tile]
            across = tile % cols
            top = pl.multiple_of((across // 2 * rows + tile // cols) * height, height)
            left = pl.multiple_of(across % 2 * BLK, BLK)
            for number, source in enumerate(sources):

                @pl.when(kind == number)
                def _(source=source):
                    pltpu.make_async_copy(
                        source.at[row], target.at[pl.ds(top, height), pl.ds(left, BLK)], done.at[place]
                    ).start()

            return carry

        lax.fori_loop(0, rows * cols, one, 0)
        start += rows * cols
    for place, target in enumerate(targets):
        pltpu.make_async_copy(target, target, done.at[place]).wait()


def gather_strips(sources, meta, grids):
    anywhere = pl.BlockSpec(memory_space=pl.ANY)
    height = sources[0].shape[1]
    out_shape = [
        jax.ShapeDtypeStruct((cols // 2 * rows * height, 2 * BLK), jnp.bfloat16) for rows, cols in grids
    ]
    return pl.pallas_call(
        functools.partial(gather_kernel, grids),
        out_shape=out_shape,
        grid_spec=pltpu.PrefetchScalarGridSpec(
            num_scalar_prefetch=1,
            grid=(1,),
            in_specs=[anywhere] * len(sources),
            out_specs=[pl.BlockSpec(shape.shape, lambda i, *_: (0, 0)) for shape in out_shape],
            scratch_shapes=[pltpu.SemaphoreType.DMA((len(grids),))],
        ),
        compiler_params=pltpu.CompilerParams(vmem_limit_bytes=32 * 2**20),
        cost_estimate=pl.CostEstimate(
            flops=0, bytes_accessed=sum(4 * shape.size for shape in out_shape), transcendentals=0
        ),
    )(meta, *sources)


def place_kernel(entries, rows, cols, meta, low, high, out_ref, done):
    out_ref[...] = jnp.zeros_like(out_ref)
    height = low.shape[1]

    def copies(tile):
        entry, rest = tile // (rows * cols), tile % (rows * cols)
        top = rest // cols * (2 * height)
        left = pl.multiple_of(rest % cols * BLK, BLK)
        return [
            pltpu.make_async_copy(
                half.at[meta[1, tile]],
                out_ref.at[entry, pl.ds(pl.multiple_of(top + part * height, height), height), pl.ds(left, BLK)],
                done.at[part],
            )
            for part, half in enumerate((low, high))
        ]

    def begin(tile, carry):
        @pl.when(meta[0, tile] == 1)
        def _():
            for copy in copies(tile):
                copy.start()

        return carry

    def finish(tile, carry):
        @pl.when(meta[0, tile] == 1)
        def _():
            for copy in copies(tile):
                copy.wait()

        return carry

    lax.fori_loop(0, entries * rows * cols, begin, 0)
    lax.fori_loop(0, entries * rows * cols, finish, 0)


def place_tiles(low, high, meta, entries, rows, cols):
    shape = (entries, rows * BLK, cols * BLK)
    anywhere = pl.BlockSpec(memory_space=pl.ANY)
    return pl.pallas_call(
        functools.partial(place_kernel, entries, rows, cols),
        out_shape=jax.ShapeDtypeStruct(shape, jnp.bfloat16),
        grid_spec=pltpu.PrefetchScalarGridSpec(
            num_scalar_prefetch=1,
            grid=(1,),
            in_specs=[anywhere, anywhere],
            out_specs=pl.BlockSpec(shape, lambda i, *_: (0, 0, 0)),
            scratch_shapes=[pltpu.SemaphoreType.DMA((2,))],
        ),
        compiler_params=pltpu.CompilerParams(vmem_limit_bytes=32 * 2**20),
        cost_estimate=pl.CostEstimate(
            flops=0, bytes_accessed=4 * entries * rows * cols * BLK * BLK, transcendentals=0
        ),
    )(meta, low, high)


def half_turn(values):
    lane = lax.broadcasted_iota(jnp.int32, values.shape, 1)
    lanes = values.shape[1]
    first = lane % HD < HD // 2
    return first, jnp.where(
        first, pltpu.roll(values, lanes - HD // 2, 1), pltpu.roll(values, HD // 2, 1)
    )


def strip_copies(early, late, target, done):
    return [
        pltpu.make_async_copy(half, target.at[:, :, number], done.at[number])
        for number, half in enumerate((early, late))
    ]


def forward_kernel(x_ref, early, late, gate_ref, up_ref, act_ref, weights, done):
    step, steps = pl.program_id(0), pl.num_programs(0)
    slot = step % 2
    width = weights.shape[-1]

    def copies(number, at_step, at_slot):
        strip = number * steps + at_step
        return strip_copies(
            early.at[:, strip], late.at[:, strip], weights.at[number, at_slot], done.at[number, at_slot]
        )

    def fetch(at_step, at_slot):
        for number in range(2):
            for copy in copies(number, at_step, at_slot):
                copy.start()

    @pl.when(step == 0)
    def _():
        fetch(0, 0)

    @pl.when(step + 1 < steps)
    def _():
        fetch(step + 1, 1 - slot)

    for number in range(2):
        for copy in copies(number, step, slot):
            copy.wait()
    gate_weight, up_weight = (weights[number, slot].reshape(-1, width) for number in range(2))
    chunk = min(2 * BLK, x_ref.shape[0])
    for first in range(0, x_ref.shape[0], chunk):
        rows = slice(first, first + chunk)
        gate = jnp.dot(x_ref[rows], gate_weight, preferred_element_type=jnp.float32)
        up = jnp.dot(x_ref[rows], up_weight, preferred_element_type=jnp.float32)
        gate_ref[rows] = gate.astype(jnp.bfloat16)
        up_ref[rows] = up.astype(jnp.bfloat16)
        act_ref[rows] = (gate * jax.nn.sigmoid(gate) * up).astype(jnp.bfloat16)


def forward_products(rows, early, late, columns):
    tokens, depth = rows.shape
    bands, _, tiles, half, width = early.shape
    block = pl.BlockSpec((tokens, width), lambda n: (0, n))
    anywhere = pl.BlockSpec(memory_space=pl.ANY)
    return pl.pallas_call(
        forward_kernel,
        out_shape=[jax.ShapeDtypeStruct((tokens, columns), jnp.bfloat16)] * 3,
        grid=(columns // width,),
        in_specs=[pl.BlockSpec(rows.shape, lambda n: (0, 0)), anywhere, anywhere],
        out_specs=[block] * 3,
        scratch_shapes=[
            pltpu.VMEM((2, 2, bands, tiles, 2, half, width), jnp.bfloat16),
            pltpu.SemaphoreType.DMA((2, 2, 2)),
        ],
        compiler_params=pltpu.CompilerParams(vmem_limit_bytes=48 * 2**20),
        cost_estimate=pl.CostEstimate(
            flops=tokens * depth * columns // 8, bytes_accessed=2 * rows.size, transcendentals=0
        ),
    )(rows, early, late)


def backward_kernel(top_ref, gate_ref, up_ref, act_ref, early, late, late_down, *refs):
    dgate_ref, dup_ref = refs[:2]
    pieces, branch_pieces = refs[2:6], refs[6:10]
    weights, downs, total, branch, done, down_done = refs[10:]
    step, steps = pl.program_id(0), pl.num_programs(0)
    slot = step % 2
    strips, width = downs.shape[1], downs.shape[-1]

    def down_copies(at_step, at_slot):
        wanted = pl.ds(2 * steps, strips)
        return strip_copies(
            early.at[at_step, wanted], late_down.at[at_step], downs.at[at_slot], down_done.at[at_slot]
        )

    def copies(number, at_step, at_slot):
        strip = number * steps + at_step
        return strip_copies(
            early.at[:, strip], late.at[:, strip], weights.at[number, at_slot], done.at[number, at_slot]
        )

    def fetch(at_step, at_slot):
        for copy in down_copies(at_step, at_slot):
            copy.start()
        for number in range(2):
            for copy in copies(number, at_step, at_slot):
                copy.start()

    @pl.when(step == 0)
    def _():
        fetch(0, 0)
        total[...] = jnp.zeros_like(total)
        branch[...] = jnp.zeros_like(branch)

    @pl.when(step + 1 < steps)
    def _():
        fetch(step + 1, 1 - slot)

    for copy in down_copies(step, slot):
        copy.wait()
    for number in range(2):
        for copy in copies(number, step, slot):
            copy.wait()
    gate_weight, up_weight = (weights[number, slot].reshape(-1, width) for number in range(2))
    chunk = min(4 * BLK, top_ref.shape[0])
    for first in range(0, top_ref.shape[0], chunk):
        rows = slice(first, first + chunk)
        grad_act = 0.0
        for strip in range(strips):
            lanes = slice(strip * width, (strip + 1) * width)
            down = downs[slot, strip].reshape(-1, width)
            grad_act = grad_act + over_last(top_ref[rows, lanes], down)
            branch[rows, lanes] += jnp.dot(act_ref[rows], down, preferred_element_type=jnp.float32)
        gate = gate_ref[rows].astype(jnp.float32)
        up = up_ref[rows].astype(jnp.float32)
        sigmoid_gate = jax.nn.sigmoid(gate)
        grad_gate = grad_act * up * sigmoid_gate * (1.0 + gate * (1.0 - sigmoid_gate))
        grad_gate = grad_gate.astype(jnp.bfloat16)
        grad_up = (grad_act * (gate * sigmoid_gate)).astype(jnp.bfloat16)
        dgate_ref[rows] = grad_gate
        dup_ref[rows] = grad_up
        total[rows] += over_last(grad_gate, gate_weight) + over_last(grad_up, up_weight)

    @pl.when(step == steps - 1)
    def _():
        rows = total.shape[0] // 4
        for entry in range(4):
            part = slice(entry * rows, (entry + 1) * rows)
            write_pieces(entry, slice(0, rows), total[part], pieces)
            write_pieces(entry, slice(0, rows), branch[part], branch_pieces)


def backward_products(top, gate, up, act, early, late, late_down):
    tokens, depth = top.shape
    columns = gate.shape[1]
    bands, _, tiles, half, width = early.shape
    strips = depth // width
    block = pl.BlockSpec((tokens, width), lambda n: (0, n))
    anywhere = pl.BlockSpec(memory_space=pl.ANY)
    piece = jax.ShapeDtypeStruct((2, tokens // 4, depth // 2), jnp.bfloat16)
    grads = jax.ShapeDtypeStruct((tokens, columns), jnp.bfloat16)
    outs = pl.pallas_call(
        backward_kernel,
        out_shape=[grads] * 2 + [piece] * 8,
        grid=(columns // width,),
        in_specs=[pl.BlockSpec(top.shape, lambda n: (0, 0))] + [block] * 3 + [anywhere] * 3,
        out_specs=[block] * 2 + [pl.BlockSpec(piece.shape, lambda n: (0, 0, 0))] * 8,
        scratch_shapes=[
            pltpu.VMEM((2, 2, bands, tiles, 2, half, width), jnp.bfloat16),
            pltpu.VMEM((2, strips, tiles, 2, half, width), jnp.bfloat16),
            pltpu.VMEM((tokens, depth), jnp.float32),
            pltpu.VMEM((tokens, depth), jnp.float32),
            pltpu.SemaphoreType.DMA((2, 2, 2)),
            pltpu.SemaphoreType.DMA((2, 2)),
        ],
        compiler_params=pltpu.CompilerParams(vmem_limit_bytes=60 * 2**20),
        cost_estimate=pl.CostEstimate(
            flops=8 * tokens * depth * columns, bytes_accessed=8 * columns * depth, transcendentals=0
        ),
    )(top, gate, up, act, early, late, late_down)
    return outs[0], outs[1], outs[2:6], outs[6:10]


def rope_kernel(q_width, kv_width, x_ref, cos_ref, sin_ref, *outs):
    width = x_ref.shape[-1]
    for start in range(0, width, BLK):
        values = x_ref[0, :, start : start + BLK]
        first, turned = half_turn(values)
        sines = sin_ref[0]
        turned_rows = values * cos_ref[0] + turned * jnp.where(first, -sines, sines)
        if start + BLK > q_width + kv_width:
            column = lax.broadcasted_iota(jnp.int32, values.shape, 1) + start
            turned_rows = jnp.where(column >= q_width + kv_width, values, turned_rows)
        if start < q_width:
            outs[0][0, :, start : start + BLK] = (turned_rows * HD ** (-0.5)).astype(jnp.bfloat16)
        else:
            outs[-1][0, :, start - q_width : start - q_width + BLK] = turned_rows.astype(jnp.bfloat16)


def rope_rows(inner, rows, row_block, q_width, kv_width, cosines, sines, with_queries=True):
    seqs, _, width = inner.shape
    shared = cosines.shape[0] == 1
    table = pl.BlockSpec((1, rows, BLK), lambda s: (0 if shared else s, 0, 0))
    widths = [q_width, 2 * kv_width]
    column_block = 0
    if not with_queries:
        width, column_block = 2 * kv_width, q_width // (2 * kv_width)
        widths, q_width = widths[1:], 0
    return pl.pallas_call(
        functools.partial(rope_kernel, q_width, kv_width),
        out_shape=[jax.ShapeDtypeStruct((seqs, rows, w), jnp.bfloat16) for w in widths],
        grid=(seqs,),
        in_specs=[pl.BlockSpec((1, rows, width), lambda s: (s, row_block, column_block)), table, table],
        out_specs=[pl.BlockSpec((1, rows, w), lambda s: (s, 0, 0)) for w in widths],
        cost_estimate=pl.CostEstimate(
            flops=6 * seqs * rows * width, bytes_accessed=6 * seqs * rows * width, transcendentals=0
        ),
    )(inner, cosines, sines)


def fill_bias(band_ref, gpos_ref, bias_ref, rows, window_len):
    band = band_ref[0]

    @pl.when(pl.program_id(0) == 0)
    def _():
        key = lax.broadcasted_iota(jnp.int32, (window_len, rows), 0) + (
            band * rows - (window_len - rows)
        )
        query = lax.broadcasted_iota(jnp.int32, (window_len, rows), 1) + band * rows
        inside = (key > query - WINDOW) & (key <= query) & (key >= 0)
        bias_ref[:window_len] = jnp.where(inside, 0.0, masked_value)

    glob_total = gpos_ref.shape[1]
    query = lax.broadcasted_iota(jnp.int32, (glob_total, rows), 1) + (band * rows - WINDOW)
    spot = jnp.broadcast_to(gpos_ref[0][:, :1], (glob_total, rows))
    bias_ref[window_len:] = jnp.where(spot <= query.astype(jnp.float32), 0.0, masked_value)


def over_last(left, right):
    return lax.dot_general(left, right, (((1,), (1,)), ((), ())), preferred_element_type=jnp.float32)


def over_first(left, right):
    return lax.dot_general(left, right, (((0,), (0,)), ((), ())), preferred_element_type=jnp.float32)


def attend_kernel(block_total, band_ref, gpos_ref, q_ref, *refs):
    blocks, (out_ref, lse_ref, bias_ref) = refs[:block_total], refs[block_total:]
    rows, q_width = q_ref.shape[1:]
    kv_width = blocks[0].shape[2] // 2
    heads, group = q_width // HD, q_width // kv_width
    window_len = rows * (block_total - 1)
    fill_bias(band_ref, gpos_ref, bias_ref, rows, window_len)
    starts = [rows * number for number in range(block_total)]
    pending = []
    for head in range(heads):
        left = head // group * HD
        queries = q_ref[0, :, head * HD : (head + 1) * HD]
        scores = [
            over_last(block[0, :, left : left + HD], queries)
            + bias_ref[start : start + block.shape[1]]
            for block, start in zip(blocks, starts)
        ]
        top = functools.reduce(jnp.maximum, [jnp.max(part, 0, keepdims=True) for part in scores])
        total = 0.0
        mixed = 0.0
        for block, part in zip(blocks, scores):
            weights = jnp.exp(part - top)
            total = total + jnp.sum(weights, 0, keepdims=True)
            mixed = mixed + over_first(
                block[0, :, kv_width + left : kv_width + left + HD], weights.astype(jnp.bfloat16)
            )
        lse_ref[0, head : head + 1, :] = top + jnp.log(total)
        pending.append(mixed / total)
        if len(pending) * HD == BLK or head == heads - 1:
            stop = (head + 1) * HD
            both = jnp.concatenate(pending, 0).T
            out_ref[0, :, stop - both.shape[1] : stop] = both.astype(jnp.bfloat16)
            pending = []


def attend(band, gpos, queries, blocks):
    seqs, rows, q_width = queries.shape
    heads = q_width // HD
    key_total = sum(block.shape[1] for block in blocks)

    def whole(array):
        return pl.BlockSpec((1,) + array.shape[1:], lambda s, *_: (s, 0, 0))

    out_shape = [
        jax.ShapeDtypeStruct((seqs, rows, q_width), jnp.bfloat16),
        jax.ShapeDtypeStruct((seqs, heads, rows), jnp.float32),
    ]
    return pl.pallas_call(
        functools.partial(attend_kernel, len(blocks)),
        out_shape=out_shape,
        grid_spec=pltpu.PrefetchScalarGridSpec(
            num_scalar_prefetch=1,
            grid=(seqs,),
            in_specs=[whole(array) for array in (gpos, queries, *blocks)],
            out_specs=[whole(array) for array in out_shape],
            scratch_shapes=[pltpu.VMEM((key_total, rows), jnp.float32)],
        ),
        compiler_params=pltpu.CompilerParams(vmem_limit_bytes=48 * 2**20),
        cost_estimate=pl.CostEstimate(
            flops=16 * seqs * heads * rows * key_total * HD,
            bytes_accessed=4 * queries.size,
            transcendentals=seqs * heads * rows * key_total,
        ),
    )(band, gpos, queries, *blocks)


def attend_back_kernel(block_total, band_ref, gpos_ref, cos_ref, sin_ref, q_ref, grad_ref, lse_ref, *refs):
    blocks = refs[:block_total]
    dq_ref = refs[block_total]
    out_refs = refs[block_total + 1 : 2 * block_total + 1]
    bias_ref = refs[-1]
    rows, q_width = q_ref.shape[1:]
    kv_width = blocks[0].shape[2] // 2
    heads, group = q_width // HD, q_width // kv_width
    window_len = rows * (block_total - 1)
    fill_bias(band_ref, gpos_ref, bias_ref, rows, window_len)
    starts = [rows * number for number in range(block_total)]
    pending = []
    for kv_head in range(kv_width // HD):
        left = kv_head * HD
        key_sums = [0.0] * block_total
        value_sums = [0.0] * block_total
        for head in range(kv_head * group, (kv_head + 1) * group):
            queries = q_ref[0, :, head * HD : (head + 1) * HD]
            grads = grad_ref[0, :, head * HD : (head + 1) * HD]
            lse = lse_ref[0, head : head + 1, :]
            soft, soft_grads = [], []
            inner = 0.0
            for number, (block, start) in enumerate(zip(blocks, starts)):
                part = over_last(block[0, :, left : left + HD], queries)
                part = jnp.exp(part + bias_ref[start : start + block.shape[1]] - lse)
                slope = over_last(block[0, :, kv_width + left : kv_width + left + HD], grads)
                inner = inner + jnp.sum(part * slope, 0, keepdims=True)
                soft.append(part)
                soft_grads.append(slope)
            turned = 0.0
            for number, block in enumerate(blocks):
                score_grads = (soft[number] * (soft_grads[number] - inner)).astype(jnp.bfloat16)
                value_sums[number] = value_sums[number] + jnp.dot(
                    soft[number].astype(jnp.bfloat16), grads, preferred_element_type=jnp.float32
                )
                key_sums[number] = key_sums[number] + jnp.dot(
                    score_grads, queries, preferred_element_type=jnp.float32
                )
                turned = turned + over_first(block[0, :, left : left + HD], score_grads)
            pending.append(turned)
            if len(pending) * HD == BLK or head == heads - 1:
                stop = (head + 1) * HD
                both = jnp.concatenate(pending, 0).T * HD ** (-0.5)
                pending = []
                first, other = half_turn(both * sin_ref[0])
                both = both * cos_ref[0] + jnp.where(first, other, -other)
                dq_ref[0, :, stop - both.shape[1] : stop] = both.astype(jnp.bfloat16)
        for number, out_ref in enumerate(out_refs):
            out_ref[0, :, left : left + HD] = key_sums[number].astype(out_ref.dtype)
            out_ref[0, :, kv_width + left : kv_width + left + HD] = value_sums[number].astype(
                out_ref.dtype
            )


def attend_back(band, gpos, cosines, sines, queries, grads, lse, blocks):
    seqs, rows, q_width = queries.shape
    heads = q_width // HD
    key_total = sum(block.shape[1] for block in blocks)

    def whole(array):
        return pl.BlockSpec((1,) + array.shape[1:], lambda s, *_: (s, 0, 0))

    table = pl.BlockSpec((1, rows, BLK), lambda s, *_: (0, 0, 0))
    out_shape = [jax.ShapeDtypeStruct(queries.shape, jnp.bfloat16)]
    for number, block in enumerate(blocks):
        own = number == len(blocks) - 2
        out_shape.append(jax.ShapeDtypeStruct(block.shape, jnp.float32 if own else jnp.bfloat16))
    return pl.pallas_call(
        functools.partial(attend_back_kernel, len(blocks)),
        out_shape=out_shape,
        grid_spec=pltpu.PrefetchScalarGridSpec(
            num_scalar_prefetch=1,
            grid=(seqs,),
            in_specs=[whole(gpos), table, table]
            + [whole(array) for array in (queries, grads, lse, *blocks)],
            out_specs=[whole(array) for array in out_shape],
            scratch_shapes=[pltpu.VMEM((key_total, rows), jnp.float32)],
        ),
        compiler_params=pltpu.CompilerParams(vmem_limit_bytes=48 * 2**20),
        cost_estimate=pl.CostEstimate(
            flops=40 * seqs * heads * rows * key_total * HD,
            bytes_accessed=8 * queries.size,
            transcendentals=seqs * heads * rows * key_total,
        ),
    )(band, gpos, cosines, sines, queries, grads, lse, *blocks)


def join_kernel(q_width, kv_width, dq_ref, own_ref, pick_ref, glob_ref, cos_ref, sin_ref, *refs):
    back_refs, out_ref = refs[:-1], refs[-1]
    out_ref[0, :, :q_width] = dq_ref[0]
    picked = lax.dot_general(
        pick_ref[0].astype(jnp.float32),
        glob_ref[0],
        (((0,), (0,)), ((), ())),
        precision=lax.Precision.HIGHEST,
        preferred_element_type=jnp.float32,
    )
    for start in range(0, 2 * kv_width, BLK):
        lanes = slice(start, start + BLK)
        total = own_ref[0, :, lanes] + picked[:, lanes]
        for back_ref in back_refs:
            total = total + back_ref[0, :, lanes].astype(jnp.float32)
        first, other = half_turn(total * sin_ref[0])
        turned = total * cos_ref[0] + jnp.where(first, other, -other)
        column = lax.broadcasted_iota(jnp.int32, total.shape, 1) + start
        turned = jnp.where(column >= kv_width, total, turned)
        out_ref[0, :, q_width + start : q_width + start + BLK] = turned.astype(jnp.bfloat16)


def join_grads(dq, own, picks, globs, cosines, sines, backs):
    seqs, rows, q_width = dq.shape
    kv_width = own.shape[2] // 2

    def whole(array):
        return pl.BlockSpec((1,) + array.shape[1:], lambda s: (s, 0, 0))

    table = pl.BlockSpec((1, rows, BLK), lambda s: (0, 0, 0))
    out_shape = jax.ShapeDtypeStruct((seqs, rows, q_width + 2 * kv_width), jnp.bfloat16)
    return pl.pallas_call(
        functools.partial(join_kernel, q_width, kv_width),
        out_shape=out_shape,
        grid=(seqs,),
        in_specs=[whole(dq), whole(own), whole(picks), whole(globs), table, table]
        + [whole(back) for back in backs],
        out_specs=whole(out_shape),
        cost_estimate=pl.CostEstimate(
            flops=20 * own.size, bytes_accessed=4 * dq.size + 12 * own.size, transcendentals=0
        ),
    )(dq, own, picks, globs, cosines, sines, *backs)


def adam_kernel(batch, meta, rates, *refs):
    master_ref, first_ref, second_ref, left_ref, right_ref = refs[:5]
    sources = refs[5:-6]
    new_first_ref, new_second_ref, new_master_ref, copy_ref, tiles, arrived = refs[-6:]
    step, steps = pl.program_id(0), pl.num_programs(0)
    slot = step % 2

    def fetch(at_step, at_slot):
        for place in range(batch):
            tile = at_step * batch + place
            for number, source in enumerate(sources):

                @pl.when(meta[0, tile] == number)
                def _(source=source, tile=tile, place=place):
                    top = pl.multiple_of(meta[2, tile], BLK)
                    left = pl.multiple_of(meta[3, tile], BLK)
                    pltpu.make_async_copy(
                        source.at[meta[1, tile], pl.ds(top, BLK), pl.ds(left, BLK)],
                        tiles.at[at_slot, place],
                        arrived.at[at_slot],
                    ).start()

    @pl.when(step == 0)
    def _():
        fetch(0, 0)

    @pl.when(step + 1 < steps)
    def _():
        fetch(step + 1, 1 - slot)

    pltpu.make_async_copy(tiles.at[slot], tiles.at[slot], arrived.at[slot]).wait()
    places = range(batch)
    lefts = [left_ref[place].astype(jnp.bfloat16) for place in places]
    rights = [right_ref[place].astype(jnp.bfloat16) for place in places]
    turned = [over_first(lefts[place], tiles[slot, place]).astype(jnp.bfloat16) for place in places]
    rotated = [
        jnp.dot(turned[place], rights[place], preferred_element_type=jnp.float32) for place in places
    ]
    directions = []
    for place in places:
        new_first = beta_one * first_ref[place] + (1.0 - beta_one) * rotated[place]
        new_second = beta_two * second_ref[place] + (1.0 - beta_two) * rotated[place] * rotated[place]
        direction = (new_first * (1.0 / (1.0 - beta_one**STEP))) / (
            jnp.sqrt(new_second * (1.0 / (1.0 - beta_two**STEP))) + adam_eps
        )
        new_first_ref[place] = new_first
        new_second_ref[place] = new_second
        directions.append(direction.astype(jnp.bfloat16))
    updates = [
        jnp.dot(lefts[place], directions[place], preferred_element_type=jnp.float32) for place in places
    ]
    updates = [over_last(updates[place].astype(jnp.bfloat16), rights[place]) for place in places]
    for place in places:
        old = master_ref[place]
        new_master = old - rates[step * batch + place] * (updates[place] + weight_decay * old)
        new_master_ref[place] = new_master
        copy_ref[place] = new_master.astype(jnp.bfloat16)


def adam(meta, rates, state, sources):
    count = state[0].shape[0]
    batch = max(size for size in range(1, 33) if count % size == 0)
    block = pl.BlockSpec((batch, BLK, BLK), lambda s, *_: (s, 0, 0))
    anywhere = pl.BlockSpec(memory_space=pl.ANY)
    shape = (count, BLK, BLK)
    return pl.pallas_call(
        functools.partial(adam_kernel, batch),
        out_shape=[jax.ShapeDtypeStruct(shape, jnp.float32)] * 3
        + [jax.ShapeDtypeStruct(shape, jnp.bfloat16)],
        grid_spec=pltpu.PrefetchScalarGridSpec(
            num_scalar_prefetch=2,
            grid=(count // batch,),
            in_specs=[block] * 5 + [anywhere] * len(sources),
            out_specs=[block] * 4,
            scratch_shapes=[
                pltpu.VMEM((2, batch, BLK, BLK), jnp.bfloat16),
                pltpu.SemaphoreType.DMA((2,)),
            ],
        ),
        compiler_params=pltpu.CompilerParams(vmem_limit_bytes=56 * 2**20),
        cost_estimate=pl.CostEstimate(
            flops=8 * count * BLK**3, bytes_accessed=36 * count * BLK**2, transcendentals=0
        ),
    )(meta, rates, *state, *sources)


def per_device(
    block_input,
    cotangent,
    glob_select,
    assignment,
    master,
    first_moment,
    second_moment,
    left_basis,
    right_basis,
    gains,
    gain_first,
    gain_second,
):
    band_total = lax.axis_size("fsdp")
    rep_total = lax.axis_size("rep")
    place = lax.axis_index("rep")
    band = lax.axis_index("fsdp")
    heads = H // rep_total
    kv_heads = KVH // rep_total
    q_width = heads * HD
    kv_width = kv_heads * HD
    tok_count = block_input.shape[1]
    own_count = master.shape[1]
    tile_total = own_count * rep_total
    aligned = square() and whole_tiles(band_total, rep_total)
    tile_order = assignment[0]

    residual = block_input[0].astype(jnp.float32)
    grad_top = cotangent[0]
    position = band * tok_count + jnp.arange(tok_count, dtype=jnp.int32)
    cosine_table, sine_table = rope_tables(position)
    wide_cosine = jnp.concatenate([cosine_table, cosine_table], 1)[None]
    wide_sine = jnp.concatenate([sine_table, sine_table], 1)[None]
    scale_one = lax.rsqrt(jnp.mean(residual * residual, -1, keepdims=True) + norm_eps)
    normed_one = (residual * scale_one * gains[0]).astype(jnp.bfloat16)
    pick_rows = glob_select[0]
    glob_total = pick_rows.shape[0]
    selector = pick_rows.astype(jnp.bfloat16)
    glob_pos_part = jnp.sum(pick_rows * position[None, :], 1)
    digits = jnp.concatenate([glob_pos_part // 256, glob_pos_part % 256]).astype(jnp.bfloat16)
    digits = jnp.pad(digits[None], ((0, 7), (0, D - 2 * glob_total)))
    glob_rows = jnp.dot(selector, normed_one, preferred_element_type=jnp.float32).astype(jnp.bfloat16)
    glob_rows = add_all(jnp.concatenate([glob_rows, digits], 0), "fsdp").astype(jnp.bfloat16)
    packed = [normed_one, glob_rows, selector.reshape(-1, D)]
    packed = jnp.concatenate(packed, 0)
    packed = jnp.pad(packed, ((0, -packed.shape[0] % 32), (0, 0)))

    def over_bands(slice_rows):
        return lax.all_gather(slice_rows, "fsdp", axis=0, tiled=True)

    if aligned:
        half = BLK // 2
        low, high = (master[0, :, rows].astype(jnp.bfloat16) for rows in (slice(0, half), slice(half, BLK)))
        layout = slice_layout(band_total, rep_total)
        attn_layout = jnp.asarray(np.concatenate(layout[:4], 2))
        wanted = jnp.take(tile_order, by_place(attn_layout).reshape(-1), mode="clip")
        meta = jnp.stack([wanted // own_count == place, wanted % own_count], 0).astype(jnp.int32)
        attn_part = place_tiles(low, high, meta, *attn_layout.shape)
        attn_part = rep_scatter(attn_part).astype(jnp.bfloat16)
        low, attn_part = lax.optimization_barrier((low, attn_part))
        slots = square_pieces(low)
        attn = over_bands(attn_part)
        grids = [lax.dynamic_index_in_dim(jnp.asarray(grid), place, 0, False) for grid in layout]

        def find(wanted):
            wanted = jnp.take(tile_order, jnp.concatenate([grid.reshape(-1) for grid in wanted]), mode="clip")
            entry, row = (wanted // own_count) ^ place, wanted % own_count
            cut = own_count // 2
            high = (entry == 3) & (row >= cut)
            found = jnp.stack([jnp.where(high, 4, entry), jnp.where(high, row - cut, row)], 0)
            return found.astype(jnp.int32)

        all_grid = jnp.concatenate(grids[4:], 1)
        (first_part,) = gather_strips(slots, find([all_grid]), [all_grid.shape])
        packed, first_part, attn = lax.optimization_barrier((packed, first_part, attn))
        early = over_bands(first_part)
    packed_all = rep_gather(packed)
    if aligned:
        packed_all, high = lax.optimization_barrier((packed_all, high))
        later_slots = square_pieces(high)
    normed_one_all = packed_all[:, :tok_count].reshape(-1, D)
    at = tok_count + glob_total
    glob_digits = packed_all[:, at, : 2 * glob_total].astype(jnp.float32)
    glob_place = glob_digits[:, :glob_total] * 256.0 + glob_digits[:, glob_total:]
    at += 8
    selector_all = packed_all[:, at : at + selector.size // D].reshape(rep_total, glob_total, tok_count)

    if aligned:
        in_width = q_width + 2 * kv_width
        w_inner, w_output = attn[:, :in_width], attn[:, in_width:]
    else:
        slots = lax.all_gather(master[0].astype(jnp.bfloat16), "rep", axis=0, tiled=True)
        tiles = jnp.take(slots, tile_order, axis=0, mode="clip")
        slices = cut_slices(band_matrices(tiles, band_total), band_total, rep_total)
        w_inner = over_bands(jnp.concatenate(slices[0:3], 1))
        w_output = over_bands(slices[3])
        w_gate = over_bands(slices[4])
        w_up = over_bands(slices[5])
        w_down = over_bands(slices[6])

    w_output = by_place(w_output.reshape(rep_total, q_width, -1)).reshape(D, -1)

    def mul(rows, weight):
        return jnp.dot(rows, weight, preferred_element_type=jnp.float32)

    def mul_back(rows, weight):
        return lax.dot_general(rows, weight, (((1,), (1,)), ((), ())), preferred_element_type=jnp.float32)

    def weight_grad(rows, grad_rows):
        return lax.dot_general(
            rows, grad_rows, (((0,), (0,)), ((), ())), preferred_element_type=jnp.float32
        ).astype(jnp.bfloat16)

    def own_sum(partial):
        return rep_scatter(partial.astype(jnp.bfloat16).reshape(rep_total, tok_count, D))

    inner_rows = mul(packed_all.reshape(-1, D), w_inner).reshape(rep_total, -1, w_inner.shape[1])
    packed_all, normed_one_all = lax.optimization_barrier((packed_all, normed_one_all))
    queries, own_pairs = rope_rows(inner_rows, tok_count, 0, q_width, kv_width, wide_cosine, wide_sine)
    glob_cosine, glob_sine = rope_tables(glob_place.reshape(-1))
    glob_cosine = jnp.concatenate([glob_cosine, glob_cosine], 1).reshape(rep_total, glob_total, -1)
    glob_sine = jnp.concatenate([glob_sine, glob_sine], 1).reshape(rep_total, glob_total, -1)
    (glob_pairs,) = rope_rows(
        inner_rows, glob_total, tok_count // glob_total, q_width, kv_width, glob_cosine, glob_sine, False
    )
    back_count = (WINDOW + tok_count - 2) // tok_count
    odd = band % 2 == 1
    by_chip = back_count == 2 and band_total % 2 == 0
    if by_chip:
        two_back = shifted(own_pairs, "fsdp", 2)
        pair_blocks = [two_back, to_core(jnp.where(odd, two_back, own_pairs))]
    else:
        pair_blocks = [shifted(own_pairs, "fsdp", distance) for distance in range(back_count, 0, -1)]
    pair_blocks = pair_blocks + [own_pairs, glob_pairs]
    glob_spots = jnp.broadcast_to(glob_place[:, :, None], (rep_total, glob_total, BLK))
    band_number = band.astype(jnp.int32).reshape(1)
    attended_low, lse = attend(band_number, glob_spots, queries, pair_blocks)
    if aligned:
        *later_slots, attended_low, early = lax.optimization_barrier((*later_slots, attended_low, early))
        last_grid = jnp.concatenate(grids[4:6], 1)
        last_part, down_part = gather_strips(
            later_slots, find([last_grid, grids[6]]), [last_grid.shape, grids[6].shape]
        )

        def by_strips(gathered):
            return gathered.reshape(band_total, -1, all_grid.shape[0], half, gathered.shape[-1])

        early, late, late_down = by_strips(early), by_strips(over_bands(last_part)), by_strips(over_bands(down_part))
    attended_all = rep_features(attended_low).reshape(-1, D)
    columns = mul(attended_all, w_output).astype(jnp.bfloat16).reshape(rep_total, tok_count, -1)
    branch = by_place(rep_exchange(columns)).transpose(1, 0, 2).reshape(tok_count, D)
    middle = residual + branch.astype(jnp.float32)
    scale_two = lax.rsqrt(jnp.mean(middle * middle, -1, keepdims=True) + norm_eps)
    normed_two = (middle * scale_two * gains[1]).astype(jnp.bfloat16)
    normed_two_all = rep_gather(normed_two).reshape(-1, D)
    normed_two_all, grad_top_now = lax.optimization_barrier((normed_two_all, grad_top))
    top_first = gather_first(grad_top_now)

    if aligned:
        gate_rows, up_rows, activation = forward_products(normed_two_all, early, late, FF // rep_total)
        top_first, activation = after(top_first, activation)
        grad_top_all = gather_join(gather_second(top_first)).reshape(-1, D)
        g_down = weight_grad(activation, grad_top_all)
        grad_top_all, g_down = lax.optimization_barrier((grad_top_all, g_down))
        grad_gate, grad_up, pieces, branch_pieces = backward_products(
            grad_top_all, gate_rows, up_rows, activation, early, late, late_down
        )
        normed_first = sum_first(pieces)
        normed_first, g_gate = after(normed_first, weight_grad(normed_two_all, grad_gate))
        grad_normed_two = sum_second(normed_first)
    else:
        gate_rows = mul(normed_two_all, w_gate)
        up_rows = mul(normed_two_all, w_up)
        sigmoid_gate = jax.nn.sigmoid(gate_rows)
        silu_gate = gate_rows * sigmoid_gate
        activation = (silu_gate * up_rows).astype(jnp.bfloat16)
        grad_top_all = gather_join(gather_second(top_first)).reshape(-1, D)
        g_down = weight_grad(activation, grad_top_all)
        grad_act = mul_back(grad_top_all, w_down)
        grad_gate = (
            grad_act * up_rows * sigmoid_gate * (1.0 + gate_rows * (1.0 - sigmoid_gate))
        ).astype(jnp.bfloat16)
        grad_up = (grad_act * silu_gate).astype(jnp.bfloat16)
        grad_normed_two = own_sum(mul_back(grad_gate, w_gate) + mul_back(grad_up, w_up))
        branch_pieces = (mul(activation, w_down),)
        g_gate = weight_grad(normed_two_all, grad_gate)
    grad_normed_two, g_gate = lax.optimization_barrier((grad_normed_two, g_gate))

    def over_tokens(partial):
        return lax.psum_scatter(partial, "fsdp", scatter_dimension=0, tiled=True)

    s_down = over_tokens(g_down)
    s_gate = over_tokens(g_gate)

    grad_middle = grad_top.astype(jnp.float32) + norm_back(middle, scale_two, gains[1], grad_normed_two)
    grad_parts = grad_middle.astype(jnp.bfloat16).reshape(tok_count, rep_total, -1).transpose(1, 0, 2)
    grad_columns = rep_exchange(by_place(grad_parts)).reshape(rep_total * tok_count, -1)
    grad_columns, grad_up = lax.optimization_barrier((grad_columns, grad_up))
    grad_attended, g_up = rep_features_sum(
        grad_columns.reshape(rep_total, tok_count, -1),
        w_output,
        lambda: weight_grad(normed_two_all, grad_up),
    )
    grad_attended = grad_attended.astype(jnp.bfloat16)
    (s_down, g_up), grad_attended = after((s_down, g_up), grad_attended)
    down_first = gather_first(s_down)
    grad_queries, *grad_blocks = attend_back(
        band_number, glob_spots, wide_cosine, wide_sine, queries, grad_attended, lse, pair_blocks
    )
    down_first, *grad_blocks = after(down_first, *grad_blocks)
    down_second = gather_second(down_first)
    branch_pieces, *down_second = after(tuple(branch_pieces), *down_second)
    branch_first = sum_first(branch_pieces) if aligned else (own_sum(branch_pieces[0]),)
    if by_chip:
        came = to_core(jnp.concatenate([grad_blocks[1], grad_blocks[-1]], 1))
        came, glob_came = came[:, :tok_count], came[:, tok_count:]
        total = grad_blocks[0].astype(jnp.float32) + came.astype(jnp.float32)
        sent = jnp.where(odd, total.astype(jnp.bfloat16), grad_blocks[0])
        returned = [shifted(sent, "fsdp", -2), jnp.where(odd, jnp.zeros_like(came), came)]
    else:
        returned = [
            shifted(grad_blocks[back_count - distance], "fsdp", -distance)
            for distance in range(1, back_count + 1)
        ]
    if by_chip:
        glob_both = grad_blocks[-1].astype(jnp.float32) + glob_came.astype(jnp.float32)
        glob_grads = add_all(glob_both.astype(jnp.bfloat16), "fsdp", 2)
    else:
        glob_grads = add_all(grad_blocks[-1], "fsdp")
    branch_first, g_up, glob_grads, s_gate, *returned = lax.optimization_barrier(
        (branch_first, g_up, glob_grads, s_gate, *returned)
    )
    s_up = over_tokens(g_up)
    s_down = gather_join(down_second)
    gate_first = gather_first(s_gate)
    block_out = middle + (sum_second(branch_first) if aligned else branch_first[0])
    grad_inner = join_grads(
        grad_queries, grad_blocks[-2], selector_all, glob_grads, wide_cosine, wide_sine, returned
    ).reshape(-1, q_width + 2 * kv_width)
    grad_normed_parts = mul_back(grad_inner, w_inner).astype(jnp.bfloat16).reshape(rep_total, tok_count, D)
    if square():
        normed_first = sum_first(split_pieces(grad_normed_parts))
    else:
        normed_first = (rep_scatter(grad_normed_parts),)
    grad_inner, grad_normed_parts = lax.optimization_barrier((grad_inner, grad_normed_parts))
    g_inner = weight_grad(normed_one_all, grad_inner)
    attended_all, g_inner = lax.optimization_barrier((attended_all, g_inner))
    g_output = weight_grad(attended_all, grad_columns)
    g_output = by_place(g_output.reshape(rep_total, q_width, -1)).reshape(D, -1)
    g_attn = with_layout_constraint(jnp.concatenate([g_inner, g_output], 1), Layout((0, 1)))
    gate_first, block_out, *normed_first = after(gate_first, block_out, *normed_first)
    gate_second = gather_second(gate_first)
    grad_normed_one = sum_second(normed_first) if square() else normed_first[0]
    gate_second, s_up, g_attn, grad_normed_one = after(gate_second, s_up, g_attn, grad_normed_one)
    s_attn = over_tokens(g_attn)
    s_gate = gather_join(gate_second)
    up_first = gather_first(s_up)
    grad_input = grad_middle + norm_back(residual, scale_one, gains[0], grad_normed_one)

    gain_terms = jnp.stack(
        [
            jnp.sum(grad_normed_one * residual * scale_one, 0),
            jnp.sum(grad_normed_two * middle * scale_two, 0),
        ]
    )
    square_terms = jnp.stack(
        [jnp.sum(residual * residual), jnp.sum(middle * middle), jnp.sum(block_out * block_out)]
    )
    sums = jnp.concatenate([gain_terms.reshape(-1), square_terms])

    up_first, sums = after(up_first, sums)
    s_up = gather_join(gather_second(up_first))
    sums = add_all(add_all(sums, "rep"), "fsdp")
    sums, s_attn, s_up, s_gate, s_down = lax.optimization_barrier((sums, s_attn, s_up, s_gate, s_down))
    gain_grad, square_total = sums[: 2 * D].reshape(2, D), sums[2 * D :]

    slot_ids = jnp.arange(tile_total, dtype=jnp.int32)
    inverse = jnp.sum(jnp.where(tile_order[None, :] == slot_ids[:, None], slot_ids[None, :], 0), 1)
    own_slots = place * own_count + jnp.arange(own_count, dtype=jnp.int32)
    owned_tiles = jnp.take(inverse, own_slots, mode="clip")
    if aligned:
        sources = [rep_gather(s_attn), s_gate, s_up, s_down]
        where = np.zeros((4, rep_total, tile_total), np.int32)
        first_col = 0
        for kind, grid in enumerate(layout):
            rows, cols = grid.shape[1:]
            first_col = 0 if kind >= 4 else first_col
            for there in range(rep_total):
                numbers = grid[there].reshape(-1)
                at = np.arange(rows * cols)
                where[0, :, numbers] = max(kind - 3, 0)
                where[2, :, numbers] = (at // cols * BLK)[:, None]
                where[3, :, numbers] = (at % cols * BLK + first_col)[:, None]
                for here in range(rep_total):
                    where[1, here, numbers] = here ^ there
            first_col += cols * BLK
        tile_spots = lax.dynamic_index_in_dim(jnp.asarray(where), place, 1, False)
        meta = jnp.take(tile_spots, owned_tiles, axis=1, mode="clip")
    else:
        splits = [0, q_width, q_width + kv_width, q_width + 2 * kv_width, s_attn.shape[1]]
        stacks = [rep_gather(s_attn[:, low:high]) for low, high in zip(splits, splits[1:])]
        stacks += [s_gate, s_up, s_down]
        sources = [band_tiles(join_slices(stacks, band_total, rep_total))]
        meta = jnp.stack([0 * owned_tiles, owned_tiles, 0 * owned_tiles, 0 * owned_tiles], 0)
    slot_rates = jnp.take(kind_rates(band_total), owned_tiles, mode="clip")
    new_first, new_second, new_master, master_copy = adam(
        meta,
        slot_rates,
        (master[0], first_moment[0], second_moment[0], left_basis[0], right_basis[0]),
        sources,
    )
    new_gain_first = beta_one * gain_first + (1.0 - beta_one) * gain_grad
    new_gain_second = beta_two * gain_second + (1.0 - beta_two) * gain_grad * gain_grad
    gain_step = (
        new_gain_first
        / (1.0 - beta_one**STEP)
        / (jnp.sqrt(new_gain_second / (1.0 - beta_two**STEP)) + adam_eps)
    )
    new_gains = gains - gain_rate * gain_step
    rms_stats = jnp.sqrt(square_total / (rep_total * band_total * tok_count * D))
    return (
        block_out[None],
        grad_input[None],
        new_first[None],
        new_second[None],
        new_master[None],
        master_copy[None],
        new_gain_first,
        new_gain_second,
        new_gains,
        rms_stats,
    )


def solution(mesh):
    in_specs = (
        P("rep", "fsdp", None),
        P("rep", "fsdp", None),
        P("rep", None, "fsdp"),
        P("fsdp", None),
        P("fsdp", "rep", None, None),
        P("fsdp", "rep", None, None),
        P("fsdp", "rep", None, None),
        P("fsdp", "rep", None, None),
        P("fsdp", "rep", None, None),
        P(),
        P(),
        P(),
    )
    out_specs = (
        P("rep", "fsdp", None),
        P("rep", "fsdp", None),
        P("fsdp", "rep", None, None),
        P("fsdp", "rep", None, None),
        P("fsdp", "rep", None, None),
        P("fsdp", "rep", None, None),
        P(),
        P(),
        P(),
        P(),
    )
    return jax.shard_map(
        per_device, mesh=mesh, in_specs=in_specs, out_specs=out_specs, check_vma=False
    )
```

```python
import functools

import jax
import jax.numpy as jnp
import numpy as np
from jax import lax
from jax.experimental import pallas as pl
from jax.experimental.layout import Layout, with_layout_constraint
from jax.experimental.pallas import tpu as pltpu
from jax.sharding import PartitionSpec as P

D = 2048
H = 32
KVH = 8
HD = 64
FF = 8192
WINDOW = 512
BLK = 128
STEP = 10


norm_eps = 1e-05
rope_theta = 500000.0
beta_one = 0.5
beta_two = 0.5
adam_eps = 1e-08
weight_decay = 0.1
gain_rate = 0.5
masked_value = -1e30


def matrix_shapes():
    kv_width = KVH * HD
    return [(D, D), (D, kv_width), (D, kv_width), (D, D), (D, FF), (D, FF), (FF, D)]


def kind_rates(band_total):
    rate_list = [
        D ** (-0.5),
        D ** (-0.5),
        D ** (-0.5),
        (D * 8 // WINDOW) ** (-0.5),
        D ** (-0.5),
        D ** (-0.5),
        FF ** (-0.5),
    ]
    pieces = []
    for (row_total, col_total), rate_value in zip(matrix_shapes(), rate_list):
        tile_count = row_total // band_total // BLK * (col_total // BLK)
        pieces.append(jnp.full((tile_count,), rate_value, jnp.float32))
    return jnp.concatenate(pieces)


def band_matrices(tiles, band_total):
    matrices = []
    offset = 0
    for row_total, col_total in matrix_shapes():
        band_rows = row_total // band_total
        tile_count = band_rows // BLK * (col_total // BLK)
        segment = tiles[offset : offset + tile_count].reshape(
            band_rows // BLK, col_total // BLK, BLK, BLK
        )
        matrices.append(segment.transpose(0, 2, 1, 3).reshape(band_rows, col_total))
        offset += tile_count
    return matrices


def band_tiles(matrices):
    pieces = []
    for matrix in matrices:
        row_count, col_count = matrix.shape
        segment = matrix.reshape(row_count // BLK, BLK, col_count // BLK, BLK).transpose(0, 2, 1, 3)
        pieces.append(segment.reshape(-1, BLK, BLK))
    return jnp.concatenate(pieces, 0)


def rope_tables(position):
    halves = jnp.arange(HD // 2, dtype=jnp.float32) * (2.0 / HD)
    frequency = rope_theta ** (-halves)
    angles = position.astype(jnp.float32)[:, None] * frequency[None, :]
    angles = jnp.concatenate([angles, angles], 1)
    return (jnp.cos(angles), jnp.sin(angles))


def rotate(vectors, cosine_table, sine_table):
    half_width = vectors.shape[-1] // 2
    turned = jnp.concatenate([-vectors[..., half_width:], vectors[..., :half_width]], -1)
    return vectors * cosine_table[:, None, :] + turned * sine_table[:, None, :]


def rotate_back(grad_rows, cosine_table, sine_table):
    half_width = grad_rows.shape[-1] // 2
    scaled = grad_rows * sine_table[:, None, :]
    turned = jnp.concatenate([scaled[..., half_width:], -scaled[..., :half_width]], -1)
    return grad_rows * cosine_table[:, None, :] + turned


def norm_back(values, row_scale, gain_row, grad_rows):
    weighted = grad_rows * gain_row
    return row_scale * weighted - values * row_scale**3 * jnp.mean(
        weighted * values, -1, keepdims=True
    )


def to_rep(block, distance):
    route = [(i, i ^ distance) for i in range(lax.axis_size("rep"))]
    return lax.ppermute(block, "rep", route)


def square():
    return lax.axis_size("rep") == 4


def gather_first(block):
    if not square():
        return (lax.all_gather(block, "rep", axis=0),)
    return block, to_rep(block, 1), to_rep(block, 2)


def gather_second(first):
    if not square():
        return first
    block, near, far = first
    cut = block.shape[0] // 2
    return block, near, far, to_rep(near[:cut], 2), to_rep(far[cut:], 1)


def gather_join(pieces):
    if not square():
        return pieces[0]
    return jnp.concatenate(pieces, 0).reshape((4,) + pieces[0].shape)


def square_pieces(block):
    return gather_second(gather_first(block))


def rep_gather(block):
    return gather_join(gather_second(gather_first(block)))


def after(values, *others):
    count = len(values)
    tied = lax.optimization_barrier((*values, *others))
    return tuple(tied[:count]), *tied[count:]


def rep_of(entry):
    place = lax.axis_index("rep")
    return place ^ entry if square() else entry


def rep_scatter(parts):
    if not square():
        flat = parts.reshape(-1, parts.shape[-1])
        return lax.psum_scatter(flat, "rep", scatter_dimension=0, tiled=True).astype(jnp.float32)
    return sum_pieces(*split_pieces(parts))


def split_pieces(parts):
    half = parts.shape[-1] // 2
    low, high = parts[..., :half], parts[..., half:]
    return jnp.stack([low[0], low[2]], 0), jnp.stack([low[1], low[3]], 0), high[:2], high[2:]


def sum_first(pieces):
    low_kept, low_sent, high_kept, high_sent = pieces
    parts = []
    for kept, sent, first in ((low_kept, low_sent, 1), (high_kept, high_sent, 2)):
        came = to_rep(sent, first)
        parts.append(kept[0].astype(jnp.float32) + came[0].astype(jnp.float32))
        parts.append((kept[1].astype(jnp.float32) + came[1].astype(jnp.float32)).astype(kept.dtype))
    return tuple(parts)


def sum_second(parts):
    low, low_other, high, high_other = parts
    low = low + to_rep(low_other, 2).astype(jnp.float32)
    high = high + to_rep(high_other, 1).astype(jnp.float32)
    return jnp.concatenate([low, high], -1)


def sum_pieces(*pieces):
    return sum_second(sum_first(pieces))


def add_all(value, axis, distance=1):
    size = lax.axis_size(axis)
    total = value.astype(jnp.float32)
    while distance < size:
        count = 2 if (size // distance).bit_length() % 2 == 0 else 4
        low = total.astype(value.dtype)
        others = []
        for step in range(1, count):
            route = [(i, i ^ (step * distance)) for i in range(size)]
            others.append(lax.ppermute(low, axis, route).astype(jnp.float32))
        total = total + others[0]
        if count == 4:
            total = total + (others[1] + others[2])
        distance *= count
    return total


def rep_features(block):
    if not square():
        return lax.all_gather(block, "rep", axis=2, tiled=True)
    own, near, far, low, high = square_pieces(block)
    return jnp.concatenate(
        [
            own,
            jnp.stack([near[1], near[0], near[3], near[2]], 0),
            jnp.stack([far[2], far[3], far[0], far[1]], 0),
            jnp.stack([high[1], high[0], low[1], low[0]], 0),
        ],
        2,
    )


def write_pieces(entry, rows, values, refs):
    low_kept, low_sent, high_kept, high_sent = refs
    half = low_kept.shape[-1]
    values = values.astype(jnp.bfloat16)
    (low_sent if entry % 2 else low_kept)[entry // 2, rows] = values[:, :half]
    (high_sent if entry // 2 else high_kept)[entry % 2, rows] = values[:, half:]


def swapped_kernel(x_ref, w_ref, *refs):
    reps, rows, _ = x_ref.shape
    width = w_ref.shape[0] // reps
    for entry in range(reps):
        weight = w_ref[entry * width : (entry + 1) * width]
        for there in range(reps):
            product = over_last(x_ref[there ^ entry], weight)
            write_pieces(entry, slice(there * rows, (there + 1) * rows), product, refs)


def rep_features_sum(columns, weight, meanwhile):
    reps, rows, depth = columns.shape
    width = weight.shape[0] // reps
    if square():
        pieces = pl.pallas_call(
            swapped_kernel,
            out_shape=[jax.ShapeDtypeStruct((2, reps * rows, width // 2), jnp.bfloat16)] * 4,
            compiler_params=pltpu.CompilerParams(vmem_limit_bytes=32 * 2**20),
            cost_estimate=pl.CostEstimate(
                flops=2 * reps * columns.size * width,
                bytes_accessed=10 * columns.size,
                transcendentals=0,
            ),
        )(columns, weight)
        first = sum_first(pieces)
        first, *other = after(first, *meanwhile())
        total = sum_second(first)
    else:
        other = meanwhile()
        product = over_last(columns.reshape(-1, depth), weight).astype(jnp.bfloat16)
        swapped = product.reshape(reps, rows, reps, width).transpose(2, 0, 1, 3)
        total = rep_scatter(swapped.reshape(reps, reps * rows, width))
    return total.reshape(reps, rows, width), other


def rep_exchange(parts):
    if not square():
        return lax.all_to_all(parts, "rep", 0, 0)
    return jnp.stack([parts[0]] + [to_rep(parts[entry], entry) for entry in (1, 2, 3)], 0)


def by_place(parts):
    entries = [rep_of(entry) for entry in range(parts.shape[0])]
    return jnp.stack([lax.dynamic_index_in_dim(parts, entry, 0, False) for entry in entries], 0)


def to_core(block):
    return lax.ppermute(block, "fsdp", [(i, i ^ 1) for i in range(lax.axis_size("fsdp"))])


def shifted(block, axis, distance):
    devices = range(lax.axis_size(axis))
    route = [(i - distance, i) for i in devices if i - distance in devices]
    return lax.ppermute(block, axis, route)


def tile_offsets(band_total):
    offsets = [0]
    for row_total, col_total in matrix_shapes():
        offsets.append(offsets[-1] + row_total // band_total // BLK * (col_total // BLK))
    return offsets


def whole_tiles(band_total, rep_total):
    return KVH * HD // rep_total % BLK == 0 and FF // band_total // rep_total % BLK == 0


def slice_layout(band_total, rep_total):
    offsets = tile_offsets(band_total)
    layout = []
    for kind, (row_total, col_total) in enumerate(matrix_shapes()):
        rows, cols = row_total // band_total // BLK, col_total // BLK
        grid = offsets[kind] + np.arange(rows * cols).reshape(rows, cols)
        if kind == 6:
            layout.append(grid.reshape(rep_total, rows // rep_total, cols))
        elif kind in (4, 5):
            cut = grid.reshape(rows, band_total, rep_total, -1).transpose(2, 0, 1, 3)
            layout.append(cut.reshape(rep_total, rows, -1))
        else:
            layout.append(grid.reshape(rows, rep_total, -1).transpose(1, 0, 2))
    return layout


def tiles_to_matrix(tiles):
    rows, cols = tiles.shape[:2]
    return tiles.transpose(0, 2, 1, 3).reshape(rows * BLK, cols * BLK)


def matrix_to_tiles(matrix):
    rows, cols = matrix.shape
    cut = matrix.reshape(rows // BLK, BLK, cols // BLK, BLK)
    return cut.transpose(0, 2, 1, 3).reshape(-1, BLK, BLK)


def cut_slices(matrices, band_total, rep_total):
    place = lax.axis_index("rep")
    slices = []
    for kind, matrix in enumerate(matrices):
        rows, cols = matrix.shape
        if kind == 6:
            slices.append(lax.dynamic_slice_in_dim(matrix, place * (rows // rep_total), rows // rep_total, 0))
        elif kind in (4, 5):
            cut = matrix.reshape(rows, band_total, rep_total, -1)
            slices.append(lax.dynamic_index_in_dim(cut, place, 2, False).reshape(rows, -1))
        else:
            slices.append(lax.dynamic_slice_in_dim(matrix, place * (cols // rep_total), cols // rep_total, 1))
    return slices


def join_slices(stacks, band_total, rep_total):
    matrices = []
    for kind, stack in enumerate(stacks):
        rows, cols = stack.shape[1:]
        if kind == 6:
            matrices.append(stack.reshape(-1, cols))
        elif kind in (4, 5):
            cut = stack.reshape(rep_total, rows, band_total, -1).transpose(1, 2, 0, 3)
            matrices.append(cut.reshape(rows, -1))
        else:
            matrices.append(stack.transpose(1, 0, 2).reshape(rows, -1))
    return matrices


def gather_kernel(grids, meta, *refs):
    source_total = len(refs) - len(grids) - 1
    sources, targets, done = refs[:source_total], refs[source_total:-1], refs[-1]
    height = sources[0].shape[1]
    start = 0
    for place, (target, (rows, cols)) in enumerate(zip(targets, grids)):

        def one(tile, carry, target=target, rows=rows, cols=cols, start=start, place=place):
            kind = meta[0, start + tile]
            row = meta[1, start + tile]
            across = tile % cols
            top = pl.multiple_of((across // 2 * rows + tile // cols) * height, height)
            left = pl.multiple_of(across % 2 * BLK, BLK)
            for number, source in enumerate(sources):

                @pl.when(kind == number)
                def _(source=source):
                    pltpu.make_async_copy(
                        source.at[row], target.at[pl.ds(top, height), pl.ds(left, BLK)], done.at[place]
                    ).start()

            return carry

        lax.fori_loop(0, rows * cols, one, 0)
        start += rows * cols
    for place, target in enumerate(targets):
        pltpu.make_async_copy(target, target, done.at[place]).wait()


def gather_strips(sources, meta, grids):
    anywhere = pl.BlockSpec(memory_space=pl.ANY)
    height = sources[0].shape[1]
    out_shape = [
        jax.ShapeDtypeStruct((cols // 2 * rows * height, 2 * BLK), jnp.bfloat16) for rows, cols in grids
    ]
    return pl.pallas_call(
        functools.partial(gather_kernel, grids),
        out_shape=out_shape,
        grid_spec=pltpu.PrefetchScalarGridSpec(
            num_scalar_prefetch=1,
            grid=(1,),
            in_specs=[anywhere] * len(sources),
            out_specs=[pl.BlockSpec(shape.shape, lambda i, *_: (0, 0)) for shape in out_shape],
            scratch_shapes=[pltpu.SemaphoreType.DMA((len(grids),))],
        ),
        compiler_params=pltpu.CompilerParams(vmem_limit_bytes=32 * 2**20),
        cost_estimate=pl.CostEstimate(
            flops=0, bytes_accessed=sum(4 * shape.size for shape in out_shape), transcendentals=0
        ),
    )(meta, *sources)


def place_kernel(entries, rows, cols, meta, low, high, out_ref, done):
    out_ref[...] = jnp.zeros_like(out_ref)
    height = low.shape[1]

    def copies(tile):
        entry, rest = tile // (rows * cols), tile % (rows * cols)
        top = rest // cols * (2 * height)
        left = pl.multiple_of(rest % cols * BLK, BLK)
        return [
            pltpu.make_async_copy(
                half.at[meta[1, tile]],
                out_ref.at[entry, pl.ds(pl.multiple_of(top + part * height, height), height), pl.ds(left, BLK)],
                done.at[part],
            )
            for part, half in enumerate((low, high))
        ]

    def begin(tile, carry):
        @pl.when(meta[0, tile] == 1)
        def _():
            for copy in copies(tile):
                copy.start()

        return carry

    def finish(tile, carry):
        @pl.when(meta[0, tile] == 1)
        def _():
            for copy in copies(tile):
                copy.wait()

        return carry

    lax.fori_loop(0, entries * rows * cols, begin, 0)
    lax.fori_loop(0, entries * rows * cols, finish, 0)


def place_tiles(low, high, meta, entries, rows, cols):
    shape = (entries, rows * BLK, cols * BLK)
    anywhere = pl.BlockSpec(memory_space=pl.ANY)
    return pl.pallas_call(
        functools.partial(place_kernel, entries, rows, cols),
        out_shape=jax.ShapeDtypeStruct(shape, jnp.bfloat16),
        grid_spec=pltpu.PrefetchScalarGridSpec(
            num_scalar_prefetch=1,
            grid=(1,),
            in_specs=[anywhere, anywhere],
            out_specs=pl.BlockSpec(shape, lambda i, *_: (0, 0, 0)),
            scratch_shapes=[pltpu.SemaphoreType.DMA((2,))],
        ),
        compiler_params=pltpu.CompilerParams(vmem_limit_bytes=32 * 2**20),
        cost_estimate=pl.CostEstimate(
            flops=0, bytes_accessed=4 * entries * rows * cols * BLK * BLK, transcendentals=0
        ),
    )(meta, low, high)


def half_turn(values):
    lane = lax.broadcasted_iota(jnp.int32, values.shape, 1)
    lanes = values.shape[1]
    first = lane % HD < HD // 2
    return first, jnp.where(
        first, pltpu.roll(values, lanes - HD // 2, 1), pltpu.roll(values, HD // 2, 1)
    )


def strip_copies(early, late, target, done):
    return [
        pltpu.make_async_copy(half, target.at[:, :, number], done.at[number])
        for number, half in enumerate((early, late))
    ]


def forward_kernel(x_ref, early, late, gate_ref, up_ref, act_ref, weights, done):
    step, steps = pl.program_id(0), pl.num_programs(0)
    slot = step % 2
    width = weights.shape[-1]

    def copies(number, at_step, at_slot):
        strip = number * steps + at_step
        return strip_copies(
            early.at[:, strip], late.at[:, strip], weights.at[number, at_slot], done.at[number, at_slot]
        )

    def fetch(at_step, at_slot):
        for number in range(2):
            for copy in copies(number, at_step, at_slot):
                copy.start()

    @pl.when(step == 0)
    def _():
        fetch(0, 0)

    @pl.when(step + 1 < steps)
    def _():
        fetch(step + 1, 1 - slot)

    for number in range(2):
        for copy in copies(number, step, slot):
            copy.wait()
    gate_weight, up_weight = (weights[number, slot].reshape(-1, width) for number in range(2))
    chunk = min(2 * BLK, x_ref.shape[0])
    for first in range(0, x_ref.shape[0], chunk):
        rows = slice(first, first + chunk)
        gate = jnp.dot(x_ref[rows], gate_weight, preferred_element_type=jnp.float32)
        up = jnp.dot(x_ref[rows], up_weight, preferred_element_type=jnp.float32)
        gate_ref[rows] = gate.astype(jnp.bfloat16)
        up_ref[rows] = up.astype(jnp.bfloat16)
        act_ref[rows] = (gate * jax.nn.sigmoid(gate) * up).astype(jnp.bfloat16)


def forward_products(rows, early, late, columns):
    tokens, depth = rows.shape
    bands, _, tiles, half, width = early.shape
    block = pl.BlockSpec((tokens, width), lambda n: (0, n))
    anywhere = pl.BlockSpec(memory_space=pl.ANY)
    return pl.pallas_call(
        forward_kernel,
        out_shape=[jax.ShapeDtypeStruct((tokens, columns), jnp.bfloat16)] * 3,
        grid=(columns // width,),
        in_specs=[pl.BlockSpec(rows.shape, lambda n: (0, 0)), anywhere, anywhere],
        out_specs=[block] * 3,
        scratch_shapes=[
            pltpu.VMEM((2, 2, bands, tiles, 2, half, width), jnp.bfloat16),
            pltpu.SemaphoreType.DMA((2, 2, 2)),
        ],
        compiler_params=pltpu.CompilerParams(vmem_limit_bytes=48 * 2**20),
        cost_estimate=pl.CostEstimate(
            flops=tokens * depth * columns // 8, bytes_accessed=2 * rows.size, transcendentals=0
        ),
    )(rows, early, late)


def backward_kernel(top_ref, gate_ref, up_ref, act_ref, early, late, late_down, *refs):
    dgate_ref, dup_ref = refs[:2]
    pieces, branch_pieces = refs[2:6], refs[6:10]
    weights, downs, total, branch, done, down_done = refs[10:]
    step, steps = pl.program_id(0), pl.num_programs(0)
    slot = step % 2
    strips, width = downs.shape[1], downs.shape[-1]

    def down_copies(at_step, at_slot):
        wanted = pl.ds(2 * steps, strips)
        return strip_copies(
            early.at[at_step, wanted], late_down.at[at_step], downs.at[at_slot], down_done.at[at_slot]
        )

    def copies(number, at_step, at_slot):
        strip = number * steps + at_step
        return strip_copies(
            early.at[:, strip], late.at[:, strip], weights.at[number, at_slot], done.at[number, at_slot]
        )

    def fetch(at_step, at_slot):
        for copy in down_copies(at_step, at_slot):
            copy.start()
        for number in range(2):
            for copy in copies(number, at_step, at_slot):
                copy.start()

    @pl.when(step == 0)
    def _():
        fetch(0, 0)
        total[...] = jnp.zeros_like(total)
        branch[...] = jnp.zeros_like(branch)

    @pl.when(step + 1 < steps)
    def _():
        fetch(step + 1, 1 - slot)

    for copy in down_copies(step, slot):
        copy.wait()
    for number in range(2):
        for copy in copies(number, step, slot):
            copy.wait()
    gate_weight, up_weight = (weights[number, slot].reshape(-1, width) for number in range(2))
    chunk = min(4 * BLK, top_ref.shape[0])
    for first in range(0, top_ref.shape[0], chunk):
        rows = slice(first, first + chunk)
        grad_act = 0.0
        for strip in range(strips):
            lanes = slice(strip * width, (strip + 1) * width)
            down = downs[slot, strip].reshape(-1, width)
            grad_act = grad_act + over_last(top_ref[rows, lanes], down)
            branch[rows, lanes] += jnp.dot(act_ref[rows], down, preferred_element_type=jnp.float32)
        gate = gate_ref[rows].astype(jnp.float32)
        up = up_ref[rows].astype(jnp.float32)
        sigmoid_gate = jax.nn.sigmoid(gate)
        grad_gate = grad_act * up * sigmoid_gate * (1.0 + gate * (1.0 - sigmoid_gate))
        grad_gate = grad_gate.astype(jnp.bfloat16)
        grad_up = (grad_act * (gate * sigmoid_gate)).astype(jnp.bfloat16)
        dgate_ref[rows] = grad_gate
        dup_ref[rows] = grad_up
        total[rows] += over_last(grad_gate, gate_weight) + over_last(grad_up, up_weight)

    @pl.when(step == steps - 1)
    def _():
        rows = total.shape[0] // 4
        for entry in range(4):
            part = slice(entry * rows, (entry + 1) * rows)
            write_pieces(entry, slice(0, rows), total[part], pieces)
            write_pieces(entry, slice(0, rows), branch[part], branch_pieces)


def backward_products(top, gate, up, act, early, late, late_down):
    tokens, depth = top.shape
    columns = gate.shape[1]
    bands, _, tiles, half, width = early.shape
    strips = depth // width
    block = pl.BlockSpec((tokens, width), lambda n: (0, n))
    anywhere = pl.BlockSpec(memory_space=pl.ANY)
    piece = jax.ShapeDtypeStruct((2, tokens // 4, depth // 2), jnp.bfloat16)
    grads = jax.ShapeDtypeStruct((tokens, columns), jnp.bfloat16)
    outs = pl.pallas_call(
        backward_kernel,
        out_shape=[grads] * 2 + [piece] * 8,
        grid=(columns // width,),
        in_specs=[pl.BlockSpec(top.shape, lambda n: (0, 0))] + [block] * 3 + [anywhere] * 3,
        out_specs=[block] * 2 + [pl.BlockSpec(piece.shape, lambda n: (0, 0, 0))] * 8,
        scratch_shapes=[
            pltpu.VMEM((2, 2, bands, tiles, 2, half, width), jnp.bfloat16),
            pltpu.VMEM((2, strips, tiles, 2, half, width), jnp.bfloat16),
            pltpu.VMEM((tokens, depth), jnp.float32),
            pltpu.VMEM((tokens, depth), jnp.float32),
            pltpu.SemaphoreType.DMA((2, 2, 2)),
            pltpu.SemaphoreType.DMA((2, 2)),
        ],
        compiler_params=pltpu.CompilerParams(vmem_limit_bytes=60 * 2**20),
        cost_estimate=pl.CostEstimate(
            flops=8 * tokens * depth * columns, bytes_accessed=8 * columns * depth, transcendentals=0
        ),
    )(top, gate, up, act, early, late, late_down)
    return outs[0], outs[1], outs[2:6], outs[6:10]


def rope_kernel(q_width, kv_width, x_ref, cos_ref, sin_ref, *outs):
    width = x_ref.shape[-1]
    for start in range(0, width, BLK):
        values = x_ref[0, :, start : start + BLK]
        first, turned = half_turn(values)
        sines = sin_ref[0]
        turned_rows = values * cos_ref[0] + turned * jnp.where(first, -sines, sines)
        if start + BLK > q_width + kv_width:
            column = lax.broadcasted_iota(jnp.int32, values.shape, 1) + start
            turned_rows = jnp.where(column >= q_width + kv_width, values, turned_rows)
        if start < q_width:
            outs[0][0, :, start : start + BLK] = (turned_rows * HD ** (-0.5)).astype(jnp.bfloat16)
        else:
            outs[-1][0, :, start - q_width : start - q_width + BLK] = turned_rows.astype(jnp.bfloat16)


def rope_rows(inner, rows, row_block, q_width, kv_width, cosines, sines, with_queries=True):
    seqs, _, width = inner.shape
    shared = cosines.shape[0] == 1
    table = pl.BlockSpec((1, rows, BLK), lambda s: (0 if shared else s, 0, 0))
    widths = [q_width, 2 * kv_width]
    column_block = 0
    if not with_queries:
        width, column_block = 2 * kv_width, q_width // (2 * kv_width)
        widths, q_width = widths[1:], 0
    return pl.pallas_call(
        functools.partial(rope_kernel, q_width, kv_width),
        out_shape=[jax.ShapeDtypeStruct((seqs, rows, w), jnp.bfloat16) for w in widths],
        grid=(seqs,),
        in_specs=[pl.BlockSpec((1, rows, width), lambda s: (s, row_block, column_block)), table, table],
        out_specs=[pl.BlockSpec((1, rows, w), lambda s: (s, 0, 0)) for w in widths],
        cost_estimate=pl.CostEstimate(
            flops=6 * seqs * rows * width, bytes_accessed=6 * seqs * rows * width, transcendentals=0
        ),
    )(inner, cosines, sines)


def fill_bias(band_ref, gpos_ref, bias_ref, rows, window_len):
    band = band_ref[0]

    @pl.when(pl.program_id(0) == 0)
    def _():
        key = lax.broadcasted_iota(jnp.int32, (window_len, rows), 0) + (
            band * rows - (window_len - rows)
        )
        query = lax.broadcasted_iota(jnp.int32, (window_len, rows), 1) + band * rows
        inside = (key > query - WINDOW) & (key <= query) & (key >= 0)
        bias_ref[:window_len] = jnp.where(inside, 0.0, masked_value)

    glob_total = gpos_ref.shape[1]
    query = lax.broadcasted_iota(jnp.int32, (glob_total, rows), 1) + (band * rows - WINDOW)
    spot = jnp.broadcast_to(gpos_ref[0][:, :1], (glob_total, rows))
    bias_ref[window_len:] = jnp.where(spot <= query.astype(jnp.float32), 0.0, masked_value)


def over_last(left, right):
    return lax.dot_general(left, right, (((1,), (1,)), ((), ())), preferred_element_type=jnp.float32)


def over_first(left, right):
    return lax.dot_general(left, right, (((0,), (0,)), ((), ())), preferred_element_type=jnp.float32)


def attend_kernel(block_total, band_ref, gpos_ref, q_ref, *refs):
    blocks, (out_ref, lse_ref, bias_ref) = refs[:block_total], refs[block_total:]
    rows, q_width = q_ref.shape[1:]
    kv_width = blocks[0].shape[2] // 2
    heads, group = q_width // HD, q_width // kv_width
    window_len = rows * (block_total - 1)
    fill_bias(band_ref, gpos_ref, bias_ref, rows, window_len)
    starts = [rows * number for number in range(block_total)]
    pending = []
    for head in range(heads):
        left = head // group * HD
        queries = q_ref[0, :, head * HD : (head + 1) * HD]
        scores = [
            over_last(block[0, :, left : left + HD], queries)
            + bias_ref[start : start + block.shape[1]]
            for block, start in zip(blocks, starts)
        ]
        top = functools.reduce(jnp.maximum, [jnp.max(part, 0, keepdims=True) for part in scores])
        total = 0.0
        mixed = 0.0
        for block, part in zip(blocks, scores):
            weights = jnp.exp(part - top)
            total = total + jnp.sum(weights, 0, keepdims=True)
            mixed = mixed + over_first(
                block[0, :, kv_width + left : kv_width + left + HD], weights.astype(jnp.bfloat16)
            )
        lse_ref[0, head : head + 1, :] = top + jnp.log(total)
        pending.append(mixed / total)
        if len(pending) * HD == BLK or head == heads - 1:
            stop = (head + 1) * HD
            both = jnp.concatenate(pending, 0).T
            out_ref[0, :, stop - both.shape[1] : stop] = both.astype(jnp.bfloat16)
            pending = []


def attend(band, gpos, queries, blocks):
    seqs, rows, q_width = queries.shape
    heads = q_width // HD
    key_total = sum(block.shape[1] for block in blocks)

    def whole(array):
        return pl.BlockSpec((1,) + array.shape[1:], lambda s, *_: (s, 0, 0))

    out_shape = [
        jax.ShapeDtypeStruct((seqs, rows, q_width), jnp.bfloat16),
        jax.ShapeDtypeStruct((seqs, heads, rows), jnp.float32),
    ]
    return pl.pallas_call(
        functools.partial(attend_kernel, len(blocks)),
        out_shape=out_shape,
        grid_spec=pltpu.PrefetchScalarGridSpec(
            num_scalar_prefetch=1,
            grid=(seqs,),
            in_specs=[whole(array) for array in (gpos, queries, *blocks)],
            out_specs=[whole(array) for array in out_shape],
            scratch_shapes=[pltpu.VMEM((key_total, rows), jnp.float32)],
        ),
        compiler_params=pltpu.CompilerParams(vmem_limit_bytes=48 * 2**20),
        cost_estimate=pl.CostEstimate(
            flops=16 * seqs * heads * rows * key_total * HD,
            bytes_accessed=4 * queries.size,
            transcendentals=seqs * heads * rows * key_total,
        ),
    )(band, gpos, queries, *blocks)


def attend_back_kernel(block_total, band_ref, gpos_ref, cos_ref, sin_ref, q_ref, grad_ref, lse_ref, *refs):
    blocks = refs[:block_total]
    dq_ref = refs[block_total]
    out_refs = refs[block_total + 1 : 2 * block_total + 1]
    bias_ref = refs[-1]
    rows, q_width = q_ref.shape[1:]
    kv_width = blocks[0].shape[2] // 2
    heads, group = q_width // HD, q_width // kv_width
    window_len = rows * (block_total - 1)
    fill_bias(band_ref, gpos_ref, bias_ref, rows, window_len)
    starts = [rows * number for number in range(block_total)]
    pending = []
    for kv_head in range(kv_width // HD):
        left = kv_head * HD
        key_sums = [0.0] * block_total
        value_sums = [0.0] * block_total
        for head in range(kv_head * group, (kv_head + 1) * group):
            queries = q_ref[0, :, head * HD : (head + 1) * HD]
            grads = grad_ref[0, :, head * HD : (head + 1) * HD]
            lse = lse_ref[0, head : head + 1, :]
            soft, soft_grads = [], []
            inner = 0.0
            for number, (block, start) in enumerate(zip(blocks, starts)):
                part = over_last(block[0, :, left : left + HD], queries)
                part = jnp.exp(part + bias_ref[start : start + block.shape[1]] - lse)
                slope = over_last(block[0, :, kv_width + left : kv_width + left + HD], grads)
                inner = inner + jnp.sum(part * slope, 0, keepdims=True)
                soft.append(part)
                soft_grads.append(slope)
            turned = 0.0
            for number, block in enumerate(blocks):
                score_grads = (soft[number] * (soft_grads[number] - inner)).astype(jnp.bfloat16)
                value_sums[number] = value_sums[number] + jnp.dot(
                    soft[number].astype(jnp.bfloat16), grads, preferred_element_type=jnp.float32
                )
                key_sums[number] = key_sums[number] + jnp.dot(
                    score_grads, queries, preferred_element_type=jnp.float32
                )
                turned = turned + over_first(block[0, :, left : left + HD], score_grads)
            pending.append(turned)
            if len(pending) * HD == BLK or head == heads - 1:
                stop = (head + 1) * HD
                both = jnp.concatenate(pending, 0).T * HD ** (-0.5)
                pending = []
                first, other = half_turn(both * sin_ref[0])
                both = both * cos_ref[0] + jnp.where(first, other, -other)
                dq_ref[0, :, stop - both.shape[1] : stop] = both.astype(jnp.bfloat16)
        for number, out_ref in enumerate(out_refs):
            out_ref[0, :, left : left + HD] = key_sums[number].astype(out_ref.dtype)
            out_ref[0, :, kv_width + left : kv_width + left + HD] = value_sums[number].astype(
                out_ref.dtype
            )


def attend_back(band, gpos, cosines, sines, queries, grads, lse, blocks):
    seqs, rows, q_width = queries.shape
    heads = q_width // HD
    key_total = sum(block.shape[1] for block in blocks)

    def whole(array):
        return pl.BlockSpec((1,) + array.shape[1:], lambda s, *_: (s, 0, 0))

    table = pl.BlockSpec((1, rows, BLK), lambda s, *_: (0, 0, 0))
    out_shape = [jax.ShapeDtypeStruct(queries.shape, jnp.bfloat16)]
    for number, block in enumerate(blocks):
        own = number == len(blocks) - 2
        out_shape.append(jax.ShapeDtypeStruct(block.shape, jnp.float32 if own else jnp.bfloat16))
    return pl.pallas_call(
        functools.partial(attend_back_kernel, len(blocks)),
        out_shape=out_shape,
        grid_spec=pltpu.PrefetchScalarGridSpec(
            num_scalar_prefetch=1,
            grid=(seqs,),
            in_specs=[whole(gpos), table, table]
            + [whole(array) for array in (queries, grads, lse, *blocks)],
            out_specs=[whole(array) for array in out_shape],
            scratch_shapes=[pltpu.VMEM((key_total, rows), jnp.float32)],
        ),
        compiler_params=pltpu.CompilerParams(vmem_limit_bytes=48 * 2**20),
        cost_estimate=pl.CostEstimate(
            flops=40 * seqs * heads * rows * key_total * HD,
            bytes_accessed=8 * queries.size,
            transcendentals=seqs * heads * rows * key_total,
        ),
    )(band, gpos, cosines, sines, queries, grads, lse, *blocks)


def join_kernel(q_width, kv_width, dq_ref, own_ref, pick_ref, glob_ref, cos_ref, sin_ref, *refs):
    back_refs, out_ref = refs[:-1], refs[-1]
    out_ref[0, :, :q_width] = dq_ref[0]
    picked = lax.dot_general(
        pick_ref[0].astype(jnp.float32),
        glob_ref[0],
        (((0,), (0,)), ((), ())),
        precision=lax.Precision.HIGHEST,
        preferred_element_type=jnp.float32,
    )
    for start in range(0, 2 * kv_width, BLK):
        lanes = slice(start, start + BLK)
        total = own_ref[0, :, lanes] + picked[:, lanes]
        for back_ref in back_refs:
            total = total + back_ref[0, :, lanes].astype(jnp.float32)
        first, other = half_turn(total * sin_ref[0])
        turned = total * cos_ref[0] + jnp.where(first, other, -other)
        column = lax.broadcasted_iota(jnp.int32, total.shape, 1) + start
        turned = jnp.where(column >= kv_width, total, turned)
        out_ref[0, :, q_width + start : q_width + start + BLK] = turned.astype(jnp.bfloat16)


def join_grads(dq, own, picks, globs, cosines, sines, backs):
    seqs, rows, q_width = dq.shape
    kv_width = own.shape[2] // 2

    def whole(array):
        return pl.BlockSpec((1,) + array.shape[1:], lambda s: (s, 0, 0))

    table = pl.BlockSpec((1, rows, BLK), lambda s: (0, 0, 0))
    out_shape = jax.ShapeDtypeStruct((seqs, rows, q_width + 2 * kv_width), jnp.bfloat16)
    return pl.pallas_call(
        functools.partial(join_kernel, q_width, kv_width),
        out_shape=out_shape,
        grid=(seqs,),
        in_specs=[whole(dq), whole(own), whole(picks), whole(globs), table, table]
        + [whole(back) for back in backs],
        out_specs=whole(out_shape),
        cost_estimate=pl.CostEstimate(
            flops=20 * own.size, bytes_accessed=4 * dq.size + 12 * own.size, transcendentals=0
        ),
    )(dq, own, picks, globs, cosines, sines, *backs)


def adam_kernel(batch, meta, rates, *refs):
    master_ref, first_ref, second_ref, left_ref, right_ref = refs[:5]
    sources = refs[5:-6]
    new_first_ref, new_second_ref, new_master_ref, copy_ref, tiles, arrived = refs[-6:]
    step, steps = pl.program_id(0), pl.num_programs(0)
    slot = step % 2

    def fetch(at_step, at_slot):
        for place in range(batch):
            tile = at_step * batch + place
            for number, source in enumerate(sources):

                @pl.when(meta[0, tile] == number)
                def _(source=source, tile=tile, place=place):
                    top = pl.multiple_of(meta[2, tile], BLK)
                    left = pl.multiple_of(meta[3, tile], BLK)
                    pltpu.make_async_copy(
                        source.at[meta[1, tile], pl.ds(top, BLK), pl.ds(left, BLK)],
                        tiles.at[at_slot, place],
                        arrived.at[at_slot],
                    ).start()

    @pl.when(step == 0)
    def _():
        fetch(0, 0)

    @pl.when(step + 1 < steps)
    def _():
        fetch(step + 1, 1 - slot)

    pltpu.make_async_copy(tiles.at[slot], tiles.at[slot], arrived.at[slot]).wait()
    places = range(batch)
    lefts = [left_ref[place].astype(jnp.bfloat16) for place in places]
    rights = [right_ref[place].astype(jnp.bfloat16) for place in places]
    turned = [over_first(lefts[place], tiles[slot, place]).astype(jnp.bfloat16) for place in places]
    rotated = [
        jnp.dot(turned[place], rights[place], preferred_element_type=jnp.float32) for place in places
    ]
    directions = []
    for place in places:
        new_first = beta_one * first_ref[place] + (1.0 - beta_one) * rotated[place]
        new_second = beta_two * second_ref[place] + (1.0 - beta_two) * rotated[place] * rotated[place]
        direction = (new_first * (1.0 / (1.0 - beta_one**STEP))) / (
            jnp.sqrt(new_second * (1.0 / (1.0 - beta_two**STEP))) + adam_eps
        )
        new_first_ref[place] = new_first
        new_second_ref[place] = new_second
        directions.append(direction.astype(jnp.bfloat16))
    updates = [
        jnp.dot(lefts[place], directions[place], preferred_element_type=jnp.float32) for place in places
    ]
    updates = [over_last(updates[place].astype(jnp.bfloat16), rights[place]) for place in places]
    for place in places:
        old = master_ref[place]
        new_master = old - rates[step * batch + place] * (updates[place] + weight_decay * old)
        new_master_ref[place] = new_master
        copy_ref[place] = new_master.astype(jnp.bfloat16)


def adam(meta, rates, state, sources):
    count = state[0].shape[0]
    batch = max(size for size in range(1, 33) if count % size == 0)
    block = pl.BlockSpec((batch, BLK, BLK), lambda s, *_: (s, 0, 0))
    anywhere = pl.BlockSpec(memory_space=pl.ANY)
    shape = (count, BLK, BLK)
    return pl.pallas_call(
        functools.partial(adam_kernel, batch),
        out_shape=[jax.ShapeDtypeStruct(shape, jnp.float32)] * 3
        + [jax.ShapeDtypeStruct(shape, jnp.bfloat16)],
        grid_spec=pltpu.PrefetchScalarGridSpec(
            num_scalar_prefetch=2,
            grid=(count // batch,),
            in_specs=[block] * 5 + [anywhere] * len(sources),
            out_specs=[block] * 4,
            scratch_shapes=[
                pltpu.VMEM((2, batch, BLK, BLK), jnp.bfloat16),
                pltpu.SemaphoreType.DMA((2,)),
            ],
        ),
        compiler_params=pltpu.CompilerParams(vmem_limit_bytes=56 * 2**20),
        cost_estimate=pl.CostEstimate(
            flops=8 * count * BLK**3, bytes_accessed=36 * count * BLK**2, transcendentals=0
        ),
    )(meta, rates, *state, *sources)


def per_device(
    block_input,
    cotangent,
    glob_select,
    assignment,
    master,
    first_moment,
    second_moment,
    left_basis,
    right_basis,
    gains,
    gain_first,
    gain_second,
):
    band_total = lax.axis_size("fsdp")
    rep_total = lax.axis_size("rep")
    place = lax.axis_index("rep")
    band = lax.axis_index("fsdp")
    heads = H // rep_total
    kv_heads = KVH // rep_total
    q_width = heads * HD
    kv_width = kv_heads * HD
    tok_count = block_input.shape[1]
    own_count = master.shape[1]
    tile_total = own_count * rep_total
    aligned = square() and whole_tiles(band_total, rep_total)
    tile_order = assignment[0]

    residual = block_input[0].astype(jnp.float32)
    grad_top = cotangent[0]
    position = band * tok_count + jnp.arange(tok_count, dtype=jnp.int32)
    cosine_table, sine_table = rope_tables(position)
    wide_cosine = jnp.concatenate([cosine_table, cosine_table], 1)[None]
    wide_sine = jnp.concatenate([sine_table, sine_table], 1)[None]
    scale_one = lax.rsqrt(jnp.mean(residual * residual, -1, keepdims=True) + norm_eps)
    normed_one = (residual * scale_one * gains[0]).astype(jnp.bfloat16)
    pick_rows = glob_select[0]
    glob_total = pick_rows.shape[0]
    selector = pick_rows.astype(jnp.bfloat16)
    glob_pos_part = jnp.sum(pick_rows * position[None, :], 1)
    digits = jnp.concatenate([glob_pos_part // 256, glob_pos_part % 256]).astype(jnp.bfloat16)
    digits = jnp.pad(digits[None], ((0, 7), (0, D - 2 * glob_total)))
    glob_rows = jnp.dot(selector, normed_one, preferred_element_type=jnp.float32).astype(jnp.bfloat16)
    glob_rows = add_all(jnp.concatenate([glob_rows, digits], 0), "fsdp").astype(jnp.bfloat16)
    packed = [normed_one, glob_rows, selector.reshape(-1, D)]
    packed = jnp.concatenate(packed, 0)
    packed = jnp.pad(packed, ((0, -packed.shape[0] % 32), (0, 0)))

    def over_bands(slice_rows):
        return lax.all_gather(slice_rows, "fsdp", axis=0, tiled=True)

    if aligned:
        half = BLK // 2
        low, high = (master[0, :, rows].astype(jnp.bfloat16) for rows in (slice(0, half), slice(half, BLK)))
        layout = slice_layout(band_total, rep_total)
        attn_layout = jnp.asarray(np.concatenate(layout[:4], 2))
        wanted = jnp.take(tile_order, by_place(attn_layout).reshape(-1), mode="clip")
        meta = jnp.stack([wanted // own_count == place, wanted % own_count], 0).astype(jnp.int32)
        attn_part = place_tiles(low, high, meta, *attn_layout.shape)
        attn_part = rep_scatter(attn_part).astype(jnp.bfloat16)
        low, attn_part = lax.optimization_barrier((low, attn_part))
        slots = square_pieces(low)
        attn = over_bands(attn_part)
        grids = [lax.dynamic_index_in_dim(jnp.asarray(grid), place, 0, False) for grid in layout]

        def find(wanted):
            wanted = jnp.take(tile_order, jnp.concatenate([grid.reshape(-1) for grid in wanted]), mode="clip")
            entry, row = (wanted // own_count) ^ place, wanted % own_count
            cut = own_count // 2
            high = (entry == 3) & (row >= cut)
            found = jnp.stack([jnp.where(high, 4, entry), jnp.where(high, row - cut, row)], 0)
            return found.astype(jnp.int32)

        all_grid = jnp.concatenate(grids[4:], 1)
        (first_part,) = gather_strips(slots, find([all_grid]), [all_grid.shape])
        packed, first_part, attn = lax.optimization_barrier((packed, first_part, attn))
        early = over_bands(first_part)
    packed_all = rep_gather(packed)
    if aligned:
        packed_all, high = lax.optimization_barrier((packed_all, high))
        later_slots = square_pieces(high)
    normed_one_all = packed_all[:, :tok_count].reshape(-1, D)
    at = tok_count + glob_total
    glob_digits = packed_all[:, at, : 2 * glob_total].astype(jnp.float32)
    glob_place = glob_digits[:, :glob_total] * 256.0 + glob_digits[:, glob_total:]
    at += 8
    selector_all = packed_all[:, at : at + selector.size // D].reshape(rep_total, glob_total, tok_count)

    if aligned:
        in_width = q_width + 2 * kv_width
        w_inner, w_output = attn[:, :in_width], attn[:, in_width:]
    else:
        slots = lax.all_gather(master[0].astype(jnp.bfloat16), "rep", axis=0, tiled=True)
        tiles = jnp.take(slots, tile_order, axis=0, mode="clip")
        slices = cut_slices(band_matrices(tiles, band_total), band_total, rep_total)
        w_inner = over_bands(jnp.concatenate(slices[0:3], 1))
        w_output = over_bands(slices[3])
        w_gate = over_bands(slices[4])
        w_up = over_bands(slices[5])
        w_down = over_bands(slices[6])

    w_output = by_place(w_output.reshape(rep_total, q_width, -1)).reshape(D, -1)

    def mul(rows, weight):
        return jnp.dot(rows, weight, preferred_element_type=jnp.float32)

    def mul_back(rows, weight):
        return lax.dot_general(rows, weight, (((1,), (1,)), ((), ())), preferred_element_type=jnp.float32)

    def weight_grad(rows, grad_rows):
        return lax.dot_general(
            rows, grad_rows, (((0,), (0,)), ((), ())), preferred_element_type=jnp.float32
        ).astype(jnp.bfloat16)

    def own_sum(partial):
        return rep_scatter(partial.astype(jnp.bfloat16).reshape(rep_total, tok_count, D))

    inner_rows = mul(packed_all.reshape(-1, D), w_inner).reshape(rep_total, -1, w_inner.shape[1])
    packed_all, normed_one_all = lax.optimization_barrier((packed_all, normed_one_all))
    queries, own_pairs = rope_rows(inner_rows, tok_count, 0, q_width, kv_width, wide_cosine, wide_sine)
    glob_cosine, glob_sine = rope_tables(glob_place.reshape(-1))
    glob_cosine = jnp.concatenate([glob_cosine, glob_cosine], 1).reshape(rep_total, glob_total, -1)
    glob_sine = jnp.concatenate([glob_sine, glob_sine], 1).reshape(rep_total, glob_total, -1)
    (glob_pairs,) = rope_rows(
        inner_rows, glob_total, tok_count // glob_total, q_width, kv_width, glob_cosine, glob_sine, False
    )
    back_count = (WINDOW + tok_count - 2) // tok_count
    odd = band % 2 == 1
    by_chip = back_count == 2 and band_total % 2 == 0
    if by_chip:
        two_back = shifted(own_pairs, "fsdp", 2)
        pair_blocks = [two_back, to_core(jnp.where(odd, two_back, own_pairs))]
    else:
        pair_blocks = [shifted(own_pairs, "fsdp", distance) for distance in range(back_count, 0, -1)]
    pair_blocks = pair_blocks + [own_pairs, glob_pairs]
    glob_spots = jnp.broadcast_to(glob_place[:, :, None], (rep_total, glob_total, BLK))
    band_number = band.astype(jnp.int32).reshape(1)
    attended_low, lse = attend(band_number, glob_spots, queries, pair_blocks)
    if aligned:
        *later_slots, attended_low, early = lax.optimization_barrier((*later_slots, attended_low, early))
        last_grid = jnp.concatenate(grids[4:6], 1)
        last_part, down_part = gather_strips(
            later_slots, find([last_grid, grids[6]]), [last_grid.shape, grids[6].shape]
        )

        def by_strips(gathered):
            return gathered.reshape(band_total, -1, all_grid.shape[0], half, gathered.shape[-1])

        early, late, late_down = by_strips(early), by_strips(over_bands(last_part)), by_strips(over_bands(down_part))
    attended_all = rep_features(attended_low).reshape(-1, D)
    columns = mul(attended_all, w_output).astype(jnp.bfloat16).reshape(rep_total, tok_count, -1)
    branch = by_place(rep_exchange(columns)).transpose(1, 0, 2).reshape(tok_count, D)
    middle = residual + branch.astype(jnp.float32)
    scale_two = lax.rsqrt(jnp.mean(middle * middle, -1, keepdims=True) + norm_eps)
    normed_two = (middle * scale_two * gains[1]).astype(jnp.bfloat16)
    normed_two_all = rep_gather(normed_two).reshape(-1, D)
    normed_two_all, grad_top_now = lax.optimization_barrier((normed_two_all, grad_top))
    top_first = gather_first(grad_top_now)

    if aligned:
        gate_rows, up_rows, activation = forward_products(normed_two_all, early, late, FF // rep_total)
        top_first, activation = after(top_first, activation)
        grad_top_all = gather_join(gather_second(top_first)).reshape(-1, D)
        g_down = weight_grad(activation, grad_top_all)
        grad_top_all, g_down = lax.optimization_barrier((grad_top_all, g_down))
        grad_gate, grad_up, pieces, branch_pieces = backward_products(
            grad_top_all, gate_rows, up_rows, activation, early, late, late_down
        )
        normed_first = sum_first(pieces)
        normed_first, g_gate = after(normed_first, weight_grad(normed_two_all, grad_gate))
        grad_normed_two = sum_second(normed_first)
    else:
        gate_rows = mul(normed_two_all, w_gate)
        up_rows = mul(normed_two_all, w_up)
        sigmoid_gate = jax.nn.sigmoid(gate_rows)
        silu_gate = gate_rows * sigmoid_gate
        activation = (silu_gate * up_rows).astype(jnp.bfloat16)
        grad_top_all = gather_join(gather_second(top_first)).reshape(-1, D)
        g_down = weight_grad(activation, grad_top_all)
        grad_act = mul_back(grad_top_all, w_down)
        grad_gate = (
            grad_act * up_rows * sigmoid_gate * (1.0 + gate_rows * (1.0 - sigmoid_gate))
        ).astype(jnp.bfloat16)
        grad_up = (grad_act * silu_gate).astype(jnp.bfloat16)
        grad_normed_two = own_sum(mul_back(grad_gate, w_gate) + mul_back(grad_up, w_up))
        branch_pieces = (mul(activation, w_down),)
        g_gate = weight_grad(normed_two_all, grad_gate)
    grad_normed_two, g_gate = lax.optimization_barrier((grad_normed_two, g_gate))

    def over_tokens(partial):
        return lax.psum_scatter(partial, "fsdp", scatter_dimension=0, tiled=True)

    s_down = over_tokens(g_down)
    s_gate = over_tokens(g_gate)

    grad_middle = grad_top.astype(jnp.float32) + norm_back(middle, scale_two, gains[1], grad_normed_two)
    grad_parts = grad_middle.astype(jnp.bfloat16).reshape(tok_count, rep_total, -1).transpose(1, 0, 2)
    grad_columns = rep_exchange(by_place(grad_parts)).reshape(rep_total * tok_count, -1)
    grad_columns, grad_up = lax.optimization_barrier((grad_columns, grad_up))
    def ready_grads():
        output = weight_grad(attended_all, grad_columns).reshape(rep_total, q_width, -1)
        return weight_grad(normed_two_all, grad_up), by_place(output).reshape(D, -1)

    grad_attended, (g_up, g_output) = rep_features_sum(
        grad_columns.reshape(rep_total, tok_count, -1), w_output, ready_grads
    )
    grad_attended = grad_attended.astype(jnp.bfloat16)
    (s_down, g_up, g_output), grad_attended = after((s_down, g_up, g_output), grad_attended)
    s_output = over_tokens(g_output)
    down_first = gather_first(s_down)
    grad_queries, *grad_blocks = attend_back(
        band_number, glob_spots, wide_cosine, wide_sine, queries, grad_attended, lse, pair_blocks
    )
    down_first, *grad_blocks = after(down_first, *grad_blocks)
    down_second = gather_second(down_first)
    branch_pieces, *down_second = after(tuple(branch_pieces), *down_second)
    branch_first = sum_first(branch_pieces) if aligned else (own_sum(branch_pieces[0]),)
    if by_chip:
        came = to_core(jnp.concatenate([grad_blocks[1], grad_blocks[-1]], 1))
        came, glob_came = came[:, :tok_count], came[:, tok_count:]
        total = grad_blocks[0].astype(jnp.float32) + came.astype(jnp.float32)
        sent = jnp.where(odd, total.astype(jnp.bfloat16), grad_blocks[0])
        returned = [shifted(sent, "fsdp", -2), jnp.where(odd, jnp.zeros_like(came), came)]
    else:
        returned = [
            shifted(grad_blocks[back_count - distance], "fsdp", -distance)
            for distance in range(1, back_count + 1)
        ]
    if by_chip:
        glob_both = grad_blocks[-1].astype(jnp.float32) + glob_came.astype(jnp.float32)
        glob_grads = add_all(glob_both.astype(jnp.bfloat16), "fsdp", 2)
    else:
        glob_grads = add_all(grad_blocks[-1], "fsdp")
    branch_first, g_up, glob_grads, s_gate, s_output, *returned = lax.optimization_barrier(
        (branch_first, g_up, glob_grads, s_gate, s_output, *returned)
    )
    s_up = over_tokens(g_up)
    s_down = gather_join(down_second)
    gate_first = gather_first(jnp.concatenate([s_gate, s_output], 1))
    block_out = middle + (sum_second(branch_first) if aligned else branch_first[0])
    grad_inner = join_grads(
        grad_queries, grad_blocks[-2], selector_all, glob_grads, wide_cosine, wide_sine, returned
    ).reshape(-1, q_width + 2 * kv_width)
    grad_normed_parts = mul_back(grad_inner, w_inner).astype(jnp.bfloat16).reshape(rep_total, tok_count, D)
    if square():
        normed_first = sum_first(split_pieces(grad_normed_parts))
    else:
        normed_first = (rep_scatter(grad_normed_parts),)
    grad_inner, grad_normed_parts = lax.optimization_barrier((grad_inner, grad_normed_parts))
    g_inner = weight_grad(normed_one_all, grad_inner)
    g_attn = with_layout_constraint(g_inner, Layout((0, 1)))
    gate_first, block_out, *normed_first = after(gate_first, block_out, *normed_first)
    gate_second = gather_second(gate_first)
    grad_normed_one = sum_second(normed_first) if square() else normed_first[0]
    gate_second, s_up, g_attn, grad_normed_one = after(gate_second, s_up, g_attn, grad_normed_one)
    s_attn = over_tokens(g_attn)
    s_gate = gather_join(gate_second)
    up_first = gather_first(s_up)
    grad_input = grad_middle + norm_back(residual, scale_one, gains[0], grad_normed_one)

    gain_terms = jnp.stack(
        [
            jnp.sum(grad_normed_one * residual * scale_one, 0),
            jnp.sum(grad_normed_two * middle * scale_two, 0),
        ]
    )
    square_terms = jnp.stack(
        [jnp.sum(residual * residual), jnp.sum(middle * middle), jnp.sum(block_out * block_out)]
    )
    sums = jnp.concatenate([gain_terms.reshape(-1), square_terms])

    up_first, sums = after(up_first, sums)
    s_up = gather_join(gather_second(up_first))
    sums = add_all(add_all(sums, "rep"), "fsdp")
    sums, s_attn, s_up, s_gate, s_down = lax.optimization_barrier((sums, s_attn, s_up, s_gate, s_down))
    gain_grad, square_total = sums[: 2 * D].reshape(2, D), sums[2 * D :]

    slot_ids = jnp.arange(tile_total, dtype=jnp.int32)
    inverse = jnp.sum(jnp.where(tile_order[None, :] == slot_ids[:, None], slot_ids[None, :], 0), 1)
    own_slots = place * own_count + jnp.arange(own_count, dtype=jnp.int32)
    owned_tiles = jnp.take(inverse, own_slots, mode="clip")
    if aligned:
        sources = [rep_gather(s_attn), s_gate, s_up, s_down]
        where = np.zeros((4, rep_total, tile_total), np.int32)
        first_col = 0
        for kind, grid in enumerate(layout):
            rows, cols = grid.shape[1:]
            first_col = 0 if kind >= 4 else FF // rep_total if kind == 3 else first_col
            for there in range(rep_total):
                numbers = grid[there].reshape(-1)
                at = np.arange(rows * cols)
                where[0, :, numbers] = 0 if kind < 3 else max(kind - 3, 1)
                where[2, :, numbers] = (at // cols * BLK)[:, None]
                where[3, :, numbers] = (at % cols * BLK + first_col)[:, None]
                for here in range(rep_total):
                    where[1, here, numbers] = here ^ there
            first_col += cols * BLK
        tile_spots = lax.dynamic_index_in_dim(jnp.asarray(where), place, 1, False)
        meta = jnp.take(tile_spots, owned_tiles, axis=1, mode="clip")
    else:
        splits = [0, q_width, q_width + kv_width, q_width + 2 * kv_width]
        stacks = [rep_gather(s_attn[:, low:high]) for low, high in zip(splits, splits[1:])]
        cut = FF // rep_total
        stacks += [s_gate[..., cut:], s_gate[..., :cut], s_up, s_down]
        sources = [band_tiles(join_slices(stacks, band_total, rep_total))]
        meta = jnp.stack([0 * owned_tiles, owned_tiles, 0 * owned_tiles, 0 * owned_tiles], 0)
    slot_rates = jnp.take(kind_rates(band_total), owned_tiles, mode="clip")
    new_first, new_second, new_master, master_copy = adam(
        meta,
        slot_rates,
        (master[0], first_moment[0], second_moment[0], left_basis[0], right_basis[0]),
        sources,
    )
    new_gain_first = beta_one * gain_first + (1.0 - beta_one) * gain_grad
    new_gain_second = beta_two * gain_second + (1.0 - beta_two) * gain_grad * gain_grad
    gain_step = (
        new_gain_first
        / (1.0 - beta_one**STEP)
        / (jnp.sqrt(new_gain_second / (1.0 - beta_two**STEP)) + adam_eps)
    )
    new_gains = gains - gain_rate * gain_step
    rms_stats = jnp.sqrt(square_total / (rep_total * band_total * tok_count * D))
    return (
        block_out[None],
        grad_input[None],
        new_first[None],
        new_second[None],
        new_master[None],
        master_copy[None],
        new_gain_first,
        new_gain_second,
        new_gains,
        rms_stats,
    )


def solution(mesh):
    in_specs = (
        P("rep", "fsdp", None),
        P("rep", "fsdp", None),
        P("rep", None, "fsdp"),
        P("fsdp", None),
        P("fsdp", "rep", None, None),
        P("fsdp", "rep", None, None),
        P("fsdp", "rep", None, None),
        P("fsdp", "rep", None, None),
        P("fsdp", "rep", None, None),
        P(),
        P(),
        P(),
    )
    out_specs = (
        P("rep", "fsdp", None),
        P("rep", "fsdp", None),
        P("fsdp", "rep", None, None),
        P("fsdp", "rep", None, None),
        P("fsdp", "rep", None, None),
        P("fsdp", "rep", None, None),
        P(),
        P(),
        P(),
        P(),
    )
    return jax.shard_map(
        per_device, mesh=mesh, in_specs=in_specs, out_specs=out_specs, check_vma=False
    )
```

```python
import functools

import jax
import jax.numpy as jnp
import numpy as np
from jax import lax
from jax.experimental import pallas as pl
from jax.experimental.layout import Layout, with_layout_constraint
from jax.experimental.pallas import tpu as pltpu
from jax.sharding import PartitionSpec as P

D = 2048
H = 32
KVH = 8
HD = 64
FF = 8192
WINDOW = 512
BLK = 128
STEP = 10


norm_eps = 1e-05
rope_theta = 500000.0
beta_one = 0.5
beta_two = 0.5
adam_eps = 1e-08
weight_decay = 0.1
gain_rate = 0.5
masked_value = -1e30


def matrix_shapes():
    kv_width = KVH * HD
    return [(D, D), (D, kv_width), (D, kv_width), (D, D), (D, FF), (D, FF), (FF, D)]


def kind_rates(band_total):
    rate_list = [
        D ** (-0.5),
        D ** (-0.5),
        D ** (-0.5),
        (D * 8 // WINDOW) ** (-0.5),
        D ** (-0.5),
        D ** (-0.5),
        FF ** (-0.5),
    ]
    pieces = []
    for (row_total, col_total), rate_value in zip(matrix_shapes(), rate_list):
        tile_count = row_total // band_total // BLK * (col_total // BLK)
        pieces.append(jnp.full((tile_count,), rate_value, jnp.float32))
    return jnp.concatenate(pieces)


def band_matrices(tiles, band_total):
    matrices = []
    offset = 0
    for row_total, col_total in matrix_shapes():
        band_rows = row_total // band_total
        tile_count = band_rows // BLK * (col_total // BLK)
        segment = tiles[offset : offset + tile_count].reshape(
            band_rows // BLK, col_total // BLK, BLK, BLK
        )
        matrices.append(segment.transpose(0, 2, 1, 3).reshape(band_rows, col_total))
        offset += tile_count
    return matrices


def band_tiles(matrices):
    pieces = []
    for matrix in matrices:
        row_count, col_count = matrix.shape
        segment = matrix.reshape(row_count // BLK, BLK, col_count // BLK, BLK).transpose(0, 2, 1, 3)
        pieces.append(segment.reshape(-1, BLK, BLK))
    return jnp.concatenate(pieces, 0)


def rope_tables(position):
    halves = jnp.arange(HD // 2, dtype=jnp.float32) * (2.0 / HD)
    frequency = rope_theta ** (-halves)
    angles = position.astype(jnp.float32)[:, None] * frequency[None, :]
    angles = jnp.concatenate([angles, angles], 1)
    return (jnp.cos(angles), jnp.sin(angles))


def rotate(vectors, cosine_table, sine_table):
    half_width = vectors.shape[-1] // 2
    turned = jnp.concatenate([-vectors[..., half_width:], vectors[..., :half_width]], -1)
    return vectors * cosine_table[:, None, :] + turned * sine_table[:, None, :]


def rotate_back(grad_rows, cosine_table, sine_table):
    half_width = grad_rows.shape[-1] // 2
    scaled = grad_rows * sine_table[:, None, :]
    turned = jnp.concatenate([scaled[..., half_width:], -scaled[..., :half_width]], -1)
    return grad_rows * cosine_table[:, None, :] + turned


def norm_back(values, row_scale, gain_row, grad_rows):
    weighted = grad_rows * gain_row
    return row_scale * weighted - values * row_scale**3 * jnp.mean(
        weighted * values, -1, keepdims=True
    )


def to_rep(block, distance):
    route = [(i, i ^ distance) for i in range(lax.axis_size("rep"))]
    return lax.ppermute(block, "rep", route)


def square():
    return lax.axis_size("rep") == 4


def gather_first(block):
    if not square():
        return (lax.all_gather(block, "rep", axis=0),)
    return block, to_rep(block, 1), to_rep(block, 2)


def gather_second(first):
    if not square():
        return first
    block, near, far = first
    cut = block.shape[0] // 2
    return block, near, far, to_rep(near[:cut], 2), to_rep(far[cut:], 1)


def gather_join(pieces):
    if not square():
        return pieces[0]
    return jnp.concatenate(pieces, 0).reshape((4,) + pieces[0].shape)


def square_pieces(block):
    return gather_second(gather_first(block))


def rep_gather(block):
    return gather_join(gather_second(gather_first(block)))


def after(values, *others):
    count = len(values)
    tied = lax.optimization_barrier((*values, *others))
    return tuple(tied[:count]), *tied[count:]


def rep_of(entry):
    place = lax.axis_index("rep")
    return place ^ entry if square() else entry


def rep_scatter(parts):
    if not square():
        flat = parts.reshape(-1, parts.shape[-1])
        return lax.psum_scatter(flat, "rep", scatter_dimension=0, tiled=True).astype(jnp.float32)
    return sum_pieces(*split_pieces(parts))


def split_pieces(parts):
    half = parts.shape[-1] // 2
    low, high = parts[..., :half], parts[..., half:]
    return jnp.stack([low[0], low[2]], 0), jnp.stack([low[1], low[3]], 0), high[:2], high[2:]


def sum_first(pieces):
    low_kept, low_sent, high_kept, high_sent = pieces
    parts = []
    for kept, sent, first in ((low_kept, low_sent, 1), (high_kept, high_sent, 2)):
        came = to_rep(sent, first)
        parts.append(kept[0].astype(jnp.float32) + came[0].astype(jnp.float32))
        parts.append((kept[1].astype(jnp.float32) + came[1].astype(jnp.float32)).astype(kept.dtype))
    return tuple(parts)


def sum_second(parts):
    low, low_other, high, high_other = parts
    low = low + to_rep(low_other, 2).astype(jnp.float32)
    high = high + to_rep(high_other, 1).astype(jnp.float32)
    return jnp.concatenate([low, high], -1)


def sum_pieces(*pieces):
    return sum_second(sum_first(pieces))


def add_all(value, axis, distance=1):
    size = lax.axis_size(axis)
    total = value.astype(jnp.float32)
    while distance < size:
        count = 2 if (size // distance).bit_length() % 2 == 0 else 4
        low = total.astype(value.dtype)
        others = []
        for step in range(1, count):
            route = [(i, i ^ (step * distance)) for i in range(size)]
            others.append(lax.ppermute(low, axis, route).astype(jnp.float32))
        total = total + others[0]
        if count == 4:
            total = total + (others[1] + others[2])
        distance *= count
    return total


def rep_features(block):
    if not square():
        return lax.all_gather(block, "rep", axis=2, tiled=True)
    own, near, far, low, high = square_pieces(block)
    return jnp.concatenate(
        [
            own,
            jnp.stack([near[1], near[0], near[3], near[2]], 0),
            jnp.stack([far[2], far[3], far[0], far[1]], 0),
            jnp.stack([high[1], high[0], low[1], low[0]], 0),
        ],
        2,
    )


def write_pieces(entry, rows, values, refs):
    low_kept, low_sent, high_kept, high_sent = refs
    half = low_kept.shape[-1]
    values = values.astype(jnp.bfloat16)
    (low_sent if entry % 2 else low_kept)[entry // 2, rows] = values[:, :half]
    (high_sent if entry // 2 else high_kept)[entry % 2, rows] = values[:, half:]


def swapped_kernel(x_ref, w_ref, *refs):
    reps, rows, _ = x_ref.shape
    width = w_ref.shape[0] // reps
    for entry in range(reps):
        weight = w_ref[entry * width : (entry + 1) * width]
        for there in range(reps):
            product = over_last(x_ref[there ^ entry], weight)
            write_pieces(entry, slice(there * rows, (there + 1) * rows), product, refs)


def rep_features_sum(columns, weight, meanwhile):
    reps, rows, depth = columns.shape
    width = weight.shape[0] // reps
    if square():
        pieces = pl.pallas_call(
            swapped_kernel,
            out_shape=[jax.ShapeDtypeStruct((2, reps * rows, width // 2), jnp.bfloat16)] * 4,
            compiler_params=pltpu.CompilerParams(vmem_limit_bytes=32 * 2**20),
            cost_estimate=pl.CostEstimate(
                flops=2 * reps * columns.size * width,
                bytes_accessed=10 * columns.size,
                transcendentals=0,
            ),
        )(columns, weight)
        first = sum_first(pieces)
        first, other = after(first, meanwhile())
        total = sum_second(first)
    else:
        other = meanwhile()
        product = over_last(columns.reshape(-1, depth), weight).astype(jnp.bfloat16)
        swapped = product.reshape(reps, rows, reps, width).transpose(2, 0, 1, 3)
        total = rep_scatter(swapped.reshape(reps, reps * rows, width))
    return total.reshape(reps, rows, width), other


def rep_exchange(parts):
    if not square():
        return lax.all_to_all(parts, "rep", 0, 0)
    return jnp.stack([parts[0]] + [to_rep(parts[entry], entry) for entry in (1, 2, 3)], 0)


def by_place(parts):
    entries = [rep_of(entry) for entry in range(parts.shape[0])]
    return jnp.stack([lax.dynamic_index_in_dim(parts, entry, 0, False) for entry in entries], 0)


def to_core(block):
    return lax.ppermute(block, "fsdp", [(i, i ^ 1) for i in range(lax.axis_size("fsdp"))])


def shifted(block, axis, distance):
    devices = range(lax.axis_size(axis))
    route = [(i - distance, i) for i in devices if i - distance in devices]
    return lax.ppermute(block, axis, route)


def tile_offsets(band_total):
    offsets = [0]
    for row_total, col_total in matrix_shapes():
        offsets.append(offsets[-1] + row_total // band_total // BLK * (col_total // BLK))
    return offsets


def whole_tiles(band_total, rep_total):
    return KVH * HD // rep_total % BLK == 0 and FF // band_total // rep_total % BLK == 0


def slice_layout(band_total, rep_total):
    offsets = tile_offsets(band_total)
    layout = []
    for kind, (row_total, col_total) in enumerate(matrix_shapes()):
        rows, cols = row_total // band_total // BLK, col_total // BLK
        grid = offsets[kind] + np.arange(rows * cols).reshape(rows, cols)
        if kind == 6:
            layout.append(grid.reshape(rep_total, rows // rep_total, cols))
        elif kind in (4, 5):
            cut = grid.reshape(rows, band_total, rep_total, -1).transpose(2, 0, 1, 3)
            layout.append(cut.reshape(rep_total, rows, -1))
        else:
            layout.append(grid.reshape(rows, rep_total, -1).transpose(1, 0, 2))
    return layout


def tiles_to_matrix(tiles):
    rows, cols = tiles.shape[:2]
    return tiles.transpose(0, 2, 1, 3).reshape(rows * BLK, cols * BLK)


def matrix_to_tiles(matrix):
    rows, cols = matrix.shape
    cut = matrix.reshape(rows // BLK, BLK, cols // BLK, BLK)
    return cut.transpose(0, 2, 1, 3).reshape(-1, BLK, BLK)


def cut_slices(matrices, band_total, rep_total):
    place = lax.axis_index("rep")
    slices = []
    for kind, matrix in enumerate(matrices):
        rows, cols = matrix.shape
        if kind == 6:
            slices.append(lax.dynamic_slice_in_dim(matrix, place * (rows // rep_total), rows // rep_total, 0))
        elif kind in (4, 5):
            cut = matrix.reshape(rows, band_total, rep_total, -1)
            slices.append(lax.dynamic_index_in_dim(cut, place, 2, False).reshape(rows, -1))
        else:
            slices.append(lax.dynamic_slice_in_dim(matrix, place * (cols // rep_total), cols // rep_total, 1))
    return slices


def join_slices(stacks, band_total, rep_total):
    matrices = []
    for kind, stack in enumerate(stacks):
        rows, cols = stack.shape[1:]
        if kind == 6:
            matrices.append(stack.reshape(-1, cols))
        elif kind in (4, 5):
            cut = stack.reshape(rep_total, rows, band_total, -1).transpose(1, 2, 0, 3)
            matrices.append(cut.reshape(rows, -1))
        else:
            matrices.append(stack.transpose(1, 0, 2).reshape(rows, -1))
    return matrices


def gather_kernel(grids, meta, *refs):
    source_total = len(refs) - len(grids) - 1
    sources, targets, done = refs[:source_total], refs[source_total:-1], refs[-1]
    height = sources[0].shape[1]
    start = 0
    for place, (target, (rows, cols)) in enumerate(zip(targets, grids)):

        def one(tile, carry, target=target, rows=rows, cols=cols, start=start, place=place):
            kind = meta[0, start + tile]
            row = meta[1, start + tile]
            across = tile % cols
            top = pl.multiple_of((across // 2 * rows + tile // cols) * height, height)
            left = pl.multiple_of(across % 2 * BLK, BLK)
            for number, source in enumerate(sources):

                @pl.when(kind == number)
                def _(source=source):
                    pltpu.make_async_copy(
                        source.at[row], target.at[pl.ds(top, height), pl.ds(left, BLK)], done.at[place]
                    ).start()

            return carry

        lax.fori_loop(0, rows * cols, one, 0)
        start += rows * cols
    for place, target in enumerate(targets):
        pltpu.make_async_copy(target, target, done.at[place]).wait()


def gather_strips(sources, meta, grids):
    anywhere = pl.BlockSpec(memory_space=pl.ANY)
    height = sources[0].shape[1]
    out_shape = [
        jax.ShapeDtypeStruct((cols // 2 * rows * height, 2 * BLK), jnp.bfloat16) for rows, cols in grids
    ]
    return pl.pallas_call(
        functools.partial(gather_kernel, grids),
        out_shape=out_shape,
        grid_spec=pltpu.PrefetchScalarGridSpec(
            num_scalar_prefetch=1,
            grid=(1,),
            in_specs=[anywhere] * len(sources),
            out_specs=[pl.BlockSpec(shape.shape, lambda i, *_: (0, 0)) for shape in out_shape],
            scratch_shapes=[pltpu.SemaphoreType.DMA((len(grids),))],
        ),
        compiler_params=pltpu.CompilerParams(vmem_limit_bytes=32 * 2**20),
        cost_estimate=pl.CostEstimate(
            flops=0, bytes_accessed=sum(4 * shape.size for shape in out_shape), transcendentals=0
        ),
    )(meta, *sources)


def place_kernel(entries, rows, cols, meta, low, high, out_ref, done):
    out_ref[...] = jnp.zeros_like(out_ref)
    height = low.shape[1]

    def copies(tile):
        entry, rest = tile // (rows * cols), tile % (rows * cols)
        top = rest // cols * (2 * height)
        left = pl.multiple_of(rest % cols * BLK, BLK)
        return [
            pltpu.make_async_copy(
                half.at[meta[1, tile]],
                out_ref.at[entry, pl.ds(pl.multiple_of(top + part * height, height), height), pl.ds(left, BLK)],
                done.at[part],
            )
            for part, half in enumerate((low, high))
        ]

    def begin(tile, carry):
        @pl.when(meta[0, tile] == 1)
        def _():
            for copy in copies(tile):
                copy.start()

        return carry

    def finish(tile, carry):
        @pl.when(meta[0, tile] == 1)
        def _():
            for copy in copies(tile):
                copy.wait()

        return carry

    lax.fori_loop(0, entries * rows * cols, begin, 0)
    lax.fori_loop(0, entries * rows * cols, finish, 0)


def place_tiles(low, high, meta, entries, rows, cols):
    shape = (entries, rows * BLK, cols * BLK)
    anywhere = pl.BlockSpec(memory_space=pl.ANY)
    return pl.pallas_call(
        functools.partial(place_kernel, entries, rows, cols),
        out_shape=jax.ShapeDtypeStruct(shape, jnp.bfloat16),
        grid_spec=pltpu.PrefetchScalarGridSpec(
            num_scalar_prefetch=1,
            grid=(1,),
            in_specs=[anywhere, anywhere],
            out_specs=pl.BlockSpec(shape, lambda i, *_: (0, 0, 0)),
            scratch_shapes=[pltpu.SemaphoreType.DMA((2,))],
        ),
        compiler_params=pltpu.CompilerParams(vmem_limit_bytes=32 * 2**20),
        cost_estimate=pl.CostEstimate(
            flops=0, bytes_accessed=4 * entries * rows * cols * BLK * BLK, transcendentals=0
        ),
    )(meta, low, high)


def half_turn(values):
    lane = lax.broadcasted_iota(jnp.int32, values.shape, 1)
    lanes = values.shape[1]
    first = lane % HD < HD // 2
    return first, jnp.where(
        first, pltpu.roll(values, lanes - HD // 2, 1), pltpu.roll(values, HD // 2, 1)
    )


def strip_copies(early, late, target, done):
    return [
        pltpu.make_async_copy(half, target.at[:, :, number], done.at[number])
        for number, half in enumerate((early, late))
    ]


def forward_kernel(x_ref, early, late, gate_ref, up_ref, act_ref, weights, done):
    step, steps = pl.program_id(0), pl.num_programs(0)
    slot = step % 2
    width = weights.shape[-1]

    def copies(number, at_step, at_slot):
        strip = number * steps + at_step
        return strip_copies(
            early.at[:, strip], late.at[:, strip], weights.at[number, at_slot], done.at[number, at_slot]
        )

    def fetch(at_step, at_slot):
        for number in range(2):
            for copy in copies(number, at_step, at_slot):
                copy.start()

    @pl.when(step == 0)
    def _():
        fetch(0, 0)

    @pl.when(step + 1 < steps)
    def _():
        fetch(step + 1, 1 - slot)

    for number in range(2):
        for copy in copies(number, step, slot):
            copy.wait()
    gate_weight, up_weight = (weights[number, slot].reshape(-1, width) for number in range(2))
    chunk = min(2 * BLK, x_ref.shape[0])
    for first in range(0, x_ref.shape[0], chunk):
        rows = slice(first, first + chunk)
        gate = jnp.dot(x_ref[rows], gate_weight, preferred_element_type=jnp.float32)
        up = jnp.dot(x_ref[rows], up_weight, preferred_element_type=jnp.float32)
        gate_ref[rows] = gate.astype(jnp.bfloat16)
        up_ref[rows] = up.astype(jnp.bfloat16)
        act_ref[rows] = (gate * jax.nn.sigmoid(gate) * up).astype(jnp.bfloat16)


def forward_products(rows, early, late, columns):
    tokens, depth = rows.shape
    bands, _, tiles, half, width = early.shape
    block = pl.BlockSpec((tokens, width), lambda n: (0, n))
    anywhere = pl.BlockSpec(memory_space=pl.ANY)
    return pl.pallas_call(
        forward_kernel,
        out_shape=[jax.ShapeDtypeStruct((tokens, columns), jnp.bfloat16)] * 3,
        grid=(columns // width,),
        in_specs=[pl.BlockSpec(rows.shape, lambda n: (0, 0)), anywhere, anywhere],
        out_specs=[block] * 3,
        scratch_shapes=[
            pltpu.VMEM((2, 2, bands, tiles, 2, half, width), jnp.bfloat16),
            pltpu.SemaphoreType.DMA((2, 2, 2)),
        ],
        compiler_params=pltpu.CompilerParams(vmem_limit_bytes=48 * 2**20),
        cost_estimate=pl.CostEstimate(
            flops=tokens * depth * columns // 8, bytes_accessed=2 * rows.size, transcendentals=0
        ),
    )(rows, early, late)


def backward_kernel(top_ref, gate_ref, up_ref, act_ref, early, late, late_down, *refs):
    dgate_ref, dup_ref = refs[:2]
    pieces, branch_pieces = refs[2:6], refs[6:10]
    weights, downs, total, branch, done, down_done = refs[10:]
    step, steps = pl.program_id(0), pl.num_programs(0)
    slot = step % 2
    strips, width = downs.shape[1], downs.shape[-1]

    def down_copies(at_step, at_slot):
        wanted = pl.ds(2 * steps, strips)
        return strip_copies(
            early.at[at_step, wanted], late_down.at[at_step], downs.at[at_slot], down_done.at[at_slot]
        )

    def copies(number, at_step, at_slot):
        strip = number * steps + at_step
        return strip_copies(
            early.at[:, strip], late.at[:, strip], weights.at[number, at_slot], done.at[number, at_slot]
        )

    def fetch(at_step, at_slot):
        for copy in down_copies(at_step, at_slot):
            copy.start()
        for number in range(2):
            for copy in copies(number, at_step, at_slot):
                copy.start()

    @pl.when(step == 0)
    def _():
        fetch(0, 0)
        total[...] = jnp.zeros_like(total)
        branch[...] = jnp.zeros_like(branch)

    @pl.when(step + 1 < steps)
    def _():
        fetch(step + 1, 1 - slot)

    for copy in down_copies(step, slot):
        copy.wait()
    for number in range(2):
        for copy in copies(number, step, slot):
            copy.wait()
    gate_weight, up_weight = (weights[number, slot].reshape(-1, width) for number in range(2))
    chunk = min(4 * BLK, top_ref.shape[0])
    for first in range(0, top_ref.shape[0], chunk):
        rows = slice(first, first + chunk)
        grad_act = 0.0
        for strip in range(strips):
            lanes = slice(strip * width, (strip + 1) * width)
            down = downs[slot, strip].reshape(-1, width)
            grad_act = grad_act + over_last(top_ref[rows, lanes], down)
            branch[rows, lanes] += jnp.dot(act_ref[rows], down, preferred_element_type=jnp.float32)
        gate = gate_ref[rows].astype(jnp.float32)
        up = up_ref[rows].astype(jnp.float32)
        sigmoid_gate = jax.nn.sigmoid(gate)
        grad_gate = grad_act * up * sigmoid_gate * (1.0 + gate * (1.0 - sigmoid_gate))
        grad_gate = grad_gate.astype(jnp.bfloat16)
        grad_up = (grad_act * (gate * sigmoid_gate)).astype(jnp.bfloat16)
        dgate_ref[rows] = grad_gate
        dup_ref[rows] = grad_up
        total[rows] += over_last(grad_gate, gate_weight) + over_last(grad_up, up_weight)

    @pl.when(step == steps - 1)
    def _():
        rows = total.shape[0] // 4
        for entry in range(4):
            part = slice(entry * rows, (entry + 1) * rows)
            write_pieces(entry, slice(0, rows), total[part], pieces)
            write_pieces(entry, slice(0, rows), branch[part], branch_pieces)


def backward_products(top, gate, up, act, early, late, late_down):
    tokens, depth = top.shape
    columns = gate.shape[1]
    bands, _, tiles, half, width = early.shape
    strips = depth // width
    block = pl.BlockSpec((tokens, width), lambda n: (0, n))
    anywhere = pl.BlockSpec(memory_space=pl.ANY)
    piece = jax.ShapeDtypeStruct((2, tokens // 4, depth // 2), jnp.bfloat16)
    grads = jax.ShapeDtypeStruct((tokens, columns), jnp.bfloat16)
    outs = pl.pallas_call(
        backward_kernel,
        out_shape=[grads] * 2 + [piece] * 8,
        grid=(columns // width,),
        in_specs=[pl.BlockSpec(top.shape, lambda n: (0, 0))] + [block] * 3 + [anywhere] * 3,
        out_specs=[block] * 2 + [pl.BlockSpec(piece.shape, lambda n: (0, 0, 0))] * 8,
        scratch_shapes=[
            pltpu.VMEM((2, 2, bands, tiles, 2, half, width), jnp.bfloat16),
            pltpu.VMEM((2, strips, tiles, 2, half, width), jnp.bfloat16),
            pltpu.VMEM((tokens, depth), jnp.float32),
            pltpu.VMEM((tokens, depth), jnp.float32),
            pltpu.SemaphoreType.DMA((2, 2, 2)),
            pltpu.SemaphoreType.DMA((2, 2)),
        ],
        compiler_params=pltpu.CompilerParams(vmem_limit_bytes=60 * 2**20),
        cost_estimate=pl.CostEstimate(
            flops=8 * tokens * depth * columns, bytes_accessed=8 * columns * depth, transcendentals=0
        ),
    )(top, gate, up, act, early, late, late_down)
    return outs[0], outs[1], outs[2:6], outs[6:10]


def rope_kernel(q_width, kv_width, x_ref, cos_ref, sin_ref, *outs):
    width = x_ref.shape[-1]
    for start in range(0, width, BLK):
        values = x_ref[0, :, start : start + BLK]
        first, turned = half_turn(values)
        sines = sin_ref[0]
        turned_rows = values * cos_ref[0] + turned * jnp.where(first, -sines, sines)
        if start + BLK > q_width + kv_width:
            column = lax.broadcasted_iota(jnp.int32, values.shape, 1) + start
            turned_rows = jnp.where(column >= q_width + kv_width, values, turned_rows)
        if start < q_width:
            outs[0][0, :, start : start + BLK] = (turned_rows * HD ** (-0.5)).astype(jnp.bfloat16)
        else:
            outs[-1][0, :, start - q_width : start - q_width + BLK] = turned_rows.astype(jnp.bfloat16)


def rope_rows(inner, rows, row_block, q_width, kv_width, cosines, sines, with_queries=True):
    seqs, _, width = inner.shape
    shared = cosines.shape[0] == 1
    table = pl.BlockSpec((1, rows, BLK), lambda s: (0 if shared else s, 0, 0))
    widths = [q_width, 2 * kv_width]
    column_block = 0
    if not with_queries:
        width, column_block = 2 * kv_width, q_width // (2 * kv_width)
        widths, q_width = widths[1:], 0
    return pl.pallas_call(
        functools.partial(rope_kernel, q_width, kv_width),
        out_shape=[jax.ShapeDtypeStruct((seqs, rows, w), jnp.bfloat16) for w in widths],
        grid=(seqs,),
        in_specs=[pl.BlockSpec((1, rows, width), lambda s: (s, row_block, column_block)), table, table],
        out_specs=[pl.BlockSpec((1, rows, w), lambda s: (s, 0, 0)) for w in widths],
        cost_estimate=pl.CostEstimate(
            flops=6 * seqs * rows * width, bytes_accessed=6 * seqs * rows * width, transcendentals=0
        ),
    )(inner, cosines, sines)


def fill_bias(band_ref, gpos_ref, bias_ref, rows, window_len):
    band = band_ref[0]

    @pl.when(pl.program_id(0) == 0)
    def _():
        key = lax.broadcasted_iota(jnp.int32, (window_len, rows), 0) + (
            band * rows - (window_len - rows)
        )
        query = lax.broadcasted_iota(jnp.int32, (window_len, rows), 1) + band * rows
        inside = (key > query - WINDOW) & (key <= query) & (key >= 0)
        bias_ref[:window_len] = jnp.where(inside, 0.0, masked_value)

    glob_total = gpos_ref.shape[1]
    query = lax.broadcasted_iota(jnp.int32, (glob_total, rows), 1) + (band * rows - WINDOW)
    spot = jnp.broadcast_to(gpos_ref[0][:, :1], (glob_total, rows))
    bias_ref[window_len:] = jnp.where(spot <= query.astype(jnp.float32), 0.0, masked_value)


def over_last(left, right):
    return lax.dot_general(left, right, (((1,), (1,)), ((), ())), preferred_element_type=jnp.float32)


def over_first(left, right):
    return lax.dot_general(left, right, (((0,), (0,)), ((), ())), preferred_element_type=jnp.float32)


def attend_kernel(block_total, band_ref, gpos_ref, q_ref, *refs):
    blocks, (out_ref, lse_ref, bias_ref) = refs[:block_total], refs[block_total:]
    rows, q_width = q_ref.shape[1:]
    kv_width = blocks[0].shape[2] // 2
    heads, group = q_width // HD, q_width // kv_width
    window_len = rows * (block_total - 1)
    fill_bias(band_ref, gpos_ref, bias_ref, rows, window_len)
    starts = [rows * number for number in range(block_total)]
    pending = []
    for head in range(heads):
        left = head // group * HD
        queries = q_ref[0, :, head * HD : (head + 1) * HD]
        scores = [
            over_last(block[0, :, left : left + HD], queries)
            + bias_ref[start : start + block.shape[1]]
            for block, start in zip(blocks, starts)
        ]
        top = functools.reduce(jnp.maximum, [jnp.max(part, 0, keepdims=True) for part in scores])
        total = 0.0
        mixed = 0.0
        for block, part in zip(blocks, scores):
            weights = jnp.exp(part - top)
            total = total + jnp.sum(weights, 0, keepdims=True)
            mixed = mixed + over_first(
                block[0, :, kv_width + left : kv_width + left + HD], weights.astype(jnp.bfloat16)
            )
        lse_ref[0, head : head + 1, :] = top + jnp.log(total)
        pending.append(mixed / total)
        if len(pending) * HD == BLK or head == heads - 1:
            stop = (head + 1) * HD
            both = jnp.concatenate(pending, 0).T
            out_ref[0, :, stop - both.shape[1] : stop] = both.astype(jnp.bfloat16)
            pending = []


def attend(band, gpos, queries, blocks):
    seqs, rows, q_width = queries.shape
    heads = q_width // HD
    key_total = sum(block.shape[1] for block in blocks)

    def whole(array):
        return pl.BlockSpec((1,) + array.shape[1:], lambda s, *_: (s, 0, 0))

    out_shape = [
        jax.ShapeDtypeStruct((seqs, rows, q_width), jnp.bfloat16),
        jax.ShapeDtypeStruct((seqs, heads, rows), jnp.float32),
    ]
    return pl.pallas_call(
        functools.partial(attend_kernel, len(blocks)),
        out_shape=out_shape,
        grid_spec=pltpu.PrefetchScalarGridSpec(
            num_scalar_prefetch=1,
            grid=(seqs,),
            in_specs=[whole(array) for array in (gpos, queries, *blocks)],
            out_specs=[whole(array) for array in out_shape],
            scratch_shapes=[pltpu.VMEM((key_total, rows), jnp.float32)],
        ),
        compiler_params=pltpu.CompilerParams(vmem_limit_bytes=48 * 2**20),
        cost_estimate=pl.CostEstimate(
            flops=16 * seqs * heads * rows * key_total * HD,
            bytes_accessed=4 * queries.size,
            transcendentals=seqs * heads * rows * key_total,
        ),
    )(band, gpos, queries, *blocks)


def attend_back_kernel(block_total, band_ref, gpos_ref, cos_ref, sin_ref, q_ref, grad_ref, lse_ref, *refs):
    blocks = refs[:block_total]
    dq_ref = refs[block_total]
    out_refs = refs[block_total + 1 : 2 * block_total + 1]
    bias_ref = refs[-1]
    rows, q_width = q_ref.shape[1:]
    kv_width = blocks[0].shape[2] // 2
    heads, group = q_width // HD, q_width // kv_width
    window_len = rows * (block_total - 1)
    fill_bias(band_ref, gpos_ref, bias_ref, rows, window_len)
    starts = [rows * number for number in range(block_total)]
    pending = []
    for kv_head in range(kv_width // HD):
        left = kv_head * HD
        key_sums = [0.0] * block_total
        value_sums = [0.0] * block_total
        for head in range(kv_head * group, (kv_head + 1) * group):
            queries = q_ref[0, :, head * HD : (head + 1) * HD]
            grads = grad_ref[0, :, head * HD : (head + 1) * HD]
            lse = lse_ref[0, head : head + 1, :]
            soft, soft_grads = [], []
            inner = 0.0
            for number, (block, start) in enumerate(zip(blocks, starts)):
                part = over_last(block[0, :, left : left + HD], queries)
                part = jnp.exp(part + bias_ref[start : start + block.shape[1]] - lse)
                slope = over_last(block[0, :, kv_width + left : kv_width + left + HD], grads)
                inner = inner + jnp.sum(part * slope, 0, keepdims=True)
                soft.append(part)
                soft_grads.append(slope)
            turned = 0.0
            for number, block in enumerate(blocks):
                score_grads = (soft[number] * (soft_grads[number] - inner)).astype(jnp.bfloat16)
                value_sums[number] = value_sums[number] + jnp.dot(
                    soft[number].astype(jnp.bfloat16), grads, preferred_element_type=jnp.float32
                )
                key_sums[number] = key_sums[number] + jnp.dot(
                    score_grads, queries, preferred_element_type=jnp.float32
                )
                turned = turned + over_first(block[0, :, left : left + HD], score_grads)
            pending.append(turned)
            if len(pending) * HD == BLK or head == heads - 1:
                stop = (head + 1) * HD
                both = jnp.concatenate(pending, 0).T * HD ** (-0.5)
                pending = []
                first, other = half_turn(both * sin_ref[0])
                both = both * cos_ref[0] + jnp.where(first, other, -other)
                dq_ref[0, :, stop - both.shape[1] : stop] = both.astype(jnp.bfloat16)
        for number, out_ref in enumerate(out_refs):
            out_ref[0, :, left : left + HD] = key_sums[number].astype(out_ref.dtype)
            out_ref[0, :, kv_width + left : kv_width + left + HD] = value_sums[number].astype(
                out_ref.dtype
            )


def attend_back(band, gpos, cosines, sines, queries, grads, lse, blocks):
    seqs, rows, q_width = queries.shape
    heads = q_width // HD
    key_total = sum(block.shape[1] for block in blocks)

    def whole(array):
        return pl.BlockSpec((1,) + array.shape[1:], lambda s, *_: (s, 0, 0))

    table = pl.BlockSpec((1, rows, BLK), lambda s, *_: (0, 0, 0))
    out_shape = [jax.ShapeDtypeStruct(queries.shape, jnp.bfloat16)]
    for number, block in enumerate(blocks):
        own = number == len(blocks) - 2
        out_shape.append(jax.ShapeDtypeStruct(block.shape, jnp.float32 if own else jnp.bfloat16))
    return pl.pallas_call(
        functools.partial(attend_back_kernel, len(blocks)),
        out_shape=out_shape,
        grid_spec=pltpu.PrefetchScalarGridSpec(
            num_scalar_prefetch=1,
            grid=(seqs,),
            in_specs=[whole(gpos), table, table]
            + [whole(array) for array in (queries, grads, lse, *blocks)],
            out_specs=[whole(array) for array in out_shape],
            scratch_shapes=[pltpu.VMEM((key_total, rows), jnp.float32)],
        ),
        compiler_params=pltpu.CompilerParams(vmem_limit_bytes=48 * 2**20),
        cost_estimate=pl.CostEstimate(
            flops=40 * seqs * heads * rows * key_total * HD,
            bytes_accessed=8 * queries.size,
            transcendentals=seqs * heads * rows * key_total,
        ),
    )(band, gpos, cosines, sines, queries, grads, lse, *blocks)


def join_kernel(q_width, kv_width, dq_ref, own_ref, pick_ref, glob_ref, cos_ref, sin_ref, *refs):
    back_refs, out_ref = refs[:-1], refs[-1]
    out_ref[0, :, :q_width] = dq_ref[0]
    picked = lax.dot_general(
        pick_ref[0].astype(jnp.float32),
        glob_ref[0],
        (((0,), (0,)), ((), ())),
        precision=lax.Precision.HIGHEST,
        preferred_element_type=jnp.float32,
    )
    for start in range(0, 2 * kv_width, BLK):
        lanes = slice(start, start + BLK)
        total = own_ref[0, :, lanes] + picked[:, lanes]
        for back_ref in back_refs:
            total = total + back_ref[0, :, lanes].astype(jnp.float32)
        first, other = half_turn(total * sin_ref[0])
        turned = total * cos_ref[0] + jnp.where(first, other, -other)
        column = lax.broadcasted_iota(jnp.int32, total.shape, 1) + start
        turned = jnp.where(column >= kv_width, total, turned)
        out_ref[0, :, q_width + start : q_width + start + BLK] = turned.astype(jnp.bfloat16)


def join_grads(dq, own, picks, globs, cosines, sines, backs):
    seqs, rows, q_width = dq.shape
    kv_width = own.shape[2] // 2

    def whole(array):
        return pl.BlockSpec((1,) + array.shape[1:], lambda s: (s, 0, 0))

    table = pl.BlockSpec((1, rows, BLK), lambda s: (0, 0, 0))
    out_shape = jax.ShapeDtypeStruct((seqs, rows, q_width + 2 * kv_width), jnp.bfloat16)
    return pl.pallas_call(
        functools.partial(join_kernel, q_width, kv_width),
        out_shape=out_shape,
        grid=(seqs,),
        in_specs=[whole(dq), whole(own), whole(picks), whole(globs), table, table]
        + [whole(back) for back in backs],
        out_specs=whole(out_shape),
        cost_estimate=pl.CostEstimate(
            flops=20 * own.size, bytes_accessed=4 * dq.size + 12 * own.size, transcendentals=0
        ),
    )(dq, own, picks, globs, cosines, sines, *backs)


def adam_kernel(batch, meta, rates, *refs):
    master_ref, first_ref, second_ref, left_ref, right_ref = refs[:5]
    sources = refs[5:-6]
    new_first_ref, new_second_ref, new_master_ref, copy_ref, tiles, arrived = refs[-6:]
    step, steps = pl.program_id(0), pl.num_programs(0)
    slot = step % 2

    def fetch(at_step, at_slot):
        for place in range(batch):
            tile = at_step * batch + place
            for number, source in enumerate(sources):

                @pl.when(meta[0, tile] == number)
                def _(source=source, tile=tile, place=place):
                    top = pl.multiple_of(meta[2, tile], BLK)
                    left = pl.multiple_of(meta[3, tile], BLK)
                    pltpu.make_async_copy(
                        source.at[meta[1, tile], pl.ds(top, BLK), pl.ds(left, BLK)],
                        tiles.at[at_slot, place],
                        arrived.at[at_slot],
                    ).start()

    @pl.when(step == 0)
    def _():
        fetch(0, 0)

    @pl.when(step + 1 < steps)
    def _():
        fetch(step + 1, 1 - slot)

    pltpu.make_async_copy(tiles.at[slot], tiles.at[slot], arrived.at[slot]).wait()
    places = range(batch)
    lefts = [left_ref[place].astype(jnp.bfloat16) for place in places]
    rights = [right_ref[place].astype(jnp.bfloat16) for place in places]
    turned = [over_first(lefts[place], tiles[slot, place]).astype(jnp.bfloat16) for place in places]
    rotated = [
        jnp.dot(turned[place], rights[place], preferred_element_type=jnp.float32) for place in places
    ]
    directions = []
    for place in places:
        new_first = beta_one * first_ref[place] + (1.0 - beta_one) * rotated[place]
        new_second = beta_two * second_ref[place] + (1.0 - beta_two) * rotated[place] * rotated[place]
        direction = (new_first * (1.0 / (1.0 - beta_one**STEP))) / (
            jnp.sqrt(new_second * (1.0 / (1.0 - beta_two**STEP))) + adam_eps
        )
        new_first_ref[place] = new_first
        new_second_ref[place] = new_second
        directions.append(direction.astype(jnp.bfloat16))
    updates = [
        jnp.dot(lefts[place], directions[place], preferred_element_type=jnp.float32) for place in places
    ]
    updates = [over_last(updates[place].astype(jnp.bfloat16), rights[place]) for place in places]
    for place in places:
        old = master_ref[place]
        new_master = old - rates[step * batch + place] * (updates[place] + weight_decay * old)
        new_master_ref[place] = new_master
        copy_ref[place] = new_master.astype(jnp.bfloat16)


def adam(meta, rates, state, sources):
    count = state[0].shape[0]
    batch = max(size for size in range(1, 33) if count % size == 0)
    block = pl.BlockSpec((batch, BLK, BLK), lambda s, *_: (s, 0, 0))
    anywhere = pl.BlockSpec(memory_space=pl.ANY)
    shape = (count, BLK, BLK)
    return pl.pallas_call(
        functools.partial(adam_kernel, batch),
        out_shape=[jax.ShapeDtypeStruct(shape, jnp.float32)] * 3
        + [jax.ShapeDtypeStruct(shape, jnp.bfloat16)],
        grid_spec=pltpu.PrefetchScalarGridSpec(
            num_scalar_prefetch=2,
            grid=(count // batch,),
            in_specs=[block] * 5 + [anywhere] * len(sources),
            out_specs=[block] * 4,
            scratch_shapes=[
                pltpu.VMEM((2, batch, BLK, BLK), jnp.bfloat16),
                pltpu.SemaphoreType.DMA((2,)),
            ],
        ),
        compiler_params=pltpu.CompilerParams(vmem_limit_bytes=56 * 2**20),
        cost_estimate=pl.CostEstimate(
            flops=8 * count * BLK**3, bytes_accessed=36 * count * BLK**2, transcendentals=0
        ),
    )(meta, rates, *state, *sources)


def per_device(
    block_input,
    cotangent,
    glob_select,
    assignment,
    master,
    first_moment,
    second_moment,
    left_basis,
    right_basis,
    gains,
    gain_first,
    gain_second,
):
    band_total = lax.axis_size("fsdp")
    rep_total = lax.axis_size("rep")
    place = lax.axis_index("rep")
    band = lax.axis_index("fsdp")
    heads = H // rep_total
    kv_heads = KVH // rep_total
    q_width = heads * HD
    kv_width = kv_heads * HD
    tok_count = block_input.shape[1]
    own_count = master.shape[1]
    tile_total = own_count * rep_total
    aligned = square() and whole_tiles(band_total, rep_total)
    tile_order = assignment[0]

    residual = block_input[0].astype(jnp.float32)
    grad_top = cotangent[0]
    position = band * tok_count + jnp.arange(tok_count, dtype=jnp.int32)
    cosine_table, sine_table = rope_tables(position)
    wide_cosine = jnp.concatenate([cosine_table, cosine_table], 1)[None]
    wide_sine = jnp.concatenate([sine_table, sine_table], 1)[None]
    scale_one = lax.rsqrt(jnp.mean(residual * residual, -1, keepdims=True) + norm_eps)
    normed_one = (residual * scale_one * gains[0]).astype(jnp.bfloat16)
    pick_rows = glob_select[0]
    glob_total = pick_rows.shape[0]
    selector = pick_rows.astype(jnp.bfloat16)
    glob_pos_part = jnp.sum(pick_rows * position[None, :], 1)
    digits = jnp.concatenate([glob_pos_part // 256, glob_pos_part % 256]).astype(jnp.bfloat16)
    digits = jnp.pad(digits[None], ((0, 7), (0, D - 2 * glob_total)))
    glob_rows = jnp.dot(selector, normed_one, preferred_element_type=jnp.float32).astype(jnp.bfloat16)
    glob_rows = add_all(jnp.concatenate([glob_rows, digits], 0), "fsdp").astype(jnp.bfloat16)
    packed = [normed_one, glob_rows, selector.reshape(-1, D)]
    packed = jnp.concatenate(packed, 0)
    packed = jnp.pad(packed, ((0, -packed.shape[0] % 32), (0, 0)))

    def over_bands(slice_rows):
        return lax.all_gather(slice_rows, "fsdp", axis=0, tiled=True)

    if aligned:
        half = BLK // 2
        low, high = (master[0, :, rows].astype(jnp.bfloat16) for rows in (slice(0, half), slice(half, BLK)))
        layout = slice_layout(band_total, rep_total)
        attn_layout = jnp.asarray(np.concatenate(layout[:4], 2))
        wanted = jnp.take(tile_order, by_place(attn_layout).reshape(-1), mode="clip")
        meta = jnp.stack([wanted // own_count == place, wanted % own_count], 0).astype(jnp.int32)
        attn_part = place_tiles(low, high, meta, *attn_layout.shape)
        attn_part = rep_scatter(attn_part).astype(jnp.bfloat16)
        low, attn_part = lax.optimization_barrier((low, attn_part))
        slots = square_pieces(low)
        attn = over_bands(attn_part)
        grids = [lax.dynamic_index_in_dim(jnp.asarray(grid), place, 0, False) for grid in layout]

        def find(wanted):
            wanted = jnp.take(tile_order, jnp.concatenate([grid.reshape(-1) for grid in wanted]), mode="clip")
            entry, row = (wanted // own_count) ^ place, wanted % own_count
            cut = own_count // 2
            high = (entry == 3) & (row >= cut)
            found = jnp.stack([jnp.where(high, 4, entry), jnp.where(high, row - cut, row)], 0)
            return found.astype(jnp.int32)

        all_grid = jnp.concatenate(grids[4:], 1)
        (first_part,) = gather_strips(slots, find([all_grid]), [all_grid.shape])
        packed, first_part, attn = lax.optimization_barrier((packed, first_part, attn))
        early = over_bands(first_part)
    packed_all = rep_gather(packed)
    if aligned:
        packed_all, high = lax.optimization_barrier((packed_all, high))
        later_slots = square_pieces(high)
    normed_one_all = packed_all[:, :tok_count].reshape(-1, D)
    at = tok_count + glob_total
    glob_digits = packed_all[:, at, : 2 * glob_total].astype(jnp.float32)
    glob_place = glob_digits[:, :glob_total] * 256.0 + glob_digits[:, glob_total:]
    at += 8
    selector_all = packed_all[:, at : at + selector.size // D].reshape(rep_total, glob_total, tok_count)

    if aligned:
        in_width = q_width + 2 * kv_width
        w_inner, w_output = attn[:, :in_width], attn[:, in_width:]
    else:
        slots = lax.all_gather(master[0].astype(jnp.bfloat16), "rep", axis=0, tiled=True)
        tiles = jnp.take(slots, tile_order, axis=0, mode="clip")
        slices = cut_slices(band_matrices(tiles, band_total), band_total, rep_total)
        w_inner = over_bands(jnp.concatenate(slices[0:3], 1))
        w_output = over_bands(slices[3])
        w_gate = over_bands(slices[4])
        w_up = over_bands(slices[5])
        w_down = over_bands(slices[6])

    w_output = by_place(w_output.reshape(rep_total, q_width, -1)).reshape(D, -1)

    def mul(rows, weight):
        return jnp.dot(rows, weight, preferred_element_type=jnp.float32)

    def mul_back(rows, weight):
        return lax.dot_general(rows, weight, (((1,), (1,)), ((), ())), preferred_element_type=jnp.float32)

    def weight_grad(rows, grad_rows):
        return lax.dot_general(
            rows, grad_rows, (((0,), (0,)), ((), ())), preferred_element_type=jnp.float32
        ).astype(jnp.bfloat16)

    def own_sum(partial):
        return rep_scatter(partial.astype(jnp.bfloat16).reshape(rep_total, tok_count, D))

    inner_rows = mul(packed_all.reshape(-1, D), w_inner).reshape(rep_total, -1, w_inner.shape[1])
    packed_all, normed_one_all = lax.optimization_barrier((packed_all, normed_one_all))
    queries, own_pairs = rope_rows(inner_rows, tok_count, 0, q_width, kv_width, wide_cosine, wide_sine)
    glob_cosine, glob_sine = rope_tables(glob_place.reshape(-1))
    glob_cosine = jnp.concatenate([glob_cosine, glob_cosine], 1).reshape(rep_total, glob_total, -1)
    glob_sine = jnp.concatenate([glob_sine, glob_sine], 1).reshape(rep_total, glob_total, -1)
    (glob_pairs,) = rope_rows(
        inner_rows, glob_total, tok_count // glob_total, q_width, kv_width, glob_cosine, glob_sine, False
    )
    back_count = (WINDOW + tok_count - 2) // tok_count
    odd = band % 2 == 1
    by_chip = back_count == 2 and band_total % 2 == 0
    if by_chip:
        two_back = shifted(own_pairs, "fsdp", 2)
        pair_blocks = [two_back, to_core(jnp.where(odd, two_back, own_pairs))]
    else:
        pair_blocks = [shifted(own_pairs, "fsdp", distance) for distance in range(back_count, 0, -1)]
    pair_blocks = pair_blocks + [own_pairs, glob_pairs]
    glob_spots = jnp.broadcast_to(glob_place[:, :, None], (rep_total, glob_total, BLK))
    band_number = band.astype(jnp.int32).reshape(1)
    attended_low, lse = attend(band_number, glob_spots, queries, pair_blocks)
    if aligned:
        *later_slots, attended_low, early = lax.optimization_barrier((*later_slots, attended_low, early))
        last_grid = jnp.concatenate(grids[4:6], 1)
        last_part, down_part = gather_strips(
            later_slots, find([last_grid, grids[6]]), [last_grid.shape, grids[6].shape]
        )

        def by_strips(gathered):
            return gathered.reshape(band_total, -1, all_grid.shape[0], half, gathered.shape[-1])

        early, late, late_down = by_strips(early), by_strips(over_bands(last_part)), by_strips(over_bands(down_part))
    attended_all = rep_features(attended_low).reshape(-1, D)
    columns = mul(attended_all, w_output).astype(jnp.bfloat16).reshape(rep_total, tok_count, -1)
    branch = by_place(rep_exchange(columns)).transpose(1, 0, 2).reshape(tok_count, D)
    middle = residual + branch.astype(jnp.float32)
    scale_two = lax.rsqrt(jnp.mean(middle * middle, -1, keepdims=True) + norm_eps)
    normed_two = (middle * scale_two * gains[1]).astype(jnp.bfloat16)
    normed_two_all = rep_gather(normed_two).reshape(-1, D)
    normed_two_all, grad_top_now = lax.optimization_barrier((normed_two_all, grad_top))
    top_first = gather_first(grad_top_now)

    if aligned:
        gate_rows, up_rows, activation = forward_products(normed_two_all, early, late, FF // rep_total)
        top_first, activation = after(top_first, activation)
        grad_top_all = gather_join(gather_second(top_first)).reshape(-1, D)
        g_down = weight_grad(activation, grad_top_all)
        grad_top_all, g_down = lax.optimization_barrier((grad_top_all, g_down))
        grad_gate, grad_up, pieces, branch_pieces = backward_products(
            grad_top_all, gate_rows, up_rows, activation, early, late, late_down
        )
        normed_first = sum_first(pieces)
        normed_first, g_gate = after(normed_first, weight_grad(normed_two_all, grad_gate))
        grad_normed_two = sum_second(normed_first)
    else:
        gate_rows = mul(normed_two_all, w_gate)
        up_rows = mul(normed_two_all, w_up)
        sigmoid_gate = jax.nn.sigmoid(gate_rows)
        silu_gate = gate_rows * sigmoid_gate
        activation = (silu_gate * up_rows).astype(jnp.bfloat16)
        grad_top_all = gather_join(gather_second(top_first)).reshape(-1, D)
        g_down = weight_grad(activation, grad_top_all)
        grad_act = mul_back(grad_top_all, w_down)
        grad_gate = (
            grad_act * up_rows * sigmoid_gate * (1.0 + gate_rows * (1.0 - sigmoid_gate))
        ).astype(jnp.bfloat16)
        grad_up = (grad_act * silu_gate).astype(jnp.bfloat16)
        grad_normed_two = own_sum(mul_back(grad_gate, w_gate) + mul_back(grad_up, w_up))
        branch_pieces = (mul(activation, w_down),)
        g_gate = weight_grad(normed_two_all, grad_gate)
    grad_normed_two, g_gate = lax.optimization_barrier((grad_normed_two, g_gate))

    def over_tokens(partial):
        return lax.psum_scatter(partial, "fsdp", scatter_dimension=0, tiled=True)

    s_down = over_tokens(g_down)
    s_gate = over_tokens(g_gate)

    grad_middle = grad_top.astype(jnp.float32) + norm_back(middle, scale_two, gains[1], grad_normed_two)
    grad_parts = grad_middle.astype(jnp.bfloat16).reshape(tok_count, rep_total, -1).transpose(1, 0, 2)
    grad_columns = rep_exchange(by_place(grad_parts)).reshape(rep_total * tok_count, -1)
    grad_columns, grad_up = lax.optimization_barrier((grad_columns, grad_up))
    grad_attended, g_up = rep_features_sum(
        grad_columns.reshape(rep_total, tok_count, -1),
        w_output,
        lambda: weight_grad(normed_two_all, grad_up),
    )
    grad_attended = grad_attended.astype(jnp.bfloat16)
    (s_down, g_up), grad_attended = after((s_down, g_up), grad_attended)
    down_first = gather_first(s_down)
    grad_queries, *grad_blocks = attend_back(
        band_number, glob_spots, wide_cosine, wide_sine, queries, grad_attended, lse, pair_blocks
    )
    down_first, *grad_blocks = after(down_first, *grad_blocks)
    attended_all, *grad_blocks = lax.optimization_barrier((attended_all, *grad_blocks))
    g_output = weight_grad(attended_all, grad_columns)
    g_output = by_place(g_output.reshape(rep_total, q_width, -1)).reshape(D, -1)
    s_output = over_tokens(g_output)
    down_second = gather_second(down_first)
    branch_pieces, *down_second = after(tuple(branch_pieces), *down_second)
    branch_first = sum_first(branch_pieces) if aligned else (own_sum(branch_pieces[0]),)
    if by_chip:
        came = to_core(jnp.concatenate([grad_blocks[1], grad_blocks[-1]], 1))
        came, glob_came = came[:, :tok_count], came[:, tok_count:]
        total = grad_blocks[0].astype(jnp.float32) + came.astype(jnp.float32)
        sent = jnp.where(odd, total.astype(jnp.bfloat16), grad_blocks[0])
        returned = [shifted(sent, "fsdp", -2), jnp.where(odd, jnp.zeros_like(came), came)]
    else:
        returned = [
            shifted(grad_blocks[back_count - distance], "fsdp", -distance)
            for distance in range(1, back_count + 1)
        ]
    if by_chip:
        glob_both = grad_blocks[-1].astype(jnp.float32) + glob_came.astype(jnp.float32)
        glob_grads = add_all(glob_both.astype(jnp.bfloat16), "fsdp", 2)
    else:
        glob_grads = add_all(grad_blocks[-1], "fsdp")
    branch_first, g_up, glob_grads, s_gate, g_output, *returned = lax.optimization_barrier(
        (branch_first, g_up, glob_grads, s_gate, g_output, *returned)
    )
    s_up = over_tokens(g_up)
    s_down = gather_join(down_second)
    gate_first = gather_first(s_gate)
    block_out = middle + (sum_second(branch_first) if aligned else branch_first[0])
    grad_inner = join_grads(
        grad_queries, grad_blocks[-2], selector_all, glob_grads, wide_cosine, wide_sine, returned
    ).reshape(-1, q_width + 2 * kv_width)
    grad_normed_parts = mul_back(grad_inner, w_inner).astype(jnp.bfloat16).reshape(rep_total, tok_count, D)
    gate_first, grad_normed_parts = after(gate_first, grad_normed_parts)
    if square():
        normed_first = sum_first(split_pieces(grad_normed_parts))
    else:
        normed_first = (rep_scatter(grad_normed_parts),)
    grad_inner, grad_normed_parts = lax.optimization_barrier((grad_inner, grad_normed_parts))
    g_inner = weight_grad(normed_one_all, grad_inner)
    g_attn = with_layout_constraint(g_inner, Layout((0, 1)))
    gate_first, block_out, *normed_first = after(gate_first, block_out, *normed_first)
    gate_second = gather_second(gate_first)
    grad_normed_one = sum_second(normed_first) if square() else normed_first[0]
    gate_second, s_up, g_attn, grad_normed_one, s_output = after(
        gate_second, s_up, g_attn, grad_normed_one, s_output
    )
    s_attn = over_tokens(g_attn)
    s_gate = gather_join(gate_second)
    up_first = gather_first(s_up)
    s_output = rep_gather(s_output)
    grad_input = grad_middle + norm_back(residual, scale_one, gains[0], grad_normed_one)

    gain_terms = jnp.stack(
        [
            jnp.sum(grad_normed_one * residual * scale_one, 0),
            jnp.sum(grad_normed_two * middle * scale_two, 0),
        ]
    )
    square_terms = jnp.stack(
        [jnp.sum(residual * residual), jnp.sum(middle * middle), jnp.sum(block_out * block_out)]
    )
    sums = jnp.concatenate([gain_terms.reshape(-1), square_terms])

    up_first, sums = after(up_first, sums)
    s_up = gather_join(gather_second(up_first))
    sums = add_all(add_all(sums, "rep"), "fsdp")
    sums, s_attn, s_up, s_gate, s_down, s_output = lax.optimization_barrier(
        (sums, s_attn, s_up, s_gate, s_down, s_output)
    )
    gain_grad, square_total = sums[: 2 * D].reshape(2, D), sums[2 * D :]

    slot_ids = jnp.arange(tile_total, dtype=jnp.int32)
    inverse = jnp.sum(jnp.where(tile_order[None, :] == slot_ids[:, None], slot_ids[None, :], 0), 1)
    own_slots = place * own_count + jnp.arange(own_count, dtype=jnp.int32)
    owned_tiles = jnp.take(inverse, own_slots, mode="clip")
    if aligned:
        sources = [rep_gather(s_attn), s_output, s_gate, s_up, s_down]
        where = np.zeros((4, rep_total, tile_total), np.int32)
        first_col = 0
        for kind, grid in enumerate(layout):
            rows, cols = grid.shape[1:]
            first_col = 0 if kind >= 3 else first_col
            for there in range(rep_total):
                numbers = grid[there].reshape(-1)
                at = np.arange(rows * cols)
                where[0, :, numbers] = max(kind - 2, 0)
                where[2, :, numbers] = (at // cols * BLK)[:, None]
                where[3, :, numbers] = (at % cols * BLK + first_col)[:, None]
                for here in range(rep_total):
                    where[1, here, numbers] = here ^ there
            first_col += cols * BLK
        tile_spots = lax.dynamic_index_in_dim(jnp.asarray(where), place, 1, False)
        meta = jnp.take(tile_spots, owned_tiles, axis=1, mode="clip")
    else:
        splits = [0, q_width, q_width + kv_width, q_width + 2 * kv_width]
        stacks = [rep_gather(s_attn[:, low:high]) for low, high in zip(splits, splits[1:])]
        stacks += [s_output, s_gate, s_up, s_down]
        sources = [band_tiles(join_slices(stacks, band_total, rep_total))]
        meta = jnp.stack([0 * owned_tiles, owned_tiles, 0 * owned_tiles, 0 * owned_tiles], 0)
    slot_rates = jnp.take(kind_rates(band_total), owned_tiles, mode="clip")
    new_first, new_second, new_master, master_copy = adam(
        meta,
        slot_rates,
        (master[0], first_moment[0], second_moment[0], left_basis[0], right_basis[0]),
        sources,
    )
    new_gain_first = beta_one * gain_first + (1.0 - beta_one) * gain_grad
    new_gain_second = beta_two * gain_second + (1.0 - beta_two) * gain_grad * gain_grad
    gain_step = (
        new_gain_first
        / (1.0 - beta_one**STEP)
        / (jnp.sqrt(new_gain_second / (1.0 - beta_two**STEP)) + adam_eps)
    )
    new_gains = gains - gain_rate * gain_step
    rms_stats = jnp.sqrt(square_total / (rep_total * band_total * tok_count * D))
    return (
        block_out[None],
        grad_input[None],
        new_first[None],
        new_second[None],
        new_master[None],
        master_copy[None],
        new_gain_first,
        new_gain_second,
        new_gains,
        rms_stats,
    )


def solution(mesh):
    in_specs = (
        P("rep", "fsdp", None),
        P("rep", "fsdp", None),
        P("rep", None, "fsdp"),
        P("fsdp", None),
        P("fsdp", "rep", None, None),
        P("fsdp", "rep", None, None),
        P("fsdp", "rep", None, None),
        P("fsdp", "rep", None, None),
        P("fsdp", "rep", None, None),
        P(),
        P(),
        P(),
    )
    out_specs = (
        P("rep", "fsdp", None),
        P("rep", "fsdp", None),
        P("fsdp", "rep", None, None),
        P("fsdp", "rep", None, None),
        P("fsdp", "rep", None, None),
        P("fsdp", "rep", None, None),
        P(),
        P(),
        P(),
        P(),
    )
    return jax.shard_map(
        per_device, mesh=mesh, in_specs=in_specs, out_specs=out_specs, check_vma=False
    )
```
